32 devices in a mesh: groups: 2 (over y), gs: 4 (over x, core), tile: 4 (over z).
Axes of the slice: x: 2, y: 2, z: 4, core: 2. Of those that a mesh axis runs over, the one named last changes fastest.
Arguments:
- params: float32 [59, 8192], P(None, ('groups', 'gs')), parts along dimension 1, as said below
- adam_m: float32 [59, 8192], P(None, ('groups', 'gs')), parts along dimension 1, may hold values from -0.6 to 0.6
- adam_v: float32 [59, 8192], P(None, ('groups', 'gs')), parts along dimension 1, may hold values from 0.0001 to 0.01
- cameras: float32 [8, 12], P('groups'), parts along dimension 0, as said below
- target: float32 [3, 16384], P(None, ('groups', 'gs', 'tile')), parts along dimension 1, may hold values from -2 to 2
- tile_ids: int32 [64], P(('groups', 'gs', 'tile')), parts along dimension 0, may hold values from 0 to 32639, as said below
- hit_shard: int32 [64, 256, 1], P(('groups', 'gs', 'tile')), parts along dimension 0, may hold values from 0 to 3, as said below
- hit_local: int32 [64, 256], P(('groups', 'gs', 'tile')), parts along dimension 0, may hold values from 0 to 1023, as said below
Outputs:
- rendered: float32 [3, 16384], P(None, ('groups', 'gs', 'tile')), parts along dimension 1
- new_params: float32 [59, 8192], P(None, ('groups', 'gs')), parts along dimension 1
- new_m: float32 [59, 8192], P(None, ('groups', 'gs')), parts along dimension 1
- new_v: float32 [59, 8192], P(None, ('groups', 'gs')), parts along dimension 1
The draws below stay inside these ranges and needn't reach their ends.
There are 2 independent parts, one for each index of `groups`. The reference program is written for one: setup_inputs(seed, part) draws one part's arguments, and reference() takes and returns one part's arrays. A program takes and returns all parts, laid end to end along the dimension named above; each array names one. Nothing has to cross between parts.
Inputs may be any that keep to these rules, and one draw needn't show every extreme that they name: `hit_shard`: among the entries of the 2 tiles of one device no shard is named more than 256 times; one shard, the same for all of that device's tiles, is named exactly 2 * 256 / 4 times in each of them. `hit_local`: no Gaussian stands twice in one list; the lists of tile slots 8 * q to 8 * q + 7 name only local indices q * 256 to (q + 1) * 256 - 1; along each list the Gaussians' third camera coordinate in the tile's view increases, and each listed Gaussian's mean projects in that view within 4 pixels of the block of eight tiles. `tile_ids`: distinct tiles of the window; tile v * 120 * 68 + r * 120 + c is column c of tile row r of view v; slots 8 * q to 8 * q + 7 hold a block of 4 by 2 tiles of one view, row by row, whose first tile has an even row and a column divisible by 4. `cameras`: orthonormal rotations; every Gaussian lies at least 50 units in front of every camera. `params`: each quaternion's first component is 0.5 or more.
All inputs are finite; a program needn't handle non-finite values.
Results may differ from the reference program's by a relative error of at most 0.0003.
Values sent between devices are 32-bit elements; how exact they have to be, the bound alone decides.
No kernel may reach another device: no remote copies, remote signals or barrier semaphores. Data moves between devices by JAX's collectives and lax.ppermute only.
A program may use at most 128 MiB of HBM per device.

```python
import math
import jax
import jax.numpy as jnp
from jax import lax

FEAT = 59
VIEWS = 4
TILES_X = 120
TILES_Y = 68
TILE_SIDE = 16
TILE_PIX = 256
K = 256
TD = 2
G_DEV = 1024
GAUSS = 4096
TILES = 32
CAP = 256
POOL = 256


def scene_cameras(key):
    key = jax.random.fold_in(key, 21)
    keys = jax.random.split(key, 3)
    heading = jax.random.uniform(keys[0], (VIEWS,), jnp.float32, -math.pi, math.pi)
    tilting = jax.random.uniform(keys[1], (VIEWS,), jnp.float32, -0.1, 0.1)
    placed = jax.random.uniform(keys[2], (VIEWS, 2), jnp.float32, -5.0, 5.0)
    cos_h = jnp.cos(heading)
    sin_h = jnp.sin(heading)
    cos_t = jnp.cos(tilting)
    sin_t = jnp.sin(tilting)
    nought = jnp.zeros_like(heading)
    return jnp.stack([cos_h, -sin_h, nought, -cos_t * sin_h, -cos_t * cos_h, sin_t, -sin_t * sin_h, -sin_t * cos_h, -cos_t, placed[:, 0], placed[:, 1], nought + 100.0], axis=1)


def patch_layout(key):
    key = jax.random.fold_in(key, 22)
    blocks_x = TILES_X // 4
    blocks_y = TILES_Y // 2
    chosen = jax.random.permutation(key, VIEWS * blocks_x * blocks_y)[:TILES // 8].astype(jnp.int32)
    view = chosen // (blocks_x * blocks_y)
    rest = chosen % (blocks_x * blocks_y)
    block_row = rest // blocks_x
    block_col = rest % blocks_x
    slot = jnp.arange(8, dtype=jnp.int32)
    rows = 2 * block_row[:, None] + slot[None, :] // 4
    cols = 4 * block_col[:, None] + slot[None, :] % 4
    return (view[:, None] * (TILES_X * TILES_Y) + rows * TILES_X + cols).reshape(-1).astype(jnp.int32)


def depth_ranks(key):
    key = jax.random.fold_in(key, 23)
    pool_all = GAUSS // G_DEV * POOL
    keys = jax.random.split(key, TILES // 8)
    return jax.vmap(lambda one_key: jax.random.permutation(one_key, pool_all))(keys).astype(jnp.int32)


def list_table(key):
    ranks = depth_ranks(key)
    key = jax.random.fold_in(key, 24)
    shards = GAUSS // G_DEV
    pool_all = shards * POOL
    hot_count = CAP // TD
    keys = jax.random.split(key, 3)
    hot = jax.random.randint(keys[0], (TILES // TD,), 0, shards).astype(jnp.int32)
    hot_of_tile = jnp.repeat(hot, TD)
    first = jax.random.randint(keys[1], (TILES, shards, POOL), 0, 4096).astype(jnp.int32)
    slot = jnp.arange(POOL, dtype=jnp.int32)
    first_key = first * POOL + slot[None, None, :]
    position = jnp.argsort(jnp.argsort(first_key, axis=2), axis=2).astype(jnp.int32)
    eligible = (position < hot_count).reshape(TILES, pool_all)
    flat = jnp.arange(pool_all, dtype=jnp.int32)
    shard_flat = flat // POOL
    is_hot = shard_flat[None, :] == hot_of_tile[:, None]
    grade = jnp.where(eligible, jnp.where(is_hot, 2, 1), 0).astype(jnp.int32)
    second = jax.random.randint(keys[2], (TILES, pool_all), 0, 4096).astype(jnp.int32)
    score = (grade * 4096 + second) * pool_all + flat[None, :]
    picked = jax.lax.top_k(score, K)[1].astype(jnp.int32)
    patch = jnp.arange(TILES, dtype=jnp.int32) // 8
    depth_of = jnp.take_along_axis(ranks[patch], picked, axis=1)
    order = jnp.argsort(depth_of, axis=1)
    listed = jnp.take_along_axis(picked, order, axis=1)
    shard_rows = (listed // POOL).astype(jnp.int32)
    local_rows = (patch[:, None] * POOL + listed % POOL).astype(jnp.int32)
    return (shard_rows, local_rows)


def draw_cameras(key, part):
    return scene_cameras(key)


def draw_tile_ids(key, part):
    return patch_layout(key)


def draw_hit_shard(key, part):
    shard_rows, local_rows = list_table(key)
    return shard_rows[:, :, None]


def draw_hit_local(key, part):
    shard_rows, local_rows = list_table(key)
    return local_rows


def draw_params(key, part):
    cams = scene_cameras(key)
    layout = patch_layout(key)
    ranks = depth_ranks(key)
    key = jax.random.fold_in(key, 11)
    keys = jax.random.split(key, 10)
    shards = GAUSS // G_DEV
    pool_all = shards * POOL
    gauss = jnp.arange(GAUSS, dtype=jnp.int32)
    shard_of = gauss // G_DEV
    local = gauss % G_DEV
    patch = local // POOL
    rank = ranks[patch, shard_of * POOL + local % POOL].astype(jnp.float32)
    first_tile = layout[8 * patch]
    view = first_tile // (TILES_X * TILES_Y)
    within = first_tile % (TILES_X * TILES_Y)
    corner_x = (within % TILES_X * TILE_SIDE).astype(jnp.float32)
    corner_y = (within // TILES_X * TILE_SIDE).astype(jnp.float32)
    pix_x = corner_x + jax.random.uniform(keys[0], (GAUSS,), jnp.float32, -4.0, 68.0)
    pix_y = corner_y + jax.random.uniform(keys[1], (GAUSS,), jnp.float32, -4.0, 36.0)
    depth = 80.0 + 12.0 * (rank + jax.random.uniform(keys[2], (GAUSS,), jnp.float32, 0.1, 0.9)) / pool_all
    cam = cams[view]
    ray_x = (pix_x - 960.0) / 1000.0 * depth
    ray_y = (pix_y - 540.0) / 1000.0 * depth
    world = jnp.stack([cam[:, 9 + axis_i] + cam[:, axis_i] * ray_x + cam[:, 3 + axis_i] * ray_y + cam[:, 6 + axis_i] * depth for axis_i in range(3)])
    sigma_px = jnp.exp(jax.random.uniform(keys[3], (GAUSS,), jnp.float32, math.log(20.0), math.log(50.0)))
    base = jnp.log(sigma_px * depth / 1000.0)
    log_scale = base[None, :] + jax.random.uniform(keys[4], (3, GAUSS), jnp.float32, -0.3, 0.3)
    quat_head = jax.random.uniform(keys[5], (1, GAUSS), jnp.float32, 0.5, 1.0)
    quat_tail = jax.random.uniform(keys[6], (3, GAUSS), jnp.float32, -0.5, 0.5)
    logit = jnp.clip(-4.0 + 0.5 * jax.random.normal(keys[7], (1, GAUSS), jnp.float32), -5.0, -3.0)
    colour_base = jnp.clip(0.6 * jax.random.normal(keys[8], (3, 1, GAUSS), jnp.float32), -1.0, 1.0)
    colour_rest = jnp.clip(0.2 * jax.random.normal(keys[9], (3, 15, GAUSS), jnp.float32), -0.4, 0.4)
    colour = jnp.concatenate([colour_base, colour_rest], axis=1).reshape(48, GAUSS)
    return jnp.concatenate([world, log_scale, quat_head, quat_tail, logit, colour], axis=0)


def block_levels(key, shape, cuts, least, largest):
    factor_of, own = 1.0, jax.random.fold_in(key, 6)
    for dim, blocks in cuts:
        draws = jnp.exp(jax.random.uniform(jax.random.fold_in(own, dim), (blocks,), jnp.float32, least / len(cuts), largest / len(cuts)))
        factor_of = factor_of * jnp.repeat(draws, shape[dim] // blocks).reshape([-1 if axis == dim else 1 for axis in range(len(shape))])
    return factor_of


def centred(own_key, dims, deviation, most, pieces=(), kind=jnp.bfloat16):
    values = jax.random.normal(own_key, dims, jnp.float32) * deviation
    if len(pieces) > 0:
        values = block_levels(own_key, dims, pieces, -0.22, 0.18) * values
    return jnp.clip(values, min=-most, max=most).astype(kind)


def setup_inputs(seed: int = 0, part: int = 0) -> dict:
    splits = jax.random.split(jax.random.key(seed), 9)
    part_keys = jax.random.split(jax.random.fold_in(splits[8], part), 9)
    return {
        "params": draw_params(jax.random.fold_in(jax.random.fold_in(splits[8], part), 71), part),
        "adam_m": centred(part_keys[1], (FEAT, GAUSS), 0.1, 0.6, ((1, 4),), jnp.float32),
        "adam_v": jnp.clip(jnp.exp(math.log(0.01) - 4.6051702 * jax.random.uniform(part_keys[2], (FEAT, GAUSS), jnp.float32) ** block_levels(part_keys[2], (FEAT, GAUSS), ((1, 4),), -0.2, 0.2)), 0.0001, 0.01),
        "cameras": draw_cameras(jax.random.fold_in(jax.random.fold_in(splits[8], part), 71), part),
        "target": centred(part_keys[4], (3, TILES * TILE_PIX), 0.3, 2.0, ((1, 16),), jnp.float32),
        "tile_ids": draw_tile_ids(jax.random.fold_in(jax.random.fold_in(splits[8], part), 71), part),
        "hit_shard": draw_hit_shard(jax.random.fold_in(jax.random.fold_in(splits[8], part), 71), part),
        "hit_local": draw_hit_local(jax.random.fold_in(jax.random.fold_in(splits[8], part), 71), part),
    }


focal_length = 1000.0
center_x = 960.0
center_y = 540.0
dilation = 0.3
beta_one = 0.9
beta_two = 0.999
learn_rate = 0.01
adam_eps = 1e-08
adam_steps = 100.0
sh_const = (0.28209479177387814, 0.4886025119029199, 1.0925484305920792, 0.31539156525252005, 0.5462742152960396, 0.5900435899266435, 2.890611442640554, 0.4570457994644658, 0.3731763325901154, 1.445305721320277)

def sh_basis(unit_x, unit_y, unit_z):
    sq_x = unit_x * unit_x
    sq_y = unit_y * unit_y
    sq_z = unit_z * unit_z
    terms = [sh_const[0] + 0.0 * unit_x, -sh_const[1] * unit_y, sh_const[1] * unit_z, -sh_const[1] * unit_x, sh_const[2] * unit_x * unit_y, -sh_const[2] * unit_y * unit_z, sh_const[3] * (2.0 * sq_z - sq_x - sq_y), -sh_const[2] * unit_x * unit_z, sh_const[4] * (sq_x - sq_y), -sh_const[5] * unit_y * (3.0 * sq_x - sq_y), sh_const[6] * unit_x * unit_y * unit_z, -sh_const[7] * unit_y * (4.0 * sq_z - sq_x - sq_y), sh_const[8] * unit_z * (2.0 * sq_z - 3.0 * sq_x - 3.0 * sq_y), -sh_const[7] * unit_x * (4.0 * sq_z - sq_x - sq_y), sh_const[9] * unit_z * (sq_x - sq_y), -sh_const[5] * unit_x * (sq_x - 3.0 * sq_y)]
    return jnp.stack(terms)

def project(params, camera):
    rotate = [[camera[3 * row_i + col_i] for col_i in range(3)] for row_i in range(3)]
    offset = [params[axis_i] - camera[9 + axis_i] for axis_i in range(3)]
    in_camera = [rotate[row_i][0] * offset[0] + rotate[row_i][1] * offset[1] + rotate[row_i][2] * offset[2] for row_i in range(3)]
    inverse = 1.0 / in_camera[2]
    mean_x = focal_length * in_camera[0] * inverse + center_x
    mean_y = focal_length * in_camera[1] * inverse + center_y
    squared = jnp.exp(2.0 * params[3:6])
    rotor = params[6:10] * lax.rsqrt(lax.optimization_barrier(jnp.sum(params[6:10] * params[6:10], axis=0)))[None, :]
    real_w, imag_x, imag_y, imag_z = (rotor[0], rotor[1], rotor[2], rotor[3])
    turn = [[1.0 - 2.0 * (imag_y * imag_y + imag_z * imag_z), 2.0 * (imag_x * imag_y - real_w * imag_z), 2.0 * (imag_x * imag_z + real_w * imag_y)], [2.0 * (imag_x * imag_y + real_w * imag_z), 1.0 - 2.0 * (imag_x * imag_x + imag_z * imag_z), 2.0 * (imag_y * imag_z - real_w * imag_x)], [2.0 * (imag_x * imag_z - real_w * imag_y), 2.0 * (imag_y * imag_z + real_w * imag_x), 1.0 - 2.0 * (imag_x * imag_x + imag_y * imag_y)]]
    spread = [[sum((turn[row_i][inner] * turn[col_i][inner] * squared[inner] for inner in range(3))) for col_i in range(3)] for row_i in range(3)]
    nought = jnp.zeros_like(inverse)
    jacobian = [[focal_length * inverse, nought, -focal_length * in_camera[0] * inverse * inverse], [nought, focal_length * inverse, -focal_length * in_camera[1] * inverse * inverse]]
    screen = [[sum((jacobian[row_i][inner] * rotate[inner][col_i] for inner in range(3))) for col_i in range(3)] for row_i in range(2)]

    def covariance(first, second):
        return sum((screen[first][row_i] * spread[row_i][col_i] * screen[second][col_i] for row_i in range(3) for col_i in range(3)))
    cov_xx = covariance(0, 0) + dilation
    cov_xy = covariance(0, 1)
    cov_yy = covariance(1, 1) + dilation
    determinant = cov_xx * cov_yy - cov_xy * cov_xy
    conic_a = cov_yy / determinant
    conic_b = -cov_xy / determinant
    conic_c = cov_xx / determinant
    opacity = jax.nn.sigmoid(params[10])
    length = jnp.sqrt(offset[0] * offset[0] + offset[1] * offset[1] + offset[2] * offset[2])
    basis = sh_basis(offset[0] / length, offset[1] / length, offset[2] / length)
    coeffs = params[11:59].reshape(3, 16, -1)
    colour = 0.5 + lax.optimization_barrier(jnp.sum(coeffs * basis[None], axis=1))
    return jnp.stack([mean_x, mean_y, conic_a, conic_b, conic_c, opacity, colour[0], colour[1], colour[2]])

def pixel_grid(tile_id, pixel_count):
    within = tile_id % (TILES_X * TILES_Y)
    tile_row = within // TILES_X
    tile_col = within % TILES_X
    pixel = jnp.arange(pixel_count, dtype=jnp.int32)
    pixel_x = (tile_col * TILE_SIDE + pixel % TILE_SIDE).astype(jnp.float32) + 0.5
    pixel_y = (tile_row * TILE_SIDE + pixel // TILE_SIDE).astype(jnp.float32) + 0.5
    return (pixel_x, pixel_y)

def composite(entry_rows, pixel_x, pixel_y):
    delta_x = pixel_x[:, None] - entry_rows[0][None, :]
    delta_y = pixel_y[:, None] - entry_rows[1][None, :]
    power = -0.5 * (entry_rows[2][None, :] * delta_x * delta_x + entry_rows[4][None, :] * delta_y * delta_y) - entry_rows[3][None, :] * delta_x * delta_y
    alpha = entry_rows[5][None, :] * jnp.exp(power)
    keeping = jnp.log1p(-alpha)
    before = jnp.cumsum(keeping, axis=1) - keeping
    weight = alpha * jnp.exp(before)
    return jnp.einsum('cj,pj->cp', entry_rows[6:9], weight, precision=lax.Precision.HIGHEST)

def adam_update(params, moment, second, grad):
    new_m = beta_one * moment + (1.0 - beta_one) * grad
    new_v = beta_two * second + (1.0 - beta_two) * grad * grad
    m_hat = new_m / (1.0 - beta_one ** adam_steps)
    v_hat = new_v / (1.0 - beta_two ** adam_steps)
    return (params - learn_rate * m_hat / (jnp.sqrt(v_hat) + adam_eps), new_m, new_v)

def reference(params, adam_m, adam_v, cameras, target, tile_ids, hit_shard, hit_local):
    gauss_ids = hit_shard[:, :, 0] * G_DEV + hit_local
    view_ids = tile_ids // (TILES_X * TILES_Y)

    def render(values):
        projected = jnp.stack([project(values, cameras[view_index]) for view_index in range(VIEWS)])

        def one_tile(inputs):
            tile_id, view_id, listed = inputs
            table = lax.dynamic_index_in_dim(projected, view_id, 0, False)
            entry_rows = jnp.take(table, listed, axis=1)
            pixel_x, pixel_y = pixel_grid(tile_id, TILE_PIX)
            return composite(entry_rows, pixel_x, pixel_y)
        images = lax.map(jax.checkpoint(one_tile), (tile_ids, view_ids, gauss_ids))
        return jnp.transpose(images, (1, 0, 2)).reshape(3, -1)
    rendered, pull = jax.vjp(render, params)
    grad = pull(rendered - target)[0]
    new_params, new_m, new_v = adam_update(params, adam_m, adam_v, grad)
    return (rendered, new_params, new_m, new_v)
```

```python
import functools

import jax
import jax.numpy as jnp
from jax import lax
from jax.experimental import pallas as pl
from jax.experimental.pallas import tpu as pltpu
from jax.sharding import PartitionSpec as P

TILES_X = 120
TILES_Y = 68
TILE_SIDE = 16
BLOCK_TILES = 8
LANES = 128
ROWS = 16
F32 = jnp.float32
BF16 = jnp.bfloat16

focal_length = 1000.0
center_x = 960.0
center_y = 540.0
dilation = 0.3
beta_one = 0.9
beta_two = 0.999
learn_rate = 0.01
adam_eps = 1e-08
adam_steps = 100.0
sh_const = (
    0.28209479177387814,
    0.4886025119029199,
    1.0925484305920792,
    0.31539156525252005,
    0.5462742152960396,
    0.5900435899266435,
    2.890611442640554,
    0.4570457994644658,
    0.3731763325901154,
    1.445305721320277,
)


def sh_basis(x, y, z):
    s = sh_const
    xx, yy, zz = x * x, y * y, z * z
    return [
        None,
        -s[1] * y,
        s[1] * z,
        -s[1] * x,
        s[2] * (x * y),
        -s[2] * (y * z),
        s[3] * (2.0 * zz - xx - yy),
        -s[2] * (x * z),
        s[4] * (xx - yy),
        -s[5] * y * (3.0 * xx - yy),
        s[6] * (x * y) * z,
        -s[7] * y * (4.0 * zz - xx - yy),
        s[8] * z * (2.0 * zz - 3.0 * xx - 3.0 * yy),
        -s[7] * x * (4.0 * zz - xx - yy),
        s[9] * z * (xx - yy),
        -s[5] * x * (xx - 3.0 * yy),
    ]


def sh_pull(h, x, y, z):
    s = sh_const
    xx, yy, zz = x * x, y * y, z * z
    xy, xz, yz = x * y, x * z, y * z
    diff = xx - yy
    ring = 4.0 * zz - xx - yy
    g_x = (
        -s[1] * h[3]
        + s[2] * (h[4] * y - h[7] * z)
        - (2.0 * s[3]) * h[6] * x
        + (2.0 * s[4]) * h[8] * x
        - (6.0 * s[5]) * h[9] * xy
        + s[6] * h[10] * yz
        + (2.0 * s[7]) * h[11] * xy
        - (6.0 * s[8]) * h[12] * xz
        - s[7] * h[13] * (ring - 2.0 * xx)
        + (2.0 * s[9]) * h[14] * xz
        - (3.0 * s[5]) * h[15] * diff
    )
    g_y = (
        -s[1] * h[1]
        + s[2] * (h[4] * x - h[5] * z)
        - (2.0 * s[3]) * h[6] * y
        - (2.0 * s[4]) * h[8] * y
        - (3.0 * s[5]) * h[9] * diff
        + s[6] * h[10] * xz
        - s[7] * h[11] * (ring - 2.0 * yy)
        - (6.0 * s[8]) * h[12] * yz
        + (2.0 * s[7]) * h[13] * xy
        - (2.0 * s[9]) * h[14] * yz
        + (6.0 * s[5]) * h[15] * xy
    )
    g_z = (
        s[1] * h[2]
        - s[2] * (h[5] * y + h[7] * x)
        + (4.0 * s[3]) * h[6] * z
        + s[6] * h[10] * xy
        - (8.0 * s[7]) * (h[11] * yz + h[13] * xz)
        + s[8] * h[12] * (6.0 * zz - 3.0 * xx - 3.0 * yy)
        + s[9] * h[14] * diff
    )
    return g_x, g_y, g_z


def project_parts(feat, cam):
    rot = [[cam[3 * r + c] for c in range(3)] for r in range(3)]
    off = [feat(a) - cam[9 + a] for a in range(3)]
    in_cam = [rot[r][0] * off[0] + rot[r][1] * off[1] + rot[r][2] * off[2] for r in range(3)]
    inv = 1.0 / in_cam[2]
    u = in_cam[0] * inv
    v = in_cam[1] * inv
    finv = focal_length * inv
    scale = [jnp.exp(2.0 * feat(3 + a)) for a in range(3)]
    quat = [feat(6 + a) for a in range(4)]
    rnorm = lax.rsqrt(quat[0] * quat[0] + quat[1] * quat[1] + quat[2] * quat[2] + quat[3] * quat[3])
    w, x, y, z = [q * rnorm for q in quat]
    turn = [
        [1.0 - 2.0 * (y * y + z * z), 2.0 * (x * y - w * z), 2.0 * (x * z + w * y)],
        [2.0 * (x * y + w * z), 1.0 - 2.0 * (x * x + z * z), 2.0 * (y * z - w * x)],
        [2.0 * (x * z - w * y), 2.0 * (y * z + w * x), 1.0 - 2.0 * (x * x + y * y)],
    ]
    screen = [
        [finv * (rot[0][c] - u * rot[2][c]) for c in range(3)],
        [finv * (rot[1][c] - v * rot[2][c]) for c in range(3)],
    ]
    axes = [
        [sum(screen[r][c] * turn[c][k] for c in range(3)) for k in range(3)] for r in range(2)
    ]
    wide = [[axes[r][k] * scale[k] for k in range(3)] for r in range(2)]
    cov_xx = sum(wide[0][k] * axes[0][k] for k in range(3)) + dilation
    cov_xy = sum(wide[0][k] * axes[1][k] for k in range(3))
    cov_yy = sum(wide[1][k] * axes[1][k] for k in range(3)) + dilation
    rdet = 1.0 / (cov_xx * cov_yy - cov_xy * cov_xy)
    conic = (cov_yy * rdet, -cov_xy * rdet, cov_xx * rdet)
    opacity = 1.0 / (1.0 + jnp.exp(-feat(10)))
    rlen = lax.rsqrt(off[0] * off[0] + off[1] * off[1] + off[2] * off[2])
    way = [off[a] * rlen for a in range(3)]
    return dict(
        rot=rot, inv=inv, u=u, v=v, finv=finv, scale=scale, rnorm=rnorm, rotor=(w, x, y, z), turn=turn,
        screen=screen, axes=axes, wide=wide, conic=conic, opacity=opacity, rlen=rlen, way=way,
    )


def project_rows(feat, cam):
    part = project_parts(feat, cam)
    basis = sh_basis(*part["way"])
    colours = []
    for k in range(3):
        total = 0.5 + sh_const[0] * feat(11 + 16 * k)
        for b in range(1, 16):
            total = total + feat(11 + 16 * k + b) * basis[b]
        colours.append(total)
    mean_x = focal_length * part["u"] + center_x
    mean_y = focal_length * part["v"] + center_y
    return [mean_x, mean_y, *part["conic"], part["opacity"], *colours]


def project_pull(feat, cam, grads, put):
    part = project_parts(feat, cam)
    g_mx, g_my, g_a, g_b, g_c, g_o = grads[:6]
    g_col = grads[6:9]
    way, rlen = part["way"], part["rlen"]
    basis = sh_basis(*way)
    pulled = [None]
    for k in range(3):
        put(11 + 16 * k, sh_const[0] * g_col[k])
    for b in range(1, 16):
        total = 0.0
        for k in range(3):
            put(11 + 16 * k + b, g_col[k] * basis[b])
            total = total + g_col[k] * feat(11 + 16 * k + b)
        pulled.append(total)
    g_way = sh_pull(pulled, *way)
    along = way[0] * g_way[0] + way[1] * g_way[1] + way[2] * g_way[2]
    g_off = [(g_way[a] - way[a] * along) * rlen for a in range(3)]
    put(10, g_o * part["opacity"] * (1.0 - part["opacity"]))
    a, b, c = part["conic"]
    g_xx = -(a * a * g_a + a * b * g_b + b * b * g_c)
    g_xy = -(2.0 * a * b * g_a + (a * c + b * b) * g_b + 2.0 * b * c * g_c)
    g_yy = -(b * b * g_a + b * c * g_b + c * c * g_c)
    axes, wide, turn, screen = part["axes"], part["wide"], part["turn"], part["screen"]
    for k in range(3):
        g_scale = (
            g_xx * axes[0][k] * wide[0][k]
            + g_xy * axes[0][k] * wide[1][k]
            + g_yy * axes[1][k] * wide[1][k]
        )
        put(3 + k, 2.0 * g_scale)
    g_axes = [
        [2.0 * g_xx * wide[0][k] + g_xy * wide[1][k] for k in range(3)],
        [2.0 * g_yy * wide[1][k] + g_xy * wide[0][k] for k in range(3)],
    ]
    g_screen = [
        [sum(g_axes[r][k] * turn[c][k] for k in range(3)) for c in range(3)] for r in range(2)
    ]
    gm = [
        [g_axes[0][k] * screen[0][c] + g_axes[1][k] * screen[1][c] for k in range(3)]
        for c in range(3)
    ]
    w, x, y, z = part["rotor"]
    up_xy, up_xz, up_yz = gm[0][1] + gm[1][0], gm[0][2] + gm[2][0], gm[1][2] + gm[2][1]
    un_xy, un_xz, un_yz = gm[1][0] - gm[0][1], gm[0][2] - gm[2][0], gm[2][1] - gm[1][2]
    g_rotor = [
        2.0 * (z * un_xy + y * un_xz + x * un_yz),
        2.0 * (y * up_xy + z * up_xz + w * un_yz - 2.0 * x * (gm[1][1] + gm[2][2])),
        2.0 * (x * up_xy + z * up_yz + w * un_xz - 2.0 * y * (gm[0][0] + gm[2][2])),
        2.0 * (x * up_xz + y * up_yz + w * un_xy - 2.0 * z * (gm[0][0] + gm[1][1])),
    ]
    rotor = (w, x, y, z)
    along = sum(rotor[i] * g_rotor[i] for i in range(4))
    for i in range(4):
        put(6 + i, (g_rotor[i] - rotor[i] * along) * part["rnorm"])
    rot, inv, finv, u, v = part["rot"], part["inv"], part["finv"], part["u"], part["v"]
    g_u = focal_length * g_mx - finv * sum(g_screen[0][c] * rot[2][c] for c in range(3))
    g_v = focal_length * g_my - finv * sum(g_screen[1][c] * rot[2][c] for c in range(3))
    g_f = sum(g_screen[r][c] * screen[r][c] for r in range(2) for c in range(3))
    g_in = [g_u * inv, g_v * inv, -(g_f + g_u * u + g_v * v) * inv]
    for axis in range(3):
        put(
            axis,
            g_off[axis] + rot[0][axis] * g_in[0] + rot[1][axis] * g_in[1] + rot[2][axis] * g_in[2],
        )


def split(value):
    high = value.astype(BF16)
    return high, (value - high.astype(F32)).astype(BF16)


def matmul(a, b, dims=((1,), (0,))):
    return lax.dot_general(a, b, (dims, ((), ())), preferred_element_type=F32)


def spread_features(parts, scratch, count):
    tiles = sum(part.shape[1] for part in parts) // LANES
    at = 0
    for part in parts:
        for first in range(0, part.shape[1], LANES):
            for row in range(0, count, 8):
                rows = min(8, count - row)
                scratch[pl.ds(row * tiles + at, rows, stride=tiles), :] = part[
                    row : row + rows, first : first + LANES
                ]
            at += 1
    return tiles


def render_kernel(blocks, pieces, *refs):
    tile_ids, cams = refs[0], refs[1]
    parts = refs[2 : 2 + pieces]
    place, inverse, target, rendered, packet = refs[2 + pieces : 7 + pieces]
    feats, rows, e_s, t_s, d_s, hi_s, lo_s, acc_s = refs[7 + pieces :]
    tile_count, listed = place.shape
    pixels = target.shape[1] // tile_count
    side = TILE_SIDE
    view = tile_ids[0] // (TILES_X * TILES_Y)
    cam = [cams[view, i] for i in range(12)]
    slabs = spread_features(parts, feats, parts[0].shape[0])
    projected = project_rows(lambda f: feats[f * slabs : (f + 1) * slabs, :], cam)
    for f, value in enumerate(projected):
        rows[pl.ds(f, slabs, stride=ROWS), :] = value
    zero_row = jnp.zeros((slabs, LANES), F32)
    for f in range(len(projected), ROWS):
        rows[pl.ds(f, slabs, stride=ROWS), :] = zero_row

    lists = []
    for t in range(tile_count):
        halves = []
        for first in range(0, listed, LANES):
            at = jnp.broadcast_to(place[t : t + 1, first : first + LANES], (ROWS, LANES))
            lane, slab = at & (LANES - 1), at >> 7
            found = jnp.zeros((ROWS, LANES), F32)
            for s in range(slabs):
                here = jnp.take_along_axis(
                    rows[s * ROWS : (s + 1) * ROWS, :], lane, axis=1, mode="promise_in_bounds"
                )
                found = jnp.where(slab == s, here, found)
            halves.append(found)
        lists.append(jnp.concatenate(halves, axis=1))

    row_i = lax.broadcasted_iota(jnp.int32, (listed, listed), 0)
    col_i = lax.broadcasted_iota(jnp.int32, (listed, listed), 1)
    earlier = jnp.where(row_i < col_i, 1.0, 0.0).astype(BF16)
    later = jnp.where(row_i > col_i, 1.0, 0.0).astype(BF16)
    step = lax.broadcasted_iota(jnp.int32, (side, listed), 0).astype(F32)

    setup = []
    for t in range(tile_count):
        entry = lists[t]
        within = tile_ids[t] % (TILES_X * TILES_Y)
        x_0 = ((within % TILES_X) * side).astype(F32) + 0.5
        y_0 = ((within // TILES_X) * side).astype(F32) + 0.5
        quad_a, quad_b, quad_c = -0.5 * entry[2:3], -entry[3:4], -0.5 * entry[4:5]
        opacity = entry[5:6]
        dx = (step + x_0) - entry[0:1]
        dy = (step + y_0) - entry[1:2]
        adx2 = quad_a * dx * dx
        bdy = quad_b * dy
        cdy2 = quad_c * dy * dy
        setup.append((entry, quad_a, quad_b, quad_c, opacity, dx, dy, adx2, bdy, cdy2))
        for row in range(side):
            at = slice(row * side, (row + 1) * side)
            power = adx2 + dx * bdy[row : row + 1] + cdy2[row : row + 1]
            bell = jnp.exp(power)
            e_s[t, at, :] = bell
            hi_s[t, at, :], lo_s[t, at, :] = split(jnp.log(1.0 - opacity * bell))

    for t in range(tile_count):
        t_s[t] = matmul(hi_s[t], earlier) + matmul(lo_s[t], earlier)

    errors = []
    for t in range(tile_count):
        entry, opacity = setup[t][0], setup[t][4]
        for row in range(side):
            at = slice(row * side, (row + 1) * side)
            passed = jnp.exp(t_s[t, at, :])
            t_s[t, at, :] = passed
            hi_s[t, at, :], lo_s[t, at, :] = split(opacity * e_s[t, at, :] * passed)
        colours = entry[6:9]
        c_hi, c_lo = split(colours)
        both = (((1,), (1,)))
        image = (
            matmul(c_hi, hi_s[t], both) + matmul(c_lo, hi_s[t], both) + matmul(c_hi, lo_s[t], both)
        )
        here = slice(t * pixels, (t + 1) * pixels)
        rendered[:, here] = image
        error = image - target[:, here]
        g_hi, g_lo = split(error)
        errors.append((g_hi, g_lo))
        first = ((0,), (0,))
        d_s[t] = matmul(g_hi, c_hi, first) + matmul(g_lo, c_hi, first) + matmul(g_hi, c_lo, first)
        g_colours = matmul(g_hi, hi_s[t]) + matmul(g_lo, hi_s[t]) + matmul(g_hi, lo_s[t])
        acc_s[t, 6:9, :] = g_colours

    for t in range(tile_count):
        opacity = setup[t][4]
        for row in range(side):
            at = slice(row * side, (row + 1) * side)
            pushed = t_s[t, at, :] * d_s[t, at, :]
            t_s[t, at, :] = pushed
            hi_s[t, at, :], lo_s[t, at, :] = split(opacity * e_s[t, at, :] * pushed)
        d_s[t] = matmul(hi_s[t], later) + matmul(lo_s[t], later)

    for t in range(tile_count):
        entry, quad_a, quad_b, quad_c, opacity, dx, dy, adx2, bdy, cdy2 = setup[t]
        r_0 = r_1 = r_2 = None
        for row in range(side):
            at = slice(row * side, (row + 1) * side)
            bell = e_s[t, at, :]
            flow = bell * (t_s[t, at, :] - d_s[t, at, :] / (1.0 - opacity * bell))
            one = flow * dy[row : row + 1]
            two = one * dy[row : row + 1]
            r_0 = flow if r_0 is None else r_0 + flow
            r_1 = one if r_1 is None else r_1 + one
            r_2 = two if r_2 is None else r_2 + two
        rdx = r_0 * dx
        m_00 = jnp.sum(r_0, axis=0, keepdims=True)
        m_10 = jnp.sum(rdx, axis=0, keepdims=True)
        m_20 = jnp.sum(rdx * dx, axis=0, keepdims=True)
        m_01 = jnp.sum(r_1, axis=0, keepdims=True)
        m_11 = jnp.sum(r_1 * dx, axis=0, keepdims=True)
        m_02 = jnp.sum(r_2, axis=0, keepdims=True)
        acc_s[t, 0:1, :] = -opacity * (2.0 * quad_a * m_10 + quad_b * m_01)
        acc_s[t, 1:2, :] = -opacity * (2.0 * quad_c * m_01 + quad_b * m_10)
        acc_s[t, 2:3, :] = -0.5 * opacity * m_20
        acc_s[t, 3:4, :] = -opacity * m_11
        acc_s[t, 4:5, :] = -0.5 * opacity * m_02
        acc_s[t, 5:6, :] = m_00
        acc_s[t, 9:16, :] = jnp.zeros((7, listed), F32)

    share = view.astype(F32) * (tile_count / BLOCK_TILES)
    row_of = lax.broadcasted_iota(jnp.int32, (ROWS, LANES), 0)
    chunk = packet.shape[2]
    for s in range(slabs):
        total = jnp.zeros((ROWS, LANES), F32)
        for t in range(tile_count):
            at = jnp.broadcast_to(inverse[t : t + 1, s * LANES : (s + 1) * LANES], (ROWS, LANES))
            lane, half = at & (LANES - 1), at >> 7
            for h in range(listed // LANES):
                here = jnp.take_along_axis(
                    acc_s[t, :, h * LANES : (h + 1) * LANES], lane, axis=1, mode="promise_in_bounds"
                )
                total = total + jnp.where(half == h, here, 0.0)
        mine = jnp.broadcast_to(
            jnp.where(inverse[tile_count : tile_count + 1, s * LANES : (s + 1) * LANES] > 0, share, 0.0),
            (ROWS, LANES),
        )
        total = jnp.where(row_of == 9, mine, total)
        packet[s * LANES // chunk, :, s * LANES % chunk : s * LANES % chunk + LANES] = total


def update_kernel(cams, params, adam_m, adam_v, packet, new_params, new_m, new_v, feats, rows, grads):
    features, width = params.shape
    slabs = spread_features([params], feats, features)
    chunk = packet.shape[2]
    for s in range(slabs):
        rows[pl.ds(s, ROWS, stride=slabs), :] = packet[
            s * LANES // chunk, :, s * LANES % chunk : s * LANES % chunk + LANES
        ]
    pulled = [rows[f * slabs : (f + 1) * slabs, :] for f in range(10)]
    view = pulled[9]
    cam = []
    for i in range(12):
        value = jnp.full((slabs, LANES), cams[0, i], F32)
        for v in range(1, cams.shape[0]):
            value = jnp.where(view == float(v), cams[v, i], value)
        cam.append(value)

    def put(f, value):
        grads[f * slabs : (f + 1) * slabs, :] = value

    project_pull(lambda f: feats[f * slabs : (f + 1) * slabs, :], cam, pulled[:9], put)
    rate = learn_rate / (1.0 - beta_one**adam_steps)
    unbias = 1.0 / (1.0 - beta_two**adam_steps)
    for s in range(slabs):
        for row in range(0, features, 8):
            count = min(8, features - row)
            at = (slice(row, row + count), slice(s * LANES, (s + 1) * LANES))
            grad = grads[pl.ds(row * slabs + s, count, stride=slabs), :]
            moment = beta_one * adam_m[at] + (1.0 - beta_one) * grad
            second = beta_two * adam_v[at] + (1.0 - beta_two) * grad * grad
            new_m[at] = moment
            new_v[at] = second
            new_params[at] = params[at] - rate * moment / (jnp.sqrt(second * unbias) + adam_eps)


def vmem():
    return pl.BlockSpec(memory_space=pltpu.VMEM)


def smem():
    return pl.BlockSpec(memory_space=pltpu.SMEM)


def render(tile_ids, cameras, parts, place, inverse, target, chunks):
    width = sum(part.shape[1] for part in parts)
    features = parts[0].shape[0]
    slabs = width // LANES
    tile_count, listed = place.shape
    pixels = target.shape[1] // tile_count
    square = (tile_count, pixels, listed)
    return pl.pallas_call(
        functools.partial(render_kernel, 1, len(parts)),
        out_shape=(
            jax.ShapeDtypeStruct(target.shape, F32),
            jax.ShapeDtypeStruct((chunks, ROWS, width // chunks), F32),
        ),
        in_specs=[smem(), smem()] + [vmem()] * (len(parts) + 3),
        out_specs=(vmem(), vmem()),
        scratch_shapes=[
            pltpu.VMEM((features * slabs, LANES), F32),
            pltpu.VMEM((ROWS * slabs, LANES), F32),
            pltpu.VMEM(square, F32),
            pltpu.VMEM(square, F32),
            pltpu.VMEM(square, F32),
            pltpu.VMEM(square, BF16),
            pltpu.VMEM(square, BF16),
            pltpu.VMEM((tile_count, ROWS, listed), F32),
        ],
        compiler_params=pltpu.CompilerParams(vmem_limit_bytes=32 * 1024 * 1024),
        name="render",
    )(tile_ids, cameras, *parts, place, inverse, target)


def update(cameras, params, adam_m, adam_v, packet):
    features, width = params.shape
    slabs = width // LANES
    shape = jax.ShapeDtypeStruct(params.shape, F32)
    return pl.pallas_call(
        update_kernel,
        out_shape=(shape, shape, shape),
        in_specs=[smem()] + [vmem()] * 4,
        out_specs=(vmem(), vmem(), vmem()),
        scratch_shapes=[
            pltpu.VMEM((features * slabs, LANES), F32),
            pltpu.VMEM((ROWS * slabs, LANES), F32),
            pltpu.VMEM((features * slabs, LANES), F32),
        ],
        compiler_params=pltpu.CompilerParams(vmem_limit_bytes=32 * 1024 * 1024),
        name="update",
    )(cameras, params, adam_m, adam_v, packet)


def local(params, adam_m, adam_v, cameras, target, tile_ids, hit_shard, hit_local):
    width = params.shape[1]
    tile_count, listed = hit_local.shape
    shards = lax.axis_size("gs")
    along = lax.axis_size("tile")
    chunk = width // shards
    group = lax.axis_index("gs")
    aligned = chunk % LANES == 0

    place = (hit_shard[:, :, 0] ^ group) * chunk + (hit_local - group * chunk)
    column = jnp.arange(width, dtype=jnp.int32)
    order = jnp.arange(listed, dtype=jnp.int32)
    named = place[:, :, None] == column[None, None, :]
    inverse = jnp.max(jnp.where(named, order[None, :, None], -1), axis=1)
    blocks = along * tile_count // BLOCK_TILES
    my_block = lax.axis_index("tile") * tile_count // BLOCK_TILES
    mine = (column % chunk) // (chunk // blocks) == my_block
    inverse = jnp.concatenate([inverse, mine.astype(jnp.int32)[None]], axis=0)

    parts = []
    for d in range(shards):
        piece = lax.dynamic_slice_in_dim(params, (group ^ d) * chunk, chunk, axis=1)
        if d > 0:
            piece = lax.ppermute(piece, "gs", [(k, k ^ d) for k in range(shards)])
        parts.append(piece)
    if not aligned:
        parts = [jnp.concatenate(parts, axis=1)]
    rendered, packet = render(
        tile_ids, cameras, parts, place, inverse, target, shards if aligned else 1
    )
    if not aligned:
        packet = packet.reshape(ROWS, shards, chunk).transpose(1, 0, 2)
    packet = packet[jnp.arange(shards) ^ group]
    packet = lax.all_to_all(packet, "gs", 0, 0)
    packet = lax.psum(packet, "tile")
    if not aligned:
        packet = packet.transpose(1, 0, 2).reshape(1, ROWS, width)
    new_params, new_m, new_v = update(cameras, params, adam_m, adam_v, packet)
    return (rendered, new_params, new_m, new_v)


def solution(mesh):
    return jax.shard_map(
        local,
        mesh=mesh,
        in_specs=(
            P(None, ("groups", "gs")),
            P(None, ("groups", "gs")),
            P(None, ("groups", "gs")),
            P("groups", None),
            P(None, ("groups", "gs", "tile")),
            P(("groups", "gs", "tile")),
            P(("groups", "gs", "tile"), None, None),
            P(("groups", "gs", "tile"), None),
        ),
        out_specs=(
            P(None, ("groups", "gs", "tile")),
            P(None, ("groups", "gs")),
            P(None, ("groups", "gs")),
            P(None, ("groups", "gs")),
        ),
        check_vma=False,
    )
```

```python
import functools

import jax
import jax.numpy as jnp
from jax import lax
from jax.experimental import pallas as pl
from jax.experimental.pallas import tpu as pltpu
from jax.sharding import PartitionSpec as P

TILES_X = 120
TILES_Y = 68
TILE_SIDE = 16
BLOCK_TILES = 8
LANES = 128
ROWS = 16
F32 = jnp.float32
BF16 = jnp.bfloat16

focal_length = 1000.0
center_x = 960.0
center_y = 540.0
dilation = 0.3
beta_one = 0.9
beta_two = 0.999
learn_rate = 0.01
adam_eps = 1e-08
adam_steps = 100.0
sh_const = (
    0.28209479177387814,
    0.4886025119029199,
    1.0925484305920792,
    0.31539156525252005,
    0.5462742152960396,
    0.5900435899266435,
    2.890611442640554,
    0.4570457994644658,
    0.3731763325901154,
    1.445305721320277,
)


def sh_basis(x, y, z):
    s = sh_const
    xx, yy, zz = x * x, y * y, z * z
    return [
        None,
        -s[1] * y,
        s[1] * z,
        -s[1] * x,
        s[2] * (x * y),
        -s[2] * (y * z),
        s[3] * (2.0 * zz - xx - yy),
        -s[2] * (x * z),
        s[4] * (xx - yy),
        -s[5] * y * (3.0 * xx - yy),
        s[6] * (x * y) * z,
        -s[7] * y * (4.0 * zz - xx - yy),
        s[8] * z * (2.0 * zz - 3.0 * xx - 3.0 * yy),
        -s[7] * x * (4.0 * zz - xx - yy),
        s[9] * z * (xx - yy),
        -s[5] * x * (xx - 3.0 * yy),
    ]


def sh_pull(h, x, y, z):
    s = sh_const
    xx, yy, zz = x * x, y * y, z * z
    xy, xz, yz = x * y, x * z, y * z
    diff = xx - yy
    ring = 4.0 * zz - xx - yy
    g_x = (
        -s[1] * h[3]
        + s[2] * (h[4] * y - h[7] * z)
        - (2.0 * s[3]) * h[6] * x
        + (2.0 * s[4]) * h[8] * x
        - (6.0 * s[5]) * h[9] * xy
        + s[6] * h[10] * yz
        + (2.0 * s[7]) * h[11] * xy
        - (6.0 * s[8]) * h[12] * xz
        - s[7] * h[13] * (ring - 2.0 * xx)
        + (2.0 * s[9]) * h[14] * xz
        - (3.0 * s[5]) * h[15] * diff
    )
    g_y = (
        -s[1] * h[1]
        + s[2] * (h[4] * x - h[5] * z)
        - (2.0 * s[3]) * h[6] * y
        - (2.0 * s[4]) * h[8] * y
        - (3.0 * s[5]) * h[9] * diff
        + s[6] * h[10] * xz
        - s[7] * h[11] * (ring - 2.0 * yy)
        - (6.0 * s[8]) * h[12] * yz
        + (2.0 * s[7]) * h[13] * xy
        - (2.0 * s[9]) * h[14] * yz
        + (6.0 * s[5]) * h[15] * xy
    )
    g_z = (
        s[1] * h[2]
        - s[2] * (h[5] * y + h[7] * x)
        + (4.0 * s[3]) * h[6] * z
        + s[6] * h[10] * xy
        - (8.0 * s[7]) * (h[11] * yz + h[13] * xz)
        + s[8] * h[12] * (6.0 * zz - 3.0 * xx - 3.0 * yy)
        + s[9] * h[14] * diff
    )
    return g_x, g_y, g_z


def project_parts(feat, cam):
    rot = [[cam[3 * r + c] for c in range(3)] for r in range(3)]
    off = [feat(a) - cam[9 + a] for a in range(3)]
    in_cam = [rot[r][0] * off[0] + rot[r][1] * off[1] + rot[r][2] * off[2] for r in range(3)]
    inv = 1.0 / in_cam[2]
    u = in_cam[0] * inv
    v = in_cam[1] * inv
    finv = focal_length * inv
    scale = [jnp.exp(2.0 * feat(3 + a)) for a in range(3)]
    quat = [feat(6 + a) for a in range(4)]
    rnorm = lax.rsqrt(quat[0] * quat[0] + quat[1] * quat[1] + quat[2] * quat[2] + quat[3] * quat[3])
    w, x, y, z = [q * rnorm for q in quat]
    turn = [
        [1.0 - 2.0 * (y * y + z * z), 2.0 * (x * y - w * z), 2.0 * (x * z + w * y)],
        [2.0 * (x * y + w * z), 1.0 - 2.0 * (x * x + z * z), 2.0 * (y * z - w * x)],
        [2.0 * (x * z - w * y), 2.0 * (y * z + w * x), 1.0 - 2.0 * (x * x + y * y)],
    ]
    screen = [
        [finv * (rot[0][c] - u * rot[2][c]) for c in range(3)],
        [finv * (rot[1][c] - v * rot[2][c]) for c in range(3)],
    ]
    axes = [
        [sum(screen[r][c] * turn[c][k] for c in range(3)) for k in range(3)] for r in range(2)
    ]
    wide = [[axes[r][k] * scale[k] for k in range(3)] for r in range(2)]
    cov_xx = sum(wide[0][k] * axes[0][k] for k in range(3)) + dilation
    cov_xy = sum(wide[0][k] * axes[1][k] for k in range(3))
    cov_yy = sum(wide[1][k] * axes[1][k] for k in range(3)) + dilation
    rdet = 1.0 / (cov_xx * cov_yy - cov_xy * cov_xy)
    conic = (cov_yy * rdet, -cov_xy * rdet, cov_xx * rdet)
    opacity = 1.0 / (1.0 + jnp.exp(-feat(10)))
    rlen = lax.rsqrt(off[0] * off[0] + off[1] * off[1] + off[2] * off[2])
    way = [off[a] * rlen for a in range(3)]
    return dict(
        rot=rot, inv=inv, u=u, v=v, finv=finv, scale=scale, rnorm=rnorm, rotor=(w, x, y, z), turn=turn,
        screen=screen, axes=axes, wide=wide, conic=conic, opacity=opacity, rlen=rlen, way=way,
    )


def project_rows(feat, cam):
    part = project_parts(feat, cam)
    basis = sh_basis(*part["way"])
    colours = []
    for k in range(3):
        total = 0.5 + sh_const[0] * feat(11 + 16 * k)
        for b in range(1, 16):
            total = total + feat(11 + 16 * k + b) * basis[b]
        colours.append(total)
    mean_x = focal_length * part["u"] + center_x
    mean_y = focal_length * part["v"] + center_y
    return [mean_x, mean_y, *part["conic"], part["opacity"], *colours]


def project_pull(feat, cam, grads, put):
    part = project_parts(feat, cam)
    g_mx, g_my, g_a, g_b, g_c, g_o = grads[:6]
    g_col = grads[6:9]
    way, rlen = part["way"], part["rlen"]
    basis = sh_basis(*way)
    pulled = [None]
    for k in range(3):
        put(11 + 16 * k, sh_const[0] * g_col[k])
    for b in range(1, 16):
        total = 0.0
        for k in range(3):
            put(11 + 16 * k + b, g_col[k] * basis[b])
            total = total + g_col[k] * feat(11 + 16 * k + b)
        pulled.append(total)
    g_way = sh_pull(pulled, *way)
    along = way[0] * g_way[0] + way[1] * g_way[1] + way[2] * g_way[2]
    g_off = [(g_way[a] - way[a] * along) * rlen for a in range(3)]
    put(10, g_o * part["opacity"] * (1.0 - part["opacity"]))
    a, b, c = part["conic"]
    g_xx = -(a * a * g_a + a * b * g_b + b * b * g_c)
    g_xy = -(2.0 * a * b * g_a + (a * c + b * b) * g_b + 2.0 * b * c * g_c)
    g_yy = -(b * b * g_a + b * c * g_b + c * c * g_c)
    axes, wide, turn, screen = part["axes"], part["wide"], part["turn"], part["screen"]
    for k in range(3):
        g_scale = (
            g_xx * axes[0][k] * wide[0][k]
            + g_xy * axes[0][k] * wide[1][k]
            + g_yy * axes[1][k] * wide[1][k]
        )
        put(3 + k, 2.0 * g_scale)
    g_axes = [
        [2.0 * g_xx * wide[0][k] + g_xy * wide[1][k] for k in range(3)],
        [2.0 * g_yy * wide[1][k] + g_xy * wide[0][k] for k in range(3)],
    ]
    g_screen = [
        [sum(g_axes[r][k] * turn[c][k] for k in range(3)) for c in range(3)] for r in range(2)
    ]
    gm = [
        [g_axes[0][k] * screen[0][c] + g_axes[1][k] * screen[1][c] for k in range(3)]
        for c in range(3)
    ]
    w, x, y, z = part["rotor"]
    up_xy, up_xz, up_yz = gm[0][1] + gm[1][0], gm[0][2] + gm[2][0], gm[1][2] + gm[2][1]
    un_xy, un_xz, un_yz = gm[1][0] - gm[0][1], gm[0][2] - gm[2][0], gm[2][1] - gm[1][2]
    g_rotor = [
        2.0 * (z * un_xy + y * un_xz + x * un_yz),
        2.0 * (y * up_xy + z * up_xz + w * un_yz - 2.0 * x * (gm[1][1] + gm[2][2])),
        2.0 * (x * up_xy + z * up_yz + w * un_xz - 2.0 * y * (gm[0][0] + gm[2][2])),
        2.0 * (x * up_xz + y * up_yz + w * un_xy - 2.0 * z * (gm[0][0] + gm[1][1])),
    ]
    rotor = (w, x, y, z)
    along = sum(rotor[i] * g_rotor[i] for i in range(4))
    for i in range(4):
        put(6 + i, (g_rotor[i] - rotor[i] * along) * part["rnorm"])
    rot, inv, finv, u, v = part["rot"], part["inv"], part["finv"], part["u"], part["v"]
    g_u = focal_length * g_mx - finv * sum(g_screen[0][c] * rot[2][c] for c in range(3))
    g_v = focal_length * g_my - finv * sum(g_screen[1][c] * rot[2][c] for c in range(3))
    g_f = sum(g_screen[r][c] * screen[r][c] for r in range(2) for c in range(3))
    g_in = [g_u * inv, g_v * inv, -(g_f + g_u * u + g_v * v) * inv]
    for axis in range(3):
        put(
            axis,
            g_off[axis] + rot[0][axis] * g_in[0] + rot[1][axis] * g_in[1] + rot[2][axis] * g_in[2],
        )


def split(value):
    high = value.astype(BF16)
    return high, (value - high.astype(F32)).astype(BF16)


def matmul(a, b, dims=((1,), (0,))):
    return lax.dot_general(a, b, (dims, ((), ())), preferred_element_type=F32)


def spread_features(parts, scratch, count):
    tiles = sum(part.shape[1] for part in parts) // LANES
    at = 0
    for part in parts:
        for first in range(0, part.shape[1], LANES):
            for row in range(0, count, 8):
                rows = min(8, count - row)
                scratch[pl.ds(row * tiles + at, rows, stride=tiles), :] = part[
                    row : row + rows, first : first + LANES
                ]
            at += 1
    return tiles


def render_kernel(pieces, groups, blocks, *refs):
    tile_ids, cams, where = refs[:3]
    parts = refs[3 : 3 + pieces]
    infos = refs[3 + pieces : 3 + pieces + groups]
    inverse, rendered = refs[3 + pieces + groups : 5 + pieces + groups]
    rest = refs[5 + pieces + groups :]
    packets = rest[: len(rest) - 9]
    feats, rows, e_s, t_s, d_s, hi_s, lo_s, acc_s, info_s = rest[len(rest) - 9 :]
    tile_count, listed = e_s.shape[0], e_s.shape[2]
    pixels = e_s.shape[1]
    side = TILE_SIDE
    view = tile_ids[0] // (TILES_X * TILES_Y)
    cam = [cams[view, i] for i in range(12)]
    slabs = spread_features(parts, feats, parts[0].shape[0])
    projected = project_rows(lambda f: feats[f * slabs : (f + 1) * slabs, :], cam)
    for f, value in enumerate(projected):
        rows[pl.ds(f, slabs, stride=ROWS), :] = value
    zero_row = jnp.zeros((slabs, LANES), F32)
    for f in range(len(projected), ROWS):
        rows[pl.ds(f, slabs, stride=ROWS), :] = zero_row
    for g in range(groups):
        info_s[g] = infos[g][...]

    row_i = lax.broadcasted_iota(jnp.int32, (listed, listed), 0)
    col_i = lax.broadcasted_iota(jnp.int32, (listed, listed), 1)
    earlier = jnp.where(row_i < col_i, 1.0, 0.0).astype(BF16)
    later = jnp.where(row_i > col_i, 1.0, 0.0).astype(BF16)
    step = lax.broadcasted_iota(jnp.int32, (side, listed), 0).astype(F32)
    within = tile_ids[0] % (TILES_X * TILES_Y)
    first_row = (within // TILES_X) // 2 * 2
    first_col = (within % TILES_X) // 4 * 4
    me = where[0]

    def one_group(g, carry):
        lists = []
        for t in range(tile_count):
            halves = []
            for first in range(t * listed, (t + 1) * listed, LANES):
                at = info_s[g, 3:4, first : first + LANES].astype(jnp.int32)
                at = jnp.broadcast_to(at, (ROWS, LANES))
                lane, slab = at & (LANES - 1), at >> 7
                found = jnp.zeros((ROWS, LANES), F32)
                for s in range(slabs):
                    here = jnp.take_along_axis(
                        rows[s * ROWS : (s + 1) * ROWS, :], lane, axis=1, mode="promise_in_bounds"
                    )
                    found = jnp.where(slab == s, here, found)
                halves.append(found)
            lists.append(jnp.concatenate(halves, axis=1))

        setup = []
        for t in range(tile_count):
            entry = lists[t]
            slot = (me ^ g) * tile_count + t
            x_0 = ((first_col + slot % 4) * side).astype(F32) + 0.5
            y_0 = ((first_row + slot // 4) * side).astype(F32) + 0.5
            quad_a, quad_b, quad_c = -0.5 * entry[2:3], -entry[3:4], -0.5 * entry[4:5]
            opacity = entry[5:6]
            dx = (step + x_0) - entry[0:1]
            dy = (step + y_0) - entry[1:2]
            adx2 = quad_a * dx * dx
            bdy = quad_b * dy
            cdy2 = quad_c * dy * dy
            setup.append((entry, quad_a, quad_b, quad_c, opacity, dx, dy))
            for row in range(side):
                at = slice(row * side, (row + 1) * side)
                power = adx2 + dx * bdy[row : row + 1] + cdy2[row : row + 1]
                bell = jnp.exp(power)
                e_s[t, at, :] = bell
                hi_s[t, at, :], lo_s[t, at, :] = split(jnp.log(1.0 - opacity * bell))

        for t in range(tile_count):
            t_s[t] = matmul(hi_s[t], earlier) + matmul(lo_s[t], earlier)

        for t in range(tile_count):
            entry, opacity = setup[t][0], setup[t][4]
            for row in range(side):
                at = slice(row * side, (row + 1) * side)
                passed = jnp.exp(t_s[t, at, :])
                t_s[t, at, :] = passed
                hi_s[t, at, :], lo_s[t, at, :] = split(opacity * e_s[t, at, :] * passed)
            c_hi, c_lo = split(entry[6:9])
            both = ((1,), (1,))
            image = (
                matmul(c_hi, hi_s[t], both)
                + matmul(c_lo, hi_s[t], both)
                + matmul(c_hi, lo_s[t], both)
            )
            here = slice(t * pixels, (t + 1) * pixels)

            @pl.when(g == 0)
            def _():
                rendered[:, here] = image

            error = image - info_s[g, 0:3, here]
            g_hi, g_lo = split(error)
            first = ((0,), (0,))
            d_s[t] = (
                matmul(g_hi, c_hi, first) + matmul(g_lo, c_hi, first) + matmul(g_hi, c_lo, first)
            )
            g_colours = matmul(g_hi, hi_s[t]) + matmul(g_lo, hi_s[t]) + matmul(g_hi, lo_s[t])
            acc_s[g, t, 6:9, :] = g_colours

        for t in range(tile_count):
            opacity = setup[t][4]
            for row in range(side):
                at = slice(row * side, (row + 1) * side)
                pushed = t_s[t, at, :] * d_s[t, at, :]
                t_s[t, at, :] = pushed
                hi_s[t, at, :], lo_s[t, at, :] = split(opacity * e_s[t, at, :] * pushed)
            d_s[t] = matmul(hi_s[t], later) + matmul(lo_s[t], later)

        for t in range(tile_count):
            entry, quad_a, quad_b, quad_c, opacity, dx, dy = setup[t]
            r_0 = r_1 = r_2 = None
            for row in range(side):
                at = slice(row * side, (row + 1) * side)
                bell = e_s[t, at, :]
                flow = bell * (t_s[t, at, :] - d_s[t, at, :] / (1.0 - opacity * bell))
                one = flow * dy[row : row + 1]
                two = one * dy[row : row + 1]
                r_0 = flow if r_0 is None else r_0 + flow
                r_1 = one if r_1 is None else r_1 + one
                r_2 = two if r_2 is None else r_2 + two
            rdx = r_0 * dx
            m_00 = jnp.sum(r_0, axis=0, keepdims=True)
            m_10 = jnp.sum(rdx, axis=0, keepdims=True)
            m_20 = jnp.sum(rdx * dx, axis=0, keepdims=True)
            m_01 = jnp.sum(r_1, axis=0, keepdims=True)
            m_11 = jnp.sum(r_1 * dx, axis=0, keepdims=True)
            m_02 = jnp.sum(r_2, axis=0, keepdims=True)
            acc_s[g, t, 0:1, :] = -opacity * (2.0 * quad_a * m_10 + quad_b * m_01)
            acc_s[g, t, 1:2, :] = -opacity * (2.0 * quad_c * m_01 + quad_b * m_10)
            acc_s[g, t, 2:3, :] = -0.5 * opacity * m_20
            acc_s[g, t, 3:4, :] = -opacity * m_11
            acc_s[g, t, 4:5, :] = -0.5 * opacity * m_02
            acc_s[g, t, 5:6, :] = m_00
            acc_s[g, t, 9:16, :] = jnp.zeros((7, listed), F32)
        return carry

    lax.fori_loop(0, groups, one_group, 0)

    share = view.astype(F32)
    row_of = lax.broadcasted_iota(jnp.int32, (ROWS, LANES), 0)
    lane_of = lax.broadcasted_iota(jnp.int32, (ROWS, LANES), 1)
    chunk = packets[0].shape[1]
    for s in range(slabs):
        totals = []
        for g in range(groups):
            total = jnp.zeros((ROWS, LANES), F32)
            for t in range(tile_count):
                at = inverse[g * tile_count + t : g * tile_count + t + 1, s * LANES : (s + 1) * LANES]
                at = jnp.broadcast_to(at, (ROWS, LANES))
                lane, half = at & (LANES - 1), at >> 7
                for h in range(listed // LANES):
                    here = jnp.take_along_axis(
                        acc_s[g, t, :, h * LANES : (h + 1) * LANES],
                        lane,
                        axis=1,
                        mode="promise_in_bounds",
                    )
                    total = total + jnp.where(half == h, here, 0.0)
            totals.append(total)
        while len(totals) > 1:
            totals = [totals[k] + totals[k + 1] for k in range(0, len(totals), 2)]
        total = totals[0]
        if blocks == 1:
            mine = share
        else:
            column = s * LANES + lane_of
            mine = jnp.where(column % where[2] // (where[2] // blocks) == where[1], share, 0.0)
        total = jnp.where(row_of == 9, mine, total)
        packets[s * LANES // chunk][:, s * LANES % chunk : s * LANES % chunk + LANES] = total


def update_kernel(pieces, where, cams, params, adam_m, adam_v, *refs):
    packets = refs[:pieces]
    new_params, new_m, new_v, feats, rows, grads = refs[pieces:]
    features, width = params.shape
    slabs = spread_features([params], feats, features)
    chunk = packets[0].shape[1]
    for d in range(pieces):
        for h in range(chunk // LANES):
            slab = (where[0] ^ d) * (chunk // LANES) + h
            rows[pl.ds(slab, ROWS, stride=slabs), :] = packets[d][:, h * LANES : (h + 1) * LANES]
    pulled = [rows[f * slabs : (f + 1) * slabs, :] for f in range(10)]
    view = pulled[9]
    cam = []
    for i in range(12):
        value = jnp.full((slabs, LANES), cams[0, i], F32)
        for v in range(1, cams.shape[0]):
            value = jnp.where(view == float(v), cams[v, i], value)
        cam.append(value)

    def put(f, value):
        grads[f * slabs : (f + 1) * slabs, :] = value

    project_pull(lambda f: feats[f * slabs : (f + 1) * slabs, :], cam, pulled[:9], put)
    rate = learn_rate / (1.0 - beta_one**adam_steps)
    unbias = 1.0 / (1.0 - beta_two**adam_steps)
    for s in range(slabs):
        for row in range(0, features, 8):
            count = min(8, features - row)
            at = (slice(row, row + count), slice(s * LANES, (s + 1) * LANES))
            grad = grads[pl.ds(row * slabs + s, count, stride=slabs), :]
            moment = beta_one * adam_m[at] + (1.0 - beta_one) * grad
            second = beta_two * adam_v[at] + (1.0 - beta_two) * grad * grad
            new_m[at] = moment
            new_v[at] = second
            new_params[at] = params[at] - rate * moment / (jnp.sqrt(second * unbias) + adam_eps)


def vmem():
    return pl.BlockSpec(memory_space=pltpu.VMEM)


def smem():
    return pl.BlockSpec(memory_space=pltpu.SMEM)


def render(tile_ids, cameras, where, parts, infos, inverse, tile_count, blocks):
    width = sum(part.shape[1] for part in parts)
    features = parts[0].shape[0]
    slabs = width // LANES
    pixels = listed = infos[0].shape[1] // tile_count
    square = (tile_count, pixels, listed)
    groups = len(infos)
    packet = jax.ShapeDtypeStruct((ROWS, parts[0].shape[1]), F32)
    out = pl.pallas_call(
        functools.partial(render_kernel, len(parts), groups, blocks),
        out_shape=(jax.ShapeDtypeStruct((3, tile_count * pixels), F32),) + (packet,) * len(parts),
        in_specs=[smem()] * 3 + [vmem()] * (len(parts) + groups + 1),
        out_specs=(vmem(),) * (1 + len(parts)),
        scratch_shapes=[
            pltpu.VMEM((features * slabs, LANES), F32),
            pltpu.VMEM((ROWS * slabs, LANES), F32),
            pltpu.VMEM(square, F32),
            pltpu.VMEM(square, F32),
            pltpu.VMEM(square, F32),
            pltpu.VMEM(square, BF16),
            pltpu.VMEM(square, BF16),
            pltpu.VMEM((groups, tile_count, ROWS, listed), F32),
            pltpu.VMEM((groups,) + infos[0].shape, F32),
        ],
        compiler_params=pltpu.CompilerParams(vmem_limit_bytes=32 * 1024 * 1024),
        name="render",
    )(tile_ids, cameras, where, *parts, *infos, inverse)
    return out[0], list(out[1:])


def update(where, cameras, params, adam_m, adam_v, packets):
    features, width = params.shape
    slabs = width // LANES
    shape = jax.ShapeDtypeStruct(params.shape, F32)
    return pl.pallas_call(
        functools.partial(update_kernel, len(packets)),
        out_shape=(shape, shape, shape),
        in_specs=[smem()] * 2 + [vmem()] * (3 + len(packets)),
        out_specs=(vmem(), vmem(), vmem()),
        scratch_shapes=[
            pltpu.VMEM((features * slabs, LANES), F32),
            pltpu.VMEM((ROWS * slabs, LANES), F32),
            pltpu.VMEM((features * slabs, LANES), F32),
        ],
        compiler_params=pltpu.CompilerParams(vmem_limit_bytes=32 * 1024 * 1024),
        name="update",
    )(where, cameras, params, adam_m, adam_v, *packets)


def swap(value, axis, d):
    if d == 0:
        return value
    return lax.ppermute(value, axis, [(k, k ^ d) for k in range(lax.axis_size(axis))])


def local(params, adam_m, adam_v, cameras, target, tile_ids, hit_shard, hit_local):
    width = params.shape[1]
    tile_count, listed = hit_local.shape
    shards = lax.axis_size("gs")
    along = lax.axis_size("tile")
    chunk = width // shards
    group = lax.axis_index("gs")
    seat = lax.axis_index("tile")
    aligned = chunk % LANES == 0
    team = BLOCK_TILES // tile_count
    blocks = along // team

    place = (hit_shard[:, :, 0] ^ group) * chunk + (hit_local - group * chunk)
    info = jnp.concatenate([target, place.reshape(1, -1).astype(F32)], axis=0)
    infos = [swap(info, "tile", d) for d in range(team)]
    parts = [
        swap(lax.dynamic_slice_in_dim(params, (group ^ d) * chunk, chunk, axis=1), "gs", d)
        for d in range(shards)
    ]
    column = jnp.arange(width, dtype=jnp.int32).astype(F32)
    order = jnp.arange(listed, dtype=jnp.int32)
    places = jnp.concatenate([each[3].reshape(tile_count, listed) for each in infos], axis=0)
    named = places[:, :, None] == column[None, None, :]
    inverse = jnp.max(jnp.where(named, order[None, :, None], -1), axis=1)

    if not aligned:
        parts = [jnp.concatenate(parts, axis=1)]
    where = jnp.stack([seat % team, seat // team, jnp.int32(chunk)]).astype(jnp.int32)
    rendered, packets = render(
        tile_ids, cameras, where, parts, infos, inverse, tile_count, blocks
    )
    if not aligned:
        packets = [packets[0][:, d * chunk : (d + 1) * chunk] for d in range(shards)]
    packets = [swap(packets[d], "gs", d) for d in range(shards)]
    if blocks > 1:
        packets = [block_sum(packet, along, team) for packet in packets]
    if aligned:
        own = group
    else:
        packets = [jnp.stack(packets)[jnp.arange(shards) ^ group].transpose(1, 0, 2).reshape(ROWS, -1)]
        own = jnp.int32(0)
    new_params, new_m, new_v = update(
        own.reshape(1), cameras, params, adam_m, adam_v, packets
    )
    return (rendered, new_params, new_m, new_v)


def block_sum(packet, along, team):
    step = team
    while step < along:
        packet = packet + swap(packet, "tile", step)
        step *= 2
    return packet


def solution(mesh):
    return jax.shard_map(
        local,
        mesh=mesh,
        in_specs=(
            P(None, ("groups", "gs")),
            P(None, ("groups", "gs")),
            P(None, ("groups", "gs")),
            P("groups", None),
            P(None, ("groups", "gs", "tile")),
            P(("groups", "gs", "tile")),
            P(("groups", "gs", "tile"), None, None),
            P(("groups", "gs", "tile"), None),
        ),
        out_specs=(
            P(None, ("groups", "gs", "tile")),
            P(None, ("groups", "gs")),
            P(None, ("groups", "gs")),
            P(None, ("groups", "gs")),
        ),
        check_vma=False,
    )
```

```python
import functools

import jax
import jax.numpy as jnp
from jax import lax
from jax.experimental import pallas as pl
from jax.experimental.pallas import tpu as pltpu
from jax.sharding import PartitionSpec as P

TILES_X = 120
TILES_Y = 68
TILE_SIDE = 16
BLOCK_TILES = 8
LANES = 128
ROWS = 16
F32 = jnp.float32
BF16 = jnp.bfloat16

focal_length = 1000.0
center_x = 960.0
center_y = 540.0
dilation = 0.3
beta_one = 0.9
beta_two = 0.999
learn_rate = 0.01
adam_eps = 1e-08
adam_steps = 100.0
sh_const = (
    0.28209479177387814,
    0.4886025119029199,
    1.0925484305920792,
    0.31539156525252005,
    0.5462742152960396,
    0.5900435899266435,
    2.890611442640554,
    0.4570457994644658,
    0.3731763325901154,
    1.445305721320277,
)


def sh_basis(x, y, z):
    s = sh_const
    xx, yy, zz = x * x, y * y, z * z
    return [
        None,
        -s[1] * y,
        s[1] * z,
        -s[1] * x,
        s[2] * (x * y),
        -s[2] * (y * z),
        s[3] * (2.0 * zz - xx - yy),
        -s[2] * (x * z),
        s[4] * (xx - yy),
        -s[5] * y * (3.0 * xx - yy),
        s[6] * (x * y) * z,
        -s[7] * y * (4.0 * zz - xx - yy),
        s[8] * z * (2.0 * zz - 3.0 * xx - 3.0 * yy),
        -s[7] * x * (4.0 * zz - xx - yy),
        s[9] * z * (xx - yy),
        -s[5] * x * (xx - 3.0 * yy),
    ]


def sh_pull(h, x, y, z):
    s = sh_const
    xx, yy, zz = x * x, y * y, z * z
    xy, xz, yz = x * y, x * z, y * z
    diff = xx - yy
    ring = 4.0 * zz - xx - yy
    g_x = (
        -s[1] * h[3]
        + s[2] * (h[4] * y - h[7] * z)
        - (2.0 * s[3]) * h[6] * x
        + (2.0 * s[4]) * h[8] * x
        - (6.0 * s[5]) * h[9] * xy
        + s[6] * h[10] * yz
        + (2.0 * s[7]) * h[11] * xy
        - (6.0 * s[8]) * h[12] * xz
        - s[7] * h[13] * (ring - 2.0 * xx)
        + (2.0 * s[9]) * h[14] * xz
        - (3.0 * s[5]) * h[15] * diff
    )
    g_y = (
        -s[1] * h[1]
        + s[2] * (h[4] * x - h[5] * z)
        - (2.0 * s[3]) * h[6] * y
        - (2.0 * s[4]) * h[8] * y
        - (3.0 * s[5]) * h[9] * diff
        + s[6] * h[10] * xz
        - s[7] * h[11] * (ring - 2.0 * yy)
        - (6.0 * s[8]) * h[12] * yz
        + (2.0 * s[7]) * h[13] * xy
        - (2.0 * s[9]) * h[14] * yz
        + (6.0 * s[5]) * h[15] * xy
    )
    g_z = (
        s[1] * h[2]
        - s[2] * (h[5] * y + h[7] * x)
        + (4.0 * s[3]) * h[6] * z
        + s[6] * h[10] * xy
        - (8.0 * s[7]) * (h[11] * yz + h[13] * xz)
        + s[8] * h[12] * (6.0 * zz - 3.0 * xx - 3.0 * yy)
        + s[9] * h[14] * diff
    )
    return g_x, g_y, g_z


def project_parts(feat, cam):
    rot = [[cam[3 * r + c] for c in range(3)] for r in range(3)]
    off = [feat(a) - cam[9 + a] for a in range(3)]
    in_cam = [rot[r][0] * off[0] + rot[r][1] * off[1] + rot[r][2] * off[2] for r in range(3)]
    inv = 1.0 / in_cam[2]
    u = in_cam[0] * inv
    v = in_cam[1] * inv
    finv = focal_length * inv
    scale = [jnp.exp(2.0 * feat(3 + a)) for a in range(3)]
    quat = [feat(6 + a) for a in range(4)]
    rnorm = lax.rsqrt(quat[0] * quat[0] + quat[1] * quat[1] + quat[2] * quat[2] + quat[3] * quat[3])
    w, x, y, z = [q * rnorm for q in quat]
    turn = [
        [1.0 - 2.0 * (y * y + z * z), 2.0 * (x * y - w * z), 2.0 * (x * z + w * y)],
        [2.0 * (x * y + w * z), 1.0 - 2.0 * (x * x + z * z), 2.0 * (y * z - w * x)],
        [2.0 * (x * z - w * y), 2.0 * (y * z + w * x), 1.0 - 2.0 * (x * x + y * y)],
    ]
    screen = [
        [finv * (rot[0][c] - u * rot[2][c]) for c in range(3)],
        [finv * (rot[1][c] - v * rot[2][c]) for c in range(3)],
    ]
    axes = [
        [sum(screen[r][c] * turn[c][k] for c in range(3)) for k in range(3)] for r in range(2)
    ]
    wide = [[axes[r][k] * scale[k] for k in range(3)] for r in range(2)]
    cov_xx = sum(wide[0][k] * axes[0][k] for k in range(3)) + dilation
    cov_xy = sum(wide[0][k] * axes[1][k] for k in range(3))
    cov_yy = sum(wide[1][k] * axes[1][k] for k in range(3)) + dilation
    rdet = 1.0 / (cov_xx * cov_yy - cov_xy * cov_xy)
    conic = (cov_yy * rdet, -cov_xy * rdet, cov_xx * rdet)
    opacity = 1.0 / (1.0 + jnp.exp(-feat(10)))
    rlen = lax.rsqrt(off[0] * off[0] + off[1] * off[1] + off[2] * off[2])
    way = [off[a] * rlen for a in range(3)]
    return dict(
        rot=rot, inv=inv, u=u, v=v, finv=finv, scale=scale, rnorm=rnorm, rotor=(w, x, y, z), turn=turn,
        screen=screen, axes=axes, wide=wide, conic=conic, opacity=opacity, rlen=rlen, way=way,
    )


def project_rows(feat, cam):
    part = project_parts(feat, cam)
    basis = sh_basis(*part["way"])
    colours = []
    for k in range(3):
        total = 0.5 + sh_const[0] * feat(11 + 16 * k)
        for b in range(1, 16):
            total = total + feat(11 + 16 * k + b) * basis[b]
        colours.append(total)
    mean_x = focal_length * part["u"] + center_x
    mean_y = focal_length * part["v"] + center_y
    return [mean_x, mean_y, *part["conic"], part["opacity"], *colours]


def project_pull(feat, cam, grads, put):
    part = project_parts(feat, cam)
    g_mx, g_my, g_a, g_b, g_c, g_o = grads[:6]
    g_col = grads[6:9]
    way, rlen = part["way"], part["rlen"]
    basis = sh_basis(*way)
    pulled = [None]
    for k in range(3):
        put(11 + 16 * k, sh_const[0] * g_col[k])
    for b in range(1, 16):
        total = 0.0
        for k in range(3):
            put(11 + 16 * k + b, g_col[k] * basis[b])
            total = total + g_col[k] * feat(11 + 16 * k + b)
        pulled.append(total)
    g_way = sh_pull(pulled, *way)
    along = way[0] * g_way[0] + way[1] * g_way[1] + way[2] * g_way[2]
    g_off = [(g_way[a] - way[a] * along) * rlen for a in range(3)]
    put(10, g_o * part["opacity"] * (1.0 - part["opacity"]))
    a, b, c = part["conic"]
    g_xx = -(a * a * g_a + a * b * g_b + b * b * g_c)
    g_xy = -(2.0 * a * b * g_a + (a * c + b * b) * g_b + 2.0 * b * c * g_c)
    g_yy = -(b * b * g_a + b * c * g_b + c * c * g_c)
    axes, wide, turn, screen = part["axes"], part["wide"], part["turn"], part["screen"]
    for k in range(3):
        g_scale = (
            g_xx * axes[0][k] * wide[0][k]
            + g_xy * axes[0][k] * wide[1][k]
            + g_yy * axes[1][k] * wide[1][k]
        )
        put(3 + k, 2.0 * g_scale)
    g_axes = [
        [2.0 * g_xx * wide[0][k] + g_xy * wide[1][k] for k in range(3)],
        [2.0 * g_yy * wide[1][k] + g_xy * wide[0][k] for k in range(3)],
    ]
    g_screen = [
        [sum(g_axes[r][k] * turn[c][k] for k in range(3)) for c in range(3)] for r in range(2)
    ]
    gm = [
        [g_axes[0][k] * screen[0][c] + g_axes[1][k] * screen[1][c] for k in range(3)]
        for c in range(3)
    ]
    w, x, y, z = part["rotor"]
    up_xy, up_xz, up_yz = gm[0][1] + gm[1][0], gm[0][2] + gm[2][0], gm[1][2] + gm[2][1]
    un_xy, un_xz, un_yz = gm[1][0] - gm[0][1], gm[0][2] - gm[2][0], gm[2][1] - gm[1][2]
    g_rotor = [
        2.0 * (z * un_xy + y * un_xz + x * un_yz),
        2.0 * (y * up_xy + z * up_xz + w * un_yz - 2.0 * x * (gm[1][1] + gm[2][2])),
        2.0 * (x * up_xy + z * up_yz + w * un_xz - 2.0 * y * (gm[0][0] + gm[2][2])),
        2.0 * (x * up_xz + y * up_yz + w * un_xy - 2.0 * z * (gm[0][0] + gm[1][1])),
    ]
    rotor = (w, x, y, z)
    along = sum(rotor[i] * g_rotor[i] for i in range(4))
    for i in range(4):
        put(6 + i, (g_rotor[i] - rotor[i] * along) * part["rnorm"])
    rot, inv, finv, u, v = part["rot"], part["inv"], part["finv"], part["u"], part["v"]
    g_u = focal_length * g_mx - finv * sum(g_screen[0][c] * rot[2][c] for c in range(3))
    g_v = focal_length * g_my - finv * sum(g_screen[1][c] * rot[2][c] for c in range(3))
    g_f = sum(g_screen[r][c] * screen[r][c] for r in range(2) for c in range(3))
    g_in = [g_u * inv, g_v * inv, -(g_f + g_u * u + g_v * v) * inv]
    for axis in range(3):
        put(
            axis,
            g_off[axis] + rot[0][axis] * g_in[0] + rot[1][axis] * g_in[1] + rot[2][axis] * g_in[2],
        )


def split(value):
    high = value.astype(BF16)
    return high, (value - high.astype(F32)).astype(BF16)


def matmul(a, b, dims=((1,), (0,))):
    return lax.dot_general(a, b, (dims, ((), ())), preferred_element_type=F32)


def spread_features(parts, scratch, count):
    tiles = sum(part.shape[1] for part in parts) // LANES
    at = 0
    for part in parts:
        for first in range(0, part.shape[1], LANES):
            for row in range(0, count, 8):
                rows = min(8, count - row)
                scratch[pl.ds(row * tiles + at, rows, stride=tiles), :] = part[
                    row : row + rows, first : first + LANES
                ]
            at += 1
    return tiles


def cut_kernel(shards, where, params, *refs):
    pieces, sems = refs[:shards], refs[shards]
    chunk = params.shape[1] // shards
    copies = []
    for d in range(shards):
        first = pl.multiple_of((where[0] ^ d) * chunk, LANES)
        copies.append(
            pltpu.make_async_copy(params.at[:, pl.ds(first, chunk)], pieces[d], sems.at[d])
        )
    for copy in copies:
        copy.start()
    for copy in copies:
        copy.wait()


def cut(group, params, shards):
    features, columns = params.shape
    piece = jax.ShapeDtypeStruct((features, columns // shards), F32)
    return pl.pallas_call(
        functools.partial(cut_kernel, shards),
        out_shape=(piece,) * shards,
        in_specs=[smem(), pl.BlockSpec(memory_space=pl.ANY)],
        out_specs=(vmem(),) * shards,
        scratch_shapes=[pltpu.SemaphoreType.DMA((shards,))],
        compiler_params=pltpu.CompilerParams(vmem_limit_bytes=32 * 1024 * 1024),
        name="cut",
    )(group.reshape(1), params)


def pack_kernel(shards, where, shard_of, local_of, target, _, info, place_s):
    group = where[0]
    width = info.shape[1]
    tile_count, listed = local_of.shape
    rows_each = (info.shape[0] - 4) // tile_count
    columns = rows_each * width
    chunk = columns // shards
    info[0:3, :] = target[...]
    for t in range(tile_count):
        place = (shard_of[t] ^ group) * chunk + (local_of[t : t + 1, :] - group * chunk)
        info[3:4, t * listed : (t + 1) * listed] = place.astype(F32)
        row_i = lax.broadcasted_iota(jnp.int32, (LANES, LANES), 0)
        col_i = lax.broadcasted_iota(jnp.int32, (LANES, LANES), 1)
        for first in range(0, listed, LANES):
            spread = jnp.broadcast_to(place[:, first : first + LANES].astype(F32), (LANES, LANES))
            place_s[first : first + LANES, :] = jnp.broadcast_to(
                jnp.sum(jnp.where(row_i == col_i, spread, 0.0), axis=1, keepdims=True), (LANES, LANES)
            )
        lane_of = lax.broadcasted_iota(jnp.int32, (8, LANES), 1).astype(F32)
        row_of = lax.broadcasted_iota(jnp.int32, (8, LANES), 0).astype(F32)
        for s in range(columns // LANES):
            best = jnp.full((8, LANES), -1.0, F32)
            column = lane_of + float(s * LANES)
            for first in range(0, listed, 8):
                best = jnp.where(
                    place_s[first : first + 8, :] == column, row_of + float(first), best
                )
            best = jnp.max(best, axis=0, keepdims=True)
            row, at = 4 + t * rows_each + s * LANES // width, s * LANES % width
            info[row : row + 1, at : at + LANES] = best


def pack(group, columns, target, hit_shard, hit_local, shards, after):
    tile_count, listed = hit_local.shape
    width = target.shape[1]
    rows = 4 + tile_count * (columns // width)
    return pl.pallas_call(
        functools.partial(pack_kernel, shards),
        out_shape=jax.ShapeDtypeStruct((rows, width), F32),
        in_specs=[smem()] + [vmem()] * 3 + [pl.BlockSpec(memory_space=pl.ANY)],
        out_specs=vmem(),
        scratch_shapes=[pltpu.VMEM((listed, LANES), F32)],
        compiler_params=pltpu.CompilerParams(vmem_limit_bytes=32 * 1024 * 1024),
        name="pack",
    )(group.reshape(1), hit_shard.reshape(tile_count, 1, listed), hit_local, target, after)


def render_kernel(pieces, groups, blocks, *refs):
    tile_ids, cams, where = refs[:3]
    parts = refs[3 : 3 + pieces]
    infos = refs[3 + pieces : 3 + pieces + groups]
    rendered = refs[3 + pieces + groups]
    rest = refs[4 + pieces + groups :]
    packets = rest[: len(rest) - 9]
    feats, rows, e_s, t_s, d_s, hi_s, lo_s, acc_s, info_s = rest[len(rest) - 9 :]
    tile_count, listed = e_s.shape[0], e_s.shape[2]
    pixels = e_s.shape[1]
    side = TILE_SIDE
    view = tile_ids[0] // (TILES_X * TILES_Y)
    cam = [cams[view, i] for i in range(12)]
    slabs = spread_features(parts, feats, parts[0].shape[0])
    projected = project_rows(lambda f: feats[f * slabs : (f + 1) * slabs, :], cam)
    for f, value in enumerate(projected):
        rows[pl.ds(f, slabs, stride=ROWS), :] = value
    zero_row = jnp.zeros((slabs, LANES), F32)
    for f in range(len(projected), ROWS):
        rows[pl.ds(f, slabs, stride=ROWS), :] = zero_row
    for g in range(groups):
        info_s[g] = infos[g][...]

    row_i = lax.broadcasted_iota(jnp.int32, (listed, listed), 0)
    col_i = lax.broadcasted_iota(jnp.int32, (listed, listed), 1)
    earlier = jnp.where(row_i < col_i, 1.0, 0.0).astype(BF16)
    later = jnp.where(row_i > col_i, 1.0, 0.0).astype(BF16)
    step = lax.broadcasted_iota(jnp.int32, (side, listed), 0).astype(F32)
    within = tile_ids[0] % (TILES_X * TILES_Y)
    first_row = (within // TILES_X) // 2 * 2
    first_col = (within % TILES_X) // 4 * 4
    me = where[0]

    def one_group(g, carry):
        lists = []
        for t in range(tile_count):
            halves = []
            for first in range(t * listed, (t + 1) * listed, LANES):
                at = info_s[g, 3:4, first : first + LANES].astype(jnp.int32)
                at = jnp.broadcast_to(at, (ROWS, LANES))
                lane, slab = at & (LANES - 1), at >> 7
                found = jnp.zeros((ROWS, LANES), F32)
                for s in range(slabs):
                    here = jnp.take_along_axis(
                        rows[s * ROWS : (s + 1) * ROWS, :], lane, axis=1, mode="promise_in_bounds"
                    )
                    found = jnp.where(slab == s, here, found)
                halves.append(found)
            lists.append(jnp.concatenate(halves, axis=1))

        setup = []
        for t in range(tile_count):
            entry = lists[t]
            slot = (me ^ g) * tile_count + t
            x_0 = ((first_col + slot % 4) * side).astype(F32) + 0.5
            y_0 = ((first_row + slot // 4) * side).astype(F32) + 0.5
            quad_a, quad_b, quad_c = -0.5 * entry[2:3], -entry[3:4], -0.5 * entry[4:5]
            opacity = entry[5:6]
            dx = (step + x_0) - entry[0:1]
            dy = (step + y_0) - entry[1:2]
            adx2 = quad_a * dx * dx
            bdy = quad_b * dy
            cdy2 = quad_c * dy * dy
            setup.append((entry, quad_a, quad_b, quad_c, opacity, dx, dy))
            for row in range(side):
                at = slice(row * side, (row + 1) * side)
                power = adx2 + dx * bdy[row : row + 1] + cdy2[row : row + 1]
                bell = jnp.exp(power)
                e_s[t, at, :] = bell
                hi_s[t, at, :], lo_s[t, at, :] = split(jnp.log(1.0 - opacity * bell))

        for t in range(tile_count):
            t_s[t] = matmul(hi_s[t], earlier) + matmul(lo_s[t], earlier)

        for t in range(tile_count):
            entry, opacity = setup[t][0], setup[t][4]
            for row in range(side):
                at = slice(row * side, (row + 1) * side)
                passed = jnp.exp(t_s[t, at, :])
                t_s[t, at, :] = passed
                hi_s[t, at, :], lo_s[t, at, :] = split(opacity * e_s[t, at, :] * passed)
            c_hi, c_lo = split(entry[6:9])
            both = ((1,), (1,))
            image = (
                matmul(c_hi, hi_s[t], both)
                + matmul(c_lo, hi_s[t], both)
                + matmul(c_hi, lo_s[t], both)
            )
            here = slice(t * pixels, (t + 1) * pixels)

            @pl.when(g == 0)
            def _():
                rendered[:, here] = image

            error = image - info_s[g, 0:3, here]
            g_hi, g_lo = split(error)
            first = ((0,), (0,))
            d_s[t] = (
                matmul(g_hi, c_hi, first) + matmul(g_lo, c_hi, first) + matmul(g_hi, c_lo, first)
            )
            g_colours = matmul(g_hi, hi_s[t]) + matmul(g_lo, hi_s[t]) + matmul(g_hi, lo_s[t])
            acc_s[g, t, 6:9, :] = g_colours

        for t in range(tile_count):
            opacity = setup[t][4]
            for row in range(side):
                at = slice(row * side, (row + 1) * side)
                pushed = t_s[t, at, :] * d_s[t, at, :]
                t_s[t, at, :] = pushed
                hi_s[t, at, :], lo_s[t, at, :] = split(opacity * e_s[t, at, :] * pushed)
            d_s[t] = matmul(hi_s[t], later) + matmul(lo_s[t], later)

        for t in range(tile_count):
            entry, quad_a, quad_b, quad_c, opacity, dx, dy = setup[t]
            r_0 = r_1 = r_2 = None
            for row in range(side):
                at = slice(row * side, (row + 1) * side)
                bell = e_s[t, at, :]
                flow = bell * (t_s[t, at, :] - d_s[t, at, :] / (1.0 - opacity * bell))
                one = flow * dy[row : row + 1]
                two = one * dy[row : row + 1]
                r_0 = flow if r_0 is None else r_0 + flow
                r_1 = one if r_1 is None else r_1 + one
                r_2 = two if r_2 is None else r_2 + two
            rdx = r_0 * dx
            m_00 = jnp.sum(r_0, axis=0, keepdims=True)
            m_10 = jnp.sum(rdx, axis=0, keepdims=True)
            m_20 = jnp.sum(rdx * dx, axis=0, keepdims=True)
            m_01 = jnp.sum(r_1, axis=0, keepdims=True)
            m_11 = jnp.sum(r_1 * dx, axis=0, keepdims=True)
            m_02 = jnp.sum(r_2, axis=0, keepdims=True)
            acc_s[g, t, 0:1, :] = -opacity * (2.0 * quad_a * m_10 + quad_b * m_01)
            acc_s[g, t, 1:2, :] = -opacity * (2.0 * quad_c * m_01 + quad_b * m_10)
            acc_s[g, t, 2:3, :] = -0.5 * opacity * m_20
            acc_s[g, t, 3:4, :] = -opacity * m_11
            acc_s[g, t, 4:5, :] = -0.5 * opacity * m_02
            acc_s[g, t, 5:6, :] = m_00
            acc_s[g, t, 9:16, :] = jnp.zeros((7, listed), F32)
        return carry

    lax.fori_loop(0, groups, one_group, 0)

    share = view.astype(F32)
    row_of = lax.broadcasted_iota(jnp.int32, (ROWS, LANES), 0)
    lane_of = lax.broadcasted_iota(jnp.int32, (ROWS, LANES), 1)
    chunk = packets[0].shape[1]
    width = info_s.shape[2]
    rows_each = slabs * LANES // width
    for s in range(slabs):
        totals = []
        for g in range(groups):
            total = jnp.zeros((ROWS, LANES), F32)
            for t in range(tile_count):
                row, first = 4 + t * rows_each + s * LANES // width, s * LANES % width
                at = info_s[g, row : row + 1, first : first + LANES].astype(jnp.int32)
                at = jnp.broadcast_to(at, (ROWS, LANES))
                lane, half = at & (LANES - 1), at >> 7
                for h in range(listed // LANES):
                    here = jnp.take_along_axis(
                        acc_s[g, t, :, h * LANES : (h + 1) * LANES],
                        lane,
                        axis=1,
                        mode="promise_in_bounds",
                    )
                    total = total + jnp.where(half == h, here, 0.0)
            totals.append(total)
        while len(totals) > 1:
            totals = [totals[k] + totals[k + 1] for k in range(0, len(totals), 2)]
        total = totals[0]
        if blocks == 1:
            mine = share
        else:
            column = s * LANES + lane_of
            mine = jnp.where(column % where[2] // (where[2] // blocks) == where[1], share, 0.0)
        total = jnp.where(row_of == 9, mine, total)
        packets[s * LANES // chunk][:, s * LANES % chunk : s * LANES % chunk + LANES] = total


def update_kernel(pieces, where, cams, params, adam_m, adam_v, *refs):
    packets = refs[:pieces]
    new_params, new_m, new_v, feats, rows, grads = refs[pieces:]
    features, width = params.shape
    slabs = spread_features([params], feats, features)
    chunk = packets[0].shape[1]
    for d in range(pieces):
        for h in range(chunk // LANES):
            slab = (where[0] ^ d) * (chunk // LANES) + h
            rows[pl.ds(slab, ROWS, stride=slabs), :] = packets[d][:, h * LANES : (h + 1) * LANES]
    pulled = [rows[f * slabs : (f + 1) * slabs, :] for f in range(10)]
    view = pulled[9]
    cam = []
    for i in range(12):
        value = jnp.full((slabs, LANES), cams[0, i], F32)
        for v in range(1, cams.shape[0]):
            value = jnp.where(view == float(v), cams[v, i], value)
        cam.append(value)

    def put(f, value):
        grads[f * slabs : (f + 1) * slabs, :] = value

    project_pull(lambda f: feats[f * slabs : (f + 1) * slabs, :], cam, pulled[:9], put)
    rate = learn_rate / (1.0 - beta_one**adam_steps)
    unbias = 1.0 / (1.0 - beta_two**adam_steps)
    for s in range(slabs):
        for row in range(0, features, 8):
            count = min(8, features - row)
            at = (slice(row, row + count), slice(s * LANES, (s + 1) * LANES))
            grad = grads[pl.ds(row * slabs + s, count, stride=slabs), :]
            moment = beta_one * adam_m[at] + (1.0 - beta_one) * grad
            second = beta_two * adam_v[at] + (1.0 - beta_two) * grad * grad
            new_m[at] = moment
            new_v[at] = second
            new_params[at] = params[at] - rate * moment / (jnp.sqrt(second * unbias) + adam_eps)


def vmem():
    return pl.BlockSpec(memory_space=pltpu.VMEM)


def smem():
    return pl.BlockSpec(memory_space=pltpu.SMEM)


def render(tile_ids, cameras, where, parts, infos, tile_count, blocks):
    width = sum(part.shape[1] for part in parts)
    features = parts[0].shape[0]
    slabs = width // LANES
    pixels = listed = infos[0].shape[1] // tile_count
    square = (tile_count, pixels, listed)
    groups = len(infos)
    packet = jax.ShapeDtypeStruct((ROWS, parts[0].shape[1]), F32)
    out = pl.pallas_call(
        functools.partial(render_kernel, len(parts), groups, blocks),
        out_shape=(jax.ShapeDtypeStruct((3, tile_count * pixels), F32),) + (packet,) * len(parts),
        in_specs=[smem()] * 3 + [vmem()] * (len(parts) + groups),
        out_specs=(vmem(),) * (1 + len(parts)),
        scratch_shapes=[
            pltpu.VMEM((features * slabs, LANES), F32),
            pltpu.VMEM((ROWS * slabs, LANES), F32),
            pltpu.VMEM(square, F32),
            pltpu.VMEM(square, F32),
            pltpu.VMEM(square, F32),
            pltpu.VMEM(square, BF16),
            pltpu.VMEM(square, BF16),
            pltpu.VMEM((groups, tile_count, ROWS, listed), F32),
            pltpu.VMEM((groups,) + infos[0].shape, F32),
        ],
        compiler_params=pltpu.CompilerParams(vmem_limit_bytes=32 * 1024 * 1024),
        name="render",
    )(tile_ids, cameras, where, *parts, *infos)
    return out[0], list(out[1:])


def update(where, cameras, params, adam_m, adam_v, packets):
    features, width = params.shape
    slabs = width // LANES
    shape = jax.ShapeDtypeStruct(params.shape, F32)
    return pl.pallas_call(
        functools.partial(update_kernel, len(packets)),
        out_shape=(shape, shape, shape),
        in_specs=[smem()] * 2 + [vmem()] * (3 + len(packets)),
        out_specs=(vmem(), vmem(), vmem()),
        scratch_shapes=[
            pltpu.VMEM((features * slabs, LANES), F32),
            pltpu.VMEM((ROWS * slabs, LANES), F32),
            pltpu.VMEM((features * slabs, LANES), F32),
        ],
        compiler_params=pltpu.CompilerParams(vmem_limit_bytes=32 * 1024 * 1024),
        name="update",
    )(where, cameras, params, adam_m, adam_v, *packets)


def swap(value, axis, d):
    if d == 0:
        return value
    return lax.ppermute(value, axis, [(k, k ^ d) for k in range(lax.axis_size(axis))])


def local(params, adam_m, adam_v, cameras, target, tile_ids, hit_shard, hit_local):
    width = params.shape[1]
    tile_count, listed = hit_local.shape
    shards = lax.axis_size("gs")
    along = lax.axis_size("tile")
    chunk = width // shards
    group = lax.axis_index("gs")
    seat = lax.axis_index("tile")
    aligned = chunk % LANES == 0
    team = BLOCK_TILES // tile_count
    blocks = along // team

    if aligned:
        parts = cut(group, params, shards)
    else:
        parts = [
            lax.dynamic_slice_in_dim(params, (group ^ d) * chunk, chunk, axis=1)
            for d in range(shards)
        ]
    info = pack(group, width, target, hit_shard, hit_local, shards, parts[0])
    parts = [swap(parts[d], "gs", d) for d in range(shards)]
    info, parts[1] = lax.optimization_barrier((info, parts[1]))
    infos = [swap(info, "tile", d) for d in range(team)]
    if not aligned:
        parts = [jnp.concatenate(parts, axis=1)]
    where = jnp.stack([seat % team, seat // team, jnp.int32(chunk)]).astype(jnp.int32)
    rendered, packets = render(tile_ids, cameras, where, parts, infos, tile_count, blocks)
    if not aligned:
        packets = [packets[0][:, d * chunk : (d + 1) * chunk] for d in range(shards)]
    packets = [swap(packets[d], "gs", d) for d in range(shards)]
    if blocks > 1:
        packets = [block_sum(packet, along, team) for packet in packets]
    if aligned:
        own = group
    else:
        packets = [jnp.stack(packets)[jnp.arange(shards) ^ group].transpose(1, 0, 2).reshape(ROWS, -1)]
        own = jnp.int32(0)
    new_params, new_m, new_v = update(
        own.reshape(1), cameras, params, adam_m, adam_v, packets
    )
    return (rendered, new_params, new_m, new_v)


def block_sum(packet, along, team):
    step = team
    while step < along:
        packet = packet + swap(packet, "tile", step)
        step *= 2
    return packet


def solution(mesh):
    return jax.shard_map(
        local,
        mesh=mesh,
        in_specs=(
            P(None, ("groups", "gs")),
            P(None, ("groups", "gs")),
            P(None, ("groups", "gs")),
            P("groups", None),
            P(None, ("groups", "gs", "tile")),
            P(("groups", "gs", "tile")),
            P(("groups", "gs", "tile"), None, None),
            P(("groups", "gs", "tile"), None),
        ),
        out_specs=(
            P(None, ("groups", "gs", "tile")),
            P(None, ("groups", "gs")),
            P(None, ("groups", "gs")),
            P(None, ("groups", "gs")),
        ),
        check_vma=False,
    )
```

```python
import functools

import jax
import jax.numpy as jnp
from jax import lax
from jax.experimental import pallas as pl
from jax.experimental.pallas import tpu as pltpu
from jax.sharding import PartitionSpec as P

TILES_X = 120
TILES_Y = 68
TILE_SIDE = 16
BLOCK_TILES = 8
LANES = 128
ROWS = 16
F32 = jnp.float32
BF16 = jnp.bfloat16

focal_length = 1000.0
center_x = 960.0
center_y = 540.0
dilation = 0.3
beta_one = 0.9
beta_two = 0.999
learn_rate = 0.01
adam_eps = 1e-08
adam_steps = 100.0
sh_const = (
    0.28209479177387814,
    0.4886025119029199,
    1.0925484305920792,
    0.31539156525252005,
    0.5462742152960396,
    0.5900435899266435,
    2.890611442640554,
    0.4570457994644658,
    0.3731763325901154,
    1.445305721320277,
)


def sh_basis(x, y, z):
    s = sh_const
    xx, yy, zz = x * x, y * y, z * z
    return [
        None,
        -s[1] * y,
        s[1] * z,
        -s[1] * x,
        s[2] * (x * y),
        -s[2] * (y * z),
        s[3] * (2.0 * zz - xx - yy),
        -s[2] * (x * z),
        s[4] * (xx - yy),
        -s[5] * y * (3.0 * xx - yy),
        s[6] * (x * y) * z,
        -s[7] * y * (4.0 * zz - xx - yy),
        s[8] * z * (2.0 * zz - 3.0 * xx - 3.0 * yy),
        -s[7] * x * (4.0 * zz - xx - yy),
        s[9] * z * (xx - yy),
        -s[5] * x * (xx - 3.0 * yy),
    ]


def sh_pull(h, x, y, z):
    s = sh_const
    xx, yy, zz = x * x, y * y, z * z
    xy, xz, yz = x * y, x * z, y * z
    diff = xx - yy
    ring = 4.0 * zz - xx - yy
    g_x = (
        -s[1] * h[3]
        + s[2] * (h[4] * y - h[7] * z)
        - (2.0 * s[3]) * h[6] * x
        + (2.0 * s[4]) * h[8] * x
        - (6.0 * s[5]) * h[9] * xy
        + s[6] * h[10] * yz
        + (2.0 * s[7]) * h[11] * xy
        - (6.0 * s[8]) * h[12] * xz
        - s[7] * h[13] * (ring - 2.0 * xx)
        + (2.0 * s[9]) * h[14] * xz
        - (3.0 * s[5]) * h[15] * diff
    )
    g_y = (
        -s[1] * h[1]
        + s[2] * (h[4] * x - h[5] * z)
        - (2.0 * s[3]) * h[6] * y
        - (2.0 * s[4]) * h[8] * y
        - (3.0 * s[5]) * h[9] * diff
        + s[6] * h[10] * xz
        - s[7] * h[11] * (ring - 2.0 * yy)
        - (6.0 * s[8]) * h[12] * yz
        + (2.0 * s[7]) * h[13] * xy
        - (2.0 * s[9]) * h[14] * yz
        + (6.0 * s[5]) * h[15] * xy
    )
    g_z = (
        s[1] * h[2]
        - s[2] * (h[5] * y + h[7] * x)
        + (4.0 * s[3]) * h[6] * z
        + s[6] * h[10] * xy
        - (8.0 * s[7]) * (h[11] * yz + h[13] * xz)
        + s[8] * h[12] * (6.0 * zz - 3.0 * xx - 3.0 * yy)
        + s[9] * h[14] * diff
    )
    return g_x, g_y, g_z


def project_parts(feat, cam):
    rot = [[cam[3 * r + c] for c in range(3)] for r in range(3)]
    off = [feat(a) - cam[9 + a] for a in range(3)]
    in_cam = [rot[r][0] * off[0] + rot[r][1] * off[1] + rot[r][2] * off[2] for r in range(3)]
    inv = 1.0 / in_cam[2]
    u = in_cam[0] * inv
    v = in_cam[1] * inv
    finv = focal_length * inv
    scale = [jnp.exp(2.0 * feat(3 + a)) for a in range(3)]
    quat = [feat(6 + a) for a in range(4)]
    rnorm = lax.rsqrt(quat[0] * quat[0] + quat[1] * quat[1] + quat[2] * quat[2] + quat[3] * quat[3])
    w, x, y, z = [q * rnorm for q in quat]
    turn = [
        [1.0 - 2.0 * (y * y + z * z), 2.0 * (x * y - w * z), 2.0 * (x * z + w * y)],
        [2.0 * (x * y + w * z), 1.0 - 2.0 * (x * x + z * z), 2.0 * (y * z - w * x)],
        [2.0 * (x * z - w * y), 2.0 * (y * z + w * x), 1.0 - 2.0 * (x * x + y * y)],
    ]
    screen = [
        [finv * (rot[0][c] - u * rot[2][c]) for c in range(3)],
        [finv * (rot[1][c] - v * rot[2][c]) for c in range(3)],
    ]
    axes = [
        [sum(screen[r][c] * turn[c][k] for c in range(3)) for k in range(3)] for r in range(2)
    ]
    wide = [[axes[r][k] * scale[k] for k in range(3)] for r in range(2)]
    cov_xx = sum(wide[0][k] * axes[0][k] for k in range(3)) + dilation
    cov_xy = sum(wide[0][k] * axes[1][k] for k in range(3))
    cov_yy = sum(wide[1][k] * axes[1][k] for k in range(3)) + dilation
    rdet = 1.0 / (cov_xx * cov_yy - cov_xy * cov_xy)
    conic = (cov_yy * rdet, -cov_xy * rdet, cov_xx * rdet)
    opacity = 1.0 / (1.0 + jnp.exp(-feat(10)))
    rlen = lax.rsqrt(off[0] * off[0] + off[1] * off[1] + off[2] * off[2])
    way = [off[a] * rlen for a in range(3)]
    return dict(
        rot=rot, inv=inv, u=u, v=v, finv=finv, scale=scale, rnorm=rnorm, rotor=(w, x, y, z), turn=turn,
        screen=screen, axes=axes, wide=wide, conic=conic, opacity=opacity, rlen=rlen, way=way,
    )


def project_rows(feat, cam):
    part = project_parts(feat, cam)
    basis = sh_basis(*part["way"])
    colours = []
    for k in range(3):
        total = 0.5 + sh_const[0] * feat(11 + 16 * k)
        for b in range(1, 16):
            total = total + feat(11 + 16 * k + b) * basis[b]
        colours.append(total)
    mean_x = focal_length * part["u"] + center_x
    mean_y = focal_length * part["v"] + center_y
    return [mean_x, mean_y, *part["conic"], part["opacity"], *colours]


def project_pull(feat, cam, grads, put):
    part = project_parts(feat, cam)
    g_mx, g_my, g_a, g_b, g_c, g_o = grads[:6]
    g_col = grads[6:9]
    way, rlen = part["way"], part["rlen"]
    basis = sh_basis(*way)
    pulled = [None]
    for k in range(3):
        put(11 + 16 * k, sh_const[0] * g_col[k])
    for b in range(1, 16):
        total = 0.0
        for k in range(3):
            put(11 + 16 * k + b, g_col[k] * basis[b])
            total = total + g_col[k] * feat(11 + 16 * k + b)
        pulled.append(total)
    g_way = sh_pull(pulled, *way)
    along = way[0] * g_way[0] + way[1] * g_way[1] + way[2] * g_way[2]
    g_off = [(g_way[a] - way[a] * along) * rlen for a in range(3)]
    put(10, g_o * part["opacity"] * (1.0 - part["opacity"]))
    a, b, c = part["conic"]
    g_xx = -(a * a * g_a + a * b * g_b + b * b * g_c)
    g_xy = -(2.0 * a * b * g_a + (a * c + b * b) * g_b + 2.0 * b * c * g_c)
    g_yy = -(b * b * g_a + b * c * g_b + c * c * g_c)
    axes, wide, turn, screen = part["axes"], part["wide"], part["turn"], part["screen"]
    for k in range(3):
        g_scale = (
            g_xx * axes[0][k] * wide[0][k]
            + g_xy * axes[0][k] * wide[1][k]
            + g_yy * axes[1][k] * wide[1][k]
        )
        put(3 + k, 2.0 * g_scale)
    g_axes = [
        [2.0 * g_xx * wide[0][k] + g_xy * wide[1][k] for k in range(3)],
        [2.0 * g_yy * wide[1][k] + g_xy * wide[0][k] for k in range(3)],
    ]
    g_screen = [
        [sum(g_axes[r][k] * turn[c][k] for k in range(3)) for c in range(3)] for r in range(2)
    ]
    gm = [
        [g_axes[0][k] * screen[0][c] + g_axes[1][k] * screen[1][c] for k in range(3)]
        for c in range(3)
    ]
    w, x, y, z = part["rotor"]
    up_xy, up_xz, up_yz = gm[0][1] + gm[1][0], gm[0][2] + gm[2][0], gm[1][2] + gm[2][1]
    un_xy, un_xz, un_yz = gm[1][0] - gm[0][1], gm[0][2] - gm[2][0], gm[2][1] - gm[1][2]
    g_rotor = [
        2.0 * (z * un_xy + y * un_xz + x * un_yz),
        2.0 * (y * up_xy + z * up_xz + w * un_yz - 2.0 * x * (gm[1][1] + gm[2][2])),
        2.0 * (x * up_xy + z * up_yz + w * un_xz - 2.0 * y * (gm[0][0] + gm[2][2])),
        2.0 * (x * up_xz + y * up_yz + w * un_xy - 2.0 * z * (gm[0][0] + gm[1][1])),
    ]
    rotor = (w, x, y, z)
    along = sum(rotor[i] * g_rotor[i] for i in range(4))
    for i in range(4):
        put(6 + i, (g_rotor[i] - rotor[i] * along) * part["rnorm"])
    rot, inv, finv, u, v = part["rot"], part["inv"], part["finv"], part["u"], part["v"]
    g_u = focal_length * g_mx - finv * sum(g_screen[0][c] * rot[2][c] for c in range(3))
    g_v = focal_length * g_my - finv * sum(g_screen[1][c] * rot[2][c] for c in range(3))
    g_f = sum(g_screen[r][c] * screen[r][c] for r in range(2) for c in range(3))
    g_in = [g_u * inv, g_v * inv, -(g_f + g_u * u + g_v * v) * inv]
    for axis in range(3):
        put(
            axis,
            g_off[axis] + rot[0][axis] * g_in[0] + rot[1][axis] * g_in[1] + rot[2][axis] * g_in[2],
        )


def split(value):
    high = value.astype(BF16)
    return high, (value - high.astype(F32)).astype(BF16)


def matmul(a, b, dims=((1,), (0,))):
    return lax.dot_general(a, b, (dims, ((), ())), preferred_element_type=F32)


def spread_features(parts, scratch, count):
    tiles = sum(part.shape[1] for part in parts) // LANES
    at = 0
    for part in parts:
        for first in range(0, part.shape[1], LANES):
            for row in range(0, count, 8):
                rows = min(8, count - row)
                scratch[pl.ds(row * tiles + at, rows, stride=tiles), :] = part[
                    row : row + rows, first : first + LANES
                ]
            at += 1
    return tiles


def pack_kernel(shards, pieces, where, *refs):
    sources, refs = refs[: 3 + (pieces > 0)], refs[3 + (pieces > 0) :]
    info, parts, refs = refs[0], refs[1 : 1 + pieces], refs[1 + pieces :]
    shard_of, local_of, goal, place_s, sems, cut_sems = refs
    group = where[0]
    loads = [
        pltpu.make_async_copy(source, held, sems.at[k])
        for k, (source, held) in enumerate(zip(sources, (shard_of, local_of, goal)))
    ]
    for d in range(pieces):
        chunk = parts[d].shape[1]
        first = pl.multiple_of((group ^ d) * chunk, LANES)
        loads.append(
            pltpu.make_async_copy(sources[3].at[:, pl.ds(first, chunk)], parts[d], cut_sems.at[d])
        )
    for load in loads:
        load.start()
    for load in loads[:3]:
        load.wait()
    width = info.shape[1]
    tile_count, listed = local_of.shape
    rows_each = (info.shape[0] - 4) // tile_count
    columns = rows_each * width
    chunk = columns // shards
    info[0:3, :] = goal[...]
    for t in range(tile_count):
        place = (shard_of[t] ^ group) * chunk + (local_of[t : t + 1, :] - group * chunk)
        info[3:4, t * listed : (t + 1) * listed] = place.astype(F32)
        row_i = lax.broadcasted_iota(jnp.int32, (LANES, LANES), 0)
        col_i = lax.broadcasted_iota(jnp.int32, (LANES, LANES), 1)
        for first in range(0, listed, LANES):
            spread = jnp.broadcast_to(place[:, first : first + LANES].astype(F32), (LANES, LANES))
            place_s[first : first + LANES, :] = jnp.broadcast_to(
                jnp.sum(jnp.where(row_i == col_i, spread, 0.0), axis=1, keepdims=True), (LANES, LANES)
            )
        lane_of = lax.broadcasted_iota(jnp.int32, (8, LANES), 1).astype(F32)
        row_of = lax.broadcasted_iota(jnp.int32, (8, LANES), 0).astype(F32)
        for s in range(columns // LANES):
            best = jnp.full((8, LANES), -1.0, F32)
            column = lane_of + float(s * LANES)
            for first in range(0, listed, 8):
                best = jnp.where(
                    place_s[first : first + 8, :] == column, row_of + float(first), best
                )
            best = jnp.max(best, axis=0, keepdims=True)
            row, at = 4 + t * rows_each + s * LANES // width, s * LANES % width
            info[row : row + 1, at : at + LANES] = best
    for load in loads[3:]:
        load.wait()


def pack(group, params, target, hit_shard, hit_local, shards, aligned):
    features, columns = params.shape
    tile_count, listed = hit_local.shape
    width = target.shape[1]
    rows = 4 + tile_count * (columns // width)
    pieces = shards if aligned else 0
    piece = jax.ShapeDtypeStruct((features, columns // shards), F32)
    args = (hit_shard.reshape(tile_count, 1, listed), hit_local, target) + (params,) * aligned
    out = call(
        functools.partial(pack_kernel, shards, pieces),
        "pack",
        (jax.ShapeDtypeStruct((rows, width), F32),) + (piece,) * pieces,
        [smem()] + [pl.BlockSpec(memory_space=pltpu.HBM)] * len(args),
        [
            pltpu.VMEM((tile_count, 1, listed), jnp.int32),
            pltpu.VMEM((tile_count, listed), jnp.int32),
            pltpu.VMEM(target.shape, F32),
            pltpu.VMEM((listed, LANES), F32),
            pltpu.SemaphoreType.DMA((3,)),
            pltpu.SemaphoreType.DMA((shards,)),
        ],
        (group.reshape(1),) + args,
    )
    return out[0], list(out[1:])


def composite(tiles, first_group, me, rows, info_s, rendered, work):
    e_s, t_s, d_s, hi_s, lo_s, acc_s = work
    tile_count, pixels, listed = e_s.shape
    slabs = rows.shape[0] // ROWS
    side = TILE_SIDE
    first_col, first_row = tiles
    row_i = lax.broadcasted_iota(jnp.int32, (listed, listed), 0)
    col_i = lax.broadcasted_iota(jnp.int32, (listed, listed), 1)
    earlier = jnp.where(row_i < col_i, 1.0, 0.0).astype(BF16)
    later = jnp.where(row_i > col_i, 1.0, 0.0).astype(BF16)
    step = lax.broadcasted_iota(jnp.int32, (side, listed), 0).astype(F32)

    def one_group(g, carry):
        lists = []
        for t in range(tile_count):
            halves = []
            for first in range(t * listed, (t + 1) * listed, LANES):
                at = info_s[g, 3:4, first : first + LANES].astype(jnp.int32)
                at = jnp.broadcast_to(at, (ROWS, LANES))
                lane, slab = at & (LANES - 1), at >> 7
                found = jnp.zeros((ROWS, LANES), F32)
                for s in range(slabs):
                    here = jnp.take_along_axis(
                        rows[s * ROWS : (s + 1) * ROWS, :], lane, axis=1, mode="promise_in_bounds"
                    )
                    found = jnp.where(slab == s, here, found)
                halves.append(found)
            lists.append(jnp.concatenate(halves, axis=1))

        setup = []
        for t in range(tile_count):
            entry = lists[t]
            slot = (me ^ (first_group + g)) * tile_count + t
            x_0 = ((first_col + slot % 4) * side).astype(F32) + 0.5
            y_0 = ((first_row + slot // 4) * side).astype(F32) + 0.5
            quad_a, quad_b, quad_c = -0.5 * entry[2:3], -entry[3:4], -0.5 * entry[4:5]
            opacity = entry[5:6]
            dx = (step + x_0) - entry[0:1]
            dy = (step + y_0) - entry[1:2]
            adx2 = quad_a * dx * dx
            bdy = quad_b * dy
            cdy2 = quad_c * dy * dy
            setup.append((entry, quad_a, quad_b, quad_c, opacity, dx, dy))
            for row in range(side):
                at = slice(row * side, (row + 1) * side)
                power = adx2 + dx * bdy[row : row + 1] + cdy2[row : row + 1]
                bell = jnp.exp(power)
                e_s[t, at, :] = bell
                hi_s[t, at, :], lo_s[t, at, :] = split(jnp.log(1.0 - opacity * bell))

        for t in range(tile_count):
            t_s[t] = matmul(hi_s[t], earlier) + matmul(lo_s[t], earlier)

        for t in range(tile_count):
            entry, opacity = setup[t][0], setup[t][4]
            for row in range(side):
                at = slice(row * side, (row + 1) * side)
                passed = jnp.exp(t_s[t, at, :])
                t_s[t, at, :] = passed
                hi_s[t, at, :], lo_s[t, at, :] = split(opacity * e_s[t, at, :] * passed)
            c_hi, c_lo = split(entry[6:9])
            both = ((1,), (1,))
            image = (
                matmul(c_hi, hi_s[t], both)
                + matmul(c_lo, hi_s[t], both)
                + matmul(c_hi, lo_s[t], both)
            )
            here = slice(t * pixels, (t + 1) * pixels)
            if rendered is not None:

                @pl.when(g == 0)
                def _():
                    rendered[:, here] = image

            error = image - info_s[g, 0:3, here]
            g_hi, g_lo = split(error)
            first = ((0,), (0,))
            d_s[t] = (
                matmul(g_hi, c_hi, first) + matmul(g_lo, c_hi, first) + matmul(g_hi, c_lo, first)
            )
            g_colours = matmul(g_hi, hi_s[t]) + matmul(g_lo, hi_s[t]) + matmul(g_hi, lo_s[t])
            acc_s[g, t, 6:9, :] = g_colours

        for t in range(tile_count):
            opacity = setup[t][4]
            for row in range(side):
                at = slice(row * side, (row + 1) * side)
                pushed = t_s[t, at, :] * d_s[t, at, :]
                t_s[t, at, :] = pushed
                hi_s[t, at, :], lo_s[t, at, :] = split(opacity * e_s[t, at, :] * pushed)
            d_s[t] = matmul(hi_s[t], later) + matmul(lo_s[t], later)

        for t in range(tile_count):
            entry, quad_a, quad_b, quad_c, opacity, dx, dy = setup[t]
            r_0 = r_1 = r_2 = None
            for row in range(side):
                at = slice(row * side, (row + 1) * side)
                bell = e_s[t, at, :]
                flow = bell * (t_s[t, at, :] - d_s[t, at, :] / (1.0 - opacity * bell))
                one = flow * dy[row : row + 1]
                two = one * dy[row : row + 1]
                r_0 = flow if r_0 is None else r_0 + flow
                r_1 = one if r_1 is None else r_1 + one
                r_2 = two if r_2 is None else r_2 + two
            rdx = r_0 * dx
            m_00 = jnp.sum(r_0, axis=0, keepdims=True)
            m_10 = jnp.sum(rdx, axis=0, keepdims=True)
            m_20 = jnp.sum(rdx * dx, axis=0, keepdims=True)
            m_01 = jnp.sum(r_1, axis=0, keepdims=True)
            m_11 = jnp.sum(r_1 * dx, axis=0, keepdims=True)
            m_02 = jnp.sum(r_2, axis=0, keepdims=True)
            acc_s[g, t, 0:1, :] = -opacity * (2.0 * quad_a * m_10 + quad_b * m_01)
            acc_s[g, t, 1:2, :] = -opacity * (2.0 * quad_c * m_01 + quad_b * m_10)
            acc_s[g, t, 2:3, :] = -0.5 * opacity * m_20
            acc_s[g, t, 3:4, :] = -opacity * m_11
            acc_s[g, t, 4:5, :] = -0.5 * opacity * m_02
            acc_s[g, t, 5:6, :] = m_00
            acc_s[g, t, 9:16, :] = jnp.zeros((7, listed), F32)
        return carry

    lax.fori_loop(0, acc_s.shape[0], one_group, 0)


def pool_sum(slab, info_s, acc_s):
    _, tile_count, _, listed = acc_s.shape
    width = info_s.shape[2]
    rows_each = (info_s.shape[1] - 4) // tile_count
    totals = []
    for g in range(2):
        total = jnp.zeros((ROWS, LANES), F32)
        for t in range(tile_count):
            row, first = 4 + t * rows_each + slab * LANES // width, slab * LANES % width
            at = info_s[g, row : row + 1, first : first + LANES].astype(jnp.int32)
            at = jnp.broadcast_to(at, (ROWS, LANES))
            lane, half = at & (LANES - 1), at >> 7
            for h in range(listed // LANES):
                here = jnp.take_along_axis(
                    acc_s[g, t, :, h * LANES : (h + 1) * LANES],
                    lane,
                    axis=1,
                    mode="promise_in_bounds",
                )
                total = total + jnp.where(half == h, here, 0.0)
        totals.append(total)
    return totals[0] + totals[1]


def block_start(tile_id):
    within = tile_id % (TILES_X * TILES_Y)
    return (within % TILES_X) // 4 * 4, (within // TILES_X) // 2 * 2


def near_kernel(pieces, tile_ids, cams, where, own, other, *refs):
    parts = refs[:pieces]
    rendered, rows, partial, feats, info_s, *work = refs[pieces:]
    view = tile_ids[0] // (TILES_X * TILES_Y)
    cam = [cams[view, i] for i in range(12)]
    slabs = spread_features(parts, feats, parts[0].shape[0])
    projected = project_rows(lambda f: feats[f * slabs : (f + 1) * slabs, :], cam)
    for f, value in enumerate(projected):
        rows[pl.ds(f, slabs, stride=ROWS), :] = value
    zero_row = jnp.zeros((slabs, LANES), F32)
    for f in range(len(projected), ROWS):
        rows[pl.ds(f, slabs, stride=ROWS), :] = zero_row
    info_s[0] = own[...]
    info_s[1] = other[...]
    composite(block_start(tile_ids[0]), 0, where[0], rows, info_s, rendered, work)
    for s in range(slabs):
        partial[:, s * LANES : (s + 1) * LANES] = pool_sum(s, info_s, work[-1])


def far_kernel(blocks, tile_ids, where, rows, partial, infos, *refs):
    *packets, info_s = refs[: len(refs) - 6]
    work = refs[len(refs) - 6 :]
    half = infos.shape[0] // 2
    info_s[0] = infos[:half, :]
    info_s[1] = infos[half:, :]
    composite(block_start(tile_ids[0]), 2, where[0], rows, info_s, None, work)
    share = (tile_ids[0] // (TILES_X * TILES_Y)).astype(F32)
    row_of = lax.broadcasted_iota(jnp.int32, (ROWS, LANES), 0)
    lane_of = lax.broadcasted_iota(jnp.int32, (ROWS, LANES), 1)
    chunk = packets[0].shape[1]
    for s in range(rows.shape[0] // ROWS):
        total = partial[:, s * LANES : (s + 1) * LANES] + pool_sum(s, info_s, work[-1])
        if blocks == 1:
            mine = share
        else:
            column = s * LANES + lane_of
            mine = jnp.where(column % where[2] // (where[2] // blocks) == where[1], share, 0.0)
        total = jnp.where(row_of == 9, mine, total)
        packets[s * LANES // chunk][:, s * LANES % chunk : s * LANES % chunk + LANES] = total


def join_kernel(first, second, out):
    half = first.shape[0]
    out[:half, :] = first[...]
    out[half:, :] = second[...]


def update_kernel(pieces, where, cams, *refs):
    packets = refs[:pieces]
    sources, sinks = refs[pieces : pieces + 3], refs[pieces + 3 : pieces + 6]
    feats, rows, grads, held, made, in_sems, out_sems = refs[pieces + 6 :]
    params, adam_m, adam_v = held.at[0], held.at[1], held.at[2]
    features, width = params.shape
    loads = [pltpu.make_async_copy(sources[k], held.at[k], in_sems.at[k]) for k in range(3)]
    for load in loads:
        load.start()
    chunk = packets[0].shape[1]
    slabs = width // LANES
    for d in range(pieces):
        for h in range(chunk // LANES):
            slab = (where[0] ^ d) * (chunk // LANES) + h
            rows[pl.ds(slab, ROWS, stride=slabs), :] = packets[d][:, h * LANES : (h + 1) * LANES]
    pulled = [rows[f * slabs : (f + 1) * slabs, :] for f in range(10)]
    view = pulled[9]
    cam = []
    for i in range(12):
        value = jnp.full((slabs, LANES), cams[0, i], F32)
        for v in range(1, cams.shape[0]):
            value = jnp.where(view == float(v), cams[v, i], value)
        cam.append(value)

    def put(f, value):
        grads[f * slabs : (f + 1) * slabs, :] = value

    loads[0].wait()
    spread_features([params], feats, features)
    project_pull(lambda f: feats[f * slabs : (f + 1) * slabs, :], cam, pulled[:9], put)
    rate = learn_rate / (1.0 - beta_one**adam_steps)
    unbias = 1.0 / (1.0 - beta_two**adam_steps)
    loads[1].wait()
    loads[2].wait()
    stores = []
    for row in range(0, features, 8):
        count = min(8, features - row)
        for s in range(slabs):
            at = (slice(row, row + count), slice(s * LANES, (s + 1) * LANES))
            grad = grads[pl.ds(row * slabs + s, count, stride=slabs), :]
            moment = beta_one * adam_m[at] + (1.0 - beta_one) * grad
            second = beta_two * adam_v[at] + (1.0 - beta_two) * grad * grad
            made.at[1][at] = moment
            made.at[2][at] = second
            made.at[0][at] = params[at] - rate * moment / (jnp.sqrt(second * unbias) + adam_eps)
        if row % 16 == 8 or row + count == features:
            first = row // 16 * 16
            span = pl.ds(first, row + count - first)
            for k in range(3):
                store = pltpu.make_async_copy(
                    made.at[k, span], sinks[k].at[span], out_sems.at[k, first // 16]
                )
                store.start()
                stores.append(store)
    for store in stores:
        store.wait()


def vmem():
    return pl.BlockSpec(memory_space=pltpu.VMEM)


def smem():
    return pl.BlockSpec(memory_space=pltpu.SMEM)


def any_space():
    return pl.BlockSpec(memory_space=pl.ANY)


def call(kernel, name, out_shape, in_specs, scratch, args, out_specs=None):
    return pl.pallas_call(
        kernel,
        out_shape=out_shape,
        in_specs=in_specs,
        out_specs=out_specs or tuple(vmem() for _ in out_shape),
        scratch_shapes=scratch,
        compiler_params=pltpu.CompilerParams(vmem_limit_bytes=32 * 1024 * 1024),
        name=name,
    )(*args)


def work_shapes(tile_count, pixels, listed):
    square = (tile_count, pixels, listed)
    return [
        pltpu.VMEM(square, F32),
        pltpu.VMEM(square, F32),
        pltpu.VMEM(square, F32),
        pltpu.VMEM(square, BF16),
        pltpu.VMEM(square, BF16),
        pltpu.VMEM((2, tile_count, ROWS, listed), F32),
    ]


def near(tile_ids, cameras, where, own, other, parts, tile_count):
    width = sum(part.shape[1] for part in parts)
    features = parts[0].shape[0]
    slabs = width // LANES
    pixels = listed = own.shape[1] // tile_count
    return call(
        functools.partial(near_kernel, len(parts)),
        "near",
        (
            jax.ShapeDtypeStruct((3, own.shape[1]), F32),
            jax.ShapeDtypeStruct((ROWS * slabs, LANES), F32),
            jax.ShapeDtypeStruct((ROWS, width), F32),
        ),
        [smem()] * 3 + [vmem()] * (2 + len(parts)),
        [pltpu.VMEM((features * slabs, LANES), F32), pltpu.VMEM((2,) + own.shape, F32)]
        + work_shapes(tile_count, pixels, listed),
        (tile_ids, cameras, where, own, other, *parts),
    )


def far(tile_ids, where, rows, partial, infos, pieces, tile_count, blocks):
    width = partial.shape[1]
    pixels = listed = infos.shape[1] // tile_count
    info = (infos.shape[0] // 2, infos.shape[1])
    return call(
        functools.partial(far_kernel, blocks),
        "far",
        (jax.ShapeDtypeStruct((ROWS, width // pieces), F32),) * pieces,
        [smem()] * 2 + [vmem()] * 3,
        [pltpu.VMEM((2,) + info, F32)] + work_shapes(tile_count, pixels, listed),
        (tile_ids, where, rows, partial, infos),
    )


def join(first, second):
    shape = (2 * first.shape[0], first.shape[1])
    return call(
        join_kernel, "join", (jax.ShapeDtypeStruct(shape, F32),), [vmem()] * 2, [], (first, second)
    )[0]


def update(where, cameras, params, adam_m, adam_v, packets):
    features, width = params.shape
    slabs = width // LANES
    shape = jax.ShapeDtypeStruct(params.shape, F32)
    return call(
        functools.partial(update_kernel, len(packets)),
        "update",
        (shape, shape, shape),
        [smem()] * 2 + [vmem()] * len(packets) + [any_space()] * 3,
        [
            pltpu.VMEM((features * slabs, LANES), F32),
            pltpu.VMEM((ROWS * slabs, LANES), F32),
            pltpu.VMEM((features * slabs, LANES), F32),
            pltpu.VMEM((3,) + params.shape, F32),
            pltpu.VMEM((3,) + params.shape, F32),
            pltpu.SemaphoreType.DMA((3,)),
            pltpu.SemaphoreType.DMA((3, (features + 15) // 16)),
        ],
        (where, cameras, *packets, params, adam_m, adam_v),
        (any_space(),) * 3,
    )


def swap(value, axis, d):
    if d == 0:
        return value
    return lax.ppermute(value, axis, [(k, k ^ d) for k in range(lax.axis_size(axis))])


def local(params, adam_m, adam_v, cameras, target, tile_ids, hit_shard, hit_local):
    width = params.shape[1]
    tile_count, listed = hit_local.shape
    shards = lax.axis_size("gs")
    along = lax.axis_size("tile")
    chunk = width // shards
    group = lax.axis_index("gs")
    seat = lax.axis_index("tile")
    aligned = chunk % LANES == 0
    team = BLOCK_TILES // tile_count
    assert team == 4
    blocks = along // team

    info, parts = pack(group, params, target, hit_shard, hit_local, shards, aligned)
    if not aligned:
        parts = [
            lax.dynamic_slice_in_dim(params, (group ^ d) * chunk, chunk, axis=1)
            for d in range(shards)
        ]
    parts = [swap(parts[d], "gs", d) for d in range(shards)]
    beside = swap(info, "tile", 1)
    beyond = swap(join(info, beside), "tile", 2)
    if not aligned:
        parts = [jnp.concatenate(parts, axis=1)]
    where = jnp.stack([seat % team, seat // team, jnp.int32(chunk)]).astype(jnp.int32)
    rendered, rows, partial = near(tile_ids, cameras, where, info, beside, parts, tile_count)
    packets = far(tile_ids, where, rows, partial, beyond, len(parts), tile_count, blocks)
    if not aligned:
        packets = [packets[0][:, d * chunk : (d + 1) * chunk] for d in range(shards)]
    packets = [swap(packets[d], "gs", d) for d in range(shards)]
    if blocks > 1:
        packets = [block_sum(packet, along, team) for packet in packets]
    if aligned:
        own = group
    else:
        packets = [jnp.stack(packets)[jnp.arange(shards) ^ group].transpose(1, 0, 2).reshape(ROWS, -1)]
        own = jnp.int32(0)
    new_params, new_m, new_v = update(
        own.reshape(1), cameras, params, adam_m, adam_v, packets
    )
    return (rendered, new_params, new_m, new_v)


def block_sum(packet, along, team):
    step = team
    while step < along:
        packet = packet + swap(packet, "tile", step)
        step *= 2
    return packet


def solution(mesh):
    return jax.shard_map(
        local,
        mesh=mesh,
        in_specs=(
            P(None, ("groups", "gs")),
            P(None, ("groups", "gs")),
            P(None, ("groups", "gs")),
            P("groups", None),
            P(None, ("groups", "gs", "tile")),
            P(("groups", "gs", "tile")),
            P(("groups", "gs", "tile"), None, None),
            P(("groups", "gs", "tile"), None),
        ),
        out_specs=(
            P(None, ("groups", "gs", "tile")),
            P(None, ("groups", "gs")),
            P(None, ("groups", "gs")),
            P(None, ("groups", "gs")),
        ),
        check_vma=False,
    )
```

```python
import functools

import jax
import jax.numpy as jnp
from jax import lax
from jax.experimental import pallas as pl
from jax.experimental.pallas import tpu as pltpu
from jax.sharding import PartitionSpec as P

TILES_X = 120
TILES_Y = 68
TILE_SIDE = 16
BLOCK_TILES = 8
LANES = 128
ROWS = 16
F32 = jnp.float32
BF16 = jnp.bfloat16

focal_length = 1000.0
center_x = 960.0
center_y = 540.0
dilation = 0.3
beta_one = 0.9
beta_two = 0.999
learn_rate = 0.01
adam_eps = 1e-08
adam_steps = 100.0
sh_const = (
    0.28209479177387814,
    0.4886025119029199,
    1.0925484305920792,
    0.31539156525252005,
    0.5462742152960396,
    0.5900435899266435,
    2.890611442640554,
    0.4570457994644658,
    0.3731763325901154,
    1.445305721320277,
)


def sh_basis(x, y, z):
    s = sh_const
    xx, yy, zz = x * x, y * y, z * z
    return [
        None,
        -s[1] * y,
        s[1] * z,
        -s[1] * x,
        s[2] * (x * y),
        -s[2] * (y * z),
        s[3] * (2.0 * zz - xx - yy),
        -s[2] * (x * z),
        s[4] * (xx - yy),
        -s[5] * y * (3.0 * xx - yy),
        s[6] * (x * y) * z,
        -s[7] * y * (4.0 * zz - xx - yy),
        s[8] * z * (2.0 * zz - 3.0 * xx - 3.0 * yy),
        -s[7] * x * (4.0 * zz - xx - yy),
        s[9] * z * (xx - yy),
        -s[5] * x * (xx - 3.0 * yy),
    ]


def sh_pull(h, x, y, z):
    s = sh_const
    xx, yy, zz = x * x, y * y, z * z
    xy, xz, yz = x * y, x * z, y * z
    diff = xx - yy
    ring = 4.0 * zz - xx - yy
    g_x = (
        -s[1] * h[3]
        + s[2] * (h[4] * y - h[7] * z)
        - (2.0 * s[3]) * h[6] * x
        + (2.0 * s[4]) * h[8] * x
        - (6.0 * s[5]) * h[9] * xy
        + s[6] * h[10] * yz
        + (2.0 * s[7]) * h[11] * xy
        - (6.0 * s[8]) * h[12] * xz
        - s[7] * h[13] * (ring - 2.0 * xx)
        + (2.0 * s[9]) * h[14] * xz
        - (3.0 * s[5]) * h[15] * diff
    )
    g_y = (
        -s[1] * h[1]
        + s[2] * (h[4] * x - h[5] * z)
        - (2.0 * s[3]) * h[6] * y
        - (2.0 * s[4]) * h[8] * y
        - (3.0 * s[5]) * h[9] * diff
        + s[6] * h[10] * xz
        - s[7] * h[11] * (ring - 2.0 * yy)
        - (6.0 * s[8]) * h[12] * yz
        + (2.0 * s[7]) * h[13] * xy
        - (2.0 * s[9]) * h[14] * yz
        + (6.0 * s[5]) * h[15] * xy
    )
    g_z = (
        s[1] * h[2]
        - s[2] * (h[5] * y + h[7] * x)
        + (4.0 * s[3]) * h[6] * z
        + s[6] * h[10] * xy
        - (8.0 * s[7]) * (h[11] * yz + h[13] * xz)
        + s[8] * h[12] * (6.0 * zz - 3.0 * xx - 3.0 * yy)
        + s[9] * h[14] * diff
    )
    return g_x, g_y, g_z


def project_parts(feat, cam):
    rot = [[cam[3 * r + c] for c in range(3)] for r in range(3)]
    off = [feat(a) - cam[9 + a] for a in range(3)]
    in_cam = [rot[r][0] * off[0] + rot[r][1] * off[1] + rot[r][2] * off[2] for r in range(3)]
    inv = 1.0 / in_cam[2]
    u = in_cam[0] * inv
    v = in_cam[1] * inv
    finv = focal_length * inv
    scale = [jnp.exp(2.0 * feat(3 + a)) for a in range(3)]
    quat = [feat(6 + a) for a in range(4)]
    rnorm = lax.rsqrt(quat[0] * quat[0] + quat[1] * quat[1] + quat[2] * quat[2] + quat[3] * quat[3])
    w, x, y, z = [q * rnorm for q in quat]
    turn = [
        [1.0 - 2.0 * (y * y + z * z), 2.0 * (x * y - w * z), 2.0 * (x * z + w * y)],
        [2.0 * (x * y + w * z), 1.0 - 2.0 * (x * x + z * z), 2.0 * (y * z - w * x)],
        [2.0 * (x * z - w * y), 2.0 * (y * z + w * x), 1.0 - 2.0 * (x * x + y * y)],
    ]
    screen = [
        [finv * (rot[0][c] - u * rot[2][c]) for c in range(3)],
        [finv * (rot[1][c] - v * rot[2][c]) for c in range(3)],
    ]
    axes = [
        [sum(screen[r][c] * turn[c][k] for c in range(3)) for k in range(3)] for r in range(2)
    ]
    wide = [[axes[r][k] * scale[k] for k in range(3)] for r in range(2)]
    cov_xx = sum(wide[0][k] * axes[0][k] for k in range(3)) + dilation
    cov_xy = sum(wide[0][k] * axes[1][k] for k in range(3))
    cov_yy = sum(wide[1][k] * axes[1][k] for k in range(3)) + dilation
    rdet = 1.0 / (cov_xx * cov_yy - cov_xy * cov_xy)
    conic = (cov_yy * rdet, -cov_xy * rdet, cov_xx * rdet)
    opacity = 1.0 / (1.0 + jnp.exp(-feat(10)))
    rlen = lax.rsqrt(off[0] * off[0] + off[1] * off[1] + off[2] * off[2])
    way = [off[a] * rlen for a in range(3)]
    return dict(
        rot=rot, inv=inv, u=u, v=v, finv=finv, scale=scale, rnorm=rnorm, rotor=(w, x, y, z), turn=turn,
        screen=screen, axes=axes, wide=wide, conic=conic, opacity=opacity, rlen=rlen, way=way,
    )


def project_rows(feat, cam):
    part = project_parts(feat, cam)
    basis = sh_basis(*part["way"])
    colours = []
    for k in range(3):
        total = 0.5 + sh_const[0] * feat(11 + 16 * k)
        for b in range(1, 16):
            total = total + feat(11 + 16 * k + b) * basis[b]
        colours.append(total)
    mean_x = focal_length * part["u"] + center_x
    mean_y = focal_length * part["v"] + center_y
    return [mean_x, mean_y, *part["conic"], part["opacity"], *colours]


def project_pull(feat, cam, grads, put):
    part = project_parts(feat, cam)
    g_mx, g_my, g_a, g_b, g_c, g_o = grads[:6]
    g_col = grads[6:9]
    way, rlen = part["way"], part["rlen"]
    basis = sh_basis(*way)
    pulled = [None]
    for k in range(3):
        put(11 + 16 * k, sh_const[0] * g_col[k])
    for b in range(1, 16):
        total = 0.0
        for k in range(3):
            put(11 + 16 * k + b, g_col[k] * basis[b])
            total = total + g_col[k] * feat(11 + 16 * k + b)
        pulled.append(total)
    g_way = sh_pull(pulled, *way)
    along = way[0] * g_way[0] + way[1] * g_way[1] + way[2] * g_way[2]
    g_off = [(g_way[a] - way[a] * along) * rlen for a in range(3)]
    put(10, g_o * part["opacity"] * (1.0 - part["opacity"]))
    a, b, c = part["conic"]
    g_xx = -(a * a * g_a + a * b * g_b + b * b * g_c)
    g_xy = -(2.0 * a * b * g_a + (a * c + b * b) * g_b + 2.0 * b * c * g_c)
    g_yy = -(b * b * g_a + b * c * g_b + c * c * g_c)
    axes, wide, turn, screen = part["axes"], part["wide"], part["turn"], part["screen"]
    for k in range(3):
        g_scale = (
            g_xx * axes[0][k] * wide[0][k]
            + g_xy * axes[0][k] * wide[1][k]
            + g_yy * axes[1][k] * wide[1][k]
        )
        put(3 + k, 2.0 * g_scale)
    g_axes = [
        [2.0 * g_xx * wide[0][k] + g_xy * wide[1][k] for k in range(3)],
        [2.0 * g_yy * wide[1][k] + g_xy * wide[0][k] for k in range(3)],
    ]
    g_screen = [
        [sum(g_axes[r][k] * turn[c][k] for k in range(3)) for c in range(3)] for r in range(2)
    ]
    gm = [
        [g_axes[0][k] * screen[0][c] + g_axes[1][k] * screen[1][c] for k in range(3)]
        for c in range(3)
    ]
    w, x, y, z = part["rotor"]
    up_xy, up_xz, up_yz = gm[0][1] + gm[1][0], gm[0][2] + gm[2][0], gm[1][2] + gm[2][1]
    un_xy, un_xz, un_yz = gm[1][0] - gm[0][1], gm[0][2] - gm[2][0], gm[2][1] - gm[1][2]
    g_rotor = [
        2.0 * (z * un_xy + y * un_xz + x * un_yz),
        2.0 * (y * up_xy + z * up_xz + w * un_yz - 2.0 * x * (gm[1][1] + gm[2][2])),
        2.0 * (x * up_xy + z * up_yz + w * un_xz - 2.0 * y * (gm[0][0] + gm[2][2])),
        2.0 * (x * up_xz + y * up_yz + w * un_xy - 2.0 * z * (gm[0][0] + gm[1][1])),
    ]
    rotor = (w, x, y, z)
    along = sum(rotor[i] * g_rotor[i] for i in range(4))
    for i in range(4):
        put(6 + i, (g_rotor[i] - rotor[i] * along) * part["rnorm"])
    rot, inv, finv, u, v = part["rot"], part["inv"], part["finv"], part["u"], part["v"]
    g_u = focal_length * g_mx - finv * sum(g_screen[0][c] * rot[2][c] for c in range(3))
    g_v = focal_length * g_my - finv * sum(g_screen[1][c] * rot[2][c] for c in range(3))
    g_f = sum(g_screen[r][c] * screen[r][c] for r in range(2) for c in range(3))
    g_in = [g_u * inv, g_v * inv, -(g_f + g_u * u + g_v * v) * inv]
    for axis in range(3):
        put(
            axis,
            g_off[axis] + rot[0][axis] * g_in[0] + rot[1][axis] * g_in[1] + rot[2][axis] * g_in[2],
        )


def split(value):
    high = value.astype(BF16)
    return high, (value - high.astype(F32)).astype(BF16)


def matmul(a, b, dims=((1,), (0,))):
    return lax.dot_general(a, b, (dims, ((), ())), preferred_element_type=F32)


def spread_features(parts, scratch, count):
    tiles = sum(part.shape[1] for part in parts) // LANES
    at = 0
    for part in parts:
        for first in range(0, part.shape[1], LANES):
            for row in range(0, count, 8):
                rows = min(8, count - row)
                scratch[pl.ds(row * tiles + at, rows, stride=tiles), :] = part[
                    row : row + rows, first : first + LANES
                ]
            at += 1
    return tiles


def pack_kernel(shards, pieces, where, *refs):
    sources, refs = refs[: 3 + (pieces > 0)], refs[3 + (pieces > 0) :]
    info, parts, refs = refs[0], refs[1 : 1 + pieces], refs[1 + pieces :]
    shard_of, local_of, goal, place_s, sems, cut_sems = refs
    group = where[0]
    loads = [
        pltpu.make_async_copy(source, held, sems.at[k])
        for k, (source, held) in enumerate(zip(sources, (shard_of, local_of, goal)))
    ]
    for d in range(pieces):
        chunk = parts[d].shape[1]
        first = pl.multiple_of((group ^ d) * chunk, LANES)
        loads.append(
            pltpu.make_async_copy(sources[3].at[:, pl.ds(first, chunk)], parts[d], cut_sems.at[d])
        )
    for load in loads:
        load.start()
    for load in loads[:3]:
        load.wait()
    width = info.shape[1]
    tile_count, listed = local_of.shape
    rows_each = (info.shape[0] - 4) // tile_count
    columns = rows_each * width
    chunk = columns // shards
    info[0:3, :] = goal[...]
    for t in range(tile_count):
        place = (shard_of[t] ^ group) * chunk + (local_of[t : t + 1, :] - group * chunk)
        info[3:4, t * listed : (t + 1) * listed] = place.astype(F32)
        row_i = lax.broadcasted_iota(jnp.int32, (LANES, LANES), 0)
        col_i = lax.broadcasted_iota(jnp.int32, (LANES, LANES), 1)
        for first in range(0, listed, LANES):
            spread = jnp.broadcast_to(place[:, first : first + LANES].astype(F32), (LANES, LANES))
            place_s[first : first + LANES, :] = jnp.broadcast_to(
                jnp.sum(jnp.where(row_i == col_i, spread, 0.0), axis=1, keepdims=True), (LANES, LANES)
            )
        lane_of = lax.broadcasted_iota(jnp.int32, (8, LANES), 1).astype(F32)
        row_of = lax.broadcasted_iota(jnp.int32, (8, LANES), 0).astype(F32)
        for s in range(columns // LANES):
            best = jnp.full((8, LANES), -1.0, F32)
            column = lane_of + float(s * LANES)
            for first in range(0, listed, 8):
                best = jnp.where(
                    place_s[first : first + 8, :] == column, row_of + float(first), best
                )
            best = jnp.max(best, axis=0, keepdims=True)
            row, at = 4 + t * rows_each + s * LANES // width, s * LANES % width
            info[row : row + 1, at : at + LANES] = best
    for load in loads[3:]:
        load.wait()


def pack(group, params, target, hit_shard, hit_local, shards, aligned):
    features, columns = params.shape
    tile_count, listed = hit_local.shape
    width = target.shape[1]
    rows = 4 + tile_count * (columns // width)
    pieces = shards if aligned else 0
    piece = jax.ShapeDtypeStruct((features, columns // shards), F32)
    args = (hit_shard.reshape(tile_count, 1, listed), hit_local, target) + (params,) * aligned
    out = call(
        functools.partial(pack_kernel, shards, pieces),
        "pack",
        (jax.ShapeDtypeStruct((rows, width), F32),) + (piece,) * pieces,
        [smem()] + [pl.BlockSpec(memory_space=pltpu.HBM)] * len(args),
        [
            pltpu.VMEM((tile_count, 1, listed), jnp.int32),
            pltpu.VMEM((tile_count, listed), jnp.int32),
            pltpu.VMEM(target.shape, F32),
            pltpu.VMEM((listed, LANES), F32),
            pltpu.SemaphoreType.DMA((3,)),
            pltpu.SemaphoreType.DMA((shards,)),
        ],
        (group.reshape(1),) + tuple(pltpu.with_memory_space_constraint(a, pltpu.HBM) for a in args),
    )
    return out[0], list(out[1:])


def composite(tiles, first_group, me, rows, info_s, rendered, work):
    e_s, t_s, d_s, hi_s, lo_s, acc_s = work
    tile_count, pixels, listed = e_s.shape
    slabs = rows.shape[0] // ROWS
    side = TILE_SIDE
    first_col, first_row = tiles
    row_i = lax.broadcasted_iota(jnp.int32, (listed, listed), 0)
    col_i = lax.broadcasted_iota(jnp.int32, (listed, listed), 1)
    earlier = jnp.where(row_i < col_i, 1.0, 0.0).astype(BF16)
    later = jnp.where(row_i > col_i, 1.0, 0.0).astype(BF16)
    step = lax.broadcasted_iota(jnp.int32, (side, listed), 0).astype(F32)

    def one_group(g, carry):
        lists = []
        for t in range(tile_count):
            halves = []
            for first in range(t * listed, (t + 1) * listed, LANES):
                at = info_s[g, 3:4, first : first + LANES].astype(jnp.int32)
                at = jnp.broadcast_to(at, (ROWS, LANES))
                lane, slab = at & (LANES - 1), at >> 7
                found = jnp.zeros((ROWS, LANES), F32)
                for s in range(slabs):
                    here = jnp.take_along_axis(
                        rows[s * ROWS : (s + 1) * ROWS, :], lane, axis=1, mode="promise_in_bounds"
                    )
                    found = jnp.where(slab == s, here, found)
                halves.append(found)
            lists.append(jnp.concatenate(halves, axis=1))

        setup = []
        for t in range(tile_count):
            entry = lists[t]
            slot = (me ^ (first_group + g)) * tile_count + t
            x_0 = ((first_col + slot % 4) * side).astype(F32) + 0.5
            y_0 = ((first_row + slot // 4) * side).astype(F32) + 0.5
            quad_a, quad_b, quad_c = -0.5 * entry[2:3], -entry[3:4], -0.5 * entry[4:5]
            opacity = entry[5:6]
            dx = (step + x_0) - entry[0:1]
            dy = (step + y_0) - entry[1:2]
            adx2 = quad_a * dx * dx
            bdy = quad_b * dy
            cdy2 = quad_c * dy * dy
            setup.append((entry, quad_a, quad_b, quad_c, opacity, dx, dy))
            for row in range(side):
                at = slice(row * side, (row + 1) * side)
                power = adx2 + dx * bdy[row : row + 1] + cdy2[row : row + 1]
                bell = jnp.exp(power)
                e_s[t, at, :] = bell
                hi_s[t, at, :], lo_s[t, at, :] = split(jnp.log(1.0 - opacity * bell))

        for t in range(tile_count):
            t_s[t] = matmul(hi_s[t], earlier) + matmul(lo_s[t], earlier)

        for t in range(tile_count):
            entry, opacity = setup[t][0], setup[t][4]
            for row in range(side):
                at = slice(row * side, (row + 1) * side)
                passed = jnp.exp(t_s[t, at, :])
                t_s[t, at, :] = passed
                hi_s[t, at, :], lo_s[t, at, :] = split(opacity * e_s[t, at, :] * passed)
            c_hi, c_lo = split(entry[6:9])
            both = ((1,), (1,))
            image = (
                matmul(c_hi, hi_s[t], both)
                + matmul(c_lo, hi_s[t], both)
                + matmul(c_hi, lo_s[t], both)
            )
            here = slice(t * pixels, (t + 1) * pixels)
            if rendered is not None:

                @pl.when(g == 0)
                def _():
                    rendered[:, here] = image

            error = image - info_s[g, 0:3, here]
            g_hi, g_lo = split(error)
            first = ((0,), (0,))
            d_s[t] = (
                matmul(g_hi, c_hi, first) + matmul(g_lo, c_hi, first) + matmul(g_hi, c_lo, first)
            )
            g_colours = matmul(g_hi, hi_s[t]) + matmul(g_lo, hi_s[t]) + matmul(g_hi, lo_s[t])
            acc_s[g, t, 6:9, :] = g_colours

        for t in range(tile_count):
            opacity = setup[t][4]
            for row in range(side):
                at = slice(row * side, (row + 1) * side)
                pushed = t_s[t, at, :] * d_s[t, at, :]
                t_s[t, at, :] = pushed
                hi_s[t, at, :], lo_s[t, at, :] = split(opacity * e_s[t, at, :] * pushed)
            d_s[t] = matmul(hi_s[t], later) + matmul(lo_s[t], later)

        for t in range(tile_count):
            entry, quad_a, quad_b, quad_c, opacity, dx, dy = setup[t]
            r_0 = r_1 = r_2 = None
            for row in range(side):
                at = slice(row * side, (row + 1) * side)
                bell = e_s[t, at, :]
                flow = bell * (t_s[t, at, :] - d_s[t, at, :] / (1.0 - opacity * bell))
                one = flow * dy[row : row + 1]
                two = one * dy[row : row + 1]
                r_0 = flow if r_0 is None else r_0 + flow
                r_1 = one if r_1 is None else r_1 + one
                r_2 = two if r_2 is None else r_2 + two
            rdx = r_0 * dx
            m_00 = jnp.sum(r_0, axis=0, keepdims=True)
            m_10 = jnp.sum(rdx, axis=0, keepdims=True)
            m_20 = jnp.sum(rdx * dx, axis=0, keepdims=True)
            m_01 = jnp.sum(r_1, axis=0, keepdims=True)
            m_11 = jnp.sum(r_1 * dx, axis=0, keepdims=True)
            m_02 = jnp.sum(r_2, axis=0, keepdims=True)
            acc_s[g, t, 0:1, :] = -opacity * (2.0 * quad_a * m_10 + quad_b * m_01)
            acc_s[g, t, 1:2, :] = -opacity * (2.0 * quad_c * m_01 + quad_b * m_10)
            acc_s[g, t, 2:3, :] = -0.5 * opacity * m_20
            acc_s[g, t, 3:4, :] = -opacity * m_11
            acc_s[g, t, 4:5, :] = -0.5 * opacity * m_02
            acc_s[g, t, 5:6, :] = m_00
            acc_s[g, t, 9:16, :] = jnp.zeros((7, listed), F32)
        return carry

    lax.fori_loop(0, acc_s.shape[0], one_group, 0)


def pool_sum(slab, info_s, acc_s):
    _, tile_count, _, listed = acc_s.shape
    width = info_s.shape[2]
    rows_each = (info_s.shape[1] - 4) // tile_count
    totals = []
    for g in range(2):
        total = jnp.zeros((ROWS, LANES), F32)
        for t in range(tile_count):
            row, first = 4 + t * rows_each + slab * LANES // width, slab * LANES % width
            at = info_s[g, row : row + 1, first : first + LANES].astype(jnp.int32)
            at = jnp.broadcast_to(at, (ROWS, LANES))
            lane, half = at & (LANES - 1), at >> 7
            for h in range(listed // LANES):
                here = jnp.take_along_axis(
                    acc_s[g, t, :, h * LANES : (h + 1) * LANES],
                    lane,
                    axis=1,
                    mode="promise_in_bounds",
                )
                total = total + jnp.where(half == h, here, 0.0)
        totals.append(total)
    return totals[0] + totals[1]


def block_start(tile_id):
    within = tile_id % (TILES_X * TILES_Y)
    return (within % TILES_X) // 4 * 4, (within // TILES_X) // 2 * 2


def near_kernel(pieces, tile_ids, cams, where, own, other, *refs):
    parts = refs[:pieces]
    rendered, rows, partial, feats, info_s, *work = refs[pieces:]
    view = tile_ids[0] // (TILES_X * TILES_Y)
    cam = [cams[view, i] for i in range(12)]
    slabs = spread_features(parts, feats, parts[0].shape[0])
    projected = project_rows(lambda f: feats[f * slabs : (f + 1) * slabs, :], cam)
    for f, value in enumerate(projected):
        rows[pl.ds(f, slabs, stride=ROWS), :] = value
    zero_row = jnp.zeros((slabs, LANES), F32)
    for f in range(len(projected), ROWS):
        rows[pl.ds(f, slabs, stride=ROWS), :] = zero_row
    info_s[0] = own[...]
    info_s[1] = other[...]
    composite(block_start(tile_ids[0]), 0, where[0], rows, info_s, rendered, work)
    for s in range(slabs):
        partial[:, s * LANES : (s + 1) * LANES] = pool_sum(s, info_s, work[-1])


def far_kernel(blocks, tile_ids, where, rows, partial, infos, *refs):
    *packets, info_s = refs[: len(refs) - 6]
    work = refs[len(refs) - 6 :]
    half = infos.shape[0] // 2
    info_s[0] = infos[:half, :]
    info_s[1] = infos[half:, :]
    composite(block_start(tile_ids[0]), 2, where[0], rows, info_s, None, work)
    share = (tile_ids[0] // (TILES_X * TILES_Y)).astype(F32)
    row_of = lax.broadcasted_iota(jnp.int32, (ROWS, LANES), 0)
    lane_of = lax.broadcasted_iota(jnp.int32, (ROWS, LANES), 1)
    chunk = packets[0].shape[1]
    for s in range(rows.shape[0] // ROWS):
        total = partial[:, s * LANES : (s + 1) * LANES] + pool_sum(s, info_s, work[-1])
        if blocks == 1:
            mine = share
        else:
            column = s * LANES + lane_of
            mine = jnp.where(column % where[2] // (where[2] // blocks) == where[1], share, 0.0)
        total = jnp.where(row_of == 9, mine, total)
        packets[s * LANES // chunk][:, s * LANES % chunk : s * LANES % chunk + LANES] = total


def join_kernel(first, second, out):
    half = first.shape[0]
    out[:half, :] = first[...]
    out[half:, :] = second[...]


def update_kernel(pieces, where, cams, *refs):
    packets = refs[:pieces]
    sources, sinks = refs[pieces : pieces + 3], refs[pieces + 3 : pieces + 6]
    feats, rows, grads, held, made, in_sems, out_sems = refs[pieces + 6 :]
    params, adam_m, adam_v = held.at[0], held.at[1], held.at[2]
    features, width = params.shape
    loads = [pltpu.make_async_copy(sources[k], held.at[k], in_sems.at[k]) for k in range(3)]
    for load in loads:
        load.start()
    chunk = packets[0].shape[1]
    slabs = width // LANES
    for d in range(pieces):
        for h in range(chunk // LANES):
            slab = (where[0] ^ d) * (chunk // LANES) + h
            rows[pl.ds(slab, ROWS, stride=slabs), :] = packets[d][:, h * LANES : (h + 1) * LANES]
    pulled = [rows[f * slabs : (f + 1) * slabs, :] for f in range(10)]
    view = pulled[9]
    cam = []
    for i in range(12):
        value = jnp.full((slabs, LANES), cams[0, i], F32)
        for v in range(1, cams.shape[0]):
            value = jnp.where(view == float(v), cams[v, i], value)
        cam.append(value)

    def put(f, value):
        grads[f * slabs : (f + 1) * slabs, :] = value

    loads[0].wait()
    spread_features([params], feats, features)
    project_pull(lambda f: feats[f * slabs : (f + 1) * slabs, :], cam, pulled[:9], put)
    rate = learn_rate / (1.0 - beta_one**adam_steps)
    unbias = 1.0 / (1.0 - beta_two**adam_steps)
    loads[1].wait()
    loads[2].wait()
    stores = []
    for row in range(0, features, 8):
        count = min(8, features - row)
        for s in range(slabs):
            at = (slice(row, row + count), slice(s * LANES, (s + 1) * LANES))
            grad = grads[pl.ds(row * slabs + s, count, stride=slabs), :]
            moment = beta_one * adam_m[at] + (1.0 - beta_one) * grad
            second = beta_two * adam_v[at] + (1.0 - beta_two) * grad * grad
            made.at[1][at] = moment
            made.at[2][at] = second
            made.at[0][at] = params[at] - rate * moment / (jnp.sqrt(second * unbias) + adam_eps)
        if row % 16 == 8 or row + count == features:
            first = row // 16 * 16
            span = pl.ds(first, row + count - first)
            for k in range(3):
                store = pltpu.make_async_copy(
                    made.at[k, span], sinks[k].at[span], out_sems.at[k, first // 16]
                )
                store.start()
                stores.append(store)
    for store in stores:
        store.wait()


def vmem():
    return pl.BlockSpec(memory_space=pltpu.VMEM)


def smem():
    return pl.BlockSpec(memory_space=pltpu.SMEM)


def any_space():
    return pl.BlockSpec(memory_space=pl.ANY)


def call(kernel, name, out_shape, in_specs, scratch, args, out_specs=None, grant=32):
    return pl.pallas_call(
        kernel,
        out_shape=out_shape,
        in_specs=in_specs,
        out_specs=out_specs or tuple(vmem() for _ in out_shape),
        scratch_shapes=scratch,
        compiler_params=pltpu.CompilerParams(vmem_limit_bytes=grant * 1024 * 1024),
        name=name,
    )(*args)


def work_shapes(tile_count, pixels, listed):
    square = (tile_count, pixels, listed)
    return [
        pltpu.VMEM(square, F32),
        pltpu.VMEM(square, F32),
        pltpu.VMEM(square, F32),
        pltpu.VMEM(square, BF16),
        pltpu.VMEM(square, BF16),
        pltpu.VMEM((2, tile_count, ROWS, listed), F32),
    ]


def near(tile_ids, cameras, where, own, other, parts, tile_count):
    width = sum(part.shape[1] for part in parts)
    features = parts[0].shape[0]
    slabs = width // LANES
    pixels = listed = own.shape[1] // tile_count
    return call(
        functools.partial(near_kernel, len(parts)),
        "near",
        (
            jax.ShapeDtypeStruct((3, own.shape[1]), F32),
            jax.ShapeDtypeStruct((ROWS * slabs, LANES), F32),
            jax.ShapeDtypeStruct((ROWS, width), F32),
        ),
        [smem()] * 3 + [vmem()] * (2 + len(parts)),
        [pltpu.VMEM((features * slabs, LANES), F32), pltpu.VMEM((2,) + own.shape, F32)]
        + work_shapes(tile_count, pixels, listed),
        (tile_ids, cameras, where, own, other, *parts),
    )


def far(tile_ids, where, rows, partial, infos, pieces, tile_count, blocks):
    width = partial.shape[1]
    pixels = listed = infos.shape[1] // tile_count
    info = (infos.shape[0] // 2, infos.shape[1])
    return call(
        functools.partial(far_kernel, blocks),
        "far",
        (jax.ShapeDtypeStruct((ROWS, width // pieces), F32),) * pieces,
        [smem()] * 2 + [vmem()] * 3,
        [pltpu.VMEM((2,) + info, F32)] + work_shapes(tile_count, pixels, listed),
        (tile_ids, where, rows, partial, infos),
    )


def join(first, second):
    shape = (2 * first.shape[0], first.shape[1])
    return call(
        join_kernel, "join", (jax.ShapeDtypeStruct(shape, F32),), [vmem()] * 2, [], (first, second)
    )[0]


def update(where, cameras, params, adam_m, adam_v, packets):
    features, width = params.shape
    slabs = width // LANES
    shape = jax.ShapeDtypeStruct(params.shape, F32)
    return call(
        functools.partial(update_kernel, len(packets)),
        "update",
        (shape, shape, shape),
        [smem()] * 2 + [vmem()] * len(packets) + [any_space()] * 3,
        [
            pltpu.VMEM((features * slabs, LANES), F32),
            pltpu.VMEM((ROWS * slabs, LANES), F32),
            pltpu.VMEM((features * slabs, LANES), F32),
            pltpu.VMEM((3,) + params.shape, F32),
            pltpu.VMEM((3,) + params.shape, F32),
            pltpu.SemaphoreType.DMA((3,)),
            pltpu.SemaphoreType.DMA((3, (features + 15) // 16)),
        ],
        (where, cameras, *packets, params, adam_m, adam_v),
        (any_space(),) * 3,
    )


def swap(value, axis, d):
    if d == 0:
        return value
    return lax.ppermute(value, axis, [(k, k ^ d) for k in range(lax.axis_size(axis))])


def local(params, adam_m, adam_v, cameras, target, tile_ids, hit_shard, hit_local):
    width = params.shape[1]
    tile_count, listed = hit_local.shape
    shards = lax.axis_size("gs")
    along = lax.axis_size("tile")
    chunk = width // shards
    group = lax.axis_index("gs")
    seat = lax.axis_index("tile")
    aligned = chunk % LANES == 0
    team = BLOCK_TILES // tile_count
    assert team == 4
    blocks = along // team

    info, parts = pack(group, params, target, hit_shard, hit_local, shards, aligned)
    if not aligned:
        parts = [
            lax.dynamic_slice_in_dim(params, (group ^ d) * chunk, chunk, axis=1)
            for d in range(shards)
        ]
    parts = [swap(parts[d], "gs", d) for d in range(shards)]
    beside = swap(info, "tile", 1)
    beyond = swap(join(info, beside), "tile", 2)
    if not aligned:
        parts = [jnp.concatenate(parts, axis=1)]
    where = jnp.stack([seat % team, seat // team, jnp.int32(chunk)]).astype(jnp.int32)
    rendered, rows, partial = near(tile_ids, cameras, where, info, beside, parts, tile_count)
    packets = far(tile_ids, where, rows, partial, beyond, len(parts), tile_count, blocks)
    if not aligned:
        packets = [packets[0][:, d * chunk : (d + 1) * chunk] for d in range(shards)]
    packets = [swap(packets[d], "gs", d) for d in range(shards)]
    if blocks > 1:
        packets = [block_sum(packet, along, team) for packet in packets]
    if aligned:
        own = group
    else:
        packets = [jnp.stack(packets)[jnp.arange(shards) ^ group].transpose(1, 0, 2).reshape(ROWS, -1)]
        own = jnp.int32(0)
    new_params, new_m, new_v = update(
        own.reshape(1), cameras, params, adam_m, adam_v, packets
    )
    return (rendered, new_params, new_m, new_v)


def block_sum(packet, along, team):
    step = team
    while step < along:
        packet = packet + swap(packet, "tile", step)
        step *= 2
    return packet


def solution(mesh):
    return jax.shard_map(
        local,
        mesh=mesh,
        in_specs=(
            P(None, ("groups", "gs")),
            P(None, ("groups", "gs")),
            P(None, ("groups", "gs")),
            P("groups", None),
            P(None, ("groups", "gs", "tile")),
            P(("groups", "gs", "tile")),
            P(("groups", "gs", "tile"), None, None),
            P(("groups", "gs", "tile"), None),
        ),
        out_specs=(
            P(None, ("groups", "gs", "tile")),
            P(None, ("groups", "gs")),
            P(None, ("groups", "gs")),
            P(None, ("groups", "gs")),
        ),
        check_vma=False,
    )
```

```python
import functools

import jax
import jax.numpy as jnp
from jax import lax
from jax.experimental import pallas as pl
from jax.experimental.pallas import tpu as pltpu
from jax.sharding import PartitionSpec as P

TILES_X = 120
TILES_Y = 68
TILE_SIDE = 16
BLOCK_TILES = 8
LANES = 128
ROWS = 16
F32 = jnp.float32
BF16 = jnp.bfloat16

focal_length = 1000.0
center_x = 960.0
center_y = 540.0
dilation = 0.3
beta_one = 0.9
beta_two = 0.999
learn_rate = 0.01
adam_eps = 1e-08
adam_steps = 100.0
sh_const = (
    0.28209479177387814,
    0.4886025119029199,
    1.0925484305920792,
    0.31539156525252005,
    0.5462742152960396,
    0.5900435899266435,
    2.890611442640554,
    0.4570457994644658,
    0.3731763325901154,
    1.445305721320277,
)


def sh_basis(x, y, z):
    s = sh_const
    xx, yy, zz = x * x, y * y, z * z
    return [
        None,
        -s[1] * y,
        s[1] * z,
        -s[1] * x,
        s[2] * (x * y),
        -s[2] * (y * z),
        s[3] * (2.0 * zz - xx - yy),
        -s[2] * (x * z),
        s[4] * (xx - yy),
        -s[5] * y * (3.0 * xx - yy),
        s[6] * (x * y) * z,
        -s[7] * y * (4.0 * zz - xx - yy),
        s[8] * z * (2.0 * zz - 3.0 * xx - 3.0 * yy),
        -s[7] * x * (4.0 * zz - xx - yy),
        s[9] * z * (xx - yy),
        -s[5] * x * (xx - 3.0 * yy),
    ]


def sh_pull(h, x, y, z):
    s = sh_const
    xx, yy, zz = x * x, y * y, z * z
    xy, xz, yz = x * y, x * z, y * z
    diff = xx - yy
    ring = 4.0 * zz - xx - yy
    g_x = (
        -s[1] * h[3]
        + s[2] * (h[4] * y - h[7] * z)
        - (2.0 * s[3]) * h[6] * x
        + (2.0 * s[4]) * h[8] * x
        - (6.0 * s[5]) * h[9] * xy
        + s[6] * h[10] * yz
        + (2.0 * s[7]) * h[11] * xy
        - (6.0 * s[8]) * h[12] * xz
        - s[7] * h[13] * (ring - 2.0 * xx)
        + (2.0 * s[9]) * h[14] * xz
        - (3.0 * s[5]) * h[15] * diff
    )
    g_y = (
        -s[1] * h[1]
        + s[2] * (h[4] * x - h[5] * z)
        - (2.0 * s[3]) * h[6] * y
        - (2.0 * s[4]) * h[8] * y
        - (3.0 * s[5]) * h[9] * diff
        + s[6] * h[10] * xz
        - s[7] * h[11] * (ring - 2.0 * yy)
        - (6.0 * s[8]) * h[12] * yz
        + (2.0 * s[7]) * h[13] * xy
        - (2.0 * s[9]) * h[14] * yz
        + (6.0 * s[5]) * h[15] * xy
    )
    g_z = (
        s[1] * h[2]
        - s[2] * (h[5] * y + h[7] * x)
        + (4.0 * s[3]) * h[6] * z
        + s[6] * h[10] * xy
        - (8.0 * s[7]) * (h[11] * yz + h[13] * xz)
        + s[8] * h[12] * (6.0 * zz - 3.0 * xx - 3.0 * yy)
        + s[9] * h[14] * diff
    )
    return g_x, g_y, g_z


def project_parts(feat, cam):
    rot = [[cam[3 * r + c] for c in range(3)] for r in range(3)]
    off = [feat(a) - cam[9 + a] for a in range(3)]
    in_cam = [rot[r][0] * off[0] + rot[r][1] * off[1] + rot[r][2] * off[2] for r in range(3)]
    inv = 1.0 / in_cam[2]
    u = in_cam[0] * inv
    v = in_cam[1] * inv
    finv = focal_length * inv
    scale = [jnp.exp(2.0 * feat(3 + a)) for a in range(3)]
    quat = [feat(6 + a) for a in range(4)]
    rnorm = lax.rsqrt(quat[0] * quat[0] + quat[1] * quat[1] + quat[2] * quat[2] + quat[3] * quat[3])
    w, x, y, z = [q * rnorm for q in quat]
    turn = [
        [1.0 - 2.0 * (y * y + z * z), 2.0 * (x * y - w * z), 2.0 * (x * z + w * y)],
        [2.0 * (x * y + w * z), 1.0 - 2.0 * (x * x + z * z), 2.0 * (y * z - w * x)],
        [2.0 * (x * z - w * y), 2.0 * (y * z + w * x), 1.0 - 2.0 * (x * x + y * y)],
    ]
    screen = [
        [finv * (rot[0][c] - u * rot[2][c]) for c in range(3)],
        [finv * (rot[1][c] - v * rot[2][c]) for c in range(3)],
    ]
    axes = [
        [sum(screen[r][c] * turn[c][k] for c in range(3)) for k in range(3)] for r in range(2)
    ]
    wide = [[axes[r][k] * scale[k] for k in range(3)] for r in range(2)]
    cov_xx = sum(wide[0][k] * axes[0][k] for k in range(3)) + dilation
    cov_xy = sum(wide[0][k] * axes[1][k] for k in range(3))
    cov_yy = sum(wide[1][k] * axes[1][k] for k in range(3)) + dilation
    rdet = 1.0 / (cov_xx * cov_yy - cov_xy * cov_xy)
    conic = (cov_yy * rdet, -cov_xy * rdet, cov_xx * rdet)
    rlen = lax.rsqrt(off[0] * off[0] + off[1] * off[1] + off[2] * off[2])
    way = [off[a] * rlen for a in range(3)]
    return dict(
        rot=rot, inv=inv, u=u, v=v, finv=finv, scale=scale, rnorm=rnorm, rotor=(w, x, y, z), turn=turn,
        screen=screen, axes=axes, wide=wide, conic=conic, rlen=rlen, way=way,
    )


def project_rows(feat, cam):
    part = project_parts(feat, cam)
    basis = sh_basis(*part["way"])
    colours = []
    for k in range(3):
        total = 0.5 + sh_const[0] * feat(11 + 16 * k)
        for b in range(1, 16):
            total = total + feat(11 + 16 * k + b) * basis[b]
        colours.append(total)
    mean_x = focal_length * part["u"] + center_x
    mean_y = focal_length * part["v"] + center_y
    logit = feat(10)
    log_opacity = jnp.minimum(logit, 0.0) - jnp.log(1.0 + jnp.exp(-jnp.abs(logit)))
    return [mean_x, mean_y, *part["conic"], log_opacity, *colours]


def project_pull(feat, cam, grads, put):
    part = project_parts(feat, cam)
    g_mx, g_my, g_a, g_b, g_c, g_o = grads[:6]
    g_col = grads[6:9]
    way, rlen = part["way"], part["rlen"]
    basis = sh_basis(*way)
    pulled = [None]
    for k in range(3):
        put(11 + 16 * k, sh_const[0] * g_col[k])
    for b in range(1, 16):
        total = 0.0
        for k in range(3):
            put(11 + 16 * k + b, g_col[k] * basis[b])
            total = total + g_col[k] * feat(11 + 16 * k + b)
        pulled.append(total)
    g_way = sh_pull(pulled, *way)
    along = way[0] * g_way[0] + way[1] * g_way[1] + way[2] * g_way[2]
    g_off = [(g_way[a] - way[a] * along) * rlen for a in range(3)]
    put(10, g_o / (1.0 + jnp.exp(feat(10))))
    a, b, c = part["conic"]
    g_xx = -(a * a * g_a + a * b * g_b + b * b * g_c)
    g_xy = -(2.0 * a * b * g_a + (a * c + b * b) * g_b + 2.0 * b * c * g_c)
    g_yy = -(b * b * g_a + b * c * g_b + c * c * g_c)
    axes, wide, turn, screen = part["axes"], part["wide"], part["turn"], part["screen"]
    for k in range(3):
        g_scale = (
            g_xx * axes[0][k] * wide[0][k]
            + g_xy * axes[0][k] * wide[1][k]
            + g_yy * axes[1][k] * wide[1][k]
        )
        put(3 + k, 2.0 * g_scale)
    g_axes = [
        [2.0 * g_xx * wide[0][k] + g_xy * wide[1][k] for k in range(3)],
        [2.0 * g_yy * wide[1][k] + g_xy * wide[0][k] for k in range(3)],
    ]
    g_screen = [
        [sum(g_axes[r][k] * turn[c][k] for k in range(3)) for c in range(3)] for r in range(2)
    ]
    gm = [
        [g_axes[0][k] * screen[0][c] + g_axes[1][k] * screen[1][c] for k in range(3)]
        for c in range(3)
    ]
    w, x, y, z = part["rotor"]
    up_xy, up_xz, up_yz = gm[0][1] + gm[1][0], gm[0][2] + gm[2][0], gm[1][2] + gm[2][1]
    un_xy, un_xz, un_yz = gm[1][0] - gm[0][1], gm[0][2] - gm[2][0], gm[2][1] - gm[1][2]
    g_rotor = [
        2.0 * (z * un_xy + y * un_xz + x * un_yz),
        2.0 * (y * up_xy + z * up_xz + w * un_yz - 2.0 * x * (gm[1][1] + gm[2][2])),
        2.0 * (x * up_xy + z * up_yz + w * un_xz - 2.0 * y * (gm[0][0] + gm[2][2])),
        2.0 * (x * up_xz + y * up_yz + w * un_xy - 2.0 * z * (gm[0][0] + gm[1][1])),
    ]
    rotor = (w, x, y, z)
    along = sum(rotor[i] * g_rotor[i] for i in range(4))
    for i in range(4):
        put(6 + i, (g_rotor[i] - rotor[i] * along) * part["rnorm"])
    rot, inv, finv, u, v = part["rot"], part["inv"], part["finv"], part["u"], part["v"]
    g_u = focal_length * g_mx - finv * sum(g_screen[0][c] * rot[2][c] for c in range(3))
    g_v = focal_length * g_my - finv * sum(g_screen[1][c] * rot[2][c] for c in range(3))
    g_f = sum(g_screen[r][c] * screen[r][c] for r in range(2) for c in range(3))
    g_in = [g_u * inv, g_v * inv, -(g_f + g_u * u + g_v * v) * inv]
    for axis in range(3):
        put(
            axis,
            g_off[axis] + rot[0][axis] * g_in[0] + rot[1][axis] * g_in[1] + rot[2][axis] * g_in[2],
        )


def split(value):
    high = value.astype(BF16)
    return high, (value - high.astype(F32)).astype(BF16)


def matmul(a, b, dims=((1,), (0,))):
    return lax.dot_general(a, b, (dims, ((), ())), preferred_element_type=F32)


def spread_features(parts, scratch, count):
    tiles = sum(part.shape[1] for part in parts) // LANES
    at = 0
    for part in parts:
        for first in range(0, part.shape[1], LANES):
            for row in range(0, count, 8):
                rows = min(8, count - row)
                scratch[pl.ds(row * tiles + at, rows, stride=tiles), :] = part[
                    row : row + rows, first : first + LANES
                ]
            at += 1
    return tiles


def pack_kernel(shards, pieces, where, *refs):
    sources, refs = refs[: 3 + (pieces > 0)], refs[3 + (pieces > 0) :]
    info, parts, refs = refs[0], refs[1 : 1 + pieces], refs[1 + pieces :]
    shard_of, local_of, goal, place_s, sems, cut_sems = refs
    group = where[0]
    loads = [
        pltpu.make_async_copy(source, held, sems.at[k])
        for k, (source, held) in enumerate(zip(sources, (shard_of, local_of, goal)))
    ]
    for d in range(pieces):
        chunk = parts[d].shape[1]
        first = pl.multiple_of((group ^ d) * chunk, LANES)
        loads.append(
            pltpu.make_async_copy(sources[3].at[:, pl.ds(first, chunk)], parts[d], cut_sems.at[d])
        )
    for load in loads:
        load.start()
    for load in loads[:3]:
        load.wait()
    width = info.shape[1]
    tile_count, listed = local_of.shape
    rows_each = (info.shape[0] - 4) // tile_count
    columns = rows_each * width
    chunk = columns // shards
    info[0:3, :] = goal[...]
    for t in range(tile_count):
        place = (shard_of[t] ^ group) * chunk + (local_of[t : t + 1, :] - group * chunk)
        info[3:4, t * listed : (t + 1) * listed] = place.astype(F32)
        row_i = lax.broadcasted_iota(jnp.int32, (LANES, LANES), 0)
        col_i = lax.broadcasted_iota(jnp.int32, (LANES, LANES), 1)
        for first in range(0, listed, LANES):
            spread = jnp.broadcast_to(place[:, first : first + LANES].astype(F32), (LANES, LANES))
            place_s[first : first + LANES, :] = jnp.broadcast_to(
                jnp.sum(jnp.where(row_i == col_i, spread, 0.0), axis=1, keepdims=True), (LANES, LANES)
            )
        lane_of = lax.broadcasted_iota(jnp.int32, (8, LANES), 1).astype(F32)
        row_of = lax.broadcasted_iota(jnp.int32, (8, LANES), 0).astype(F32)
        for s in range(columns // LANES):
            best = jnp.full((8, LANES), -1.0, F32)
            column = lane_of + float(s * LANES)
            for first in range(0, listed, 8):
                best = jnp.where(
                    place_s[first : first + 8, :] == column, row_of + float(first), best
                )
            best = jnp.max(best, axis=0, keepdims=True)
            row, at = 4 + t * rows_each + s * LANES // width, s * LANES % width
            info[row : row + 1, at : at + LANES] = best
    for load in loads[3:]:
        load.wait()


def pack(group, params, target, hit_shard, hit_local, shards, aligned):
    features, columns = params.shape
    tile_count, listed = hit_local.shape
    width = target.shape[1]
    rows = 4 + tile_count * (columns // width)
    pieces = shards if aligned else 0
    piece = jax.ShapeDtypeStruct((features, columns // shards), F32)
    args = (hit_shard.reshape(tile_count, 1, listed), hit_local, target) + (params,) * aligned
    out = call(
        functools.partial(pack_kernel, shards, pieces),
        "pack",
        (jax.ShapeDtypeStruct((rows, width), F32),) + (piece,) * pieces,
        [smem()] + [pl.BlockSpec(memory_space=pltpu.HBM)] * len(args),
        [
            pltpu.VMEM((tile_count, 1, listed), jnp.int32),
            pltpu.VMEM((tile_count, listed), jnp.int32),
            pltpu.VMEM(target.shape, F32),
            pltpu.VMEM((listed, LANES), F32),
            pltpu.SemaphoreType.DMA((3,)),
            pltpu.SemaphoreType.DMA((shards,)),
        ],
        (group.reshape(1),) + tuple(pltpu.with_memory_space_constraint(a, pltpu.HBM) for a in args),
    )
    return out[0], list(out[1:])


def pixel_basis(pixels):
    pixel = lax.broadcasted_iota(jnp.int32, (8, pixels), 1)
    row = lax.broadcasted_iota(jnp.int32, (8, pixels), 0)
    middle = 0.5 * TILE_SIDE - 0.5
    u = (pixel % TILE_SIDE).astype(F32) - middle
    v = (pixel // TILE_SIDE).astype(F32) - middle
    value = jnp.where(row == 0, 1.0, 0.0)
    for at, term in ((1, u), (2, v), (3, u * u), (4, u * v), (5, v * v)):
        value = jnp.where(row == at, term, value)
    return value


def composite(tiles, first_group, me, rows, info_s, rendered, work):
    alpha_s, weight_s, push_s, colour_s, goal_s, coef_s, mix_s, acc_s = work
    groups, tile_count, _, listed = acc_s.shape
    pixels = info_s.shape[2] // tile_count
    parts = pixels // LANES
    spans = groups * tile_count * parts
    slabs = rows.shape[0] // ROWS
    side = TILE_SIDE
    first_col, first_row = tiles
    basis = pixel_basis(pixels)
    basis_3 = jnp.concatenate([basis, basis, basis], axis=0).astype(BF16)

    means = []
    for g in range(groups):
        for t in range(tile_count):
            halves = []
            for first in range(t * listed, (t + 1) * listed, LANES):
                at = info_s[g, 3:4, first : first + LANES].astype(jnp.int32)
                at = jnp.broadcast_to(at, (ROWS, LANES))
                lane, slab = at & (LANES - 1), at >> 7
                found = jnp.zeros((ROWS, LANES), F32)
                for s in range(slabs):
                    here = jnp.take_along_axis(
                        rows[s * ROWS : (s + 1) * ROWS, :], lane, axis=1, mode="promise_in_bounds"
                    )
                    found = jnp.where(slab == s, here, found)
                halves.append(found)
            entry = jnp.concatenate(halves, axis=1)
            slot = (me ^ (first_group + g)) * tile_count + t
            mean_u = entry[0:1] - (((first_col + slot % 4) * side).astype(F32) + 0.5 * side)
            mean_v = entry[1:2] - (((first_row + slot // 4) * side).astype(F32) + 0.5 * side)
            quad_a, quad_b, quad_c = -0.5 * entry[2:3], -entry[3:4], -0.5 * entry[4:5]
            means.append((mean_u, mean_v, quad_a, quad_b, quad_c))
            slope_u = 2.0 * quad_a * mean_u + quad_b * mean_v
            slope_v = 2.0 * quad_c * mean_v + quad_b * mean_u
            level = 0.5 * (slope_u * mean_u + slope_v * mean_v) + entry[5:6]
            zero = jnp.zeros_like(level)
            coef = jnp.concatenate(
                [level, -slope_u, -slope_v, quad_a, quad_b, quad_c, zero, zero], axis=0
            )
            for part in range(3):
                term = coef.astype(BF16).astype(F32)
                coef_s[part * 8 : part * 8 + 8, :] = term
                coef = coef - term
            power = matmul(coef_s[...].astype(BF16), basis_3, ((0,), (0,)))
            n = g * tile_count + t
            for part in range(parts):
                span = n * parts + part
                at = slice(part * LANES, (part + 1) * LANES)
                alpha_s[pl.ds(span, listed, stride=spans), :] = jnp.exp(power[:, at])
                for k in range(3):
                    colour_s[k, span : span + 1, :] = entry[6 + k : 7 + k]
                    first = t * pixels + part * LANES
                    goal_s[k, span : span + 1, :] = info_s[g, k : k + 1, first : first + LANES]

    unroll = 32
    steps = listed // unroll

    def colours_of(step):
        first = step * unroll
        at = pl.ds(pl.multiple_of(first // LANES * LANES, LANES), LANES)
        turn = (LANES - first % LANES) % LANES
        return [pltpu.roll(colour_s[k, :, at], turn, 1) for k in range(3)]

    def forward(step, carry):
        passed, *image = carry
        colours = colours_of(step)
        for j in range(unroll):
            at = pl.ds(pl.multiple_of((step * unroll + j) * spans, spans), spans)
            alpha = alpha_s[at, :]
            weight = alpha * passed
            passed = passed * (1.0 - alpha)
            weight_s[at, :] = weight
            image = [
                image[k] + weight * jnp.broadcast_to(colours[k][:, j : j + 1], (spans, LANES))
                for k in range(3)
            ]
        return (passed, *image)

    nought = jnp.zeros((spans, LANES), F32)
    _, *image = lax.fori_loop(0, steps, forward, (nought + 1.0, nought, nought, nought))
    if rendered is not None:
        for k in range(3):
            for span in range(tile_count * parts):
                rendered[k : k + 1, span * LANES : (span + 1) * LANES] = image[k][span : span + 1]
    error = [image[k] - goal_s[k] for k in range(3)]

    def backward(back, behind):
        step = steps - 1 - back
        colours = colours_of(step)
        for j in reversed(range(unroll)):
            at = pl.ds(pl.multiple_of((step * unroll + j) * spans, spans), spans)
            alpha, weight = alpha_s[at, :], weight_s[at, :]
            pull = sum(
                error[k] * jnp.broadcast_to(colours[k][:, j : j + 1], (spans, LANES))
                for k in range(3)
            )
            push_s[at, :] = weight * (pull - behind)
            behind = behind * (1.0 - alpha) + alpha * pull
        return behind

    lax.fori_loop(0, steps, backward, nought)

    error_hi = [each.astype(BF16).astype(F32) for each in error]
    error_lo = [error[k] - error_hi[k] for k in range(3)]
    mix_s[...] = jnp.zeros(mix_s.shape, F32)
    for n in range(groups * tile_count):
        for part in range(parts):
            span = n * parts + part
            at = slice(span * LANES, (span + 1) * LANES)
            mix_s[0, n * ROWS : n * ROWS + 8, at] = basis[:, part * LANES : (part + 1) * LANES]
            for k in range(3):
                row = n * ROWS + 6 + k
                mix_s[1, row : row + 1, at] = error_hi[k][span : span + 1]
                mix_s[1, row + 3 : row + 4, at] = error_lo[k][span : span + 1]
    sums = 0.0
    for which, source in ((0, push_s), (1, weight_s)):
        whole = jnp.concatenate(
            [source[pl.ds(span, listed, stride=spans), :] for span in range(spans)], axis=1
        )
        high, low = split(whole)
        mix = mix_s[which].astype(BF16)
        sums = sums + matmul(high, mix, ((1,), (1,))) + matmul(low, mix, ((1,), (1,)))
    sums = sums.T
    for g in range(groups):
        for t in range(tile_count):
            n = g * tile_count + t
            mean_u, mean_v, quad_a, quad_b, quad_c = means[n]
            m_00, m_10, m_01, m_20, m_11, m_02 = [
                sums[n * ROWS + m : n * ROWS + m + 1] for m in range(6)
            ]
            n_10 = m_10 - mean_u * m_00
            n_01 = m_01 - mean_v * m_00
            acc_s[g, t, 0:1, :] = -(2.0 * quad_a * n_10 + quad_b * n_01)
            acc_s[g, t, 1:2, :] = -(2.0 * quad_c * n_01 + quad_b * n_10)
            acc_s[g, t, 2:3, :] = -0.5 * (m_20 - mean_u * (m_10 + n_10))
            acc_s[g, t, 3:4, :] = -(m_11 - mean_u * m_01 - mean_v * n_10)
            acc_s[g, t, 4:5, :] = -0.5 * (m_02 - mean_v * (m_01 + n_01))
            acc_s[g, t, 5:6, :] = m_00
            at = n * ROWS + 6
            acc_s[g, t, 6:9, :] = sums[at : at + 3] + sums[at + 3 : at + 6]
            acc_s[g, t, 9:16, :] = jnp.zeros((7, listed), F32)


def pool_sum(slab, info_s, acc_s):
    _, tile_count, _, listed = acc_s.shape
    width = info_s.shape[2]
    rows_each = (info_s.shape[1] - 4) // tile_count
    totals = []
    for g in range(2):
        total = jnp.zeros((ROWS, LANES), F32)
        for t in range(tile_count):
            row, first = 4 + t * rows_each + slab * LANES // width, slab * LANES % width
            at = info_s[g, row : row + 1, first : first + LANES].astype(jnp.int32)
            at = jnp.broadcast_to(at, (ROWS, LANES))
            lane, half = at & (LANES - 1), at >> 7
            for h in range(listed // LANES):
                here = jnp.take_along_axis(
                    acc_s[g, t, :, h * LANES : (h + 1) * LANES],
                    lane,
                    axis=1,
                    mode="promise_in_bounds",
                )
                total = total + jnp.where(half == h, here, 0.0)
        totals.append(total)
    return totals[0] + totals[1]


def block_start(tile_id):
    within = tile_id % (TILES_X * TILES_Y)
    return (within % TILES_X) // 4 * 4, (within // TILES_X) // 2 * 2


def near_kernel(pieces, tile_ids, cams, where, own, other, *refs):
    parts = refs[:pieces]
    rendered, rows, partial, feats, info_s, *work = refs[pieces:]
    view = tile_ids[0] // (TILES_X * TILES_Y)
    cam = [cams[view, i] for i in range(12)]
    slabs = spread_features(parts, feats, parts[0].shape[0])
    projected = project_rows(lambda f: feats[f * slabs : (f + 1) * slabs, :], cam)
    for f, value in enumerate(projected):
        rows[pl.ds(f, slabs, stride=ROWS), :] = value
    zero_row = jnp.zeros((slabs, LANES), F32)
    for f in range(len(projected), ROWS):
        rows[pl.ds(f, slabs, stride=ROWS), :] = zero_row
    info_s[0] = own[...]
    info_s[1] = other[...]
    composite(block_start(tile_ids[0]), 0, where[0], rows, info_s, rendered, work)
    for s in range(slabs):
        partial[:, s * LANES : (s + 1) * LANES] = pool_sum(s, info_s, work[-1])


def far_kernel(blocks, tile_ids, where, rows, partial, infos, *refs):
    *packets, info_s = refs[: len(refs) - 8]
    work = refs[len(refs) - 8 :]
    half = infos.shape[0] // 2
    info_s[0] = infos[:half, :]
    info_s[1] = infos[half:, :]
    composite(block_start(tile_ids[0]), 2, where[0], rows, info_s, None, work)
    share = (tile_ids[0] // (TILES_X * TILES_Y)).astype(F32)
    row_of = lax.broadcasted_iota(jnp.int32, (ROWS, LANES), 0)
    lane_of = lax.broadcasted_iota(jnp.int32, (ROWS, LANES), 1)
    chunk = packets[0].shape[1]
    for s in range(rows.shape[0] // ROWS):
        total = partial[:, s * LANES : (s + 1) * LANES] + pool_sum(s, info_s, work[-1])
        if blocks == 1:
            mine = share
        else:
            column = s * LANES + lane_of
            mine = jnp.where(column % where[2] // (where[2] // blocks) == where[1], share, 0.0)
        total = jnp.where(row_of == 9, mine, total)
        packets[s * LANES // chunk][:, s * LANES % chunk : s * LANES % chunk + LANES] = total


def join_kernel(first, second, out):
    half = first.shape[0]
    out[:half, :] = first[...]
    out[half:, :] = second[...]


def update_kernel(pieces, where, cams, *refs):
    packets = refs[:pieces]
    sources, sinks = refs[pieces : pieces + 3], refs[pieces + 3 : pieces + 6]
    feats, rows, grads, held, made, in_sems, out_sems = refs[pieces + 6 :]
    params, adam_m, adam_v = held.at[0], held.at[1], held.at[2]
    features, width = params.shape
    loads = [pltpu.make_async_copy(sources[k], held.at[k], in_sems.at[k]) for k in range(3)]
    for load in loads:
        load.start()
    chunk = packets[0].shape[1]
    slabs = width // LANES
    for d in range(pieces):
        for h in range(chunk // LANES):
            slab = (where[0] ^ d) * (chunk // LANES) + h
            rows[pl.ds(slab, ROWS, stride=slabs), :] = packets[d][:, h * LANES : (h + 1) * LANES]
    pulled = [rows[f * slabs : (f + 1) * slabs, :] for f in range(10)]
    view = pulled[9]
    cam = []
    for i in range(12):
        value = jnp.full((slabs, LANES), cams[0, i], F32)
        for v in range(1, cams.shape[0]):
            value = jnp.where(view == float(v), cams[v, i], value)
        cam.append(value)

    def put(f, value):
        grads[f * slabs : (f + 1) * slabs, :] = value

    loads[0].wait()
    spread_features([params], feats, features)
    project_pull(lambda f: feats[f * slabs : (f + 1) * slabs, :], cam, pulled[:9], put)
    rate = learn_rate / (1.0 - beta_one**adam_steps)
    unbias = 1.0 / (1.0 - beta_two**adam_steps)
    loads[1].wait()
    loads[2].wait()
    stores = []
    for row in range(0, features, 8):
        count = min(8, features - row)
        for s in range(slabs):
            at = (slice(row, row + count), slice(s * LANES, (s + 1) * LANES))
            grad = grads[pl.ds(row * slabs + s, count, stride=slabs), :]
            moment = beta_one * adam_m[at] + (1.0 - beta_one) * grad
            second = beta_two * adam_v[at] + (1.0 - beta_two) * grad * grad
            made.at[1][at] = moment
            made.at[2][at] = second
            made.at[0][at] = params[at] - rate * moment / (jnp.sqrt(second * unbias) + adam_eps)
        if row % 16 == 8 or row + count == features:
            first = row // 16 * 16
            span = pl.ds(first, row + count - first)
            for k in range(3):
                store = pltpu.make_async_copy(
                    made.at[k, span], sinks[k].at[span], out_sems.at[k, first // 16]
                )
                store.start()
                stores.append(store)
    for store in stores:
        store.wait()


def vmem():
    return pl.BlockSpec(memory_space=pltpu.VMEM)


def smem():
    return pl.BlockSpec(memory_space=pltpu.SMEM)


def any_space():
    return pl.BlockSpec(memory_space=pl.ANY)


def call(kernel, name, out_shape, in_specs, scratch, args, out_specs=None, grant=32):
    return pl.pallas_call(
        kernel,
        out_shape=out_shape,
        in_specs=in_specs,
        out_specs=out_specs or tuple(vmem() for _ in out_shape),
        scratch_shapes=scratch,
        compiler_params=pltpu.CompilerParams(vmem_limit_bytes=grant * 1024 * 1024),
        name=name,
    )(*args)


def work_shapes(tile_count, pixels, listed):
    spans = 2 * tile_count * pixels // LANES
    return [
        pltpu.VMEM((listed * spans, LANES), F32),
        pltpu.VMEM((listed * spans, LANES), F32),
        pltpu.VMEM((listed * spans, LANES), F32),
        pltpu.VMEM((3, spans, listed), F32),
        pltpu.VMEM((3, spans, LANES), F32),
        pltpu.VMEM((24, listed), F32),
        pltpu.VMEM((2, LANES, spans * LANES), F32),
        pltpu.VMEM((2, tile_count, ROWS, listed), F32),
    ]


def near(tile_ids, cameras, where, own, other, parts, tile_count):
    width = sum(part.shape[1] for part in parts)
    features = parts[0].shape[0]
    slabs = width // LANES
    pixels = listed = own.shape[1] // tile_count
    return call(
        functools.partial(near_kernel, len(parts)),
        "near",
        (
            jax.ShapeDtypeStruct((3, own.shape[1]), F32),
            jax.ShapeDtypeStruct((ROWS * slabs, LANES), F32),
            jax.ShapeDtypeStruct((ROWS, width), F32),
        ),
        [smem()] * 3 + [vmem()] * (2 + len(parts)),
        [pltpu.VMEM((features * slabs, LANES), F32), pltpu.VMEM((2,) + own.shape, F32)]
        + work_shapes(tile_count, pixels, listed),
        (tile_ids, cameras, where, own, other, *parts),
    )


def far(tile_ids, where, rows, partial, infos, pieces, tile_count, blocks):
    width = partial.shape[1]
    pixels = listed = infos.shape[1] // tile_count
    info = (infos.shape[0] // 2, infos.shape[1])
    return call(
        functools.partial(far_kernel, blocks),
        "far",
        (jax.ShapeDtypeStruct((ROWS, width // pieces), F32),) * pieces,
        [smem()] * 2 + [vmem()] * 3,
        [pltpu.VMEM((2,) + info, F32)] + work_shapes(tile_count, pixels, listed),
        (tile_ids, where, rows, partial, infos),
    )


def join(first, second):
    shape = (2 * first.shape[0], first.shape[1])
    return call(
        join_kernel, "join", (jax.ShapeDtypeStruct(shape, F32),), [vmem()] * 2, [], (first, second)
    )[0]


def update(where, cameras, params, adam_m, adam_v, packets):
    features, width = params.shape
    slabs = width // LANES
    shape = jax.ShapeDtypeStruct(params.shape, F32)
    return call(
        functools.partial(update_kernel, len(packets)),
        "update",
        (shape, shape, shape),
        [smem()] * 2 + [vmem()] * len(packets) + [any_space()] * 3,
        [
            pltpu.VMEM((features * slabs, LANES), F32),
            pltpu.VMEM((ROWS * slabs, LANES), F32),
            pltpu.VMEM((features * slabs, LANES), F32),
            pltpu.VMEM((3,) + params.shape, F32),
            pltpu.VMEM((3,) + params.shape, F32),
            pltpu.SemaphoreType.DMA((3,)),
            pltpu.SemaphoreType.DMA((3, (features + 15) // 16)),
        ],
        (where, cameras, *packets, params, adam_m, adam_v),
        (any_space(),) * 3,
    )


def swap(value, axis, d):
    if d == 0:
        return value
    return lax.ppermute(value, axis, [(k, k ^ d) for k in range(lax.axis_size(axis))])


def local(params, adam_m, adam_v, cameras, target, tile_ids, hit_shard, hit_local):
    width = params.shape[1]
    tile_count, listed = hit_local.shape
    shards = lax.axis_size("gs")
    along = lax.axis_size("tile")
    chunk = width // shards
    group = lax.axis_index("gs")
    seat = lax.axis_index("tile")
    aligned = chunk % LANES == 0
    team = BLOCK_TILES // tile_count
    assert team == 4
    blocks = along // team

    info, parts = pack(group, params, target, hit_shard, hit_local, shards, aligned)
    if not aligned:
        parts = [
            lax.dynamic_slice_in_dim(params, (group ^ d) * chunk, chunk, axis=1)
            for d in range(shards)
        ]
    parts = [swap(parts[d], "gs", d) for d in range(shards)]
    beside = swap(info, "tile", 1)
    beyond = swap(join(info, beside), "tile", 2)
    if not aligned:
        parts = [jnp.concatenate(parts, axis=1)]
    where = jnp.stack([seat % team, seat // team, jnp.int32(chunk)]).astype(jnp.int32)
    rendered, rows, partial = near(tile_ids, cameras, where, info, beside, parts, tile_count)
    packets = far(tile_ids, where, rows, partial, beyond, len(parts), tile_count, blocks)
    if not aligned:
        packets = [packets[0][:, d * chunk : (d + 1) * chunk] for d in range(shards)]
    packets = [swap(packets[d], "gs", d) for d in range(shards)]
    if blocks > 1:
        packets = [block_sum(packet, along, team) for packet in packets]
    if aligned:
        own = group
    else:
        packets = [jnp.stack(packets)[jnp.arange(shards) ^ group].transpose(1, 0, 2).reshape(ROWS, -1)]
        own = jnp.int32(0)
    new_params, new_m, new_v = update(
        own.reshape(1), cameras, params, adam_m, adam_v, packets
    )
    return (rendered, new_params, new_m, new_v)


def block_sum(packet, along, team):
    step = team
    while step < along:
        packet = packet + swap(packet, "tile", step)
        step *= 2
    return packet


def solution(mesh):
    return jax.shard_map(
        local,
        mesh=mesh,
        in_specs=(
            P(None, ("groups", "gs")),
            P(None, ("groups", "gs")),
            P(None, ("groups", "gs")),
            P("groups", None),
            P(None, ("groups", "gs", "tile")),
            P(("groups", "gs", "tile")),
            P(("groups", "gs", "tile"), None, None),
            P(("groups", "gs", "tile"), None),
        ),
        out_specs=(
            P(None, ("groups", "gs", "tile")),
            P(None, ("groups", "gs")),
            P(None, ("groups", "gs")),
            P(None, ("groups", "gs")),
        ),
        check_vma=False,
    )
```

```python
import functools

import jax
import jax.numpy as jnp
from jax import lax
from jax.experimental import pallas as pl
from jax.experimental.pallas import tpu as pltpu
from jax.sharding import PartitionSpec as P

TILES_X = 120
TILES_Y = 68
TILE_SIDE = 16
BLOCK_TILES = 8
LANES = 128
ROWS = 16
SPAN_STEP, LIST_STEP = 3, 25
F32 = jnp.float32
BF16 = jnp.bfloat16

focal_length = 1000.0
center_x = 960.0
center_y = 540.0
dilation = 0.3
beta_one = 0.9
beta_two = 0.999
learn_rate = 0.01
adam_eps = 1e-08
adam_steps = 100.0
sh_const = (
    0.28209479177387814,
    0.4886025119029199,
    1.0925484305920792,
    0.31539156525252005,
    0.5462742152960396,
    0.5900435899266435,
    2.890611442640554,
    0.4570457994644658,
    0.3731763325901154,
    1.445305721320277,
)


def sh_basis(x, y, z):
    s = sh_const
    xx, yy, zz = x * x, y * y, z * z
    return [
        None,
        -s[1] * y,
        s[1] * z,
        -s[1] * x,
        s[2] * (x * y),
        -s[2] * (y * z),
        s[3] * (2.0 * zz - xx - yy),
        -s[2] * (x * z),
        s[4] * (xx - yy),
        -s[5] * y * (3.0 * xx - yy),
        s[6] * (x * y) * z,
        -s[7] * y * (4.0 * zz - xx - yy),
        s[8] * z * (2.0 * zz - 3.0 * xx - 3.0 * yy),
        -s[7] * x * (4.0 * zz - xx - yy),
        s[9] * z * (xx - yy),
        -s[5] * x * (xx - 3.0 * yy),
    ]


def sh_pull(h, x, y, z):
    s = sh_const
    xx, yy, zz = x * x, y * y, z * z
    xy, xz, yz = x * y, x * z, y * z
    diff = xx - yy
    ring = 4.0 * zz - xx - yy
    g_x = (
        -s[1] * h[3]
        + s[2] * (h[4] * y - h[7] * z)
        - (2.0 * s[3]) * h[6] * x
        + (2.0 * s[4]) * h[8] * x
        - (6.0 * s[5]) * h[9] * xy
        + s[6] * h[10] * yz
        + (2.0 * s[7]) * h[11] * xy
        - (6.0 * s[8]) * h[12] * xz
        - s[7] * h[13] * (ring - 2.0 * xx)
        + (2.0 * s[9]) * h[14] * xz
        - (3.0 * s[5]) * h[15] * diff
    )
    g_y = (
        -s[1] * h[1]
        + s[2] * (h[4] * x - h[5] * z)
        - (2.0 * s[3]) * h[6] * y
        - (2.0 * s[4]) * h[8] * y
        - (3.0 * s[5]) * h[9] * diff
        + s[6] * h[10] * xz
        - s[7] * h[11] * (ring - 2.0 * yy)
        - (6.0 * s[8]) * h[12] * yz
        + (2.0 * s[7]) * h[13] * xy
        - (2.0 * s[9]) * h[14] * yz
        + (6.0 * s[5]) * h[15] * xy
    )
    g_z = (
        s[1] * h[2]
        - s[2] * (h[5] * y + h[7] * x)
        + (4.0 * s[3]) * h[6] * z
        + s[6] * h[10] * xy
        - (8.0 * s[7]) * (h[11] * yz + h[13] * xz)
        + s[8] * h[12] * (6.0 * zz - 3.0 * xx - 3.0 * yy)
        + s[9] * h[14] * diff
    )
    return g_x, g_y, g_z


def project_parts(feat, cam):
    rot = [[cam[3 * r + c] for c in range(3)] for r in range(3)]
    off = [feat(a) - cam[9 + a] for a in range(3)]
    in_cam = [rot[r][0] * off[0] + rot[r][1] * off[1] + rot[r][2] * off[2] for r in range(3)]
    inv = 1.0 / in_cam[2]
    u = in_cam[0] * inv
    v = in_cam[1] * inv
    finv = focal_length * inv
    scale = [jnp.exp(2.0 * feat(3 + a)) for a in range(3)]
    quat = [feat(6 + a) for a in range(4)]
    rnorm = lax.rsqrt(quat[0] * quat[0] + quat[1] * quat[1] + quat[2] * quat[2] + quat[3] * quat[3])
    w, x, y, z = [q * rnorm for q in quat]
    turn = [
        [1.0 - 2.0 * (y * y + z * z), 2.0 * (x * y - w * z), 2.0 * (x * z + w * y)],
        [2.0 * (x * y + w * z), 1.0 - 2.0 * (x * x + z * z), 2.0 * (y * z - w * x)],
        [2.0 * (x * z - w * y), 2.0 * (y * z + w * x), 1.0 - 2.0 * (x * x + y * y)],
    ]
    screen = [
        [finv * (rot[0][c] - u * rot[2][c]) for c in range(3)],
        [finv * (rot[1][c] - v * rot[2][c]) for c in range(3)],
    ]
    axes = [
        [sum(screen[r][c] * turn[c][k] for c in range(3)) for k in range(3)] for r in range(2)
    ]
    wide = [[axes[r][k] * scale[k] for k in range(3)] for r in range(2)]
    cov_xx = sum(wide[0][k] * axes[0][k] for k in range(3)) + dilation
    cov_xy = sum(wide[0][k] * axes[1][k] for k in range(3))
    cov_yy = sum(wide[1][k] * axes[1][k] for k in range(3)) + dilation
    rdet = 1.0 / (cov_xx * cov_yy - cov_xy * cov_xy)
    conic = (cov_yy * rdet, -cov_xy * rdet, cov_xx * rdet)
    rlen = lax.rsqrt(off[0] * off[0] + off[1] * off[1] + off[2] * off[2])
    way = [off[a] * rlen for a in range(3)]
    return dict(
        rot=rot, inv=inv, u=u, v=v, finv=finv, scale=scale, rnorm=rnorm, rotor=(w, x, y, z), turn=turn,
        screen=screen, axes=axes, wide=wide, conic=conic, rlen=rlen, way=way,
    )


def project_rows(feat, cam):
    part = project_parts(feat, cam)
    basis = sh_basis(*part["way"])
    colours = []
    for k in range(3):
        total = 0.5 + sh_const[0] * feat(11 + 16 * k)
        for b in range(1, 16):
            total = total + feat(11 + 16 * k + b) * basis[b]
        colours.append(total)
    mean_x = focal_length * part["u"] + center_x
    mean_y = focal_length * part["v"] + center_y
    logit = feat(10)
    log_opacity = jnp.minimum(logit, 0.0) - jnp.log(1.0 + jnp.exp(-jnp.abs(logit)))
    return [mean_x, mean_y, *part["conic"], log_opacity, *colours]


def project_pull(feat, cam, grads, put):
    part = project_parts(feat, cam)
    g_mx, g_my, g_a, g_b, g_c, g_o = grads[:6]
    g_col = grads[6:9]
    way, rlen = part["way"], part["rlen"]
    basis = sh_basis(*way)
    pulled = [None]
    for k in range(3):
        put(11 + 16 * k, sh_const[0] * g_col[k])
    for b in range(1, 16):
        total = 0.0
        for k in range(3):
            put(11 + 16 * k + b, g_col[k] * basis[b])
            total = total + g_col[k] * feat(11 + 16 * k + b)
        pulled.append(total)
    g_way = sh_pull(pulled, *way)
    along = way[0] * g_way[0] + way[1] * g_way[1] + way[2] * g_way[2]
    g_off = [(g_way[a] - way[a] * along) * rlen for a in range(3)]
    put(10, g_o / (1.0 + jnp.exp(feat(10))))
    a, b, c = part["conic"]
    g_xx = -(a * a * g_a + a * b * g_b + b * b * g_c)
    g_xy = -(2.0 * a * b * g_a + (a * c + b * b) * g_b + 2.0 * b * c * g_c)
    g_yy = -(b * b * g_a + b * c * g_b + c * c * g_c)
    axes, wide, turn, screen = part["axes"], part["wide"], part["turn"], part["screen"]
    for k in range(3):
        g_scale = (
            g_xx * axes[0][k] * wide[0][k]
            + g_xy * axes[0][k] * wide[1][k]
            + g_yy * axes[1][k] * wide[1][k]
        )
        put(3 + k, 2.0 * g_scale)
    g_axes = [
        [2.0 * g_xx * wide[0][k] + g_xy * wide[1][k] for k in range(3)],
        [2.0 * g_yy * wide[1][k] + g_xy * wide[0][k] for k in range(3)],
    ]
    g_screen = [
        [sum(g_axes[r][k] * turn[c][k] for k in range(3)) for c in range(3)] for r in range(2)
    ]
    gm = [
        [g_axes[0][k] * screen[0][c] + g_axes[1][k] * screen[1][c] for k in range(3)]
        for c in range(3)
    ]
    w, x, y, z = part["rotor"]
    up_xy, up_xz, up_yz = gm[0][1] + gm[1][0], gm[0][2] + gm[2][0], gm[1][2] + gm[2][1]
    un_xy, un_xz, un_yz = gm[1][0] - gm[0][1], gm[0][2] - gm[2][0], gm[2][1] - gm[1][2]
    g_rotor = [
        2.0 * (z * un_xy + y * un_xz + x * un_yz),
        2.0 * (y * up_xy + z * up_xz + w * un_yz - 2.0 * x * (gm[1][1] + gm[2][2])),
        2.0 * (x * up_xy + z * up_yz + w * un_xz - 2.0 * y * (gm[0][0] + gm[2][2])),
        2.0 * (x * up_xz + y * up_yz + w * un_xy - 2.0 * z * (gm[0][0] + gm[1][1])),
    ]
    rotor = (w, x, y, z)
    along = sum(rotor[i] * g_rotor[i] for i in range(4))
    for i in range(4):
        put(6 + i, (g_rotor[i] - rotor[i] * along) * part["rnorm"])
    rot, inv, finv, u, v = part["rot"], part["inv"], part["finv"], part["u"], part["v"]
    g_u = focal_length * g_mx - finv * sum(g_screen[0][c] * rot[2][c] for c in range(3))
    g_v = focal_length * g_my - finv * sum(g_screen[1][c] * rot[2][c] for c in range(3))
    g_f = sum(g_screen[r][c] * screen[r][c] for r in range(2) for c in range(3))
    g_in = [g_u * inv, g_v * inv, -(g_f + g_u * u + g_v * v) * inv]
    for axis in range(3):
        put(
            axis,
            g_off[axis] + rot[0][axis] * g_in[0] + rot[1][axis] * g_in[1] + rot[2][axis] * g_in[2],
        )


def split(value):
    high = value.astype(BF16)
    return high, (value - high.astype(F32)).astype(BF16)


def matmul(a, b, dims=((1,), (0,))):
    return lax.dot_general(a, b, (dims, ((), ())), preferred_element_type=F32)


def spread_features(parts, scratch, count):
    tiles = sum(part.shape[1] for part in parts) // LANES
    at = 0
    for part in parts:
        for first in range(0, part.shape[1], LANES):
            for row in range(0, count, 8):
                rows = min(8, count - row)
                scratch[pl.ds(row * tiles + at, rows, stride=tiles), :] = part[
                    row : row + rows, first : first + LANES
                ]
            at += 1
    return tiles


def pack_kernel(shards, pieces, where, *refs):
    sources, refs = refs[: 3 + (pieces > 0)], refs[3 + (pieces > 0) :]
    info, parts, refs = refs[0], refs[1 : 1 + pieces], refs[1 + pieces :]
    shard_of, local_of, goal, place_s, sems, cut_sems = refs
    group = where[0]
    loads = [
        pltpu.make_async_copy(source, held, sems.at[k])
        for k, (source, held) in enumerate(zip(sources, (shard_of, local_of, goal)))
    ]
    for d in range(pieces):
        chunk = parts[d].shape[1]
        first = pl.multiple_of((group ^ d) * chunk, LANES)
        loads.append(
            pltpu.make_async_copy(sources[3].at[:, pl.ds(first, chunk)], parts[d], cut_sems.at[d])
        )
    for load in loads:
        load.start()
    for load in loads[:3]:
        load.wait()
    width = info.shape[1]
    tile_count, listed = local_of.shape
    rows_each = (info.shape[0] - 4) // tile_count
    columns = rows_each * width
    chunk = columns // shards
    info[0:3, :] = goal[...]
    for t in range(tile_count):
        place = (shard_of[t] ^ group) * chunk + (local_of[t : t + 1, :] - group * chunk)
        info[3:4, t * listed : (t + 1) * listed] = place.astype(F32)
        row_i = lax.broadcasted_iota(jnp.int32, (LANES, LANES), 0)
        col_i = lax.broadcasted_iota(jnp.int32, (LANES, LANES), 1)
        for first in range(0, listed, LANES):
            spread = jnp.broadcast_to(place[:, first : first + LANES].astype(F32), (LANES, LANES))
            place_s[first : first + LANES, :] = jnp.broadcast_to(
                jnp.sum(jnp.where(row_i == col_i, spread, 0.0), axis=1, keepdims=True), (LANES, LANES)
            )
        lane_of = lax.broadcasted_iota(jnp.int32, (8, LANES), 1).astype(F32)
        row_of = lax.broadcasted_iota(jnp.int32, (8, LANES), 0).astype(F32)
        for s in range(columns // LANES):
            best = jnp.full((8, LANES), -1.0, F32)
            column = lane_of + float(s * LANES)
            for first in range(0, listed, 8):
                best = jnp.where(
                    place_s[first : first + 8, :] == column, row_of + float(first), best
                )
            best = jnp.max(best, axis=0, keepdims=True)
            row, at = 4 + t * rows_each + s * LANES // width, s * LANES % width
            info[row : row + 1, at : at + LANES] = best
    for load in loads[3:]:
        load.wait()


def pack(group, params, target, hit_shard, hit_local, shards, aligned):
    features, columns = params.shape
    tile_count, listed = hit_local.shape
    width = target.shape[1]
    rows = 4 + tile_count * (columns // width)
    pieces = shards if aligned else 0
    piece = jax.ShapeDtypeStruct((features, columns // shards), F32)
    args = (hit_shard.reshape(tile_count, 1, listed), hit_local, target) + (params,) * aligned
    out = call(
        functools.partial(pack_kernel, shards, pieces),
        "pack",
        (jax.ShapeDtypeStruct((rows, width), F32),) + (piece,) * pieces,
        [smem()] + [pl.BlockSpec(memory_space=pltpu.HBM)] * len(args),
        [
            pltpu.VMEM((tile_count, 1, listed), jnp.int32),
            pltpu.VMEM((tile_count, listed), jnp.int32),
            pltpu.VMEM(target.shape, F32),
            pltpu.VMEM((listed, LANES), F32),
            pltpu.SemaphoreType.DMA((3,)),
            pltpu.SemaphoreType.DMA((shards,)),
        ],
        (group.reshape(1),) + tuple(pltpu.with_memory_space_constraint(a, pltpu.HBM) for a in args),
    )
    return out[0], list(out[1:])


def pixel_basis(pixels):
    pixel = lax.broadcasted_iota(jnp.int32, (8, pixels), 1)
    row = lax.broadcasted_iota(jnp.int32, (8, pixels), 0)
    middle = 0.5 * TILE_SIDE - 0.5
    u = (pixel % TILE_SIDE).astype(F32) - middle
    v = (pixel // TILE_SIDE).astype(F32) - middle
    value = jnp.where(row == 0, 1.0, 0.0)
    for at, term in ((1, u), (2, v), (3, u * u), (4, u * v), (5, v * v)):
        value = jnp.where(row == at, term, value)
    return value


def composite(tiles, first_group, me, rows, info_s, rendered, work):
    alpha_s, weight_s, pull_s, push_s, weight_hi, weight_lo, coef_s, mix_s, acc_s = work
    groups, tile_count, _, listed = acc_s.shape
    pixels = info_s.shape[2] // tile_count
    parts = pixels // LANES
    spans = groups * tile_count * parts
    slabs = rows.shape[0] // ROWS
    side = TILE_SIDE
    first_col, first_row = tiles

    def of_span(span):
        return pl.ds(span * SPAN_STEP, listed, stride=LIST_STEP)

    def of_place(place):
        return pl.ds(place * LIST_STEP, spans, stride=SPAN_STEP)

    basis = pixel_basis(pixels)
    basis_3 = jnp.concatenate([basis, basis, basis], axis=0).astype(BF16)

    means, colours = [], []
    for g in range(groups):
        for t in range(tile_count):
            halves = []
            for first in range(t * listed, (t + 1) * listed, LANES):
                at = info_s[g, 3:4, first : first + LANES].astype(jnp.int32)
                at = jnp.broadcast_to(at, (ROWS, LANES))
                lane, slab = at & (LANES - 1), at >> 7
                found = jnp.zeros((ROWS, LANES), F32)
                for s in range(slabs):
                    here = jnp.take_along_axis(
                        rows[s * ROWS : (s + 1) * ROWS, :], lane, axis=1, mode="promise_in_bounds"
                    )
                    found = jnp.where(slab == s, here, found)
                halves.append(found)
            entry = jnp.concatenate(halves, axis=1)
            slot = (me ^ (first_group + g)) * tile_count + t
            mean_u = entry[0:1] - (((first_col + slot % 4) * side).astype(F32) + 0.5 * side)
            mean_v = entry[1:2] - (((first_row + slot // 4) * side).astype(F32) + 0.5 * side)
            quad_a, quad_b, quad_c = -0.5 * entry[2:3], -entry[3:4], -0.5 * entry[4:5]
            means.append((mean_u, mean_v, quad_a, quad_b, quad_c))
            slope_u = 2.0 * quad_a * mean_u + quad_b * mean_v
            slope_v = 2.0 * quad_c * mean_v + quad_b * mean_u
            level = 0.5 * (slope_u * mean_u + slope_v * mean_v) + entry[5:6]
            zero = jnp.zeros_like(level)
            coef = jnp.concatenate(
                [level, -slope_u, -slope_v, quad_a, quad_b, quad_c, zero, zero], axis=0
            )
            for part in range(3):
                term = coef.astype(BF16).astype(F32)
                coef_s[part * 8 : part * 8 + 8, :] = term
                coef = coef - term
            power = matmul(coef_s[...].astype(BF16), basis_3, ((0,), (0,)))
            n = g * tile_count + t
            for part in range(parts):
                at = slice(part * LANES, (part + 1) * LANES)
                alpha_s[of_span(n * parts + part), :] = jnp.exp(power[:, at])
            high = entry[6:9].astype(BF16).astype(F32)
            low = entry[6:9] - high
            zero = jnp.zeros((2, listed), F32)
            colours.append(jnp.concatenate([high, low, zero], axis=0).astype(BF16))

    unroll = 32
    steps = listed // unroll

    def forward(step, passed):
        for j in range(unroll):
            at = of_place(step * unroll + j)
            alpha = alpha_s[at, :]
            weight_s[at, :] = alpha * passed
            passed = passed * (1.0 - alpha)
        return passed

    nought = jnp.zeros((spans, LANES), F32)
    lax.fori_loop(0, steps, forward, nought + 1.0)

    errors = []
    for n in range(groups * tile_count):
        g, t = n // tile_count, n % tile_count
        for part in range(parts):
            at = slice((n * parts + part) * LANES, (n * parts + part + 1) * LANES)
            weight_hi[:, at], weight_lo[:, at] = split(weight_s[of_span(n * parts + part), :])
        at = slice(n * pixels, (n + 1) * pixels)
        image = matmul(colours[n], weight_hi[:, at])
        image = image[0:3] + image[3:6] + matmul(colours[n], weight_lo[:, at])[0:3]
        here = slice(t * pixels, (t + 1) * pixels)
        if rendered is not None and g == 0:
            rendered[:, here] = image
        error = image - info_s[g, 0:3, here]
        high = error.astype(BF16).astype(F32)
        low = error - high
        errors.append((high, low))
        zero = jnp.zeros((2, pixels), F32)
        both = jnp.concatenate([high, high, zero], axis=0).astype(BF16)
        rest = jnp.concatenate([low, jnp.zeros((5, pixels), F32)], axis=0).astype(BF16)
        first = ((0,), (0,))
        pull = matmul(colours[n], both, first) + matmul(colours[n], rest, first)
        for part in range(parts):
            at = slice(part * LANES, (part + 1) * LANES)
            pull_s[of_span(n * parts + part), :] = pull[:, at]

    def backward(back, behind):
        for j in range(unroll):
            at = of_place(listed - 1 - (back * unroll + j))
            alpha, pull = alpha_s[at, :], pull_s[at, :]
            push_s[at, :] = weight_s[at, :] * (pull - behind)
            behind = behind * (1.0 - alpha) + alpha * pull
        return behind

    lax.fori_loop(0, steps, backward, nought)

    mix_s[...] = jnp.zeros(mix_s.shape, F32)
    for n in range(groups * tile_count):
        at = slice(n * pixels, (n + 1) * pixels)
        mix_s[0, n * ROWS : n * ROWS + 8, at] = basis
        high, low = errors[n]
        mix_s[1, n * ROWS + 6 : n * ROWS + 9, at] = high
        mix_s[1, n * ROWS + 9 : n * ROWS + 12, at] = low
    moments, colour_sums = mix_s[0].astype(BF16), mix_s[1].astype(BF16)
    high, low = split(jnp.concatenate([push_s[of_span(span), :] for span in range(spans)], axis=1))
    across = ((1,), (1,))
    sums = matmul(high, moments, across) + matmul(low, moments, across)
    sums = sums + matmul(weight_hi[...], colour_sums, across)
    sums = sums + matmul(weight_lo[...], colour_sums, across)
    sums = sums.T
    for g in range(groups):
        for t in range(tile_count):
            n = g * tile_count + t
            mean_u, mean_v, quad_a, quad_b, quad_c = means[n]
            m_00, m_10, m_01, m_20, m_11, m_02 = [
                sums[n * ROWS + m : n * ROWS + m + 1] for m in range(6)
            ]
            n_10 = m_10 - mean_u * m_00
            n_01 = m_01 - mean_v * m_00
            acc_s[g, t, 0:1, :] = -(2.0 * quad_a * n_10 + quad_b * n_01)
            acc_s[g, t, 1:2, :] = -(2.0 * quad_c * n_01 + quad_b * n_10)
            acc_s[g, t, 2:3, :] = -0.5 * (m_20 - mean_u * (m_10 + n_10))
            acc_s[g, t, 3:4, :] = -(m_11 - mean_u * m_01 - mean_v * n_10)
            acc_s[g, t, 4:5, :] = -0.5 * (m_02 - mean_v * (m_01 + n_01))
            acc_s[g, t, 5:6, :] = m_00
            at = n * ROWS + 6
            acc_s[g, t, 6:9, :] = sums[at : at + 3] + sums[at + 3 : at + 6]
            acc_s[g, t, 9:16, :] = jnp.zeros((7, listed), F32)


def pool_sum(slab, info_s, acc_s):
    _, tile_count, _, listed = acc_s.shape
    width = info_s.shape[2]
    rows_each = (info_s.shape[1] - 4) // tile_count
    totals = []
    for g in range(2):
        total = jnp.zeros((ROWS, LANES), F32)
        for t in range(tile_count):
            row, first = 4 + t * rows_each + slab * LANES // width, slab * LANES % width
            at = info_s[g, row : row + 1, first : first + LANES].astype(jnp.int32)
            at = jnp.broadcast_to(at, (ROWS, LANES))
            lane, half = at & (LANES - 1), at >> 7
            for h in range(listed // LANES):
                here = jnp.take_along_axis(
                    acc_s[g, t, :, h * LANES : (h + 1) * LANES],
                    lane,
                    axis=1,
                    mode="promise_in_bounds",
                )
                total = total + jnp.where(half == h, here, 0.0)
        totals.append(total)
    return totals[0] + totals[1]


def block_start(tile_id):
    within = tile_id % (TILES_X * TILES_Y)
    return (within % TILES_X) // 4 * 4, (within // TILES_X) // 2 * 2


def near_kernel(pieces, tile_ids, cams, where, own, other, *refs):
    parts = refs[:pieces]
    rendered, rows, partial, feats, info_s, *work = refs[pieces:]
    view = tile_ids[0] // (TILES_X * TILES_Y)
    cam = [cams[view, i] for i in range(12)]
    slabs = spread_features(parts, feats, parts[0].shape[0])
    projected = project_rows(lambda f: feats[f * slabs : (f + 1) * slabs, :], cam)
    for f, value in enumerate(projected):
        rows[pl.ds(f, slabs, stride=ROWS), :] = value
    zero_row = jnp.zeros((slabs, LANES), F32)
    for f in range(len(projected), ROWS):
        rows[pl.ds(f, slabs, stride=ROWS), :] = zero_row
    info_s[0] = own[...]
    info_s[1] = other[...]
    composite(block_start(tile_ids[0]), 0, where[0], rows, info_s, rendered, work)
    for s in range(slabs):
        partial[:, s * LANES : (s + 1) * LANES] = pool_sum(s, info_s, work[-1])


def far_kernel(blocks, tile_ids, where, rows, partial, infos, *refs):
    *packets, info_s = refs[: len(refs) - 9]
    work = refs[len(refs) - 9 :]
    half = infos.shape[0] // 2
    info_s[0] = infos[:half, :]
    info_s[1] = infos[half:, :]
    composite(block_start(tile_ids[0]), 2, where[0], rows, info_s, None, work)
    share = (tile_ids[0] // (TILES_X * TILES_Y)).astype(F32)
    row_of = lax.broadcasted_iota(jnp.int32, (ROWS, LANES), 0)
    lane_of = lax.broadcasted_iota(jnp.int32, (ROWS, LANES), 1)
    chunk = packets[0].shape[1]
    for s in range(rows.shape[0] // ROWS):
        total = partial[:, s * LANES : (s + 1) * LANES] + pool_sum(s, info_s, work[-1])
        if blocks == 1:
            mine = share
        else:
            column = s * LANES + lane_of
            mine = jnp.where(column % where[2] // (where[2] // blocks) == where[1], share, 0.0)
        total = jnp.where(row_of == 9, mine, total)
        packets[s * LANES // chunk][:, s * LANES % chunk : s * LANES % chunk + LANES] = total


def join_kernel(first, second, out):
    half = first.shape[0]
    out[:half, :] = first[...]
    out[half:, :] = second[...]


def update_kernel(pieces, where, cams, *refs):
    packets = refs[:pieces]
    sources, sinks = refs[pieces : pieces + 3], refs[pieces + 3 : pieces + 6]
    feats, rows, grads, held, made, in_sems, out_sems = refs[pieces + 6 :]
    params, adam_m, adam_v = held.at[0], held.at[1], held.at[2]
    features, width = params.shape
    loads = [pltpu.make_async_copy(sources[k], held.at[k], in_sems.at[k]) for k in range(3)]
    for load in loads:
        load.start()
    chunk = packets[0].shape[1]
    slabs = width // LANES
    for d in range(pieces):
        for h in range(chunk // LANES):
            slab = (where[0] ^ d) * (chunk // LANES) + h
            rows[pl.ds(slab, ROWS, stride=slabs), :] = packets[d][:, h * LANES : (h + 1) * LANES]
    pulled = [rows[f * slabs : (f + 1) * slabs, :] for f in range(10)]
    view = pulled[9]
    cam = []
    for i in range(12):
        value = jnp.full((slabs, LANES), cams[0, i], F32)
        for v in range(1, cams.shape[0]):
            value = jnp.where(view == float(v), cams[v, i], value)
        cam.append(value)

    def put(f, value):
        grads[f * slabs : (f + 1) * slabs, :] = value

    loads[0].wait()
    spread_features([params], feats, features)
    project_pull(lambda f: feats[f * slabs : (f + 1) * slabs, :], cam, pulled[:9], put)
    rate = learn_rate / (1.0 - beta_one**adam_steps)
    unbias = 1.0 / (1.0 - beta_two**adam_steps)
    loads[1].wait()
    loads[2].wait()
    stores = []
    for row in range(0, features, 8):
        count = min(8, features - row)
        for s in range(slabs):
            at = (slice(row, row + count), slice(s * LANES, (s + 1) * LANES))
            grad = grads[pl.ds(row * slabs + s, count, stride=slabs), :]
            moment = beta_one * adam_m[at] + (1.0 - beta_one) * grad
            second = beta_two * adam_v[at] + (1.0 - beta_two) * grad * grad
            made.at[1][at] = moment
            made.at[2][at] = second
            made.at[0][at] = params[at] - rate * moment / (jnp.sqrt(second * unbias) + adam_eps)
        if row % 16 == 8 or row + count == features:
            first = row // 16 * 16
            span = pl.ds(first, row + count - first)
            for k in range(3):
                store = pltpu.make_async_copy(
                    made.at[k, span], sinks[k].at[span], out_sems.at[k, first // 16]
                )
                store.start()
                stores.append(store)
    for store in stores:
        store.wait()


def vmem():
    return pl.BlockSpec(memory_space=pltpu.VMEM)


def smem():
    return pl.BlockSpec(memory_space=pltpu.SMEM)


def any_space():
    return pl.BlockSpec(memory_space=pl.ANY)


def call(kernel, name, out_shape, in_specs, scratch, args, out_specs=None, grant=32):
    return pl.pallas_call(
        kernel,
        out_shape=out_shape,
        in_specs=in_specs,
        out_specs=out_specs or tuple(vmem() for _ in out_shape),
        scratch_shapes=scratch,
        compiler_params=pltpu.CompilerParams(vmem_limit_bytes=grant * 1024 * 1024),
        name=name,
    )(*args)


def work_shapes(tile_count, pixels, listed):
    spans = 2 * tile_count * pixels // LANES
    assert (spans - 1) * SPAN_STEP < LIST_STEP
    return [pltpu.VMEM((listed * LIST_STEP, LANES), F32)] * 4 + [
        pltpu.VMEM((listed, spans * LANES), BF16),
        pltpu.VMEM((listed, spans * LANES), BF16),
        pltpu.VMEM((24, listed), F32),
        pltpu.VMEM((2, LANES, spans * LANES), F32),
        pltpu.VMEM((2, tile_count, ROWS, listed), F32),
    ]


def near(tile_ids, cameras, where, own, other, parts, tile_count):
    width = sum(part.shape[1] for part in parts)
    features = parts[0].shape[0]
    slabs = width // LANES
    pixels = listed = own.shape[1] // tile_count
    return call(
        functools.partial(near_kernel, len(parts)),
        "near",
        (
            jax.ShapeDtypeStruct((3, own.shape[1]), F32),
            jax.ShapeDtypeStruct((ROWS * slabs, LANES), F32),
            jax.ShapeDtypeStruct((ROWS, width), F32),
        ),
        [smem()] * 3 + [vmem()] * (2 + len(parts)),
        [pltpu.VMEM((features * slabs, LANES), F32), pltpu.VMEM((2,) + own.shape, F32)]
        + work_shapes(tile_count, pixels, listed),
        (tile_ids, cameras, where, own, other, *parts),
    )


def far(tile_ids, where, rows, partial, infos, pieces, tile_count, blocks):
    width = partial.shape[1]
    pixels = listed = infos.shape[1] // tile_count
    info = (infos.shape[0] // 2, infos.shape[1])
    return call(
        functools.partial(far_kernel, blocks),
        "far",
        (jax.ShapeDtypeStruct((ROWS, width // pieces), F32),) * pieces,
        [smem()] * 2 + [vmem()] * 3,
        [pltpu.VMEM((2,) + info, F32)] + work_shapes(tile_count, pixels, listed),
        (tile_ids, where, rows, partial, infos),
    )


def join(first, second):
    shape = (2 * first.shape[0], first.shape[1])
    return call(
        join_kernel, "join", (jax.ShapeDtypeStruct(shape, F32),), [vmem()] * 2, [], (first, second)
    )[0]


def update(where, cameras, params, adam_m, adam_v, packets):
    features, width = params.shape
    slabs = width // LANES
    shape = jax.ShapeDtypeStruct(params.shape, F32)
    return call(
        functools.partial(update_kernel, len(packets)),
        "update",
        (shape, shape, shape),
        [smem()] * 2 + [vmem()] * len(packets) + [any_space()] * 3,
        [
            pltpu.VMEM((features * slabs, LANES), F32),
            pltpu.VMEM((ROWS * slabs, LANES), F32),
            pltpu.VMEM((features * slabs, LANES), F32),
            pltpu.VMEM((3,) + params.shape, F32),
            pltpu.VMEM((3,) + params.shape, F32),
            pltpu.SemaphoreType.DMA((3,)),
            pltpu.SemaphoreType.DMA((3, (features + 15) // 16)),
        ],
        (where, cameras, *packets, params, adam_m, adam_v),
        (any_space(),) * 3,
    )


def swap(value, axis, d):
    if d == 0:
        return value
    return lax.ppermute(value, axis, [(k, k ^ d) for k in range(lax.axis_size(axis))])


def local(params, adam_m, adam_v, cameras, target, tile_ids, hit_shard, hit_local):
    width = params.shape[1]
    tile_count, listed = hit_local.shape
    shards = lax.axis_size("gs")
    along = lax.axis_size("tile")
    chunk = width // shards
    group = lax.axis_index("gs")
    seat = lax.axis_index("tile")
    aligned = chunk % LANES == 0
    team = BLOCK_TILES // tile_count
    assert team == 4
    blocks = along // team

    info, parts = pack(group, params, target, hit_shard, hit_local, shards, aligned)
    if not aligned:
        parts = [
            lax.dynamic_slice_in_dim(params, (group ^ d) * chunk, chunk, axis=1)
            for d in range(shards)
        ]
    parts = [swap(parts[d], "gs", d) for d in range(shards)]
    beside = swap(info, "tile", 1)
    beyond = swap(join(info, beside), "tile", 2)
    if not aligned:
        parts = [jnp.concatenate(parts, axis=1)]
    where = jnp.stack([seat % team, seat // team, jnp.int32(chunk)]).astype(jnp.int32)
    rendered, rows, partial = near(tile_ids, cameras, where, info, beside, parts, tile_count)
    packets = far(tile_ids, where, rows, partial, beyond, len(parts), tile_count, blocks)
    if not aligned:
        packets = [packets[0][:, d * chunk : (d + 1) * chunk] for d in range(shards)]
    packets = [swap(packets[d], "gs", d) for d in range(shards)]
    if blocks > 1:
        packets = [block_sum(packet, along, team) for packet in packets]
    if aligned:
        own = group
    else:
        packets = [jnp.stack(packets)[jnp.arange(shards) ^ group].transpose(1, 0, 2).reshape(ROWS, -1)]
        own = jnp.int32(0)
    new_params, new_m, new_v = update(
        own.reshape(1), cameras, params, adam_m, adam_v, packets
    )
    return (rendered, new_params, new_m, new_v)


def block_sum(packet, along, team):
    step = team
    while step < along:
        packet = packet + swap(packet, "tile", step)
        step *= 2
    return packet


def solution(mesh):
    return jax.shard_map(
        local,
        mesh=mesh,
        in_specs=(
            P(None, ("groups", "gs")),
            P(None, ("groups", "gs")),
            P(None, ("groups", "gs")),
            P("groups", None),
            P(None, ("groups", "gs", "tile")),
            P(("groups", "gs", "tile")),
            P(("groups", "gs", "tile"), None, None),
            P(("groups", "gs", "tile"), None),
        ),
        out_specs=(
            P(None, ("groups", "gs", "tile")),
            P(None, ("groups", "gs")),
            P(None, ("groups", "gs")),
            P(None, ("groups", "gs")),
        ),
        check_vma=False,
    )
```

```python
import functools

import jax
import jax.numpy as jnp
from jax import lax
from jax.experimental import pallas as pl
from jax.experimental.pallas import tpu as pltpu
from jax.sharding import PartitionSpec as P

TILES_X = 120
TILES_Y = 68
TILE_SIDE = 16
BLOCK_TILES = 8
LANES = 128
ROWS = 16
SPAN_STEP, LIST_STEP = 3, 25
F32 = jnp.float32
BF16 = jnp.bfloat16

focal_length = 1000.0
center_x = 960.0
center_y = 540.0
dilation = 0.3
beta_one = 0.9
beta_two = 0.999
learn_rate = 0.01
adam_eps = 1e-08
adam_steps = 100.0
sh_const = (
    0.28209479177387814,
    0.4886025119029199,
    1.0925484305920792,
    0.31539156525252005,
    0.5462742152960396,
    0.5900435899266435,
    2.890611442640554,
    0.4570457994644658,
    0.3731763325901154,
    1.445305721320277,
)


def sh_basis(x, y, z):
    s = sh_const
    xx, yy, zz = x * x, y * y, z * z
    return [
        None,
        -s[1] * y,
        s[1] * z,
        -s[1] * x,
        s[2] * (x * y),
        -s[2] * (y * z),
        s[3] * (2.0 * zz - xx - yy),
        -s[2] * (x * z),
        s[4] * (xx - yy),
        -s[5] * y * (3.0 * xx - yy),
        s[6] * (x * y) * z,
        -s[7] * y * (4.0 * zz - xx - yy),
        s[8] * z * (2.0 * zz - 3.0 * xx - 3.0 * yy),
        -s[7] * x * (4.0 * zz - xx - yy),
        s[9] * z * (xx - yy),
        -s[5] * x * (xx - 3.0 * yy),
    ]


def sh_pull(h, x, y, z):
    s = sh_const
    xx, yy, zz = x * x, y * y, z * z
    xy, xz, yz = x * y, x * z, y * z
    diff = xx - yy
    ring = 4.0 * zz - xx - yy
    g_x = (
        -s[1] * h[3]
        + s[2] * (h[4] * y - h[7] * z)
        - (2.0 * s[3]) * h[6] * x
        + (2.0 * s[4]) * h[8] * x
        - (6.0 * s[5]) * h[9] * xy
        + s[6] * h[10] * yz
        + (2.0 * s[7]) * h[11] * xy
        - (6.0 * s[8]) * h[12] * xz
        - s[7] * h[13] * (ring - 2.0 * xx)
        + (2.0 * s[9]) * h[14] * xz
        - (3.0 * s[5]) * h[15] * diff
    )
    g_y = (
        -s[1] * h[1]
        + s[2] * (h[4] * x - h[5] * z)
        - (2.0 * s[3]) * h[6] * y
        - (2.0 * s[4]) * h[8] * y
        - (3.0 * s[5]) * h[9] * diff
        + s[6] * h[10] * xz
        - s[7] * h[11] * (ring - 2.0 * yy)
        - (6.0 * s[8]) * h[12] * yz
        + (2.0 * s[7]) * h[13] * xy
        - (2.0 * s[9]) * h[14] * yz
        + (6.0 * s[5]) * h[15] * xy
    )
    g_z = (
        s[1] * h[2]
        - s[2] * (h[5] * y + h[7] * x)
        + (4.0 * s[3]) * h[6] * z
        + s[6] * h[10] * xy
        - (8.0 * s[7]) * (h[11] * yz + h[13] * xz)
        + s[8] * h[12] * (6.0 * zz - 3.0 * xx - 3.0 * yy)
        + s[9] * h[14] * diff
    )
    return g_x, g_y, g_z


def project_parts(feat, cam):
    rot = [[cam[3 * r + c] for c in range(3)] for r in range(3)]
    off = [feat(a) - cam[9 + a] for a in range(3)]
    in_cam = [rot[r][0] * off[0] + rot[r][1] * off[1] + rot[r][2] * off[2] for r in range(3)]
    inv = 1.0 / in_cam[2]
    u = in_cam[0] * inv
    v = in_cam[1] * inv
    finv = focal_length * inv
    scale = [jnp.exp(2.0 * feat(3 + a)) for a in range(3)]
    quat = [feat(6 + a) for a in range(4)]
    rnorm = lax.rsqrt(quat[0] * quat[0] + quat[1] * quat[1] + quat[2] * quat[2] + quat[3] * quat[3])
    w, x, y, z = [q * rnorm for q in quat]
    turn = [
        [1.0 - 2.0 * (y * y + z * z), 2.0 * (x * y - w * z), 2.0 * (x * z + w * y)],
        [2.0 * (x * y + w * z), 1.0 - 2.0 * (x * x + z * z), 2.0 * (y * z - w * x)],
        [2.0 * (x * z - w * y), 2.0 * (y * z + w * x), 1.0 - 2.0 * (x * x + y * y)],
    ]
    screen = [
        [finv * (rot[0][c] - u * rot[2][c]) for c in range(3)],
        [finv * (rot[1][c] - v * rot[2][c]) for c in range(3)],
    ]
    axes = [
        [sum(screen[r][c] * turn[c][k] for c in range(3)) for k in range(3)] for r in range(2)
    ]
    wide = [[axes[r][k] * scale[k] for k in range(3)] for r in range(2)]
    cov_xx = sum(wide[0][k] * axes[0][k] for k in range(3)) + dilation
    cov_xy = sum(wide[0][k] * axes[1][k] for k in range(3))
    cov_yy = sum(wide[1][k] * axes[1][k] for k in range(3)) + dilation
    rdet = 1.0 / (cov_xx * cov_yy - cov_xy * cov_xy)
    conic = (cov_yy * rdet, -cov_xy * rdet, cov_xx * rdet)
    rlen = lax.rsqrt(off[0] * off[0] + off[1] * off[1] + off[2] * off[2])
    way = [off[a] * rlen for a in range(3)]
    return dict(
        rot=rot, inv=inv, u=u, v=v, finv=finv, scale=scale, rnorm=rnorm, rotor=(w, x, y, z), turn=turn,
        screen=screen, axes=axes, wide=wide, conic=conic, rlen=rlen, way=way,
    )


def project_rows(feat, cam):
    part = project_parts(feat, cam)
    basis = sh_basis(*part["way"])
    colours = []
    for k in range(3):
        total = 0.5 + sh_const[0] * feat(11 + 16 * k)
        for b in range(1, 16):
            total = total + feat(11 + 16 * k + b) * basis[b]
        colours.append(total)
    mean_x = focal_length * part["u"] + center_x
    mean_y = focal_length * part["v"] + center_y
    logit = feat(10)
    log_opacity = jnp.minimum(logit, 0.0) - jnp.log(1.0 + jnp.exp(-jnp.abs(logit)))
    return [mean_x, mean_y, *part["conic"], log_opacity, *colours]


def project_pull(feat, cam, grads, put):
    part = project_parts(feat, cam)
    g_mx, g_my, g_a, g_b, g_c, g_o = grads[:6]
    g_col = grads[6:9]
    way, rlen = part["way"], part["rlen"]
    basis = sh_basis(*way)
    pulled = [None]
    for k in range(3):
        put(11 + 16 * k, sh_const[0] * g_col[k])
    for b in range(1, 16):
        total = 0.0
        for k in range(3):
            put(11 + 16 * k + b, g_col[k] * basis[b])
            total = total + g_col[k] * feat(11 + 16 * k + b)
        pulled.append(total)
    g_way = sh_pull(pulled, *way)
    along = way[0] * g_way[0] + way[1] * g_way[1] + way[2] * g_way[2]
    g_off = [(g_way[a] - way[a] * along) * rlen for a in range(3)]
    put(10, g_o / (1.0 + jnp.exp(feat(10))))
    a, b, c = part["conic"]
    g_xx = -(a * a * g_a + a * b * g_b + b * b * g_c)
    g_xy = -(2.0 * a * b * g_a + (a * c + b * b) * g_b + 2.0 * b * c * g_c)
    g_yy = -(b * b * g_a + b * c * g_b + c * c * g_c)
    axes, wide, turn, screen = part["axes"], part["wide"], part["turn"], part["screen"]
    for k in range(3):
        g_scale = (
            g_xx * axes[0][k] * wide[0][k]
            + g_xy * axes[0][k] * wide[1][k]
            + g_yy * axes[1][k] * wide[1][k]
        )
        put(3 + k, 2.0 * g_scale)
    g_axes = [
        [2.0 * g_xx * wide[0][k] + g_xy * wide[1][k] for k in range(3)],
        [2.0 * g_yy * wide[1][k] + g_xy * wide[0][k] for k in range(3)],
    ]
    g_screen = [
        [sum(g_axes[r][k] * turn[c][k] for k in range(3)) for c in range(3)] for r in range(2)
    ]
    gm = [
        [g_axes[0][k] * screen[0][c] + g_axes[1][k] * screen[1][c] for k in range(3)]
        for c in range(3)
    ]
    w, x, y, z = part["rotor"]
    up_xy, up_xz, up_yz = gm[0][1] + gm[1][0], gm[0][2] + gm[2][0], gm[1][2] + gm[2][1]
    un_xy, un_xz, un_yz = gm[1][0] - gm[0][1], gm[0][2] - gm[2][0], gm[2][1] - gm[1][2]
    g_rotor = [
        2.0 * (z * un_xy + y * un_xz + x * un_yz),
        2.0 * (y * up_xy + z * up_xz + w * un_yz - 2.0 * x * (gm[1][1] + gm[2][2])),
        2.0 * (x * up_xy + z * up_yz + w * un_xz - 2.0 * y * (gm[0][0] + gm[2][2])),
        2.0 * (x * up_xz + y * up_yz + w * un_xy - 2.0 * z * (gm[0][0] + gm[1][1])),
    ]
    rotor = (w, x, y, z)
    along = sum(rotor[i] * g_rotor[i] for i in range(4))
    for i in range(4):
        put(6 + i, (g_rotor[i] - rotor[i] * along) * part["rnorm"])
    rot, inv, finv, u, v = part["rot"], part["inv"], part["finv"], part["u"], part["v"]
    g_u = focal_length * g_mx - finv * sum(g_screen[0][c] * rot[2][c] for c in range(3))
    g_v = focal_length * g_my - finv * sum(g_screen[1][c] * rot[2][c] for c in range(3))
    g_f = sum(g_screen[r][c] * screen[r][c] for r in range(2) for c in range(3))
    g_in = [g_u * inv, g_v * inv, -(g_f + g_u * u + g_v * v) * inv]
    for axis in range(3):
        put(
            axis,
            g_off[axis] + rot[0][axis] * g_in[0] + rot[1][axis] * g_in[1] + rot[2][axis] * g_in[2],
        )


def split(value):
    high = value.astype(BF16)
    return high, (value - high.astype(F32)).astype(BF16)


def matmul(a, b, dims=((1,), (0,))):
    return lax.dot_general(a, b, (dims, ((), ())), preferred_element_type=F32)


def spread_features(parts, scratch, count):
    tiles = sum(part.shape[1] for part in parts) // LANES
    at = 0
    for part in parts:
        for first in range(0, part.shape[1], LANES):
            for row in range(0, count, 8):
                rows = min(8, count - row)
                scratch[pl.ds(row * tiles + at, rows, stride=tiles), :] = part[
                    row : row + rows, first : first + LANES
                ]
            at += 1
    return tiles


def pack_kernel(shards, pieces, where, *refs):
    sources, refs = refs[: 3 + (pieces > 0)], refs[3 + (pieces > 0) :]
    info, parts, refs = refs[0], refs[1 : 1 + pieces], refs[1 + pieces :]
    shard_of, local_of, goal, place_s, sems, cut_sems = refs
    group = where[0]
    loads = [
        pltpu.make_async_copy(source, held, sems.at[k])
        for k, (source, held) in enumerate(zip(sources, (shard_of, local_of, goal)))
    ]
    for d in range(pieces):
        chunk = parts[d].shape[1]
        first = pl.multiple_of((group ^ d) * chunk, LANES)
        loads.append(
            pltpu.make_async_copy(sources[3].at[:, pl.ds(first, chunk)], parts[d], cut_sems.at[d])
        )
    for load in loads:
        load.start()
    for load in loads[:3]:
        load.wait()
    width = info.shape[1]
    tile_count, listed = local_of.shape
    rows_each = (info.shape[0] - 4) // tile_count
    columns = rows_each * width
    chunk = columns // shards
    info[0:3, :] = goal[...]
    for t in range(tile_count):
        place = (shard_of[t] ^ group) * chunk + (local_of[t : t + 1, :] - group * chunk)
        info[3:4, t * listed : (t + 1) * listed] = place.astype(F32)
        row_i = lax.broadcasted_iota(jnp.int32, (LANES, LANES), 0)
        col_i = lax.broadcasted_iota(jnp.int32, (LANES, LANES), 1)
        for first in range(0, listed, LANES):
            spread = jnp.broadcast_to(place[:, first : first + LANES].astype(F32), (LANES, LANES))
            place_s[first : first + LANES, :] = jnp.broadcast_to(
                jnp.sum(jnp.where(row_i == col_i, spread, 0.0), axis=1, keepdims=True), (LANES, LANES)
            )
        lane_of = lax.broadcasted_iota(jnp.int32, (8, LANES), 1).astype(F32)
        row_of = lax.broadcasted_iota(jnp.int32, (8, LANES), 0).astype(F32)
        for s in range(columns // LANES):
            best = jnp.full((8, LANES), -1.0, F32)
            column = lane_of + float(s * LANES)
            for first in range(0, listed, 8):
                best = jnp.where(
                    place_s[first : first + 8, :] == column, row_of + float(first), best
                )
            best = jnp.max(best, axis=0, keepdims=True)
            row, at = 4 + t * rows_each + s * LANES // width, s * LANES % width
            info[row : row + 1, at : at + LANES] = best
    for load in loads[3:]:
        load.wait()


def pack(group, params, target, hit_shard, hit_local, shards, aligned):
    features, columns = params.shape
    tile_count, listed = hit_local.shape
    width = target.shape[1]
    rows = 4 + tile_count * (columns // width)
    pieces = shards if aligned else 0
    piece = jax.ShapeDtypeStruct((features, columns // shards), F32)
    args = (hit_shard.reshape(tile_count, 1, listed), hit_local, target) + (params,) * aligned
    out = call(
        functools.partial(pack_kernel, shards, pieces),
        "pack",
        (jax.ShapeDtypeStruct((rows, width), F32),) + (piece,) * pieces,
        [smem()] + [pl.BlockSpec(memory_space=pltpu.HBM)] * len(args),
        [
            pltpu.VMEM((tile_count, 1, listed), jnp.int32),
            pltpu.VMEM((tile_count, listed), jnp.int32),
            pltpu.VMEM(target.shape, F32),
            pltpu.VMEM((listed, LANES), F32),
            pltpu.SemaphoreType.DMA((3,)),
            pltpu.SemaphoreType.DMA((shards,)),
        ],
        (group.reshape(1),) + tuple(pltpu.with_memory_space_constraint(a, pltpu.HBM) for a in args),
    )
    return out[0], list(out[1:])


def pixel_basis(pixels):
    pixel = lax.broadcasted_iota(jnp.int32, (8, pixels), 1)
    row = lax.broadcasted_iota(jnp.int32, (8, pixels), 0)
    middle = 0.5 * TILE_SIDE - 0.5
    u = (pixel % TILE_SIDE).astype(F32) - middle
    v = (pixel // TILE_SIDE).astype(F32) - middle
    value = jnp.where(row == 0, 1.0, 0.0)
    for at, term in ((1, u), (2, v), (3, u * u), (4, u * v), (5, v * v)):
        value = jnp.where(row == at, term, value)
    return value


def composite(tiles, first_group, me, rows, info_s, rendered, work):
    alpha_s, weight_s, pull_s, push_s, weight_2, coef_s, colour_s, error_s, mix_s, index_s, acc_s = work
    groups, tile_count, _, listed = acc_s.shape
    pixels = info_s.shape[2] // tile_count
    parts = pixels // LANES
    halves = listed // LANES
    tiles_here = groups * tile_count
    spans = tiles_here * parts
    slabs = rows.shape[0] // ROWS
    side = TILE_SIDE
    first_col, first_row = tiles

    def of_span(span):
        return pl.ds(span * SPAN_STEP, listed, stride=LIST_STEP)

    def of_place(place):
        return pl.ds(place * LIST_STEP, spans, stride=SPAN_STEP)

    def lane_gather(source, lane):
        return jnp.take_along_axis(source, lane, axis=1, mode="promise_in_bounds")

    basis = pixel_basis(pixels)
    basis_3 = jnp.concatenate([basis, basis, basis], axis=0).astype(BF16)

    entries = []
    for n in range(tiles_here):
        g, t = n // tile_count, n % tile_count
        found = []
        for h in range(halves):
            first = t * listed + h * LANES
            at = info_s[g, 3:4, first : first + LANES].astype(jnp.int32)
            index_s[n * halves + h : n * halves + h + 1, :] = at
            at = jnp.broadcast_to(at, (8, LANES))
            lane, slab = at & (LANES - 1), at >> 7
            value = lane_gather(rows[0:8, :], lane)
            for s in range(1, slabs):
                value = jnp.where(
                    slab == s, lane_gather(rows[s * ROWS : s * ROWS + 8, :], lane), value
                )
            found.append(value)
        entries.append(jnp.concatenate(found, axis=1))
    at = index_s[...]
    lane, slab = at & (LANES - 1), at >> 7
    ninth = lane_gather(rows[8:16, :], lane)
    for s in range(1, slabs):
        ninth = jnp.where(
            slab == s, lane_gather(rows[s * ROWS + 8 : s * ROWS + 16, :], lane), ninth
        )

    means = []
    colour_s[...] = jnp.zeros(colour_s.shape, F32)
    for n in range(tiles_here):
        g, t = n // tile_count, n % tile_count
        entry = entries[n]
        slot = (me ^ (first_group + g)) * tile_count + t
        mean_u = entry[0:1] - (((first_col + slot % 4) * side).astype(F32) + 0.5 * side)
        mean_v = entry[1:2] - (((first_row + slot // 4) * side).astype(F32) + 0.5 * side)
        quad_a, quad_b, quad_c = -0.5 * entry[2:3], -entry[3:4], -0.5 * entry[4:5]
        means.append((mean_u, mean_v, quad_a, quad_b, quad_c))
        slope_u = 2.0 * quad_a * mean_u + quad_b * mean_v
        slope_v = 2.0 * quad_c * mean_v + quad_b * mean_u
        level = 0.5 * (slope_u * mean_u + slope_v * mean_v) + entry[5:6]
        zero = jnp.zeros_like(level)
        coef = jnp.concatenate(
            [level, -slope_u, -slope_v, quad_a, quad_b, quad_c, zero, zero], axis=0
        )
        here = slice(n * listed, (n + 1) * listed)
        for part in range(3):
            term = coef.astype(BF16).astype(F32)
            coef_s[part * 8 : part * 8 + 8, here] = term
            coef = coef - term
        last = [ninth[n * halves + h : n * halves + h + 1] for h in range(halves)]
        colours = jnp.concatenate([entry[6:8], jnp.concatenate(last, axis=1)], axis=0)
        high = colours.astype(BF16).astype(F32)
        colour_s[n * ROWS : n * ROWS + 3, here] = high
        colour_s[n * ROWS + 3 : n * ROWS + 6, here] = colours - high
        colour_s[n * ROWS + 6 : n * ROWS + 9, here] = high

    down = ((0,), (0,))
    power = matmul(coef_s[...].astype(BF16), basis_3, down)
    for n in range(tiles_here):
        for part in range(parts):
            alpha_s[of_span(n * parts + part), :] = jnp.exp(
                power[n * listed : (n + 1) * listed, part * LANES : (part + 1) * LANES]
            )

    unroll, quad = 32, 4
    steps = listed // unroll

    def forward(step, passed):
        for j in range(0, unroll, quad):
            at = [of_place(step * unroll + j + i) for i in range(quad)]
            alpha = [alpha_s[at[i], :] for i in range(quad)]
            keep = [1.0 - alpha[i] for i in range(quad)]
            two = keep[0] * keep[1]
            three = two * keep[2]
            weight_s[at[0], :] = alpha[0] * passed
            weight_s[at[1], :] = (alpha[1] * keep[0]) * passed
            weight_s[at[2], :] = (alpha[2] * two) * passed
            weight_s[at[3], :] = (alpha[3] * three) * passed
            passed = passed * (two * (keep[2] * keep[3]))
        return passed

    nought = jnp.zeros((spans, LANES), F32)
    lax.fori_loop(0, steps, forward, nought + 1.0)

    error_s[...] = jnp.zeros(error_s.shape, F32)
    mix_s[...] = jnp.zeros(mix_s.shape, F32)
    for n in range(tiles_here):
        g, t = n // tile_count, n % tile_count
        for part in range(parts):
            at = slice((n * parts + part) * LANES, (n * parts + part + 1) * LANES)
            weight_2[:listed, at], weight_2[listed:, at] = split(
                weight_s[of_span(n * parts + part), :]
            )
        at = slice(n * pixels, (n + 1) * pixels)
        colours = colour_s[n * ROWS : (n + 1) * ROWS, n * listed : (n + 1) * listed].astype(BF16)
        image = matmul(colours, weight_2[:listed, at])
        image = image[0:3] + image[3:6] + matmul(colours, weight_2[listed:, at])[0:3]
        here = slice(t * pixels, (t + 1) * pixels)
        if rendered is not None and g == 0:
            rendered[:, here] = image
        error = image - info_s[g, 0:3, here]
        high = error.astype(BF16).astype(F32)
        low = error - high
        error_s[n * ROWS : n * ROWS + 3, :] = high
        error_s[n * ROWS + 3 : n * ROWS + 6, :] = high
        error_s[n * ROWS + 6 : n * ROWS + 9, :] = low
        mix_s[0, n * ROWS : n * ROWS + 8, at] = basis
        mix_s[1, n * ROWS + 6 : n * ROWS + 9, at] = high
        mix_s[1, n * ROWS + 9 : n * ROWS + 12, at] = low
    pull = matmul(colour_s[...].astype(BF16), error_s[...].astype(BF16), down)
    for n in range(tiles_here):
        for part in range(parts):
            pull_s[of_span(n * parts + part), :] = pull[
                n * listed : (n + 1) * listed, part * LANES : (part + 1) * LANES
            ]

    def backward(back, behind):
        for j in range(0, unroll, quad):
            at = [of_place(listed - 1 - (back * unroll + j + i)) for i in range(quad)]
            alpha = [alpha_s[at[i], :] for i in range(quad)]
            pull = [pull_s[at[i], :] for i in range(quad)]
            keep = [1.0 - alpha[i] for i in range(quad)]
            own = alpha[0] * pull[0]
            seen, through = behind, keep[0]
            for i in range(quad):
                push_s[at[i], :] = weight_s[at[i], :] * (pull[i] - seen)
                if i > 0:
                    own = own * keep[i] + alpha[i] * pull[i]
                    through = through * keep[i]
                seen = behind * through + own
            behind = seen
        return behind

    lax.fori_loop(0, steps, backward, nought)

    across = ((1,), (1,))
    high, low = split(jnp.concatenate([push_s[of_span(span), :] for span in range(spans)], axis=1))
    sums = matmul(jnp.concatenate([high, low], axis=0), mix_s[0].astype(BF16), across)
    sums = sums + matmul(weight_2[...], mix_s[1].astype(BF16), across)
    sums = (sums[:listed] + sums[listed:]).T
    for n in range(tiles_here):
        g, t = n // tile_count, n % tile_count
        mean_u, mean_v, quad_a, quad_b, quad_c = means[n]
        m_00, m_10, m_01, m_20, m_11, m_02 = [
            sums[n * ROWS + m : n * ROWS + m + 1] for m in range(6)
        ]
        n_10 = m_10 - mean_u * m_00
        n_01 = m_01 - mean_v * m_00
        acc_s[g, t, 0:1, :] = -(2.0 * quad_a * n_10 + quad_b * n_01)
        acc_s[g, t, 1:2, :] = -(2.0 * quad_c * n_01 + quad_b * n_10)
        acc_s[g, t, 2:3, :] = -0.5 * (m_20 - mean_u * (m_10 + n_10))
        acc_s[g, t, 3:4, :] = -(m_11 - mean_u * m_01 - mean_v * n_10)
        acc_s[g, t, 4:5, :] = -0.5 * (m_02 - mean_v * (m_01 + n_01))
        acc_s[g, t, 5:6, :] = m_00
        at = n * ROWS + 6
        grads = sums[at : at + 3] + sums[at + 3 : at + 6]
        acc_s[g, t, 6:8, :] = grads[0:2]
        for h in range(halves):
            row = n * halves + h
            acc_s[0, 0, 8 + row : 9 + row, :LANES] = grads[2:3, h * LANES : (h + 1) * LANES]


def pool_sum(slab, info_s, acc_s):
    groups, tile_count, _, listed = acc_s.shape
    halves = listed // LANES
    width = info_s.shape[2]
    rows_each = (info_s.shape[1] - 4) // tile_count
    row_of = lax.broadcasted_iota(jnp.int32, (8, LANES), 0)

    def lane_gather(source, lane):
        return jnp.take_along_axis(source, lane, axis=1, mode="promise_in_bounds")

    totals, every = [], None
    for g in range(groups):
        total = jnp.zeros((8, LANES), F32)
        for t in range(tile_count):
            row, first = 4 + t * rows_each + slab * LANES // width, slab * LANES % width
            at = info_s[g, row : row + 1, first : first + LANES].astype(jnp.int32)
            at = jnp.broadcast_to(at, (8, LANES))
            n = g * tile_count + t
            every = at if every is None else jnp.where(row_of >= n * halves, at, every)
            lane, half = at & (LANES - 1), at >> 7
            for h in range(halves):
                here = lane_gather(acc_s[g, t, 0:8, h * LANES : (h + 1) * LANES], lane)
                total = total + jnp.where(half == h, here, 0.0)
        totals.append(total)
    here = lane_gather(acc_s[0, 0, 8:16, :LANES], every & (LANES - 1))
    ninth = jnp.where(every >> 7 == row_of % halves, here, 0.0)
    return totals[0] + totals[1], jnp.sum(ninth, axis=0, keepdims=True)


def block_start(tile_id):
    within = tile_id % (TILES_X * TILES_Y)
    return (within % TILES_X) // 4 * 4, (within // TILES_X) // 2 * 2


def near_kernel(pieces, tile_ids, cams, where, own, other, *refs):
    parts = refs[:pieces]
    rendered, rows, partial, feats, info_s, *work = refs[pieces:]
    view = tile_ids[0] // (TILES_X * TILES_Y)
    cam = [cams[view, i] for i in range(12)]
    slabs = spread_features(parts, feats, parts[0].shape[0])
    projected = project_rows(lambda f: feats[f * slabs : (f + 1) * slabs, :], cam)
    for f, value in enumerate(projected):
        rows[pl.ds(f, slabs, stride=ROWS), :] = value
    for f in range(len(projected), ROWS):
        rows[pl.ds(f, slabs, stride=ROWS), :] = projected[8]
    info_s[0] = own[...]
    info_s[1] = other[...]
    composite(block_start(tile_ids[0]), 0, where[0], rows, info_s, rendered, work)
    for s in range(slabs):
        at = slice(s * LANES, (s + 1) * LANES)
        partial[0:8, at], partial[8:9, at] = pool_sum(s, info_s, work[-1])


def far_kernel(blocks, tile_ids, where, rows, partial, infos, *refs):
    *packets, info_s = refs[: len(refs) - 11]
    work = refs[len(refs) - 11 :]
    half = infos.shape[0] // 2
    info_s[0] = infos[:half, :]
    info_s[1] = infos[half:, :]
    composite(block_start(tile_ids[0]), 2, where[0], rows, info_s, None, work)
    share = (tile_ids[0] // (TILES_X * TILES_Y)).astype(F32)
    row_of = lax.broadcasted_iota(jnp.int32, (8, LANES), 0)
    lane_of = lax.broadcasted_iota(jnp.int32, (8, LANES), 1)
    chunk = packets[0].shape[1]
    for s in range(rows.shape[0] // ROWS):
        total, ninth = pool_sum(s, info_s, work[-1])
        total = total + partial[0:8, s * LANES : (s + 1) * LANES]
        ninth = ninth + partial[8:9, s * LANES : (s + 1) * LANES]
        if blocks == 1:
            mine = share
        else:
            column = s * LANES + lane_of
            mine = jnp.where(column % where[2] // (where[2] // blocks) == where[1], share, 0.0)
        at = slice(s * LANES % chunk, s * LANES % chunk + LANES)
        packets[s * LANES // chunk][0:8, at] = total
        packets[s * LANES // chunk][8:16, at] = jnp.where(
            row_of == 0, jnp.broadcast_to(ninth, (8, LANES)), mine
        )


def join_kernel(first, second, out):
    half = first.shape[0]
    out[:half, :] = first[...]
    out[half:, :] = second[...]


def update_kernel(pieces, where, cams, *refs):
    packets = refs[:pieces]
    sources, sinks = refs[pieces : pieces + 3], refs[pieces + 3 : pieces + 6]
    feats, rows, grads, held, made, in_sems, out_sems = refs[pieces + 6 :]
    params, adam_m, adam_v = held.at[0], held.at[1], held.at[2]
    features, width = params.shape
    loads = [pltpu.make_async_copy(sources[k], held.at[k], in_sems.at[k]) for k in range(3)]
    for load in loads:
        load.start()
    chunk = packets[0].shape[1]
    slabs = width // LANES
    for d in range(pieces):
        for h in range(chunk // LANES):
            slab = (where[0] ^ d) * (chunk // LANES) + h
            rows[pl.ds(slab, ROWS, stride=slabs), :] = packets[d][:, h * LANES : (h + 1) * LANES]
    pulled = [rows[f * slabs : (f + 1) * slabs, :] for f in range(10)]
    view = pulled[9]
    cam = []
    for i in range(12):
        value = jnp.full((slabs, LANES), cams[0, i], F32)
        for v in range(1, cams.shape[0]):
            value = jnp.where(view == float(v), cams[v, i], value)
        cam.append(value)

    def put(f, value):
        grads[f * slabs : (f + 1) * slabs, :] = value

    loads[0].wait()
    spread_features([params], feats, features)
    project_pull(lambda f: feats[f * slabs : (f + 1) * slabs, :], cam, pulled[:9], put)
    rate = learn_rate / (1.0 - beta_one**adam_steps)
    unbias = 1.0 / (1.0 - beta_two**adam_steps)
    loads[1].wait()
    loads[2].wait()
    stores = []
    for row in range(0, features, 8):
        count = min(8, features - row)
        for s in range(slabs):
            at = (slice(row, row + count), slice(s * LANES, (s + 1) * LANES))
            grad = grads[pl.ds(row * slabs + s, count, stride=slabs), :]
            moment = beta_one * adam_m[at] + (1.0 - beta_one) * grad
            second = beta_two * adam_v[at] + (1.0 - beta_two) * grad * grad
            made.at[1][at] = moment
            made.at[2][at] = second
            made.at[0][at] = params[at] - rate * moment / (jnp.sqrt(second * unbias) + adam_eps)
        if row % 16 == 8 or row + count == features:
            first = row // 16 * 16
            span = pl.ds(first, row + count - first)
            for k in range(3):
                store = pltpu.make_async_copy(
                    made.at[k, span], sinks[k].at[span], out_sems.at[k, first // 16]
                )
                store.start()
                stores.append(store)
    for store in stores:
        store.wait()


def vmem():
    return pl.BlockSpec(memory_space=pltpu.VMEM)


def smem():
    return pl.BlockSpec(memory_space=pltpu.SMEM)


def any_space():
    return pl.BlockSpec(memory_space=pl.ANY)


def call(kernel, name, out_shape, in_specs, scratch, args, out_specs=None, grant=32):
    return pl.pallas_call(
        kernel,
        out_shape=out_shape,
        in_specs=in_specs,
        out_specs=out_specs or tuple(vmem() for _ in out_shape),
        scratch_shapes=scratch,
        compiler_params=pltpu.CompilerParams(vmem_limit_bytes=grant * 1024 * 1024),
        name=name,
    )(*args)


def work_shapes(tile_count, pixels, listed):
    tiles = 2 * tile_count
    spans = tiles * pixels // LANES
    assert (spans - 1) * SPAN_STEP < LIST_STEP and tiles * listed // LANES == 8
    return [pltpu.VMEM((listed * LIST_STEP, LANES), F32)] * 4 + [
        pltpu.VMEM((2 * listed, spans * LANES), BF16),
        pltpu.VMEM((24, tiles * listed), F32),
        pltpu.VMEM((tiles * ROWS, tiles * listed), F32),
        pltpu.VMEM((tiles * ROWS, pixels), F32),
        pltpu.VMEM((2, LANES, spans * LANES), F32),
        pltpu.VMEM((8, LANES), jnp.int32),
        pltpu.VMEM((2, tile_count, ROWS, listed), F32),
    ]


def near(tile_ids, cameras, where, own, other, parts, tile_count):
    width = sum(part.shape[1] for part in parts)
    features = parts[0].shape[0]
    slabs = width // LANES
    pixels = listed = own.shape[1] // tile_count
    return call(
        functools.partial(near_kernel, len(parts)),
        "near",
        (
            jax.ShapeDtypeStruct((3, own.shape[1]), F32),
            jax.ShapeDtypeStruct((ROWS * slabs, LANES), F32),
            jax.ShapeDtypeStruct((ROWS, width), F32),
        ),
        [smem()] * 3 + [vmem()] * (2 + len(parts)),
        [pltpu.VMEM((features * slabs, LANES), F32), pltpu.VMEM((2,) + own.shape, F32)]
        + work_shapes(tile_count, pixels, listed),
        (tile_ids, cameras, where, own, other, *parts),
    )


def far(tile_ids, where, rows, partial, infos, pieces, tile_count, blocks):
    width = partial.shape[1]
    pixels = listed = infos.shape[1] // tile_count
    info = (infos.shape[0] // 2, infos.shape[1])
    return call(
        functools.partial(far_kernel, blocks),
        "far",
        (jax.ShapeDtypeStruct((ROWS, width // pieces), F32),) * pieces,
        [smem()] * 2 + [vmem()] * 3,
        [pltpu.VMEM((2,) + info, F32)] + work_shapes(tile_count, pixels, listed),
        (tile_ids, where, rows, partial, infos),
    )


def join(first, second):
    shape = (2 * first.shape[0], first.shape[1])
    return call(
        join_kernel, "join", (jax.ShapeDtypeStruct(shape, F32),), [vmem()] * 2, [], (first, second)
    )[0]


def update(where, cameras, params, adam_m, adam_v, packets):
    features, width = params.shape
    slabs = width // LANES
    shape = jax.ShapeDtypeStruct(params.shape, F32)
    return call(
        functools.partial(update_kernel, len(packets)),
        "update",
        (shape, shape, shape),
        [smem()] * 2 + [vmem()] * len(packets) + [any_space()] * 3,
        [
            pltpu.VMEM((features * slabs, LANES), F32),
            pltpu.VMEM((ROWS * slabs, LANES), F32),
            pltpu.VMEM((features * slabs, LANES), F32),
            pltpu.VMEM((3,) + params.shape, F32),
            pltpu.VMEM((3,) + params.shape, F32),
            pltpu.SemaphoreType.DMA((3,)),
            pltpu.SemaphoreType.DMA((3, (features + 15) // 16)),
        ],
        (where, cameras, *packets, params, adam_m, adam_v),
        (any_space(),) * 3,
    )


def swap(value, axis, d):
    if d == 0:
        return value
    return lax.ppermute(value, axis, [(k, k ^ d) for k in range(lax.axis_size(axis))])


def local(params, adam_m, adam_v, cameras, target, tile_ids, hit_shard, hit_local):
    width = params.shape[1]
    tile_count, listed = hit_local.shape
    shards = lax.axis_size("gs")
    along = lax.axis_size("tile")
    chunk = width // shards
    group = lax.axis_index("gs")
    seat = lax.axis_index("tile")
    aligned = chunk % LANES == 0
    team = BLOCK_TILES // tile_count
    assert team == 4
    blocks = along // team

    info, parts = pack(group, params, target, hit_shard, hit_local, shards, aligned)
    if not aligned:
        parts = [
            lax.dynamic_slice_in_dim(params, (group ^ d) * chunk, chunk, axis=1)
            for d in range(shards)
        ]
    parts = [swap(parts[d], "gs", d) for d in range(shards)]
    beside = swap(info, "tile", 1)
    beyond = swap(join(info, beside), "tile", 2)
    if not aligned:
        parts = [jnp.concatenate(parts, axis=1)]
    where = jnp.stack([seat % team, seat // team, jnp.int32(chunk)]).astype(jnp.int32)
    rendered, rows, partial = near(tile_ids, cameras, where, info, beside, parts, tile_count)
    packets = far(tile_ids, where, rows, partial, beyond, len(parts), tile_count, blocks)
    if not aligned:
        packets = [packets[0][:, d * chunk : (d + 1) * chunk] for d in range(shards)]
    packets = [swap(packets[d], "gs", d) for d in range(shards)]
    if blocks > 1:
        packets = [block_sum(packet, along, team) for packet in packets]
    if aligned:
        own = group
    else:
        packets = [jnp.stack(packets)[jnp.arange(shards) ^ group].transpose(1, 0, 2).reshape(ROWS, -1)]
        own = jnp.int32(0)
    new_params, new_m, new_v = update(
        own.reshape(1), cameras, params, adam_m, adam_v, packets
    )
    return (rendered, new_params, new_m, new_v)


def block_sum(packet, along, team):
    step = team
    while step < along:
        packet = packet + swap(packet, "tile", step)
        step *= 2
    return packet


def solution(mesh):
    return jax.shard_map(
        local,
        mesh=mesh,
        in_specs=(
            P(None, ("groups", "gs")),
            P(None, ("groups", "gs")),
            P(None, ("groups", "gs")),
            P("groups", None),
            P(None, ("groups", "gs", "tile")),
            P(("groups", "gs", "tile")),
            P(("groups", "gs", "tile"), None, None),
            P(("groups", "gs", "tile"), None),
        ),
        out_specs=(
            P(None, ("groups", "gs", "tile")),
            P(None, ("groups", "gs")),
            P(None, ("groups", "gs")),
            P(None, ("groups", "gs")),
        ),
        check_vma=False,
    )
```

```python
import functools

import jax
import jax.numpy as jnp
from jax import lax
from jax.experimental import pallas as pl
from jax.experimental.pallas import tpu as pltpu
from jax.sharding import PartitionSpec as P

TILES_X = 120
TILES_Y = 68
TILE_SIDE = 16
BLOCK_TILES = 8
LANES = 128
ROWS = 16
F32 = jnp.float32
BF16 = jnp.bfloat16

focal_length = 1000.0
center_x = 960.0
center_y = 540.0
dilation = 0.3
beta_one = 0.9
beta_two = 0.999
learn_rate = 0.01
adam_eps = 1e-08
adam_steps = 100.0
sh_const = (
    0.28209479177387814,
    0.4886025119029199,
    1.0925484305920792,
    0.31539156525252005,
    0.5462742152960396,
    0.5900435899266435,
    2.890611442640554,
    0.4570457994644658,
    0.3731763325901154,
    1.445305721320277,
)


def sh_basis(x, y, z):
    s = sh_const
    xx, yy, zz = x * x, y * y, z * z
    return [
        None,
        -s[1] * y,
        s[1] * z,
        -s[1] * x,
        s[2] * (x * y),
        -s[2] * (y * z),
        s[3] * (2.0 * zz - xx - yy),
        -s[2] * (x * z),
        s[4] * (xx - yy),
        -s[5] * y * (3.0 * xx - yy),
        s[6] * (x * y) * z,
        -s[7] * y * (4.0 * zz - xx - yy),
        s[8] * z * (2.0 * zz - 3.0 * xx - 3.0 * yy),
        -s[7] * x * (4.0 * zz - xx - yy),
        s[9] * z * (xx - yy),
        -s[5] * x * (xx - 3.0 * yy),
    ]


def sh_pull(h, x, y, z):
    s = sh_const
    xx, yy, zz = x * x, y * y, z * z
    xy, xz, yz = x * y, x * z, y * z
    diff = xx - yy
    ring = 4.0 * zz - xx - yy
    g_x = (
        -s[1] * h[3]
        + s[2] * (h[4] * y - h[7] * z)
        - (2.0 * s[3]) * h[6] * x
        + (2.0 * s[4]) * h[8] * x
        - (6.0 * s[5]) * h[9] * xy
        + s[6] * h[10] * yz
        + (2.0 * s[7]) * h[11] * xy
        - (6.0 * s[8]) * h[12] * xz
        - s[7] * h[13] * (ring - 2.0 * xx)
        + (2.0 * s[9]) * h[14] * xz
        - (3.0 * s[5]) * h[15] * diff
    )
    g_y = (
        -s[1] * h[1]
        + s[2] * (h[4] * x - h[5] * z)
        - (2.0 * s[3]) * h[6] * y
        - (2.0 * s[4]) * h[8] * y
        - (3.0 * s[5]) * h[9] * diff
        + s[6] * h[10] * xz
        - s[7] * h[11] * (ring - 2.0 * yy)
        - (6.0 * s[8]) * h[12] * yz
        + (2.0 * s[7]) * h[13] * xy
        - (2.0 * s[9]) * h[14] * yz
        + (6.0 * s[5]) * h[15] * xy
    )
    g_z = (
        s[1] * h[2]
        - s[2] * (h[5] * y + h[7] * x)
        + (4.0 * s[3]) * h[6] * z
        + s[6] * h[10] * xy
        - (8.0 * s[7]) * (h[11] * yz + h[13] * xz)
        + s[8] * h[12] * (6.0 * zz - 3.0 * xx - 3.0 * yy)
        + s[9] * h[14] * diff
    )
    return g_x, g_y, g_z


def project_parts(feat, cam):
    rot = [[cam[3 * r + c] for c in range(3)] for r in range(3)]
    off = [feat(a) - cam[9 + a] for a in range(3)]
    in_cam = [rot[r][0] * off[0] + rot[r][1] * off[1] + rot[r][2] * off[2] for r in range(3)]
    inv = 1.0 / in_cam[2]
    u = in_cam[0] * inv
    v = in_cam[1] * inv
    finv = focal_length * inv
    scale = [jnp.exp(2.0 * feat(3 + a)) for a in range(3)]
    quat = [feat(6 + a) for a in range(4)]
    rnorm = lax.rsqrt(quat[0] * quat[0] + quat[1] * quat[1] + quat[2] * quat[2] + quat[3] * quat[3])
    w, x, y, z = [q * rnorm for q in quat]
    turn = [
        [1.0 - 2.0 * (y * y + z * z), 2.0 * (x * y - w * z), 2.0 * (x * z + w * y)],
        [2.0 * (x * y + w * z), 1.0 - 2.0 * (x * x + z * z), 2.0 * (y * z - w * x)],
        [2.0 * (x * z - w * y), 2.0 * (y * z + w * x), 1.0 - 2.0 * (x * x + y * y)],
    ]
    screen = [
        [finv * (rot[0][c] - u * rot[2][c]) for c in range(3)],
        [finv * (rot[1][c] - v * rot[2][c]) for c in range(3)],
    ]
    axes = [
        [sum(screen[r][c] * turn[c][k] for c in range(3)) for k in range(3)] for r in range(2)
    ]
    wide = [[axes[r][k] * scale[k] for k in range(3)] for r in range(2)]
    cov_xx = sum(wide[0][k] * axes[0][k] for k in range(3)) + dilation
    cov_xy = sum(wide[0][k] * axes[1][k] for k in range(3))
    cov_yy = sum(wide[1][k] * axes[1][k] for k in range(3)) + dilation
    rdet = 1.0 / (cov_xx * cov_yy - cov_xy * cov_xy)
    conic = (cov_yy * rdet, -cov_xy * rdet, cov_xx * rdet)
    rlen = lax.rsqrt(off[0] * off[0] + off[1] * off[1] + off[2] * off[2])
    way = [off[a] * rlen for a in range(3)]
    return dict(
        rot=rot, inv=inv, u=u, v=v, finv=finv, scale=scale, rnorm=rnorm, rotor=(w, x, y, z), turn=turn,
        screen=screen, axes=axes, wide=wide, conic=conic, rlen=rlen, way=way,
    )


def project_rows(feat, cam):
    part = project_parts(feat, cam)
    basis = sh_basis(*part["way"])
    colours = []
    for k in range(3):
        total = 0.5 + sh_const[0] * feat(11 + 16 * k)
        for b in range(1, 16):
            total = total + feat(11 + 16 * k + b) * basis[b]
        colours.append(total)
    mean_x = focal_length * part["u"] + center_x
    mean_y = focal_length * part["v"] + center_y
    logit = feat(10)
    log_opacity = jnp.minimum(logit, 0.0) - jnp.log(1.0 + jnp.exp(-jnp.abs(logit)))
    return [mean_x, mean_y, *part["conic"], log_opacity, *colours]


def project_pull(feat, cam, grads, put):
    part = project_parts(feat, cam)
    g_mx, g_my, g_a, g_b, g_c, g_o = grads[:6]
    g_col = grads[6:9]
    way, rlen = part["way"], part["rlen"]
    basis = sh_basis(*way)
    pulled = [None]
    for k in range(3):
        put(11 + 16 * k, sh_const[0] * g_col[k])
    for b in range(1, 16):
        total = 0.0
        for k in range(3):
            put(11 + 16 * k + b, g_col[k] * basis[b])
            total = total + g_col[k] * feat(11 + 16 * k + b)
        pulled.append(total)
    g_way = sh_pull(pulled, *way)
    along = way[0] * g_way[0] + way[1] * g_way[1] + way[2] * g_way[2]
    g_off = [(g_way[a] - way[a] * along) * rlen for a in range(3)]
    put(10, g_o / (1.0 + jnp.exp(feat(10))))
    a, b, c = part["conic"]
    g_xx = -(a * a * g_a + a * b * g_b + b * b * g_c)
    g_xy = -(2.0 * a * b * g_a + (a * c + b * b) * g_b + 2.0 * b * c * g_c)
    g_yy = -(b * b * g_a + b * c * g_b + c * c * g_c)
    axes, wide, turn, screen = part["axes"], part["wide"], part["turn"], part["screen"]
    for k in range(3):
        g_scale = (
            g_xx * axes[0][k] * wide[0][k]
            + g_xy * axes[0][k] * wide[1][k]
            + g_yy * axes[1][k] * wide[1][k]
        )
        put(3 + k, 2.0 * g_scale)
    g_axes = [
        [2.0 * g_xx * wide[0][k] + g_xy * wide[1][k] for k in range(3)],
        [2.0 * g_yy * wide[1][k] + g_xy * wide[0][k] for k in range(3)],
    ]
    g_screen = [
        [sum(g_axes[r][k] * turn[c][k] for k in range(3)) for c in range(3)] for r in range(2)
    ]
    gm = [
        [g_axes[0][k] * screen[0][c] + g_axes[1][k] * screen[1][c] for k in range(3)]
        for c in range(3)
    ]
    w, x, y, z = part["rotor"]
    up_xy, up_xz, up_yz = gm[0][1] + gm[1][0], gm[0][2] + gm[2][0], gm[1][2] + gm[2][1]
    un_xy, un_xz, un_yz = gm[1][0] - gm[0][1], gm[0][2] - gm[2][0], gm[2][1] - gm[1][2]
    g_rotor = [
        2.0 * (z * un_xy + y * un_xz + x * un_yz),
        2.0 * (y * up_xy + z * up_xz + w * un_yz - 2.0 * x * (gm[1][1] + gm[2][2])),
        2.0 * (x * up_xy + z * up_yz + w * un_xz - 2.0 * y * (gm[0][0] + gm[2][2])),
        2.0 * (x * up_xz + y * up_yz + w * un_xy - 2.0 * z * (gm[0][0] + gm[1][1])),
    ]
    rotor = (w, x, y, z)
    along = sum(rotor[i] * g_rotor[i] for i in range(4))
    for i in range(4):
        put(6 + i, (g_rotor[i] - rotor[i] * along) * part["rnorm"])
    rot, inv, finv, u, v = part["rot"], part["inv"], part["finv"], part["u"], part["v"]
    g_u = focal_length * g_mx - finv * sum(g_screen[0][c] * rot[2][c] for c in range(3))
    g_v = focal_length * g_my - finv * sum(g_screen[1][c] * rot[2][c] for c in range(3))
    g_f = sum(g_screen[r][c] * screen[r][c] for r in range(2) for c in range(3))
    g_in = [g_u * inv, g_v * inv, -(g_f + g_u * u + g_v * v) * inv]
    for axis in range(3):
        put(
            axis,
            g_off[axis] + rot[0][axis] * g_in[0] + rot[1][axis] * g_in[1] + rot[2][axis] * g_in[2],
        )


def split(value):
    high = value.astype(BF16)
    return high, (value - high.astype(F32)).astype(BF16)


def matmul(a, b, dims=((1,), (0,))):
    return lax.dot_general(a, b, (dims, ((), ())), preferred_element_type=F32)


def spread_features(parts, scratch, count):
    tiles = sum(part.shape[1] for part in parts) // LANES
    at = 0
    for part in parts:
        for first in range(0, part.shape[1], LANES):
            for row in range(0, count, 8):
                rows = min(8, count - row)
                scratch[pl.ds(row * tiles + at, rows, stride=tiles), :] = part[
                    row : row + rows, first : first + LANES
                ]
            at += 1
    return tiles


def pack_kernel(shards, pieces, where, *refs):
    sources, refs = refs[: 3 + (pieces > 0)], refs[3 + (pieces > 0) :]
    info, parts, refs = refs[0], refs[1 : 1 + pieces], refs[1 + pieces :]
    shard_of, local_of, goal, place_s, sems, cut_sems = refs
    group = where[0]
    loads = [
        pltpu.make_async_copy(source, held, sems.at[k])
        for k, (source, held) in enumerate(zip(sources, (shard_of, local_of, goal)))
    ]
    for d in range(pieces):
        chunk = parts[d].shape[1]
        first = pl.multiple_of((group ^ d) * chunk, LANES)
        loads.append(
            pltpu.make_async_copy(sources[3].at[:, pl.ds(first, chunk)], parts[d], cut_sems.at[d])
        )
    for load in loads:
        load.start()
    for load in loads[:3]:
        load.wait()
    width = info.shape[1]
    tile_count, listed = local_of.shape
    rows_each = (info.shape[0] - 4) // tile_count
    columns = rows_each * width
    chunk = columns // shards
    info[0:3, :] = goal[...]
    for t in range(tile_count):
        place = (shard_of[t] ^ group) * chunk + (local_of[t : t + 1, :] - group * chunk)
        info[3:4, t * listed : (t + 1) * listed] = place.astype(F32)
        row_i = lax.broadcasted_iota(jnp.int32, (LANES, LANES), 0)
        col_i = lax.broadcasted_iota(jnp.int32, (LANES, LANES), 1)
        for first in range(0, listed, LANES):
            spread = jnp.broadcast_to(place[:, first : first + LANES].astype(F32), (LANES, LANES))
            place_s[first : first + LANES, :] = jnp.broadcast_to(
                jnp.sum(jnp.where(row_i == col_i, spread, 0.0), axis=1, keepdims=True), (LANES, LANES)
            )
        lane_of = lax.broadcasted_iota(jnp.int32, (8, LANES), 1).astype(F32)
        row_of = lax.broadcasted_iota(jnp.int32, (8, LANES), 0).astype(F32)
        for s in range(columns // LANES):
            best = jnp.full((8, LANES), -1.0, F32)
            column = lane_of + float(s * LANES)
            for first in range(0, listed, 8):
                best = jnp.where(
                    place_s[first : first + 8, :] == column, row_of + float(first), best
                )
            best = jnp.max(best, axis=0, keepdims=True)
            row, at = 4 + t * rows_each + s * LANES // width, s * LANES % width
            info[row : row + 1, at : at + LANES] = best
    for load in loads[3:]:
        load.wait()


def pack(group, params, target, hit_shard, hit_local, shards, aligned):
    features, columns = params.shape
    tile_count, listed = hit_local.shape
    width = target.shape[1]
    rows = 4 + tile_count * (columns // width)
    pieces = shards if aligned else 0
    piece = jax.ShapeDtypeStruct((features, columns // shards), F32)
    args = (hit_shard.reshape(tile_count, 1, listed), hit_local, target) + (params,) * aligned
    out = call(
        functools.partial(pack_kernel, shards, pieces),
        "pack",
        (jax.ShapeDtypeStruct((rows, width), F32),) + (piece,) * pieces,
        [smem()] + [pl.BlockSpec(memory_space=pltpu.HBM)] * len(args),
        [
            pltpu.VMEM((tile_count, 1, listed), jnp.int32),
            pltpu.VMEM((tile_count, listed), jnp.int32),
            pltpu.VMEM(target.shape, F32),
            pltpu.VMEM((listed, LANES), F32),
            pltpu.SemaphoreType.DMA((3,)),
            pltpu.SemaphoreType.DMA((shards,)),
        ],
        (group.reshape(1),) + tuple(pltpu.with_memory_space_constraint(a, pltpu.HBM) for a in args),
    )
    return out[0], list(out[1:])


def lane_gather(source, lane):
    return jnp.take_along_axis(source, lane, axis=1, mode="promise_in_bounds")


def spread(row):
    return jnp.broadcast_to(row, (8, LANES))


def composite(tiles, first_group, me, rows, info_s, rendered, work):
    alpha_s, weight_s, left_s, image_s, before_s, behind_s, error_s, joined_s, wrong_s, coef_s, line_s, sum_s, acc_s = work
    groups, tile_count, _, listed = acc_s.shape
    pixels = info_s.shape[2] // tile_count
    tiles_here = groups * tile_count
    segments = LANES // tiles_here
    steps = listed // segments
    halves = listed // LANES
    slabs = rows.shape[0] // ROWS
    side = TILE_SIDE
    middle = 0.5 * side - 0.5
    first_col, first_row = tiles
    lane = lax.broadcasted_iota(jnp.int32, (8, LANES), 1)
    sub = lax.broadcasted_iota(jnp.int32, (8, LANES), 0)
    segment = lane % segments

    pattern = (lane % (LANES // steps)) * steps + sub
    place = jnp.zeros((8, LANES), F32)
    col_0 = row_0 = jnp.zeros((8, LANES), F32)
    for n in range(tiles_here):
        g, t = n // tile_count, n % tile_count
        for h in range(halves):
            first = t * listed + h * LANES
            here = lane_gather(spread(info_s[g, 3:4, first : first + LANES]), pattern)
            place = jnp.where(lane // (LANES // steps) == n * halves + h, here, place)
        slot = (me ^ (first_group + g)) * tile_count + t
        own = lane // segments == n
        col_0 = jnp.where(own, ((first_col + slot % 4) * side).astype(F32) + 0.5 * side, col_0)
        row_0 = jnp.where(own, ((first_row + slot // 4) * side).astype(F32) + 0.5 * side, row_0)
    place = place.astype(jnp.int32)
    at, slab = place & (LANES - 1), place >> 7
    entry = []
    for f in range(9):
        value = lane_gather(spread(rows[f : f + 1, :]), at)
        for s in range(1, slabs):
            here = lane_gather(spread(rows[s * ROWS + f : s * ROWS + f + 1, :]), at)
            value = jnp.where(slab == s, here, value)
        entry.append(value)
    mean_u, mean_v = entry[0] - col_0, entry[1] - row_0
    quad_a, quad_b, quad_c = -0.5 * entry[2], -entry[3], -0.5 * entry[4]
    slope_u = 2.0 * quad_a * mean_u + quad_b * mean_v
    slope_v = 2.0 * quad_c * mean_v + quad_b * mean_u
    level = 0.5 * (slope_u * mean_u + slope_v * mean_v) + entry[5]
    for f, value in enumerate(
        (level, -slope_u, quad_a, -slope_v, quad_b, quad_c, entry[6], entry[7], entry[8])
    ):
        coef_s[f] = value
    for s in range(steps):
        c = [spread(coef_s[f, s : s + 1, :]) for f in range(5)]
        for half in range(side // 8):
            u = sub.astype(F32) + (8.0 * half - middle)
            line_s[0, s, half] = c[0] + u * (c[1] + u * c[2])
            line_s[1, s, half] = c[3] + u * c[4]

    rows_each = 2

    def forward(i, carry):
        for j in range(rows_each):
            row = i * rows_each + j
            v = row.astype(F32) - middle
            left = [None] * (side // 8)
            image = [[None] * 3 for _ in left]
            for s in range(steps):
                quad = spread(coef_s[5, s : s + 1, :]) * v
                colour = [spread(coef_s[6 + k, s : s + 1, :]) for k in range(3)]
                for half in range(side // 8):
                    power = line_s[0, s, half] + v * (line_s[1, s, half] + quad)
                    alpha = jnp.exp(power)
                    at = pl.ds(pl.multiple_of(row * side, side) + (s * pixels + half * 8), 8)
                    alpha_s[at, :] = alpha
                    if s == 0:
                        weight = alpha
                        left[half] = 1.0 - alpha
                        image[half] = [weight * colour[k] for k in range(3)]
                    else:
                        weight = alpha * left[half]
                        left[half] = left[half] - weight
                        image[half] = [
                            image[half][k] + weight * colour[k] for k in range(3)
                        ]
                    weight_s[at, :] = weight
            for half in range(side // 8):
                at = pl.ds(pl.multiple_of(row * side, side) + half * 8, 8)
                left_s[at, :] = left[half]
                for k in range(3):
                    image_s[k, at, :] = image[half][k]
        return carry

    lax.fori_loop(0, side // rows_each, forward, 0)

    tall = 32
    segment_t = lax.broadcasted_iota(jnp.int32, (tall, LANES), 1) % segments
    for first in range(0, pixels, tall):
        at = slice(first, first + tall)
        passed = left_s[at, :]
        step = 1
        while step < segments:
            passed = passed * jnp.where(segment_t >= step, pltpu.roll(passed, step, 1), 1.0)
            step *= 2
        before = jnp.where(segment_t >= 1, pltpu.roll(passed, 1, 1), 1.0)
        before_s[at, :] = before
        for k in range(3):
            joined_s[k, at, :LANES], joined_s[k, at, LANES:] = split(before * image_s[k, at, :])
    pick = lax.broadcasted_iota(jnp.int32, (16, 2 * LANES), 1) % LANES // segments
    pick = jnp.where(
        pick == lax.broadcasted_iota(jnp.int32, (16, 2 * LANES), 0), 1.0, 0.0
    ).astype(BF16)
    wrong_s[...] = jnp.zeros(wrong_s.shape, F32)
    for k in range(3):
        image = matmul(pick, joined_s[k], ((1,), (1,)))
        for n in range(tiles_here):
            g, t = n // tile_count, n % tile_count
            here = slice(t * pixels, (t + 1) * pixels)
            if rendered is not None and g == 0:
                rendered[k : k + 1, here] = image[n : n + 1]
            wrong = image[n : n + 1] - info_s[g, k : k + 1, here]
            high = wrong.astype(BF16).astype(F32)
            wrong_s[k, n : n + 1, :] = high
            wrong_s[k, 8 + n : 9 + n, :] = wrong - high
    back = lax.broadcasted_iota(jnp.int32, (16, LANES), 1) // segments
    back = jnp.where(
        back == lax.broadcasted_iota(jnp.int32, (16, LANES), 0) % 8, 1.0, 0.0
    ).astype(BF16)
    for k in range(3):
        error_s[k] = matmul(wrong_s[k].astype(BF16), back, ((0,), (0,)))

    for first in range(0, pixels, tall):
        at = slice(first, first + tall)
        error = [error_s[k, at, :] for k in range(3)]
        through = left_s[at, :]
        own = sum(error[k] * image_s[k, at, :] for k in range(3))
        step = 1
        while step < segments:
            inside = segment_t < segments - step
            own = own + through * jnp.where(inside, pltpu.roll(own, LANES - step, 1), 0.0)
            if 2 * step < segments:
                through = through * jnp.where(inside, pltpu.roll(through, LANES - step, 1), 1.0)
            step *= 2
        before = before_s[at, :]
        behind = jnp.where(segment_t < segments - 1, pltpu.roll(own, LANES - 1, 1), 0.0)
        behind_s[at, :] = before * behind
        for k in range(3):
            error_s[k, at, :] = before * error[k]

    def backward(i, carry):
        s = steps - 1 - i
        colour = [spread(coef_s[6 + k, pl.ds(s, 1), :]) for k in range(3)]
        plain = [[None] * 3 for _ in range(side // 8)]
        hues = [None] * 3
        for row in range(side):
            v = row - middle
            for half in range(side // 8):
                at = pl.ds(row * side + half * 8, 8)
                of_step = pl.ds(pl.multiple_of(s * pixels, pixels) + (row * side + half * 8), 8)
                weight = weight_s[of_step, :]
                error = [error_s[k, at, :] for k in range(3)]
                pull = error[0] * colour[0] + error[1] * colour[1] + error[2] * colour[2]
                behind = behind_s[at, :]
                gap = pull - behind
                behind_s[at, :] = behind + alpha_s[of_step, :] * gap
                push = weight * gap
                terms = (push, v * push, (v * v) * push)
                hue = [weight * error[k] for k in range(3)]
                if row == 0:
                    plain[half] = list(terms)
                else:
                    plain[half] = [plain[half][m] + terms[m] for m in range(3)]
                hues = [hue[k] if hues[k] is None else hues[k] + hue[k] for k in range(3)]
        u = [sub.astype(F32) + (8.0 * half - middle) for half in range(side // 8)]

        def over(m, power):
            total = 0.0
            for half in range(side // 8):
                value = plain[half][m]
                for _ in range(power):
                    value = value * u[half]
                total = total + value
            return total

        for m, value in enumerate(
            (over(0, 0), over(0, 1), over(1, 0), over(0, 2), over(1, 1), over(2, 0), *hues)
        ):
            sum_s[m, pl.ds(s, 1), :] = jnp.sum(value, axis=0, keepdims=True)
        return carry

    lax.fori_loop(0, steps, backward, 0)

    m_00, m_10, m_01, m_20, m_11, m_02, *grads = [sum_s[m] for m in range(9)]
    n_10 = m_10 - mean_u * m_00
    n_01 = m_01 - mean_v * m_00
    grads = [
        -(2.0 * quad_a * n_10 + quad_b * n_01),
        -(2.0 * quad_c * n_01 + quad_b * n_10),
        -0.5 * (m_20 - mean_u * (m_10 + n_10)),
        -(m_11 - mean_u * m_01 - mean_v * n_10),
        -0.5 * (m_02 - mean_v * (m_01 + n_01)),
        m_00,
    ] + grads
    mine = sub == lane % steps
    for n in range(tiles_here):
        g, t = n // tile_count, n % tile_count
        for h in range(halves):
            at = lane // steps + (n * segments + h * (LANES // steps))
            for f in range(9):
                row = jnp.sum(
                    jnp.where(mine, lane_gather(grads[f], at), 0.0), axis=0, keepdims=True
                )
                if f < 8:
                    acc_s[g, t, f : f + 1, h * LANES : (h + 1) * LANES] = row
                else:
                    acc_s[0, 0, 8 + n * halves + h : 9 + n * halves + h, :LANES] = row


def pool_sum(slab, info_s, acc_s):
    groups, tile_count, _, listed = acc_s.shape
    halves = listed // LANES
    width = info_s.shape[2]
    rows_each = (info_s.shape[1] - 4) // tile_count
    row_of = lax.broadcasted_iota(jnp.int32, (8, LANES), 0)

    totals, every = [], None
    for g in range(groups):
        total = jnp.zeros((8, LANES), F32)
        for t in range(tile_count):
            row, first = 4 + t * rows_each + slab * LANES // width, slab * LANES % width
            at = info_s[g, row : row + 1, first : first + LANES].astype(jnp.int32)
            at = jnp.broadcast_to(at, (8, LANES))
            n = g * tile_count + t
            every = at if every is None else jnp.where(row_of >= n * halves, at, every)
            lane, half = at & (LANES - 1), at >> 7
            for h in range(halves):
                here = lane_gather(acc_s[g, t, 0:8, h * LANES : (h + 1) * LANES], lane)
                total = total + jnp.where(half == h, here, 0.0)
        totals.append(total)
    here = lane_gather(acc_s[0, 0, 8:16, :LANES], every & (LANES - 1))
    ninth = jnp.where(every >> 7 == row_of % halves, here, 0.0)
    return totals[0] + totals[1], jnp.sum(ninth, axis=0, keepdims=True)


def block_start(tile_id):
    within = tile_id % (TILES_X * TILES_Y)
    return (within % TILES_X) // 4 * 4, (within // TILES_X) // 2 * 2


def near_kernel(pieces, tile_ids, cams, where, own, other, *refs):
    parts = refs[:pieces]
    rendered, rows, partial, feats, info_s, *work = refs[pieces:]
    view = tile_ids[0] // (TILES_X * TILES_Y)
    cam = [cams[view, i] for i in range(12)]
    slabs = spread_features(parts, feats, parts[0].shape[0])
    projected = project_rows(lambda f: feats[f * slabs : (f + 1) * slabs, :], cam)
    for f, value in enumerate(projected):
        rows[pl.ds(f, slabs, stride=ROWS), :] = value
    info_s[0] = own[...]
    info_s[1] = other[...]
    composite(block_start(tile_ids[0]), 0, where[0], rows, info_s, rendered, work)
    for s in range(slabs):
        at = slice(s * LANES, (s + 1) * LANES)
        partial[0:8, at], partial[8:9, at] = pool_sum(s, info_s, work[-1])


def far_kernel(blocks, tile_ids, where, rows, partial, infos, *refs):
    *packets, info_s = refs[: len(refs) - 13]
    work = refs[len(refs) - 13 :]
    half = infos.shape[0] // 2
    info_s[0] = infos[:half, :]
    info_s[1] = infos[half:, :]
    composite(block_start(tile_ids[0]), 2, where[0], rows, info_s, None, work)
    share = (tile_ids[0] // (TILES_X * TILES_Y)).astype(F32)
    row_of = lax.broadcasted_iota(jnp.int32, (8, LANES), 0)
    lane_of = lax.broadcasted_iota(jnp.int32, (8, LANES), 1)
    chunk = packets[0].shape[1]
    for s in range(rows.shape[0] // ROWS):
        total, ninth = pool_sum(s, info_s, work[-1])
        total = total + partial[0:8, s * LANES : (s + 1) * LANES]
        ninth = ninth + partial[8:9, s * LANES : (s + 1) * LANES]
        if blocks == 1:
            mine = share
        else:
            column = s * LANES + lane_of
            mine = jnp.where(column % where[2] // (where[2] // blocks) == where[1], share, 0.0)
        at = slice(s * LANES % chunk, s * LANES % chunk + LANES)
        packets[s * LANES // chunk][0:8, at] = total
        packets[s * LANES // chunk][8:16, at] = jnp.where(
            row_of == 0, jnp.broadcast_to(ninth, (8, LANES)), mine
        )


def join_kernel(first, second, out):
    half = first.shape[0]
    out[:half, :] = first[...]
    out[half:, :] = second[...]


def update_kernel(pieces, where, cams, *refs):
    packets = refs[:pieces]
    sources, sinks = refs[pieces : pieces + 3], refs[pieces + 3 : pieces + 6]
    feats, rows, grads, held, made, in_sems, out_sems = refs[pieces + 6 :]
    params, adam_m, adam_v = held.at[0], held.at[1], held.at[2]
    features, width = params.shape
    loads = [pltpu.make_async_copy(sources[k], held.at[k], in_sems.at[k]) for k in range(3)]
    for load in loads:
        load.start()
    chunk = packets[0].shape[1]
    slabs = width // LANES
    for d in range(pieces):
        for h in range(chunk // LANES):
            slab = (where[0] ^ d) * (chunk // LANES) + h
            rows[pl.ds(slab, ROWS, stride=slabs), :] = packets[d][:, h * LANES : (h + 1) * LANES]
    pulled = [rows[f * slabs : (f + 1) * slabs, :] for f in range(10)]
    view = pulled[9]
    cam = []
    for i in range(12):
        value = jnp.full((slabs, LANES), cams[0, i], F32)
        for v in range(1, cams.shape[0]):
            value = jnp.where(view == float(v), cams[v, i], value)
        cam.append(value)

    def put(f, value):
        grads[f * slabs : (f + 1) * slabs, :] = value

    loads[0].wait()
    spread_features([params], feats, features)
    project_pull(lambda f: feats[f * slabs : (f + 1) * slabs, :], cam, pulled[:9], put)
    rate = learn_rate / (1.0 - beta_one**adam_steps)
    unbias = 1.0 / (1.0 - beta_two**adam_steps)
    loads[1].wait()
    loads[2].wait()
    stores = []
    for row in range(0, features, 8):
        count = min(8, features - row)
        for s in range(slabs):
            at = (slice(row, row + count), slice(s * LANES, (s + 1) * LANES))
            grad = grads[pl.ds(row * slabs + s, count, stride=slabs), :]
            moment = beta_one * adam_m[at] + (1.0 - beta_one) * grad
            second = beta_two * adam_v[at] + (1.0 - beta_two) * grad * grad
            made.at[1][at] = moment
            made.at[2][at] = second
            made.at[0][at] = params[at] - rate * moment / (jnp.sqrt(second * unbias) + adam_eps)
        if row % 16 == 8 or row + count == features:
            first = row // 16 * 16
            span = pl.ds(first, row + count - first)
            for k in range(3):
                store = pltpu.make_async_copy(
                    made.at[k, span], sinks[k].at[span], out_sems.at[k, first // 16]
                )
                store.start()
                stores.append(store)
    for store in stores:
        store.wait()


def vmem():
    return pl.BlockSpec(memory_space=pltpu.VMEM)


def smem():
    return pl.BlockSpec(memory_space=pltpu.SMEM)


def any_space():
    return pl.BlockSpec(memory_space=pl.ANY)


def call(kernel, name, out_shape, in_specs, scratch, args, out_specs=None, grant=32):
    return pl.pallas_call(
        kernel,
        out_shape=out_shape,
        in_specs=in_specs,
        out_specs=out_specs or tuple(vmem() for _ in out_shape),
        scratch_shapes=scratch,
        compiler_params=pltpu.CompilerParams(vmem_limit_bytes=grant * 1024 * 1024),
        name=name,
    )(*args)


def work_shapes(tile_count, pixels, listed):
    steps = 2 * tile_count * listed // LANES
    assert steps == 8
    return [
        pltpu.VMEM((steps * pixels, LANES), F32),
        pltpu.VMEM((steps * pixels, LANES), F32),
        pltpu.VMEM((pixels, LANES), F32),
        pltpu.VMEM((3, pixels, LANES), F32),
        pltpu.VMEM((pixels, LANES), F32),
        pltpu.VMEM((pixels, LANES), F32),
        pltpu.VMEM((3, pixels, LANES), F32),
        pltpu.VMEM((3, pixels, 2 * LANES), BF16),
        pltpu.VMEM((3, 16, pixels), F32),
        pltpu.VMEM((9, steps, LANES), F32),
        pltpu.VMEM((2, steps, TILE_SIDE // 8, 8, LANES), F32),
        pltpu.VMEM((9, steps, LANES), F32),
        pltpu.VMEM((2, tile_count, ROWS, listed), F32),
    ]


def near(tile_ids, cameras, where, own, other, parts, tile_count):
    width = sum(part.shape[1] for part in parts)
    features = parts[0].shape[0]
    slabs = width // LANES
    pixels = listed = own.shape[1] // tile_count
    return call(
        functools.partial(near_kernel, len(parts)),
        "near",
        (
            jax.ShapeDtypeStruct((3, own.shape[1]), F32),
            jax.ShapeDtypeStruct((ROWS * slabs, LANES), F32),
            jax.ShapeDtypeStruct((ROWS, width), F32),
        ),
        [smem()] * 3 + [vmem()] * (2 + len(parts)),
        [pltpu.VMEM((features * slabs, LANES), F32), pltpu.VMEM((2,) + own.shape, F32)]
        + work_shapes(tile_count, pixels, listed),
        (tile_ids, cameras, where, own, other, *parts),
    )


def far(tile_ids, where, rows, partial, infos, pieces, tile_count, blocks):
    width = partial.shape[1]
    pixels = listed = infos.shape[1] // tile_count
    info = (infos.shape[0] // 2, infos.shape[1])
    return call(
        functools.partial(far_kernel, blocks),
        "far",
        (jax.ShapeDtypeStruct((ROWS, width // pieces), F32),) * pieces,
        [smem()] * 2 + [vmem()] * 3,
        [pltpu.VMEM((2,) + info, F32)] + work_shapes(tile_count, pixels, listed),
        (tile_ids, where, rows, partial, infos),
    )


def join(first, second):
    shape = (2 * first.shape[0], first.shape[1])
    return call(
        join_kernel, "join", (jax.ShapeDtypeStruct(shape, F32),), [vmem()] * 2, [], (first, second)
    )[0]


def update(where, cameras, params, adam_m, adam_v, packets):
    features, width = params.shape
    slabs = width // LANES
    shape = jax.ShapeDtypeStruct(params.shape, F32)
    return call(
        functools.partial(update_kernel, len(packets)),
        "update",
        (shape, shape, shape),
        [smem()] * 2 + [vmem()] * len(packets) + [any_space()] * 3,
        [
            pltpu.VMEM((features * slabs, LANES), F32),
            pltpu.VMEM((ROWS * slabs, LANES), F32),
            pltpu.VMEM((features * slabs, LANES), F32),
            pltpu.VMEM((3,) + params.shape, F32),
            pltpu.VMEM((3,) + params.shape, F32),
            pltpu.SemaphoreType.DMA((3,)),
            pltpu.SemaphoreType.DMA((3, (features + 15) // 16)),
        ],
        (where, cameras, *packets, params, adam_m, adam_v),
        (any_space(),) * 3,
    )


def swap(value, axis, d):
    if d == 0:
        return value
    return lax.ppermute(value, axis, [(k, k ^ d) for k in range(lax.axis_size(axis))])


def local(params, adam_m, adam_v, cameras, target, tile_ids, hit_shard, hit_local):
    width = params.shape[1]
    tile_count, listed = hit_local.shape
    shards = lax.axis_size("gs")
    along = lax.axis_size("tile")
    chunk = width // shards
    group = lax.axis_index("gs")
    seat = lax.axis_index("tile")
    aligned = chunk % LANES == 0
    team = BLOCK_TILES // tile_count
    assert team == 4
    blocks = along // team

    info, parts = pack(group, params, target, hit_shard, hit_local, shards, aligned)
    if not aligned:
        parts = [
            lax.dynamic_slice_in_dim(params, (group ^ d) * chunk, chunk, axis=1)
            for d in range(shards)
        ]
    parts = [swap(parts[d], "gs", d) for d in range(shards)]
    beside = swap(info, "tile", 1)
    beyond = swap(join(info, beside), "tile", 2)
    if not aligned:
        parts = [jnp.concatenate(parts, axis=1)]
    where = jnp.stack([seat % team, seat // team, jnp.int32(chunk)]).astype(jnp.int32)
    rendered, rows, partial = near(tile_ids, cameras, where, info, beside, parts, tile_count)
    packets = far(tile_ids, where, rows, partial, beyond, len(parts), tile_count, blocks)
    if not aligned:
        packets = [packets[0][:, d * chunk : (d + 1) * chunk] for d in range(shards)]
    packets = [swap(packets[d], "gs", d) for d in range(shards)]
    if blocks > 1:
        packets = [block_sum(packet, along, team) for packet in packets]
    if aligned:
        own = group
    else:
        packets = [jnp.stack(packets)[jnp.arange(shards) ^ group].transpose(1, 0, 2).reshape(ROWS, -1)]
        own = jnp.int32(0)
    new_params, new_m, new_v = update(
        own.reshape(1), cameras, params, adam_m, adam_v, packets
    )
    return (rendered, new_params, new_m, new_v)


def block_sum(packet, along, team):
    step = team
    while step < along:
        packet = packet + swap(packet, "tile", step)
        step *= 2
    return packet


def solution(mesh):
    return jax.shard_map(
        local,
        mesh=mesh,
        in_specs=(
            P(None, ("groups", "gs")),
            P(None, ("groups", "gs")),
            P(None, ("groups", "gs")),
            P("groups", None),
            P(None, ("groups", "gs", "tile")),
            P(("groups", "gs", "tile")),
            P(("groups", "gs", "tile"), None, None),
            P(("groups", "gs", "tile"), None),
        ),
        out_specs=(
            P(None, ("groups", "gs", "tile")),
            P(None, ("groups", "gs")),
            P(None, ("groups", "gs")),
            P(None, ("groups", "gs")),
        ),
        check_vma=False,
    )
```

```python
import functools

import jax
import jax.numpy as jnp
from jax import lax
from jax.experimental import pallas as pl
from jax.experimental.pallas import tpu as pltpu
from jax.sharding import PartitionSpec as P

TILES_X = 120
TILES_Y = 68
TILE_SIDE = 16
BLOCK_TILES = 8
LANES = 128
ROWS = 16
F32 = jnp.float32
BF16 = jnp.bfloat16

focal_length = 1000.0
center_x = 960.0
center_y = 540.0
dilation = 0.3
beta_one = 0.9
beta_two = 0.999
learn_rate = 0.01
adam_eps = 1e-08
adam_steps = 100.0
sh_const = (
    0.28209479177387814,
    0.4886025119029199,
    1.0925484305920792,
    0.31539156525252005,
    0.5462742152960396,
    0.5900435899266435,
    2.890611442640554,
    0.4570457994644658,
    0.3731763325901154,
    1.445305721320277,
)


def sh_basis(x, y, z):
    s = sh_const
    xx, yy, zz = x * x, y * y, z * z
    return [
        None,
        -s[1] * y,
        s[1] * z,
        -s[1] * x,
        s[2] * (x * y),
        -s[2] * (y * z),
        s[3] * (2.0 * zz - xx - yy),
        -s[2] * (x * z),
        s[4] * (xx - yy),
        -s[5] * y * (3.0 * xx - yy),
        s[6] * (x * y) * z,
        -s[7] * y * (4.0 * zz - xx - yy),
        s[8] * z * (2.0 * zz - 3.0 * xx - 3.0 * yy),
        -s[7] * x * (4.0 * zz - xx - yy),
        s[9] * z * (xx - yy),
        -s[5] * x * (xx - 3.0 * yy),
    ]


def sh_pull(h, x, y, z):
    s = sh_const
    xx, yy, zz = x * x, y * y, z * z
    xy, xz, yz = x * y, x * z, y * z
    diff = xx - yy
    ring = 4.0 * zz - xx - yy
    g_x = (
        -s[1] * h[3]
        + s[2] * (h[4] * y - h[7] * z)
        - (2.0 * s[3]) * h[6] * x
        + (2.0 * s[4]) * h[8] * x
        - (6.0 * s[5]) * h[9] * xy
        + s[6] * h[10] * yz
        + (2.0 * s[7]) * h[11] * xy
        - (6.0 * s[8]) * h[12] * xz
        - s[7] * h[13] * (ring - 2.0 * xx)
        + (2.0 * s[9]) * h[14] * xz
        - (3.0 * s[5]) * h[15] * diff
    )
    g_y = (
        -s[1] * h[1]
        + s[2] * (h[4] * x - h[5] * z)
        - (2.0 * s[3]) * h[6] * y
        - (2.0 * s[4]) * h[8] * y
        - (3.0 * s[5]) * h[9] * diff
        + s[6] * h[10] * xz
        - s[7] * h[11] * (ring - 2.0 * yy)
        - (6.0 * s[8]) * h[12] * yz
        + (2.0 * s[7]) * h[13] * xy
        - (2.0 * s[9]) * h[14] * yz
        + (6.0 * s[5]) * h[15] * xy
    )
    g_z = (
        s[1] * h[2]
        - s[2] * (h[5] * y + h[7] * x)
        + (4.0 * s[3]) * h[6] * z
        + s[6] * h[10] * xy
        - (8.0 * s[7]) * (h[11] * yz + h[13] * xz)
        + s[8] * h[12] * (6.0 * zz - 3.0 * xx - 3.0 * yy)
        + s[9] * h[14] * diff
    )
    return g_x, g_y, g_z


def project_parts(feat, cam):
    rot = [[cam[3 * r + c] for c in range(3)] for r in range(3)]
    off = [feat(a) - cam[9 + a] for a in range(3)]
    in_cam = [rot[r][0] * off[0] + rot[r][1] * off[1] + rot[r][2] * off[2] for r in range(3)]
    inv = 1.0 / in_cam[2]
    u = in_cam[0] * inv
    v = in_cam[1] * inv
    finv = focal_length * inv
    scale = [jnp.exp(2.0 * feat(3 + a)) for a in range(3)]
    quat = [feat(6 + a) for a in range(4)]
    rnorm = lax.rsqrt(quat[0] * quat[0] + quat[1] * quat[1] + quat[2] * quat[2] + quat[3] * quat[3])
    w, x, y, z = [q * rnorm for q in quat]
    turn = [
        [1.0 - 2.0 * (y * y + z * z), 2.0 * (x * y - w * z), 2.0 * (x * z + w * y)],
        [2.0 * (x * y + w * z), 1.0 - 2.0 * (x * x + z * z), 2.0 * (y * z - w * x)],
        [2.0 * (x * z - w * y), 2.0 * (y * z + w * x), 1.0 - 2.0 * (x * x + y * y)],
    ]
    screen = [
        [finv * (rot[0][c] - u * rot[2][c]) for c in range(3)],
        [finv * (rot[1][c] - v * rot[2][c]) for c in range(3)],
    ]
    axes = [
        [sum(screen[r][c] * turn[c][k] for c in range(3)) for k in range(3)] for r in range(2)
    ]
    wide = [[axes[r][k] * scale[k] for k in range(3)] for r in range(2)]
    cov_xx = sum(wide[0][k] * axes[0][k] for k in range(3)) + dilation
    cov_xy = sum(wide[0][k] * axes[1][k] for k in range(3))
    cov_yy = sum(wide[1][k] * axes[1][k] for k in range(3)) + dilation
    rdet = 1.0 / (cov_xx * cov_yy - cov_xy * cov_xy)
    conic = (cov_yy * rdet, -cov_xy * rdet, cov_xx * rdet)
    rlen = lax.rsqrt(off[0] * off[0] + off[1] * off[1] + off[2] * off[2])
    way = [off[a] * rlen for a in range(3)]
    return dict(
        rot=rot, inv=inv, u=u, v=v, finv=finv, scale=scale, rnorm=rnorm, rotor=(w, x, y, z), turn=turn,
        screen=screen, axes=axes, wide=wide, conic=conic, rlen=rlen, way=way,
    )


def project_rows(feat, cam):
    part = project_parts(feat, cam)
    basis = sh_basis(*part["way"])
    colours = []
    for k in range(3):
        total = 0.5 + sh_const[0] * feat(11 + 16 * k)
        for b in range(1, 16):
            total = total + feat(11 + 16 * k + b) * basis[b]
        colours.append(total)
    mean_x = focal_length * part["u"] + center_x
    mean_y = focal_length * part["v"] + center_y
    logit = feat(10)
    log_opacity = jnp.minimum(logit, 0.0) - jnp.log(1.0 + jnp.exp(-jnp.abs(logit)))
    return [mean_x, mean_y, *part["conic"], log_opacity, *colours]


def project_pull(feat, cam, grads, put):
    part = project_parts(feat, cam)
    g_mx, g_my, g_a, g_b, g_c, g_o = grads[:6]
    g_col = grads[6:9]
    way, rlen = part["way"], part["rlen"]
    basis = sh_basis(*way)
    pulled = [None]
    for k in range(3):
        put(11 + 16 * k, sh_const[0] * g_col[k])
    for b in range(1, 16):
        total = 0.0
        for k in range(3):
            put(11 + 16 * k + b, g_col[k] * basis[b])
            total = total + g_col[k] * feat(11 + 16 * k + b)
        pulled.append(total)
    g_way = sh_pull(pulled, *way)
    along = way[0] * g_way[0] + way[1] * g_way[1] + way[2] * g_way[2]
    g_off = [(g_way[a] - way[a] * along) * rlen for a in range(3)]
    put(10, g_o / (1.0 + jnp.exp(feat(10))))
    a, b, c = part["conic"]
    g_xx = -(a * a * g_a + a * b * g_b + b * b * g_c)
    g_xy = -(2.0 * a * b * g_a + (a * c + b * b) * g_b + 2.0 * b * c * g_c)
    g_yy = -(b * b * g_a + b * c * g_b + c * c * g_c)
    axes, wide, turn, screen = part["axes"], part["wide"], part["turn"], part["screen"]
    for k in range(3):
        g_scale = (
            g_xx * axes[0][k] * wide[0][k]
            + g_xy * axes[0][k] * wide[1][k]
            + g_yy * axes[1][k] * wide[1][k]
        )
        put(3 + k, 2.0 * g_scale)
    g_axes = [
        [2.0 * g_xx * wide[0][k] + g_xy * wide[1][k] for k in range(3)],
        [2.0 * g_yy * wide[1][k] + g_xy * wide[0][k] for k in range(3)],
    ]
    g_screen = [
        [sum(g_axes[r][k] * turn[c][k] for k in range(3)) for c in range(3)] for r in range(2)
    ]
    gm = [
        [g_axes[0][k] * screen[0][c] + g_axes[1][k] * screen[1][c] for k in range(3)]
        for c in range(3)
    ]
    w, x, y, z = part["rotor"]
    up_xy, up_xz, up_yz = gm[0][1] + gm[1][0], gm[0][2] + gm[2][0], gm[1][2] + gm[2][1]
    un_xy, un_xz, un_yz = gm[1][0] - gm[0][1], gm[0][2] - gm[2][0], gm[2][1] - gm[1][2]
    g_rotor = [
        2.0 * (z * un_xy + y * un_xz + x * un_yz),
        2.0 * (y * up_xy + z * up_xz + w * un_yz - 2.0 * x * (gm[1][1] + gm[2][2])),
        2.0 * (x * up_xy + z * up_yz + w * un_xz - 2.0 * y * (gm[0][0] + gm[2][2])),
        2.0 * (x * up_xz + y * up_yz + w * un_xy - 2.0 * z * (gm[0][0] + gm[1][1])),
    ]
    rotor = (w, x, y, z)
    along = sum(rotor[i] * g_rotor[i] for i in range(4))
    for i in range(4):
        put(6 + i, (g_rotor[i] - rotor[i] * along) * part["rnorm"])
    rot, inv, finv, u, v = part["rot"], part["inv"], part["finv"], part["u"], part["v"]
    g_u = focal_length * g_mx - finv * sum(g_screen[0][c] * rot[2][c] for c in range(3))
    g_v = focal_length * g_my - finv * sum(g_screen[1][c] * rot[2][c] for c in range(3))
    g_f = sum(g_screen[r][c] * screen[r][c] for r in range(2) for c in range(3))
    g_in = [g_u * inv, g_v * inv, -(g_f + g_u * u + g_v * v) * inv]
    for axis in range(3):
        put(
            axis,
            g_off[axis] + rot[0][axis] * g_in[0] + rot[1][axis] * g_in[1] + rot[2][axis] * g_in[2],
        )


def split(value):
    high = value.astype(BF16)
    return high, (value - high.astype(F32)).astype(BF16)


def matmul(a, b, dims=((1,), (0,))):
    return lax.dot_general(a, b, (dims, ((), ())), preferred_element_type=F32)


def spread_features(parts, scratch, count):
    tiles = sum(part.shape[1] for part in parts) // LANES
    at = 0
    for part in parts:
        for first in range(0, part.shape[1], LANES):
            for row in range(0, count, 8):
                rows = min(8, count - row)
                scratch[pl.ds(row * tiles + at, rows, stride=tiles), :] = part[
                    row : row + rows, first : first + LANES
                ]
            at += 1
    return tiles


def pack_kernel(shards, pieces, where, *refs):
    sources, refs = refs[: 3 + (pieces > 0)], refs[3 + (pieces > 0) :]
    info, parts, refs = refs[0], refs[1 : 1 + pieces], refs[1 + pieces :]
    shard_of, local_of, goal, place_s, sems, cut_sems = refs
    group = where[0]
    loads = [
        pltpu.make_async_copy(source, held, sems.at[k])
        for k, (source, held) in enumerate(zip(sources, (shard_of, local_of, goal)))
    ]
    for d in range(pieces):
        chunk = parts[d].shape[1]
        first = pl.multiple_of((group ^ d) * chunk, LANES)
        loads.append(
            pltpu.make_async_copy(sources[3].at[:, pl.ds(first, chunk)], parts[d], cut_sems.at[d])
        )
    for load in loads:
        load.start()
    for load in loads[:3]:
        load.wait()
    width = info.shape[1]
    tile_count, listed = local_of.shape
    rows_each = (info.shape[0] - 4) // tile_count
    columns = rows_each * width
    chunk = columns // shards
    info[0:3, :] = goal[...]
    for t in range(tile_count):
        place = (shard_of[t] ^ group) * chunk + (local_of[t : t + 1, :] - group * chunk)
        info[3:4, t * listed : (t + 1) * listed] = place.astype(F32)
        row_i = lax.broadcasted_iota(jnp.int32, (LANES, LANES), 0)
        col_i = lax.broadcasted_iota(jnp.int32, (LANES, LANES), 1)
        for first in range(0, listed, LANES):
            spread = jnp.broadcast_to(place[:, first : first + LANES].astype(F32), (LANES, LANES))
            place_s[first : first + LANES, :] = jnp.broadcast_to(
                jnp.sum(jnp.where(row_i == col_i, spread, 0.0), axis=1, keepdims=True), (LANES, LANES)
            )
        lane_of = lax.broadcasted_iota(jnp.int32, (8, LANES), 1).astype(F32)
        row_of = lax.broadcasted_iota(jnp.int32, (8, LANES), 0).astype(F32)
        for s in range(columns // LANES):
            best = jnp.full((8, LANES), -1.0, F32)
            column = lane_of + float(s * LANES)
            for first in range(0, listed, 8):
                best = jnp.where(
                    place_s[first : first + 8, :] == column, row_of + float(first), best
                )
            best = jnp.max(best, axis=0, keepdims=True)
            row, at = 4 + t * rows_each + s * LANES // width, s * LANES % width
            info[row : row + 1, at : at + LANES] = best
    for load in loads[3:]:
        load.wait()


def pack(group, params, target, hit_shard, hit_local, shards, aligned):
    features, columns = params.shape
    tile_count, listed = hit_local.shape
    width = target.shape[1]
    rows = 4 + tile_count * (columns // width)
    pieces = shards if aligned else 0
    piece = jax.ShapeDtypeStruct((features, columns // shards), F32)
    args = (hit_shard.reshape(tile_count, 1, listed), hit_local, target) + (params,) * aligned
    out = call(
        functools.partial(pack_kernel, shards, pieces),
        "pack",
        (jax.ShapeDtypeStruct((rows, width), F32),) + (piece,) * pieces,
        [smem()] + [pl.BlockSpec(memory_space=pltpu.HBM)] * len(args),
        [
            pltpu.VMEM((tile_count, 1, listed), jnp.int32),
            pltpu.VMEM((tile_count, listed), jnp.int32),
            pltpu.VMEM(target.shape, F32),
            pltpu.VMEM((listed, LANES), F32),
            pltpu.SemaphoreType.DMA((3,)),
            pltpu.SemaphoreType.DMA((shards,)),
        ],
        (group.reshape(1),) + tuple(pltpu.with_memory_space_constraint(a, pltpu.HBM) for a in args),
    )
    return out[0], list(out[1:])


def pixel_basis(pixels):
    pixel = lax.broadcasted_iota(jnp.int32, (8, pixels), 1)
    row = lax.broadcasted_iota(jnp.int32, (8, pixels), 0)
    middle = 0.5 * TILE_SIDE - 0.5
    u = (pixel % TILE_SIDE).astype(F32) - middle
    v = (pixel // TILE_SIDE).astype(F32) - middle
    value = jnp.where(row == 0, 1.0, 0.0)
    for at, term in ((1, u), (2, v), (3, u * u), (4, u * v), (5, v * v)):
        value = jnp.where(row == at, term, value)
    return value


def lane_gather(source, lane):
    return jnp.take_along_axis(source, lane, axis=1, mode="promise_in_bounds")


def spread(row):
    return jnp.broadcast_to(row, (8, LANES))


def composite(tiles, first_group, me, rows, info_s, rendered, work):
    (
        alpha_s, weight_s, pull_s, left_s, image_s, before_s, behind_s, error_s,
        joined_s, wrong_s, colour_s, term_s, hue_s, sum_s, acc_s,
    ) = work
    groups, tile_count, _, listed = acc_s.shape
    pixels = info_s.shape[2] // tile_count
    tiles_here = groups * tile_count
    segments = LANES // tiles_here
    steps = listed // segments
    halves = listed // LANES
    slabs = rows.shape[0] // ROWS
    side = TILE_SIDE
    middle = 0.5 * side - 0.5
    first_col, first_row = tiles
    lane = lax.broadcasted_iota(jnp.int32, (8, LANES), 1)
    sub = lax.broadcasted_iota(jnp.int32, (8, LANES), 0)
    segment = lane % segments

    pattern = (lane % (LANES // steps)) * steps + sub
    place = jnp.zeros((8, LANES), F32)
    col_0 = row_0 = jnp.zeros((8, LANES), F32)
    for n in range(tiles_here):
        g, t = n // tile_count, n % tile_count
        for h in range(halves):
            first = t * listed + h * LANES
            here = lane_gather(spread(info_s[g, 3:4, first : first + LANES]), pattern)
            place = jnp.where(lane // (LANES // steps) == n * halves + h, here, place)
        slot = (me ^ (first_group + g)) * tile_count + t
        own = lane // segments == n
        col_0 = jnp.where(own, ((first_col + slot % 4) * side).astype(F32) + 0.5 * side, col_0)
        row_0 = jnp.where(own, ((first_row + slot // 4) * side).astype(F32) + 0.5 * side, row_0)
    place = place.astype(jnp.int32)
    at, slab = place & (LANES - 1), place >> 7
    entry = []
    for f in range(9):
        value = lane_gather(spread(rows[f : f + 1, :]), at)
        for s in range(1, slabs):
            here = lane_gather(spread(rows[s * ROWS + f : s * ROWS + f + 1, :]), at)
            value = jnp.where(slab == s, here, value)
        entry.append(value)
    mean_u, mean_v = entry[0] - col_0, entry[1] - row_0
    quad_a, quad_b, quad_c = -0.5 * entry[2], -entry[3], -0.5 * entry[4]
    slope_u = 2.0 * quad_a * mean_u + quad_b * mean_v
    slope_v = 2.0 * quad_c * mean_v + quad_b * mean_u
    level = 0.5 * (slope_u * mean_u + slope_v * mean_v) + entry[5]
    zero = jnp.zeros((8, LANES), F32)
    for f, value in enumerate((level, -slope_u, -slope_v, quad_a, quad_b, quad_c, zero, zero)):
        for term in range(3):
            high = value.astype(BF16).astype(F32)
            term_s[pl.ds(8 * term + f, steps, stride=24), :] = high
            value = value - high
    down = ((0,), (0,))

    def by_step(ref, count):
        return jnp.concatenate(
            [ref[s * count : (s + 1) * count, :] for s in range(steps)], axis=1
        ).astype(BF16)

    basis = pixel_basis(pixels)
    basis = jnp.concatenate([basis, basis, basis], axis=0).astype(BF16)
    alpha_s[...] = jnp.exp(matmul(basis, by_step(term_s, 24), down))
    hue_s[...] = jnp.zeros(hue_s.shape, F32)
    for k in range(3):
        colour_s[k] = entry[6 + k]
        high = entry[6 + k].astype(BF16).astype(F32)
        low = entry[6 + k] - high
        for n in range(tiles_here):
            own = lane // segments == n
            for at, value in ((0, high), (3, low), (6, high)):
                hue_s[pl.ds(n * 16 + at + k, steps, stride=16 * tiles_here), :] = jnp.where(
                    own, value, 0.0
                )

    rows_each = 2

    def forward(i, carry):
        for j in range(rows_each):
            row = i * rows_each + j
            left = [None] * (side // 8)
            image = [[None] * 3 for _ in left]
            for s in range(steps):
                colour = [spread(colour_s[k, s : s + 1, :]) for k in range(3)]
                of_step = slice(s * LANES, (s + 1) * LANES)
                for half in range(side // 8):
                    at = pl.ds(pl.multiple_of(row * side, side) + half * 8, 8)
                    alpha = alpha_s[at, of_step]
                    if s == 0:
                        weight = alpha
                        left[half] = 1.0 - alpha
                        image[half] = [weight * colour[k] for k in range(3)]
                    else:
                        weight = alpha * left[half]
                        left[half] = left[half] - weight
                        image[half] = [
                            image[half][k] + weight * colour[k] for k in range(3)
                        ]
                    weight_s[at, of_step] = weight
            for half in range(side // 8):
                at = pl.ds(pl.multiple_of(row * side, side) + half * 8, 8)
                left_s[at, :] = left[half]
                for k in range(3):
                    image_s[k, at, :] = image[half][k]
        return carry

    lax.fori_loop(0, side // rows_each, forward, 0)

    tall = 32
    segment_t = lax.broadcasted_iota(jnp.int32, (tall, LANES), 1) % segments
    for first in range(0, pixels, tall):
        at = slice(first, first + tall)
        passed = left_s[at, :]
        step = 1
        while step < segments:
            passed = passed * jnp.where(segment_t >= step, pltpu.roll(passed, step, 1), 1.0)
            step *= 2
        before = jnp.where(segment_t >= 1, pltpu.roll(passed, 1, 1), 1.0)
        before_s[at, :] = before
        for k in range(3):
            joined_s[k, at, :LANES], joined_s[k, at, LANES:] = split(before * image_s[k, at, :])
    pick = lax.broadcasted_iota(jnp.int32, (16, 2 * LANES), 1) % LANES // segments
    pick = jnp.where(
        pick == lax.broadcasted_iota(jnp.int32, (16, 2 * LANES), 0), 1.0, 0.0
    ).astype(BF16)
    wrong_s[...] = jnp.zeros(wrong_s.shape, F32)
    for k in range(3):
        image = matmul(pick, joined_s[k], ((1,), (1,)))
        for n in range(tiles_here):
            g, t = n // tile_count, n % tile_count
            here = slice(t * pixels, (t + 1) * pixels)
            if rendered is not None and g == 0:
                rendered[k : k + 1, here] = image[n : n + 1]
            wrong = image[n : n + 1] - info_s[g, k : k + 1, here]
            high = wrong.astype(BF16).astype(F32)
            wrong_s[n * 16 + k : n * 16 + k + 1, :] = high
            wrong_s[n * 16 + 3 + k : n * 16 + 4 + k, :] = high
            wrong_s[n * 16 + 6 + k : n * 16 + 7 + k, :] = wrong - high
    wrong = wrong_s[...].astype(BF16)
    pull_s[...] = matmul(wrong, by_step(hue_s, 16 * tiles_here), down)
    row_of = lax.broadcasted_iota(jnp.int32, (16 * tiles_here, LANES), 0)
    own = lax.broadcasted_iota(jnp.int32, (16 * tiles_here, LANES), 1) // segments == row_of // 16
    for k in range(3):
        pick = own & ((row_of % 16 == k) | (row_of % 16 == 6 + k))
        error_s[k] = matmul(wrong, jnp.where(pick, 1.0, 0.0).astype(BF16), down)

    for first in range(0, pixels, tall):
        at = slice(first, first + tall)
        error = [error_s[k, at, :] for k in range(3)]
        through = left_s[at, :]
        own = sum(error[k] * image_s[k, at, :] for k in range(3))
        step = 1
        while step < segments:
            inside = segment_t < segments - step
            own = own + through * jnp.where(inside, pltpu.roll(own, LANES - step, 1), 0.0)
            if 2 * step < segments:
                through = through * jnp.where(inside, pltpu.roll(through, LANES - step, 1), 1.0)
            step *= 2
        before = before_s[at, :]
        behind = jnp.where(segment_t < segments - 1, pltpu.roll(own, LANES - 1, 1), 0.0)
        behind_s[at, :] = before * behind
        for k in range(3):
            error_s[k, at, :] = before * error[k]

    def backward(i, carry):
        s = steps - 1 - i
        of_step = pl.ds(pl.multiple_of(s * LANES, LANES), LANES)
        plain = [[None] * 3 for _ in range(side // 8)]
        hues = [None] * 3
        for row in range(side):
            for half in range(side // 8):
                at = pl.ds(row * side + half * 8, 8)
                weight = weight_s[at, of_step]
                behind = behind_s[at, :]
                gap = before_s[at, :] * pull_s[at, of_step] - behind
                behind_s[at, :] = behind + alpha_s[at, of_step] * gap
                push = weight * gap
                if row == 0:
                    plain[half] = [push, push, push]
                else:
                    plain[half][0] = plain[half][0] + push
                    plain[half][1] = plain[half][1] + plain[half][0]
                    plain[half][2] = plain[half][2] + plain[half][1]
                hue = [weight * error_s[k, at, :] for k in range(3)]
                hues = [hue[k] if hues[k] is None else hues[k] + hue[k] for k in range(3)]
        u = [sub.astype(F32) + (8.0 * half - middle) for half in range(side // 8)]
        shift = side - middle
        for half in range(side // 8):
            one, two, three = plain[half]
            plain[half][1] = shift * one - two
            plain[half][2] = shift * shift * one - (2.0 * shift + 1.0) * two + 2.0 * three

        def over(m, power):
            total = 0.0
            for half in range(side // 8):
                value = plain[half][m]
                for _ in range(power):
                    value = value * u[half]
                total = total + value
            return total

        for m, value in enumerate(
            (over(0, 0), over(0, 1), over(1, 0), over(0, 2), over(1, 1), over(2, 0), *hues)
        ):
            sum_s[m, pl.ds(s, 1), :] = jnp.sum(value, axis=0, keepdims=True)
        return carry

    lax.fori_loop(0, steps, backward, 0)

    m_00, m_10, m_01, m_20, m_11, m_02, *grads = [sum_s[m] for m in range(9)]
    n_10 = m_10 - mean_u * m_00
    n_01 = m_01 - mean_v * m_00
    grads = [
        -(2.0 * quad_a * n_10 + quad_b * n_01),
        -(2.0 * quad_c * n_01 + quad_b * n_10),
        -0.5 * (m_20 - mean_u * (m_10 + n_10)),
        -(m_11 - mean_u * m_01 - mean_v * n_10),
        -0.5 * (m_02 - mean_v * (m_01 + n_01)),
        m_00,
    ] + grads
    mine = sub == lane % steps
    for n in range(tiles_here):
        g, t = n // tile_count, n % tile_count
        for h in range(halves):
            at = lane // steps + (n * segments + h * (LANES // steps))
            for f in range(9):
                row = jnp.sum(
                    jnp.where(mine, lane_gather(grads[f], at), 0.0), axis=0, keepdims=True
                )
                if f < 8:
                    acc_s[g, t, f : f + 1, h * LANES : (h + 1) * LANES] = row
                else:
                    acc_s[0, 0, 8 + n * halves + h : 9 + n * halves + h, :LANES] = row


def pool_sum(slab, info_s, acc_s):
    groups, tile_count, _, listed = acc_s.shape
    halves = listed // LANES
    width = info_s.shape[2]
    rows_each = (info_s.shape[1] - 4) // tile_count
    row_of = lax.broadcasted_iota(jnp.int32, (8, LANES), 0)

    totals, every = [], None
    for g in range(groups):
        total = jnp.zeros((8, LANES), F32)
        for t in range(tile_count):
            row, first = 4 + t * rows_each + slab * LANES // width, slab * LANES % width
            at = info_s[g, row : row + 1, first : first + LANES].astype(jnp.int32)
            at = jnp.broadcast_to(at, (8, LANES))
            n = g * tile_count + t
            every = at if every is None else jnp.where(row_of >= n * halves, at, every)
            lane, half = at & (LANES - 1), at >> 7
            for h in range(halves):
                here = lane_gather(acc_s[g, t, 0:8, h * LANES : (h + 1) * LANES], lane)
                total = total + jnp.where(half == h, here, 0.0)
        totals.append(total)
    here = lane_gather(acc_s[0, 0, 8:16, :LANES], every & (LANES - 1))
    ninth = jnp.where(every >> 7 == row_of % halves, here, 0.0)
    return totals[0] + totals[1], jnp.sum(ninth, axis=0, keepdims=True)


def block_start(tile_id):
    within = tile_id % (TILES_X * TILES_Y)
    return (within % TILES_X) // 4 * 4, (within // TILES_X) // 2 * 2


def near_kernel(pieces, tile_ids, cams, where, own, other, *refs):
    parts = refs[:pieces]
    rendered, rows, partial, feats, info_s, *work = refs[pieces:]
    view = tile_ids[0] // (TILES_X * TILES_Y)
    cam = [cams[view, i] for i in range(12)]
    slabs = spread_features(parts, feats, parts[0].shape[0])
    projected = project_rows(lambda f: feats[f * slabs : (f + 1) * slabs, :], cam)
    for f, value in enumerate(projected):
        rows[pl.ds(f, slabs, stride=ROWS), :] = value
    info_s[0] = own[...]
    info_s[1] = other[...]
    composite(block_start(tile_ids[0]), 0, where[0], rows, info_s, rendered, work)
    for s in range(slabs):
        at = slice(s * LANES, (s + 1) * LANES)
        partial[0:8, at], partial[8:9, at] = pool_sum(s, info_s, work[-1])


def far_kernel(blocks, tile_ids, where, rows, partial, infos, *refs):
    *packets, info_s = refs[: len(refs) - 15]
    work = refs[len(refs) - 15 :]
    half = infos.shape[0] // 2
    info_s[0] = infos[:half, :]
    info_s[1] = infos[half:, :]
    composite(block_start(tile_ids[0]), 2, where[0], rows, info_s, None, work)
    share = (tile_ids[0] // (TILES_X * TILES_Y)).astype(F32)
    row_of = lax.broadcasted_iota(jnp.int32, (8, LANES), 0)
    lane_of = lax.broadcasted_iota(jnp.int32, (8, LANES), 1)
    chunk = packets[0].shape[1]
    for s in range(rows.shape[0] // ROWS):
        total, ninth = pool_sum(s, info_s, work[-1])
        total = total + partial[0:8, s * LANES : (s + 1) * LANES]
        ninth = ninth + partial[8:9, s * LANES : (s + 1) * LANES]
        if blocks == 1:
            mine = share
        else:
            column = s * LANES + lane_of
            mine = jnp.where(column % where[2] // (where[2] // blocks) == where[1], share, 0.0)
        at = slice(s * LANES % chunk, s * LANES % chunk + LANES)
        packets[s * LANES // chunk][0:8, at] = total
        packets[s * LANES // chunk][8:16, at] = jnp.where(
            row_of == 0, jnp.broadcast_to(ninth, (8, LANES)), mine
        )


def join_kernel(first, second, out):
    half = first.shape[0]
    out[:half, :] = first[...]
    out[half:, :] = second[...]


def update_kernel(pieces, where, cams, *refs):
    packets = refs[:pieces]
    sources, sinks = refs[pieces : pieces + 3], refs[pieces + 3 : pieces + 6]
    feats, rows, grads, held, made, in_sems, out_sems = refs[pieces + 6 :]
    params, adam_m, adam_v = held.at[0], held.at[1], held.at[2]
    features, width = params.shape
    loads = [pltpu.make_async_copy(sources[k], held.at[k], in_sems.at[k]) for k in range(3)]
    for load in loads:
        load.start()
    chunk = packets[0].shape[1]
    slabs = width // LANES
    for d in range(pieces):
        for h in range(chunk // LANES):
            slab = (where[0] ^ d) * (chunk // LANES) + h
            rows[pl.ds(slab, ROWS, stride=slabs), :] = packets[d][:, h * LANES : (h + 1) * LANES]
    pulled = [rows[f * slabs : (f + 1) * slabs, :] for f in range(10)]
    view = pulled[9]
    cam = []
    for i in range(12):
        value = jnp.full((slabs, LANES), cams[0, i], F32)
        for v in range(1, cams.shape[0]):
            value = jnp.where(view == float(v), cams[v, i], value)
        cam.append(value)

    def put(f, value):
        grads[f * slabs : (f + 1) * slabs, :] = value

    loads[0].wait()
    spread_features([params], feats, features)
    project_pull(lambda f: feats[f * slabs : (f + 1) * slabs, :], cam, pulled[:9], put)
    rate = learn_rate / (1.0 - beta_one**adam_steps)
    unbias = 1.0 / (1.0 - beta_two**adam_steps)
    loads[1].wait()
    loads[2].wait()
    stores = []
    for row in range(0, features, 8):
        count = min(8, features - row)
        for s in range(slabs):
            at = (slice(row, row + count), slice(s * LANES, (s + 1) * LANES))
            grad = grads[pl.ds(row * slabs + s, count, stride=slabs), :]
            moment = beta_one * adam_m[at] + (1.0 - beta_one) * grad
            second = beta_two * adam_v[at] + (1.0 - beta_two) * grad * grad
            made.at[1][at] = moment
            made.at[2][at] = second
            made.at[0][at] = params[at] - rate * moment / (jnp.sqrt(second * unbias) + adam_eps)
        if row % 16 == 8 or row + count == features:
            first = row // 16 * 16
            span = pl.ds(first, row + count - first)
            for k in range(3):
                store = pltpu.make_async_copy(
                    made.at[k, span], sinks[k].at[span], out_sems.at[k, first // 16]
                )
                store.start()
                stores.append(store)
    for store in stores:
        store.wait()


def vmem():
    return pl.BlockSpec(memory_space=pltpu.VMEM)


def smem():
    return pl.BlockSpec(memory_space=pltpu.SMEM)


def any_space():
    return pl.BlockSpec(memory_space=pl.ANY)


def call(kernel, name, out_shape, in_specs, scratch, args, out_specs=None, grant=32):
    return pl.pallas_call(
        kernel,
        out_shape=out_shape,
        in_specs=in_specs,
        out_specs=out_specs or tuple(vmem() for _ in out_shape),
        scratch_shapes=scratch,
        compiler_params=pltpu.CompilerParams(vmem_limit_bytes=grant * 1024 * 1024),
        name=name,
    )(*args)


def work_shapes(tile_count, pixels, listed):
    tiles = 2 * tile_count
    steps = tiles * listed // LANES
    assert steps == 8
    return [pltpu.VMEM((pixels, steps * LANES), F32)] * 3 + [
        pltpu.VMEM((pixels, LANES), F32),
        pltpu.VMEM((3, pixels, LANES), F32),
        pltpu.VMEM((pixels, LANES), F32),
        pltpu.VMEM((pixels, LANES), F32),
        pltpu.VMEM((3, pixels, LANES), F32),
        pltpu.VMEM((3, pixels, 2 * LANES), BF16),
        pltpu.VMEM((tiles * 16, pixels), F32),
        pltpu.VMEM((3, steps, LANES), F32),
        pltpu.VMEM((steps * 24, LANES), F32),
        pltpu.VMEM((steps * 16 * tiles, LANES), F32),
        pltpu.VMEM((9, steps, LANES), F32),
        pltpu.VMEM((2, tile_count, ROWS, listed), F32),
    ]


def near(tile_ids, cameras, where, own, other, parts, tile_count):
    width = sum(part.shape[1] for part in parts)
    features = parts[0].shape[0]
    slabs = width // LANES
    pixels = listed = own.shape[1] // tile_count
    return call(
        functools.partial(near_kernel, len(parts)),
        "near",
        (
            jax.ShapeDtypeStruct((3, own.shape[1]), F32),
            jax.ShapeDtypeStruct((ROWS * slabs, LANES), F32),
            jax.ShapeDtypeStruct((ROWS, width), F32),
        ),
        [smem()] * 3 + [vmem()] * (2 + len(parts)),
        [pltpu.VMEM((features * slabs, LANES), F32), pltpu.VMEM((2,) + own.shape, F32)]
        + work_shapes(tile_count, pixels, listed),
        (tile_ids, cameras, where, own, other, *parts),
    )


def far(tile_ids, where, rows, partial, infos, pieces, tile_count, blocks):
    width = partial.shape[1]
    pixels = listed = infos.shape[1] // tile_count
    info = (infos.shape[0] // 2, infos.shape[1])
    return call(
        functools.partial(far_kernel, blocks),
        "far",
        (jax.ShapeDtypeStruct((ROWS, width // pieces), F32),) * pieces,
        [smem()] * 2 + [vmem()] * 3,
        [pltpu.VMEM((2,) + info, F32)] + work_shapes(tile_count, pixels, listed),
        (tile_ids, where, rows, partial, infos),
    )


def join(first, second):
    shape = (2 * first.shape[0], first.shape[1])
    return call(
        join_kernel, "join", (jax.ShapeDtypeStruct(shape, F32),), [vmem()] * 2, [], (first, second)
    )[0]


def update(where, cameras, params, adam_m, adam_v, packets):
    features, width = params.shape
    slabs = width // LANES
    shape = jax.ShapeDtypeStruct(params.shape, F32)
    return call(
        functools.partial(update_kernel, len(packets)),
        "update",
        (shape, shape, shape),
        [smem()] * 2 + [vmem()] * len(packets) + [any_space()] * 3,
        [
            pltpu.VMEM((features * slabs, LANES), F32),
            pltpu.VMEM((ROWS * slabs, LANES), F32),
            pltpu.VMEM((features * slabs, LANES), F32),
            pltpu.VMEM((3,) + params.shape, F32),
            pltpu.VMEM((3,) + params.shape, F32),
            pltpu.SemaphoreType.DMA((3,)),
            pltpu.SemaphoreType.DMA((3, (features + 15) // 16)),
        ],
        (where, cameras, *packets, params, adam_m, adam_v),
        (any_space(),) * 3,
    )


def swap(value, axis, d):
    if d == 0:
        return value
    return lax.ppermute(value, axis, [(k, k ^ d) for k in range(lax.axis_size(axis))])


def local(params, adam_m, adam_v, cameras, target, tile_ids, hit_shard, hit_local):
    width = params.shape[1]
    tile_count, listed = hit_local.shape
    shards = lax.axis_size("gs")
    along = lax.axis_size("tile")
    chunk = width // shards
    group = lax.axis_index("gs")
    seat = lax.axis_index("tile")
    aligned = chunk % LANES == 0
    team = BLOCK_TILES // tile_count
    assert team == 4
    blocks = along // team

    info, parts = pack(group, params, target, hit_shard, hit_local, shards, aligned)
    if not aligned:
        parts = [
            lax.dynamic_slice_in_dim(params, (group ^ d) * chunk, chunk, axis=1)
            for d in range(shards)
        ]
    parts = [swap(parts[d], "gs", d) for d in range(shards)]
    beside = swap(info, "tile", 1)
    beyond = swap(join(info, beside), "tile", 2)
    if not aligned:
        parts = [jnp.concatenate(parts, axis=1)]
    where = jnp.stack([seat % team, seat // team, jnp.int32(chunk)]).astype(jnp.int32)
    rendered, rows, partial = near(tile_ids, cameras, where, info, beside, parts, tile_count)
    packets = far(tile_ids, where, rows, partial, beyond, len(parts), tile_count, blocks)
    if not aligned:
        packets = [packets[0][:, d * chunk : (d + 1) * chunk] for d in range(shards)]
    packets = [swap(packets[d], "gs", d) for d in range(shards)]
    if blocks > 1:
        packets = [block_sum(packet, along, team) for packet in packets]
    if aligned:
        own = group
    else:
        packets = [jnp.stack(packets)[jnp.arange(shards) ^ group].transpose(1, 0, 2).reshape(ROWS, -1)]
        own = jnp.int32(0)
    new_params, new_m, new_v = update(
        own.reshape(1), cameras, params, adam_m, adam_v, packets
    )
    return (rendered, new_params, new_m, new_v)


def block_sum(packet, along, team):
    step = team
    while step < along:
        packet = packet + swap(packet, "tile", step)
        step *= 2
    return packet


def solution(mesh):
    return jax.shard_map(
        local,
        mesh=mesh,
        in_specs=(
            P(None, ("groups", "gs")),
            P(None, ("groups", "gs")),
            P(None, ("groups", "gs")),
            P("groups", None),
            P(None, ("groups", "gs", "tile")),
            P(("groups", "gs", "tile")),
            P(("groups", "gs", "tile"), None, None),
            P(("groups", "gs", "tile"), None),
        ),
        out_specs=(
            P(None, ("groups", "gs", "tile")),
            P(None, ("groups", "gs")),
            P(None, ("groups", "gs")),
            P(None, ("groups", "gs")),
        ),
        check_vma=False,
    )
```

```python
import functools

import jax
import jax.numpy as jnp
from jax import lax
from jax.experimental import pallas as pl
from jax.experimental.pallas import tpu as pltpu
from jax.sharding import PartitionSpec as P

TILES_X = 120
TILES_Y = 68
TILE_SIDE = 16
BLOCK_TILES = 8
LANES = 128
ROWS = 16
F32 = jnp.float32
BF16 = jnp.bfloat16

focal_length = 1000.0
center_x = 960.0
center_y = 540.0
dilation = 0.3
beta_one = 0.9
beta_two = 0.999
learn_rate = 0.01
adam_eps = 1e-08
adam_steps = 100.0
sh_const = (
    0.28209479177387814,
    0.4886025119029199,
    1.0925484305920792,
    0.31539156525252005,
    0.5462742152960396,
    0.5900435899266435,
    2.890611442640554,
    0.4570457994644658,
    0.3731763325901154,
    1.445305721320277,
)


def sh_basis(x, y, z):
    s = sh_const
    xx, yy, zz = x * x, y * y, z * z
    return [
        None,
        -s[1] * y,
        s[1] * z,
        -s[1] * x,
        s[2] * (x * y),
        -s[2] * (y * z),
        s[3] * (2.0 * zz - xx - yy),
        -s[2] * (x * z),
        s[4] * (xx - yy),
        -s[5] * y * (3.0 * xx - yy),
        s[6] * (x * y) * z,
        -s[7] * y * (4.0 * zz - xx - yy),
        s[8] * z * (2.0 * zz - 3.0 * xx - 3.0 * yy),
        -s[7] * x * (4.0 * zz - xx - yy),
        s[9] * z * (xx - yy),
        -s[5] * x * (xx - 3.0 * yy),
    ]


def sh_pull(h, x, y, z):
    s = sh_const
    xx, yy, zz = x * x, y * y, z * z
    xy, xz, yz = x * y, x * z, y * z
    diff = xx - yy
    ring = 4.0 * zz - xx - yy
    g_x = (
        -s[1] * h[3]
        + s[2] * (h[4] * y - h[7] * z)
        - (2.0 * s[3]) * h[6] * x
        + (2.0 * s[4]) * h[8] * x
        - (6.0 * s[5]) * h[9] * xy
        + s[6] * h[10] * yz
        + (2.0 * s[7]) * h[11] * xy
        - (6.0 * s[8]) * h[12] * xz
        - s[7] * h[13] * (ring - 2.0 * xx)
        + (2.0 * s[9]) * h[14] * xz
        - (3.0 * s[5]) * h[15] * diff
    )
    g_y = (
        -s[1] * h[1]
        + s[2] * (h[4] * x - h[5] * z)
        - (2.0 * s[3]) * h[6] * y
        - (2.0 * s[4]) * h[8] * y
        - (3.0 * s[5]) * h[9] * diff
        + s[6] * h[10] * xz
        - s[7] * h[11] * (ring - 2.0 * yy)
        - (6.0 * s[8]) * h[12] * yz
        + (2.0 * s[7]) * h[13] * xy
        - (2.0 * s[9]) * h[14] * yz
        + (6.0 * s[5]) * h[15] * xy
    )
    g_z = (
        s[1] * h[2]
        - s[2] * (h[5] * y + h[7] * x)
        + (4.0 * s[3]) * h[6] * z
        + s[6] * h[10] * xy
        - (8.0 * s[7]) * (h[11] * yz + h[13] * xz)
        + s[8] * h[12] * (6.0 * zz - 3.0 * xx - 3.0 * yy)
        + s[9] * h[14] * diff
    )
    return g_x, g_y, g_z


def project_parts(feat, cam):
    rot = [[cam[3 * r + c] for c in range(3)] for r in range(3)]
    off = [feat(a) - cam[9 + a] for a in range(3)]
    in_cam = [rot[r][0] * off[0] + rot[r][1] * off[1] + rot[r][2] * off[2] for r in range(3)]
    inv = 1.0 / in_cam[2]
    u = in_cam[0] * inv
    v = in_cam[1] * inv
    finv = focal_length * inv
    scale = [jnp.exp(2.0 * feat(3 + a)) for a in range(3)]
    quat = [feat(6 + a) for a in range(4)]
    rnorm = lax.rsqrt(quat[0] * quat[0] + quat[1] * quat[1] + quat[2] * quat[2] + quat[3] * quat[3])
    w, x, y, z = [q * rnorm for q in quat]
    turn = [
        [1.0 - 2.0 * (y * y + z * z), 2.0 * (x * y - w * z), 2.0 * (x * z + w * y)],
        [2.0 * (x * y + w * z), 1.0 - 2.0 * (x * x + z * z), 2.0 * (y * z - w * x)],
        [2.0 * (x * z - w * y), 2.0 * (y * z + w * x), 1.0 - 2.0 * (x * x + y * y)],
    ]
    screen = [
        [finv * (rot[0][c] - u * rot[2][c]) for c in range(3)],
        [finv * (rot[1][c] - v * rot[2][c]) for c in range(3)],
    ]
    axes = [
        [sum(screen[r][c] * turn[c][k] for c in range(3)) for k in range(3)] for r in range(2)
    ]
    wide = [[axes[r][k] * scale[k] for k in range(3)] for r in range(2)]
    cov_xx = sum(wide[0][k] * axes[0][k] for k in range(3)) + dilation
    cov_xy = sum(wide[0][k] * axes[1][k] for k in range(3))
    cov_yy = sum(wide[1][k] * axes[1][k] for k in range(3)) + dilation
    rdet = 1.0 / (cov_xx * cov_yy - cov_xy * cov_xy)
    conic = (cov_yy * rdet, -cov_xy * rdet, cov_xx * rdet)
    rlen = lax.rsqrt(off[0] * off[0] + off[1] * off[1] + off[2] * off[2])
    way = [off[a] * rlen for a in range(3)]
    return dict(
        rot=rot, inv=inv, u=u, v=v, finv=finv, scale=scale, rnorm=rnorm, rotor=(w, x, y, z), turn=turn,
        screen=screen, axes=axes, wide=wide, conic=conic, rlen=rlen, way=way,
    )


def project_rows(feat, cam):
    part = project_parts(feat, cam)
    basis = sh_basis(*part["way"])
    colours = []
    for k in range(3):
        total = 0.5 + sh_const[0] * feat(11 + 16 * k)
        for b in range(1, 16):
            total = total + feat(11 + 16 * k + b) * basis[b]
        colours.append(total)
    mean_x = focal_length * part["u"] + center_x
    mean_y = focal_length * part["v"] + center_y
    logit = feat(10)
    log_opacity = jnp.minimum(logit, 0.0) - jnp.log(1.0 + jnp.exp(-jnp.abs(logit)))
    return [mean_x, mean_y, *part["conic"], log_opacity, *colours]


def project_pull(feat, cam, grads, put):
    part = project_parts(feat, cam)
    g_mx, g_my, g_a, g_b, g_c, g_o = grads[:6]
    g_col = grads[6:9]
    way, rlen = part["way"], part["rlen"]
    basis = sh_basis(*way)
    pulled = [None]
    for k in range(3):
        put(11 + 16 * k, sh_const[0] * g_col[k])
    for b in range(1, 16):
        total = 0.0
        for k in range(3):
            put(11 + 16 * k + b, g_col[k] * basis[b])
            total = total + g_col[k] * feat(11 + 16 * k + b)
        pulled.append(total)
    g_way = sh_pull(pulled, *way)
    along = way[0] * g_way[0] + way[1] * g_way[1] + way[2] * g_way[2]
    g_off = [(g_way[a] - way[a] * along) * rlen for a in range(3)]
    put(10, g_o / (1.0 + jnp.exp(feat(10))))
    a, b, c = part["conic"]
    g_xx = -(a * a * g_a + a * b * g_b + b * b * g_c)
    g_xy = -(2.0 * a * b * g_a + (a * c + b * b) * g_b + 2.0 * b * c * g_c)
    g_yy = -(b * b * g_a + b * c * g_b + c * c * g_c)
    axes, wide, turn, screen = part["axes"], part["wide"], part["turn"], part["screen"]
    for k in range(3):
        g_scale = (
            g_xx * axes[0][k] * wide[0][k]
            + g_xy * axes[0][k] * wide[1][k]
            + g_yy * axes[1][k] * wide[1][k]
        )
        put(3 + k, 2.0 * g_scale)
    g_axes = [
        [2.0 * g_xx * wide[0][k] + g_xy * wide[1][k] for k in range(3)],
        [2.0 * g_yy * wide[1][k] + g_xy * wide[0][k] for k in range(3)],
    ]
    g_screen = [
        [sum(g_axes[r][k] * turn[c][k] for k in range(3)) for c in range(3)] for r in range(2)
    ]
    gm = [
        [g_axes[0][k] * screen[0][c] + g_axes[1][k] * screen[1][c] for k in range(3)]
        for c in range(3)
    ]
    w, x, y, z = part["rotor"]
    up_xy, up_xz, up_yz = gm[0][1] + gm[1][0], gm[0][2] + gm[2][0], gm[1][2] + gm[2][1]
    un_xy, un_xz, un_yz = gm[1][0] - gm[0][1], gm[0][2] - gm[2][0], gm[2][1] - gm[1][2]
    g_rotor = [
        2.0 * (z * un_xy + y * un_xz + x * un_yz),
        2.0 * (y * up_xy + z * up_xz + w * un_yz - 2.0 * x * (gm[1][1] + gm[2][2])),
        2.0 * (x * up_xy + z * up_yz + w * un_xz - 2.0 * y * (gm[0][0] + gm[2][2])),
        2.0 * (x * up_xz + y * up_yz + w * un_xy - 2.0 * z * (gm[0][0] + gm[1][1])),
    ]
    rotor = (w, x, y, z)
    along = sum(rotor[i] * g_rotor[i] for i in range(4))
    for i in range(4):
        put(6 + i, (g_rotor[i] - rotor[i] * along) * part["rnorm"])
    rot, inv, finv, u, v = part["rot"], part["inv"], part["finv"], part["u"], part["v"]
    g_u = focal_length * g_mx - finv * sum(g_screen[0][c] * rot[2][c] for c in range(3))
    g_v = focal_length * g_my - finv * sum(g_screen[1][c] * rot[2][c] for c in range(3))
    g_f = sum(g_screen[r][c] * screen[r][c] for r in range(2) for c in range(3))
    g_in = [g_u * inv, g_v * inv, -(g_f + g_u * u + g_v * v) * inv]
    for axis in range(3):
        put(
            axis,
            g_off[axis] + rot[0][axis] * g_in[0] + rot[1][axis] * g_in[1] + rot[2][axis] * g_in[2],
        )


def split(value):
    high = value.astype(BF16)
    return high, (value - high.astype(F32)).astype(BF16)


def matmul(a, b, dims=((1,), (0,))):
    return lax.dot_general(a, b, (dims, ((), ())), preferred_element_type=F32)


def spread_features(parts, scratch, count):
    tiles = sum(part.shape[1] for part in parts) // LANES
    at = 0
    for part in parts:
        for first in range(0, part.shape[1], LANES):
            for row in range(0, count, 8):
                rows = min(8, count - row)
                scratch[pl.ds(row * tiles + at, rows, stride=tiles), :] = part[
                    row : row + rows, first : first + LANES
                ]
            at += 1
    return tiles


def pack_kernel(shards, pieces, where, *refs):
    sources, refs = refs[: 3 + (pieces > 0)], refs[3 + (pieces > 0) :]
    info, parts, refs = refs[0], refs[1 : 1 + pieces], refs[1 + pieces :]
    shard_of, local_of, goal, place_s, sems, cut_sems = refs
    group = where[0]
    loads = [
        pltpu.make_async_copy(source, held, sems.at[k])
        for k, (source, held) in enumerate(zip(sources, (shard_of, local_of, goal)))
    ]
    for d in range(pieces):
        chunk = parts[d].shape[1]
        first = pl.multiple_of((group ^ d) * chunk, LANES)
        loads.append(
            pltpu.make_async_copy(sources[3].at[:, pl.ds(first, chunk)], parts[d], cut_sems.at[d])
        )
    for load in loads:
        load.start()
    for load in loads[:3]:
        load.wait()
    width = info.shape[1]
    tile_count, listed = local_of.shape
    rows_each = (info.shape[0] - 4) // tile_count
    columns = rows_each * width
    chunk = columns // shards
    info[0:3, :] = goal[...]
    for t in range(tile_count):
        place = (shard_of[t] ^ group) * chunk + (local_of[t : t + 1, :] - group * chunk)
        info[3:4, t * listed : (t + 1) * listed] = place.astype(F32)
        row_i = lax.broadcasted_iota(jnp.int32, (LANES, LANES), 0)
        col_i = lax.broadcasted_iota(jnp.int32, (LANES, LANES), 1)
        for first in range(0, listed, LANES):
            spread = jnp.broadcast_to(place[:, first : first + LANES].astype(F32), (LANES, LANES))
            place_s[first : first + LANES, :] = jnp.broadcast_to(
                jnp.sum(jnp.where(row_i == col_i, spread, 0.0), axis=1, keepdims=True), (LANES, LANES)
            )
        lane_of = lax.broadcasted_iota(jnp.int32, (8, LANES), 1).astype(F32)
        row_of = lax.broadcasted_iota(jnp.int32, (8, LANES), 0).astype(F32)
        for s in range(columns // LANES):
            best = jnp.full((8, LANES), -1.0, F32)
            column = lane_of + float(s * LANES)
            for first in range(0, listed, 8):
                best = jnp.where(
                    place_s[first : first + 8, :] == column, row_of + float(first), best
                )
            best = jnp.max(best, axis=0, keepdims=True)
            row, at = 4 + t * rows_each + s * LANES // width, s * LANES % width
            info[row : row + 1, at : at + LANES] = best
    for load in loads[3:]:
        load.wait()


def pack(group, params, target, hit_shard, hit_local, shards, aligned):
    features, columns = params.shape
    tile_count, listed = hit_local.shape
    width = target.shape[1]
    rows = 4 + tile_count * (columns // width)
    pieces = shards if aligned else 0
    piece = jax.ShapeDtypeStruct((features, columns // shards), F32)
    args = (hit_shard.reshape(tile_count, 1, listed), hit_local, target) + (params,) * aligned
    out = call(
        functools.partial(pack_kernel, shards, pieces),
        "pack",
        (jax.ShapeDtypeStruct((rows, width), F32),) + (piece,) * pieces,
        [smem()] + [pl.BlockSpec(memory_space=pltpu.HBM)] * len(args),
        [
            pltpu.VMEM((tile_count, 1, listed), jnp.int32),
            pltpu.VMEM((tile_count, listed), jnp.int32),
            pltpu.VMEM(target.shape, F32),
            pltpu.VMEM((listed, LANES), F32),
            pltpu.SemaphoreType.DMA((3,)),
            pltpu.SemaphoreType.DMA((shards,)),
        ],
        (group.reshape(1),) + tuple(pltpu.with_memory_space_constraint(a, pltpu.HBM) for a in args),
    )
    return out[0], list(out[1:])


def lane_gather(source, lane):
    return jnp.take_along_axis(source, lane, axis=1, mode="promise_in_bounds")


def fold(values):
    sub = lax.broadcasted_iota(jnp.int32, (8, LANES), 0)
    values = list(values)
    step = 4
    while step:
        low = (sub & step) == 0
        moved = [jnp.where(low, values[i + step], values[i]) for i in range(step)]
        if step < 4:
            moved = [
                jnp.where(low, pltpu.roll(each, 8 - step, 0), pltpu.roll(each, step, 0))
                for each in moved
            ]
        else:
            moved = [pltpu.roll(each, step, 0) for each in moved]
        values = [jnp.where(low, values[i], values[i + step]) + moved[i] for i in range(step)]
        step //= 2
    return values[0]


def spread(row):
    return jnp.broadcast_to(row, (8, LANES))


def composite(tiles, first_group, me, rows, info_s, rendered, work):
    alpha_s, weight_s, left_s, image_s, before_s, behind_s, error_s, joined_s, wrong_s, coef_s, line_s, part_s, acc_s = work
    groups, tile_count, _, listed = acc_s.shape
    pixels = info_s.shape[2] // tile_count
    tiles_here = groups * tile_count
    segments = LANES // tiles_here
    steps = listed // segments
    halves = listed // LANES
    slabs = rows.shape[0] // ROWS
    side = TILE_SIDE
    middle = 0.5 * side - 0.5
    first_col, first_row = tiles
    lane = lax.broadcasted_iota(jnp.int32, (8, LANES), 1)
    sub = lax.broadcasted_iota(jnp.int32, (8, LANES), 0)
    segment = lane % segments

    pattern = (lane % (LANES // steps)) * steps + sub
    place = jnp.zeros((8, LANES), F32)
    col_0 = row_0 = jnp.zeros((8, LANES), F32)
    for n in range(tiles_here):
        g, t = n // tile_count, n % tile_count
        for h in range(halves):
            first = t * listed + h * LANES
            here = lane_gather(spread(info_s[g, 3:4, first : first + LANES]), pattern)
            place = jnp.where(lane // (LANES // steps) == n * halves + h, here, place)
        slot = (me ^ (first_group + g)) * tile_count + t
        own = lane // segments == n
        col_0 = jnp.where(own, ((first_col + slot % 4) * side).astype(F32) + 0.5 * side, col_0)
        row_0 = jnp.where(own, ((first_row + slot // 4) * side).astype(F32) + 0.5 * side, row_0)
    place = place.astype(jnp.int32)
    at, slab = place & (LANES - 1), place >> 7
    entry = []
    for f in range(9):
        value = lane_gather(spread(rows[f : f + 1, :]), at)
        for s in range(1, slabs):
            here = lane_gather(spread(rows[s * ROWS + f : s * ROWS + f + 1, :]), at)
            value = jnp.where(slab == s, here, value)
        entry.append(value)
    mean_u, mean_v = entry[0] - col_0, entry[1] - row_0
    quad_a, quad_b, quad_c = -0.5 * entry[2], -entry[3], -0.5 * entry[4]
    slope_u = 2.0 * quad_a * mean_u + quad_b * mean_v
    slope_v = 2.0 * quad_c * mean_v + quad_b * mean_u
    level = 0.5 * (slope_u * mean_u + slope_v * mean_v) + entry[5]
    for f, value in enumerate(
        (level, -slope_u, quad_a, -slope_v, quad_b, quad_c, entry[6], entry[7], entry[8])
    ):
        coef_s[f] = value
    for s in range(steps):
        c = [spread(coef_s[f, s : s + 1, :]) for f in range(5)]
        for half in range(side // 8):
            u = sub.astype(F32) + (8.0 * half - middle)
            line_s[0, s, half] = c[0] + u * (c[1] + u * c[2])
            line_s[1, s, half] = c[3] + u * c[4]

    rows_each = 4

    def forward(i, carry):
        for j in range(rows_each):
            row = i * rows_each + j
            v = row.astype(F32) - middle
            left = [None] * (side // 8)
            image = [[None] * 3 for _ in left]
            for s in range(steps):
                quad = spread(coef_s[5, s : s + 1, :]) * v
                colour = [spread(coef_s[6 + k, s : s + 1, :]) for k in range(3)]
                for half in range(side // 8):
                    power = line_s[0, s, half] + v * (line_s[1, s, half] + quad)
                    alpha = jnp.exp(power)
                    at = pl.ds(pl.multiple_of(row * side, side) + (s * pixels + half * 8), 8)
                    alpha_s[at, :] = alpha
                    if s == 0:
                        weight = alpha
                        left[half] = 1.0 - alpha
                        image[half] = [weight * colour[k] for k in range(3)]
                    else:
                        weight = alpha * left[half]
                        left[half] = left[half] - weight
                        image[half] = [
                            image[half][k] + weight * colour[k] for k in range(3)
                        ]
                    weight_s[at, :] = weight
            for half in range(side // 8):
                at = pl.ds(pl.multiple_of(row * side, side) + half * 8, 8)
                left_s[at, :] = left[half]
                for k in range(3):
                    image_s[k, at, :] = image[half][k]
        return carry

    lax.fori_loop(0, side // rows_each, forward, 0)

    tall = 32
    segment_t = lax.broadcasted_iota(jnp.int32, (tall, LANES), 1) % segments
    for first in range(0, pixels, tall):
        at = slice(first, first + tall)
        passed = left_s[at, :]
        step = 1
        while step < segments:
            passed = passed * jnp.where(segment_t >= step, pltpu.roll(passed, step, 1), 1.0)
            step *= 2
        before = jnp.where(segment_t >= 1, pltpu.roll(passed, 1, 1), 1.0)
        before_s[at, :] = before
        for k in range(3):
            joined_s[k, at, :LANES], joined_s[k, at, LANES:] = split(before * image_s[k, at, :])
    pick = lax.broadcasted_iota(jnp.int32, (16, 2 * LANES), 1) % LANES // segments
    pick = jnp.where(
        pick == lax.broadcasted_iota(jnp.int32, (16, 2 * LANES), 0), 1.0, 0.0
    ).astype(BF16)
    wrong_s[...] = jnp.zeros(wrong_s.shape, F32)
    for k in range(3):
        image = matmul(pick, joined_s[k], ((1,), (1,)))
        for n in range(tiles_here):
            g, t = n // tile_count, n % tile_count
            here = slice(t * pixels, (t + 1) * pixels)
            if rendered is not None and g == 0:
                rendered[k : k + 1, here] = image[n : n + 1]
            wrong = image[n : n + 1] - info_s[g, k : k + 1, here]
            high = wrong.astype(BF16).astype(F32)
            wrong_s[k, n : n + 1, :] = high
            wrong_s[k, 8 + n : 9 + n, :] = wrong - high
    back = lax.broadcasted_iota(jnp.int32, (16, LANES), 1) // segments
    back = jnp.where(
        back == lax.broadcasted_iota(jnp.int32, (16, LANES), 0) % 8, 1.0, 0.0
    ).astype(BF16)
    for k in range(3):
        error_s[k] = matmul(wrong_s[k].astype(BF16), back, ((0,), (0,)))

    for first in range(0, pixels, tall):
        at = slice(first, first + tall)
        error = [error_s[k, at, :] for k in range(3)]
        through = left_s[at, :]
        own = sum(error[k] * image_s[k, at, :] for k in range(3))
        step = 1
        while step < segments:
            inside = segment_t < segments - step
            own = own + through * jnp.where(inside, pltpu.roll(own, LANES - step, 1), 0.0)
            if 2 * step < segments:
                through = through * jnp.where(inside, pltpu.roll(through, LANES - step, 1), 1.0)
            step *= 2
        before = before_s[at, :]
        behind = jnp.where(segment_t < segments - 1, pltpu.roll(own, LANES - 1, 1), 0.0)
        behind_s[at, :] = before * behind
        for k in range(3):
            error_s[k, at, :] = before * error[k]

    def backward(i, carry):
        s = steps - 1 - i
        colour = [spread(coef_s[6 + k, pl.ds(s, 1), :]) for k in range(3)]
        plain = [[None] * 3 for _ in range(side // 8)]
        hues = [None] * 3
        for row in range(side):
            for half in range(side // 8):
                at = pl.ds(row * side + half * 8, 8)
                of_step = pl.ds(pl.multiple_of(s * pixels, pixels) + (row * side + half * 8), 8)
                weight = weight_s[of_step, :]
                error = [error_s[k, at, :] for k in range(3)]
                pull = error[0] * colour[0] + error[1] * colour[1] + error[2] * colour[2]
                behind = behind_s[at, :]
                gap = pull - behind
                behind_s[at, :] = behind + alpha_s[of_step, :] * gap
                push = weight * gap
                hue = [weight * error[k] for k in range(3)]
                if row == 0:
                    plain[half] = [push, push, push]
                else:
                    plain[half][0] = plain[half][0] + push
                    plain[half][1] = plain[half][1] + plain[half][0]
                    plain[half][2] = plain[half][2] + plain[half][1]
                hues = [hue[k] if hues[k] is None else hues[k] + hue[k] for k in range(3)]
        for half in range(side // 8):
            for m in range(3):
                part_s[3 * half + m, s] = plain[half][m]
        for k in range(3):
            part_s[6 + k, s] = hues[k]
        return carry

    lax.fori_loop(0, steps, backward, 0)

    shift = side - middle
    u = [sub.astype(F32) + (8.0 * half - middle) for half in range(side // 8)]
    parts = []
    for s in range(steps):
        moments = [0.0] * 6
        for half in range(side // 8):
            one, two, three = [part_s[3 * half + m, s] for m in range(3)]
            by_v = shift * one - two
            by_vv = shift * shift * one - (2.0 * shift + 1.0) * two + 2.0 * three
            by_u = u[half] * one
            terms = (one, by_u, by_v, u[half] * by_u, u[half] * by_v, by_vv)
            moments = [moments[m] + terms[m] for m in range(6)]
        parts.append(moments + [part_s[6 + k, s] for k in range(3)])
    sums = [fold([parts[s][m] for s in range(steps)]) for m in range(9)]
    m_00, m_10, m_01, m_20, m_11, m_02, *grads = sums
    n_10 = m_10 - mean_u * m_00
    n_01 = m_01 - mean_v * m_00
    grads = [
        -(2.0 * quad_a * n_10 + quad_b * n_01),
        -(2.0 * quad_c * n_01 + quad_b * n_10),
        -0.5 * (m_20 - mean_u * (m_10 + n_10)),
        -(m_11 - mean_u * m_01 - mean_v * n_10),
        -0.5 * (m_02 - mean_v * (m_01 + n_01)),
        m_00,
    ] + grads
    mine = sub == lane % steps
    last = []
    for n in range(tiles_here):
        g, t = n // tile_count, n % tile_count
        for h in range(halves):
            at = lane // steps + (n * segments + h * (LANES // steps))
            found = [jnp.where(mine, lane_gather(grads[f], at), 0.0) for f in range(9)]
            acc_s[g, t, 0:8, h * LANES : (h + 1) * LANES] = fold(found[:8])
            last.append(found[8])
    acc_s[0, 0, 8:16, :LANES] = fold(last)


def pool_sum(slab, info_s, acc_s):
    groups, tile_count, _, listed = acc_s.shape
    halves = listed // LANES
    width = info_s.shape[2]
    rows_each = (info_s.shape[1] - 4) // tile_count
    row_of = lax.broadcasted_iota(jnp.int32, (8, LANES), 0)

    totals, every = [], None
    for g in range(groups):
        total = jnp.zeros((8, LANES), F32)
        for t in range(tile_count):
            row, first = 4 + t * rows_each + slab * LANES // width, slab * LANES % width
            at = info_s[g, row : row + 1, first : first + LANES].astype(jnp.int32)
            at = jnp.broadcast_to(at, (8, LANES))
            n = g * tile_count + t
            every = at if every is None else jnp.where(row_of >= n * halves, at, every)
            lane, half = at & (LANES - 1), at >> 7
            for h in range(halves):
                here = lane_gather(acc_s[g, t, 0:8, h * LANES : (h + 1) * LANES], lane)
                total = total + jnp.where(half == h, here, 0.0)
        totals.append(total)
    here = lane_gather(acc_s[0, 0, 8:16, :LANES], every & (LANES - 1))
    ninth = jnp.where(every >> 7 == row_of % halves, here, 0.0)
    return totals[0] + totals[1], jnp.sum(ninth, axis=0, keepdims=True)


def block_start(tile_id):
    within = tile_id % (TILES_X * TILES_Y)
    return (within % TILES_X) // 4 * 4, (within // TILES_X) // 2 * 2


def near_kernel(pieces, tile_ids, cams, where, own, other, *refs):
    parts = refs[:pieces]
    rendered, rows, partial, feats, info_s, *work = refs[pieces:]
    view = tile_ids[0] // (TILES_X * TILES_Y)
    cam = [cams[view, i] for i in range(12)]
    slabs = spread_features(parts, feats, parts[0].shape[0])
    projected = project_rows(lambda f: feats[f * slabs : (f + 1) * slabs, :], cam)
    for f, value in enumerate(projected):
        rows[pl.ds(f, slabs, stride=ROWS), :] = value
    info_s[0] = own[...]
    info_s[1] = other[...]
    composite(block_start(tile_ids[0]), 0, where[0], rows, info_s, rendered, work)
    for s in range(slabs):
        at = slice(s * LANES, (s + 1) * LANES)
        partial[0:8, at], partial[8:9, at] = pool_sum(s, info_s, work[-1])


def far_kernel(blocks, tile_ids, where, rows, partial, infos, *refs):
    *packets, info_s = refs[: len(refs) - 13]
    work = refs[len(refs) - 13 :]
    half = infos.shape[0] // 2
    info_s[0] = infos[:half, :]
    info_s[1] = infos[half:, :]
    composite(block_start(tile_ids[0]), 2, where[0], rows, info_s, None, work)
    share = (tile_ids[0] // (TILES_X * TILES_Y)).astype(F32)
    row_of = lax.broadcasted_iota(jnp.int32, (8, LANES), 0)
    lane_of = lax.broadcasted_iota(jnp.int32, (8, LANES), 1)
    chunk = packets[0].shape[1]
    for s in range(rows.shape[0] // ROWS):
        total, ninth = pool_sum(s, info_s, work[-1])
        total = total + partial[0:8, s * LANES : (s + 1) * LANES]
        ninth = ninth + partial[8:9, s * LANES : (s + 1) * LANES]
        if blocks == 1:
            mine = share
        else:
            column = s * LANES + lane_of
            mine = jnp.where(column % where[2] // (where[2] // blocks) == where[1], share, 0.0)
        at = slice(s * LANES % chunk, s * LANES % chunk + LANES)
        packets[s * LANES // chunk][0:8, at] = total
        packets[s * LANES // chunk][8:16, at] = jnp.where(
            row_of == 0, jnp.broadcast_to(ninth, (8, LANES)), mine
        )


def join_kernel(first, second, out):
    half = first.shape[0]
    out[:half, :] = first[...]
    out[half:, :] = second[...]


def update_kernel(pieces, where, cams, *refs):
    packets = refs[:pieces]
    sources, sinks = refs[pieces : pieces + 3], refs[pieces + 3 : pieces + 6]
    feats, rows, grads, held, made, in_sems, out_sems = refs[pieces + 6 :]
    params, adam_m, adam_v = held.at[0], held.at[1], held.at[2]
    features, width = params.shape
    loads = [pltpu.make_async_copy(sources[k], held.at[k], in_sems.at[k]) for k in range(3)]
    for load in loads:
        load.start()
    chunk = packets[0].shape[1]
    slabs = width // LANES
    for d in range(pieces):
        for h in range(chunk // LANES):
            slab = (where[0] ^ d) * (chunk // LANES) + h
            rows[pl.ds(slab, ROWS, stride=slabs), :] = packets[d][:, h * LANES : (h + 1) * LANES]
    pulled = [rows[f * slabs : (f + 1) * slabs, :] for f in range(10)]
    view = pulled[9]
    cam = []
    for i in range(12):
        value = jnp.full((slabs, LANES), cams[0, i], F32)
        for v in range(1, cams.shape[0]):
            value = jnp.where(view == float(v), cams[v, i], value)
        cam.append(value)

    def put(f, value):
        grads[f * slabs : (f + 1) * slabs, :] = value

    loads[0].wait()
    spread_features([params], feats, features)
    project_pull(lambda f: feats[f * slabs : (f + 1) * slabs, :], cam, pulled[:9], put)
    rate = learn_rate / (1.0 - beta_one**adam_steps)
    unbias = 1.0 / (1.0 - beta_two**adam_steps)
    loads[1].wait()
    loads[2].wait()
    stores = []
    for row in range(0, features, 8):
        count = min(8, features - row)
        for s in range(slabs):
            at = (slice(row, row + count), slice(s * LANES, (s + 1) * LANES))
            grad = grads[pl.ds(row * slabs + s, count, stride=slabs), :]
            moment = beta_one * adam_m[at] + (1.0 - beta_one) * grad
            second = beta_two * adam_v[at] + (1.0 - beta_two) * grad * grad
            made.at[1][at] = moment
            made.at[2][at] = second
            made.at[0][at] = params[at] - rate * moment / (jnp.sqrt(second * unbias) + adam_eps)
        if row % 16 == 8 or row + count == features:
            first = row // 16 * 16
            span = pl.ds(first, row + count - first)
            for k in range(3):
                store = pltpu.make_async_copy(
                    made.at[k, span], sinks[k].at[span], out_sems.at[k, first // 16]
                )
                store.start()
                stores.append(store)
    for store in stores:
        store.wait()


def vmem():
    return pl.BlockSpec(memory_space=pltpu.VMEM)


def smem():
    return pl.BlockSpec(memory_space=pltpu.SMEM)


def any_space():
    return pl.BlockSpec(memory_space=pl.ANY)


def call(kernel, name, out_shape, in_specs, scratch, args, out_specs=None, grant=32):
    return pl.pallas_call(
        kernel,
        out_shape=out_shape,
        in_specs=in_specs,
        out_specs=out_specs or tuple(vmem() for _ in out_shape),
        scratch_shapes=scratch,
        compiler_params=pltpu.CompilerParams(vmem_limit_bytes=grant * 1024 * 1024),
        name=name,
    )(*args)


def work_shapes(tile_count, pixels, listed):
    steps = 2 * tile_count * listed // LANES
    assert steps == 8
    return [
        pltpu.VMEM((steps * pixels, LANES), F32),
        pltpu.VMEM((steps * pixels, LANES), F32),
        pltpu.VMEM((pixels, LANES), F32),
        pltpu.VMEM((3, pixels, LANES), F32),
        pltpu.VMEM((pixels, LANES), F32),
        pltpu.VMEM((pixels, LANES), F32),
        pltpu.VMEM((3, pixels, LANES), F32),
        pltpu.VMEM((3, pixels, 2 * LANES), BF16),
        pltpu.VMEM((3, 16, pixels), F32),
        pltpu.VMEM((9, steps, LANES), F32),
        pltpu.VMEM((2, steps, TILE_SIDE // 8, 8, LANES), F32),
        pltpu.VMEM((9, steps, 8, LANES), F32),
        pltpu.VMEM((2, tile_count, ROWS, listed), F32),
    ]


def near(tile_ids, cameras, where, own, other, parts, tile_count):
    width = sum(part.shape[1] for part in parts)
    features = parts[0].shape[0]
    slabs = width // LANES
    pixels = listed = own.shape[1] // tile_count
    return call(
        functools.partial(near_kernel, len(parts)),
        "near",
        (
            jax.ShapeDtypeStruct((3, own.shape[1]), F32),
            jax.ShapeDtypeStruct((ROWS * slabs, LANES), F32),
            jax.ShapeDtypeStruct((ROWS, width), F32),
        ),
        [smem()] * 3 + [vmem()] * (2 + len(parts)),
        [pltpu.VMEM((features * slabs, LANES), F32), pltpu.VMEM((2,) + own.shape, F32)]
        + work_shapes(tile_count, pixels, listed),
        (tile_ids, cameras, where, own, other, *parts),
    )


def far(tile_ids, where, rows, partial, infos, pieces, tile_count, blocks):
    width = partial.shape[1]
    pixels = listed = infos.shape[1] // tile_count
    info = (infos.shape[0] // 2, infos.shape[1])
    return call(
        functools.partial(far_kernel, blocks),
        "far",
        (jax.ShapeDtypeStruct((ROWS, width // pieces), F32),) * pieces,
        [smem()] * 2 + [vmem()] * 3,
        [pltpu.VMEM((2,) + info, F32)] + work_shapes(tile_count, pixels, listed),
        (tile_ids, where, rows, partial, infos),
    )


def join(first, second):
    shape = (2 * first.shape[0], first.shape[1])
    return call(
        join_kernel, "join", (jax.ShapeDtypeStruct(shape, F32),), [vmem()] * 2, [], (first, second)
    )[0]


def update(where, cameras, params, adam_m, adam_v, packets):
    features, width = params.shape
    slabs = width // LANES
    shape = jax.ShapeDtypeStruct(params.shape, F32)
    return call(
        functools.partial(update_kernel, len(packets)),
        "update",
        (shape, shape, shape),
        [smem()] * 2 + [vmem()] * len(packets) + [any_space()] * 3,
        [
            pltpu.VMEM((features * slabs, LANES), F32),
            pltpu.VMEM((ROWS * slabs, LANES), F32),
            pltpu.VMEM((features * slabs, LANES), F32),
            pltpu.VMEM((3,) + params.shape, F32),
            pltpu.VMEM((3,) + params.shape, F32),
            pltpu.SemaphoreType.DMA((3,)),
            pltpu.SemaphoreType.DMA((3, (features + 15) // 16)),
        ],
        (where, cameras, *packets, params, adam_m, adam_v),
        (any_space(),) * 3,
    )


def swap(value, axis, d):
    if d == 0:
        return value
    return lax.ppermute(value, axis, [(k, k ^ d) for k in range(lax.axis_size(axis))])


def local(params, adam_m, adam_v, cameras, target, tile_ids, hit_shard, hit_local):
    width = params.shape[1]
    tile_count, listed = hit_local.shape
    shards = lax.axis_size("gs")
    along = lax.axis_size("tile")
    chunk = width // shards
    group = lax.axis_index("gs")
    seat = lax.axis_index("tile")
    aligned = chunk % LANES == 0
    team = BLOCK_TILES // tile_count
    assert team == 4
    blocks = along // team

    info, parts = pack(group, params, target, hit_shard, hit_local, shards, aligned)
    if not aligned:
        parts = [
            lax.dynamic_slice_in_dim(params, (group ^ d) * chunk, chunk, axis=1)
            for d in range(shards)
        ]
    parts = [swap(parts[d], "gs", d) for d in range(shards)]
    beside = swap(info, "tile", 1)
    beyond = swap(join(info, beside), "tile", 2)
    if not aligned:
        parts = [jnp.concatenate(parts, axis=1)]
    where = jnp.stack([seat % team, seat // team, jnp.int32(chunk)]).astype(jnp.int32)
    rendered, rows, partial = near(tile_ids, cameras, where, info, beside, parts, tile_count)
    packets = far(tile_ids, where, rows, partial, beyond, len(parts), tile_count, blocks)
    if not aligned:
        packets = [packets[0][:, d * chunk : (d + 1) * chunk] for d in range(shards)]
    packets = [swap(packets[d], "gs", d) for d in range(shards)]
    if blocks > 1:
        packets = [block_sum(packet, along, team) for packet in packets]
    if aligned:
        own = group
    else:
        packets = [jnp.stack(packets)[jnp.arange(shards) ^ group].transpose(1, 0, 2).reshape(ROWS, -1)]
        own = jnp.int32(0)
    new_params, new_m, new_v = update(
        own.reshape(1), cameras, params, adam_m, adam_v, packets
    )
    return (rendered, new_params, new_m, new_v)


def block_sum(packet, along, team):
    step = team
    while step < along:
        packet = packet + swap(packet, "tile", step)
        step *= 2
    return packet


def solution(mesh):
    return jax.shard_map(
        local,
        mesh=mesh,
        in_specs=(
            P(None, ("groups", "gs")),
            P(None, ("groups", "gs")),
            P(None, ("groups", "gs")),
            P("groups", None),
            P(None, ("groups", "gs", "tile")),
            P(("groups", "gs", "tile")),
            P(("groups", "gs", "tile"), None, None),
            P(("groups", "gs", "tile"), None),
        ),
        out_specs=(
            P(None, ("groups", "gs", "tile")),
            P(None, ("groups", "gs")),
            P(None, ("groups", "gs")),
            P(None, ("groups", "gs")),
        ),
        check_vma=False,
    )
```

```python
import functools

import jax
import jax.numpy as jnp
from jax import lax
from jax.experimental import pallas as pl
from jax.experimental.pallas import tpu as pltpu
from jax.sharding import PartitionSpec as P

TILES_X = 120
TILES_Y = 68
TILE_SIDE = 16
BLOCK_TILES = 8
LANES = 128
ROWS = 16
SPAN_STEP, LIST_STEP = 3, 25
F32 = jnp.float32
BF16 = jnp.bfloat16

focal_length = 1000.0
center_x = 960.0
center_y = 540.0
dilation = 0.3
beta_one = 0.9
beta_two = 0.999
learn_rate = 0.01
adam_eps = 1e-08
adam_steps = 100.0
sh_const = (
    0.28209479177387814,
    0.4886025119029199,
    1.0925484305920792,
    0.31539156525252005,
    0.5462742152960396,
    0.5900435899266435,
    2.890611442640554,
    0.4570457994644658,
    0.3731763325901154,
    1.445305721320277,
)


def sh_basis(x, y, z):
    s = sh_const
    xx, yy, zz = x * x, y * y, z * z
    return [
        None,
        -s[1] * y,
        s[1] * z,
        -s[1] * x,
        s[2] * (x * y),
        -s[2] * (y * z),
        s[3] * (2.0 * zz - xx - yy),
        -s[2] * (x * z),
        s[4] * (xx - yy),
        -s[5] * y * (3.0 * xx - yy),
        s[6] * (x * y) * z,
        -s[7] * y * (4.0 * zz - xx - yy),
        s[8] * z * (2.0 * zz - 3.0 * xx - 3.0 * yy),
        -s[7] * x * (4.0 * zz - xx - yy),
        s[9] * z * (xx - yy),
        -s[5] * x * (xx - 3.0 * yy),
    ]


def sh_pull(h, x, y, z):
    s = sh_const
    xx, yy, zz = x * x, y * y, z * z
    xy, xz, yz = x * y, x * z, y * z
    diff = xx - yy
    ring = 4.0 * zz - xx - yy
    g_x = (
        -s[1] * h[3]
        + s[2] * (h[4] * y - h[7] * z)
        - (2.0 * s[3]) * h[6] * x
        + (2.0 * s[4]) * h[8] * x
        - (6.0 * s[5]) * h[9] * xy
        + s[6] * h[10] * yz
        + (2.0 * s[7]) * h[11] * xy
        - (6.0 * s[8]) * h[12] * xz
        - s[7] * h[13] * (ring - 2.0 * xx)
        + (2.0 * s[9]) * h[14] * xz
        - (3.0 * s[5]) * h[15] * diff
    )
    g_y = (
        -s[1] * h[1]
        + s[2] * (h[4] * x - h[5] * z)
        - (2.0 * s[3]) * h[6] * y
        - (2.0 * s[4]) * h[8] * y
        - (3.0 * s[5]) * h[9] * diff
        + s[6] * h[10] * xz
        - s[7] * h[11] * (ring - 2.0 * yy)
        - (6.0 * s[8]) * h[12] * yz
        + (2.0 * s[7]) * h[13] * xy
        - (2.0 * s[9]) * h[14] * yz
        + (6.0 * s[5]) * h[15] * xy
    )
    g_z = (
        s[1] * h[2]
        - s[2] * (h[5] * y + h[7] * x)
        + (4.0 * s[3]) * h[6] * z
        + s[6] * h[10] * xy
        - (8.0 * s[7]) * (h[11] * yz + h[13] * xz)
        + s[8] * h[12] * (6.0 * zz - 3.0 * xx - 3.0 * yy)
        + s[9] * h[14] * diff
    )
    return g_x, g_y, g_z


def project_parts(feat, cam):
    rot = [[cam[3 * r + c] for c in range(3)] for r in range(3)]
    off = [feat(a) - cam[9 + a] for a in range(3)]
    in_cam = [rot[r][0] * off[0] + rot[r][1] * off[1] + rot[r][2] * off[2] for r in range(3)]
    inv = 1.0 / in_cam[2]
    u = in_cam[0] * inv
    v = in_cam[1] * inv
    finv = focal_length * inv
    scale = [jnp.exp(2.0 * feat(3 + a)) for a in range(3)]
    quat = [feat(6 + a) for a in range(4)]
    rnorm = lax.rsqrt(quat[0] * quat[0] + quat[1] * quat[1] + quat[2] * quat[2] + quat[3] * quat[3])
    w, x, y, z = [q * rnorm for q in quat]
    turn = [
        [1.0 - 2.0 * (y * y + z * z), 2.0 * (x * y - w * z), 2.0 * (x * z + w * y)],
        [2.0 * (x * y + w * z), 1.0 - 2.0 * (x * x + z * z), 2.0 * (y * z - w * x)],
        [2.0 * (x * z - w * y), 2.0 * (y * z + w * x), 1.0 - 2.0 * (x * x + y * y)],
    ]
    screen = [
        [finv * (rot[0][c] - u * rot[2][c]) for c in range(3)],
        [finv * (rot[1][c] - v * rot[2][c]) for c in range(3)],
    ]
    axes = [
        [sum(screen[r][c] * turn[c][k] for c in range(3)) for k in range(3)] for r in range(2)
    ]
    wide = [[axes[r][k] * scale[k] for k in range(3)] for r in range(2)]
    cov_xx = sum(wide[0][k] * axes[0][k] for k in range(3)) + dilation
    cov_xy = sum(wide[0][k] * axes[1][k] for k in range(3))
    cov_yy = sum(wide[1][k] * axes[1][k] for k in range(3)) + dilation
    rdet = 1.0 / (cov_xx * cov_yy - cov_xy * cov_xy)
    conic = (cov_yy * rdet, -cov_xy * rdet, cov_xx * rdet)
    rlen = lax.rsqrt(off[0] * off[0] + off[1] * off[1] + off[2] * off[2])
    way = [off[a] * rlen for a in range(3)]
    return dict(
        rot=rot, inv=inv, u=u, v=v, finv=finv, scale=scale, rnorm=rnorm, rotor=(w, x, y, z), turn=turn,
        screen=screen, axes=axes, wide=wide, conic=conic, rlen=rlen, way=way,
    )


def project_rows(feat, cam):
    part = project_parts(feat, cam)
    basis = sh_basis(*part["way"])
    colours = []
    for k in range(3):
        total = 0.5 + sh_const[0] * feat(11 + 16 * k)
        for b in range(1, 16):
            total = total + feat(11 + 16 * k + b) * basis[b]
        colours.append(total)
    mean_x = focal_length * part["u"] + center_x
    mean_y = focal_length * part["v"] + center_y
    logit = feat(10)
    log_opacity = jnp.minimum(logit, 0.0) - jnp.log(1.0 + jnp.exp(-jnp.abs(logit)))
    return [mean_x, mean_y, *part["conic"], log_opacity, *colours]


def project_pull(feat, cam, grads, put):
    part = project_parts(feat, cam)
    g_mx, g_my, g_a, g_b, g_c, g_o = grads[:6]
    g_col = grads[6:9]
    way, rlen = part["way"], part["rlen"]
    basis = sh_basis(*way)
    pulled = [None]
    for k in range(3):
        put(11 + 16 * k, sh_const[0] * g_col[k])
    for b in range(1, 16):
        total = 0.0
        for k in range(3):
            put(11 + 16 * k + b, g_col[k] * basis[b])
            total = total + g_col[k] * feat(11 + 16 * k + b)
        pulled.append(total)
    g_way = sh_pull(pulled, *way)
    along = way[0] * g_way[0] + way[1] * g_way[1] + way[2] * g_way[2]
    g_off = [(g_way[a] - way[a] * along) * rlen for a in range(3)]
    put(10, g_o / (1.0 + jnp.exp(feat(10))))
    a, b, c = part["conic"]
    g_xx = -(a * a * g_a + a * b * g_b + b * b * g_c)
    g_xy = -(2.0 * a * b * g_a + (a * c + b * b) * g_b + 2.0 * b * c * g_c)
    g_yy = -(b * b * g_a + b * c * g_b + c * c * g_c)
    axes, wide, turn, screen = part["axes"], part["wide"], part["turn"], part["screen"]
    for k in range(3):
        g_scale = (
            g_xx * axes[0][k] * wide[0][k]
            + g_xy * axes[0][k] * wide[1][k]
            + g_yy * axes[1][k] * wide[1][k]
        )
        put(3 + k, 2.0 * g_scale)
    g_axes = [
        [2.0 * g_xx * wide[0][k] + g_xy * wide[1][k] for k in range(3)],
        [2.0 * g_yy * wide[1][k] + g_xy * wide[0][k] for k in range(3)],
    ]
    g_screen = [
        [sum(g_axes[r][k] * turn[c][k] for k in range(3)) for c in range(3)] for r in range(2)
    ]
    gm = [
        [g_axes[0][k] * screen[0][c] + g_axes[1][k] * screen[1][c] for k in range(3)]
        for c in range(3)
    ]
    w, x, y, z = part["rotor"]
    up_xy, up_xz, up_yz = gm[0][1] + gm[1][0], gm[0][2] + gm[2][0], gm[1][2] + gm[2][1]
    un_xy, un_xz, un_yz = gm[1][0] - gm[0][1], gm[0][2] - gm[2][0], gm[2][1] - gm[1][2]
    g_rotor = [
        2.0 * (z * un_xy + y * un_xz + x * un_yz),
        2.0 * (y * up_xy + z * up_xz + w * un_yz - 2.0 * x * (gm[1][1] + gm[2][2])),
        2.0 * (x * up_xy + z * up_yz + w * un_xz - 2.0 * y * (gm[0][0] + gm[2][2])),
        2.0 * (x * up_xz + y * up_yz + w * un_xy - 2.0 * z * (gm[0][0] + gm[1][1])),
    ]
    rotor = (w, x, y, z)
    along = sum(rotor[i] * g_rotor[i] for i in range(4))
    for i in range(4):
        put(6 + i, (g_rotor[i] - rotor[i] * along) * part["rnorm"])
    rot, inv, finv, u, v = part["rot"], part["inv"], part["finv"], part["u"], part["v"]
    g_u = focal_length * g_mx - finv * sum(g_screen[0][c] * rot[2][c] for c in range(3))
    g_v = focal_length * g_my - finv * sum(g_screen[1][c] * rot[2][c] for c in range(3))
    g_f = sum(g_screen[r][c] * screen[r][c] for r in range(2) for c in range(3))
    g_in = [g_u * inv, g_v * inv, -(g_f + g_u * u + g_v * v) * inv]
    for axis in range(3):
        put(
            axis,
            g_off[axis] + rot[0][axis] * g_in[0] + rot[1][axis] * g_in[1] + rot[2][axis] * g_in[2],
        )


def split(value):
    high = value.astype(BF16)
    return high, (value - high.astype(F32)).astype(BF16)


def matmul(a, b, dims=((1,), (0,))):
    return lax.dot_general(a, b, (dims, ((), ())), preferred_element_type=F32)


def spread_features(parts, scratch, count):
    tiles = sum(part.shape[1] for part in parts) // LANES
    at = 0
    for part in parts:
        for first in range(0, part.shape[1], LANES):
            for row in range(0, count, 8):
                rows = min(8, count - row)
                scratch[pl.ds(row * tiles + at, rows, stride=tiles), :] = part[
                    row : row + rows, first : first + LANES
                ]
            at += 1
    return tiles


def pack_kernel(shards, pieces, where, *refs):
    sources, refs = refs[: 3 + (pieces > 0)], refs[3 + (pieces > 0) :]
    info, parts, refs = refs[0], refs[1 : 1 + pieces], refs[1 + pieces :]
    shard_of, local_of, goal, place_s, sems, cut_sems = refs
    group = where[0]
    loads = [
        pltpu.make_async_copy(source, held, sems.at[k])
        for k, (source, held) in enumerate(zip(sources, (shard_of, local_of, goal)))
    ]
    for d in range(pieces):
        chunk = parts[d].shape[1]
        first = pl.multiple_of((group ^ d) * chunk, LANES)
        loads.append(
            pltpu.make_async_copy(sources[3].at[:, pl.ds(first, chunk)], parts[d], cut_sems.at[d])
        )
    for load in loads:
        load.start()
    for load in loads[:3]:
        load.wait()
    width = info.shape[1]
    tile_count, listed = local_of.shape
    rows_each = (info.shape[0] - 4) // tile_count
    columns = rows_each * width
    chunk = columns // shards
    info[0:3, :] = goal[...]
    for t in range(tile_count):
        place = (shard_of[t] ^ group) * chunk + (local_of[t : t + 1, :] - group * chunk)
        info[3:4, t * listed : (t + 1) * listed] = place.astype(F32)
        row_i = lax.broadcasted_iota(jnp.int32, (LANES, LANES), 0)
        col_i = lax.broadcasted_iota(jnp.int32, (LANES, LANES), 1)
        for first in range(0, listed, LANES):
            spread = jnp.broadcast_to(place[:, first : first + LANES].astype(F32), (LANES, LANES))
            place_s[first : first + LANES, :] = jnp.broadcast_to(
                jnp.sum(jnp.where(row_i == col_i, spread, 0.0), axis=1, keepdims=True), (LANES, LANES)
            )
        lane_of = lax.broadcasted_iota(jnp.int32, (8, LANES), 1).astype(F32)
        row_of = lax.broadcasted_iota(jnp.int32, (8, LANES), 0).astype(F32)
        for s in range(columns // LANES):
            best = jnp.full((8, LANES), -1.0, F32)
            column = lane_of + float(s * LANES)
            for first in range(0, listed, 8):
                best = jnp.where(
                    place_s[first : first + 8, :] == column, row_of + float(first), best
                )
            best = jnp.max(best, axis=0, keepdims=True)
            row, at = 4 + t * rows_each + s * LANES // width, s * LANES % width
            info[row : row + 1, at : at + LANES] = best
    for load in loads[3:]:
        load.wait()


def pack(group, params, target, hit_shard, hit_local, shards, aligned):
    features, columns = params.shape
    tile_count, listed = hit_local.shape
    width = target.shape[1]
    rows = 4 + tile_count * (columns // width)
    pieces = shards if aligned else 0
    piece = jax.ShapeDtypeStruct((features, columns // shards), F32)
    args = (hit_shard.reshape(tile_count, 1, listed), hit_local, target) + (params,) * aligned
    out = call(
        functools.partial(pack_kernel, shards, pieces),
        "pack",
        (jax.ShapeDtypeStruct((rows, width), F32),) + (piece,) * pieces,
        [smem()] + [pl.BlockSpec(memory_space=pltpu.HBM)] * len(args),
        [
            pltpu.VMEM((tile_count, 1, listed), jnp.int32),
            pltpu.VMEM((tile_count, listed), jnp.int32),
            pltpu.VMEM(target.shape, F32),
            pltpu.VMEM((listed, LANES), F32),
            pltpu.SemaphoreType.DMA((3,)),
            pltpu.SemaphoreType.DMA((shards,)),
        ],
        (group.reshape(1),) + tuple(pltpu.with_memory_space_constraint(a, pltpu.HBM) for a in args),
    )
    return out[0], list(out[1:])


def pixel_basis(pixels):
    pixel = lax.broadcasted_iota(jnp.int32, (8, pixels), 1)
    row = lax.broadcasted_iota(jnp.int32, (8, pixels), 0)
    middle = 0.5 * TILE_SIDE - 0.5
    u = (pixel % TILE_SIDE).astype(F32) - middle
    v = (pixel // TILE_SIDE).astype(F32) - middle
    value = jnp.where(row == 0, 1.0, 0.0)
    for at, term in ((1, u), (2, v), (3, u * u), (4, u * v), (5, v * v)):
        value = jnp.where(row == at, term, value)
    return value


def composite(tiles, first_group, me, rows, info_s, rendered, work):
    alpha_s, weight_s, pull_s, push_s, weight_2, coef_s, colour_s, error_s, mix_s, index_s, acc_s = work
    groups, tile_count, _, listed = acc_s.shape
    pixels = info_s.shape[2] // tile_count
    parts = pixels // LANES
    halves = listed // LANES
    tiles_here = groups * tile_count
    spans = tiles_here * parts
    slabs = rows.shape[0] // ROWS
    side = TILE_SIDE
    first_col, first_row = tiles

    def of_span(span):
        return pl.ds(span * SPAN_STEP, listed, stride=LIST_STEP)

    def of_place(place):
        return pl.ds(place * LIST_STEP, spans, stride=SPAN_STEP)

    def lane_gather(source, lane):
        return jnp.take_along_axis(source, lane, axis=1, mode="promise_in_bounds")

    basis = pixel_basis(pixels)
    basis_3 = jnp.concatenate([basis, basis, basis], axis=0).astype(BF16)

    entries = []
    for n in range(tiles_here):
        g, t = n // tile_count, n % tile_count
        found = []
        for h in range(halves):
            first = t * listed + h * LANES
            at = info_s[g, 3:4, first : first + LANES].astype(jnp.int32)
            index_s[n * halves + h : n * halves + h + 1, :] = at
            at = jnp.broadcast_to(at, (8, LANES))
            lane, slab = at & (LANES - 1), at >> 7
            value = lane_gather(rows[0:8, :], lane)
            for s in range(1, slabs):
                value = jnp.where(
                    slab == s, lane_gather(rows[s * ROWS : s * ROWS + 8, :], lane), value
                )
            found.append(value)
        entries.append(jnp.concatenate(found, axis=1))
    at = index_s[...]
    lane, slab = at & (LANES - 1), at >> 7
    ninth = lane_gather(rows[8:16, :], lane)
    for s in range(1, slabs):
        ninth = jnp.where(
            slab == s, lane_gather(rows[s * ROWS + 8 : s * ROWS + 16, :], lane), ninth
        )

    means = []
    colour_s[...] = jnp.zeros(colour_s.shape, F32)
    for n in range(tiles_here):
        g, t = n // tile_count, n % tile_count
        entry = entries[n]
        slot = (me ^ (first_group + g)) * tile_count + t
        mean_u = entry[0:1] - (((first_col + slot % 4) * side).astype(F32) + 0.5 * side)
        mean_v = entry[1:2] - (((first_row + slot // 4) * side).astype(F32) + 0.5 * side)
        quad_a, quad_b, quad_c = -0.5 * entry[2:3], -entry[3:4], -0.5 * entry[4:5]
        means.append((mean_u, mean_v, quad_a, quad_b, quad_c))
        slope_u = 2.0 * quad_a * mean_u + quad_b * mean_v
        slope_v = 2.0 * quad_c * mean_v + quad_b * mean_u
        level = 0.5 * (slope_u * mean_u + slope_v * mean_v) + entry[5:6]
        zero = jnp.zeros_like(level)
        coef = jnp.concatenate(
            [level, -slope_u, -slope_v, quad_a, quad_b, quad_c, zero, zero], axis=0
        )
        here = slice(n * listed, (n + 1) * listed)
        for part in range(3):
            term = coef.astype(BF16).astype(F32)
            coef_s[part * 8 : part * 8 + 8, here] = term
            coef = coef - term
        last = [ninth[n * halves + h : n * halves + h + 1] for h in range(halves)]
        colours = jnp.concatenate([entry[6:8], jnp.concatenate(last, axis=1)], axis=0)
        high = colours.astype(BF16).astype(F32)
        colour_s[n * ROWS : n * ROWS + 3, here] = high
        colour_s[n * ROWS + 3 : n * ROWS + 6, here] = colours - high
        colour_s[n * ROWS + 6 : n * ROWS + 9, here] = high

    down = ((0,), (0,))
    power = matmul(coef_s[...].astype(BF16), basis_3, down)
    for n in range(tiles_here):
        for part in range(parts):
            alpha_s[of_span(n * parts + part), :] = jnp.exp(
                power[n * listed : (n + 1) * listed, part * LANES : (part + 1) * LANES]
            )

    unroll, quad = 32, 4
    steps = listed // unroll

    def forward(step, passed):
        for j in range(0, unroll, quad):
            at = [of_place(step * unroll + j + i) for i in range(quad)]
            alpha = [alpha_s[at[i], :] for i in range(quad)]
            keep = [1.0 - alpha[i] for i in range(quad)]
            two = keep[0] * keep[1]
            three = two * keep[2]
            weight_s[at[0], :] = alpha[0] * passed
            weight_s[at[1], :] = (alpha[1] * keep[0]) * passed
            weight_s[at[2], :] = (alpha[2] * two) * passed
            weight_s[at[3], :] = (alpha[3] * three) * passed
            passed = passed * (two * (keep[2] * keep[3]))
        return passed

    nought = jnp.zeros((spans, LANES), F32)
    lax.fori_loop(0, steps, forward, nought + 1.0)

    error_s[...] = jnp.zeros(error_s.shape, F32)
    mix_s[...] = jnp.zeros(mix_s.shape, F32)
    for n in range(tiles_here):
        g, t = n // tile_count, n % tile_count
        for part in range(parts):
            at = slice((n * parts + part) * LANES, (n * parts + part + 1) * LANES)
            weight_2[:listed, at], weight_2[listed:, at] = split(
                weight_s[of_span(n * parts + part), :]
            )
        at = slice(n * pixels, (n + 1) * pixels)
        colours = colour_s[n * ROWS : (n + 1) * ROWS, n * listed : (n + 1) * listed].astype(BF16)
        image = matmul(colours, weight_2[:listed, at])
        image = image[0:3] + image[3:6] + matmul(colours, weight_2[listed:, at])[0:3]
        here = slice(t * pixels, (t + 1) * pixels)
        if rendered is not None and g == 0:
            rendered[:, here] = image
        error = image - info_s[g, 0:3, here]
        high = error.astype(BF16).astype(F32)
        low = error - high
        error_s[n * ROWS : n * ROWS + 3, :] = high
        error_s[n * ROWS + 3 : n * ROWS + 6, :] = high
        error_s[n * ROWS + 6 : n * ROWS + 9, :] = low
        mix_s[0, n * ROWS : n * ROWS + 8, at] = basis
        mix_s[1, n * ROWS + 6 : n * ROWS + 9, at] = high
        mix_s[1, n * ROWS + 9 : n * ROWS + 12, at] = low
    pull = matmul(colour_s[...].astype(BF16), error_s[...].astype(BF16), down)
    for n in range(tiles_here):
        for part in range(parts):
            pull_s[of_span(n * parts + part), :] = pull[
                n * listed : (n + 1) * listed, part * LANES : (part + 1) * LANES
            ]

    def backward(back, behind):
        for j in range(0, unroll, quad):
            at = [of_place(listed - 1 - (back * unroll + j + i)) for i in range(quad)]
            alpha = [alpha_s[at[i], :] for i in range(quad)]
            pull = [pull_s[at[i], :] for i in range(quad)]
            keep = [1.0 - alpha[i] for i in range(quad)]
            own = alpha[0] * pull[0]
            seen, through = behind, keep[0]
            for i in range(quad):
                push_s[at[i], :] = weight_s[at[i], :] * (pull[i] - seen)
                if i > 0:
                    own = own * keep[i] + alpha[i] * pull[i]
                    through = through * keep[i]
                seen = behind * through + own
            behind = seen
        return behind

    lax.fori_loop(0, steps, backward, nought)

    across = ((1,), (1,))
    high, low = split(jnp.concatenate([push_s[of_span(span), :] for span in range(spans)], axis=1))
    sums = matmul(jnp.concatenate([high, low], axis=0), mix_s[0].astype(BF16), across)
    sums = sums + matmul(weight_2[...], mix_s[1].astype(BF16), across)
    sums = (sums[:listed] + sums[listed:]).T
    for n in range(tiles_here):
        g, t = n // tile_count, n % tile_count
        mean_u, mean_v, quad_a, quad_b, quad_c = means[n]
        m_00, m_10, m_01, m_20, m_11, m_02 = [
            sums[n * ROWS + m : n * ROWS + m + 1] for m in range(6)
        ]
        n_10 = m_10 - mean_u * m_00
        n_01 = m_01 - mean_v * m_00
        acc_s[g, t, 0:1, :] = -(2.0 * quad_a * n_10 + quad_b * n_01)
        acc_s[g, t, 1:2, :] = -(2.0 * quad_c * n_01 + quad_b * n_10)
        acc_s[g, t, 2:3, :] = -0.5 * (m_20 - mean_u * (m_10 + n_10))
        acc_s[g, t, 3:4, :] = -(m_11 - mean_u * m_01 - mean_v * n_10)
        acc_s[g, t, 4:5, :] = -0.5 * (m_02 - mean_v * (m_01 + n_01))
        acc_s[g, t, 5:6, :] = m_00
        at = n * ROWS + 6
        grads = sums[at : at + 3] + sums[at + 3 : at + 6]
        acc_s[g, t, 6:8, :] = grads[0:2]
        for h in range(halves):
            row = n * halves + h
            acc_s[0, 0, 8 + row : 9 + row, :LANES] = grads[2:3, h * LANES : (h + 1) * LANES]


def pool_sum(slab, info_s, acc_s):
    groups, tile_count, _, listed = acc_s.shape
    halves = listed // LANES
    width = info_s.shape[2]
    rows_each = (info_s.shape[1] - 4) // tile_count
    row_of = lax.broadcasted_iota(jnp.int32, (8, LANES), 0)

    def lane_gather(source, lane):
        return jnp.take_along_axis(source, lane, axis=1, mode="promise_in_bounds")

    totals, every = [], None
    for g in range(groups):
        total = jnp.zeros((8, LANES), F32)
        for t in range(tile_count):
            row, first = 4 + t * rows_each + slab * LANES // width, slab * LANES % width
            at = info_s[g, row : row + 1, first : first + LANES].astype(jnp.int32)
            at = jnp.broadcast_to(at, (8, LANES))
            n = g * tile_count + t
            every = at if every is None else jnp.where(row_of >= n * halves, at, every)
            lane, half = at & (LANES - 1), at >> 7
            for h in range(halves):
                here = lane_gather(acc_s[g, t, 0:8, h * LANES : (h + 1) * LANES], lane)
                total = total + jnp.where(half == h, here, 0.0)
        totals.append(total)
    here = lane_gather(acc_s[0, 0, 8:16, :LANES], every & (LANES - 1))
    ninth = jnp.where(every >> 7 == row_of % halves, here, 0.0)
    return totals[0] + totals[1], jnp.sum(ninth, axis=0, keepdims=True)


def block_start(tile_id):
    within = tile_id % (TILES_X * TILES_Y)
    return (within % TILES_X) // 4 * 4, (within // TILES_X) // 2 * 2


def near_kernel(pieces, tile_ids, cams, where, own, other, *refs):
    parts = refs[:pieces]
    rendered, rows, partial, feats, info_s, *work = refs[pieces:]
    view = tile_ids[0] // (TILES_X * TILES_Y)
    cam = [cams[view, i] for i in range(12)]
    slabs = spread_features(parts, feats, parts[0].shape[0])
    projected = project_rows(lambda f: feats[f * slabs : (f + 1) * slabs, :], cam)
    for f, value in enumerate(projected):
        rows[pl.ds(f, slabs, stride=ROWS), :] = value
    for f in range(len(projected), ROWS):
        rows[pl.ds(f, slabs, stride=ROWS), :] = projected[8]
    info_s[0] = own[...]
    info_s[1] = other[...]
    composite(block_start(tile_ids[0]), 0, where[0], rows, info_s, rendered, work)
    for s in range(slabs):
        at = slice(s * LANES, (s + 1) * LANES)
        partial[0:8, at], partial[8:9, at] = pool_sum(s, info_s, work[-1])


def far_kernel(blocks, tile_ids, where, rows, partial, infos, *refs):
    *packets, info_s = refs[: len(refs) - 11]
    work = refs[len(refs) - 11 :]
    half = infos.shape[0] // 2
    info_s[0] = infos[:half, :]
    info_s[1] = infos[half:, :]
    composite(block_start(tile_ids[0]), 2, where[0], rows, info_s, None, work)
    share = (tile_ids[0] // (TILES_X * TILES_Y)).astype(F32)
    row_of = lax.broadcasted_iota(jnp.int32, (8, LANES), 0)
    lane_of = lax.broadcasted_iota(jnp.int32, (8, LANES), 1)
    chunk = packets[0].shape[1]
    for s in range(rows.shape[0] // ROWS):
        total, ninth = pool_sum(s, info_s, work[-1])
        total = total + partial[0:8, s * LANES : (s + 1) * LANES]
        ninth = ninth + partial[8:9, s * LANES : (s + 1) * LANES]
        if blocks == 1:
            mine = share
        else:
            column = s * LANES + lane_of
            mine = jnp.where(column % where[2] // (where[2] // blocks) == where[1], share, 0.0)
        at = slice(s * LANES % chunk, s * LANES % chunk + LANES)
        packets[s * LANES // chunk][0:8, at] = total
        packets[s * LANES // chunk][8:16, at] = jnp.where(
            row_of == 0, jnp.broadcast_to(ninth, (8, LANES)), mine
        )


def join_kernel(first, second, out):
    half = first.shape[0]
    out[:half, :] = first[...]
    out[half:, :] = second[...]


def update_kernel(pieces, follows, where, cams, params, adam_m, adam_v, *refs):
    packets, refs = refs[:pieces], refs[pieces + 3 * follows :]
    sinks, (feats, rows, grads, made, sems) = refs[:3], refs[3:]
    features = params.shape[0]
    chunk = packets[0].shape[1]
    width = pieces * chunk
    slabs = width // LANES
    start = (where[0] ^ where[1]) // pieces * pieces * chunk
    for d in range(pieces):
        for h in range(chunk // LANES):
            slab = (where[0] ^ where[1] ^ d) % pieces * (chunk // LANES) + h
            rows[pl.ds(slab, ROWS, stride=slabs), :] = packets[d][:, h * LANES : (h + 1) * LANES]
    pulled = [rows[f * slabs : (f + 1) * slabs, :] for f in range(10)]
    view = pulled[9]
    cam = []
    for i in range(12):
        value = jnp.full((slabs, LANES), cams[0, i], F32)
        for v in range(1, cams.shape[0]):
            value = jnp.where(view == float(v), cams[v, i], value)
        cam.append(value)

    def put(f, value):
        grads[f * slabs : (f + 1) * slabs, :] = value

    def column(s):
        return pl.ds(pl.multiple_of(start + s * LANES, LANES), LANES)

    for s in range(slabs):
        for row in range(0, features, 8):
            count = min(8, features - row)
            feats[pl.ds(row * slabs + s, count, stride=slabs), :] = params[
                row : row + count, column(s)
            ]
    project_pull(lambda f: feats[f * slabs : (f + 1) * slabs, :], cam, pulled[:9], put)
    rate = learn_rate / (1.0 - beta_one**adam_steps)
    unbias = 1.0 / (1.0 - beta_two**adam_steps)
    stores = []
    for row in range(0, features, 8):
        count = min(8, features - row)
        span = slice(row, row + count)
        for s in range(slabs):
            here = (span, slice(s * LANES, (s + 1) * LANES))
            grad = grads[pl.ds(row * slabs + s, count, stride=slabs), :]
            moment = beta_one * adam_m[span, column(s)] + (1.0 - beta_one) * grad
            second = beta_two * adam_v[span, column(s)] + (1.0 - beta_two) * grad * grad
            made.at[1][here] = moment
            made.at[2][here] = second
            made.at[0][here] = params[span, column(s)] - rate * moment / (
                jnp.sqrt(second * unbias) + adam_eps
            )
        if row % 16 == 8 or row + count == features:
            first = row // 16 * 16
            span = pl.ds(first, row + count - first)
            columns = pl.ds(pl.multiple_of(start, LANES), width)
            for k in range(3):
                store = pltpu.make_async_copy(
                    made.at[k, span], sinks[k].at[span, columns], sems.at[k, first // 16]
                )
                store.start()
                stores.append(store)
    for store in stores:
        store.wait()


def vmem():
    return pl.BlockSpec(memory_space=pltpu.VMEM)


def smem():
    return pl.BlockSpec(memory_space=pltpu.SMEM)


def any_space():
    return pl.BlockSpec(memory_space=pl.ANY)


def call(kernel, name, out_shape, in_specs, scratch, args, out_specs=None, grant=32):
    return pl.pallas_call(
        kernel,
        out_shape=out_shape,
        in_specs=in_specs,
        out_specs=out_specs or tuple(vmem() for _ in out_shape),
        scratch_shapes=scratch,
        compiler_params=pltpu.CompilerParams(vmem_limit_bytes=grant * 1024 * 1024),
        name=name,
    )(*args)


def work_shapes(tile_count, pixels, listed):
    tiles = 2 * tile_count
    spans = tiles * pixels // LANES
    assert (spans - 1) * SPAN_STEP < LIST_STEP and tiles * listed // LANES == 8
    return [pltpu.VMEM((listed * LIST_STEP, LANES), F32)] * 4 + [
        pltpu.VMEM((2 * listed, spans * LANES), BF16),
        pltpu.VMEM((24, tiles * listed), F32),
        pltpu.VMEM((tiles * ROWS, tiles * listed), F32),
        pltpu.VMEM((tiles * ROWS, pixels), F32),
        pltpu.VMEM((2, LANES, spans * LANES), F32),
        pltpu.VMEM((8, LANES), jnp.int32),
        pltpu.VMEM((2, tile_count, ROWS, listed), F32),
    ]


def near(tile_ids, cameras, where, own, other, parts, tile_count):
    width = sum(part.shape[1] for part in parts)
    features = parts[0].shape[0]
    slabs = width // LANES
    pixels = listed = own.shape[1] // tile_count
    return call(
        functools.partial(near_kernel, len(parts)),
        "near",
        (
            jax.ShapeDtypeStruct((3, own.shape[1]), F32),
            jax.ShapeDtypeStruct((ROWS * slabs, LANES), F32),
            jax.ShapeDtypeStruct((ROWS, width), F32),
        ),
        [smem()] * 3 + [vmem()] * (2 + len(parts)),
        [pltpu.VMEM((features * slabs, LANES), F32), pltpu.VMEM((2,) + own.shape, F32)]
        + work_shapes(tile_count, pixels, listed),
        (tile_ids, cameras, where, own, other, *parts),
    )


def far(tile_ids, where, rows, partial, infos, pieces, tile_count, blocks):
    width = partial.shape[1]
    pixels = listed = infos.shape[1] // tile_count
    info = (infos.shape[0] // 2, infos.shape[1])
    return call(
        functools.partial(far_kernel, blocks),
        "far",
        (jax.ShapeDtypeStruct((ROWS, width // pieces), F32),) * pieces,
        [smem()] * 2 + [vmem()] * 3,
        [pltpu.VMEM((2,) + info, F32)] + work_shapes(tile_count, pixels, listed),
        (tile_ids, where, rows, partial, infos),
    )


def join(first, second):
    shape = (2 * first.shape[0], first.shape[1])
    return call(
        join_kernel, "join", (jax.ShapeDtypeStruct(shape, F32),), [vmem()] * 2, [], (first, second)
    )[0]


def update(own, first, cameras, params, adam_m, adam_v, packets, before):
    features = params.shape[0]
    width = sum(packet.shape[1] for packet in packets)
    slabs = width // LANES
    shape = jax.ShapeDtypeStruct(params.shape, F32)
    at = 5 + len(packets)
    return pl.pallas_call(
        functools.partial(update_kernel, len(packets), len(before) > 0),
        out_shape=(shape, shape, shape),
        in_specs=[smem()] * 2
        + [vmem()] * (3 + len(packets))
        + [any_space()] * len(before),
        out_specs=(any_space(),) * 3,
        scratch_shapes=[
            pltpu.VMEM((features * slabs, LANES), F32),
            pltpu.VMEM((ROWS * slabs, LANES), F32),
            pltpu.VMEM((features * slabs, LANES), F32),
            pltpu.VMEM((3, features, width), F32),
            pltpu.SemaphoreType.DMA((3, (features + 15) // 16)),
        ],
        input_output_aliases={at + k: k for k in range(len(before))},
        compiler_params=pltpu.CompilerParams(vmem_limit_bytes=32 * 1024 * 1024),
        name="update",
    )(
        jnp.stack([own, jnp.int32(first)]).astype(jnp.int32),
        cameras, params, adam_m, adam_v, *packets, *before,
    )


def swap(value, axis, d):
    if d == 0:
        return value
    return lax.ppermute(value, axis, [(k, k ^ d) for k in range(lax.axis_size(axis))])


def local(params, adam_m, adam_v, cameras, target, tile_ids, hit_shard, hit_local):
    width = params.shape[1]
    tile_count, listed = hit_local.shape
    shards = lax.axis_size("gs")
    along = lax.axis_size("tile")
    chunk = width // shards
    group = lax.axis_index("gs")
    seat = lax.axis_index("tile")
    aligned = chunk % LANES == 0
    team = BLOCK_TILES // tile_count
    assert team == 4
    blocks = along // team

    info, parts = pack(group, params, target, hit_shard, hit_local, shards, aligned)
    if not aligned:
        parts = [
            lax.dynamic_slice_in_dim(params, (group ^ d) * chunk, chunk, axis=1)
            for d in range(shards)
        ]
    parts = [swap(parts[d], "gs", d) for d in range(shards)]
    beside = swap(info, "tile", 1)
    beyond = swap(join(info, beside), "tile", 2)
    if not aligned:
        parts = [jnp.concatenate(parts, axis=1)]
    where = jnp.stack([seat % team, seat // team, jnp.int32(chunk)]).astype(jnp.int32)
    rendered, rows, partial = near(tile_ids, cameras, where, info, beside, parts, tile_count)
    packets = far(tile_ids, where, rows, partial, beyond, len(parts), tile_count, blocks)
    if not aligned:
        packets = [packets[0][:, d * chunk : (d + 1) * chunk] for d in range(shards)]
    packets = [swap(packets[d], "gs", d) for d in range(shards)]
    if blocks > 1:
        packets = [block_sum(packet, along, team) for packet in packets]
    if aligned:
        own = group
    else:
        packets = [jnp.stack(packets)[jnp.arange(shards) ^ group].transpose(1, 0, 2).reshape(ROWS, -1)]
        own = jnp.int32(0)
    made = ()
    count = max(1, len(packets) // 2)
    for first in range(0, len(packets), count):
        made = update(
            own, first, cameras, params, adam_m, adam_v, packets[first : first + count], made
        )
    new_params, new_m, new_v = made
    return (rendered, new_params, new_m, new_v)


def block_sum(packet, along, team):
    step = team
    while step < along:
        packet = packet + swap(packet, "tile", step)
        step *= 2
    return packet


def solution(mesh):
    return jax.shard_map(
        local,
        mesh=mesh,
        in_specs=(
            P(None, ("groups", "gs")),
            P(None, ("groups", "gs")),
            P(None, ("groups", "gs")),
            P("groups", None),
            P(None, ("groups", "gs", "tile")),
            P(("groups", "gs", "tile")),
            P(("groups", "gs", "tile"), None, None),
            P(("groups", "gs", "tile"), None),
        ),
        out_specs=(
            P(None, ("groups", "gs", "tile")),
            P(None, ("groups", "gs")),
            P(None, ("groups", "gs")),
            P(None, ("groups", "gs")),
        ),
        check_vma=False,
    )
```

```python
import functools

import jax
import jax.numpy as jnp
from jax import lax
from jax.experimental import pallas as pl
from jax.experimental.pallas import tpu as pltpu
from jax.sharding import PartitionSpec as P

TILES_X = 120
TILES_Y = 68
TILE_SIDE = 16
BLOCK_TILES = 8
LANES = 128
ROWS = 16
SPAN_STEP, LIST_STEP = 3, 25
F32 = jnp.float32
BF16 = jnp.bfloat16

focal_length = 1000.0
center_x = 960.0
center_y = 540.0
dilation = 0.3
beta_one = 0.9
beta_two = 0.999
learn_rate = 0.01
adam_eps = 1e-08
adam_steps = 100.0
sh_const = (
    0.28209479177387814,
    0.4886025119029199,
    1.0925484305920792,
    0.31539156525252005,
    0.5462742152960396,
    0.5900435899266435,
    2.890611442640554,
    0.4570457994644658,
    0.3731763325901154,
    1.445305721320277,
)


def sh_basis(x, y, z):
    s = sh_const
    xx, yy, zz = x * x, y * y, z * z
    return [
        None,
        -s[1] * y,
        s[1] * z,
        -s[1] * x,
        s[2] * (x * y),
        -s[2] * (y * z),
        s[3] * (2.0 * zz - xx - yy),
        -s[2] * (x * z),
        s[4] * (xx - yy),
        -s[5] * y * (3.0 * xx - yy),
        s[6] * (x * y) * z,
        -s[7] * y * (4.0 * zz - xx - yy),
        s[8] * z * (2.0 * zz - 3.0 * xx - 3.0 * yy),
        -s[7] * x * (4.0 * zz - xx - yy),
        s[9] * z * (xx - yy),
        -s[5] * x * (xx - 3.0 * yy),
    ]


def sh_pull(h, x, y, z):
    s = sh_const
    xx, yy, zz = x * x, y * y, z * z
    xy, xz, yz = x * y, x * z, y * z
    diff = xx - yy
    ring = 4.0 * zz - xx - yy
    g_x = (
        -s[1] * h[3]
        + s[2] * (h[4] * y - h[7] * z)
        - (2.0 * s[3]) * h[6] * x
        + (2.0 * s[4]) * h[8] * x
        - (6.0 * s[5]) * h[9] * xy
        + s[6] * h[10] * yz
        + (2.0 * s[7]) * h[11] * xy
        - (6.0 * s[8]) * h[12] * xz
        - s[7] * h[13] * (ring - 2.0 * xx)
        + (2.0 * s[9]) * h[14] * xz
        - (3.0 * s[5]) * h[15] * diff
    )
    g_y = (
        -s[1] * h[1]
        + s[2] * (h[4] * x - h[5] * z)
        - (2.0 * s[3]) * h[6] * y
        - (2.0 * s[4]) * h[8] * y
        - (3.0 * s[5]) * h[9] * diff
        + s[6] * h[10] * xz
        - s[7] * h[11] * (ring - 2.0 * yy)
        - (6.0 * s[8]) * h[12] * yz
        + (2.0 * s[7]) * h[13] * xy
        - (2.0 * s[9]) * h[14] * yz
        + (6.0 * s[5]) * h[15] * xy
    )
    g_z = (
        s[1] * h[2]
        - s[2] * (h[5] * y + h[7] * x)
        + (4.0 * s[3]) * h[6] * z
        + s[6] * h[10] * xy
        - (8.0 * s[7]) * (h[11] * yz + h[13] * xz)
        + s[8] * h[12] * (6.0 * zz - 3.0 * xx - 3.0 * yy)
        + s[9] * h[14] * diff
    )
    return g_x, g_y, g_z


def project_parts(feat, cam):
    rot = [[cam[3 * r + c] for c in range(3)] for r in range(3)]
    off = [feat(a) - cam[9 + a] for a in range(3)]
    in_cam = [rot[r][0] * off[0] + rot[r][1] * off[1] + rot[r][2] * off[2] for r in range(3)]
    inv = 1.0 / in_cam[2]
    u = in_cam[0] * inv
    v = in_cam[1] * inv
    finv = focal_length * inv
    scale = [jnp.exp(2.0 * feat(3 + a)) for a in range(3)]
    quat = [feat(6 + a) for a in range(4)]
    rnorm = lax.rsqrt(quat[0] * quat[0] + quat[1] * quat[1] + quat[2] * quat[2] + quat[3] * quat[3])
    w, x, y, z = [q * rnorm for q in quat]
    turn = [
        [1.0 - 2.0 * (y * y + z * z), 2.0 * (x * y - w * z), 2.0 * (x * z + w * y)],
        [2.0 * (x * y + w * z), 1.0 - 2.0 * (x * x + z * z), 2.0 * (y * z - w * x)],
        [2.0 * (x * z - w * y), 2.0 * (y * z + w * x), 1.0 - 2.0 * (x * x + y * y)],
    ]
    screen = [
        [finv * (rot[0][c] - u * rot[2][c]) for c in range(3)],
        [finv * (rot[1][c] - v * rot[2][c]) for c in range(3)],
    ]
    axes = [
        [sum(screen[r][c] * turn[c][k] for c in range(3)) for k in range(3)] for r in range(2)
    ]
    wide = [[axes[r][k] * scale[k] for k in range(3)] for r in range(2)]
    cov_xx = sum(wide[0][k] * axes[0][k] for k in range(3)) + dilation
    cov_xy = sum(wide[0][k] * axes[1][k] for k in range(3))
    cov_yy = sum(wide[1][k] * axes[1][k] for k in range(3)) + dilation
    rdet = 1.0 / (cov_xx * cov_yy - cov_xy * cov_xy)
    conic = (cov_yy * rdet, -cov_xy * rdet, cov_xx * rdet)
    rlen = lax.rsqrt(off[0] * off[0] + off[1] * off[1] + off[2] * off[2])
    way = [off[a] * rlen for a in range(3)]
    return dict(
        rot=rot, inv=inv, u=u, v=v, finv=finv, scale=scale, rnorm=rnorm, rotor=(w, x, y, z), turn=turn,
        screen=screen, axes=axes, wide=wide, conic=conic, rlen=rlen, way=way,
    )


def shade(feat, cam):
    off = [feat(a) - cam[9 + a] for a in range(3)]
    rlen = lax.rsqrt(off[0] * off[0] + off[1] * off[1] + off[2] * off[2])
    basis = sh_basis(*[off[a] * rlen for a in range(3)])
    colours = []
    for k in range(3):
        total = 0.5 + sh_const[0] * feat(11 + 16 * k)
        for b in range(1, 16):
            total = total + feat(11 + 16 * k + b) * basis[b]
        colours.append(total)
    return colours


def project_rows(feat, cam):
    part = project_parts(feat, cam)
    mean_x = focal_length * part["u"] + center_x
    mean_y = focal_length * part["v"] + center_y
    logit = feat(10)
    log_opacity = jnp.minimum(logit, 0.0) - jnp.log(1.0 + jnp.exp(-jnp.abs(logit)))
    return [mean_x, mean_y, *part["conic"], log_opacity]


def project_pull(feat, cam, grads, put):
    part = project_parts(feat, cam)
    g_mx, g_my, g_a, g_b, g_c, g_o = grads[:6]
    g_col = grads[6:9]
    way, rlen = part["way"], part["rlen"]
    basis = sh_basis(*way)
    pulled = [None]
    for k in range(3):
        put(11 + 16 * k, sh_const[0] * g_col[k])
    for b in range(1, 16):
        total = 0.0
        for k in range(3):
            put(11 + 16 * k + b, g_col[k] * basis[b])
            total = total + g_col[k] * feat(11 + 16 * k + b)
        pulled.append(total)
    g_way = sh_pull(pulled, *way)
    along = way[0] * g_way[0] + way[1] * g_way[1] + way[2] * g_way[2]
    g_off = [(g_way[a] - way[a] * along) * rlen for a in range(3)]
    put(10, g_o / (1.0 + jnp.exp(feat(10))))
    a, b, c = part["conic"]
    g_xx = -(a * a * g_a + a * b * g_b + b * b * g_c)
    g_xy = -(2.0 * a * b * g_a + (a * c + b * b) * g_b + 2.0 * b * c * g_c)
    g_yy = -(b * b * g_a + b * c * g_b + c * c * g_c)
    axes, wide, turn, screen = part["axes"], part["wide"], part["turn"], part["screen"]
    for k in range(3):
        g_scale = (
            g_xx * axes[0][k] * wide[0][k]
            + g_xy * axes[0][k] * wide[1][k]
            + g_yy * axes[1][k] * wide[1][k]
        )
        put(3 + k, 2.0 * g_scale)
    g_axes = [
        [2.0 * g_xx * wide[0][k] + g_xy * wide[1][k] for k in range(3)],
        [2.0 * g_yy * wide[1][k] + g_xy * wide[0][k] for k in range(3)],
    ]
    g_screen = [
        [sum(g_axes[r][k] * turn[c][k] for k in range(3)) for c in range(3)] for r in range(2)
    ]
    gm = [
        [g_axes[0][k] * screen[0][c] + g_axes[1][k] * screen[1][c] for k in range(3)]
        for c in range(3)
    ]
    w, x, y, z = part["rotor"]
    up_xy, up_xz, up_yz = gm[0][1] + gm[1][0], gm[0][2] + gm[2][0], gm[1][2] + gm[2][1]
    un_xy, un_xz, un_yz = gm[1][0] - gm[0][1], gm[0][2] - gm[2][0], gm[2][1] - gm[1][2]
    g_rotor = [
        2.0 * (z * un_xy + y * un_xz + x * un_yz),
        2.0 * (y * up_xy + z * up_xz + w * un_yz - 2.0 * x * (gm[1][1] + gm[2][2])),
        2.0 * (x * up_xy + z * up_yz + w * un_xz - 2.0 * y * (gm[0][0] + gm[2][2])),
        2.0 * (x * up_xz + y * up_yz + w * un_xy - 2.0 * z * (gm[0][0] + gm[1][1])),
    ]
    rotor = (w, x, y, z)
    along = sum(rotor[i] * g_rotor[i] for i in range(4))
    for i in range(4):
        put(6 + i, (g_rotor[i] - rotor[i] * along) * part["rnorm"])
    rot, inv, finv, u, v = part["rot"], part["inv"], part["finv"], part["u"], part["v"]
    g_u = focal_length * g_mx - finv * sum(g_screen[0][c] * rot[2][c] for c in range(3))
    g_v = focal_length * g_my - finv * sum(g_screen[1][c] * rot[2][c] for c in range(3))
    g_f = sum(g_screen[r][c] * screen[r][c] for r in range(2) for c in range(3))
    g_in = [g_u * inv, g_v * inv, -(g_f + g_u * u + g_v * v) * inv]
    for axis in range(3):
        put(
            axis,
            g_off[axis] + rot[0][axis] * g_in[0] + rot[1][axis] * g_in[1] + rot[2][axis] * g_in[2],
        )


def split(value):
    high = value.astype(BF16)
    return high, (value - high.astype(F32)).astype(BF16)


def matmul(a, b, dims=((1,), (0,))):
    return lax.dot_general(a, b, (dims, ((), ())), preferred_element_type=F32)


def spread_features(parts, scratch, count):
    tiles = sum(part.shape[1] for part in parts) // LANES
    at = 0
    for part in parts:
        for first in range(0, part.shape[1], LANES):
            for row in range(0, count, 8):
                rows = min(8, count - row)
                scratch[pl.ds(row * tiles + at, rows, stride=tiles), :] = part[
                    row : row + rows, first : first + LANES
                ]
            at += 1
    return tiles


def pack_kernel(shards, where, *refs):
    sources, (info, params, shard_of, local_of, goal, place_s, sems) = refs[:4], refs[4:]
    group = where[0]
    loads = [
        pltpu.make_async_copy(source, held, sems.at[k])
        for k, (source, held) in enumerate(zip(sources, (shard_of, local_of, goal, params)))
    ]
    for load in loads:
        load.start()
    for load in loads[:3]:
        load.wait()
    width = info.shape[1]
    tile_count, listed = local_of.shape
    rows_each = (info.shape[0] - 4) // tile_count
    columns = rows_each * width
    chunk = columns // shards
    info[0:3, :] = goal[...]
    for t in range(tile_count):
        place = (shard_of[t] ^ group) * chunk + (local_of[t : t + 1, :] - group * chunk)
        info[3:4, t * listed : (t + 1) * listed] = place.astype(F32)
        row_i = lax.broadcasted_iota(jnp.int32, (LANES, LANES), 0)
        col_i = lax.broadcasted_iota(jnp.int32, (LANES, LANES), 1)
        for first in range(0, listed, LANES):
            spread = jnp.broadcast_to(place[:, first : first + LANES].astype(F32), (LANES, LANES))
            place_s[first : first + LANES, :] = jnp.broadcast_to(
                jnp.sum(jnp.where(row_i == col_i, spread, 0.0), axis=1, keepdims=True), (LANES, LANES)
            )
        lane_of = lax.broadcasted_iota(jnp.int32, (8, LANES), 1).astype(F32)
        row_of = lax.broadcasted_iota(jnp.int32, (8, LANES), 0).astype(F32)
        for s in range(columns // LANES):
            best = jnp.full((8, LANES), -1.0, F32)
            column = lane_of + float(s * LANES)
            for first in range(0, listed, 8):
                best = jnp.where(
                    place_s[first : first + 8, :] == column, row_of + float(first), best
                )
            best = jnp.max(best, axis=0, keepdims=True)
            row, at = 4 + t * rows_each + s * LANES // width, s * LANES % width
            info[row : row + 1, at : at + LANES] = best
    loads[3].wait()


def pack(group, params, target, hit_shard, hit_local, shards):
    columns = params.shape[1]
    tile_count, listed = hit_local.shape
    width = target.shape[1]
    rows = 4 + tile_count * (columns // width)
    args = (hit_shard.reshape(tile_count, 1, listed), hit_local, target, params)
    return call(
        functools.partial(pack_kernel, shards),
        "pack",
        (jax.ShapeDtypeStruct((rows, width), F32), jax.ShapeDtypeStruct(params.shape, F32)),
        [smem()] + [pl.BlockSpec(memory_space=pltpu.HBM)] * 4,
        [
            pltpu.VMEM((tile_count, 1, listed), jnp.int32),
            pltpu.VMEM((tile_count, listed), jnp.int32),
            pltpu.VMEM(target.shape, F32),
            pltpu.VMEM((listed, LANES), F32),
            pltpu.SemaphoreType.DMA((4,)),
        ],
        (group.reshape(1),) + tuple(pltpu.with_memory_space_constraint(a, pltpu.HBM) for a in args),
        (vmem(), any_space()),
    )


def sent_rows(views):
    return (11 + 3 * views + 7) // 8 * 8


def cut_kernel(pieces, where, cams, params, *refs):
    parts, (feats, rows) = refs[:pieces], refs[pieces:]
    views = cams.shape[0]
    count = sent_rows(views)
    slabs = spread_features([params], feats, params.shape[0])

    def feat(f):
        return feats[f * slabs : (f + 1) * slabs, :]

    values = [feat(f) for f in range(11)]
    for v in range(views):
        values += shade(feat, [cams[v, i] for i in range(12)])
    values += [jnp.zeros((slabs, LANES), F32)] * (count - len(values))
    for f, value in enumerate(values):
        rows[pl.ds(f, slabs, stride=count), :] = value
    each = slabs // pieces
    for d in range(pieces):
        for h in range(each):
            first = (((where[0] ^ d) % pieces) * each + h) * count
            parts[d][:, h * LANES : (h + 1) * LANES] = rows[
                pl.ds(pl.multiple_of(first, 8), count), :
            ]


def cut(group, cameras, params, pieces):
    features, columns = params.shape
    slabs = columns // LANES
    count = sent_rows(cameras.shape[0])
    return list(
        call(
            functools.partial(cut_kernel, pieces),
            "cut",
            (jax.ShapeDtypeStruct((count, columns // pieces), F32),) * pieces,
            [smem()] * 2 + [vmem()],
            [
                pltpu.VMEM((features * slabs, LANES), F32),
                pltpu.VMEM((count * slabs, LANES), F32),
            ],
            (group.reshape(1), cameras, params),
        )
    )


def pixel_basis(pixels):
    pixel = lax.broadcasted_iota(jnp.int32, (8, pixels), 1)
    row = lax.broadcasted_iota(jnp.int32, (8, pixels), 0)
    middle = 0.5 * TILE_SIDE - 0.5
    u = (pixel % TILE_SIDE).astype(F32) - middle
    v = (pixel // TILE_SIDE).astype(F32) - middle
    value = jnp.where(row == 0, 1.0, 0.0)
    for at, term in ((1, u), (2, v), (3, u * u), (4, u * v), (5, v * v)):
        value = jnp.where(row == at, term, value)
    return value


def composite(tiles, first_group, me, rows, info_s, rendered, work):
    alpha_s, weight_s, pull_s, push_s, weight_2, coef_s, colour_s, error_s, mix_s, index_s, acc_s = work
    groups, tile_count, _, listed = acc_s.shape
    pixels = info_s.shape[2] // tile_count
    parts = pixels // LANES
    halves = listed // LANES
    tiles_here = groups * tile_count
    spans = tiles_here * parts
    slabs = rows.shape[0] // ROWS
    side = TILE_SIDE
    first_col, first_row = tiles

    def of_span(span):
        return pl.ds(span * SPAN_STEP, listed, stride=LIST_STEP)

    def of_place(place):
        return pl.ds(place * LIST_STEP, spans, stride=SPAN_STEP)

    def lane_gather(source, lane):
        return jnp.take_along_axis(source, lane, axis=1, mode="promise_in_bounds")

    basis = pixel_basis(pixels)
    basis_3 = jnp.concatenate([basis, basis, basis], axis=0).astype(BF16)

    entries = []
    for n in range(tiles_here):
        g, t = n // tile_count, n % tile_count
        found = []
        for h in range(halves):
            first = t * listed + h * LANES
            at = info_s[g, 3:4, first : first + LANES].astype(jnp.int32)
            index_s[n * halves + h : n * halves + h + 1, :] = at
            at = jnp.broadcast_to(at, (8, LANES))
            lane, slab = at & (LANES - 1), at >> 7
            value = lane_gather(rows[0:8, :], lane)
            for s in range(1, slabs):
                value = jnp.where(
                    slab == s, lane_gather(rows[s * ROWS : s * ROWS + 8, :], lane), value
                )
            found.append(value)
        entries.append(jnp.concatenate(found, axis=1))
    at = index_s[...]
    lane, slab = at & (LANES - 1), at >> 7
    ninth = lane_gather(rows[8:16, :], lane)
    for s in range(1, slabs):
        ninth = jnp.where(
            slab == s, lane_gather(rows[s * ROWS + 8 : s * ROWS + 16, :], lane), ninth
        )

    means = []
    colour_s[...] = jnp.zeros(colour_s.shape, F32)
    for n in range(tiles_here):
        g, t = n // tile_count, n % tile_count
        entry = entries[n]
        slot = (me ^ (first_group + g)) * tile_count + t
        mean_u = entry[0:1] - (((first_col + slot % 4) * side).astype(F32) + 0.5 * side)
        mean_v = entry[1:2] - (((first_row + slot // 4) * side).astype(F32) + 0.5 * side)
        quad_a, quad_b, quad_c = -0.5 * entry[2:3], -entry[3:4], -0.5 * entry[4:5]
        means.append((mean_u, mean_v, quad_a, quad_b, quad_c))
        slope_u = 2.0 * quad_a * mean_u + quad_b * mean_v
        slope_v = 2.0 * quad_c * mean_v + quad_b * mean_u
        level = 0.5 * (slope_u * mean_u + slope_v * mean_v) + entry[5:6]
        zero = jnp.zeros_like(level)
        coef = jnp.concatenate(
            [level, -slope_u, -slope_v, quad_a, quad_b, quad_c, zero, zero], axis=0
        )
        here = slice(n * listed, (n + 1) * listed)
        for part in range(3):
            term = coef.astype(BF16).astype(F32)
            coef_s[part * 8 : part * 8 + 8, here] = term
            coef = coef - term
        last = [ninth[n * halves + h : n * halves + h + 1] for h in range(halves)]
        colours = jnp.concatenate([entry[6:8], jnp.concatenate(last, axis=1)], axis=0)
        high = colours.astype(BF16).astype(F32)
        colour_s[n * ROWS : n * ROWS + 3, here] = high
        colour_s[n * ROWS + 3 : n * ROWS + 6, here] = colours - high
        colour_s[n * ROWS + 6 : n * ROWS + 9, here] = high

    down = ((0,), (0,))
    power = matmul(coef_s[...].astype(BF16), basis_3, down)
    for n in range(tiles_here):
        for part in range(parts):
            alpha_s[of_span(n * parts + part), :] = jnp.exp(
                power[n * listed : (n + 1) * listed, part * LANES : (part + 1) * LANES]
            )

    unroll, quad = 32, 4
    steps = listed // unroll

    def forward(step, passed):
        for j in range(0, unroll, quad):
            at = [of_place(step * unroll + j + i) for i in range(quad)]
            alpha = [alpha_s[at[i], :] for i in range(quad)]
            keep = [1.0 - alpha[i] for i in range(quad)]
            two = keep[0] * keep[1]
            three = two * keep[2]
            weight_s[at[0], :] = alpha[0] * passed
            weight_s[at[1], :] = (alpha[1] * keep[0]) * passed
            weight_s[at[2], :] = (alpha[2] * two) * passed
            weight_s[at[3], :] = (alpha[3] * three) * passed
            passed = passed * (two * (keep[2] * keep[3]))
        return passed

    nought = jnp.zeros((spans, LANES), F32)
    lax.fori_loop(0, steps, forward, nought + 1.0)

    error_s[...] = jnp.zeros(error_s.shape, F32)
    mix_s[...] = jnp.zeros(mix_s.shape, F32)
    for n in range(tiles_here):
        g, t = n // tile_count, n % tile_count
        for part in range(parts):
            at = slice((n * parts + part) * LANES, (n * parts + part + 1) * LANES)
            weight_2[:listed, at], weight_2[listed:, at] = split(
                weight_s[of_span(n * parts + part), :]
            )
        at = slice(n * pixels, (n + 1) * pixels)
        colours = colour_s[n * ROWS : (n + 1) * ROWS, n * listed : (n + 1) * listed].astype(BF16)
        image = matmul(colours, weight_2[:listed, at])
        image = image[0:3] + image[3:6] + matmul(colours, weight_2[listed:, at])[0:3]
        here = slice(t * pixels, (t + 1) * pixels)
        if rendered is not None and g == 0:
            rendered[:, here] = image
        error = image - info_s[g, 0:3, here]
        high = error.astype(BF16).astype(F32)
        low = error - high
        error_s[n * ROWS : n * ROWS + 3, :] = high
        error_s[n * ROWS + 3 : n * ROWS + 6, :] = high
        error_s[n * ROWS + 6 : n * ROWS + 9, :] = low
        mix_s[0, n * ROWS : n * ROWS + 8, at] = basis
        mix_s[1, n * ROWS + 6 : n * ROWS + 9, at] = high
        mix_s[1, n * ROWS + 9 : n * ROWS + 12, at] = low
    pull = matmul(colour_s[...].astype(BF16), error_s[...].astype(BF16), down)
    for n in range(tiles_here):
        for part in range(parts):
            pull_s[of_span(n * parts + part), :] = pull[
                n * listed : (n + 1) * listed, part * LANES : (part + 1) * LANES
            ]

    def backward(back, behind):
        for j in range(0, unroll, quad):
            at = [of_place(listed - 1 - (back * unroll + j + i)) for i in range(quad)]
            alpha = [alpha_s[at[i], :] for i in range(quad)]
            pull = [pull_s[at[i], :] for i in range(quad)]
            keep = [1.0 - alpha[i] for i in range(quad)]
            own = alpha[0] * pull[0]
            seen, through = behind, keep[0]
            for i in range(quad):
                push_s[at[i], :] = weight_s[at[i], :] * (pull[i] - seen)
                if i > 0:
                    own = own * keep[i] + alpha[i] * pull[i]
                    through = through * keep[i]
                seen = behind * through + own
            behind = seen
        return behind

    lax.fori_loop(0, steps, backward, nought)

    across = ((1,), (1,))
    high, low = split(jnp.concatenate([push_s[of_span(span), :] for span in range(spans)], axis=1))
    sums = matmul(jnp.concatenate([high, low], axis=0), mix_s[0].astype(BF16), across)
    sums = sums + matmul(weight_2[...], mix_s[1].astype(BF16), across)
    sums = (sums[:listed] + sums[listed:]).T
    for n in range(tiles_here):
        g, t = n // tile_count, n % tile_count
        mean_u, mean_v, quad_a, quad_b, quad_c = means[n]
        m_00, m_10, m_01, m_20, m_11, m_02 = [
            sums[n * ROWS + m : n * ROWS + m + 1] for m in range(6)
        ]
        n_10 = m_10 - mean_u * m_00
        n_01 = m_01 - mean_v * m_00
        acc_s[g, t, 0:1, :] = -(2.0 * quad_a * n_10 + quad_b * n_01)
        acc_s[g, t, 1:2, :] = -(2.0 * quad_c * n_01 + quad_b * n_10)
        acc_s[g, t, 2:3, :] = -0.5 * (m_20 - mean_u * (m_10 + n_10))
        acc_s[g, t, 3:4, :] = -(m_11 - mean_u * m_01 - mean_v * n_10)
        acc_s[g, t, 4:5, :] = -0.5 * (m_02 - mean_v * (m_01 + n_01))
        acc_s[g, t, 5:6, :] = m_00
        at = n * ROWS + 6
        grads = sums[at : at + 3] + sums[at + 3 : at + 6]
        acc_s[g, t, 6:8, :] = grads[0:2]
        for h in range(halves):
            row = n * halves + h
            acc_s[0, 0, 8 + row : 9 + row, :LANES] = grads[2:3, h * LANES : (h + 1) * LANES]


def pool_sum(slab, info_s, acc_s):
    groups, tile_count, _, listed = acc_s.shape
    halves = listed // LANES
    width = info_s.shape[2]
    rows_each = (info_s.shape[1] - 4) // tile_count
    row_of = lax.broadcasted_iota(jnp.int32, (8, LANES), 0)

    def lane_gather(source, lane):
        return jnp.take_along_axis(source, lane, axis=1, mode="promise_in_bounds")

    totals, every = [], None
    for g in range(groups):
        total = jnp.zeros((8, LANES), F32)
        for t in range(tile_count):
            row, first = 4 + t * rows_each + slab * LANES // width, slab * LANES % width
            at = info_s[g, row : row + 1, first : first + LANES].astype(jnp.int32)
            at = jnp.broadcast_to(at, (8, LANES))
            n = g * tile_count + t
            every = at if every is None else jnp.where(row_of >= n * halves, at, every)
            lane, half = at & (LANES - 1), at >> 7
            for h in range(halves):
                here = lane_gather(acc_s[g, t, 0:8, h * LANES : (h + 1) * LANES], lane)
                total = total + jnp.where(half == h, here, 0.0)
        totals.append(total)
    here = lane_gather(acc_s[0, 0, 8:16, :LANES], every & (LANES - 1))
    ninth = jnp.where(every >> 7 == row_of % halves, here, 0.0)
    return totals[0] + totals[1], jnp.sum(ninth, axis=0, keepdims=True)


def block_start(tile_id):
    within = tile_id % (TILES_X * TILES_Y)
    return (within % TILES_X) // 4 * 4, (within // TILES_X) // 2 * 2


def near_kernel(pieces, tile_ids, cams, where, own, other, *refs):
    parts = refs[:pieces]
    rendered, rows, partial, feats, info_s, *work = refs[pieces:]
    view = tile_ids[0] // (TILES_X * TILES_Y)
    cam = [cams[view, i] for i in range(12)]
    slabs = spread_features(parts, feats, parts[0].shape[0])
    projected = project_rows(lambda f: feats[f * slabs : (f + 1) * slabs, :], cam)
    for k in range(3):
        first = pl.multiple_of((11 + 3 * view + k) * slabs, slabs)
        projected.append(feats[pl.ds(first, slabs), :])
    for f, value in enumerate(projected):
        rows[pl.ds(f, slabs, stride=ROWS), :] = value
    for f in range(len(projected), ROWS):
        rows[pl.ds(f, slabs, stride=ROWS), :] = projected[8]
    info_s[0] = own[...]
    info_s[1] = other[...]
    composite(block_start(tile_ids[0]), 0, where[0], rows, info_s, rendered, work)
    for s in range(slabs):
        at = slice(s * LANES, (s + 1) * LANES)
        partial[0:8, at], partial[8:9, at] = pool_sum(s, info_s, work[-1])


def far_kernel(blocks, tile_ids, where, rows, partial, infos, *refs):
    *packets, info_s = refs[: len(refs) - 11]
    work = refs[len(refs) - 11 :]
    half = infos.shape[0] // 2
    info_s[0] = infos[:half, :]
    info_s[1] = infos[half:, :]
    composite(block_start(tile_ids[0]), 2, where[0], rows, info_s, None, work)
    share = (tile_ids[0] // (TILES_X * TILES_Y)).astype(F32)
    row_of = lax.broadcasted_iota(jnp.int32, (8, LANES), 0)
    lane_of = lax.broadcasted_iota(jnp.int32, (8, LANES), 1)
    chunk = packets[0].shape[1]
    for s in range(rows.shape[0] // ROWS):
        total, ninth = pool_sum(s, info_s, work[-1])
        total = total + partial[0:8, s * LANES : (s + 1) * LANES]
        ninth = ninth + partial[8:9, s * LANES : (s + 1) * LANES]
        if blocks == 1:
            mine = share
        else:
            column = s * LANES + lane_of
            mine = jnp.where(column % where[2] // (where[2] // blocks) == where[1], share, 0.0)
        at = slice(s * LANES % chunk, s * LANES % chunk + LANES)
        packets[s * LANES // chunk][0:8, at] = total
        packets[s * LANES // chunk][8:16, at] = jnp.where(
            row_of == 0, jnp.broadcast_to(ninth, (8, LANES)), mine
        )


def join_kernel(first, second, out):
    half = first.shape[0]
    out[:half, :] = first[...]
    out[half:, :] = second[...]


def update_kernel(pieces, follows, where, cams, params, adam_m, adam_v, *refs):
    packets, refs = refs[:pieces], refs[pieces + 3 * follows :]
    sinks, (feats, rows, grads, made, sems) = refs[:3], refs[3:]
    features = params.shape[0]
    chunk = packets[0].shape[1]
    width = pieces * chunk
    slabs = width // LANES
    start = (where[0] ^ where[1]) // pieces * pieces * chunk
    for d in range(pieces):
        for h in range(chunk // LANES):
            slab = (where[0] ^ where[1] ^ d) % pieces * (chunk // LANES) + h
            rows[pl.ds(slab, ROWS, stride=slabs), :] = packets[d][:, h * LANES : (h + 1) * LANES]
    pulled = [rows[f * slabs : (f + 1) * slabs, :] for f in range(10)]
    view = pulled[9]
    cam = []
    for i in range(12):
        value = jnp.full((slabs, LANES), cams[0, i], F32)
        for v in range(1, cams.shape[0]):
            value = jnp.where(view == float(v), cams[v, i], value)
        cam.append(value)

    def put(f, value):
        grads[f * slabs : (f + 1) * slabs, :] = value

    def column(s):
        return pl.ds(pl.multiple_of(start + s * LANES, LANES), LANES)

    for s in range(slabs):
        for row in range(0, features, 8):
            count = min(8, features - row)
            feats[pl.ds(row * slabs + s, count, stride=slabs), :] = params[
                row : row + count, column(s)
            ]
    project_pull(lambda f: feats[f * slabs : (f + 1) * slabs, :], cam, pulled[:9], put)
    rate = learn_rate / (1.0 - beta_one**adam_steps)
    unbias = 1.0 / (1.0 - beta_two**adam_steps)
    stores = []
    order = list(range(16, features, 8)) + [0, 8]
    for row in order:
        count = min(8, features - row)
        span = slice(row, row + count)
        for s in range(slabs):
            here = (span, slice(s * LANES, (s + 1) * LANES))
            grad = grads[pl.ds(row * slabs + s, count, stride=slabs), :]
            moment = beta_one * adam_m[span, column(s)] + (1.0 - beta_one) * grad
            second = beta_two * adam_v[span, column(s)] + (1.0 - beta_two) * grad * grad
            made.at[1][here] = moment
            made.at[2][here] = second
            made.at[0][here] = params[span, column(s)] - rate * moment / (
                jnp.sqrt(second * unbias) + adam_eps
            )
        if row % 16 == 8 or row + count == features:
            first = row // 16 * 16
            span = pl.ds(first, row + count - first)
            columns = pl.ds(pl.multiple_of(start, LANES), width)
            for k in range(3):
                store = pltpu.make_async_copy(
                    made.at[k, span], sinks[k].at[span, columns], sems.at[k, first // 16]
                )
                store.start()
                stores.append(store)
    for store in stores:
        store.wait()


def vmem():
    return pl.BlockSpec(memory_space=pltpu.VMEM)


def smem():
    return pl.BlockSpec(memory_space=pltpu.SMEM)


def any_space():
    return pl.BlockSpec(memory_space=pl.ANY)


def call(kernel, name, out_shape, in_specs, scratch, args, out_specs=None, grant=32):
    return pl.pallas_call(
        kernel,
        out_shape=out_shape,
        in_specs=in_specs,
        out_specs=out_specs or tuple(vmem() for _ in out_shape),
        scratch_shapes=scratch,
        compiler_params=pltpu.CompilerParams(vmem_limit_bytes=grant * 1024 * 1024),
        name=name,
    )(*args)


def work_shapes(tile_count, pixels, listed):
    tiles = 2 * tile_count
    spans = tiles * pixels // LANES
    assert (spans - 1) * SPAN_STEP < LIST_STEP and tiles * listed // LANES == 8
    return [pltpu.VMEM((listed * LIST_STEP, LANES), F32)] * 4 + [
        pltpu.VMEM((2 * listed, spans * LANES), BF16),
        pltpu.VMEM((24, tiles * listed), F32),
        pltpu.VMEM((tiles * ROWS, tiles * listed), F32),
        pltpu.VMEM((tiles * ROWS, pixels), F32),
        pltpu.VMEM((2, LANES, spans * LANES), F32),
        pltpu.VMEM((8, LANES), jnp.int32),
        pltpu.VMEM((2, tile_count, ROWS, listed), F32),
    ]


def near(tile_ids, cameras, where, own, other, parts, tile_count):
    width = sum(part.shape[1] for part in parts)
    features = parts[0].shape[0]
    slabs = width // LANES
    pixels = listed = own.shape[1] // tile_count
    return call(
        functools.partial(near_kernel, len(parts)),
        "near",
        (
            jax.ShapeDtypeStruct((3, own.shape[1]), F32),
            jax.ShapeDtypeStruct((ROWS * slabs, LANES), F32),
            jax.ShapeDtypeStruct((ROWS, width), F32),
        ),
        [smem()] * 3 + [vmem()] * (2 + len(parts)),
        [pltpu.VMEM((features * slabs, LANES), F32), pltpu.VMEM((2,) + own.shape, F32)]
        + work_shapes(tile_count, pixels, listed),
        (tile_ids, cameras, where, own, other, *parts),
    )


def far(tile_ids, where, rows, partial, infos, pieces, tile_count, blocks):
    width = partial.shape[1]
    pixels = listed = infos.shape[1] // tile_count
    info = (infos.shape[0] // 2, infos.shape[1])
    return call(
        functools.partial(far_kernel, blocks),
        "far",
        (jax.ShapeDtypeStruct((ROWS, width // pieces), F32),) * pieces,
        [smem()] * 2 + [vmem()] * 3,
        [pltpu.VMEM((2,) + info, F32)] + work_shapes(tile_count, pixels, listed),
        (tile_ids, where, rows, partial, infos),
    )


def join(first, second):
    shape = (2 * first.shape[0], first.shape[1])
    return call(
        join_kernel, "join", (jax.ShapeDtypeStruct(shape, F32),), [vmem()] * 2, [], (first, second)
    )[0]


def update(own, first, cameras, params, adam_m, adam_v, packets, before):
    features = params.shape[0]
    width = sum(packet.shape[1] for packet in packets)
    slabs = width // LANES
    shape = jax.ShapeDtypeStruct(params.shape, F32)
    at = 5 + len(packets)
    return pl.pallas_call(
        functools.partial(update_kernel, len(packets), len(before) > 0),
        out_shape=(shape, shape, shape),
        in_specs=[smem()] * 2
        + [vmem()] * (3 + len(packets))
        + [any_space()] * len(before),
        out_specs=(any_space(),) * 3,
        scratch_shapes=[
            pltpu.VMEM((features * slabs, LANES), F32),
            pltpu.VMEM((ROWS * slabs, LANES), F32),
            pltpu.VMEM((features * slabs, LANES), F32),
            pltpu.VMEM((3, features, width), F32),
            pltpu.SemaphoreType.DMA((3, (features + 15) // 16)),
        ],
        input_output_aliases={at + k: k for k in range(len(before))},
        compiler_params=pltpu.CompilerParams(vmem_limit_bytes=32 * 1024 * 1024),
        name="update",
    )(
        jnp.stack([own, jnp.int32(first)]).astype(jnp.int32),
        cameras, params, adam_m, adam_v, *packets, *before,
    )


def swap(value, axis, d):
    if d == 0:
        return value
    return lax.ppermute(value, axis, [(k, k ^ d) for k in range(lax.axis_size(axis))])


def local(params, adam_m, adam_v, cameras, target, tile_ids, hit_shard, hit_local):
    width = params.shape[1]
    tile_count, listed = hit_local.shape
    shards = lax.axis_size("gs")
    along = lax.axis_size("tile")
    chunk = width // shards
    group = lax.axis_index("gs")
    seat = lax.axis_index("tile")
    aligned = chunk % LANES == 0
    team = BLOCK_TILES // tile_count
    assert team == 4
    blocks = along // team

    info, params = pack(group, params, target, hit_shard, hit_local, shards)
    parts = cut(group, cameras, params, shards if aligned else 1)
    if not aligned:
        parts = [
            lax.dynamic_slice_in_dim(parts[0], (group ^ d) * chunk, chunk, axis=1)
            for d in range(shards)
        ]
    parts = [swap(parts[d], "gs", d) for d in range(shards)]
    beside = swap(info, "tile", 1)
    beyond = swap(join(info, beside), "tile", 2)
    if not aligned:
        parts = [jnp.concatenate(parts, axis=1)]
    where = jnp.stack([seat % team, seat // team, jnp.int32(chunk)]).astype(jnp.int32)
    rendered, rows, partial = near(tile_ids, cameras, where, info, beside, parts, tile_count)
    packets = far(tile_ids, where, rows, partial, beyond, len(parts), tile_count, blocks)
    if not aligned:
        packets = [packets[0][:, d * chunk : (d + 1) * chunk] for d in range(shards)]
    packets = [swap(packets[d], "gs", d) for d in range(shards)]
    if blocks > 1:
        packets = [block_sum(packet, along, team) for packet in packets]
    if aligned:
        own = group
    else:
        packets = [jnp.stack(packets)[jnp.arange(shards) ^ group].transpose(1, 0, 2).reshape(ROWS, -1)]
        own = jnp.int32(0)
    made = ()
    count = max(1, len(packets) // 2)
    for first in range(0, len(packets), count):
        made = update(
            own, first, cameras, params, adam_m, adam_v, packets[first : first + count], made
        )
    new_params, new_m, new_v = made
    return (rendered, new_params, new_m, new_v)


def block_sum(packet, along, team):
    step = team
    while step < along:
        packet = packet + swap(packet, "tile", step)
        step *= 2
    return packet


def solution(mesh):
    return jax.shard_map(
        local,
        mesh=mesh,
        in_specs=(
            P(None, ("groups", "gs")),
            P(None, ("groups", "gs")),
            P(None, ("groups", "gs")),
            P("groups", None),
            P(None, ("groups", "gs", "tile")),
            P(("groups", "gs", "tile")),
            P(("groups", "gs", "tile"), None, None),
            P(("groups", "gs", "tile"), None),
        ),
        out_specs=(
            P(None, ("groups", "gs", "tile")),
            P(None, ("groups", "gs")),
            P(None, ("groups", "gs")),
            P(None, ("groups", "gs")),
        ),
        check_vma=False,
    )
```

```python
import functools

import jax
import jax.numpy as jnp
from jax import lax
from jax.experimental import pallas as pl
from jax.experimental.pallas import tpu as pltpu
from jax.sharding import PartitionSpec as P

TILES_X = 120
TILES_Y = 68
TILE_SIDE = 16
BLOCK_TILES = 8
LANES = 128
ROWS = 16
SPAN_STEP, LIST_STEP = 3, 25
F32 = jnp.float32
BF16 = jnp.bfloat16

focal_length = 1000.0
center_x = 960.0
center_y = 540.0
dilation = 0.3
beta_one = 0.9
beta_two = 0.999
learn_rate = 0.01
adam_eps = 1e-08
adam_steps = 100.0
sh_const = (
    0.28209479177387814,
    0.4886025119029199,
    1.0925484305920792,
    0.31539156525252005,
    0.5462742152960396,
    0.5900435899266435,
    2.890611442640554,
    0.4570457994644658,
    0.3731763325901154,
    1.445305721320277,
)


def sh_basis(x, y, z):
    s = sh_const
    xx, yy, zz = x * x, y * y, z * z
    return [
        None,
        -s[1] * y,
        s[1] * z,
        -s[1] * x,
        s[2] * (x * y),
        -s[2] * (y * z),
        s[3] * (2.0 * zz - xx - yy),
        -s[2] * (x * z),
        s[4] * (xx - yy),
        -s[5] * y * (3.0 * xx - yy),
        s[6] * (x * y) * z,
        -s[7] * y * (4.0 * zz - xx - yy),
        s[8] * z * (2.0 * zz - 3.0 * xx - 3.0 * yy),
        -s[7] * x * (4.0 * zz - xx - yy),
        s[9] * z * (xx - yy),
        -s[5] * x * (xx - 3.0 * yy),
    ]


def sh_pull(h, x, y, z):
    s = sh_const
    xx, yy, zz = x * x, y * y, z * z
    xy, xz, yz = x * y, x * z, y * z
    diff = xx - yy
    ring = 4.0 * zz - xx - yy
    g_x = (
        -s[1] * h[3]
        + s[2] * (h[4] * y - h[7] * z)
        - (2.0 * s[3]) * h[6] * x
        + (2.0 * s[4]) * h[8] * x
        - (6.0 * s[5]) * h[9] * xy
        + s[6] * h[10] * yz
        + (2.0 * s[7]) * h[11] * xy
        - (6.0 * s[8]) * h[12] * xz
        - s[7] * h[13] * (ring - 2.0 * xx)
        + (2.0 * s[9]) * h[14] * xz
        - (3.0 * s[5]) * h[15] * diff
    )
    g_y = (
        -s[1] * h[1]
        + s[2] * (h[4] * x - h[5] * z)
        - (2.0 * s[3]) * h[6] * y
        - (2.0 * s[4]) * h[8] * y
        - (3.0 * s[5]) * h[9] * diff
        + s[6] * h[10] * xz
        - s[7] * h[11] * (ring - 2.0 * yy)
        - (6.0 * s[8]) * h[12] * yz
        + (2.0 * s[7]) * h[13] * xy
        - (2.0 * s[9]) * h[14] * yz
        + (6.0 * s[5]) * h[15] * xy
    )
    g_z = (
        s[1] * h[2]
        - s[2] * (h[5] * y + h[7] * x)
        + (4.0 * s[3]) * h[6] * z
        + s[6] * h[10] * xy
        - (8.0 * s[7]) * (h[11] * yz + h[13] * xz)
        + s[8] * h[12] * (6.0 * zz - 3.0 * xx - 3.0 * yy)
        + s[9] * h[14] * diff
    )
    return g_x, g_y, g_z


def project_parts(feat, cam):
    rot = [[cam[3 * r + c] for c in range(3)] for r in range(3)]
    off = [feat(a) - cam[9 + a] for a in range(3)]
    in_cam = [rot[r][0] * off[0] + rot[r][1] * off[1] + rot[r][2] * off[2] for r in range(3)]
    inv = 1.0 / in_cam[2]
    u = in_cam[0] * inv
    v = in_cam[1] * inv
    finv = focal_length * inv
    scale = [jnp.exp(2.0 * feat(3 + a)) for a in range(3)]
    quat = [feat(6 + a) for a in range(4)]
    rnorm = lax.rsqrt(quat[0] * quat[0] + quat[1] * quat[1] + quat[2] * quat[2] + quat[3] * quat[3])
    w, x, y, z = [q * rnorm for q in quat]
    turn = [
        [1.0 - 2.0 * (y * y + z * z), 2.0 * (x * y - w * z), 2.0 * (x * z + w * y)],
        [2.0 * (x * y + w * z), 1.0 - 2.0 * (x * x + z * z), 2.0 * (y * z - w * x)],
        [2.0 * (x * z - w * y), 2.0 * (y * z + w * x), 1.0 - 2.0 * (x * x + y * y)],
    ]
    screen = [
        [finv * (rot[0][c] - u * rot[2][c]) for c in range(3)],
        [finv * (rot[1][c] - v * rot[2][c]) for c in range(3)],
    ]
    axes = [
        [sum(screen[r][c] * turn[c][k] for c in range(3)) for k in range(3)] for r in range(2)
    ]
    wide = [[axes[r][k] * scale[k] for k in range(3)] for r in range(2)]
    cov_xx = sum(wide[0][k] * axes[0][k] for k in range(3)) + dilation
    cov_xy = sum(wide[0][k] * axes[1][k] for k in range(3))
    cov_yy = sum(wide[1][k] * axes[1][k] for k in range(3)) + dilation
    rdet = 1.0 / (cov_xx * cov_yy - cov_xy * cov_xy)
    conic = (cov_yy * rdet, -cov_xy * rdet, cov_xx * rdet)
    rlen = lax.rsqrt(off[0] * off[0] + off[1] * off[1] + off[2] * off[2])
    way = [off[a] * rlen for a in range(3)]
    return dict(
        rot=rot, inv=inv, u=u, v=v, finv=finv, scale=scale, rnorm=rnorm, rotor=(w, x, y, z), turn=turn,
        screen=screen, axes=axes, wide=wide, conic=conic, rlen=rlen, way=way,
    )


def shade(feat, cam):
    off = [feat(a) - cam[9 + a] for a in range(3)]
    rlen = lax.rsqrt(off[0] * off[0] + off[1] * off[1] + off[2] * off[2])
    basis = sh_basis(*[off[a] * rlen for a in range(3)])
    colours = []
    for k in range(3):
        total = 0.5 + sh_const[0] * feat(11 + 16 * k)
        for b in range(1, 16):
            total = total + feat(11 + 16 * k + b) * basis[b]
        colours.append(total)
    return colours


def project_rows(feat, cam):
    part = project_parts(feat, cam)
    mean_x = focal_length * part["u"] + center_x
    mean_y = focal_length * part["v"] + center_y
    logit = feat(10)
    log_opacity = jnp.minimum(logit, 0.0) - jnp.log(1.0 + jnp.exp(-jnp.abs(logit)))
    return [mean_x, mean_y, *part["conic"], log_opacity]


def project_pull(feat, cam, grads, put):
    part = project_parts(feat, cam)
    g_mx, g_my, g_a, g_b, g_c, g_o = grads[:6]
    g_col = grads[6:9]
    way, rlen = part["way"], part["rlen"]
    basis = sh_basis(*way)
    pulled = [None]
    for k in range(3):
        put(11 + 16 * k, sh_const[0] * g_col[k])
    for b in range(1, 16):
        total = 0.0
        for k in range(3):
            put(11 + 16 * k + b, g_col[k] * basis[b])
            total = total + g_col[k] * feat(11 + 16 * k + b)
        pulled.append(total)
    g_way = sh_pull(pulled, *way)
    along = way[0] * g_way[0] + way[1] * g_way[1] + way[2] * g_way[2]
    g_off = [(g_way[a] - way[a] * along) * rlen for a in range(3)]
    put(10, g_o / (1.0 + jnp.exp(feat(10))))
    a, b, c = part["conic"]
    g_xx = -(a * a * g_a + a * b * g_b + b * b * g_c)
    g_xy = -(2.0 * a * b * g_a + (a * c + b * b) * g_b + 2.0 * b * c * g_c)
    g_yy = -(b * b * g_a + b * c * g_b + c * c * g_c)
    axes, wide, turn, screen = part["axes"], part["wide"], part["turn"], part["screen"]
    for k in range(3):
        g_scale = (
            g_xx * axes[0][k] * wide[0][k]
            + g_xy * axes[0][k] * wide[1][k]
            + g_yy * axes[1][k] * wide[1][k]
        )
        put(3 + k, 2.0 * g_scale)
    g_axes = [
        [2.0 * g_xx * wide[0][k] + g_xy * wide[1][k] for k in range(3)],
        [2.0 * g_yy * wide[1][k] + g_xy * wide[0][k] for k in range(3)],
    ]
    g_screen = [
        [sum(g_axes[r][k] * turn[c][k] for k in range(3)) for c in range(3)] for r in range(2)
    ]
    gm = [
        [g_axes[0][k] * screen[0][c] + g_axes[1][k] * screen[1][c] for k in range(3)]
        for c in range(3)
    ]
    w, x, y, z = part["rotor"]
    up_xy, up_xz, up_yz = gm[0][1] + gm[1][0], gm[0][2] + gm[2][0], gm[1][2] + gm[2][1]
    un_xy, un_xz, un_yz = gm[1][0] - gm[0][1], gm[0][2] - gm[2][0], gm[2][1] - gm[1][2]
    g_rotor = [
        2.0 * (z * un_xy + y * un_xz + x * un_yz),
        2.0 * (y * up_xy + z * up_xz + w * un_yz - 2.0 * x * (gm[1][1] + gm[2][2])),
        2.0 * (x * up_xy + z * up_yz + w * un_xz - 2.0 * y * (gm[0][0] + gm[2][2])),
        2.0 * (x * up_xz + y * up_yz + w * un_xy - 2.0 * z * (gm[0][0] + gm[1][1])),
    ]
    rotor = (w, x, y, z)
    along = sum(rotor[i] * g_rotor[i] for i in range(4))
    for i in range(4):
        put(6 + i, (g_rotor[i] - rotor[i] * along) * part["rnorm"])
    rot, inv, finv, u, v = part["rot"], part["inv"], part["finv"], part["u"], part["v"]
    g_u = focal_length * g_mx - finv * sum(g_screen[0][c] * rot[2][c] for c in range(3))
    g_v = focal_length * g_my - finv * sum(g_screen[1][c] * rot[2][c] for c in range(3))
    g_f = sum(g_screen[r][c] * screen[r][c] for r in range(2) for c in range(3))
    g_in = [g_u * inv, g_v * inv, -(g_f + g_u * u + g_v * v) * inv]
    for axis in range(3):
        put(
            axis,
            g_off[axis] + rot[0][axis] * g_in[0] + rot[1][axis] * g_in[1] + rot[2][axis] * g_in[2],
        )


def split(value):
    high = value.astype(BF16)
    return high, (value - high.astype(F32)).astype(BF16)


def matmul(a, b, dims=((1,), (0,))):
    return lax.dot_general(a, b, (dims, ((), ())), preferred_element_type=F32)


def spread_features(parts, scratch, count):
    tiles = sum(part.shape[1] for part in parts) // LANES
    at = 0
    for part in parts:
        for first in range(0, part.shape[1], LANES):
            for row in range(0, count, 8):
                rows = min(8, count - row)
                scratch[pl.ds(row * tiles + at, rows, stride=tiles), :] = part[
                    row : row + rows, first : first + LANES
                ]
            at += 1
    return tiles


def pack_kernel(shards, where, *refs):
    sources, (info, params, shard_of, local_of, goal, place_s, sems) = refs[:4], refs[4:]
    group = where[0]
    loads = [
        pltpu.make_async_copy(source, held, sems.at[k])
        for k, (source, held) in enumerate(zip(sources, (shard_of, local_of, goal, params)))
    ]
    for load in loads:
        load.start()
    for load in loads[:3]:
        load.wait()
    width = info.shape[1]
    tile_count, listed = local_of.shape
    rows_each = (info.shape[0] - 4) // tile_count
    columns = rows_each * width
    chunk = columns // shards
    info[0:3, :] = goal[...]
    for t in range(tile_count):
        place = (shard_of[t] ^ group) * chunk + (local_of[t : t + 1, :] - group * chunk)
        info[3:4, t * listed : (t + 1) * listed] = place.astype(F32)
        row_i = lax.broadcasted_iota(jnp.int32, (LANES, LANES), 0)
        col_i = lax.broadcasted_iota(jnp.int32, (LANES, LANES), 1)
        for first in range(0, listed, LANES):
            spread = jnp.broadcast_to(place[:, first : first + LANES].astype(F32), (LANES, LANES))
            place_s[first : first + LANES, :] = jnp.broadcast_to(
                jnp.sum(jnp.where(row_i == col_i, spread, 0.0), axis=1, keepdims=True), (LANES, LANES)
            )
        lane_of = lax.broadcasted_iota(jnp.int32, (8, LANES), 1).astype(F32)
        row_of = lax.broadcasted_iota(jnp.int32, (8, LANES), 0).astype(F32)
        for s in range(columns // LANES):
            best = jnp.full((8, LANES), -1.0, F32)
            column = lane_of + float(s * LANES)
            for first in range(0, listed, 8):
                best = jnp.where(
                    place_s[first : first + 8, :] == column, row_of + float(first), best
                )
            best = jnp.max(best, axis=0, keepdims=True)
            row, at = 4 + t * rows_each + s * LANES // width, s * LANES % width
            info[row : row + 1, at : at + LANES] = best
    loads[3].wait()


def pack(group, params, target, hit_shard, hit_local, shards):
    columns = params.shape[1]
    tile_count, listed = hit_local.shape
    width = target.shape[1]
    rows = 4 + tile_count * (columns // width)
    args = (hit_shard.reshape(tile_count, 1, listed), hit_local, target, params)
    return call(
        functools.partial(pack_kernel, shards),
        "pack",
        (jax.ShapeDtypeStruct((rows, width), F32), jax.ShapeDtypeStruct(params.shape, F32)),
        [smem()] + [pl.BlockSpec(memory_space=pltpu.HBM)] * 4,
        [
            pltpu.VMEM((tile_count, 1, listed), jnp.int32),
            pltpu.VMEM((tile_count, listed), jnp.int32),
            pltpu.VMEM(target.shape, F32),
            pltpu.VMEM((listed, LANES), F32),
            pltpu.SemaphoreType.DMA((4,)),
        ],
        (group.reshape(1),) + tuple(pltpu.with_memory_space_constraint(a, pltpu.HBM) for a in args),
        (vmem(), any_space()),
    )


def sent_rows(views):
    return (11 + 3 * views + 7) // 8 * 8


def cut_kernel(pieces, where, cams, params, *refs):
    parts, (feats, rows) = refs[:pieces], refs[pieces:]
    views = cams.shape[0]
    count = sent_rows(views)
    slabs = spread_features([params], feats, params.shape[0])

    def feat(f):
        return feats[f * slabs : (f + 1) * slabs, :]

    values = [feat(f) for f in range(11)]
    for v in range(views):
        values += shade(feat, [cams[v, i] for i in range(12)])
    values += [jnp.zeros((slabs, LANES), F32)] * (count - len(values))
    for f, value in enumerate(values):
        rows[pl.ds(f, slabs, stride=count), :] = value
    each = slabs // pieces
    for d in range(pieces):
        for h in range(each):
            first = (((where[0] ^ d) % pieces) * each + h) * count
            parts[d][:, h * LANES : (h + 1) * LANES] = rows[
                pl.ds(pl.multiple_of(first, 8), count), :
            ]


def cut(group, cameras, params, pieces):
    features, columns = params.shape
    slabs = columns // LANES
    count = sent_rows(cameras.shape[0])
    return list(
        call(
            functools.partial(cut_kernel, pieces),
            "cut",
            (jax.ShapeDtypeStruct((count, columns // pieces), F32),) * pieces,
            [smem()] * 2 + [vmem()],
            [
                pltpu.VMEM((features * slabs, LANES), F32),
                pltpu.VMEM((count * slabs, LANES), F32),
            ],
            (group.reshape(1), cameras, params),
        )
    )


def lane_gather(source, lane):
    return jnp.take_along_axis(source, lane, axis=1, mode="promise_in_bounds")


def pixel_basis(pixels):
    pixel = lax.broadcasted_iota(jnp.int32, (8, pixels), 1)
    row = lax.broadcasted_iota(jnp.int32, (8, pixels), 0)
    middle = 0.5 * TILE_SIDE - 0.5
    u = (pixel % TILE_SIDE).astype(F32) - middle
    v = (pixel // TILE_SIDE).astype(F32) - middle
    value = jnp.where(row == 0, 1.0, 0.0)
    for at, term in ((1, u), (2, v), (3, u * u), (4, u * v), (5, v * v)):
        value = jnp.where(row == at, term, value)
    return value


def composite(tiles, first_group, me, rows, info_s, rendered, work):
    alpha_s, weight_s, pull_s, push_s, weight_2, entry_s, coef_s, colour_s, sums_s, index_s, acc_s, ninth_s = work
    groups = info_s.shape[0]
    listed = acc_s.shape[0] * LANES
    tile_count = info_s.shape[2] // listed
    pixels = info_s.shape[2] // tile_count
    parts = pixels // LANES
    halves = listed // LANES
    tiles_here = groups * tile_count
    spans = tiles_here * parts
    slabs = rows.shape[0] // ROWS
    side = TILE_SIDE
    first_col, first_row = tiles

    def of_span(span):
        return pl.ds(span * SPAN_STEP, listed, stride=LIST_STEP)

    def of_place(place):
        return pl.ds(place * LIST_STEP, spans, stride=SPAN_STEP)

    basis = pixel_basis(pixels)
    basis_3 = jnp.concatenate([basis, basis, basis], axis=0).astype(BF16)
    row_of = lax.broadcasted_iota(jnp.int32, (8, listed), 0)

    entries = []
    for n in range(tiles_here):
        g, t = n // tile_count, n % tile_count
        found = []
        for h in range(halves):
            first = t * listed + h * LANES
            at = info_s[g, 3:4, first : first + LANES].astype(jnp.int32)
            index_s[n * halves + h : n * halves + h + 1, :] = at
            at = jnp.broadcast_to(at, (8, LANES))
            lane, slab = at & (LANES - 1), at >> 7
            value = lane_gather(rows[0:8, :], lane)
            for s in range(1, slabs):
                value = jnp.where(
                    slab == s, lane_gather(rows[s * ROWS : s * ROWS + 8, :], lane), value
                )
            found.append(value)
        entries.append(jnp.concatenate(found, axis=1))
        for h in range(halves):
            entry_s[h, 8 * n : 8 * n + 8, :] = found[h]
    at = index_s[...]
    lane, slab = at & (LANES - 1), at >> 7
    ninth = lane_gather(rows[8:16, :], lane)
    for s in range(1, slabs):
        ninth = jnp.where(
            slab == s, lane_gather(rows[s * ROWS + 8 : s * ROWS + 16, :], lane), ninth
        )

    def of_lists(ref, f):
        at = pl.ds(f, tiles_here, stride=8)
        return jnp.concatenate([ref[h, at, :] for h in range(halves)], axis=1)

    tile_of = lax.broadcasted_iota(jnp.int32, (tiles_here, listed), 0)
    slot = (me ^ (first_group + tile_of // tile_count)) * tile_count + tile_of % tile_count
    mean_u = of_lists(entry_s, 2) - (((first_col + slot % 4) * side).astype(F32) + 0.5 * side)
    mean_v = of_lists(entry_s, 3) - (((first_row + slot // 4) * side).astype(F32) + 0.5 * side)
    quad_a = -0.5 * of_lists(entry_s, 4)
    quad_b = -of_lists(entry_s, 5)
    quad_c = -0.5 * of_lists(entry_s, 6)
    slope_u = 2.0 * quad_a * mean_u + quad_b * mean_v
    slope_v = 2.0 * quad_c * mean_v + quad_b * mean_u
    level = 0.5 * (slope_u * mean_u + slope_v * mean_v) + of_lists(entry_s, 7)
    for f, value in enumerate((level, -slope_u, -slope_v, quad_a, quad_b, quad_c)):
        for n in range(tiles_here):
            coef_s[f : f + 1, n * listed : (n + 1) * listed] = value[n : n + 1]
    coef_s[6:8, :] = jnp.zeros((2, tiles_here * listed), F32)
    coef = coef_s[...]
    terms = []
    for _ in range(3):
        terms.append(coef.astype(BF16).astype(F32))
        coef = coef - terms[-1]
    down = ((0,), (0,))
    power = matmul(jnp.concatenate(terms, axis=0).astype(BF16), basis_3, down)
    for n in range(tiles_here):
        for part in range(parts):
            alpha_s[of_span(n * parts + part), :] = jnp.exp(
                power[n * listed : (n + 1) * listed, part * LANES : (part + 1) * LANES]
            )
    colour_s[...] = jnp.zeros(colour_s.shape, F32)
    hues = []
    for n in range(tiles_here):
        last = jnp.concatenate([ninth[n * halves + h : n * halves + h + 1] for h in range(halves)], axis=1)
        colours = jnp.where(row_of < 2, entries[n], jnp.where(row_of == 2, last, 0.0))
        high = colours.astype(BF16).astype(F32)
        low = colours - high
        here = slice(n * listed, (n + 1) * listed)
        for at, value in ((0, high), (8, low), (16, high)):
            colour_s[24 * n + at : 24 * n + at + 8, here] = value
        hues.append(jnp.concatenate([high, low], axis=0).astype(BF16))

    unroll, quad = 32, 4
    steps = listed // unroll

    def forward(step, passed):
        for j in range(0, unroll, quad):
            at = [of_place(step * unroll + j + i) for i in range(quad)]
            alpha = [alpha_s[at[i], :] for i in range(quad)]
            keep = [1.0 - alpha[i] for i in range(quad)]
            two = keep[0] * keep[1]
            three = two * keep[2]
            weight_s[at[0], :] = alpha[0] * passed
            weight_s[at[1], :] = (alpha[1] * keep[0]) * passed
            weight_s[at[2], :] = (alpha[2] * two) * passed
            weight_s[at[3], :] = (alpha[3] * three) * passed
            passed = passed * (two * (keep[2] * keep[3]))
        return passed

    nought = jnp.zeros((spans, LANES), F32)
    lax.fori_loop(0, steps, forward, nought + 1.0)

    errors, wrongs, moments = [], [], []
    for n in range(tiles_here):
        g, t = n // tile_count, n % tile_count
        for part in range(parts):
            at = slice((n * parts + part) * LANES, (n * parts + part + 1) * LANES)
            weight_2[:listed, at], weight_2[listed:, at] = split(
                weight_s[of_span(n * parts + part), :]
            )
        at = slice(n * pixels, (n + 1) * pixels)
        image = matmul(hues[n], weight_2[:listed, at])
        image = image[0:8] + image[8:16] + matmul(hues[n], weight_2[listed:, at])[0:8]
        here = slice(t * pixels, (t + 1) * pixels)
        if rendered is not None and g == 0:
            rendered[:, here] = image[0:3]
        error = image - info_s[g, 0:8, here]
        high = error.astype(BF16).astype(F32)
        low = error - high
        errors += [high, high, low]

        def block(values, first, total):
            rows_in = sum(value.shape[0] for value in values)
            return jnp.concatenate(
                [jnp.zeros((first, pixels), F32)] * (first > 0)
                + values
                + [jnp.zeros((total - first - rows_in, pixels), F32)],
                axis=0,
            ).astype(BF16)

        wrongs.append(block([high, low], 16 * n, LANES))
        moments.append(block([basis], 16 * tiles_here + 8 * n, LANES))
    pull = matmul(colour_s[...].astype(BF16), jnp.concatenate(errors, axis=0).astype(BF16), down)
    for n in range(tiles_here):
        for part in range(parts):
            pull_s[of_span(n * parts + part), :] = pull[
                n * listed : (n + 1) * listed, part * LANES : (part + 1) * LANES
            ]

    def backward(back, behind):
        for j in range(0, unroll, quad):
            at = [of_place(listed - 1 - (back * unroll + j + i)) for i in range(quad)]
            alpha = [alpha_s[at[i], :] for i in range(quad)]
            pull = [pull_s[at[i], :] for i in range(quad)]
            keep = [1.0 - alpha[i] for i in range(quad)]
            own = alpha[0] * pull[0]
            seen, through = behind, keep[0]
            for i in range(quad):
                push_s[at[i], :] = weight_s[at[i], :] * (pull[i] - seen)
                if i > 0:
                    own = own * keep[i] + alpha[i] * pull[i]
                    through = through * keep[i]
                seen = behind * through + own
            behind = seen
        return behind

    lax.fori_loop(0, steps, backward, nought)

    across = ((1,), (1,))
    high, low = split(jnp.concatenate([push_s[of_span(span), :] for span in range(spans)], axis=1))
    sums = matmul(weight_2[...], jnp.concatenate(wrongs, axis=1), across)
    sums = sums + matmul(
        jnp.concatenate([high, low], axis=0), jnp.concatenate(moments, axis=1), across
    )
    sums = (sums[:listed] + sums[listed:]).T
    for h in range(halves):
        sums_s[h] = sums[:, h * LANES : (h + 1) * LANES]
    m_00, m_10, m_01, m_20, m_11, m_02 = [
        of_lists(sums_s, 16 * tiles_here + m) for m in range(6)
    ]
    n_10 = m_10 - mean_u * m_00
    n_01 = m_01 - mean_v * m_00
    for n in range(tiles_here):
        for h in range(halves):
            grads = sums_s[h, 16 * n : 16 * n + 8, :] + sums_s[h, 16 * n + 8 : 16 * n + 16, :]
            acc_s[h, 8 * n : 8 * n + 8, :] = grads
            row = n * halves + h
            ninth_s[row : row + 1, :] = grads[2:3, :]
    for f, value in (
        (2, -(2.0 * quad_a * n_10 + quad_b * n_01)),
        (3, -(2.0 * quad_c * n_01 + quad_b * n_10)),
        (4, -0.5 * (m_20 - mean_u * (m_10 + n_10))),
        (5, -(m_11 - mean_u * m_01 - mean_v * n_10)),
        (6, -0.5 * (m_02 - mean_v * (m_01 + n_01))),
        (7, m_00),
    ):
        for h in range(halves):
            acc_s[h, pl.ds(f, tiles_here, stride=8), :] = value[:, h * LANES : (h + 1) * LANES]


def pool_sum(slab, info_s, acc_s, ninth_s):
    groups, _, width = info_s.shape
    listed = acc_s.shape[0] * LANES
    tile_count = width // listed
    halves = listed // LANES
    rows_each = (info_s.shape[1] - 4) // tile_count
    row_of = lax.broadcasted_iota(jnp.int32, (8, LANES), 0)

    totals, every = [], None
    for g in range(groups):
        total = jnp.zeros((8, LANES), F32)
        for t in range(tile_count):
            row, first = 4 + t * rows_each + slab * LANES // width, slab * LANES % width
            at = info_s[g, row : row + 1, first : first + LANES].astype(jnp.int32)
            at = jnp.broadcast_to(at, (8, LANES))
            n = g * tile_count + t
            every = at if every is None else jnp.where(row_of >= n * halves, at, every)
            lane, half = at & (LANES - 1), at >> 7
            for h in range(halves):
                here = lane_gather(acc_s[h, 8 * n : 8 * n + 8, :], lane)
                total = total + jnp.where(half == h, here, 0.0)
        totals.append(total)
    here = lane_gather(ninth_s[...], every & (LANES - 1))
    ninth = jnp.where(every >> 7 == row_of % halves, here, 0.0)
    return totals[0] + totals[1], jnp.sum(ninth, axis=0, keepdims=True)


def block_start(tile_id):
    within = tile_id % (TILES_X * TILES_Y)
    return (within % TILES_X) // 4 * 4, (within // TILES_X) // 2 * 2


def near_kernel(pieces, tile_ids, cams, where, own, other, *refs):
    parts = refs[:pieces]
    rendered, rows, partial, feats, info_s, *work = refs[pieces:]
    view = tile_ids[0] // (TILES_X * TILES_Y)
    cam = [cams[view, i] for i in range(12)]
    slabs = spread_features(parts, feats, parts[0].shape[0])
    projected = project_rows(lambda f: feats[f * slabs : (f + 1) * slabs, :], cam)
    colours = []
    for k in range(3):
        first = pl.multiple_of((11 + 3 * view + k) * slabs, slabs)
        colours.append(feats[pl.ds(first, slabs), :])
    for f, value in enumerate(colours[:2] + projected + [colours[2]] * 8):
        rows[pl.ds(f, slabs, stride=ROWS), :] = value
    info_s[0] = own[...]
    info_s[1] = other[...]
    composite(block_start(tile_ids[0]), 0, where[0], rows, info_s, rendered, work)
    for s in range(slabs):
        at = slice(s * LANES, (s + 1) * LANES)
        partial[0:8, at], partial[8:9, at] = pool_sum(s, info_s, *work[-2:])


def far_kernel(blocks, tile_ids, where, rows, partial, infos, *refs):
    *packets, info_s = refs[: len(refs) - 12]
    work = refs[len(refs) - 12 :]
    half = infos.shape[0] // 2
    info_s[0] = infos[:half, :]
    info_s[1] = infos[half:, :]
    composite(block_start(tile_ids[0]), 2, where[0], rows, info_s, None, work)
    share = (tile_ids[0] // (TILES_X * TILES_Y)).astype(F32)
    row_of = lax.broadcasted_iota(jnp.int32, (8, LANES), 0)
    lane_of = lax.broadcasted_iota(jnp.int32, (8, LANES), 1)
    chunk = packets[0].shape[1]
    for s in range(rows.shape[0] // ROWS):
        total, ninth = pool_sum(s, info_s, *work[-2:])
        total = total + partial[0:8, s * LANES : (s + 1) * LANES]
        ninth = ninth + partial[8:9, s * LANES : (s + 1) * LANES]
        if blocks == 1:
            mine = share
        else:
            column = s * LANES + lane_of
            mine = jnp.where(column % where[2] // (where[2] // blocks) == where[1], share, 0.0)
        at = slice(s * LANES % chunk, s * LANES % chunk + LANES)
        packets[s * LANES // chunk][0:8, at] = total
        packets[s * LANES // chunk][8:16, at] = jnp.where(
            row_of == 0, jnp.broadcast_to(ninth, (8, LANES)), mine
        )


def join_kernel(first, second, out):
    half = first.shape[0]
    out[:half, :] = first[...]
    out[half:, :] = second[...]


def update_kernel(pieces, follows, where, cams, params, adam_m, adam_v, *refs):
    packets, refs = refs[:pieces], refs[pieces + 3 * follows :]
    sinks, (feats, rows, grads, made, sems) = refs[:3], refs[3:]
    features = params.shape[0]
    chunk = packets[0].shape[1]
    width = pieces * chunk
    slabs = width // LANES
    start = (where[0] ^ where[1]) // pieces * pieces * chunk
    for d in range(pieces):
        for h in range(chunk // LANES):
            slab = (where[0] ^ where[1] ^ d) % pieces * (chunk // LANES) + h
            rows[pl.ds(slab, ROWS, stride=slabs), :] = packets[d][:, h * LANES : (h + 1) * LANES]
    pulled = [rows[f * slabs : (f + 1) * slabs, :] for f in range(10)]
    view = pulled[9]
    cam = []
    for i in range(12):
        value = jnp.full((slabs, LANES), cams[0, i], F32)
        for v in range(1, cams.shape[0]):
            value = jnp.where(view == float(v), cams[v, i], value)
        cam.append(value)

    def put(f, value):
        grads[f * slabs : (f + 1) * slabs, :] = value

    def column(s):
        return pl.ds(pl.multiple_of(start + s * LANES, LANES), LANES)

    for s in range(slabs):
        for row in range(0, features, 8):
            count = min(8, features - row)
            feats[pl.ds(row * slabs + s, count, stride=slabs), :] = params[
                row : row + count, column(s)
            ]
    project_pull(
        lambda f: feats[f * slabs : (f + 1) * slabs, :], cam, pulled[2:8] + pulled[:2] + pulled[8:9], put
    )
    rate = learn_rate / (1.0 - beta_one**adam_steps)
    unbias = 1.0 / (1.0 - beta_two**adam_steps)
    stores = []
    order = list(range(16, features, 8)) + [0, 8]
    for row in order:
        count = min(8, features - row)
        span = slice(row, row + count)
        for s in range(slabs):
            here = (span, slice(s * LANES, (s + 1) * LANES))
            grad = grads[pl.ds(row * slabs + s, count, stride=slabs), :]
            moment = beta_one * adam_m[span, column(s)] + (1.0 - beta_one) * grad
            second = beta_two * adam_v[span, column(s)] + (1.0 - beta_two) * grad * grad
            made.at[1][here] = moment
            made.at[2][here] = second
            made.at[0][here] = params[span, column(s)] - rate * moment / (
                jnp.sqrt(second * unbias) + adam_eps
            )
        if row % 16 == 8 or row + count == features:
            first = row // 16 * 16
            span = pl.ds(first, row + count - first)
            columns = pl.ds(pl.multiple_of(start, LANES), width)
            for k in range(3):
                store = pltpu.make_async_copy(
                    made.at[k, span], sinks[k].at[span, columns], sems.at[k, first // 16]
                )
                store.start()
                stores.append(store)
    for store in stores:
        store.wait()


def vmem():
    return pl.BlockSpec(memory_space=pltpu.VMEM)


def smem():
    return pl.BlockSpec(memory_space=pltpu.SMEM)


def any_space():
    return pl.BlockSpec(memory_space=pl.ANY)


def call(kernel, name, out_shape, in_specs, scratch, args, out_specs=None, grant=32):
    return pl.pallas_call(
        kernel,
        out_shape=out_shape,
        in_specs=in_specs,
        out_specs=out_specs or tuple(vmem() for _ in out_shape),
        scratch_shapes=scratch,
        compiler_params=pltpu.CompilerParams(vmem_limit_bytes=grant * 1024 * 1024),
        name=name,
    )(*args)


def work_shapes(tile_count, pixels, listed):
    tiles = 2 * tile_count
    spans = tiles * pixels // LANES
    assert (spans - 1) * SPAN_STEP < LIST_STEP and tiles * listed // LANES == 8 and tiles == 4
    return [pltpu.VMEM((listed * LIST_STEP, LANES), F32)] * 4 + [
        pltpu.VMEM((2 * listed, spans * LANES), BF16),
        pltpu.VMEM((listed // LANES, 8 * tiles, LANES), F32),
        pltpu.VMEM((8, tiles * listed), F32),
        pltpu.VMEM((24 * tiles, tiles * listed), F32),
        pltpu.VMEM((listed // LANES, LANES, LANES), F32),
        pltpu.VMEM((8, LANES), jnp.int32),
        pltpu.VMEM((listed // LANES, 8 * tiles, LANES), F32),
        pltpu.VMEM((8, LANES), F32),
    ]


def near(tile_ids, cameras, where, own, other, parts, tile_count):
    width = sum(part.shape[1] for part in parts)
    features = parts[0].shape[0]
    slabs = width // LANES
    pixels = listed = own.shape[1] // tile_count
    return call(
        functools.partial(near_kernel, len(parts)),
        "near",
        (
            jax.ShapeDtypeStruct((3, own.shape[1]), F32),
            jax.ShapeDtypeStruct((ROWS * slabs, LANES), F32),
            jax.ShapeDtypeStruct((ROWS, width), F32),
        ),
        [smem()] * 3 + [vmem()] * (2 + len(parts)),
        [pltpu.VMEM((features * slabs, LANES), F32), pltpu.VMEM((2,) + own.shape, F32)]
        + work_shapes(tile_count, pixels, listed),
        (tile_ids, cameras, where, own, other, *parts),
    )


def far(tile_ids, where, rows, partial, infos, pieces, tile_count, blocks):
    width = partial.shape[1]
    pixels = listed = infos.shape[1] // tile_count
    info = (infos.shape[0] // 2, infos.shape[1])
    return call(
        functools.partial(far_kernel, blocks),
        "far",
        (jax.ShapeDtypeStruct((ROWS, width // pieces), F32),) * pieces,
        [smem()] * 2 + [vmem()] * 3,
        [pltpu.VMEM((2,) + info, F32)] + work_shapes(tile_count, pixels, listed),
        (tile_ids, where, rows, partial, infos),
    )


def join(first, second):
    shape = (2 * first.shape[0], first.shape[1])
    return call(
        join_kernel, "join", (jax.ShapeDtypeStruct(shape, F32),), [vmem()] * 2, [], (first, second)
    )[0]


def update(own, first, cameras, params, adam_m, adam_v, packets, before):
    features = params.shape[0]
    width = sum(packet.shape[1] for packet in packets)
    slabs = width // LANES
    shape = jax.ShapeDtypeStruct(params.shape, F32)
    at = 5 + len(packets)
    return pl.pallas_call(
        functools.partial(update_kernel, len(packets), len(before) > 0),
        out_shape=(shape, shape, shape),
        in_specs=[smem()] * 2
        + [vmem()] * (3 + len(packets))
        + [any_space()] * len(before),
        out_specs=(any_space(),) * 3,
        scratch_shapes=[
            pltpu.VMEM((features * slabs, LANES), F32),
            pltpu.VMEM((ROWS * slabs, LANES), F32),
            pltpu.VMEM((features * slabs, LANES), F32),
            pltpu.VMEM((3, features, width), F32),
            pltpu.SemaphoreType.DMA((3, (features + 15) // 16)),
        ],
        input_output_aliases={at + k: k for k in range(len(before))},
        compiler_params=pltpu.CompilerParams(vmem_limit_bytes=32 * 1024 * 1024),
        name="update",
    )(
        jnp.stack([own, jnp.int32(first)]).astype(jnp.int32),
        cameras, params, adam_m, adam_v, *packets, *before,
    )


def swap(value, axis, d):
    if d == 0:
        return value
    return lax.ppermute(value, axis, [(k, k ^ d) for k in range(lax.axis_size(axis))])


def local(params, adam_m, adam_v, cameras, target, tile_ids, hit_shard, hit_local):
    width = params.shape[1]
    tile_count, listed = hit_local.shape
    shards = lax.axis_size("gs")
    along = lax.axis_size("tile")
    chunk = width // shards
    group = lax.axis_index("gs")
    seat = lax.axis_index("tile")
    aligned = chunk % LANES == 0
    team = BLOCK_TILES // tile_count
    assert team == 4
    blocks = along // team

    info, params = pack(group, params, target, hit_shard, hit_local, shards)
    parts = cut(group, cameras, params, shards if aligned else 1)
    if not aligned:
        parts = [
            lax.dynamic_slice_in_dim(parts[0], (group ^ d) * chunk, chunk, axis=1)
            for d in range(shards)
        ]
    parts = [swap(parts[d], "gs", d) for d in range(shards)]
    beside = swap(info, "tile", 1)
    beyond = swap(join(info, beside), "tile", 2)
    if not aligned:
        parts = [jnp.concatenate(parts, axis=1)]
    where = jnp.stack([seat % team, seat // team, jnp.int32(chunk)]).astype(jnp.int32)
    rendered, rows, partial = near(tile_ids, cameras, where, info, beside, parts, tile_count)
    packets = far(tile_ids, where, rows, partial, beyond, len(parts), tile_count, blocks)
    if not aligned:
        packets = [packets[0][:, d * chunk : (d + 1) * chunk] for d in range(shards)]
    packets = [swap(packets[d], "gs", d) for d in range(shards)]
    if blocks > 1:
        packets = [block_sum(packet, along, team) for packet in packets]
    if aligned:
        own = group
    else:
        packets = [jnp.stack(packets)[jnp.arange(shards) ^ group].transpose(1, 0, 2).reshape(ROWS, -1)]
        own = jnp.int32(0)
    made = ()
    count = max(1, len(packets) // 2)
    for first in range(0, len(packets), count):
        made = update(
            own, first, cameras, params, adam_m, adam_v, packets[first : first + count], made
        )
    new_params, new_m, new_v = made
    return (rendered, new_params, new_m, new_v)


def block_sum(packet, along, team):
    step = team
    while step < along:
        packet = packet + swap(packet, "tile", step)
        step *= 2
    return packet


def solution(mesh):
    return jax.shard_map(
        local,
        mesh=mesh,
        in_specs=(
            P(None, ("groups", "gs")),
            P(None, ("groups", "gs")),
            P(None, ("groups", "gs")),
            P("groups", None),
            P(None, ("groups", "gs", "tile")),
            P(("groups", "gs", "tile")),
            P(("groups", "gs", "tile"), None, None),
            P(("groups", "gs", "tile"), None),
        ),
        out_specs=(
            P(None, ("groups", "gs", "tile")),
            P(None, ("groups", "gs")),
            P(None, ("groups", "gs")),
            P(None, ("groups", "gs")),
        ),
        check_vma=False,
    )
```

```python
import functools

import jax
import jax.numpy as jnp
from jax import lax
from jax.experimental import pallas as pl
from jax.experimental.pallas import tpu as pltpu
from jax.sharding import PartitionSpec as P

TILES_X = 120
TILES_Y = 68
TILE_SIDE = 16
BLOCK_TILES = 8
LANES = 128
ROWS = 16
LIST_STEP = 9
F32 = jnp.float32
BF16 = jnp.bfloat16

focal_length = 1000.0
center_x = 960.0
center_y = 540.0
dilation = 0.3
beta_one = 0.9
beta_two = 0.999
learn_rate = 0.01
adam_eps = 1e-08
adam_steps = 100.0
sh_const = (
    0.28209479177387814,
    0.4886025119029199,
    1.0925484305920792,
    0.31539156525252005,
    0.5462742152960396,
    0.5900435899266435,
    2.890611442640554,
    0.4570457994644658,
    0.3731763325901154,
    1.445305721320277,
)


def sh_basis(x, y, z):
    s = sh_const
    xx, yy, zz = x * x, y * y, z * z
    return [
        None,
        -s[1] * y,
        s[1] * z,
        -s[1] * x,
        s[2] * (x * y),
        -s[2] * (y * z),
        s[3] * (2.0 * zz - xx - yy),
        -s[2] * (x * z),
        s[4] * (xx - yy),
        -s[5] * y * (3.0 * xx - yy),
        s[6] * (x * y) * z,
        -s[7] * y * (4.0 * zz - xx - yy),
        s[8] * z * (2.0 * zz - 3.0 * xx - 3.0 * yy),
        -s[7] * x * (4.0 * zz - xx - yy),
        s[9] * z * (xx - yy),
        -s[5] * x * (xx - 3.0 * yy),
    ]


def sh_pull(h, x, y, z):
    s = sh_const
    xx, yy, zz = x * x, y * y, z * z
    xy, xz, yz = x * y, x * z, y * z
    diff = xx - yy
    ring = 4.0 * zz - xx - yy
    g_x = (
        -s[1] * h[3]
        + s[2] * (h[4] * y - h[7] * z)
        - (2.0 * s[3]) * h[6] * x
        + (2.0 * s[4]) * h[8] * x
        - (6.0 * s[5]) * h[9] * xy
        + s[6] * h[10] * yz
        + (2.0 * s[7]) * h[11] * xy
        - (6.0 * s[8]) * h[12] * xz
        - s[7] * h[13] * (ring - 2.0 * xx)
        + (2.0 * s[9]) * h[14] * xz
        - (3.0 * s[5]) * h[15] * diff
    )
    g_y = (
        -s[1] * h[1]
        + s[2] * (h[4] * x - h[5] * z)
        - (2.0 * s[3]) * h[6] * y
        - (2.0 * s[4]) * h[8] * y
        - (3.0 * s[5]) * h[9] * diff
        + s[6] * h[10] * xz
        - s[7] * h[11] * (ring - 2.0 * yy)
        - (6.0 * s[8]) * h[12] * yz
        + (2.0 * s[7]) * h[13] * xy
        - (2.0 * s[9]) * h[14] * yz
        + (6.0 * s[5]) * h[15] * xy
    )
    g_z = (
        s[1] * h[2]
        - s[2] * (h[5] * y + h[7] * x)
        + (4.0 * s[3]) * h[6] * z
        + s[6] * h[10] * xy
        - (8.0 * s[7]) * (h[11] * yz + h[13] * xz)
        + s[8] * h[12] * (6.0 * zz - 3.0 * xx - 3.0 * yy)
        + s[9] * h[14] * diff
    )
    return g_x, g_y, g_z


def project_parts(feat, cam):
    rot = [[cam[3 * r + c] for c in range(3)] for r in range(3)]
    off = [feat(a) - cam[9 + a] for a in range(3)]
    in_cam = [rot[r][0] * off[0] + rot[r][1] * off[1] + rot[r][2] * off[2] for r in range(3)]
    inv = 1.0 / in_cam[2]
    u = in_cam[0] * inv
    v = in_cam[1] * inv
    finv = focal_length * inv
    scale = [jnp.exp(2.0 * feat(3 + a)) for a in range(3)]
    quat = [feat(6 + a) for a in range(4)]
    rnorm = lax.rsqrt(quat[0] * quat[0] + quat[1] * quat[1] + quat[2] * quat[2] + quat[3] * quat[3])
    w, x, y, z = [q * rnorm for q in quat]
    turn = [
        [1.0 - 2.0 * (y * y + z * z), 2.0 * (x * y - w * z), 2.0 * (x * z + w * y)],
        [2.0 * (x * y + w * z), 1.0 - 2.0 * (x * x + z * z), 2.0 * (y * z - w * x)],
        [2.0 * (x * z - w * y), 2.0 * (y * z + w * x), 1.0 - 2.0 * (x * x + y * y)],
    ]
    screen = [
        [finv * (rot[0][c] - u * rot[2][c]) for c in range(3)],
        [finv * (rot[1][c] - v * rot[2][c]) for c in range(3)],
    ]
    axes = [
        [sum(screen[r][c] * turn[c][k] for c in range(3)) for k in range(3)] for r in range(2)
    ]
    wide = [[axes[r][k] * scale[k] for k in range(3)] for r in range(2)]
    cov_xx = sum(wide[0][k] * axes[0][k] for k in range(3)) + dilation
    cov_xy = sum(wide[0][k] * axes[1][k] for k in range(3))
    cov_yy = sum(wide[1][k] * axes[1][k] for k in range(3)) + dilation
    rdet = 1.0 / (cov_xx * cov_yy - cov_xy * cov_xy)
    conic = (cov_yy * rdet, -cov_xy * rdet, cov_xx * rdet)
    rlen = lax.rsqrt(off[0] * off[0] + off[1] * off[1] + off[2] * off[2])
    way = [off[a] * rlen for a in range(3)]
    return dict(
        rot=rot, inv=inv, u=u, v=v, finv=finv, scale=scale, rnorm=rnorm, rotor=(w, x, y, z), turn=turn,
        screen=screen, axes=axes, wide=wide, conic=conic, rlen=rlen, way=way,
    )


def shade(feat, cam):
    off = [feat(a) - cam[9 + a] for a in range(3)]
    rlen = lax.rsqrt(off[0] * off[0] + off[1] * off[1] + off[2] * off[2])
    basis = sh_basis(*[off[a] * rlen for a in range(3)])
    colours = []
    for k in range(3):
        total = 0.5 + sh_const[0] * feat(11 + 16 * k)
        for b in range(1, 16):
            total = total + feat(11 + 16 * k + b) * basis[b]
        colours.append(total)
    return colours


def project_rows(feat, cam):
    part = project_parts(feat, cam)
    mean_x = focal_length * part["u"] + center_x
    mean_y = focal_length * part["v"] + center_y
    logit = feat(10)
    log_opacity = jnp.minimum(logit, 0.0) - jnp.log(1.0 + jnp.exp(-jnp.abs(logit)))
    return [mean_x, mean_y, *part["conic"], log_opacity]


def project_pull(feat, cam, grads, put):
    part = project_parts(feat, cam)
    g_mx, g_my, g_a, g_b, g_c, g_o = grads[:6]
    g_col = grads[6:9]
    way, rlen = part["way"], part["rlen"]
    basis = sh_basis(*way)
    pulled = [None]
    for k in range(3):
        put(11 + 16 * k, sh_const[0] * g_col[k])
    for b in range(1, 16):
        total = 0.0
        for k in range(3):
            put(11 + 16 * k + b, g_col[k] * basis[b])
            total = total + g_col[k] * feat(11 + 16 * k + b)
        pulled.append(total)
    g_way = sh_pull(pulled, *way)
    along = way[0] * g_way[0] + way[1] * g_way[1] + way[2] * g_way[2]
    g_off = [(g_way[a] - way[a] * along) * rlen for a in range(3)]
    put(10, g_o / (1.0 + jnp.exp(feat(10))))
    a, b, c = part["conic"]
    g_xx = -(a * a * g_a + a * b * g_b + b * b * g_c)
    g_xy = -(2.0 * a * b * g_a + (a * c + b * b) * g_b + 2.0 * b * c * g_c)
    g_yy = -(b * b * g_a + b * c * g_b + c * c * g_c)
    axes, wide, turn, screen = part["axes"], part["wide"], part["turn"], part["screen"]
    for k in range(3):
        g_scale = (
            g_xx * axes[0][k] * wide[0][k]
            + g_xy * axes[0][k] * wide[1][k]
            + g_yy * axes[1][k] * wide[1][k]
        )
        put(3 + k, 2.0 * g_scale)
    g_axes = [
        [2.0 * g_xx * wide[0][k] + g_xy * wide[1][k] for k in range(3)],
        [2.0 * g_yy * wide[1][k] + g_xy * wide[0][k] for k in range(3)],
    ]
    g_screen = [
        [sum(g_axes[r][k] * turn[c][k] for k in range(3)) for c in range(3)] for r in range(2)
    ]
    gm = [
        [g_axes[0][k] * screen[0][c] + g_axes[1][k] * screen[1][c] for k in range(3)]
        for c in range(3)
    ]
    w, x, y, z = part["rotor"]
    up_xy, up_xz, up_yz = gm[0][1] + gm[1][0], gm[0][2] + gm[2][0], gm[1][2] + gm[2][1]
    un_xy, un_xz, un_yz = gm[1][0] - gm[0][1], gm[0][2] - gm[2][0], gm[2][1] - gm[1][2]
    g_rotor = [
        2.0 * (z * un_xy + y * un_xz + x * un_yz),
        2.0 * (y * up_xy + z * up_xz + w * un_yz - 2.0 * x * (gm[1][1] + gm[2][2])),
        2.0 * (x * up_xy + z * up_yz + w * un_xz - 2.0 * y * (gm[0][0] + gm[2][2])),
        2.0 * (x * up_xz + y * up_yz + w * un_xy - 2.0 * z * (gm[0][0] + gm[1][1])),
    ]
    rotor = (w, x, y, z)
    along = sum(rotor[i] * g_rotor[i] for i in range(4))
    for i in range(4):
        put(6 + i, (g_rotor[i] - rotor[i] * along) * part["rnorm"])
    rot, inv, finv, u, v = part["rot"], part["inv"], part["finv"], part["u"], part["v"]
    g_u = focal_length * g_mx - finv * sum(g_screen[0][c] * rot[2][c] for c in range(3))
    g_v = focal_length * g_my - finv * sum(g_screen[1][c] * rot[2][c] for c in range(3))
    g_f = sum(g_screen[r][c] * screen[r][c] for r in range(2) for c in range(3))
    g_in = [g_u * inv, g_v * inv, -(g_f + g_u * u + g_v * v) * inv]
    for axis in range(3):
        put(
            axis,
            g_off[axis] + rot[0][axis] * g_in[0] + rot[1][axis] * g_in[1] + rot[2][axis] * g_in[2],
        )


def split(value):
    high = value.astype(BF16)
    return high, (value - high.astype(F32)).astype(BF16)


def matmul(a, b, dims=((1,), (0,))):
    return lax.dot_general(a, b, (dims, ((), ())), preferred_element_type=F32)


def spread_features(parts, scratch, count):
    tiles = sum(part.shape[1] for part in parts) // LANES
    at = 0
    for part in parts:
        for first in range(0, part.shape[1], LANES):
            for row in range(0, count, 8):
                rows = min(8, count - row)
                scratch[pl.ds(row * tiles + at, rows, stride=tiles), :] = part[
                    row : row + rows, first : first + LANES
                ]
            at += 1
    return tiles


def pack_kernel(shards, where, *refs):
    sources, (info, params, shard_of, local_of, goal, place_s, sems) = refs[:4], refs[4:]
    group = where[0]
    loads = [
        pltpu.make_async_copy(source, held, sems.at[k])
        for k, (source, held) in enumerate(zip(sources, (shard_of, local_of, goal, params)))
    ]
    for load in loads:
        load.start()
    for load in loads[:3]:
        load.wait()
    width = info.shape[1]
    tile_count, listed = local_of.shape
    rows_each = (info.shape[0] - 4) // tile_count
    columns = rows_each * width
    chunk = columns // shards
    info[0:3, :] = goal[...]
    for t in range(tile_count):
        place = (shard_of[t] ^ group) * chunk + (local_of[t : t + 1, :] - group * chunk)
        info[3:4, t * listed : (t + 1) * listed] = place.astype(F32)
        row_i = lax.broadcasted_iota(jnp.int32, (LANES, LANES), 0)
        col_i = lax.broadcasted_iota(jnp.int32, (LANES, LANES), 1)
        for first in range(0, listed, LANES):
            spread = jnp.broadcast_to(place[:, first : first + LANES].astype(F32), (LANES, LANES))
            place_s[first : first + LANES, :] = jnp.broadcast_to(
                jnp.sum(jnp.where(row_i == col_i, spread, 0.0), axis=1, keepdims=True), (LANES, LANES)
            )
        lane_of = lax.broadcasted_iota(jnp.int32, (8, LANES), 1).astype(F32)
        row_of = lax.broadcasted_iota(jnp.int32, (8, LANES), 0).astype(F32)
        for s in range(columns // LANES):
            best = jnp.full((8, LANES), -1.0, F32)
            column = lane_of + float(s * LANES)
            for first in range(0, listed, 8):
                best = jnp.where(
                    place_s[first : first + 8, :] == column, row_of + float(first), best
                )
            best = jnp.max(best, axis=0, keepdims=True)
            row, at = 4 + t * rows_each + s * LANES // width, s * LANES % width
            info[row : row + 1, at : at + LANES] = best
    loads[3].wait()


def pack(group, params, target, hit_shard, hit_local, shards):
    columns = params.shape[1]
    tile_count, listed = hit_local.shape
    width = target.shape[1]
    rows = 4 + tile_count * (columns // width)
    args = (hit_shard.reshape(tile_count, 1, listed), hit_local, target, params)
    return call(
        functools.partial(pack_kernel, shards),
        "pack",
        (jax.ShapeDtypeStruct((rows, width), F32), jax.ShapeDtypeStruct(params.shape, F32)),
        [smem()] + [pl.BlockSpec(memory_space=pltpu.HBM)] * 4,
        [
            pltpu.VMEM((tile_count, 1, listed), jnp.int32),
            pltpu.VMEM((tile_count, listed), jnp.int32),
            pltpu.VMEM(target.shape, F32),
            pltpu.VMEM((listed, LANES), F32),
            pltpu.SemaphoreType.DMA((4,)),
        ],
        (group.reshape(1),) + tuple(pltpu.with_memory_space_constraint(a, pltpu.HBM) for a in args),
        (vmem(), any_space()),
    )


def sent_rows(views):
    return (11 + 3 * views + 7) // 8 * 8


def cut_kernel(pieces, where, cams, params, *refs):
    parts, (feats, rows) = refs[:pieces], refs[pieces:]
    views = cams.shape[0]
    count = sent_rows(views)
    slabs = spread_features([params], feats, params.shape[0])

    def feat(f):
        return feats[f * slabs : (f + 1) * slabs, :]

    values = [feat(f) for f in range(11)]
    for v in range(views):
        values += shade(feat, [cams[v, i] for i in range(12)])
    values += [jnp.zeros((slabs, LANES), F32)] * (count - len(values))
    for f, value in enumerate(values):
        rows[pl.ds(f, slabs, stride=count), :] = value
    each = slabs // pieces
    for d in range(pieces):
        for h in range(each):
            first = (((where[0] ^ d) % pieces) * each + h) * count
            parts[d][:, h * LANES : (h + 1) * LANES] = rows[
                pl.ds(pl.multiple_of(first, 8), count), :
            ]


def cut(group, cameras, params, pieces):
    features, columns = params.shape
    slabs = columns // LANES
    count = sent_rows(cameras.shape[0])
    return list(
        call(
            functools.partial(cut_kernel, pieces),
            "cut",
            (jax.ShapeDtypeStruct((count, columns // pieces), F32),) * pieces,
            [smem()] * 2 + [vmem()],
            [
                pltpu.VMEM((features * slabs, LANES), F32),
                pltpu.VMEM((count * slabs, LANES), F32),
            ],
            (group.reshape(1), cameras, params),
        )
    )


def lane_gather(source, lane):
    return jnp.take_along_axis(source, lane, axis=1, mode="promise_in_bounds")


def pixel_basis(pixels):
    pixel = lax.broadcasted_iota(jnp.int32, (8, pixels), 1)
    row = lax.broadcasted_iota(jnp.int32, (8, pixels), 0)
    middle = 0.5 * TILE_SIDE - 0.5
    u = (pixel % TILE_SIDE).astype(F32) - middle
    v = (pixel // TILE_SIDE).astype(F32) - middle
    value = jnp.where(row == 0, 1.0, 0.0)
    for at, term in ((1, u), (2, v), (3, u * u), (4, u * v), (5, v * v)):
        value = jnp.where(row == at, term, value)
    return value


def composite(tiles, first_group, me, rows, info_s, rendered, work):
    alpha_s, weight_s, pull_s, push_s, weight_2, entry_s, coef_s, colour_s, sums_s, index_s, acc_s, ninth_s = work
    groups = info_s.shape[0]
    listed = acc_s.shape[0] * LANES
    tile_count = info_s.shape[2] // listed
    pixels = info_s.shape[2] // tile_count
    parts = pixels // LANES
    halves = listed // LANES
    tiles_here = groups * tile_count
    spans = tiles_here * parts
    slabs = rows.shape[0] // ROWS
    side = TILE_SIDE
    first_col, first_row = tiles

    def of_span(span):
        return pl.ds(span, listed, stride=LIST_STEP)

    def of_place(place):
        return pl.ds(place * LIST_STEP, spans)

    basis = pixel_basis(pixels)
    basis_3 = jnp.concatenate([basis, basis, basis], axis=0).astype(BF16)
    row_of = lax.broadcasted_iota(jnp.int32, (8, listed), 0)

    entries = []
    for n in range(tiles_here):
        g, t = n // tile_count, n % tile_count
        found = []
        for h in range(halves):
            first = t * listed + h * LANES
            at = info_s[g, 3:4, first : first + LANES].astype(jnp.int32)
            index_s[n * halves + h : n * halves + h + 1, :] = at
            at = jnp.broadcast_to(at, (8, LANES))
            lane, slab = at & (LANES - 1), at >> 7
            value = lane_gather(rows[0:8, :], lane)
            for s in range(1, slabs):
                value = jnp.where(
                    slab == s, lane_gather(rows[s * ROWS : s * ROWS + 8, :], lane), value
                )
            found.append(value)
        entries.append(jnp.concatenate(found, axis=1))
        for h in range(halves):
            entry_s[h, 8 * n : 8 * n + 8, :] = found[h]
    at = index_s[...]
    lane, slab = at & (LANES - 1), at >> 7
    ninth = lane_gather(rows[8:16, :], lane)
    for s in range(1, slabs):
        ninth = jnp.where(
            slab == s, lane_gather(rows[s * ROWS + 8 : s * ROWS + 16, :], lane), ninth
        )

    def of_lists(ref, f):
        at = pl.ds(f, tiles_here, stride=8)
        return jnp.concatenate([ref[h, at, :] for h in range(halves)], axis=1)

    tile_of = lax.broadcasted_iota(jnp.int32, (tiles_here, listed), 0)
    slot = (me ^ (first_group + tile_of // tile_count)) * tile_count + tile_of % tile_count
    mean_u = of_lists(entry_s, 2) - (((first_col + slot % 4) * side).astype(F32) + 0.5 * side)
    mean_v = of_lists(entry_s, 3) - (((first_row + slot // 4) * side).astype(F32) + 0.5 * side)
    quad_a = -0.5 * of_lists(entry_s, 4)
    quad_b = -of_lists(entry_s, 5)
    quad_c = -0.5 * of_lists(entry_s, 6)
    slope_u = 2.0 * quad_a * mean_u + quad_b * mean_v
    slope_v = 2.0 * quad_c * mean_v + quad_b * mean_u
    level = 0.5 * (slope_u * mean_u + slope_v * mean_v) + of_lists(entry_s, 7)
    for f, value in enumerate((level, -slope_u, -slope_v, quad_a, quad_b, quad_c)):
        for n in range(tiles_here):
            coef_s[f : f + 1, n * listed : (n + 1) * listed] = value[n : n + 1]
    coef_s[6:8, :] = jnp.zeros((2, tiles_here * listed), F32)
    coef = coef_s[...]
    terms = []
    for _ in range(3):
        terms.append(coef.astype(BF16).astype(F32))
        coef = coef - terms[-1]
    down = ((0,), (0,))
    power = matmul(jnp.concatenate(terms, axis=0).astype(BF16), basis_3, down)
    for n in range(tiles_here):
        for part in range(parts):
            alpha_s[of_span(n * parts + part), :] = jnp.exp(
                power[n * listed : (n + 1) * listed, part * LANES : (part + 1) * LANES]
            )
    colour_s[...] = jnp.zeros(colour_s.shape, F32)
    hues = []
    for n in range(tiles_here):
        last = jnp.concatenate([ninth[n * halves + h : n * halves + h + 1] for h in range(halves)], axis=1)
        colours = jnp.where(row_of < 2, entries[n], jnp.where(row_of == 2, last, 0.0))
        high = colours.astype(BF16).astype(F32)
        low = colours - high
        here = slice(n * listed, (n + 1) * listed)
        for at, value in ((0, high), (8, low), (16, high)):
            colour_s[24 * n + at : 24 * n + at + 8, here] = value
        hues.append(jnp.concatenate([high, low], axis=0).astype(BF16))

    unroll, quad = 32, 4
    steps = listed // unroll

    def forward(step, passed):
        for j in range(0, unroll, quad):
            at = [of_place(step * unroll + j + i) for i in range(quad)]
            alpha = [alpha_s[at[i], :] for i in range(quad)]
            keep = [1.0 - alpha[i] for i in range(quad)]
            two = keep[0] * keep[1]
            three = two * keep[2]
            weight_s[at[0], :] = alpha[0] * passed
            weight_s[at[1], :] = (alpha[1] * keep[0]) * passed
            weight_s[at[2], :] = (alpha[2] * two) * passed
            weight_s[at[3], :] = (alpha[3] * three) * passed
            passed = passed * (two * (keep[2] * keep[3]))
        return passed

    nought = jnp.zeros((spans, LANES), F32)
    lax.fori_loop(0, steps, forward, nought + 1.0)

    errors, wrongs, moments = [], [], []
    for n in range(tiles_here):
        g, t = n // tile_count, n % tile_count
        for part in range(parts):
            at = slice((n * parts + part) * LANES, (n * parts + part + 1) * LANES)
            weight_2[:listed, at], weight_2[listed:, at] = split(
                weight_s[of_span(n * parts + part), :]
            )
        at = slice(n * pixels, (n + 1) * pixels)
        image = matmul(hues[n], weight_2[:listed, at])
        image = image[0:8] + image[8:16] + matmul(hues[n], weight_2[listed:, at])[0:8]
        here = slice(t * pixels, (t + 1) * pixels)
        if rendered is not None and g == 0:
            rendered[:, here] = image[0:3]
        error = image - info_s[g, 0:8, here]
        high = error.astype(BF16).astype(F32)
        low = error - high
        errors += [high, high, low]

        def block(values, first, total):
            rows_in = sum(value.shape[0] for value in values)
            return jnp.concatenate(
                [jnp.zeros((first, pixels), F32)] * (first > 0)
                + values
                + [jnp.zeros((total - first - rows_in, pixels), F32)],
                axis=0,
            ).astype(BF16)

        wrongs.append(block([high, low], 16 * n, LANES))
        moments.append(block([basis], 16 * tiles_here + 8 * n, LANES))
    pull = matmul(colour_s[...].astype(BF16), jnp.concatenate(errors, axis=0).astype(BF16), down)
    for n in range(tiles_here):
        for part in range(parts):
            pull_s[of_span(n * parts + part), :] = pull[
                n * listed : (n + 1) * listed, part * LANES : (part + 1) * LANES
            ]

    def backward(back, behind):
        for j in range(0, unroll, quad):
            at = [of_place(listed - 1 - (back * unroll + j + i)) for i in range(quad)]
            alpha = [alpha_s[at[i], :] for i in range(quad)]
            pull = [pull_s[at[i], :] for i in range(quad)]
            keep = [1.0 - alpha[i] for i in range(quad)]
            own = alpha[0] * pull[0]
            seen, through = behind, keep[0]
            for i in range(quad):
                push_s[at[i], :] = weight_s[at[i], :] * (pull[i] - seen)
                if i > 0:
                    own = own * keep[i] + alpha[i] * pull[i]
                    through = through * keep[i]
                seen = behind * through + own
            behind = seen
        return behind

    lax.fori_loop(0, steps, backward, nought)

    across = ((1,), (1,))
    high, low = split(jnp.concatenate([push_s[of_span(span), :] for span in range(spans)], axis=1))
    sums = matmul(weight_2[...], jnp.concatenate(wrongs, axis=1), across)
    sums = sums + matmul(
        jnp.concatenate([high, low], axis=0), jnp.concatenate(moments, axis=1), across
    )
    sums = (sums[:listed] + sums[listed:]).T
    for h in range(halves):
        sums_s[h] = sums[:, h * LANES : (h + 1) * LANES]
    m_00, m_10, m_01, m_20, m_11, m_02 = [
        of_lists(sums_s, 16 * tiles_here + m) for m in range(6)
    ]
    n_10 = m_10 - mean_u * m_00
    n_01 = m_01 - mean_v * m_00
    for n in range(tiles_here):
        for h in range(halves):
            grads = sums_s[h, 16 * n : 16 * n + 8, :] + sums_s[h, 16 * n + 8 : 16 * n + 16, :]
            acc_s[h, 8 * n : 8 * n + 8, :] = grads
            row = n * halves + h
            ninth_s[row : row + 1, :] = grads[2:3, :]
    for f, value in (
        (2, -(2.0 * quad_a * n_10 + quad_b * n_01)),
        (3, -(2.0 * quad_c * n_01 + quad_b * n_10)),
        (4, -0.5 * (m_20 - mean_u * (m_10 + n_10))),
        (5, -(m_11 - mean_u * m_01 - mean_v * n_10)),
        (6, -0.5 * (m_02 - mean_v * (m_01 + n_01))),
        (7, m_00),
    ):
        for h in range(halves):
            acc_s[h, pl.ds(f, tiles_here, stride=8), :] = value[:, h * LANES : (h + 1) * LANES]


def pool_sum(slab, info_s, acc_s, ninth_s):
    groups, _, width = info_s.shape
    listed = acc_s.shape[0] * LANES
    tile_count = width // listed
    halves = listed // LANES
    rows_each = (info_s.shape[1] - 4) // tile_count
    row_of = lax.broadcasted_iota(jnp.int32, (8, LANES), 0)

    totals, every = [], None
    for g in range(groups):
        total = jnp.zeros((8, LANES), F32)
        for t in range(tile_count):
            row, first = 4 + t * rows_each + slab * LANES // width, slab * LANES % width
            at = info_s[g, row : row + 1, first : first + LANES].astype(jnp.int32)
            at = jnp.broadcast_to(at, (8, LANES))
            n = g * tile_count + t
            every = at if every is None else jnp.where(row_of >= n * halves, at, every)
            lane, half = at & (LANES - 1), at >> 7
            for h in range(halves):
                here = lane_gather(acc_s[h, 8 * n : 8 * n + 8, :], lane)
                total = total + jnp.where(half == h, here, 0.0)
        totals.append(total)
    here = lane_gather(ninth_s[...], every & (LANES - 1))
    ninth = jnp.where(every >> 7 == row_of % halves, here, 0.0)
    return totals[0] + totals[1], jnp.sum(ninth, axis=0, keepdims=True)


def block_start(tile_id):
    within = tile_id % (TILES_X * TILES_Y)
    return (within % TILES_X) // 4 * 4, (within // TILES_X) // 2 * 2


def near_kernel(pieces, tile_ids, cams, where, own, other, *refs):
    parts = refs[:pieces]
    rendered, rows, partial, feats, info_s, *work = refs[pieces:]
    view = tile_ids[0] // (TILES_X * TILES_Y)
    cam = [cams[view, i] for i in range(12)]
    slabs = spread_features(parts, feats, parts[0].shape[0])
    projected = project_rows(lambda f: feats[f * slabs : (f + 1) * slabs, :], cam)
    colours = []
    for k in range(3):
        first = pl.multiple_of((11 + 3 * view + k) * slabs, slabs)
        colours.append(feats[pl.ds(first, slabs), :])
    for f, value in enumerate(colours[:2] + projected + [colours[2]] * 8):
        rows[pl.ds(f, slabs, stride=ROWS), :] = value
    info_s[0] = own[...]
    info_s[1] = other[...]
    composite(block_start(tile_ids[0]), 0, where[0], rows, info_s, rendered, work)
    for s in range(slabs):
        at = slice(s * LANES, (s + 1) * LANES)
        partial[0:8, at], partial[8:9, at] = pool_sum(s, info_s, *work[-2:])


def far_kernel(blocks, tile_ids, where, rows, partial, infos, *refs):
    *packets, info_s = refs[: len(refs) - 12]
    work = refs[len(refs) - 12 :]
    half = infos.shape[0] // 2
    info_s[0] = infos[:half, :]
    info_s[1] = infos[half:, :]
    composite(block_start(tile_ids[0]), 2, where[0], rows, info_s, None, work)
    share = (tile_ids[0] // (TILES_X * TILES_Y)).astype(F32)
    row_of = lax.broadcasted_iota(jnp.int32, (8, LANES), 0)
    lane_of = lax.broadcasted_iota(jnp.int32, (8, LANES), 1)
    chunk = packets[0].shape[1]
    for s in range(rows.shape[0] // ROWS):
        total, ninth = pool_sum(s, info_s, *work[-2:])
        total = total + partial[0:8, s * LANES : (s + 1) * LANES]
        ninth = ninth + partial[8:9, s * LANES : (s + 1) * LANES]
        if blocks == 1:
            mine = share
        else:
            column = s * LANES + lane_of
            mine = jnp.where(column % where[2] // (where[2] // blocks) == where[1], share, 0.0)
        at = slice(s * LANES % chunk, s * LANES % chunk + LANES)
        packets[s * LANES // chunk][0:8, at] = total
        packets[s * LANES // chunk][8:16, at] = jnp.where(
            row_of == 0, jnp.broadcast_to(ninth, (8, LANES)), mine
        )


def join_kernel(first, second, out):
    half = first.shape[0]
    out[:half, :] = first[...]
    out[half:, :] = second[...]


def update_kernel(pieces, follows, where, cams, params, adam_m, adam_v, *refs):
    packets, refs = refs[:pieces], refs[pieces + 3 * follows :]
    sinks, (feats, rows, grads, made, sems) = refs[:3], refs[3:]
    features = params.shape[0]
    chunk = packets[0].shape[1]
    width = pieces * chunk
    slabs = width // LANES
    start = (where[0] ^ where[1]) // pieces * pieces * chunk
    for d in range(pieces):
        for h in range(chunk // LANES):
            slab = (where[0] ^ where[1] ^ d) % pieces * (chunk // LANES) + h
            rows[pl.ds(slab, ROWS, stride=slabs), :] = packets[d][:, h * LANES : (h + 1) * LANES]
    pulled = [rows[f * slabs : (f + 1) * slabs, :] for f in range(10)]
    view = pulled[9]
    cam = []
    for i in range(12):
        value = jnp.full((slabs, LANES), cams[0, i], F32)
        for v in range(1, cams.shape[0]):
            value = jnp.where(view == float(v), cams[v, i], value)
        cam.append(value)

    def put(f, value):
        grads[f * slabs : (f + 1) * slabs, :] = value

    def column(s):
        return pl.ds(pl.multiple_of(start + s * LANES, LANES), LANES)

    for s in range(slabs):
        for row in range(0, features, 8):
            count = min(8, features - row)
            feats[pl.ds(row * slabs + s, count, stride=slabs), :] = params[
                row : row + count, column(s)
            ]
    project_pull(
        lambda f: feats[f * slabs : (f + 1) * slabs, :], cam, pulled[2:8] + pulled[:2] + pulled[8:9], put
    )
    rate = learn_rate / (1.0 - beta_one**adam_steps)
    unbias = 1.0 / (1.0 - beta_two**adam_steps)
    stores = []
    order = list(range(16, features, 8)) + [0, 8]
    for row in order:
        count = min(8, features - row)
        span = slice(row, row + count)
        for s in range(slabs):
            here = (span, slice(s * LANES, (s + 1) * LANES))
            grad = grads[pl.ds(row * slabs + s, count, stride=slabs), :]
            moment = beta_one * adam_m[span, column(s)] + (1.0 - beta_one) * grad
            second = beta_two * adam_v[span, column(s)] + (1.0 - beta_two) * grad * grad
            made.at[1][here] = moment
            made.at[2][here] = second
            made.at[0][here] = params[span, column(s)] - rate * moment / (
                jnp.sqrt(second * unbias) + adam_eps
            )
        if row % 16 == 8 or row + count == features:
            first = row // 16 * 16
            span = pl.ds(first, row + count - first)
            columns = pl.ds(pl.multiple_of(start, LANES), width)
            for k in range(3):
                store = pltpu.make_async_copy(
                    made.at[k, span], sinks[k].at[span, columns], sems.at[k, first // 16]
                )
                store.start()
                stores.append(store)
    for store in stores:
        store.wait()


def vmem():
    return pl.BlockSpec(memory_space=pltpu.VMEM)


def smem():
    return pl.BlockSpec(memory_space=pltpu.SMEM)


def any_space():
    return pl.BlockSpec(memory_space=pl.ANY)


def call(kernel, name, out_shape, in_specs, scratch, args, out_specs=None, grant=32):
    return pl.pallas_call(
        kernel,
        out_shape=out_shape,
        in_specs=in_specs,
        out_specs=out_specs or tuple(vmem() for _ in out_shape),
        scratch_shapes=scratch,
        compiler_params=pltpu.CompilerParams(vmem_limit_bytes=grant * 1024 * 1024),
        name=name,
    )(*args)


def work_shapes(tile_count, pixels, listed):
    tiles = 2 * tile_count
    spans = tiles * pixels // LANES
    assert spans < LIST_STEP and tiles * listed // LANES == 8 and tiles == 4
    return [pltpu.VMEM((listed * LIST_STEP, LANES), F32)] * 4 + [
        pltpu.VMEM((2 * listed, spans * LANES), BF16),
        pltpu.VMEM((listed // LANES, 8 * tiles, LANES), F32),
        pltpu.VMEM((8, tiles * listed), F32),
        pltpu.VMEM((24 * tiles, tiles * listed), F32),
        pltpu.VMEM((listed // LANES, LANES, LANES), F32),
        pltpu.VMEM((8, LANES), jnp.int32),
        pltpu.VMEM((listed // LANES, 8 * tiles, LANES), F32),
        pltpu.VMEM((8, LANES), F32),
    ]


def near(tile_ids, cameras, where, own, other, parts, tile_count):
    width = sum(part.shape[1] for part in parts)
    features = parts[0].shape[0]
    slabs = width // LANES
    pixels = listed = own.shape[1] // tile_count
    return call(
        functools.partial(near_kernel, len(parts)),
        "near",
        (
            jax.ShapeDtypeStruct((3, own.shape[1]), F32),
            jax.ShapeDtypeStruct((ROWS * slabs, LANES), F32),
            jax.ShapeDtypeStruct((ROWS, width), F32),
        ),
        [smem()] * 3 + [vmem()] * (2 + len(parts)),
        [pltpu.VMEM((features * slabs, LANES), F32), pltpu.VMEM((2,) + own.shape, F32)]
        + work_shapes(tile_count, pixels, listed),
        (tile_ids, cameras, where, own, other, *parts),
    )


def far(tile_ids, where, rows, partial, infos, pieces, tile_count, blocks):
    width = partial.shape[1]
    pixels = listed = infos.shape[1] // tile_count
    info = (infos.shape[0] // 2, infos.shape[1])
    return call(
        functools.partial(far_kernel, blocks),
        "far",
        (jax.ShapeDtypeStruct((ROWS, width // pieces), F32),) * pieces,
        [smem()] * 2 + [vmem()] * 3,
        [pltpu.VMEM((2,) + info, F32)] + work_shapes(tile_count, pixels, listed),
        (tile_ids, where, rows, partial, infos),
    )


def join(first, second):
    shape = (2 * first.shape[0], first.shape[1])
    return call(
        join_kernel, "join", (jax.ShapeDtypeStruct(shape, F32),), [vmem()] * 2, [], (first, second)
    )[0]


def update(own, first, cameras, params, adam_m, adam_v, packets, before):
    features = params.shape[0]
    width = sum(packet.shape[1] for packet in packets)
    slabs = width // LANES
    shape = jax.ShapeDtypeStruct(params.shape, F32)
    at = 5 + len(packets)
    return pl.pallas_call(
        functools.partial(update_kernel, len(packets), len(before) > 0),
        out_shape=(shape, shape, shape),
        in_specs=[smem()] * 2
        + [vmem()] * (3 + len(packets))
        + [any_space()] * len(before),
        out_specs=(any_space(),) * 3,
        scratch_shapes=[
            pltpu.VMEM((features * slabs, LANES), F32),
            pltpu.VMEM((ROWS * slabs, LANES), F32),
            pltpu.VMEM((features * slabs, LANES), F32),
            pltpu.VMEM((3, features, width), F32),
            pltpu.SemaphoreType.DMA((3, (features + 15) // 16)),
        ],
        input_output_aliases={at + k: k for k in range(len(before))},
        compiler_params=pltpu.CompilerParams(vmem_limit_bytes=32 * 1024 * 1024),
        name="update",
    )(
        jnp.stack([own, jnp.int32(first)]).astype(jnp.int32),
        cameras, params, adam_m, adam_v, *packets, *before,
    )


def swap(value, axis, d):
    if d == 0:
        return value
    return lax.ppermute(value, axis, [(k, k ^ d) for k in range(lax.axis_size(axis))])


def local(params, adam_m, adam_v, cameras, target, tile_ids, hit_shard, hit_local):
    width = params.shape[1]
    tile_count, listed = hit_local.shape
    shards = lax.axis_size("gs")
    along = lax.axis_size("tile")
    chunk = width // shards
    group = lax.axis_index("gs")
    seat = lax.axis_index("tile")
    aligned = chunk % LANES == 0
    team = BLOCK_TILES // tile_count
    assert team == 4
    blocks = along // team

    info, params = pack(group, params, target, hit_shard, hit_local, shards)
    parts = cut(group, cameras, params, shards if aligned else 1)
    if not aligned:
        parts = [
            lax.dynamic_slice_in_dim(parts[0], (group ^ d) * chunk, chunk, axis=1)
            for d in range(shards)
        ]
    parts = [swap(parts[d], "gs", d) for d in range(shards)]
    beside = swap(info, "tile", 1)
    beyond = swap(join(info, beside), "tile", 2)
    if not aligned:
        parts = [jnp.concatenate(parts, axis=1)]
    where = jnp.stack([seat % team, seat // team, jnp.int32(chunk)]).astype(jnp.int32)
    rendered, rows, partial = near(tile_ids, cameras, where, info, beside, parts, tile_count)
    packets = far(tile_ids, where, rows, partial, beyond, len(parts), tile_count, blocks)
    if not aligned:
        packets = [packets[0][:, d * chunk : (d + 1) * chunk] for d in range(shards)]
    packets = [swap(packets[d], "gs", d) for d in range(shards)]
    if blocks > 1:
        packets = [block_sum(packet, along, team) for packet in packets]
    if aligned:
        own = group
    else:
        packets = [jnp.stack(packets)[jnp.arange(shards) ^ group].transpose(1, 0, 2).reshape(ROWS, -1)]
        own = jnp.int32(0)
    made = ()
    count = max(1, len(packets) // 2)
    for first in range(0, len(packets), count):
        made = update(
            own, first, cameras, params, adam_m, adam_v, packets[first : first + count], made
        )
    new_params, new_m, new_v = made
    return (rendered, new_params, new_m, new_v)


def block_sum(packet, along, team):
    step = team
    while step < along:
        packet = packet + swap(packet, "tile", step)
        step *= 2
    return packet


def solution(mesh):
    return jax.shard_map(
        local,
        mesh=mesh,
        in_specs=(
            P(None, ("groups", "gs")),
            P(None, ("groups", "gs")),
            P(None, ("groups", "gs")),
            P("groups", None),
            P(None, ("groups", "gs", "tile")),
            P(("groups", "gs", "tile")),
            P(("groups", "gs", "tile"), None, None),
            P(("groups", "gs", "tile"), None),
        ),
        out_specs=(
            P(None, ("groups", "gs", "tile")),
            P(None, ("groups", "gs")),
            P(None, ("groups", "gs")),
            P(None, ("groups", "gs")),
        ),
        check_vma=False,
    )
```

```python
import functools

import jax
import jax.numpy as jnp
from jax import lax
from jax.experimental import pallas as pl
from jax.experimental.pallas import tpu as pltpu
from jax.sharding import PartitionSpec as P

TILES_X = 120
TILES_Y = 68
TILE_SIDE = 16
BLOCK_TILES = 8
LANES = 128
ROWS = 16
LIST_STEP = 9
F32 = jnp.float32
BF16 = jnp.bfloat16

focal_length = 1000.0
center_x = 960.0
center_y = 540.0
dilation = 0.3
beta_one = 0.9
beta_two = 0.999
learn_rate = 0.01
adam_eps = 1e-08
adam_steps = 100.0
sh_const = (
    0.28209479177387814,
    0.4886025119029199,
    1.0925484305920792,
    0.31539156525252005,
    0.5462742152960396,
    0.5900435899266435,
    2.890611442640554,
    0.4570457994644658,
    0.3731763325901154,
    1.445305721320277,
)


def sh_basis(x, y, z):
    s = sh_const
    xx, yy, zz = x * x, y * y, z * z
    return [
        None,
        -s[1] * y,
        s[1] * z,
        -s[1] * x,
        s[2] * (x * y),
        -s[2] * (y * z),
        s[3] * (2.0 * zz - xx - yy),
        -s[2] * (x * z),
        s[4] * (xx - yy),
        -s[5] * y * (3.0 * xx - yy),
        s[6] * (x * y) * z,
        -s[7] * y * (4.0 * zz - xx - yy),
        s[8] * z * (2.0 * zz - 3.0 * xx - 3.0 * yy),
        -s[7] * x * (4.0 * zz - xx - yy),
        s[9] * z * (xx - yy),
        -s[5] * x * (xx - 3.0 * yy),
    ]


def sh_pull(h, x, y, z):
    s = sh_const
    xx, yy, zz = x * x, y * y, z * z
    xy, xz, yz = x * y, x * z, y * z
    diff = xx - yy
    ring = 4.0 * zz - xx - yy
    g_x = (
        -s[1] * h[3]
        + s[2] * (h[4] * y - h[7] * z)
        - (2.0 * s[3]) * h[6] * x
        + (2.0 * s[4]) * h[8] * x
        - (6.0 * s[5]) * h[9] * xy
        + s[6] * h[10] * yz
        + (2.0 * s[7]) * h[11] * xy
        - (6.0 * s[8]) * h[12] * xz
        - s[7] * h[13] * (ring - 2.0 * xx)
        + (2.0 * s[9]) * h[14] * xz
        - (3.0 * s[5]) * h[15] * diff
    )
    g_y = (
        -s[1] * h[1]
        + s[2] * (h[4] * x - h[5] * z)
        - (2.0 * s[3]) * h[6] * y
        - (2.0 * s[4]) * h[8] * y
        - (3.0 * s[5]) * h[9] * diff
        + s[6] * h[10] * xz
        - s[7] * h[11] * (ring - 2.0 * yy)
        - (6.0 * s[8]) * h[12] * yz
        + (2.0 * s[7]) * h[13] * xy
        - (2.0 * s[9]) * h[14] * yz
        + (6.0 * s[5]) * h[15] * xy
    )
    g_z = (
        s[1] * h[2]
        - s[2] * (h[5] * y + h[7] * x)
        + (4.0 * s[3]) * h[6] * z
        + s[6] * h[10] * xy
        - (8.0 * s[7]) * (h[11] * yz + h[13] * xz)
        + s[8] * h[12] * (6.0 * zz - 3.0 * xx - 3.0 * yy)
        + s[9] * h[14] * diff
    )
    return g_x, g_y, g_z


def project_parts(feat, cam):
    rot = [[cam[3 * r + c] for c in range(3)] for r in range(3)]
    off = [feat(a) - cam[9 + a] for a in range(3)]
    in_cam = [rot[r][0] * off[0] + rot[r][1] * off[1] + rot[r][2] * off[2] for r in range(3)]
    inv = 1.0 / in_cam[2]
    u = in_cam[0] * inv
    v = in_cam[1] * inv
    finv = focal_length * inv
    scale = [jnp.exp(2.0 * feat(3 + a)) for a in range(3)]
    quat = [feat(6 + a) for a in range(4)]
    rnorm = lax.rsqrt(quat[0] * quat[0] + quat[1] * quat[1] + quat[2] * quat[2] + quat[3] * quat[3])
    w, x, y, z = [q * rnorm for q in quat]
    turn = [
        [1.0 - 2.0 * (y * y + z * z), 2.0 * (x * y - w * z), 2.0 * (x * z + w * y)],
        [2.0 * (x * y + w * z), 1.0 - 2.0 * (x * x + z * z), 2.0 * (y * z - w * x)],
        [2.0 * (x * z - w * y), 2.0 * (y * z + w * x), 1.0 - 2.0 * (x * x + y * y)],
    ]
    screen = [
        [finv * (rot[0][c] - u * rot[2][c]) for c in range(3)],
        [finv * (rot[1][c] - v * rot[2][c]) for c in range(3)],
    ]
    axes = [
        [sum(screen[r][c] * turn[c][k] for c in range(3)) for k in range(3)] for r in range(2)
    ]
    wide = [[axes[r][k] * scale[k] for k in range(3)] for r in range(2)]
    cov_xx = sum(wide[0][k] * axes[0][k] for k in range(3)) + dilation
    cov_xy = sum(wide[0][k] * axes[1][k] for k in range(3))
    cov_yy = sum(wide[1][k] * axes[1][k] for k in range(3)) + dilation
    rdet = 1.0 / (cov_xx * cov_yy - cov_xy * cov_xy)
    conic = (cov_yy * rdet, -cov_xy * rdet, cov_xx * rdet)
    rlen = lax.rsqrt(off[0] * off[0] + off[1] * off[1] + off[2] * off[2])
    way = [off[a] * rlen for a in range(3)]
    return dict(
        rot=rot, inv=inv, u=u, v=v, finv=finv, scale=scale, rnorm=rnorm, rotor=(w, x, y, z), turn=turn,
        screen=screen, axes=axes, wide=wide, conic=conic, rlen=rlen, way=way,
    )


def shade(feat, cam):
    off = [feat(a) - cam[9 + a] for a in range(3)]
    rlen = lax.rsqrt(off[0] * off[0] + off[1] * off[1] + off[2] * off[2])
    basis = sh_basis(*[off[a] * rlen for a in range(3)])
    colours = []
    for k in range(3):
        total = 0.5 + sh_const[0] * feat(11 + 16 * k)
        for b in range(1, 16):
            total = total + feat(11 + 16 * k + b) * basis[b]
        colours.append(total)
    return colours


def project_rows(feat, cam):
    part = project_parts(feat, cam)
    mean_x = focal_length * part["u"] + center_x
    mean_y = focal_length * part["v"] + center_y
    logit = feat(10)
    log_opacity = jnp.minimum(logit, 0.0) - jnp.log(1.0 + jnp.exp(-jnp.abs(logit)))
    return [mean_x, mean_y, *part["conic"], log_opacity]


def project_pull(feat, cam, grads, put):
    part = project_parts(feat, cam)
    g_mx, g_my, g_a, g_b, g_c, g_o = grads[:6]
    g_col = grads[6:9]
    way, rlen = part["way"], part["rlen"]
    basis = sh_basis(*way)
    pulled = [None]
    for k in range(3):
        put(11 + 16 * k, sh_const[0] * g_col[k])
    for b in range(1, 16):
        total = 0.0
        for k in range(3):
            put(11 + 16 * k + b, g_col[k] * basis[b])
            total = total + g_col[k] * feat(11 + 16 * k + b)
        pulled.append(total)
    g_way = sh_pull(pulled, *way)
    along = way[0] * g_way[0] + way[1] * g_way[1] + way[2] * g_way[2]
    g_off = [(g_way[a] - way[a] * along) * rlen for a in range(3)]
    put(10, g_o / (1.0 + jnp.exp(feat(10))))
    a, b, c = part["conic"]
    g_xx = -(a * a * g_a + a * b * g_b + b * b * g_c)
    g_xy = -(2.0 * a * b * g_a + (a * c + b * b) * g_b + 2.0 * b * c * g_c)
    g_yy = -(b * b * g_a + b * c * g_b + c * c * g_c)
    axes, wide, turn, screen = part["axes"], part["wide"], part["turn"], part["screen"]
    for k in range(3):
        g_scale = (
            g_xx * axes[0][k] * wide[0][k]
            + g_xy * axes[0][k] * wide[1][k]
            + g_yy * axes[1][k] * wide[1][k]
        )
        put(3 + k, 2.0 * g_scale)
    g_axes = [
        [2.0 * g_xx * wide[0][k] + g_xy * wide[1][k] for k in range(3)],
        [2.0 * g_yy * wide[1][k] + g_xy * wide[0][k] for k in range(3)],
    ]
    g_screen = [
        [sum(g_axes[r][k] * turn[c][k] for k in range(3)) for c in range(3)] for r in range(2)
    ]
    gm = [
        [g_axes[0][k] * screen[0][c] + g_axes[1][k] * screen[1][c] for k in range(3)]
        for c in range(3)
    ]
    w, x, y, z = part["rotor"]
    up_xy, up_xz, up_yz = gm[0][1] + gm[1][0], gm[0][2] + gm[2][0], gm[1][2] + gm[2][1]
    un_xy, un_xz, un_yz = gm[1][0] - gm[0][1], gm[0][2] - gm[2][0], gm[2][1] - gm[1][2]
    g_rotor = [
        2.0 * (z * un_xy + y * un_xz + x * un_yz),
        2.0 * (y * up_xy + z * up_xz + w * un_yz - 2.0 * x * (gm[1][1] + gm[2][2])),
        2.0 * (x * up_xy + z * up_yz + w * un_xz - 2.0 * y * (gm[0][0] + gm[2][2])),
        2.0 * (x * up_xz + y * up_yz + w * un_xy - 2.0 * z * (gm[0][0] + gm[1][1])),
    ]
    rotor = (w, x, y, z)
    along = sum(rotor[i] * g_rotor[i] for i in range(4))
    for i in range(4):
        put(6 + i, (g_rotor[i] - rotor[i] * along) * part["rnorm"])
    rot, inv, finv, u, v = part["rot"], part["inv"], part["finv"], part["u"], part["v"]
    g_u = focal_length * g_mx - finv * sum(g_screen[0][c] * rot[2][c] for c in range(3))
    g_v = focal_length * g_my - finv * sum(g_screen[1][c] * rot[2][c] for c in range(3))
    g_f = sum(g_screen[r][c] * screen[r][c] for r in range(2) for c in range(3))
    g_in = [g_u * inv, g_v * inv, -(g_f + g_u * u + g_v * v) * inv]
    for axis in range(3):
        put(
            axis,
            g_off[axis] + rot[0][axis] * g_in[0] + rot[1][axis] * g_in[1] + rot[2][axis] * g_in[2],
        )


def split(value):
    high = value.astype(BF16)
    return high, (value - high.astype(F32)).astype(BF16)


def matmul(a, b, dims=((1,), (0,))):
    return lax.dot_general(a, b, (dims, ((), ())), preferred_element_type=F32)


def spread_features(parts, scratch, count):
    tiles = sum(part.shape[1] for part in parts) // LANES
    at = 0
    for part in parts:
        for first in range(0, part.shape[1], LANES):
            for row in range(0, count, 8):
                rows = min(8, count - row)
                scratch[pl.ds(row * tiles + at, rows, stride=tiles), :] = part[
                    row : row + rows, first : first + LANES
                ]
            at += 1
    return tiles


def pack_kernel(shards, where, *refs):
    sources, (info, params, shard_of, local_of, goal, place_s, sems) = refs[:4], refs[4:]
    group = where[0]
    loads = [
        pltpu.make_async_copy(source, held, sems.at[k])
        for k, (source, held) in enumerate(zip(sources, (shard_of, local_of, goal, params)))
    ]
    for load in loads:
        load.start()
    for load in loads[:3]:
        load.wait()
    width = info.shape[1]
    tile_count, listed = local_of.shape
    rows_each = (info.shape[0] - 4) // tile_count
    columns = rows_each * width
    chunk = columns // shards
    info[0:3, :] = goal[...]
    for t in range(tile_count):
        place = (shard_of[t] ^ group) * chunk + (local_of[t : t + 1, :] - group * chunk)
        info[3:4, t * listed : (t + 1) * listed] = place.astype(F32)
        row_i = lax.broadcasted_iota(jnp.int32, (LANES, LANES), 0)
        col_i = lax.broadcasted_iota(jnp.int32, (LANES, LANES), 1)
        for first in range(0, listed, LANES):
            spread = jnp.broadcast_to(place[:, first : first + LANES].astype(F32), (LANES, LANES))
            place_s[first : first + LANES, :] = jnp.broadcast_to(
                jnp.sum(jnp.where(row_i == col_i, spread, 0.0), axis=1, keepdims=True), (LANES, LANES)
            )
        lane_of = lax.broadcasted_iota(jnp.int32, (8, LANES), 1).astype(F32)
        row_of = lax.broadcasted_iota(jnp.int32, (8, LANES), 0).astype(F32)
        for s in range(columns // LANES):
            best = jnp.full((8, LANES), -1.0, F32)
            column = lane_of + float(s * LANES)
            for first in range(0, listed, 8):
                best = jnp.where(
                    place_s[first : first + 8, :] == column, row_of + float(first), best
                )
            best = jnp.max(best, axis=0, keepdims=True)
            row, at = 4 + t * rows_each + s * LANES // width, s * LANES % width
            info[row : row + 1, at : at + LANES] = best
    loads[3].wait()


def pack(group, params, target, hit_shard, hit_local, shards):
    columns = params.shape[1]
    tile_count, listed = hit_local.shape
    width = target.shape[1]
    rows = 4 + tile_count * (columns // width)
    args = (hit_shard.reshape(tile_count, 1, listed), hit_local, target, params)
    return call(
        functools.partial(pack_kernel, shards),
        "pack",
        (jax.ShapeDtypeStruct((rows, width), F32), jax.ShapeDtypeStruct(params.shape, F32)),
        [smem()] + [pl.BlockSpec(memory_space=pltpu.HBM)] * 4,
        [
            pltpu.VMEM((tile_count, 1, listed), jnp.int32),
            pltpu.VMEM((tile_count, listed), jnp.int32),
            pltpu.VMEM(target.shape, F32),
            pltpu.VMEM((listed, LANES), F32),
            pltpu.SemaphoreType.DMA((4,)),
        ],
        (group.reshape(1),) + tuple(pltpu.with_memory_space_constraint(a, pltpu.HBM) for a in args),
        (vmem(), any_space()),
    )


def sent_rows(views):
    return (11 + 3 * views + 7) // 8 * 8


def cut_kernel(pieces, where, cams, params, *refs):
    parts, (feats, rows) = refs[:pieces], refs[pieces:]
    views = cams.shape[0]
    count = sent_rows(views)
    slabs = spread_features([params], feats, params.shape[0])

    def feat(f):
        return feats[f * slabs : (f + 1) * slabs, :]

    values = [feat(f) for f in range(11)]
    for v in range(views):
        values += shade(feat, [cams[v, i] for i in range(12)])
    values += [jnp.zeros((slabs, LANES), F32)] * (count - len(values))
    for f, value in enumerate(values):
        rows[pl.ds(f, slabs, stride=count), :] = value
    each = slabs // pieces
    for d in range(pieces):
        for h in range(each):
            first = (((where[0] ^ d) % pieces) * each + h) * count
            parts[d][:, h * LANES : (h + 1) * LANES] = rows[
                pl.ds(pl.multiple_of(first, 8), count), :
            ]


def cut(group, cameras, params, pieces):
    features, columns = params.shape
    slabs = columns // LANES
    count = sent_rows(cameras.shape[0])
    return list(
        call(
            functools.partial(cut_kernel, pieces),
            "cut",
            (jax.ShapeDtypeStruct((count, columns // pieces), F32),) * pieces,
            [smem()] * 2 + [vmem()],
            [
                pltpu.VMEM((features * slabs, LANES), F32),
                pltpu.VMEM((count * slabs, LANES), F32),
            ],
            (group.reshape(1), cameras, params),
        )
    )


def lane_gather(source, lane):
    return jnp.take_along_axis(source, lane, axis=1, mode="promise_in_bounds")


def pixel_basis(pixels):
    pixel = lax.broadcasted_iota(jnp.int32, (8, pixels), 1)
    row = lax.broadcasted_iota(jnp.int32, (8, pixels), 0)
    middle = 0.5 * TILE_SIDE - 0.5
    u = (pixel % TILE_SIDE).astype(F32) - middle
    v = (pixel // TILE_SIDE).astype(F32) - middle
    value = jnp.where(row == 0, 1.0, 0.0)
    for at, term in ((1, u), (2, v), (3, u * u), (4, u * v), (5, v * v)):
        value = jnp.where(row == at, term, value)
    return value


def composite(tiles, first_group, me, rows, info_s, rendered, work):
    alpha_s, weight_s, pull_s, push_s, weight_2, entry_s, coef_s, colour_s, sums_s, index_s, acc_s, ninth_s = work
    groups = info_s.shape[0]
    listed = acc_s.shape[0] * LANES
    tile_count = info_s.shape[2] // listed
    pixels = info_s.shape[2] // tile_count
    parts = pixels // LANES
    halves = listed // LANES
    tiles_here = groups * tile_count
    spans = tiles_here * parts
    slabs = rows.shape[0] // ROWS
    side = TILE_SIDE
    first_col, first_row = tiles

    def of_span(span):
        return pl.ds(span, listed, stride=LIST_STEP)

    def of_place(place):
        return pl.ds(place * LIST_STEP, spans)

    basis = pixel_basis(pixels)
    basis_3 = jnp.concatenate([basis, basis, basis], axis=0).astype(BF16)
    row_of = lax.broadcasted_iota(jnp.int32, (8, listed), 0)

    entries = []
    for n in range(tiles_here):
        g, t = n // tile_count, n % tile_count
        found = []
        for h in range(halves):
            first = t * listed + h * LANES
            at = info_s[g, 3:4, first : first + LANES].astype(jnp.int32)
            index_s[n * halves + h : n * halves + h + 1, :] = at
            at = jnp.broadcast_to(at, (8, LANES))
            lane, slab = at & (LANES - 1), at >> 7
            value = lane_gather(rows[0:8, :], lane)
            for s in range(1, slabs):
                value = jnp.where(
                    slab == s, lane_gather(rows[s * ROWS : s * ROWS + 8, :], lane), value
                )
            found.append(value)
        entries.append(jnp.concatenate(found, axis=1))
        for h in range(halves):
            entry_s[h, 8 * n : 8 * n + 8, :] = found[h]
    at = index_s[...]
    lane, slab = at & (LANES - 1), at >> 7
    ninth = lane_gather(rows[8:16, :], lane)
    for s in range(1, slabs):
        ninth = jnp.where(
            slab == s, lane_gather(rows[s * ROWS + 8 : s * ROWS + 16, :], lane), ninth
        )

    def of_lists(ref, f):
        at = pl.ds(f, tiles_here, stride=8)
        return jnp.concatenate([ref[h, at, :] for h in range(halves)], axis=1)

    tile_of = lax.broadcasted_iota(jnp.int32, (tiles_here, listed), 0)
    slot = (me ^ (first_group + tile_of // tile_count)) * tile_count + tile_of % tile_count
    mean_u = of_lists(entry_s, 2) - (((first_col + slot % 4) * side).astype(F32) + 0.5 * side)
    mean_v = of_lists(entry_s, 3) - (((first_row + slot // 4) * side).astype(F32) + 0.5 * side)
    quad_a = -0.5 * of_lists(entry_s, 4)
    quad_b = -of_lists(entry_s, 5)
    quad_c = -0.5 * of_lists(entry_s, 6)
    slope_u = 2.0 * quad_a * mean_u + quad_b * mean_v
    slope_v = 2.0 * quad_c * mean_v + quad_b * mean_u
    level = 0.5 * (slope_u * mean_u + slope_v * mean_v) + of_lists(entry_s, 7)
    for f, value in enumerate((level, -slope_u, -slope_v, quad_a, quad_b, quad_c)):
        for n in range(tiles_here):
            coef_s[f : f + 1, n * listed : (n + 1) * listed] = value[n : n + 1]
    coef_s[6:8, :] = jnp.zeros((2, tiles_here * listed), F32)
    coef = coef_s[...]
    terms = []
    for _ in range(3):
        terms.append(coef.astype(BF16).astype(F32))
        coef = coef - terms[-1]
    down = ((0,), (0,))
    power = matmul(jnp.concatenate(terms, axis=0).astype(BF16), basis_3, down)
    for n in range(tiles_here):
        for part in range(parts):
            alpha_s[of_span(n * parts + part), :] = jnp.exp(
                power[n * listed : (n + 1) * listed, part * LANES : (part + 1) * LANES]
            )
    colour_s[...] = jnp.zeros(colour_s.shape, F32)
    hues = []
    for n in range(tiles_here):
        last = jnp.concatenate([ninth[n * halves + h : n * halves + h + 1] for h in range(halves)], axis=1)
        colours = jnp.where(row_of < 2, entries[n], jnp.where(row_of == 2, last, 0.0))
        high = colours.astype(BF16).astype(F32)
        low = colours - high
        here = slice(n * listed, (n + 1) * listed)
        for at, value in ((0, high), (8, low), (16, high)):
            colour_s[24 * n + at : 24 * n + at + 8, here] = value
        hues.append(jnp.concatenate([high, low], axis=0).astype(BF16))

    unroll, quad = 32, 4
    steps = listed // unroll

    def forward(step, passed):
        for j in range(0, unroll, quad):
            at = [of_place(step * unroll + j + i) for i in range(quad)]
            alpha = [alpha_s[at[i], :] for i in range(quad)]
            keep = [1.0 - alpha[i] for i in range(quad)]
            two = keep[0] * keep[1]
            three = two * keep[2]
            weight_s[at[0], :] = alpha[0] * passed
            weight_s[at[1], :] = (alpha[1] * keep[0]) * passed
            weight_s[at[2], :] = (alpha[2] * two) * passed
            weight_s[at[3], :] = (alpha[3] * three) * passed
            passed = passed * (two * (keep[2] * keep[3]))
        return passed

    nought = jnp.zeros((spans, LANES), F32)
    lax.fori_loop(0, steps, forward, nought + 1.0)

    errors = []
    for n in range(tiles_here):
        g, t = n // tile_count, n % tile_count
        for part in range(parts):
            at = slice((n * parts + part) * LANES, (n * parts + part + 1) * LANES)
            weight_2[:listed, at], weight_2[listed:, at] = split(
                weight_s[of_span(n * parts + part), :]
            )
        at = slice(n * pixels, (n + 1) * pixels)
        image = matmul(hues[n], weight_2[:listed, at])
        image = image[0:8] + image[8:16] + matmul(hues[n], weight_2[listed:, at])[0:8]
        here = slice(t * pixels, (t + 1) * pixels)
        if rendered is not None and g == 0:
            rendered[:, here] = image[0:3]
        error = image - info_s[g, 0:8, here]
        high = error.astype(BF16).astype(F32)
        low = error - high
        errors += [high, high, low]

        hue = jnp.concatenate([high, low], axis=0).astype(BF16)
        across = ((1,), (1,))
        grads = matmul(hue, weight_2[:listed, at], across) + matmul(hue, weight_2[listed:, at], across)
        grads = grads[0:8] + grads[8:16]
        for h in range(halves):
            acc_s[h, 8 * n : 8 * n + 8, :] = grads[:, h * LANES : (h + 1) * LANES]
            row = n * halves + h
            ninth_s[row : row + 1, :] = grads[2:3, h * LANES : (h + 1) * LANES]
    pull = matmul(colour_s[...].astype(BF16), jnp.concatenate(errors, axis=0).astype(BF16), down)
    for n in range(tiles_here):
        for part in range(parts):
            pull_s[of_span(n * parts + part), :] = pull[
                n * listed : (n + 1) * listed, part * LANES : (part + 1) * LANES
            ]

    def backward(back, behind):
        for j in range(0, unroll, quad):
            at = [of_place(listed - 1 - (back * unroll + j + i)) for i in range(quad)]
            alpha = [alpha_s[at[i], :] for i in range(quad)]
            pull = [pull_s[at[i], :] for i in range(quad)]
            keep = [1.0 - alpha[i] for i in range(quad)]
            own = alpha[0] * pull[0]
            seen, through = behind, keep[0]
            for i in range(quad):
                push_s[at[i], :] = weight_s[at[i], :] * (pull[i] - seen)
                if i > 0:
                    own = own * keep[i] + alpha[i] * pull[i]
                    through = through * keep[i]
                seen = behind * through + own
            behind = seen
        return behind

    lax.fori_loop(0, steps, backward, nought)

    basis = basis.astype(BF16)
    for n in range(tiles_here):
        high, low = split(
            jnp.concatenate([push_s[of_span(n * parts + part), :] for part in range(parts)], axis=1)
        )
        moments = matmul(basis, high, across) + matmul(basis, low, across)
        for h in range(halves):
            sums_s[h, 8 * n : 8 * n + 8, :] = moments[:, h * LANES : (h + 1) * LANES]
    m_00, m_10, m_01, m_20, m_11, m_02 = [
        of_lists(sums_s, m) for m in range(6)
    ]
    n_10 = m_10 - mean_u * m_00
    n_01 = m_01 - mean_v * m_00
    for f, value in (
        (2, -(2.0 * quad_a * n_10 + quad_b * n_01)),
        (3, -(2.0 * quad_c * n_01 + quad_b * n_10)),
        (4, -0.5 * (m_20 - mean_u * (m_10 + n_10))),
        (5, -(m_11 - mean_u * m_01 - mean_v * n_10)),
        (6, -0.5 * (m_02 - mean_v * (m_01 + n_01))),
        (7, m_00),
    ):
        for h in range(halves):
            acc_s[h, pl.ds(f, tiles_here, stride=8), :] = value[:, h * LANES : (h + 1) * LANES]


def pool_sum(slab, info_s, acc_s, ninth_s):
    groups, _, width = info_s.shape
    listed = acc_s.shape[0] * LANES
    tile_count = width // listed
    halves = listed // LANES
    rows_each = (info_s.shape[1] - 4) // tile_count
    row_of = lax.broadcasted_iota(jnp.int32, (8, LANES), 0)

    totals, every = [], None
    for g in range(groups):
        total = jnp.zeros((8, LANES), F32)
        for t in range(tile_count):
            row, first = 4 + t * rows_each + slab * LANES // width, slab * LANES % width
            at = info_s[g, row : row + 1, first : first + LANES].astype(jnp.int32)
            at = jnp.broadcast_to(at, (8, LANES))
            n = g * tile_count + t
            every = at if every is None else jnp.where(row_of >= n * halves, at, every)
            lane, half = at & (LANES - 1), at >> 7
            for h in range(halves):
                here = lane_gather(acc_s[h, 8 * n : 8 * n + 8, :], lane)
                total = total + jnp.where(half == h, here, 0.0)
        totals.append(total)
    here = lane_gather(ninth_s[...], every & (LANES - 1))
    ninth = jnp.where(every >> 7 == row_of % halves, here, 0.0)
    return totals[0] + totals[1], jnp.sum(ninth, axis=0, keepdims=True)


def block_start(tile_id):
    within = tile_id % (TILES_X * TILES_Y)
    return (within % TILES_X) // 4 * 4, (within // TILES_X) // 2 * 2


def near_kernel(pieces, tile_ids, cams, where, own, other, *refs):
    parts = refs[:pieces]
    rendered, rows, partial, feats, info_s, *work = refs[pieces:]
    view = tile_ids[0] // (TILES_X * TILES_Y)
    cam = [cams[view, i] for i in range(12)]
    slabs = spread_features(parts, feats, parts[0].shape[0])
    projected = project_rows(lambda f: feats[f * slabs : (f + 1) * slabs, :], cam)
    colours = []
    for k in range(3):
        first = pl.multiple_of((11 + 3 * view + k) * slabs, slabs)
        colours.append(feats[pl.ds(first, slabs), :])
    for f, value in enumerate(colours[:2] + projected + [colours[2]] * 8):
        rows[pl.ds(f, slabs, stride=ROWS), :] = value
    info_s[0] = own[...]
    info_s[1] = other[...]
    composite(block_start(tile_ids[0]), 0, where[0], rows, info_s, rendered, work)
    for s in range(slabs):
        at = slice(s * LANES, (s + 1) * LANES)
        partial[0:8, at], partial[8:9, at] = pool_sum(s, info_s, *work[-2:])


def far_kernel(blocks, tile_ids, where, rows, partial, infos, *refs):
    *packets, info_s = refs[: len(refs) - 12]
    work = refs[len(refs) - 12 :]
    half = infos.shape[0] // 2
    info_s[0] = infos[:half, :]
    info_s[1] = infos[half:, :]
    composite(block_start(tile_ids[0]), 2, where[0], rows, info_s, None, work)
    share = (tile_ids[0] // (TILES_X * TILES_Y)).astype(F32)
    row_of = lax.broadcasted_iota(jnp.int32, (8, LANES), 0)
    lane_of = lax.broadcasted_iota(jnp.int32, (8, LANES), 1)
    chunk = packets[0].shape[1]
    for s in range(rows.shape[0] // ROWS):
        total, ninth = pool_sum(s, info_s, *work[-2:])
        total = total + partial[0:8, s * LANES : (s + 1) * LANES]
        ninth = ninth + partial[8:9, s * LANES : (s + 1) * LANES]
        if blocks == 1:
            mine = share
        else:
            column = s * LANES + lane_of
            mine = jnp.where(column % where[2] // (where[2] // blocks) == where[1], share, 0.0)
        at = slice(s * LANES % chunk, s * LANES % chunk + LANES)
        packets[s * LANES // chunk][0:8, at] = total
        packets[s * LANES // chunk][8:16, at] = jnp.where(
            row_of == 0, jnp.broadcast_to(ninth, (8, LANES)), mine
        )


def join_kernel(first, second, out):
    half = first.shape[0]
    out[:half, :] = first[...]
    out[half:, :] = second[...]


def update_kernel(pieces, follows, where, cams, params, adam_m, adam_v, *refs):
    packets, refs = refs[:pieces], refs[pieces + 3 * follows :]
    sinks, (feats, rows, grads, made, sems) = refs[:3], refs[3:]
    features = params.shape[0]
    chunk = packets[0].shape[1]
    width = pieces * chunk
    slabs = width // LANES
    start = (where[0] ^ where[1]) // pieces * pieces * chunk
    for d in range(pieces):
        for h in range(chunk // LANES):
            slab = (where[0] ^ where[1] ^ d) % pieces * (chunk // LANES) + h
            rows[pl.ds(slab, ROWS, stride=slabs), :] = packets[d][:, h * LANES : (h + 1) * LANES]
    pulled = [rows[f * slabs : (f + 1) * slabs, :] for f in range(10)]
    view = pulled[9]
    cam = []
    for i in range(12):
        value = jnp.full((slabs, LANES), cams[0, i], F32)
        for v in range(1, cams.shape[0]):
            value = jnp.where(view == float(v), cams[v, i], value)
        cam.append(value)

    def put(f, value):
        grads[f * slabs : (f + 1) * slabs, :] = value

    def column(s):
        return pl.ds(pl.multiple_of(start + s * LANES, LANES), LANES)

    for s in range(slabs):
        for row in range(0, features, 8):
            count = min(8, features - row)
            feats[pl.ds(row * slabs + s, count, stride=slabs), :] = params[
                row : row + count, column(s)
            ]
    project_pull(
        lambda f: feats[f * slabs : (f + 1) * slabs, :], cam, pulled[2:8] + pulled[:2] + pulled[8:9], put
    )
    rate = learn_rate / (1.0 - beta_one**adam_steps)
    unbias = 1.0 / (1.0 - beta_two**adam_steps)
    stores = []
    order = list(range(16, features, 8)) + [0, 8]
    for row in order:
        count = min(8, features - row)
        span = slice(row, row + count)
        for s in range(slabs):
            here = (span, slice(s * LANES, (s + 1) * LANES))
            grad = grads[pl.ds(row * slabs + s, count, stride=slabs), :]
            moment = beta_one * adam_m[span, column(s)] + (1.0 - beta_one) * grad
            second = beta_two * adam_v[span, column(s)] + (1.0 - beta_two) * grad * grad
            made.at[1][here] = moment
            made.at[2][here] = second
            made.at[0][here] = params[span, column(s)] - rate * moment / (
                jnp.sqrt(second * unbias) + adam_eps
            )
        if row % 16 == 8 or row + count == features:
            first = row // 16 * 16
            span = pl.ds(first, row + count - first)
            columns = pl.ds(pl.multiple_of(start, LANES), width)
            for k in range(3):
                store = pltpu.make_async_copy(
                    made.at[k, span], sinks[k].at[span, columns], sems.at[k, first // 16]
                )
                store.start()
                stores.append(store)
    for store in stores:
        store.wait()


def vmem():
    return pl.BlockSpec(memory_space=pltpu.VMEM)


def smem():
    return pl.BlockSpec(memory_space=pltpu.SMEM)


def any_space():
    return pl.BlockSpec(memory_space=pl.ANY)


def call(kernel, name, out_shape, in_specs, scratch, args, out_specs=None, grant=32):
    return pl.pallas_call(
        kernel,
        out_shape=out_shape,
        in_specs=in_specs,
        out_specs=out_specs or tuple(vmem() for _ in out_shape),
        scratch_shapes=scratch,
        compiler_params=pltpu.CompilerParams(vmem_limit_bytes=grant * 1024 * 1024),
        name=name,
    )(*args)


def work_shapes(tile_count, pixels, listed):
    tiles = 2 * tile_count
    spans = tiles * pixels // LANES
    assert spans < LIST_STEP and tiles * listed // LANES == 8 and tiles == 4
    return [pltpu.VMEM((listed * LIST_STEP, LANES), F32)] * 4 + [
        pltpu.VMEM((2 * listed, spans * LANES), BF16),
        pltpu.VMEM((listed // LANES, 8 * tiles, LANES), F32),
        pltpu.VMEM((8, tiles * listed), F32),
        pltpu.VMEM((24 * tiles, tiles * listed), F32),
        pltpu.VMEM((listed // LANES, 8 * tiles, LANES), F32),
        pltpu.VMEM((8, LANES), jnp.int32),
        pltpu.VMEM((listed // LANES, 8 * tiles, LANES), F32),
        pltpu.VMEM((8, LANES), F32),
    ]


def near(tile_ids, cameras, where, own, other, parts, tile_count):
    width = sum(part.shape[1] for part in parts)
    features = parts[0].shape[0]
    slabs = width // LANES
    pixels = listed = own.shape[1] // tile_count
    return call(
        functools.partial(near_kernel, len(parts)),
        "near",
        (
            jax.ShapeDtypeStruct((3, own.shape[1]), F32),
            jax.ShapeDtypeStruct((ROWS * slabs, LANES), F32),
            jax.ShapeDtypeStruct((ROWS, width), F32),
        ),
        [smem()] * 3 + [vmem()] * (2 + len(parts)),
        [pltpu.VMEM((features * slabs, LANES), F32), pltpu.VMEM((2,) + own.shape, F32)]
        + work_shapes(tile_count, pixels, listed),
        (tile_ids, cameras, where, own, other, *parts),
    )


def far(tile_ids, where, rows, partial, infos, pieces, tile_count, blocks):
    width = partial.shape[1]
    pixels = listed = infos.shape[1] // tile_count
    info = (infos.shape[0] // 2, infos.shape[1])
    return call(
        functools.partial(far_kernel, blocks),
        "far",
        (jax.ShapeDtypeStruct((ROWS, width // pieces), F32),) * pieces,
        [smem()] * 2 + [vmem()] * 3,
        [pltpu.VMEM((2,) + info, F32)] + work_shapes(tile_count, pixels, listed),
        (tile_ids, where, rows, partial, infos),
    )


def join(first, second):
    shape = (2 * first.shape[0], first.shape[1])
    return call(
        join_kernel, "join", (jax.ShapeDtypeStruct(shape, F32),), [vmem()] * 2, [], (first, second)
    )[0]


def update(own, first, cameras, params, adam_m, adam_v, packets, before):
    features = params.shape[0]
    width = sum(packet.shape[1] for packet in packets)
    slabs = width // LANES
    shape = jax.ShapeDtypeStruct(params.shape, F32)
    at = 5 + len(packets)
    return pl.pallas_call(
        functools.partial(update_kernel, len(packets), len(before) > 0),
        out_shape=(shape, shape, shape),
        in_specs=[smem()] * 2
        + [vmem()] * (3 + len(packets))
        + [any_space()] * len(before),
        out_specs=(any_space(),) * 3,
        scratch_shapes=[
            pltpu.VMEM((features * slabs, LANES), F32),
            pltpu.VMEM((ROWS * slabs, LANES), F32),
            pltpu.VMEM((features * slabs, LANES), F32),
            pltpu.VMEM((3, features, width), F32),
            pltpu.SemaphoreType.DMA((3, (features + 15) // 16)),
        ],
        input_output_aliases={at + k: k for k in range(len(before))},
        compiler_params=pltpu.CompilerParams(vmem_limit_bytes=32 * 1024 * 1024),
        name="update",
    )(
        jnp.stack([own, jnp.int32(first)]).astype(jnp.int32),
        cameras, params, adam_m, adam_v, *packets, *before,
    )


def swap(value, axis, d):
    if d == 0:
        return value
    return lax.ppermute(value, axis, [(k, k ^ d) for k in range(lax.axis_size(axis))])


def local(params, adam_m, adam_v, cameras, target, tile_ids, hit_shard, hit_local):
    width = params.shape[1]
    tile_count, listed = hit_local.shape
    shards = lax.axis_size("gs")
    along = lax.axis_size("tile")
    chunk = width // shards
    group = lax.axis_index("gs")
    seat = lax.axis_index("tile")
    aligned = chunk % LANES == 0
    team = BLOCK_TILES // tile_count
    assert team == 4
    blocks = along // team

    info, params = pack(group, params, target, hit_shard, hit_local, shards)
    parts = cut(group, cameras, params, shards if aligned else 1)
    if not aligned:
        parts = [
            lax.dynamic_slice_in_dim(parts[0], (group ^ d) * chunk, chunk, axis=1)
            for d in range(shards)
        ]
    parts = [swap(parts[d], "gs", d) for d in range(shards)]
    beside = swap(info, "tile", 1)
    beyond = swap(join(info, beside), "tile", 2)
    if not aligned:
        parts = [jnp.concatenate(parts, axis=1)]
    where = jnp.stack([seat % team, seat // team, jnp.int32(chunk)]).astype(jnp.int32)
    rendered, rows, partial = near(tile_ids, cameras, where, info, beside, parts, tile_count)
    packets = far(tile_ids, where, rows, partial, beyond, len(parts), tile_count, blocks)
    if not aligned:
        packets = [packets[0][:, d * chunk : (d + 1) * chunk] for d in range(shards)]
    packets = [swap(packets[d], "gs", d) for d in range(shards)]
    if blocks > 1:
        packets = [block_sum(packet, along, team) for packet in packets]
    if aligned:
        own = group
    else:
        packets = [jnp.stack(packets)[jnp.arange(shards) ^ group].transpose(1, 0, 2).reshape(ROWS, -1)]
        own = jnp.int32(0)
    made = ()
    count = max(1, len(packets) // 2)
    for first in range(0, len(packets), count):
        made = update(
            own, first, cameras, params, adam_m, adam_v, packets[first : first + count], made
        )
    new_params, new_m, new_v = made
    return (rendered, new_params, new_m, new_v)


def block_sum(packet, along, team):
    step = team
    while step < along:
        packet = packet + swap(packet, "tile", step)
        step *= 2
    return packet


def solution(mesh):
    return jax.shard_map(
        local,
        mesh=mesh,
        in_specs=(
            P(None, ("groups", "gs")),
            P(None, ("groups", "gs")),
            P(None, ("groups", "gs")),
            P("groups", None),
            P(None, ("groups", "gs", "tile")),
            P(("groups", "gs", "tile")),
            P(("groups", "gs", "tile"), None, None),
            P(("groups", "gs", "tile"), None),
        ),
        out_specs=(
            P(None, ("groups", "gs", "tile")),
            P(None, ("groups", "gs")),
            P(None, ("groups", "gs")),
            P(None, ("groups", "gs")),
        ),
        check_vma=False,
    )
```

```python
import functools

import jax
import jax.numpy as jnp
from jax import lax
from jax.experimental import pallas as pl
from jax.experimental.pallas import tpu as pltpu
from jax.sharding import PartitionSpec as P

TILES_X = 120
TILES_Y = 68
TILE_SIDE = 16
BLOCK_TILES = 8
LANES = 128
ROWS = 16
LIST_STEP = 9
F32 = jnp.float32
BF16 = jnp.bfloat16

focal_length = 1000.0
center_x = 960.0
center_y = 540.0
dilation = 0.3
beta_one = 0.9
beta_two = 0.999
learn_rate = 0.01
adam_eps = 1e-08
adam_steps = 100.0
sh_const = (
    0.28209479177387814,
    0.4886025119029199,
    1.0925484305920792,
    0.31539156525252005,
    0.5462742152960396,
    0.5900435899266435,
    2.890611442640554,
    0.4570457994644658,
    0.3731763325901154,
    1.445305721320277,
)


def sh_basis(x, y, z):
    s = sh_const
    xx, yy, zz = x * x, y * y, z * z
    return [
        None,
        -s[1] * y,
        s[1] * z,
        -s[1] * x,
        s[2] * (x * y),
        -s[2] * (y * z),
        s[3] * (2.0 * zz - xx - yy),
        -s[2] * (x * z),
        s[4] * (xx - yy),
        -s[5] * y * (3.0 * xx - yy),
        s[6] * (x * y) * z,
        -s[7] * y * (4.0 * zz - xx - yy),
        s[8] * z * (2.0 * zz - 3.0 * xx - 3.0 * yy),
        -s[7] * x * (4.0 * zz - xx - yy),
        s[9] * z * (xx - yy),
        -s[5] * x * (xx - 3.0 * yy),
    ]


def sh_pull(h, x, y, z):
    s = sh_const
    xx, yy, zz = x * x, y * y, z * z
    xy, xz, yz = x * y, x * z, y * z
    diff = xx - yy
    ring = 4.0 * zz - xx - yy
    g_x = (
        -s[1] * h[3]
        + s[2] * (h[4] * y - h[7] * z)
        - (2.0 * s[3]) * h[6] * x
        + (2.0 * s[4]) * h[8] * x
        - (6.0 * s[5]) * h[9] * xy
        + s[6] * h[10] * yz
        + (2.0 * s[7]) * h[11] * xy
        - (6.0 * s[8]) * h[12] * xz
        - s[7] * h[13] * (ring - 2.0 * xx)
        + (2.0 * s[9]) * h[14] * xz
        - (3.0 * s[5]) * h[15] * diff
    )
    g_y = (
        -s[1] * h[1]
        + s[2] * (h[4] * x - h[5] * z)
        - (2.0 * s[3]) * h[6] * y
        - (2.0 * s[4]) * h[8] * y
        - (3.0 * s[5]) * h[9] * diff
        + s[6] * h[10] * xz
        - s[7] * h[11] * (ring - 2.0 * yy)
        - (6.0 * s[8]) * h[12] * yz
        + (2.0 * s[7]) * h[13] * xy
        - (2.0 * s[9]) * h[14] * yz
        + (6.0 * s[5]) * h[15] * xy
    )
    g_z = (
        s[1] * h[2]
        - s[2] * (h[5] * y + h[7] * x)
        + (4.0 * s[3]) * h[6] * z
        + s[6] * h[10] * xy
        - (8.0 * s[7]) * (h[11] * yz + h[13] * xz)
        + s[8] * h[12] * (6.0 * zz - 3.0 * xx - 3.0 * yy)
        + s[9] * h[14] * diff
    )
    return g_x, g_y, g_z


def project_parts(feat, cam):
    rot = [[cam[3 * r + c] for c in range(3)] for r in range(3)]
    off = [feat(a) - cam[9 + a] for a in range(3)]
    in_cam = [rot[r][0] * off[0] + rot[r][1] * off[1] + rot[r][2] * off[2] for r in range(3)]
    inv = 1.0 / in_cam[2]
    u = in_cam[0] * inv
    v = in_cam[1] * inv
    finv = focal_length * inv
    scale = [jnp.exp(2.0 * feat(3 + a)) for a in range(3)]
    quat = [feat(6 + a) for a in range(4)]
    rnorm = lax.rsqrt(quat[0] * quat[0] + quat[1] * quat[1] + quat[2] * quat[2] + quat[3] * quat[3])
    w, x, y, z = [q * rnorm for q in quat]
    turn = [
        [1.0 - 2.0 * (y * y + z * z), 2.0 * (x * y - w * z), 2.0 * (x * z + w * y)],
        [2.0 * (x * y + w * z), 1.0 - 2.0 * (x * x + z * z), 2.0 * (y * z - w * x)],
        [2.0 * (x * z - w * y), 2.0 * (y * z + w * x), 1.0 - 2.0 * (x * x + y * y)],
    ]
    screen = [
        [finv * (rot[0][c] - u * rot[2][c]) for c in range(3)],
        [finv * (rot[1][c] - v * rot[2][c]) for c in range(3)],
    ]
    axes = [
        [sum(screen[r][c] * turn[c][k] for c in range(3)) for k in range(3)] for r in range(2)
    ]
    wide = [[axes[r][k] * scale[k] for k in range(3)] for r in range(2)]
    cov_xx = sum(wide[0][k] * axes[0][k] for k in range(3)) + dilation
    cov_xy = sum(wide[0][k] * axes[1][k] for k in range(3))
    cov_yy = sum(wide[1][k] * axes[1][k] for k in range(3)) + dilation
    rdet = 1.0 / (cov_xx * cov_yy - cov_xy * cov_xy)
    conic = (cov_yy * rdet, -cov_xy * rdet, cov_xx * rdet)
    rlen = lax.rsqrt(off[0] * off[0] + off[1] * off[1] + off[2] * off[2])
    way = [off[a] * rlen for a in range(3)]
    return dict(
        rot=rot, inv=inv, u=u, v=v, finv=finv, scale=scale, rnorm=rnorm, rotor=(w, x, y, z), turn=turn,
        screen=screen, axes=axes, wide=wide, conic=conic, rlen=rlen, way=way,
    )


def shade(feat, cam):
    off = [feat(a) - cam[9 + a] for a in range(3)]
    rlen = lax.rsqrt(off[0] * off[0] + off[1] * off[1] + off[2] * off[2])
    basis = sh_basis(*[off[a] * rlen for a in range(3)])
    colours = []
    for k in range(3):
        total = 0.5 + sh_const[0] * feat(11 + 16 * k)
        for b in range(1, 16):
            total = total + feat(11 + 16 * k + b) * basis[b]
        colours.append(total)
    return colours


def project_rows(feat, cam):
    part = project_parts(feat, cam)
    mean_x = focal_length * part["u"] + center_x
    mean_y = focal_length * part["v"] + center_y
    logit = feat(10)
    log_opacity = jnp.minimum(logit, 0.0) - jnp.log(1.0 + jnp.exp(-jnp.abs(logit)))
    return [mean_x, mean_y, *part["conic"], log_opacity]


def project_pull(feat, cam, grads, put):
    part = project_parts(feat, cam)
    g_mx, g_my, g_a, g_b, g_c, g_o = grads[:6]
    g_col = grads[6:9]
    way, rlen = part["way"], part["rlen"]
    basis = sh_basis(*way)
    pulled = [None]
    for k in range(3):
        put(11 + 16 * k, sh_const[0] * g_col[k])
    for b in range(1, 16):
        total = 0.0
        for k in range(3):
            put(11 + 16 * k + b, g_col[k] * basis[b])
            total = total + g_col[k] * feat(11 + 16 * k + b)
        pulled.append(total)
    g_way = sh_pull(pulled, *way)
    along = way[0] * g_way[0] + way[1] * g_way[1] + way[2] * g_way[2]
    g_off = [(g_way[a] - way[a] * along) * rlen for a in range(3)]
    put(10, g_o / (1.0 + jnp.exp(feat(10))))
    a, b, c = part["conic"]
    g_xx = -(a * a * g_a + a * b * g_b + b * b * g_c)
    g_xy = -(2.0 * a * b * g_a + (a * c + b * b) * g_b + 2.0 * b * c * g_c)
    g_yy = -(b * b * g_a + b * c * g_b + c * c * g_c)
    axes, wide, turn, screen = part["axes"], part["wide"], part["turn"], part["screen"]
    for k in range(3):
        g_scale = (
            g_xx * axes[0][k] * wide[0][k]
            + g_xy * axes[0][k] * wide[1][k]
            + g_yy * axes[1][k] * wide[1][k]
        )
        put(3 + k, 2.0 * g_scale)
    g_axes = [
        [2.0 * g_xx * wide[0][k] + g_xy * wide[1][k] for k in range(3)],
        [2.0 * g_yy * wide[1][k] + g_xy * wide[0][k] for k in range(3)],
    ]
    g_screen = [
        [sum(g_axes[r][k] * turn[c][k] for k in range(3)) for c in range(3)] for r in range(2)
    ]
    gm = [
        [g_axes[0][k] * screen[0][c] + g_axes[1][k] * screen[1][c] for k in range(3)]
        for c in range(3)
    ]
    w, x, y, z = part["rotor"]
    up_xy, up_xz, up_yz = gm[0][1] + gm[1][0], gm[0][2] + gm[2][0], gm[1][2] + gm[2][1]
    un_xy, un_xz, un_yz = gm[1][0] - gm[0][1], gm[0][2] - gm[2][0], gm[2][1] - gm[1][2]
    g_rotor = [
        2.0 * (z * un_xy + y * un_xz + x * un_yz),
        2.0 * (y * up_xy + z * up_xz + w * un_yz - 2.0 * x * (gm[1][1] + gm[2][2])),
        2.0 * (x * up_xy + z * up_yz + w * un_xz - 2.0 * y * (gm[0][0] + gm[2][2])),
        2.0 * (x * up_xz + y * up_yz + w * un_xy - 2.0 * z * (gm[0][0] + gm[1][1])),
    ]
    rotor = (w, x, y, z)
    along = sum(rotor[i] * g_rotor[i] for i in range(4))
    for i in range(4):
        put(6 + i, (g_rotor[i] - rotor[i] * along) * part["rnorm"])
    rot, inv, finv, u, v = part["rot"], part["inv"], part["finv"], part["u"], part["v"]
    g_u = focal_length * g_mx - finv * sum(g_screen[0][c] * rot[2][c] for c in range(3))
    g_v = focal_length * g_my - finv * sum(g_screen[1][c] * rot[2][c] for c in range(3))
    g_f = sum(g_screen[r][c] * screen[r][c] for r in range(2) for c in range(3))
    g_in = [g_u * inv, g_v * inv, -(g_f + g_u * u + g_v * v) * inv]
    for axis in range(3):
        put(
            axis,
            g_off[axis] + rot[0][axis] * g_in[0] + rot[1][axis] * g_in[1] + rot[2][axis] * g_in[2],
        )


def split(value):
    high = value.astype(BF16)
    return high, (value - high.astype(F32)).astype(BF16)


def matmul(a, b, dims=((1,), (0,))):
    return lax.dot_general(a, b, (dims, ((), ())), preferred_element_type=F32)


def spread_features(parts, scratch, count):
    tiles = sum(part.shape[1] for part in parts) // LANES
    at = 0
    for part in parts:
        for first in range(0, part.shape[1], LANES):
            for row in range(0, count, 8):
                rows = min(8, count - row)
                scratch[pl.ds(row * tiles + at, rows, stride=tiles), :] = part[
                    row : row + rows, first : first + LANES
                ]
            at += 1
    return tiles


def pack_kernel(shards, where, *refs):
    sources, (info, params, shard_of, local_of, goal, place_s, sems) = refs[:4], refs[4:]
    group = where[0]
    loads = [
        pltpu.make_async_copy(source, held, sems.at[k])
        for k, (source, held) in enumerate(zip(sources, (shard_of, local_of, goal, params)))
    ]
    for load in loads:
        load.start()
    for load in loads[:3]:
        load.wait()
    width = info.shape[1]
    tile_count, listed = local_of.shape
    rows_each = (info.shape[0] - 4) // tile_count
    columns = rows_each * width
    chunk = columns // shards
    info[0:3, :] = goal[...]
    for t in range(tile_count):
        place = (shard_of[t] ^ group) * chunk + (local_of[t : t + 1, :] - group * chunk)
        info[3:4, t * listed : (t + 1) * listed] = place.astype(F32)
        row_i = lax.broadcasted_iota(jnp.int32, (LANES, LANES), 0)
        col_i = lax.broadcasted_iota(jnp.int32, (LANES, LANES), 1)
        for first in range(0, listed, LANES):
            spread = jnp.broadcast_to(place[:, first : first + LANES].astype(F32), (LANES, LANES))
            place_s[first : first + LANES, :] = jnp.broadcast_to(
                jnp.sum(jnp.where(row_i == col_i, spread, 0.0), axis=1, keepdims=True), (LANES, LANES)
            )
        lane_of = lax.broadcasted_iota(jnp.int32, (8, LANES), 1).astype(F32)
        row_of = lax.broadcasted_iota(jnp.int32, (8, LANES), 0).astype(F32)
        for s in range(columns // LANES):
            best = jnp.full((8, LANES), -1.0, F32)
            column = lane_of + float(s * LANES)
            for first in range(0, listed, 8):
                best = jnp.where(
                    place_s[first : first + 8, :] == column, row_of + float(first), best
                )
            best = jnp.max(best, axis=0, keepdims=True)
            row, at = 4 + t * rows_each + s * LANES // width, s * LANES % width
            info[row : row + 1, at : at + LANES] = best
    loads[3].wait()


def pack(group, params, target, hit_shard, hit_local, shards):
    columns = params.shape[1]
    tile_count, listed = hit_local.shape
    width = target.shape[1]
    rows = 4 + tile_count * (columns // width)
    args = (hit_shard.reshape(tile_count, 1, listed), hit_local, target, params)
    return call(
        functools.partial(pack_kernel, shards),
        "pack",
        (jax.ShapeDtypeStruct((rows, width), F32), jax.ShapeDtypeStruct(params.shape, F32)),
        [smem()] + [pl.BlockSpec(memory_space=pltpu.HBM)] * 4,
        [
            pltpu.VMEM((tile_count, 1, listed), jnp.int32),
            pltpu.VMEM((tile_count, listed), jnp.int32),
            pltpu.VMEM(target.shape, F32),
            pltpu.VMEM((listed, LANES), F32),
            pltpu.SemaphoreType.DMA((4,)),
        ],
        (group.reshape(1),) + tuple(pltpu.with_memory_space_constraint(a, pltpu.HBM) for a in args),
        (vmem(), any_space()),
    )


def sent_rows(views):
    return (11 + 3 * views + 7) // 8 * 8


def cut_kernel(pieces, where, cams, params, *refs):
    parts, (feats, rows) = refs[:pieces], refs[pieces:]
    views = cams.shape[0]
    count = sent_rows(views)
    slabs = spread_features([params], feats, params.shape[0])

    def feat(f):
        return feats[f * slabs : (f + 1) * slabs, :]

    values = [feat(f) for f in range(11)]
    for v in range(views):
        values += shade(feat, [cams[v, i] for i in range(12)])
    values += [jnp.zeros((slabs, LANES), F32)] * (count - len(values))
    for f, value in enumerate(values):
        rows[pl.ds(f, slabs, stride=count), :] = value
    each = slabs // pieces
    for d in range(pieces):
        for h in range(each):
            first = (((where[0] ^ d) % pieces) * each + h) * count
            parts[d][:, h * LANES : (h + 1) * LANES] = rows[
                pl.ds(pl.multiple_of(first, 8), count), :
            ]


def cut(group, cameras, params, pieces):
    features, columns = params.shape
    slabs = columns // LANES
    count = sent_rows(cameras.shape[0])
    return list(
        call(
            functools.partial(cut_kernel, pieces),
            "cut",
            (jax.ShapeDtypeStruct((count, columns // pieces), F32),) * pieces,
            [smem()] * 2 + [vmem()],
            [
                pltpu.VMEM((features * slabs, LANES), F32),
                pltpu.VMEM((count * slabs, LANES), F32),
            ],
            (group.reshape(1), cameras, params),
        )
    )


def lane_gather(source, lane):
    return jnp.take_along_axis(source, lane, axis=1, mode="promise_in_bounds")


def pixel_basis(pixels):
    pixel = lax.broadcasted_iota(jnp.int32, (8, pixels), 1)
    row = lax.broadcasted_iota(jnp.int32, (8, pixels), 0)
    middle = 0.5 * TILE_SIDE - 0.5
    u = (pixel % TILE_SIDE).astype(F32) - middle
    v = (pixel // TILE_SIDE).astype(F32) - middle
    value = jnp.where(row == 0, 1.0, 0.0)
    for at, term in ((1, u), (2, v), (3, u * u), (4, u * v), (5, v * v)):
        value = jnp.where(row == at, term, value)
    return value


def composite(tiles, first_group, me, rows, info_s, rendered, work):
    alpha_s, weight_s, pull_s, push_s, weight_2, entry_s, coef_s, colour_s, sums_s, index_s, acc_s, ninth_s = work
    groups = info_s.shape[0]
    listed = acc_s.shape[0] * LANES
    tile_count = info_s.shape[2] // listed
    pixels = info_s.shape[2] // tile_count
    parts = pixels // LANES
    halves = listed // LANES
    tiles_here = groups * tile_count
    spans = tiles_here * parts
    slabs = rows.shape[0] // ROWS
    side = TILE_SIDE
    first_col, first_row = tiles

    def of_span(span):
        return pl.ds(span, listed, stride=LIST_STEP)

    def of_place(place):
        return pl.ds(place * LIST_STEP, spans)

    basis = pixel_basis(pixels)
    basis_3 = jnp.concatenate([basis, basis, basis], axis=0).astype(BF16)
    row_of = lax.broadcasted_iota(jnp.int32, (8, listed), 0)

    entries = []
    for n in range(tiles_here):
        g, t = n // tile_count, n % tile_count
        found = []
        for h in range(halves):
            first = t * listed + h * LANES
            at = info_s[g, 3:4, first : first + LANES].astype(jnp.int32)
            index_s[n * halves + h : n * halves + h + 1, :] = at
            at = jnp.broadcast_to(at, (8, LANES))
            lane, slab = at & (LANES - 1), at >> 7
            value = lane_gather(rows[0:8, :], lane)
            for s in range(1, slabs):
                value = jnp.where(
                    slab == s, lane_gather(rows[s * ROWS : s * ROWS + 8, :], lane), value
                )
            found.append(value)
        entries.append(jnp.concatenate(found, axis=1))
        for h in range(halves):
            entry_s[h, 8 * n : 8 * n + 8, :] = found[h]
    at = index_s[...]
    lane, slab = at & (LANES - 1), at >> 7
    ninth = lane_gather(rows[8:16, :], lane)
    for s in range(1, slabs):
        ninth = jnp.where(
            slab == s, lane_gather(rows[s * ROWS + 8 : s * ROWS + 16, :], lane), ninth
        )

    def of_lists(ref, f):
        at = pl.ds(f, tiles_here, stride=8)
        return jnp.concatenate([ref[h, at, :] for h in range(halves)], axis=1)

    tile_of = lax.broadcasted_iota(jnp.int32, (tiles_here, listed), 0)
    slot = (me ^ (first_group + tile_of // tile_count)) * tile_count + tile_of % tile_count
    mean_u = of_lists(entry_s, 2) - (((first_col + slot % 4) * side).astype(F32) + 0.5 * side)
    mean_v = of_lists(entry_s, 3) - (((first_row + slot // 4) * side).astype(F32) + 0.5 * side)
    quad_a = -0.5 * of_lists(entry_s, 4)
    quad_b = -of_lists(entry_s, 5)
    quad_c = -0.5 * of_lists(entry_s, 6)
    slope_u = 2.0 * quad_a * mean_u + quad_b * mean_v
    slope_v = 2.0 * quad_c * mean_v + quad_b * mean_u
    level = 0.5 * (slope_u * mean_u + slope_v * mean_v) + of_lists(entry_s, 7)
    for f, value in enumerate((level, -slope_u, -slope_v, quad_a, quad_b, quad_c)):
        for n in range(tiles_here):
            coef_s[f : f + 1, n * listed : (n + 1) * listed] = value[n : n + 1]
    coef_s[6:8, :] = jnp.zeros((2, tiles_here * listed), F32)
    coef = coef_s[...]
    terms = []
    for _ in range(3):
        terms.append(coef.astype(BF16).astype(F32))
        coef = coef - terms[-1]
    down = ((0,), (0,))
    power = matmul(jnp.concatenate(terms, axis=0).astype(BF16), basis_3, down)
    for n in range(tiles_here):
        for part in range(parts):
            alpha_s[of_span(n * parts + part), :] = jnp.exp(
                power[n * listed : (n + 1) * listed, part * LANES : (part + 1) * LANES]
            )
    colour_s[...] = jnp.zeros(colour_s.shape, F32)
    hues = []
    for n in range(tiles_here):
        last = jnp.concatenate([ninth[n * halves + h : n * halves + h + 1] for h in range(halves)], axis=1)
        colours = jnp.where(row_of < 2, entries[n], jnp.where(row_of == 2, last, 0.0))
        high = colours.astype(BF16).astype(F32)
        low = colours - high
        here = slice(n * listed, (n + 1) * listed)
        for at, value in ((0, high), (8, low), (16, high)):
            colour_s[24 * n + at : 24 * n + at + 8, here] = value
        hues.append(jnp.concatenate([high, low], axis=0).astype(BF16))

    unroll, quad = 128, 4
    steps = listed // unroll

    def forward(step, passed):
        for j in range(0, unroll, quad):
            at = [of_place(step * unroll + j + i) for i in range(quad)]
            alpha = [alpha_s[at[i], :] for i in range(quad)]
            keep = [1.0 - alpha[i] for i in range(quad)]
            two = keep[0] * keep[1]
            three = two * keep[2]
            weight_s[at[0], :] = alpha[0] * passed
            weight_s[at[1], :] = (alpha[1] * keep[0]) * passed
            weight_s[at[2], :] = (alpha[2] * two) * passed
            weight_s[at[3], :] = (alpha[3] * three) * passed
            passed = passed * (two * (keep[2] * keep[3]))
        return passed

    nought = jnp.zeros((spans, LANES), F32)
    lax.fori_loop(0, steps, forward, nought + 1.0)

    errors = []
    for n in range(tiles_here):
        g, t = n // tile_count, n % tile_count
        for part in range(parts):
            at = slice((n * parts + part) * LANES, (n * parts + part + 1) * LANES)
            weight_2[:listed, at], weight_2[listed:, at] = split(
                weight_s[of_span(n * parts + part), :]
            )
        at = slice(n * pixels, (n + 1) * pixels)
        image = matmul(hues[n], weight_2[:listed, at])
        image = image[0:8] + image[8:16] + matmul(hues[n], weight_2[listed:, at])[0:8]
        here = slice(t * pixels, (t + 1) * pixels)
        if rendered is not None and g == 0:
            rendered[:, here] = image[0:3]
        error = image - info_s[g, 0:8, here]
        high = error.astype(BF16).astype(F32)
        low = error - high
        errors += [high, high, low]

        hue = jnp.concatenate([high, low], axis=0).astype(BF16)
        across = ((1,), (1,))
        grads = matmul(hue, weight_2[:listed, at], across) + matmul(hue, weight_2[listed:, at], across)
        grads = grads[0:8] + grads[8:16]
        for h in range(halves):
            acc_s[h, 8 * n : 8 * n + 8, :] = grads[:, h * LANES : (h + 1) * LANES]
            row = n * halves + h
            ninth_s[row : row + 1, :] = grads[2:3, h * LANES : (h + 1) * LANES]
    pull = matmul(colour_s[...].astype(BF16), jnp.concatenate(errors, axis=0).astype(BF16), down)
    for n in range(tiles_here):
        for part in range(parts):
            pull_s[of_span(n * parts + part), :] = pull[
                n * listed : (n + 1) * listed, part * LANES : (part + 1) * LANES
            ]

    def backward(back, behind):
        for j in range(0, unroll, quad):
            at = [of_place(listed - 1 - (back * unroll + j + i)) for i in range(quad)]
            alpha = [alpha_s[at[i], :] for i in range(quad)]
            pull = [pull_s[at[i], :] for i in range(quad)]
            keep = [1.0 - alpha[i] for i in range(quad)]
            own = alpha[0] * pull[0]
            seen, through = behind, keep[0]
            for i in range(quad):
                push_s[at[i], :] = weight_s[at[i], :] * (pull[i] - seen)
                if i > 0:
                    own = own * keep[i] + alpha[i] * pull[i]
                    through = through * keep[i]
                seen = behind * through + own
            behind = seen
        return behind

    lax.fori_loop(0, steps, backward, nought)

    basis = basis.astype(BF16)
    for n in range(tiles_here):
        high, low = split(
            jnp.concatenate([push_s[of_span(n * parts + part), :] for part in range(parts)], axis=1)
        )
        moments = matmul(basis, high, across) + matmul(basis, low, across)
        for h in range(halves):
            sums_s[h, 8 * n : 8 * n + 8, :] = moments[:, h * LANES : (h + 1) * LANES]
    m_00, m_10, m_01, m_20, m_11, m_02 = [
        of_lists(sums_s, m) for m in range(6)
    ]
    n_10 = m_10 - mean_u * m_00
    n_01 = m_01 - mean_v * m_00
    for f, value in (
        (2, -(2.0 * quad_a * n_10 + quad_b * n_01)),
        (3, -(2.0 * quad_c * n_01 + quad_b * n_10)),
        (4, -0.5 * (m_20 - mean_u * (m_10 + n_10))),
        (5, -(m_11 - mean_u * m_01 - mean_v * n_10)),
        (6, -0.5 * (m_02 - mean_v * (m_01 + n_01))),
        (7, m_00),
    ):
        for h in range(halves):
            acc_s[h, pl.ds(f, tiles_here, stride=8), :] = value[:, h * LANES : (h + 1) * LANES]


def pool_sum(slab, info_s, acc_s, ninth_s):
    groups, _, width = info_s.shape
    listed = acc_s.shape[0] * LANES
    tile_count = width // listed
    halves = listed // LANES
    rows_each = (info_s.shape[1] - 4) // tile_count
    row_of = lax.broadcasted_iota(jnp.int32, (8, LANES), 0)

    totals, every = [], None
    for g in range(groups):
        total = jnp.zeros((8, LANES), F32)
        for t in range(tile_count):
            row, first = 4 + t * rows_each + slab * LANES // width, slab * LANES % width
            at = info_s[g, row : row + 1, first : first + LANES].astype(jnp.int32)
            at = jnp.broadcast_to(at, (8, LANES))
            n = g * tile_count + t
            every = at if every is None else jnp.where(row_of >= n * halves, at, every)
            lane, half = at & (LANES - 1), at >> 7
            for h in range(halves):
                here = lane_gather(acc_s[h, 8 * n : 8 * n + 8, :], lane)
                total = total + jnp.where(half == h, here, 0.0)
        totals.append(total)
    here = lane_gather(ninth_s[...], every & (LANES - 1))
    ninth = jnp.where(every >> 7 == row_of % halves, here, 0.0)
    return totals[0] + totals[1], jnp.sum(ninth, axis=0, keepdims=True)


def block_start(tile_id):
    within = tile_id % (TILES_X * TILES_Y)
    return (within % TILES_X) // 4 * 4, (within // TILES_X) // 2 * 2


def near_kernel(pieces, tile_ids, cams, where, own, other, *refs):
    parts = refs[:pieces]
    rendered, rows, partial, feats, info_s, *work = refs[pieces:]
    view = tile_ids[0] // (TILES_X * TILES_Y)
    cam = [cams[view, i] for i in range(12)]
    slabs = spread_features(parts, feats, parts[0].shape[0])
    projected = project_rows(lambda f: feats[f * slabs : (f + 1) * slabs, :], cam)
    colours = []
    for k in range(3):
        first = pl.multiple_of((11 + 3 * view + k) * slabs, slabs)
        colours.append(feats[pl.ds(first, slabs), :])
    for f, value in enumerate(colours[:2] + projected + [colours[2]] * 8):
        rows[pl.ds(f, slabs, stride=ROWS), :] = value
    info_s[0] = own[...]
    info_s[1] = other[...]
    composite(block_start(tile_ids[0]), 0, where[0], rows, info_s, rendered, work)
    for s in range(slabs):
        at = slice(s * LANES, (s + 1) * LANES)
        partial[0:8, at], partial[8:9, at] = pool_sum(s, info_s, *work[-2:])


def far_kernel(blocks, tile_ids, where, rows, partial, infos, *refs):
    *packets, info_s = refs[: len(refs) - 12]
    work = refs[len(refs) - 12 :]
    half = infos.shape[0] // 2
    info_s[0] = infos[:half, :]
    info_s[1] = infos[half:, :]
    composite(block_start(tile_ids[0]), 2, where[0], rows, info_s, None, work)
    share = (tile_ids[0] // (TILES_X * TILES_Y)).astype(F32)
    row_of = lax.broadcasted_iota(jnp.int32, (8, LANES), 0)
    lane_of = lax.broadcasted_iota(jnp.int32, (8, LANES), 1)
    chunk = packets[0].shape[1]
    for s in range(rows.shape[0] // ROWS):
        total, ninth = pool_sum(s, info_s, *work[-2:])
        total = total + partial[0:8, s * LANES : (s + 1) * LANES]
        ninth = ninth + partial[8:9, s * LANES : (s + 1) * LANES]
        if blocks == 1:
            mine = share
        else:
            column = s * LANES + lane_of
            mine = jnp.where(column % where[2] // (where[2] // blocks) == where[1], share, 0.0)
        at = slice(s * LANES % chunk, s * LANES % chunk + LANES)
        packets[s * LANES // chunk][0:8, at] = total
        packets[s * LANES // chunk][8:16, at] = jnp.where(
            row_of == 0, jnp.broadcast_to(ninth, (8, LANES)), mine
        )


def join_kernel(first, second, out):
    half = first.shape[0]
    out[:half, :] = first[...]
    out[half:, :] = second[...]


def update_kernel(pieces, follows, where, cams, params, adam_m, adam_v, *refs):
    packets, refs = refs[:pieces], refs[pieces + 3 * follows :]
    sinks, (feats, rows, grads, made, sems) = refs[:3], refs[3:]
    features = params.shape[0]
    chunk = packets[0].shape[1]
    width = pieces * chunk
    slabs = width // LANES
    start = (where[0] ^ where[1]) // pieces * pieces * chunk
    for d in range(pieces):
        for h in range(chunk // LANES):
            slab = (where[0] ^ where[1] ^ d) % pieces * (chunk // LANES) + h
            rows[pl.ds(slab, ROWS, stride=slabs), :] = packets[d][:, h * LANES : (h + 1) * LANES]
    pulled = [rows[f * slabs : (f + 1) * slabs, :] for f in range(10)]
    view = pulled[9]
    cam = []
    for i in range(12):
        value = jnp.full((slabs, LANES), cams[0, i], F32)
        for v in range(1, cams.shape[0]):
            value = jnp.where(view == float(v), cams[v, i], value)
        cam.append(value)

    def put(f, value):
        grads[f * slabs : (f + 1) * slabs, :] = value

    def column(s):
        return pl.ds(pl.multiple_of(start + s * LANES, LANES), LANES)

    for s in range(slabs):
        for row in range(0, features, 8):
            count = min(8, features - row)
            feats[pl.ds(row * slabs + s, count, stride=slabs), :] = params[
                row : row + count, column(s)
            ]
    project_pull(
        lambda f: feats[f * slabs : (f + 1) * slabs, :], cam, pulled[2:8] + pulled[:2] + pulled[8:9], put
    )
    rate = learn_rate / (1.0 - beta_one**adam_steps)
    unbias = 1.0 / (1.0 - beta_two**adam_steps)
    stores = []
    order = list(range(16, features, 8)) + [0, 8]
    for row in order:
        count = min(8, features - row)
        span = slice(row, row + count)
        for s in range(slabs):
            here = (span, slice(s * LANES, (s + 1) * LANES))
            grad = grads[pl.ds(row * slabs + s, count, stride=slabs), :]
            moment = beta_one * adam_m[span, column(s)] + (1.0 - beta_one) * grad
            second = beta_two * adam_v[span, column(s)] + (1.0 - beta_two) * grad * grad
            made.at[1][here] = moment
            made.at[2][here] = second
            made.at[0][here] = params[span, column(s)] - rate * moment / (
                jnp.sqrt(second * unbias) + adam_eps
            )
        if row % 16 == 8 or row + count == features:
            first = row // 16 * 16
            span = pl.ds(first, row + count - first)
            columns = pl.ds(pl.multiple_of(start, LANES), width)
            for k in range(3):
                store = pltpu.make_async_copy(
                    made.at[k, span], sinks[k].at[span, columns], sems.at[k, first // 16]
                )
                store.start()
                stores.append(store)
    for store in stores:
        store.wait()


def vmem():
    return pl.BlockSpec(memory_space=pltpu.VMEM)


def smem():
    return pl.BlockSpec(memory_space=pltpu.SMEM)


def any_space():
    return pl.BlockSpec(memory_space=pl.ANY)


def call(kernel, name, out_shape, in_specs, scratch, args, out_specs=None, grant=32):
    return pl.pallas_call(
        kernel,
        out_shape=out_shape,
        in_specs=in_specs,
        out_specs=out_specs or tuple(vmem() for _ in out_shape),
        scratch_shapes=scratch,
        compiler_params=pltpu.CompilerParams(vmem_limit_bytes=grant * 1024 * 1024),
        name=name,
    )(*args)


def work_shapes(tile_count, pixels, listed):
    tiles = 2 * tile_count
    spans = tiles * pixels // LANES
    assert spans < LIST_STEP and tiles * listed // LANES == 8 and tiles == 4
    return [pltpu.VMEM((listed * LIST_STEP, LANES), F32)] * 4 + [
        pltpu.VMEM((2 * listed, spans * LANES), BF16),
        pltpu.VMEM((listed // LANES, 8 * tiles, LANES), F32),
        pltpu.VMEM((8, tiles * listed), F32),
        pltpu.VMEM((24 * tiles, tiles * listed), F32),
        pltpu.VMEM((listed // LANES, 8 * tiles, LANES), F32),
        pltpu.VMEM((8, LANES), jnp.int32),
        pltpu.VMEM((listed // LANES, 8 * tiles, LANES), F32),
        pltpu.VMEM((8, LANES), F32),
    ]


def near(tile_ids, cameras, where, own, other, parts, tile_count):
    width = sum(part.shape[1] for part in parts)
    features = parts[0].shape[0]
    slabs = width // LANES
    pixels = listed = own.shape[1] // tile_count
    return call(
        functools.partial(near_kernel, len(parts)),
        "near",
        (
            jax.ShapeDtypeStruct((3, own.shape[1]), F32),
            jax.ShapeDtypeStruct((ROWS * slabs, LANES), F32),
            jax.ShapeDtypeStruct((ROWS, width), F32),
        ),
        [smem()] * 3 + [vmem()] * (2 + len(parts)),
        [pltpu.VMEM((features * slabs, LANES), F32), pltpu.VMEM((2,) + own.shape, F32)]
        + work_shapes(tile_count, pixels, listed),
        (tile_ids, cameras, where, own, other, *parts),
    )


def far(tile_ids, where, rows, partial, infos, pieces, tile_count, blocks):
    width = partial.shape[1]
    pixels = listed = infos.shape[1] // tile_count
    info = (infos.shape[0] // 2, infos.shape[1])
    return call(
        functools.partial(far_kernel, blocks),
        "far",
        (jax.ShapeDtypeStruct((ROWS, width // pieces), F32),) * pieces,
        [smem()] * 2 + [vmem()] * 3,
        [pltpu.VMEM((2,) + info, F32)] + work_shapes(tile_count, pixels, listed),
        (tile_ids, where, rows, partial, infos),
    )


def join(first, second):
    shape = (2 * first.shape[0], first.shape[1])
    return call(
        join_kernel, "join", (jax.ShapeDtypeStruct(shape, F32),), [vmem()] * 2, [], (first, second)
    )[0]


def update(own, first, cameras, params, adam_m, adam_v, packets, before):
    features = params.shape[0]
    width = sum(packet.shape[1] for packet in packets)
    slabs = width // LANES
    shape = jax.ShapeDtypeStruct(params.shape, F32)
    at = 5 + len(packets)
    return pl.pallas_call(
        functools.partial(update_kernel, len(packets), len(before) > 0),
        out_shape=(shape, shape, shape),
        in_specs=[smem()] * 2
        + [vmem()] * (3 + len(packets))
        + [any_space()] * len(before),
        out_specs=(any_space(),) * 3,
        scratch_shapes=[
            pltpu.VMEM((features * slabs, LANES), F32),
            pltpu.VMEM((ROWS * slabs, LANES), F32),
            pltpu.VMEM((features * slabs, LANES), F32),
            pltpu.VMEM((3, features, width), F32),
            pltpu.SemaphoreType.DMA((3, (features + 15) // 16)),
        ],
        input_output_aliases={at + k: k for k in range(len(before))},
        compiler_params=pltpu.CompilerParams(vmem_limit_bytes=32 * 1024 * 1024),
        name="update",
    )(
        jnp.stack([own, jnp.int32(first)]).astype(jnp.int32),
        cameras, params, adam_m, adam_v, *packets, *before,
    )


def swap(value, axis, d):
    if d == 0:
        return value
    return lax.ppermute(value, axis, [(k, k ^ d) for k in range(lax.axis_size(axis))])


def local(params, adam_m, adam_v, cameras, target, tile_ids, hit_shard, hit_local):
    width = params.shape[1]
    tile_count, listed = hit_local.shape
    shards = lax.axis_size("gs")
    along = lax.axis_size("tile")
    chunk = width // shards
    group = lax.axis_index("gs")
    seat = lax.axis_index("tile")
    aligned = chunk % LANES == 0
    team = BLOCK_TILES // tile_count
    assert team == 4
    blocks = along // team

    info, params = pack(group, params, target, hit_shard, hit_local, shards)
    parts = cut(group, cameras, params, shards if aligned else 1)
    if not aligned:
        parts = [
            lax.dynamic_slice_in_dim(parts[0], (group ^ d) * chunk, chunk, axis=1)
            for d in range(shards)
        ]
    parts = [swap(parts[d], "gs", d) for d in range(shards)]
    beside = swap(info, "tile", 1)
    beyond = swap(join(info, beside), "tile", 2)
    if not aligned:
        parts = [jnp.concatenate(parts, axis=1)]
    where = jnp.stack([seat % team, seat // team, jnp.int32(chunk)]).astype(jnp.int32)
    rendered, rows, partial = near(tile_ids, cameras, where, info, beside, parts, tile_count)
    packets = far(tile_ids, where, rows, partial, beyond, len(parts), tile_count, blocks)
    if not aligned:
        packets = [packets[0][:, d * chunk : (d + 1) * chunk] for d in range(shards)]
    packets = [swap(packets[d], "gs", d) for d in range(shards)]
    if blocks > 1:
        packets = [block_sum(packet, along, team) for packet in packets]
    if aligned:
        own = group
    else:
        packets = [jnp.stack(packets)[jnp.arange(shards) ^ group].transpose(1, 0, 2).reshape(ROWS, -1)]
        own = jnp.int32(0)
    made = ()
    count = max(1, len(packets) // 2)
    for first in range(0, len(packets), count):
        made = update(
            own, first, cameras, params, adam_m, adam_v, packets[first : first + count], made
        )
    new_params, new_m, new_v = made
    return (rendered, new_params, new_m, new_v)


def block_sum(packet, along, team):
    step = team
    while step < along:
        packet = packet + swap(packet, "tile", step)
        step *= 2
    return packet


def solution(mesh):
    return jax.shard_map(
        local,
        mesh=mesh,
        in_specs=(
            P(None, ("groups", "gs")),
            P(None, ("groups", "gs")),
            P(None, ("groups", "gs")),
            P("groups", None),
            P(None, ("groups", "gs", "tile")),
            P(("groups", "gs", "tile")),
            P(("groups", "gs", "tile"), None, None),
            P(("groups", "gs", "tile"), None),
        ),
        out_specs=(
            P(None, ("groups", "gs", "tile")),
            P(None, ("groups", "gs")),
            P(None, ("groups", "gs")),
            P(None, ("groups", "gs")),
        ),
        check_vma=False,
    )
```

```python
import functools

import jax
import jax.numpy as jnp
from jax import lax
from jax.experimental import pallas as pl
from jax.experimental.pallas import tpu as pltpu
from jax.sharding import PartitionSpec as P

TILES_X = 120
TILES_Y = 68
TILE_SIDE = 16
BLOCK_TILES = 8
LANES = 128
ROWS = 16
LIST_STEP = 9
F32 = jnp.float32
BF16 = jnp.bfloat16

focal_length = 1000.0
center_x = 960.0
center_y = 540.0
dilation = 0.3
beta_one = 0.9
beta_two = 0.999
learn_rate = 0.01
adam_eps = 1e-08
adam_steps = 100.0
sh_const = (
    0.28209479177387814,
    0.4886025119029199,
    1.0925484305920792,
    0.31539156525252005,
    0.5462742152960396,
    0.5900435899266435,
    2.890611442640554,
    0.4570457994644658,
    0.3731763325901154,
    1.445305721320277,
)


def sh_basis(x, y, z):
    s = sh_const
    xx, yy, zz = x * x, y * y, z * z
    return [
        None,
        -s[1] * y,
        s[1] * z,
        -s[1] * x,
        s[2] * (x * y),
        -s[2] * (y * z),
        s[3] * (2.0 * zz - xx - yy),
        -s[2] * (x * z),
        s[4] * (xx - yy),
        -s[5] * y * (3.0 * xx - yy),
        s[6] * (x * y) * z,
        -s[7] * y * (4.0 * zz - xx - yy),
        s[8] * z * (2.0 * zz - 3.0 * xx - 3.0 * yy),
        -s[7] * x * (4.0 * zz - xx - yy),
        s[9] * z * (xx - yy),
        -s[5] * x * (xx - 3.0 * yy),
    ]


def sh_pull(h, x, y, z):
    s = sh_const
    xx, yy, zz = x * x, y * y, z * z
    xy, xz, yz = x * y, x * z, y * z
    diff = xx - yy
    ring = 4.0 * zz - xx - yy
    g_x = (
        -s[1] * h[3]
        + s[2] * (h[4] * y - h[7] * z)
        - (2.0 * s[3]) * h[6] * x
        + (2.0 * s[4]) * h[8] * x
        - (6.0 * s[5]) * h[9] * xy
        + s[6] * h[10] * yz
        + (2.0 * s[7]) * h[11] * xy
        - (6.0 * s[8]) * h[12] * xz
        - s[7] * h[13] * (ring - 2.0 * xx)
        + (2.0 * s[9]) * h[14] * xz
        - (3.0 * s[5]) * h[15] * diff
    )
    g_y = (
        -s[1] * h[1]
        + s[2] * (h[4] * x - h[5] * z)
        - (2.0 * s[3]) * h[6] * y
        - (2.0 * s[4]) * h[8] * y
        - (3.0 * s[5]) * h[9] * diff
        + s[6] * h[10] * xz
        - s[7] * h[11] * (ring - 2.0 * yy)
        - (6.0 * s[8]) * h[12] * yz
        + (2.0 * s[7]) * h[13] * xy
        - (2.0 * s[9]) * h[14] * yz
        + (6.0 * s[5]) * h[15] * xy
    )
    g_z = (
        s[1] * h[2]
        - s[2] * (h[5] * y + h[7] * x)
        + (4.0 * s[3]) * h[6] * z
        + s[6] * h[10] * xy
        - (8.0 * s[7]) * (h[11] * yz + h[13] * xz)
        + s[8] * h[12] * (6.0 * zz - 3.0 * xx - 3.0 * yy)
        + s[9] * h[14] * diff
    )
    return g_x, g_y, g_z


def project_parts(feat, cam):
    rot = [[cam[3 * r + c] for c in range(3)] for r in range(3)]
    off = [feat(a) - cam[9 + a] for a in range(3)]
    in_cam = [rot[r][0] * off[0] + rot[r][1] * off[1] + rot[r][2] * off[2] for r in range(3)]
    inv = 1.0 / in_cam[2]
    u = in_cam[0] * inv
    v = in_cam[1] * inv
    finv = focal_length * inv
    scale = [jnp.exp(2.0 * feat(3 + a)) for a in range(3)]
    quat = [feat(6 + a) for a in range(4)]
    rnorm = lax.rsqrt(quat[0] * quat[0] + quat[1] * quat[1] + quat[2] * quat[2] + quat[3] * quat[3])
    w, x, y, z = [q * rnorm for q in quat]
    turn = [
        [1.0 - 2.0 * (y * y + z * z), 2.0 * (x * y - w * z), 2.0 * (x * z + w * y)],
        [2.0 * (x * y + w * z), 1.0 - 2.0 * (x * x + z * z), 2.0 * (y * z - w * x)],
        [2.0 * (x * z - w * y), 2.0 * (y * z + w * x), 1.0 - 2.0 * (x * x + y * y)],
    ]
    screen = [
        [finv * (rot[0][c] - u * rot[2][c]) for c in range(3)],
        [finv * (rot[1][c] - v * rot[2][c]) for c in range(3)],
    ]
    axes = [
        [sum(screen[r][c] * turn[c][k] for c in range(3)) for k in range(3)] for r in range(2)
    ]
    wide = [[axes[r][k] * scale[k] for k in range(3)] for r in range(2)]
    cov_xx = sum(wide[0][k] * axes[0][k] for k in range(3)) + dilation
    cov_xy = sum(wide[0][k] * axes[1][k] for k in range(3))
    cov_yy = sum(wide[1][k] * axes[1][k] for k in range(3)) + dilation
    rdet = 1.0 / (cov_xx * cov_yy - cov_xy * cov_xy)
    conic = (cov_yy * rdet, -cov_xy * rdet, cov_xx * rdet)
    rlen = lax.rsqrt(off[0] * off[0] + off[1] * off[1] + off[2] * off[2])
    way = [off[a] * rlen for a in range(3)]
    return dict(
        rot=rot, inv=inv, u=u, v=v, finv=finv, scale=scale, rnorm=rnorm, rotor=(w, x, y, z), turn=turn,
        screen=screen, axes=axes, wide=wide, conic=conic, rlen=rlen, way=way,
    )


def shade(feat, cam):
    off = [feat(a) - cam[9 + a] for a in range(3)]
    rlen = lax.rsqrt(off[0] * off[0] + off[1] * off[1] + off[2] * off[2])
    basis = sh_basis(*[off[a] * rlen for a in range(3)])
    colours = []
    for k in range(3):
        total = 0.5 + sh_const[0] * feat(11 + 16 * k)
        for b in range(1, 16):
            total = total + feat(11 + 16 * k + b) * basis[b]
        colours.append(total)
    return colours


def project_rows(feat, cam):
    part = project_parts(feat, cam)
    mean_x = focal_length * part["u"] + center_x
    mean_y = focal_length * part["v"] + center_y
    logit = feat(10)
    log_opacity = jnp.minimum(logit, 0.0) - jnp.log(1.0 + jnp.exp(-jnp.abs(logit)))
    return [mean_x, mean_y, *part["conic"], log_opacity]


def project_pull(feat, cam, grads, put):
    part = project_parts(feat, cam)
    g_mx, g_my, g_a, g_b, g_c, g_o = grads[:6]
    g_col = grads[6:9]
    way, rlen = part["way"], part["rlen"]
    basis = sh_basis(*way)
    pulled = [None]
    for k in range(3):
        put(11 + 16 * k, sh_const[0] * g_col[k])
    for b in range(1, 16):
        total = 0.0
        for k in range(3):
            put(11 + 16 * k + b, g_col[k] * basis[b])
            total = total + g_col[k] * feat(11 + 16 * k + b)
        pulled.append(total)
    g_way = sh_pull(pulled, *way)
    along = way[0] * g_way[0] + way[1] * g_way[1] + way[2] * g_way[2]
    g_off = [(g_way[a] - way[a] * along) * rlen for a in range(3)]
    put(10, g_o / (1.0 + jnp.exp(feat(10))))
    a, b, c = part["conic"]
    g_xx = -(a * a * g_a + a * b * g_b + b * b * g_c)
    g_xy = -(2.0 * a * b * g_a + (a * c + b * b) * g_b + 2.0 * b * c * g_c)
    g_yy = -(b * b * g_a + b * c * g_b + c * c * g_c)
    axes, wide, turn, screen = part["axes"], part["wide"], part["turn"], part["screen"]
    for k in range(3):
        g_scale = (
            g_xx * axes[0][k] * wide[0][k]
            + g_xy * axes[0][k] * wide[1][k]
            + g_yy * axes[1][k] * wide[1][k]
        )
        put(3 + k, 2.0 * g_scale)
    g_axes = [
        [2.0 * g_xx * wide[0][k] + g_xy * wide[1][k] for k in range(3)],
        [2.0 * g_yy * wide[1][k] + g_xy * wide[0][k] for k in range(3)],
    ]
    g_screen = [
        [sum(g_axes[r][k] * turn[c][k] for k in range(3)) for c in range(3)] for r in range(2)
    ]
    gm = [
        [g_axes[0][k] * screen[0][c] + g_axes[1][k] * screen[1][c] for k in range(3)]
        for c in range(3)
    ]
    w, x, y, z = part["rotor"]
    up_xy, up_xz, up_yz = gm[0][1] + gm[1][0], gm[0][2] + gm[2][0], gm[1][2] + gm[2][1]
    un_xy, un_xz, un_yz = gm[1][0] - gm[0][1], gm[0][2] - gm[2][0], gm[2][1] - gm[1][2]
    g_rotor = [
        2.0 * (z * un_xy + y * un_xz + x * un_yz),
        2.0 * (y * up_xy + z * up_xz + w * un_yz - 2.0 * x * (gm[1][1] + gm[2][2])),
        2.0 * (x * up_xy + z * up_yz + w * un_xz - 2.0 * y * (gm[0][0] + gm[2][2])),
        2.0 * (x * up_xz + y * up_yz + w * un_xy - 2.0 * z * (gm[0][0] + gm[1][1])),
    ]
    rotor = (w, x, y, z)
    along = sum(rotor[i] * g_rotor[i] for i in range(4))
    for i in range(4):
        put(6 + i, (g_rotor[i] - rotor[i] * along) * part["rnorm"])
    rot, inv, finv, u, v = part["rot"], part["inv"], part["finv"], part["u"], part["v"]
    g_u = focal_length * g_mx - finv * sum(g_screen[0][c] * rot[2][c] for c in range(3))
    g_v = focal_length * g_my - finv * sum(g_screen[1][c] * rot[2][c] for c in range(3))
    g_f = sum(g_screen[r][c] * screen[r][c] for r in range(2) for c in range(3))
    g_in = [g_u * inv, g_v * inv, -(g_f + g_u * u + g_v * v) * inv]
    for axis in range(3):
        put(
            axis,
            g_off[axis] + rot[0][axis] * g_in[0] + rot[1][axis] * g_in[1] + rot[2][axis] * g_in[2],
        )


def split(value):
    high = value.astype(BF16)
    return high, (value - high.astype(F32)).astype(BF16)


def matmul(a, b, dims=((1,), (0,))):
    return lax.dot_general(a, b, (dims, ((), ())), preferred_element_type=F32)


def spread_features(parts, scratch, count):
    tiles = sum(part.shape[1] for part in parts) // LANES
    at = 0
    for part in parts:
        for first in range(0, part.shape[1], LANES):
            for row in range(0, count, 8):
                rows = min(8, count - row)
                scratch[pl.ds(row * tiles + at, rows, stride=tiles), :] = part[
                    row : row + rows, first : first + LANES
                ]
            at += 1
    return tiles


def pack_kernel(shards, where, *refs):
    sources, (info, params, shard_of, local_of, goal, place_s, sems) = refs[:4], refs[4:]
    group = where[0]
    loads = [
        pltpu.make_async_copy(source, held, sems.at[k])
        for k, (source, held) in enumerate(zip(sources, (shard_of, local_of, goal, params)))
    ]
    for load in loads:
        load.start()
    for load in loads[:3]:
        load.wait()
    width = info.shape[1]
    tile_count, listed = local_of.shape
    rows_each = (info.shape[0] - 4) // tile_count
    columns = rows_each * width
    chunk = columns // shards
    info[0:3, :] = goal[...]
    for t in range(tile_count):
        place = (shard_of[t] ^ group) * chunk + (local_of[t : t + 1, :] - group * chunk)
        info[3:4, t * listed : (t + 1) * listed] = place.astype(F32)
        row_i = lax.broadcasted_iota(jnp.int32, (LANES, LANES), 0)
        col_i = lax.broadcasted_iota(jnp.int32, (LANES, LANES), 1)
        for first in range(0, listed, LANES):
            spread = jnp.broadcast_to(place[:, first : first + LANES].astype(F32), (LANES, LANES))
            place_s[first : first + LANES, :] = jnp.broadcast_to(
                jnp.sum(jnp.where(row_i == col_i, spread, 0.0), axis=1, keepdims=True), (LANES, LANES)
            )
        lane_of = lax.broadcasted_iota(jnp.int32, (8, LANES), 1).astype(F32)
        row_of = lax.broadcasted_iota(jnp.int32, (8, LANES), 0).astype(F32)
        for s in range(columns // LANES):
            best = jnp.full((8, LANES), -1.0, F32)
            column = lane_of + float(s * LANES)
            for first in range(0, listed, 8):
                best = jnp.where(
                    place_s[first : first + 8, :] == column, row_of + float(first), best
                )
            best = jnp.max(best, axis=0, keepdims=True)
            row, at = 4 + t * rows_each + s * LANES // width, s * LANES % width
            info[row : row + 1, at : at + LANES] = best
    loads[3].wait()


def pack(group, params, target, hit_shard, hit_local, shards):
    columns = params.shape[1]
    tile_count, listed = hit_local.shape
    width = target.shape[1]
    rows = 4 + tile_count * (columns // width)
    args = (hit_shard.reshape(tile_count, 1, listed), hit_local, target, params)
    return call(
        functools.partial(pack_kernel, shards),
        "pack",
        (jax.ShapeDtypeStruct((rows, width), F32), jax.ShapeDtypeStruct(params.shape, F32)),
        [smem()] + [pl.BlockSpec(memory_space=pltpu.HBM)] * 4,
        [
            pltpu.VMEM((tile_count, 1, listed), jnp.int32),
            pltpu.VMEM((tile_count, listed), jnp.int32),
            pltpu.VMEM(target.shape, F32),
            pltpu.VMEM((listed, LANES), F32),
            pltpu.SemaphoreType.DMA((4,)),
        ],
        (group.reshape(1),) + tuple(pltpu.with_memory_space_constraint(a, pltpu.HBM) for a in args),
        (vmem(), any_space()),
    )


def sent_rows(views):
    return (11 + 3 * views + 7) // 8 * 8


def cut_kernel(pieces, where, cams, params, *refs):
    parts, (feats, rows) = refs[:pieces], refs[pieces:]
    views = cams.shape[0]
    count = sent_rows(views)
    slabs = spread_features([params], feats, params.shape[0])

    def feat(f):
        return feats[f * slabs : (f + 1) * slabs, :]

    values = [feat(f) for f in range(11)]
    for v in range(views):
        values += shade(feat, [cams[v, i] for i in range(12)])
    values += [jnp.zeros((slabs, LANES), F32)] * (count - len(values))
    for f, value in enumerate(values):
        rows[pl.ds(f, slabs, stride=count), :] = value
    each = slabs // pieces
    for d in range(pieces):
        for h in range(each):
            first = (((where[0] ^ d) % pieces) * each + h) * count
            parts[d][:, h * LANES : (h + 1) * LANES] = rows[
                pl.ds(pl.multiple_of(first, 8), count), :
            ]


def cut(group, cameras, params, pieces):
    features, columns = params.shape
    slabs = columns // LANES
    count = sent_rows(cameras.shape[0])
    return list(
        call(
            functools.partial(cut_kernel, pieces),
            "cut",
            (jax.ShapeDtypeStruct((count, columns // pieces), F32),) * pieces,
            [smem()] * 2 + [vmem()],
            [
                pltpu.VMEM((features * slabs, LANES), F32),
                pltpu.VMEM((count * slabs, LANES), F32),
            ],
            (group.reshape(1), cameras, params),
        )
    )


def lane_gather(source, lane):
    return jnp.take_along_axis(source, lane, axis=1, mode="promise_in_bounds")


def pixel_basis(pixels):
    pixel = lax.broadcasted_iota(jnp.int32, (8, pixels), 1)
    row = lax.broadcasted_iota(jnp.int32, (8, pixels), 0)
    middle = 0.5 * TILE_SIDE - 0.5
    u = (pixel % TILE_SIDE).astype(F32) - middle
    v = (pixel // TILE_SIDE).astype(F32) - middle
    value = jnp.where(row == 0, 1.0, 0.0)
    for at, term in ((1, u), (2, v), (3, u * u), (4, u * v), (5, v * v)):
        value = jnp.where(row == at, term, value)
    return value


def composite(tiles, first_group, me, rows, info_s, rendered, work):
    alpha_s, weight_s, pull_s, push_s, weight_2, entry_s, coef_s, colour_s, sums_s, index_s, acc_s, ninth_s = work
    groups = info_s.shape[0]
    listed = acc_s.shape[0] * LANES
    tile_count = info_s.shape[2] // listed
    pixels = info_s.shape[2] // tile_count
    parts = pixels // LANES
    halves = listed // LANES
    tiles_here = groups * tile_count
    spans = tiles_here * parts
    slabs = rows.shape[0] // ROWS
    side = TILE_SIDE
    first_col, first_row = tiles

    def of_span(span):
        return pl.ds(span, listed, stride=LIST_STEP)

    def of_place(place):
        return pl.ds(place * LIST_STEP, spans)

    basis = pixel_basis(pixels)
    basis_3 = jnp.concatenate([basis, basis, basis], axis=0).astype(BF16)
    row_of = lax.broadcasted_iota(jnp.int32, (8, listed), 0)

    entries = []
    for n in range(tiles_here):
        g, t = n // tile_count, n % tile_count
        found = []
        for h in range(halves):
            first = t * listed + h * LANES
            at = info_s[g, 3:4, first : first + LANES].astype(jnp.int32)
            index_s[n * halves + h : n * halves + h + 1, :] = at
            at = jnp.broadcast_to(at, (8, LANES))
            lane, slab = at & (LANES - 1), at >> 7
            value = lane_gather(rows[0:8, :], lane)
            for s in range(1, slabs):
                value = jnp.where(
                    slab == s, lane_gather(rows[s * ROWS : s * ROWS + 8, :], lane), value
                )
            found.append(value)
        entries.append(jnp.concatenate(found, axis=1))
        for h in range(halves):
            entry_s[h, 8 * n : 8 * n + 8, :] = found[h]
    at = index_s[...]
    lane, slab = at & (LANES - 1), at >> 7
    ninth = lane_gather(rows[8:16, :], lane)
    for s in range(1, slabs):
        ninth = jnp.where(
            slab == s, lane_gather(rows[s * ROWS + 8 : s * ROWS + 16, :], lane), ninth
        )

    def of_lists(ref, f):
        at = pl.ds(f, tiles_here, stride=8)
        return jnp.concatenate([ref[h, at, :] for h in range(halves)], axis=1)

    tile_of = lax.broadcasted_iota(jnp.int32, (tiles_here, listed), 0)
    slot = (me ^ (first_group + tile_of // tile_count)) * tile_count + tile_of % tile_count
    mean_u = of_lists(entry_s, 2) - (((first_col + slot % 4) * side).astype(F32) + 0.5 * side)
    mean_v = of_lists(entry_s, 3) - (((first_row + slot // 4) * side).astype(F32) + 0.5 * side)
    quad_a = -0.5 * of_lists(entry_s, 4)
    quad_b = -of_lists(entry_s, 5)
    quad_c = -0.5 * of_lists(entry_s, 6)
    slope_u = 2.0 * quad_a * mean_u + quad_b * mean_v
    slope_v = 2.0 * quad_c * mean_v + quad_b * mean_u
    level = 0.5 * (slope_u * mean_u + slope_v * mean_v) + of_lists(entry_s, 7)
    for f, value in enumerate((level, -slope_u, -slope_v, quad_a, quad_b, quad_c)):
        for n in range(tiles_here):
            coef_s[f : f + 1, n * listed : (n + 1) * listed] = value[n : n + 1]
    coef_s[6:8, :] = jnp.zeros((2, tiles_here * listed), F32)
    coef = coef_s[...]
    terms = []
    for _ in range(3):
        terms.append(coef.astype(BF16).astype(F32))
        coef = coef - terms[-1]
    down = ((0,), (0,))
    power = matmul(jnp.concatenate(terms, axis=0).astype(BF16), basis_3, down)
    for n in range(tiles_here):
        for part in range(parts):
            alpha_s[of_span(n * parts + part), :] = jnp.exp(
                power[n * listed : (n + 1) * listed, part * LANES : (part + 1) * LANES]
            )
    colour_s[...] = jnp.zeros(colour_s.shape, F32)
    hues = []
    for n in range(tiles_here):
        last = jnp.concatenate([ninth[n * halves + h : n * halves + h + 1] for h in range(halves)], axis=1)
        colours = jnp.where(row_of < 2, entries[n], jnp.where(row_of == 2, last, 0.0))
        high = colours.astype(BF16).astype(F32)
        low = colours - high
        here = slice(n * listed, (n + 1) * listed)
        for at, value in ((0, high), (8, low), (16, high)):
            colour_s[24 * n + at : 24 * n + at + 8, here] = value
        hues.append(jnp.concatenate([high, low], axis=0).astype(BF16))

    unroll, quad = 64, 4
    steps = listed // unroll

    def forward(step, passed):
        for j in range(0, unroll, quad):
            at = [of_place(step * unroll + j + i) for i in range(quad)]
            alpha = [alpha_s[at[i], :] for i in range(quad)]
            keep = [1.0 - alpha[i] for i in range(quad)]
            two = keep[0] * keep[1]
            three = two * keep[2]
            weight_s[at[0], :] = alpha[0] * passed
            weight_s[at[1], :] = (alpha[1] * keep[0]) * passed
            weight_s[at[2], :] = (alpha[2] * two) * passed
            weight_s[at[3], :] = (alpha[3] * three) * passed
            passed = passed * (two * (keep[2] * keep[3]))
        return passed

    nought = jnp.zeros((spans, LANES), F32)
    lax.fori_loop(0, steps, forward, nought + 1.0)

    errors = []
    for n in range(tiles_here):
        g, t = n // tile_count, n % tile_count
        for part in range(parts):
            at = slice((n * parts + part) * LANES, (n * parts + part + 1) * LANES)
            weight_2[:listed, at], weight_2[listed:, at] = split(
                weight_s[of_span(n * parts + part), :]
            )
        at = slice(n * pixels, (n + 1) * pixels)
        image = matmul(hues[n], weight_2[:listed, at])
        image = image[0:8] + image[8:16] + matmul(hues[n], weight_2[listed:, at])[0:8]
        here = slice(t * pixels, (t + 1) * pixels)
        if rendered is not None and g == 0:
            rendered[:, here] = image[0:3]
        error = image - info_s[g, 0:8, here]
        high = error.astype(BF16).astype(F32)
        low = error - high
        errors += [high, high, low]

        hue = jnp.concatenate([high, low], axis=0).astype(BF16)
        across = ((1,), (1,))
        grads = matmul(hue, weight_2[:listed, at], across) + matmul(hue, weight_2[listed:, at], across)
        grads = grads[0:8] + grads[8:16]
        for h in range(halves):
            acc_s[h, 8 * n : 8 * n + 8, :] = grads[:, h * LANES : (h + 1) * LANES]
            row = n * halves + h
            ninth_s[row : row + 1, :] = grads[2:3, h * LANES : (h + 1) * LANES]
    pull = matmul(colour_s[...].astype(BF16), jnp.concatenate(errors, axis=0).astype(BF16), down)
    for n in range(tiles_here):
        for part in range(parts):
            pull_s[of_span(n * parts + part), :] = pull[
                n * listed : (n + 1) * listed, part * LANES : (part + 1) * LANES
            ]

    def backward(back, behind):
        for j in range(0, unroll, quad):
            at = [of_place(listed - 1 - (back * unroll + j + i)) for i in range(quad)]
            alpha = [alpha_s[at[i], :] for i in range(quad)]
            pull = [pull_s[at[i], :] for i in range(quad)]
            keep = [1.0 - alpha[i] for i in range(quad)]
            own = alpha[0] * pull[0]
            seen, through = behind, keep[0]
            for i in range(quad):
                push_s[at[i], :] = weight_s[at[i], :] * (pull[i] - seen)
                if i > 0:
                    own = own * keep[i] + alpha[i] * pull[i]
                    through = through * keep[i]
                seen = behind * through + own
            behind = seen
        return behind

    lax.fori_loop(0, steps, backward, nought)

    basis = basis.astype(BF16)
    for n in range(tiles_here):
        high, low = split(
            jnp.concatenate([push_s[of_span(n * parts + part), :] for part in range(parts)], axis=1)
        )
        moments = matmul(basis, high, across) + matmul(basis, low, across)
        for h in range(halves):
            sums_s[h, 8 * n : 8 * n + 8, :] = moments[:, h * LANES : (h + 1) * LANES]
    m_00, m_10, m_01, m_20, m_11, m_02 = [
        of_lists(sums_s, m) for m in range(6)
    ]
    n_10 = m_10 - mean_u * m_00
    n_01 = m_01 - mean_v * m_00
    for f, value in (
        (2, -(2.0 * quad_a * n_10 + quad_b * n_01)),
        (3, -(2.0 * quad_c * n_01 + quad_b * n_10)),
        (4, -0.5 * (m_20 - mean_u * (m_10 + n_10))),
        (5, -(m_11 - mean_u * m_01 - mean_v * n_10)),
        (6, -0.5 * (m_02 - mean_v * (m_01 + n_01))),
        (7, m_00),
    ):
        for h in range(halves):
            acc_s[h, pl.ds(f, tiles_here, stride=8), :] = value[:, h * LANES : (h + 1) * LANES]


def pool_sum(slab, info_s, acc_s, ninth_s):
    groups, _, width = info_s.shape
    listed = acc_s.shape[0] * LANES
    tile_count = width // listed
    halves = listed // LANES
    rows_each = (info_s.shape[1] - 4) // tile_count
    row_of = lax.broadcasted_iota(jnp.int32, (8, LANES), 0)

    totals, every = [], None
    for g in range(groups):
        total = jnp.zeros((8, LANES), F32)
        for t in range(tile_count):
            row, first = 4 + t * rows_each + slab * LANES // width, slab * LANES % width
            at = info_s[g, row : row + 1, first : first + LANES].astype(jnp.int32)
            at = jnp.broadcast_to(at, (8, LANES))
            n = g * tile_count + t
            every = at if every is None else jnp.where(row_of >= n * halves, at, every)
            lane, half = at & (LANES - 1), at >> 7
            for h in range(halves):
                here = lane_gather(acc_s[h, 8 * n : 8 * n + 8, :], lane)
                total = total + jnp.where(half == h, here, 0.0)
        totals.append(total)
    here = lane_gather(ninth_s[...], every & (LANES - 1))
    ninth = jnp.where(every >> 7 == row_of % halves, here, 0.0)
    return totals[0] + totals[1], jnp.sum(ninth, axis=0, keepdims=True)


def block_start(tile_id):
    within = tile_id % (TILES_X * TILES_Y)
    return (within % TILES_X) // 4 * 4, (within // TILES_X) // 2 * 2


def near_kernel(pieces, tile_ids, cams, where, own, other, *refs):
    parts = refs[:pieces]
    rendered, rows, partial, feats, info_s, *work = refs[pieces:]
    view = tile_ids[0] // (TILES_X * TILES_Y)
    cam = [cams[view, i] for i in range(12)]
    slabs = spread_features(parts, feats, parts[0].shape[0])
    projected = project_rows(lambda f: feats[f * slabs : (f + 1) * slabs, :], cam)
    colours = []
    for k in range(3):
        first = pl.multiple_of((11 + 3 * view + k) * slabs, slabs)
        colours.append(feats[pl.ds(first, slabs), :])
    for f, value in enumerate(colours[:2] + projected + [colours[2]] * 8):
        rows[pl.ds(f, slabs, stride=ROWS), :] = value
    info_s[0] = own[...]
    info_s[1] = other[...]
    composite(block_start(tile_ids[0]), 0, where[0], rows, info_s, rendered, work)
    for s in range(slabs):
        at = slice(s * LANES, (s + 1) * LANES)
        partial[0:8, at], partial[8:9, at] = pool_sum(s, info_s, *work[-2:])


def far_kernel(blocks, tile_ids, where, rows, partial, infos, *refs):
    *packets, info_s = refs[: len(refs) - 12]
    work = refs[len(refs) - 12 :]
    half = infos.shape[0] // 2
    info_s[0] = infos[:half, :]
    info_s[1] = infos[half:, :]
    composite(block_start(tile_ids[0]), 2, where[0], rows, info_s, None, work)
    share = (tile_ids[0] // (TILES_X * TILES_Y)).astype(F32)
    row_of = lax.broadcasted_iota(jnp.int32, (8, LANES), 0)
    lane_of = lax.broadcasted_iota(jnp.int32, (8, LANES), 1)
    chunk = packets[0].shape[1]
    for s in range(rows.shape[0] // ROWS):
        total, ninth = pool_sum(s, info_s, *work[-2:])
        total = total + partial[0:8, s * LANES : (s + 1) * LANES]
        ninth = ninth + partial[8:9, s * LANES : (s + 1) * LANES]
        if blocks == 1:
            mine = share
        else:
            column = s * LANES + lane_of
            mine = jnp.where(column % where[2] // (where[2] // blocks) == where[1], share, 0.0)
        at = slice(s * LANES % chunk, s * LANES % chunk + LANES)
        packets[s * LANES // chunk][0:8, at] = total
        packets[s * LANES // chunk][8:16, at] = jnp.where(
            row_of == 0, jnp.broadcast_to(ninth, (8, LANES)), mine
        )


def join_kernel(first, second, out):
    half = first.shape[0]
    out[:half, :] = first[...]
    out[half:, :] = second[...]


def update_kernel(pieces, follows, first_piece, cams, params, adam_m, adam_v, *refs):
    packets, refs = refs[:pieces], refs[pieces + 3 * follows :]
    sinks, (feats, rows, grads, made, sems) = refs[:3], refs[3:]
    features = params.shape[0]
    chunk = packets[0].shape[1]
    width = pieces * chunk
    slabs = width // LANES
    place = lax.axis_index("gs") ^ first_piece if pieces > 1 else 0
    start = place // pieces * pieces * chunk
    for d in range(pieces):
        for h in range(chunk // LANES):
            slab = (place ^ d) % pieces * (chunk // LANES) + h
            rows[pl.ds(slab, ROWS, stride=slabs), :] = packets[d][:, h * LANES : (h + 1) * LANES]
    pulled = [rows[f * slabs : (f + 1) * slabs, :] for f in range(10)]
    view = pulled[9]
    cam = []
    for i in range(12):
        value = jnp.full((slabs, LANES), cams[0, i], F32)
        for v in range(1, cams.shape[0]):
            value = jnp.where(view == float(v), cams[v, i], value)
        cam.append(value)

    def put(f, value):
        grads[f * slabs : (f + 1) * slabs, :] = value

    def column(s):
        return pl.ds(pl.multiple_of(start + s * LANES, LANES), LANES)

    for s in range(slabs):
        for row in range(0, features, 8):
            count = min(8, features - row)
            feats[pl.ds(row * slabs + s, count, stride=slabs), :] = params[
                row : row + count, column(s)
            ]
    project_pull(
        lambda f: feats[f * slabs : (f + 1) * slabs, :], cam, pulled[2:8] + pulled[:2] + pulled[8:9], put
    )
    rate = learn_rate / (1.0 - beta_one**adam_steps)
    unbias = 1.0 / (1.0 - beta_two**adam_steps)
    stores = []
    order = list(range(16, features, 8)) + [0, 8]
    for row in order:
        count = min(8, features - row)
        span = slice(row, row + count)
        for s in range(slabs):
            here = (span, slice(s * LANES, (s + 1) * LANES))
            grad = grads[pl.ds(row * slabs + s, count, stride=slabs), :]
            moment = beta_one * adam_m[span, column(s)] + (1.0 - beta_one) * grad
            second = beta_two * adam_v[span, column(s)] + (1.0 - beta_two) * grad * grad
            made.at[1][here] = moment
            made.at[2][here] = second
            made.at[0][here] = params[span, column(s)] - rate * moment / (
                jnp.sqrt(second * unbias) + adam_eps
            )
        if row % 16 == 8 or row + count == features:
            first = row // 16 * 16
            span = pl.ds(first, row + count - first)
            columns = pl.ds(pl.multiple_of(start, LANES), width)
            for k in range(3):
                store = pltpu.make_async_copy(
                    made.at[k, span], sinks[k].at[span, columns], sems.at[k, first // 16]
                )
                store.start()
                stores.append(store)
    for store in stores:
        store.wait()


def vmem():
    return pl.BlockSpec(memory_space=pltpu.VMEM)


def smem():
    return pl.BlockSpec(memory_space=pltpu.SMEM)


def any_space():
    return pl.BlockSpec(memory_space=pl.ANY)


def call(kernel, name, out_shape, in_specs, scratch, args, out_specs=None, grant=32):
    return pl.pallas_call(
        kernel,
        out_shape=out_shape,
        in_specs=in_specs,
        out_specs=out_specs or tuple(vmem() for _ in out_shape),
        scratch_shapes=scratch,
        compiler_params=pltpu.CompilerParams(vmem_limit_bytes=grant * 1024 * 1024),
        name=name,
    )(*args)


def work_shapes(tile_count, pixels, listed):
    tiles = 2 * tile_count
    spans = tiles * pixels // LANES
    assert spans < LIST_STEP and tiles * listed // LANES == 8 and tiles == 4
    return [pltpu.VMEM((listed * LIST_STEP, LANES), F32)] * 4 + [
        pltpu.VMEM((2 * listed, spans * LANES), BF16),
        pltpu.VMEM((listed // LANES, 8 * tiles, LANES), F32),
        pltpu.VMEM((8, tiles * listed), F32),
        pltpu.VMEM((24 * tiles, tiles * listed), F32),
        pltpu.VMEM((listed // LANES, 8 * tiles, LANES), F32),
        pltpu.VMEM((8, LANES), jnp.int32),
        pltpu.VMEM((listed // LANES, 8 * tiles, LANES), F32),
        pltpu.VMEM((8, LANES), F32),
    ]


def near(tile_ids, cameras, where, own, other, parts, tile_count):
    width = sum(part.shape[1] for part in parts)
    features = parts[0].shape[0]
    slabs = width // LANES
    pixels = listed = own.shape[1] // tile_count
    return call(
        functools.partial(near_kernel, len(parts)),
        "near",
        (
            jax.ShapeDtypeStruct((3, own.shape[1]), F32),
            jax.ShapeDtypeStruct((ROWS * slabs, LANES), F32),
            jax.ShapeDtypeStruct((ROWS, width), F32),
        ),
        [smem()] * 3 + [vmem()] * (2 + len(parts)),
        [pltpu.VMEM((features * slabs, LANES), F32), pltpu.VMEM((2,) + own.shape, F32)]
        + work_shapes(tile_count, pixels, listed),
        (tile_ids, cameras, where, own, other, *parts),
    )


def far(tile_ids, where, rows, partial, infos, pieces, tile_count, blocks):
    width = partial.shape[1]
    pixels = listed = infos.shape[1] // tile_count
    info = (infos.shape[0] // 2, infos.shape[1])
    return call(
        functools.partial(far_kernel, blocks),
        "far",
        (jax.ShapeDtypeStruct((ROWS, width // pieces), F32),) * pieces,
        [smem()] * 2 + [vmem()] * 3,
        [pltpu.VMEM((2,) + info, F32)] + work_shapes(tile_count, pixels, listed),
        (tile_ids, where, rows, partial, infos),
    )


def join(first, second):
    shape = (2 * first.shape[0], first.shape[1])
    return call(
        join_kernel, "join", (jax.ShapeDtypeStruct(shape, F32),), [vmem()] * 2, [], (first, second)
    )[0]


def update(first, cameras, params, adam_m, adam_v, packets, before):
    features = params.shape[0]
    width = sum(packet.shape[1] for packet in packets)
    slabs = width // LANES
    shape = jax.ShapeDtypeStruct(params.shape, F32)
    at = 4 + len(packets)
    return pl.pallas_call(
        functools.partial(update_kernel, len(packets), len(before) > 0, first),
        out_shape=(shape, shape, shape),
        in_specs=[smem()]
        + [vmem()] * (3 + len(packets))
        + [any_space()] * len(before),
        out_specs=(any_space(),) * 3,
        scratch_shapes=[
            pltpu.VMEM((features * slabs, LANES), F32),
            pltpu.VMEM((ROWS * slabs, LANES), F32),
            pltpu.VMEM((features * slabs, LANES), F32),
            pltpu.VMEM((3, features, width), F32),
            pltpu.SemaphoreType.DMA((3, (features + 15) // 16)),
        ],
        input_output_aliases={at + k: k for k in range(len(before))},
        compiler_params=pltpu.CompilerParams(vmem_limit_bytes=32 * 1024 * 1024),
        name="update",
    )(
        cameras, params, adam_m, adam_v, *packets, *before,
    )


def swap(value, axis, d):
    if d == 0:
        return value
    return lax.ppermute(value, axis, [(k, k ^ d) for k in range(lax.axis_size(axis))])


def local(params, adam_m, adam_v, cameras, target, tile_ids, hit_shard, hit_local):
    width = params.shape[1]
    tile_count, listed = hit_local.shape
    shards = lax.axis_size("gs")
    along = lax.axis_size("tile")
    chunk = width // shards
    group = lax.axis_index("gs")
    seat = lax.axis_index("tile")
    aligned = chunk % LANES == 0
    team = BLOCK_TILES // tile_count
    assert team == 4
    blocks = along // team

    info, params = pack(group, params, target, hit_shard, hit_local, shards)
    parts = cut(group, cameras, params, shards if aligned else 1)
    if not aligned:
        parts = [
            lax.dynamic_slice_in_dim(parts[0], (group ^ d) * chunk, chunk, axis=1)
            for d in range(shards)
        ]
    parts = [swap(parts[d], "gs", d) for d in range(shards)]
    beside = swap(info, "tile", 1)
    beyond = swap(join(info, beside), "tile", 2)
    if not aligned:
        parts = [jnp.concatenate(parts, axis=1)]
    where = jnp.stack([seat % team, seat // team, jnp.int32(chunk)]).astype(jnp.int32)
    rendered, rows, partial = near(tile_ids, cameras, where, info, beside, parts, tile_count)
    packets = far(tile_ids, where, rows, partial, beyond, len(parts), tile_count, blocks)
    if not aligned:
        packets = [packets[0][:, d * chunk : (d + 1) * chunk] for d in range(shards)]
    packets = [swap(packets[d], "gs", d) for d in range(shards)]
    if blocks > 1:
        packets = [block_sum(packet, along, team) for packet in packets]
    if not aligned:
        packets = [jnp.stack(packets)[jnp.arange(shards) ^ group].transpose(1, 0, 2).reshape(ROWS, -1)]
    made = ()
    count = max(1, len(packets) // 2)
    for first in range(0, len(packets), count):
        made = update(
            first, cameras, params, adam_m, adam_v, packets[first : first + count], made
        )
    new_params, new_m, new_v = made
    return (rendered, new_params, new_m, new_v)


def block_sum(packet, along, team):
    step = team
    while step < along:
        packet = packet + swap(packet, "tile", step)
        step *= 2
    return packet


def solution(mesh):
    return jax.shard_map(
        local,
        mesh=mesh,
        in_specs=(
            P(None, ("groups", "gs")),
            P(None, ("groups", "gs")),
            P(None, ("groups", "gs")),
            P("groups", None),
            P(None, ("groups", "gs", "tile")),
            P(("groups", "gs", "tile")),
            P(("groups", "gs", "tile"), None, None),
            P(("groups", "gs", "tile"), None),
        ),
        out_specs=(
            P(None, ("groups", "gs", "tile")),
            P(None, ("groups", "gs")),
            P(None, ("groups", "gs")),
            P(None, ("groups", "gs")),
        ),
        check_vma=False,
    )
```

```python
import functools

import jax
import jax.numpy as jnp
from jax import lax
from jax.experimental import pallas as pl
from jax.experimental.pallas import tpu as pltpu
from jax.sharding import PartitionSpec as P

TILES_X = 120
TILES_Y = 68
TILE_SIDE = 16
BLOCK_TILES = 8
LANES = 128
ROWS = 16
LIST_STEP = 9
F32 = jnp.float32
BF16 = jnp.bfloat16

focal_length = 1000.0
center_x = 960.0
center_y = 540.0
dilation = 0.3
beta_one = 0.9
beta_two = 0.999
learn_rate = 0.01
adam_eps = 1e-08
adam_steps = 100.0
sh_const = (
    0.28209479177387814,
    0.4886025119029199,
    1.0925484305920792,
    0.31539156525252005,
    0.5462742152960396,
    0.5900435899266435,
    2.890611442640554,
    0.4570457994644658,
    0.3731763325901154,
    1.445305721320277,
)


def sh_basis(x, y, z):
    s = sh_const
    xx, yy, zz = x * x, y * y, z * z
    return [
        None,
        -s[1] * y,
        s[1] * z,
        -s[1] * x,
        s[2] * (x * y),
        -s[2] * (y * z),
        s[3] * (2.0 * zz - xx - yy),
        -s[2] * (x * z),
        s[4] * (xx - yy),
        -s[5] * y * (3.0 * xx - yy),
        s[6] * (x * y) * z,
        -s[7] * y * (4.0 * zz - xx - yy),
        s[8] * z * (2.0 * zz - 3.0 * xx - 3.0 * yy),
        -s[7] * x * (4.0 * zz - xx - yy),
        s[9] * z * (xx - yy),
        -s[5] * x * (xx - 3.0 * yy),
    ]


def sh_pull(h, x, y, z):
    s = sh_const
    xx, yy, zz = x * x, y * y, z * z
    xy, xz, yz = x * y, x * z, y * z
    diff = xx - yy
    ring = 4.0 * zz - xx - yy
    g_x = (
        -s[1] * h[3]
        + s[2] * (h[4] * y - h[7] * z)
        - (2.0 * s[3]) * h[6] * x
        + (2.0 * s[4]) * h[8] * x
        - (6.0 * s[5]) * h[9] * xy
        + s[6] * h[10] * yz
        + (2.0 * s[7]) * h[11] * xy
        - (6.0 * s[8]) * h[12] * xz
        - s[7] * h[13] * (ring - 2.0 * xx)
        + (2.0 * s[9]) * h[14] * xz
        - (3.0 * s[5]) * h[15] * diff
    )
    g_y = (
        -s[1] * h[1]
        + s[2] * (h[4] * x - h[5] * z)
        - (2.0 * s[3]) * h[6] * y
        - (2.0 * s[4]) * h[8] * y
        - (3.0 * s[5]) * h[9] * diff
        + s[6] * h[10] * xz
        - s[7] * h[11] * (ring - 2.0 * yy)
        - (6.0 * s[8]) * h[12] * yz
        + (2.0 * s[7]) * h[13] * xy
        - (2.0 * s[9]) * h[14] * yz
        + (6.0 * s[5]) * h[15] * xy
    )
    g_z = (
        s[1] * h[2]
        - s[2] * (h[5] * y + h[7] * x)
        + (4.0 * s[3]) * h[6] * z
        + s[6] * h[10] * xy
        - (8.0 * s[7]) * (h[11] * yz + h[13] * xz)
        + s[8] * h[12] * (6.0 * zz - 3.0 * xx - 3.0 * yy)
        + s[9] * h[14] * diff
    )
    return g_x, g_y, g_z


def project_parts(feat, cam):
    rot = [[cam[3 * r + c] for c in range(3)] for r in range(3)]
    off = [feat(a) - cam[9 + a] for a in range(3)]
    in_cam = [rot[r][0] * off[0] + rot[r][1] * off[1] + rot[r][2] * off[2] for r in range(3)]
    inv = 1.0 / in_cam[2]
    u = in_cam[0] * inv
    v = in_cam[1] * inv
    finv = focal_length * inv
    scale = [jnp.exp(2.0 * feat(3 + a)) for a in range(3)]
    quat = [feat(6 + a) for a in range(4)]
    rnorm = lax.rsqrt(quat[0] * quat[0] + quat[1] * quat[1] + quat[2] * quat[2] + quat[3] * quat[3])
    w, x, y, z = [q * rnorm for q in quat]
    turn = [
        [1.0 - 2.0 * (y * y + z * z), 2.0 * (x * y - w * z), 2.0 * (x * z + w * y)],
        [2.0 * (x * y + w * z), 1.0 - 2.0 * (x * x + z * z), 2.0 * (y * z - w * x)],
        [2.0 * (x * z - w * y), 2.0 * (y * z + w * x), 1.0 - 2.0 * (x * x + y * y)],
    ]
    screen = [
        [finv * (rot[0][c] - u * rot[2][c]) for c in range(3)],
        [finv * (rot[1][c] - v * rot[2][c]) for c in range(3)],
    ]
    axes = [
        [sum(screen[r][c] * turn[c][k] for c in range(3)) for k in range(3)] for r in range(2)
    ]
    wide = [[axes[r][k] * scale[k] for k in range(3)] for r in range(2)]
    cov_xx = sum(wide[0][k] * axes[0][k] for k in range(3)) + dilation
    cov_xy = sum(wide[0][k] * axes[1][k] for k in range(3))
    cov_yy = sum(wide[1][k] * axes[1][k] for k in range(3)) + dilation
    rdet = 1.0 / (cov_xx * cov_yy - cov_xy * cov_xy)
    conic = (cov_yy * rdet, -cov_xy * rdet, cov_xx * rdet)
    rlen = lax.rsqrt(off[0] * off[0] + off[1] * off[1] + off[2] * off[2])
    way = [off[a] * rlen for a in range(3)]
    return dict(
        rot=rot, inv=inv, u=u, v=v, finv=finv, scale=scale, rnorm=rnorm, rotor=(w, x, y, z), turn=turn,
        screen=screen, axes=axes, wide=wide, conic=conic, rlen=rlen, way=way,
    )


def shade(feat, cam):
    off = [feat(a) - cam[9 + a] for a in range(3)]
    rlen = lax.rsqrt(off[0] * off[0] + off[1] * off[1] + off[2] * off[2])
    basis = sh_basis(*[off[a] * rlen for a in range(3)])
    colours = []
    for k in range(3):
        total = 0.5 + sh_const[0] * feat(11 + 16 * k)
        for b in range(1, 16):
            total = total + feat(11 + 16 * k + b) * basis[b]
        colours.append(total)
    return colours


def project_rows(feat, cam):
    part = project_parts(feat, cam)
    mean_x = focal_length * part["u"] + center_x
    mean_y = focal_length * part["v"] + center_y
    logit = feat(10)
    log_opacity = jnp.minimum(logit, 0.0) - jnp.log(1.0 + jnp.exp(-jnp.abs(logit)))
    return [mean_x, mean_y, *part["conic"], log_opacity]


def project_pull(feat, cam, grads, put):
    part = project_parts(feat, cam)
    g_mx, g_my, g_a, g_b, g_c, g_o = grads[:6]
    g_col = grads[6:9]
    way, rlen = part["way"], part["rlen"]
    basis = sh_basis(*way)
    pulled = [None]
    for k in range(3):
        put(11 + 16 * k, sh_const[0] * g_col[k])
    for b in range(1, 16):
        total = 0.0
        for k in range(3):
            put(11 + 16 * k + b, g_col[k] * basis[b])
            total = total + g_col[k] * feat(11 + 16 * k + b)
        pulled.append(total)
    g_way = sh_pull(pulled, *way)
    along = way[0] * g_way[0] + way[1] * g_way[1] + way[2] * g_way[2]
    g_off = [(g_way[a] - way[a] * along) * rlen for a in range(3)]
    put(10, g_o / (1.0 + jnp.exp(feat(10))))
    a, b, c = part["conic"]
    g_xx = -(a * a * g_a + a * b * g_b + b * b * g_c)
    g_xy = -(2.0 * a * b * g_a + (a * c + b * b) * g_b + 2.0 * b * c * g_c)
    g_yy = -(b * b * g_a + b * c * g_b + c * c * g_c)
    axes, wide, turn, screen = part["axes"], part["wide"], part["turn"], part["screen"]
    for k in range(3):
        g_scale = (
            g_xx * axes[0][k] * wide[0][k]
            + g_xy * axes[0][k] * wide[1][k]
            + g_yy * axes[1][k] * wide[1][k]
        )
        put(3 + k, 2.0 * g_scale)
    g_axes = [
        [2.0 * g_xx * wide[0][k] + g_xy * wide[1][k] for k in range(3)],
        [2.0 * g_yy * wide[1][k] + g_xy * wide[0][k] for k in range(3)],
    ]
    g_screen = [
        [sum(g_axes[r][k] * turn[c][k] for k in range(3)) for c in range(3)] for r in range(2)
    ]
    gm = [
        [g_axes[0][k] * screen[0][c] + g_axes[1][k] * screen[1][c] for k in range(3)]
        for c in range(3)
    ]
    w, x, y, z = part["rotor"]
    up_xy, up_xz, up_yz = gm[0][1] + gm[1][0], gm[0][2] + gm[2][0], gm[1][2] + gm[2][1]
    un_xy, un_xz, un_yz = gm[1][0] - gm[0][1], gm[0][2] - gm[2][0], gm[2][1] - gm[1][2]
    g_rotor = [
        2.0 * (z * un_xy + y * un_xz + x * un_yz),
        2.0 * (y * up_xy + z * up_xz + w * un_yz - 2.0 * x * (gm[1][1] + gm[2][2])),
        2.0 * (x * up_xy + z * up_yz + w * un_xz - 2.0 * y * (gm[0][0] + gm[2][2])),
        2.0 * (x * up_xz + y * up_yz + w * un_xy - 2.0 * z * (gm[0][0] + gm[1][1])),
    ]
    rotor = (w, x, y, z)
    along = sum(rotor[i] * g_rotor[i] for i in range(4))
    for i in range(4):
        put(6 + i, (g_rotor[i] - rotor[i] * along) * part["rnorm"])
    rot, inv, finv, u, v = part["rot"], part["inv"], part["finv"], part["u"], part["v"]
    g_u = focal_length * g_mx - finv * sum(g_screen[0][c] * rot[2][c] for c in range(3))
    g_v = focal_length * g_my - finv * sum(g_screen[1][c] * rot[2][c] for c in range(3))
    g_f = sum(g_screen[r][c] * screen[r][c] for r in range(2) for c in range(3))
    g_in = [g_u * inv, g_v * inv, -(g_f + g_u * u + g_v * v) * inv]
    for axis in range(3):
        put(
            axis,
            g_off[axis] + rot[0][axis] * g_in[0] + rot[1][axis] * g_in[1] + rot[2][axis] * g_in[2],
        )


def split(value):
    high = value.astype(BF16)
    return high, (value - high.astype(F32)).astype(BF16)


def matmul(a, b, dims=((1,), (0,))):
    return lax.dot_general(a, b, (dims, ((), ())), preferred_element_type=F32)


def spread_features(parts, scratch, count):
    tiles = sum(part.shape[1] for part in parts) // LANES
    at = 0
    for part in parts:
        for first in range(0, part.shape[1], LANES):
            for row in range(0, count, 8):
                rows = min(8, count - row)
                scratch[pl.ds(row * tiles + at, rows, stride=tiles), :] = part[
                    row : row + rows, first : first + LANES
                ]
            at += 1
    return tiles


def pack_kernel(shards, where, *refs):
    sources, (info, params, shard_of, local_of, goal, place_s, sems) = refs[:4], refs[4:]
    group = where[0]
    loads = [
        pltpu.make_async_copy(source, held, sems.at[k])
        for k, (source, held) in enumerate(zip(sources, (shard_of, local_of, goal, params)))
    ]
    for load in loads:
        load.start()
    for load in loads[:3]:
        load.wait()
    width = info.shape[1]
    tile_count, listed = local_of.shape
    rows_each = (info.shape[0] - 4) // tile_count
    columns = rows_each * width
    chunk = columns // shards
    info[0:3, :] = goal[...]
    for t in range(tile_count):
        place = (shard_of[t] ^ group) * chunk + (local_of[t : t + 1, :] - group * chunk)
        info[3:4, t * listed : (t + 1) * listed] = place.astype(F32)
        row_i = lax.broadcasted_iota(jnp.int32, (LANES, LANES), 0)
        col_i = lax.broadcasted_iota(jnp.int32, (LANES, LANES), 1)
        for first in range(0, listed, LANES):
            spread = jnp.broadcast_to(place[:, first : first + LANES].astype(F32), (LANES, LANES))
            place_s[first : first + LANES, :] = jnp.broadcast_to(
                jnp.sum(jnp.where(row_i == col_i, spread, 0.0), axis=1, keepdims=True), (LANES, LANES)
            )
        lane_of = lax.broadcasted_iota(jnp.int32, (8, LANES), 1).astype(F32)
        row_of = lax.broadcasted_iota(jnp.int32, (8, LANES), 0).astype(F32)
        for s in range(columns // LANES):
            best = jnp.full((8, LANES), -1.0, F32)
            column = lane_of + float(s * LANES)
            for first in range(0, listed, 8):
                best = jnp.where(
                    place_s[first : first + 8, :] == column, row_of + float(first), best
                )
            best = jnp.max(best, axis=0, keepdims=True)
            row, at = 4 + t * rows_each + s * LANES // width, s * LANES % width
            info[row : row + 1, at : at + LANES] = best
    loads[3].wait()


def pack(group, params, target, hit_shard, hit_local, shards):
    columns = params.shape[1]
    tile_count, listed = hit_local.shape
    width = target.shape[1]
    rows = 4 + tile_count * (columns // width)
    args = (hit_shard.reshape(tile_count, 1, listed), hit_local, target, params)
    return call(
        functools.partial(pack_kernel, shards),
        "pack",
        (jax.ShapeDtypeStruct((rows, width), F32), jax.ShapeDtypeStruct(params.shape, F32)),
        [smem()] + [pl.BlockSpec(memory_space=pltpu.HBM)] * 4,
        [
            pltpu.VMEM((tile_count, 1, listed), jnp.int32),
            pltpu.VMEM((tile_count, listed), jnp.int32),
            pltpu.VMEM(target.shape, F32),
            pltpu.VMEM((listed, LANES), F32),
            pltpu.SemaphoreType.DMA((4,)),
        ],
        (group.reshape(1),) + tuple(pltpu.with_memory_space_constraint(a, pltpu.HBM) for a in args),
        (vmem(), any_space()),
    )


def sent_rows(views):
    return (11 + 3 * views + 7) // 8 * 8


def cut_kernel(pieces, where, cams, params, *refs):
    parts, (feats, rows) = refs[:pieces], refs[pieces:]
    views = cams.shape[0]
    count = sent_rows(views)
    slabs = spread_features([params], feats, params.shape[0])

    def feat(f):
        return feats[f * slabs : (f + 1) * slabs, :]

    values = [feat(f) for f in range(11)]
    for v in range(views):
        values += shade(feat, [cams[v, i] for i in range(12)])
    values += [jnp.zeros((slabs, LANES), F32)] * (count - len(values))
    for f, value in enumerate(values):
        rows[pl.ds(f, slabs, stride=count), :] = value
    each = slabs // pieces
    for d in range(pieces):
        for h in range(each):
            first = (((where[0] ^ d) % pieces) * each + h) * count
            parts[d][:, h * LANES : (h + 1) * LANES] = rows[
                pl.ds(pl.multiple_of(first, 8), count), :
            ]


def cut(group, cameras, params, pieces):
    features, columns = params.shape
    slabs = columns // LANES
    count = sent_rows(cameras.shape[0])
    return list(
        call(
            functools.partial(cut_kernel, pieces),
            "cut",
            (jax.ShapeDtypeStruct((count, columns // pieces), F32),) * pieces,
            [smem()] * 2 + [vmem()],
            [
                pltpu.VMEM(((features + 8) * slabs, LANES), F32),
                pltpu.VMEM((count * (slabs + 1), LANES), F32),
            ],
            (group.reshape(1), cameras, params),
        )
    )


def lane_gather(source, lane):
    return jnp.take_along_axis(source, lane, axis=1, mode="promise_in_bounds")


def pixel_basis(pixels):
    pixel = lax.broadcasted_iota(jnp.int32, (8, pixels), 1)
    row = lax.broadcasted_iota(jnp.int32, (8, pixels), 0)
    middle = 0.5 * TILE_SIDE - 0.5
    u = (pixel % TILE_SIDE).astype(F32) - middle
    v = (pixel // TILE_SIDE).astype(F32) - middle
    value = jnp.where(row == 0, 1.0, 0.0)
    for at, term in ((1, u), (2, v), (3, u * u), (4, u * v), (5, v * v)):
        value = jnp.where(row == at, term, value)
    return value


def composite(tiles, first_group, me, rows, info_s, rendered, work):
    alpha_s, weight_s, pull_s, push_s, weight_2, entry_s, coef_s, colour_s, sums_s, index_s, acc_s, ninth_s = work
    groups = info_s.shape[0]
    listed = acc_s.shape[0] * LANES
    tile_count = info_s.shape[2] // listed
    pixels = info_s.shape[2] // tile_count
    parts = pixels // LANES
    halves = listed // LANES
    tiles_here = groups * tile_count
    spans = tiles_here * parts
    slabs = rows.shape[0] // ROWS - 1
    side = TILE_SIDE
    first_col, first_row = tiles

    def of_span(span):
        return pl.ds(span, listed, stride=LIST_STEP)

    def of_place(place):
        return pl.ds(place * LIST_STEP, spans)

    basis = pixel_basis(pixels)
    basis_3 = jnp.concatenate([basis, basis, basis], axis=0).astype(BF16)
    row_of = lax.broadcasted_iota(jnp.int32, (8, listed), 0)

    entries = []
    for n in range(tiles_here):
        g, t = n // tile_count, n % tile_count
        found = []
        for h in range(halves):
            first = t * listed + h * LANES
            at = info_s[g, 3:4, first : first + LANES].astype(jnp.int32)
            index_s[n * halves + h : n * halves + h + 1, :] = at
            at = jnp.broadcast_to(at, (8, LANES))
            lane, slab = at & (LANES - 1), at >> 7
            value = lane_gather(rows[0:8, :], lane)
            for s in range(1, slabs):
                value = jnp.where(
                    slab == s, lane_gather(rows[s * ROWS : s * ROWS + 8, :], lane), value
                )
            found.append(value)
        entries.append(jnp.concatenate(found, axis=1))
        for h in range(halves):
            entry_s[h, 8 * n : 8 * n + 8, :] = found[h]
    at = index_s[...]
    lane, slab = at & (LANES - 1), at >> 7
    ninth = lane_gather(rows[8:16, :], lane)
    for s in range(1, slabs):
        ninth = jnp.where(
            slab == s, lane_gather(rows[s * ROWS + 8 : s * ROWS + 16, :], lane), ninth
        )

    def of_lists(ref, f):
        at = pl.ds(f, tiles_here, stride=8)
        return jnp.concatenate([ref[h, at, :] for h in range(halves)], axis=1)

    tile_of = lax.broadcasted_iota(jnp.int32, (tiles_here, listed), 0)
    slot = (me ^ (first_group + tile_of // tile_count)) * tile_count + tile_of % tile_count
    mean_u = of_lists(entry_s, 2) - (((first_col + slot % 4) * side).astype(F32) + 0.5 * side)
    mean_v = of_lists(entry_s, 3) - (((first_row + slot // 4) * side).astype(F32) + 0.5 * side)
    quad_a = -0.5 * of_lists(entry_s, 4)
    quad_b = -of_lists(entry_s, 5)
    quad_c = -0.5 * of_lists(entry_s, 6)
    slope_u = 2.0 * quad_a * mean_u + quad_b * mean_v
    slope_v = 2.0 * quad_c * mean_v + quad_b * mean_u
    level = 0.5 * (slope_u * mean_u + slope_v * mean_v) + of_lists(entry_s, 7)
    for f, value in enumerate((level, -slope_u, -slope_v, quad_a, quad_b, quad_c)):
        for n in range(tiles_here):
            coef_s[f : f + 1, n * listed : (n + 1) * listed] = value[n : n + 1]
    coef_s[6:8, :] = jnp.zeros((2, tiles_here * listed), F32)
    coef = coef_s[...]
    terms = []
    for _ in range(3):
        terms.append(coef.astype(BF16).astype(F32))
        coef = coef - terms[-1]
    down = ((0,), (0,))
    power = matmul(jnp.concatenate(terms, axis=0).astype(BF16), basis_3, down)
    for n in range(tiles_here):
        for part in range(parts):
            alpha_s[of_span(n * parts + part), :] = jnp.exp(
                power[n * listed : (n + 1) * listed, part * LANES : (part + 1) * LANES]
            )
    colour_s[...] = jnp.zeros(colour_s.shape, F32)
    hues = []
    for n in range(tiles_here):
        last = jnp.concatenate([ninth[n * halves + h : n * halves + h + 1] for h in range(halves)], axis=1)
        colours = jnp.where(row_of < 2, entries[n], jnp.where(row_of == 2, last, 0.0))
        high = colours.astype(BF16).astype(F32)
        low = colours - high
        here = slice(n * listed, (n + 1) * listed)
        for at, value in ((0, high), (8, low), (16, high)):
            colour_s[24 * n + at : 24 * n + at + 8, here] = value
        hues.append(jnp.concatenate([high, low], axis=0).astype(BF16))

    unroll, quad = 16, 4
    steps = listed // unroll

    def forward(step, passed):
        for j in range(0, unroll, quad):
            at = [of_place(step * unroll + j + i) for i in range(quad)]
            alpha = [alpha_s[at[i], :] for i in range(quad)]
            keep = [1.0 - alpha[i] for i in range(quad)]
            two = keep[0] * keep[1]
            three = two * keep[2]
            weight_s[at[0], :] = alpha[0] * passed
            weight_s[at[1], :] = (alpha[1] * keep[0]) * passed
            weight_s[at[2], :] = (alpha[2] * two) * passed
            weight_s[at[3], :] = (alpha[3] * three) * passed
            passed = passed * (two * (keep[2] * keep[3]))
        return passed

    nought = jnp.zeros((spans, LANES), F32)
    lax.fori_loop(0, steps, forward, nought + 1.0)

    errors = []
    for n in range(tiles_here):
        g, t = n // tile_count, n % tile_count
        for part in range(parts):
            at = slice((n * parts + part) * LANES, (n * parts + part + 1) * LANES)
            weight_2[:listed, at], weight_2[listed:, at] = split(
                weight_s[of_span(n * parts + part), :]
            )
        at = slice(n * pixels, (n + 1) * pixels)
        image = matmul(hues[n], weight_2[:listed, at])
        image = image[0:8] + image[8:16] + matmul(hues[n], weight_2[listed:, at])[0:8]
        here = slice(t * pixels, (t + 1) * pixels)
        if rendered is not None and g == 0:
            rendered[:, here] = image[0:3]
        error = image - info_s[g, 0:8, here]
        high = error.astype(BF16).astype(F32)
        low = error - high
        errors += [high, high, low]

        hue = jnp.concatenate([high, low], axis=0).astype(BF16)
        across = ((1,), (1,))
        grads = matmul(hue, weight_2[:listed, at], across) + matmul(hue, weight_2[listed:, at], across)
        grads = grads[0:8] + grads[8:16]
        for h in range(halves):
            acc_s[h, 8 * n : 8 * n + 8, :] = grads[:, h * LANES : (h + 1) * LANES]
            row = n * halves + h
            ninth_s[row : row + 1, :] = grads[2:3, h * LANES : (h + 1) * LANES]
    pull = matmul(colour_s[...].astype(BF16), jnp.concatenate(errors, axis=0).astype(BF16), down)
    for n in range(tiles_here):
        for part in range(parts):
            pull_s[of_span(n * parts + part), :] = pull[
                n * listed : (n + 1) * listed, part * LANES : (part + 1) * LANES
            ]

    def backward(back, behind):
        for j in range(0, unroll, quad):
            at = [of_place(listed - 1 - (back * unroll + j + i)) for i in range(quad)]
            alpha = [alpha_s[at[i], :] for i in range(quad)]
            pull = [pull_s[at[i], :] for i in range(quad)]
            keep = [1.0 - alpha[i] for i in range(quad)]
            own = alpha[0] * pull[0]
            seen, through = behind, keep[0]
            for i in range(quad):
                push_s[at[i], :] = weight_s[at[i], :] * (pull[i] - seen)
                if i > 0:
                    own = own * keep[i] + alpha[i] * pull[i]
                    through = through * keep[i]
                seen = behind * through + own
            behind = seen
        return behind

    lax.fori_loop(0, steps, backward, nought)

    basis = basis.astype(BF16)
    for n in range(tiles_here):
        high, low = split(
            jnp.concatenate([push_s[of_span(n * parts + part), :] for part in range(parts)], axis=1)
        )
        moments = matmul(basis, high, across) + matmul(basis, low, across)
        for h in range(halves):
            sums_s[h, 8 * n : 8 * n + 8, :] = moments[:, h * LANES : (h + 1) * LANES]
    m_00, m_10, m_01, m_20, m_11, m_02 = [
        of_lists(sums_s, m) for m in range(6)
    ]
    n_10 = m_10 - mean_u * m_00
    n_01 = m_01 - mean_v * m_00
    for f, value in (
        (2, -(2.0 * quad_a * n_10 + quad_b * n_01)),
        (3, -(2.0 * quad_c * n_01 + quad_b * n_10)),
        (4, -0.5 * (m_20 - mean_u * (m_10 + n_10))),
        (5, -(m_11 - mean_u * m_01 - mean_v * n_10)),
        (6, -0.5 * (m_02 - mean_v * (m_01 + n_01))),
        (7, m_00),
    ):
        for h in range(halves):
            acc_s[h, pl.ds(f, tiles_here, stride=8), :] = value[:, h * LANES : (h + 1) * LANES]


def pool_sum(slab, info_s, acc_s, ninth_s):
    groups, _, width = info_s.shape
    listed = acc_s.shape[0] * LANES
    tile_count = width // listed
    halves = listed // LANES
    rows_each = (info_s.shape[1] - 4) // tile_count
    row_of = lax.broadcasted_iota(jnp.int32, (8, LANES), 0)

    totals, every = [], None
    for g in range(groups):
        total = jnp.zeros((8, LANES), F32)
        for t in range(tile_count):
            row, first = 4 + t * rows_each + slab * LANES // width, slab * LANES % width
            at = info_s[g, row : row + 1, first : first + LANES].astype(jnp.int32)
            at = jnp.broadcast_to(at, (8, LANES))
            n = g * tile_count + t
            every = at if every is None else jnp.where(row_of >= n * halves, at, every)
            lane, half = at & (LANES - 1), at >> 7
            for h in range(halves):
                here = lane_gather(acc_s[h, 8 * n : 8 * n + 8, :], lane)
                total = total + jnp.where(half == h, here, 0.0)
        totals.append(total)
    here = lane_gather(ninth_s[...], every & (LANES - 1))
    ninth = jnp.where(every >> 7 == row_of % halves, here, 0.0)
    return totals[0] + totals[1], jnp.sum(ninth, axis=0, keepdims=True)


def block_start(tile_id):
    within = tile_id % (TILES_X * TILES_Y)
    return (within % TILES_X) // 4 * 4, (within // TILES_X) // 2 * 2


def near_kernel(pieces, tile_ids, cams, where, own, other, *refs):
    parts = refs[:pieces]
    rendered, rows, partial, feats, info_s, *work = refs[pieces:]
    view = tile_ids[0] // (TILES_X * TILES_Y)
    cam = [cams[view, i] for i in range(12)]
    slabs = spread_features(parts, feats, parts[0].shape[0])
    projected = project_rows(lambda f: feats[f * slabs : (f + 1) * slabs, :], cam)
    colours = []
    for k in range(3):
        first = pl.multiple_of((11 + 3 * view + k) * slabs, slabs)
        colours.append(feats[pl.ds(first, slabs), :])
    for f, value in enumerate(colours[:2] + projected + [colours[2]] * 8):
        rows[pl.ds(f, slabs, stride=ROWS), :] = value
    info_s[0] = own[...]
    info_s[1] = other[...]
    composite(block_start(tile_ids[0]), 0, where[0], rows, info_s, rendered, work)
    for s in range(slabs):
        at = slice(s * LANES, (s + 1) * LANES)
        partial[0:8, at], partial[8:9, at] = pool_sum(s, info_s, *work[-2:])


def far_kernel(blocks, tile_ids, where, rows, partial, infos, *refs):
    *packets, info_s = refs[: len(refs) - 12]
    work = refs[len(refs) - 12 :]
    half = infos.shape[0] // 2
    info_s[0] = infos[:half, :]
    info_s[1] = infos[half:, :]
    composite(block_start(tile_ids[0]), 2, where[0], rows, info_s, None, work)
    share = (tile_ids[0] // (TILES_X * TILES_Y)).astype(F32)
    row_of = lax.broadcasted_iota(jnp.int32, (8, LANES), 0)
    lane_of = lax.broadcasted_iota(jnp.int32, (8, LANES), 1)
    chunk = packets[0].shape[1]
    for s in range(rows.shape[0] // ROWS - 1):
        total, ninth = pool_sum(s, info_s, *work[-2:])
        total = total + partial[0:8, s * LANES : (s + 1) * LANES]
        ninth = ninth + partial[8:9, s * LANES : (s + 1) * LANES]
        if blocks == 1:
            mine = share
        else:
            column = s * LANES + lane_of
            mine = jnp.where(column % where[2] // (where[2] // blocks) == where[1], share, 0.0)
        at = slice(s * LANES % chunk, s * LANES % chunk + LANES)
        packets[s * LANES // chunk][0:8, at] = total
        packets[s * LANES // chunk][8:16, at] = jnp.where(
            row_of == 0, jnp.broadcast_to(ninth, (8, LANES)), mine
        )


def join_kernel(first, second, out):
    half = first.shape[0]
    out[:half, :] = first[...]
    out[half:, :] = second[...]


def update_kernel(pieces, follows, where, cams, params, adam_m, adam_v, *refs):
    packets, refs = refs[:pieces], refs[pieces + 3 * follows :]
    sinks, (feats, rows, grads, made, sems) = refs[:3], refs[3:]
    features = params.shape[0]
    chunk = packets[0].shape[1]
    width = pieces * chunk
    slabs = width // LANES
    start = (where[0] ^ where[1]) // pieces * pieces * chunk
    for d in range(pieces):
        for h in range(chunk // LANES):
            slab = (where[0] ^ where[1] ^ d) % pieces * (chunk // LANES) + h
            rows[pl.ds(slab, ROWS, stride=slabs), :] = packets[d][:, h * LANES : (h + 1) * LANES]
    pulled = [rows[f * slabs : (f + 1) * slabs, :] for f in range(10)]
    view = pulled[9]
    cam = []
    for i in range(12):
        value = jnp.full((slabs, LANES), cams[0, i], F32)
        for v in range(1, cams.shape[0]):
            value = jnp.where(view == float(v), cams[v, i], value)
        cam.append(value)

    def put(f, value):
        grads[f * slabs : (f + 1) * slabs, :] = value

    def column(s):
        return pl.ds(pl.multiple_of(start + s * LANES, LANES), LANES)

    for s in range(slabs):
        for row in range(0, features, 8):
            count = min(8, features - row)
            feats[pl.ds(row * slabs + s, count, stride=slabs), :] = params[
                row : row + count, column(s)
            ]
    project_pull(
        lambda f: feats[f * slabs : (f + 1) * slabs, :], cam, pulled[2:8] + pulled[:2] + pulled[8:9], put
    )
    rate = learn_rate / (1.0 - beta_one**adam_steps)
    unbias = 1.0 / (1.0 - beta_two**adam_steps)
    stores = []
    order = list(range(16, features, 8)) + [0, 8]
    for row in order:
        count = min(8, features - row)
        span = slice(row, row + count)
        for s in range(slabs):
            here = (span, slice(s * LANES, (s + 1) * LANES))
            grad = grads[pl.ds(row * slabs + s, count, stride=slabs), :]
            moment = beta_one * adam_m[span, column(s)] + (1.0 - beta_one) * grad
            second = beta_two * adam_v[span, column(s)] + (1.0 - beta_two) * grad * grad
            scaled = second * unbias
            root = scaled * lax.rsqrt(scaled)
            made.at[1][here] = moment
            made.at[2][here] = second
            made.at[0][here] = params[span, column(s)] - rate * moment / (
                root + adam_eps
            )
        if row % 16 == 8 or row + count == features:
            first = row // 16 * 16
            span = pl.ds(first, row + count - first)
            columns = pl.ds(pl.multiple_of(start, LANES), width)
            for k in range(3):
                store = pltpu.make_async_copy(
                    made.at[k, span], sinks[k].at[span, columns], sems.at[k, first // 16]
                )
                store.start()
                stores.append(store)
    for store in stores:
        store.wait()


def vmem():
    return pl.BlockSpec(memory_space=pltpu.VMEM)


def smem():
    return pl.BlockSpec(memory_space=pltpu.SMEM)


def any_space():
    return pl.BlockSpec(memory_space=pl.ANY)


def call(kernel, name, out_shape, in_specs, scratch, args, out_specs=None, grant=32):
    return pl.pallas_call(
        kernel,
        out_shape=out_shape,
        in_specs=in_specs,
        out_specs=out_specs or tuple(vmem() for _ in out_shape),
        scratch_shapes=scratch,
        compiler_params=pltpu.CompilerParams(vmem_limit_bytes=grant * 1024 * 1024),
        name=name,
    )(*args)


def work_shapes(tile_count, pixels, listed):
    tiles = 2 * tile_count
    spans = tiles * pixels // LANES
    assert spans < LIST_STEP and tiles * listed // LANES == 8 and tiles == 4
    return [pltpu.VMEM(((listed + 1) * LIST_STEP, LANES), F32)] * 4 + [
        pltpu.VMEM((2 * listed, spans * LANES), BF16),
        pltpu.VMEM((listed // LANES, 8 * tiles + 8, LANES), F32),
        pltpu.VMEM((8, tiles * listed), F32),
        pltpu.VMEM((24 * tiles, tiles * listed), F32),
        pltpu.VMEM((listed // LANES, 8 * tiles + 8, LANES), F32),
        pltpu.VMEM((8, LANES), jnp.int32),
        pltpu.VMEM((listed // LANES, 8 * tiles + 8, LANES), F32),
        pltpu.VMEM((8, LANES), F32),
    ]


def near(tile_ids, cameras, where, own, other, parts, tile_count):
    width = sum(part.shape[1] for part in parts)
    features = parts[0].shape[0]
    slabs = width // LANES
    pixels = listed = own.shape[1] // tile_count
    return call(
        functools.partial(near_kernel, len(parts)),
        "near",
        (
            jax.ShapeDtypeStruct((3, own.shape[1]), F32),
            jax.ShapeDtypeStruct((ROWS * (slabs + 1), LANES), F32),
            jax.ShapeDtypeStruct((ROWS, width), F32),
        ),
        [smem()] * 3 + [vmem()] * (2 + len(parts)),
        [pltpu.VMEM(((features + 8) * slabs, LANES), F32), pltpu.VMEM((2,) + own.shape, F32)]
        + work_shapes(tile_count, pixels, listed),
        (tile_ids, cameras, where, own, other, *parts),
    )


def far(tile_ids, where, rows, partial, infos, pieces, tile_count, blocks):
    width = partial.shape[1]
    pixels = listed = infos.shape[1] // tile_count
    info = (infos.shape[0] // 2, infos.shape[1])
    return call(
        functools.partial(far_kernel, blocks),
        "far",
        (jax.ShapeDtypeStruct((ROWS, width // pieces), F32),) * pieces,
        [smem()] * 2 + [vmem()] * 3,
        [pltpu.VMEM((2,) + info, F32)] + work_shapes(tile_count, pixels, listed),
        (tile_ids, where, rows, partial, infos),
    )


def join(first, second):
    shape = (2 * first.shape[0], first.shape[1])
    return call(
        join_kernel, "join", (jax.ShapeDtypeStruct(shape, F32),), [vmem()] * 2, [], (first, second)
    )[0]


def update(own, first, cameras, params, adam_m, adam_v, packets, before):
    features = params.shape[0]
    width = sum(packet.shape[1] for packet in packets)
    slabs = width // LANES
    shape = jax.ShapeDtypeStruct(params.shape, F32)
    at = 5 + len(packets)
    return pl.pallas_call(
        functools.partial(update_kernel, len(packets), len(before) > 0),
        out_shape=(shape, shape, shape),
        in_specs=[smem()] * 2
        + [vmem()] * (3 + len(packets))
        + [any_space()] * len(before),
        out_specs=(any_space(),) * 3,
        scratch_shapes=[
            pltpu.VMEM(((features + 8) * slabs, LANES), F32),
            pltpu.VMEM(((ROWS + 1) * slabs, LANES), F32),
            pltpu.VMEM(((features + 8) * slabs, LANES), F32),
            pltpu.VMEM((3, features, width), F32),
            pltpu.SemaphoreType.DMA((3, (features + 15) // 16)),
        ],
        input_output_aliases={at + k: k for k in range(len(before))},
        compiler_params=pltpu.CompilerParams(vmem_limit_bytes=32 * 1024 * 1024),
        name="update",
    )(
        jnp.stack([own, jnp.int32(first)]).astype(jnp.int32),
        cameras, params, adam_m, adam_v, *packets, *before,
    )


def swap(value, axis, d):
    if d == 0:
        return value
    return lax.ppermute(value, axis, [(k, k ^ d) for k in range(lax.axis_size(axis))])


def local(params, adam_m, adam_v, cameras, target, tile_ids, hit_shard, hit_local):
    width = params.shape[1]
    tile_count, listed = hit_local.shape
    shards = lax.axis_size("gs")
    along = lax.axis_size("tile")
    chunk = width // shards
    group = lax.axis_index("gs")
    seat = lax.axis_index("tile")
    aligned = chunk % LANES == 0
    team = BLOCK_TILES // tile_count
    assert team == 4
    blocks = along // team

    info, params = pack(group, params, target, hit_shard, hit_local, shards)
    parts = cut(group, cameras, params, shards if aligned else 1)
    if not aligned:
        parts = [
            lax.dynamic_slice_in_dim(parts[0], (group ^ d) * chunk, chunk, axis=1)
            for d in range(shards)
        ]
    parts = [swap(parts[d], "gs", d) for d in range(shards)]
    beside = swap(info, "tile", 1)
    beyond = swap(join(info, beside), "tile", 2)
    if not aligned:
        parts = [jnp.concatenate(parts, axis=1)]
    where = jnp.stack([seat % team, seat // team, jnp.int32(chunk)]).astype(jnp.int32)
    rendered, rows, partial = near(tile_ids, cameras, where, info, beside, parts, tile_count)
    packets = far(tile_ids, where, rows, partial, beyond, len(parts), tile_count, blocks)
    if not aligned:
        packets = [packets[0][:, d * chunk : (d + 1) * chunk] for d in range(shards)]
    packets = [swap(packets[d], "gs", d) for d in range(shards)]
    if blocks > 1:
        packets = [block_sum(packet, along, team) for packet in packets]
    if aligned:
        own = group
    else:
        packets = [jnp.stack(packets)[jnp.arange(shards) ^ group].transpose(1, 0, 2).reshape(ROWS, -1)]
        own = jnp.int32(0)
    made = ()
    count = max(1, len(packets) // 2)
    for first in range(0, len(packets), count):
        made = update(
            own, first, cameras, params, adam_m, adam_v, packets[first : first + count], made
        )
    new_params, new_m, new_v = made
    return (rendered, new_params, new_m, new_v)


def block_sum(packet, along, team):
    step = team
    while step < along:
        packet = packet + swap(packet, "tile", step)
        step *= 2
    return packet


def solution(mesh):
    return jax.shard_map(
        local,
        mesh=mesh,
        in_specs=(
            P(None, ("groups", "gs")),
            P(None, ("groups", "gs")),
            P(None, ("groups", "gs")),
            P("groups", None),
            P(None, ("groups", "gs", "tile")),
            P(("groups", "gs", "tile")),
            P(("groups", "gs", "tile"), None, None),
            P(("groups", "gs", "tile"), None),
        ),
        out_specs=(
            P(None, ("groups", "gs", "tile")),
            P(None, ("groups", "gs")),
            P(None, ("groups", "gs")),
            P(None, ("groups", "gs")),
        ),
        check_vma=False,
    )
```

```python
import functools

import jax
import jax.numpy as jnp
from jax import lax
from jax.experimental import pallas as pl
from jax.experimental.pallas import tpu as pltpu
from jax.sharding import PartitionSpec as P

TILES_X = 120
TILES_Y = 68
TILE_SIDE = 16
BLOCK_TILES = 8
LANES = 128
ROWS = 16
LIST_STEP = 9
F32 = jnp.float32
BF16 = jnp.bfloat16

focal_length = 1000.0
center_x = 960.0
center_y = 540.0
dilation = 0.3
beta_one = 0.9
beta_two = 0.999
learn_rate = 0.01
adam_eps = 1e-08
adam_steps = 100.0
sh_const = (
    0.28209479177387814,
    0.4886025119029199,
    1.0925484305920792,
    0.31539156525252005,
    0.5462742152960396,
    0.5900435899266435,
    2.890611442640554,
    0.4570457994644658,
    0.3731763325901154,
    1.445305721320277,
)


def sh_basis(x, y, z):
    s = sh_const
    xx, yy, zz = x * x, y * y, z * z
    return [
        None,
        -s[1] * y,
        s[1] * z,
        -s[1] * x,
        s[2] * (x * y),
        -s[2] * (y * z),
        s[3] * (2.0 * zz - xx - yy),
        -s[2] * (x * z),
        s[4] * (xx - yy),
        -s[5] * y * (3.0 * xx - yy),
        s[6] * (x * y) * z,
        -s[7] * y * (4.0 * zz - xx - yy),
        s[8] * z * (2.0 * zz - 3.0 * xx - 3.0 * yy),
        -s[7] * x * (4.0 * zz - xx - yy),
        s[9] * z * (xx - yy),
        -s[5] * x * (xx - 3.0 * yy),
    ]


def sh_pull(h, x, y, z):
    s = sh_const
    xx, yy, zz = x * x, y * y, z * z
    xy, xz, yz = x * y, x * z, y * z
    diff = xx - yy
    ring = 4.0 * zz - xx - yy
    g_x = (
        -s[1] * h[3]
        + s[2] * (h[4] * y - h[7] * z)
        - (2.0 * s[3]) * h[6] * x
        + (2.0 * s[4]) * h[8] * x
        - (6.0 * s[5]) * h[9] * xy
        + s[6] * h[10] * yz
        + (2.0 * s[7]) * h[11] * xy
        - (6.0 * s[8]) * h[12] * xz
        - s[7] * h[13] * (ring - 2.0 * xx)
        + (2.0 * s[9]) * h[14] * xz
        - (3.0 * s[5]) * h[15] * diff
    )
    g_y = (
        -s[1] * h[1]
        + s[2] * (h[4] * x - h[5] * z)
        - (2.0 * s[3]) * h[6] * y
        - (2.0 * s[4]) * h[8] * y
        - (3.0 * s[5]) * h[9] * diff
        + s[6] * h[10] * xz
        - s[7] * h[11] * (ring - 2.0 * yy)
        - (6.0 * s[8]) * h[12] * yz
        + (2.0 * s[7]) * h[13] * xy
        - (2.0 * s[9]) * h[14] * yz
        + (6.0 * s[5]) * h[15] * xy
    )
    g_z = (
        s[1] * h[2]
        - s[2] * (h[5] * y + h[7] * x)
        + (4.0 * s[3]) * h[6] * z
        + s[6] * h[10] * xy
        - (8.0 * s[7]) * (h[11] * yz + h[13] * xz)
        + s[8] * h[12] * (6.0 * zz - 3.0 * xx - 3.0 * yy)
        + s[9] * h[14] * diff
    )
    return g_x, g_y, g_z


def project_parts(feat, cam):
    rot = [[cam[3 * r + c] for c in range(3)] for r in range(3)]
    off = [feat(a) - cam[9 + a] for a in range(3)]
    in_cam = [rot[r][0] * off[0] + rot[r][1] * off[1] + rot[r][2] * off[2] for r in range(3)]
    inv = 1.0 / in_cam[2]
    u = in_cam[0] * inv
    v = in_cam[1] * inv
    finv = focal_length * inv
    scale = [jnp.exp(2.0 * feat(3 + a)) for a in range(3)]
    quat = [feat(6 + a) for a in range(4)]
    rnorm = lax.rsqrt(quat[0] * quat[0] + quat[1] * quat[1] + quat[2] * quat[2] + quat[3] * quat[3])
    w, x, y, z = [q * rnorm for q in quat]
    turn = [
        [1.0 - 2.0 * (y * y + z * z), 2.0 * (x * y - w * z), 2.0 * (x * z + w * y)],
        [2.0 * (x * y + w * z), 1.0 - 2.0 * (x * x + z * z), 2.0 * (y * z - w * x)],
        [2.0 * (x * z - w * y), 2.0 * (y * z + w * x), 1.0 - 2.0 * (x * x + y * y)],
    ]
    screen = [
        [finv * (rot[0][c] - u * rot[2][c]) for c in range(3)],
        [finv * (rot[1][c] - v * rot[2][c]) for c in range(3)],
    ]
    axes = [
        [sum(screen[r][c] * turn[c][k] for c in range(3)) for k in range(3)] for r in range(2)
    ]
    wide = [[axes[r][k] * scale[k] for k in range(3)] for r in range(2)]
    cov_xx = sum(wide[0][k] * axes[0][k] for k in range(3)) + dilation
    cov_xy = sum(wide[0][k] * axes[1][k] for k in range(3))
    cov_yy = sum(wide[1][k] * axes[1][k] for k in range(3)) + dilation
    rdet = 1.0 / (cov_xx * cov_yy - cov_xy * cov_xy)
    conic = (cov_yy * rdet, -cov_xy * rdet, cov_xx * rdet)
    rlen = lax.rsqrt(off[0] * off[0] + off[1] * off[1] + off[2] * off[2])
    way = [off[a] * rlen for a in range(3)]
    return dict(
        rot=rot, inv=inv, u=u, v=v, finv=finv, scale=scale, rnorm=rnorm, rotor=(w, x, y, z), turn=turn,
        screen=screen, axes=axes, wide=wide, conic=conic, rlen=rlen, way=way,
    )


def shade(feat, cam):
    off = [feat(a) - cam[9 + a] for a in range(3)]
    rlen = lax.rsqrt(off[0] * off[0] + off[1] * off[1] + off[2] * off[2])
    basis = sh_basis(*[off[a] * rlen for a in range(3)])
    colours = []
    for k in range(3):
        total = 0.5 + sh_const[0] * feat(11 + 16 * k)
        for b in range(1, 16):
            total = total + feat(11 + 16 * k + b) * basis[b]
        colours.append(total)
    return colours


def project_rows(feat, cam):
    part = project_parts(feat, cam)
    mean_x = focal_length * part["u"] + center_x
    mean_y = focal_length * part["v"] + center_y
    logit = feat(10)
    log_opacity = jnp.minimum(logit, 0.0) - jnp.log(1.0 + jnp.exp(-jnp.abs(logit)))
    return [mean_x, mean_y, *part["conic"], log_opacity]


def project_pull(feat, cam, grads, put):
    part = project_parts(feat, cam)
    g_mx, g_my, g_a, g_b, g_c, g_o = grads[:6]
    g_col = grads[6:9]
    way, rlen = part["way"], part["rlen"]
    basis = sh_basis(*way)
    pulled = [None]
    for k in range(3):
        put(11 + 16 * k, sh_const[0] * g_col[k])
    for b in range(1, 16):
        total = 0.0
        for k in range(3):
            put(11 + 16 * k + b, g_col[k] * basis[b])
            total = total + g_col[k] * feat(11 + 16 * k + b)
        pulled.append(total)
    g_way = sh_pull(pulled, *way)
    along = way[0] * g_way[0] + way[1] * g_way[1] + way[2] * g_way[2]
    g_off = [(g_way[a] - way[a] * along) * rlen for a in range(3)]
    put(10, g_o / (1.0 + jnp.exp(feat(10))))
    a, b, c = part["conic"]
    g_xx = -(a * a * g_a + a * b * g_b + b * b * g_c)
    g_xy = -(2.0 * a * b * g_a + (a * c + b * b) * g_b + 2.0 * b * c * g_c)
    g_yy = -(b * b * g_a + b * c * g_b + c * c * g_c)
    axes, wide, turn, screen = part["axes"], part["wide"], part["turn"], part["screen"]
    for k in range(3):
        g_scale = (
            g_xx * axes[0][k] * wide[0][k]
            + g_xy * axes[0][k] * wide[1][k]
            + g_yy * axes[1][k] * wide[1][k]
        )
        put(3 + k, 2.0 * g_scale)
    g_axes = [
        [2.0 * g_xx * wide[0][k] + g_xy * wide[1][k] for k in range(3)],
        [2.0 * g_yy * wide[1][k] + g_xy * wide[0][k] for k in range(3)],
    ]
    g_screen = [
        [sum(g_axes[r][k] * turn[c][k] for k in range(3)) for c in range(3)] for r in range(2)
    ]
    gm = [
        [g_axes[0][k] * screen[0][c] + g_axes[1][k] * screen[1][c] for k in range(3)]
        for c in range(3)
    ]
    w, x, y, z = part["rotor"]
    up_xy, up_xz, up_yz = gm[0][1] + gm[1][0], gm[0][2] + gm[2][0], gm[1][2] + gm[2][1]
    un_xy, un_xz, un_yz = gm[1][0] - gm[0][1], gm[0][2] - gm[2][0], gm[2][1] - gm[1][2]
    g_rotor = [
        2.0 * (z * un_xy + y * un_xz + x * un_yz),
        2.0 * (y * up_xy + z * up_xz + w * un_yz - 2.0 * x * (gm[1][1] + gm[2][2])),
        2.0 * (x * up_xy + z * up_yz + w * un_xz - 2.0 * y * (gm[0][0] + gm[2][2])),
        2.0 * (x * up_xz + y * up_yz + w * un_xy - 2.0 * z * (gm[0][0] + gm[1][1])),
    ]
    rotor = (w, x, y, z)
    along = sum(rotor[i] * g_rotor[i] for i in range(4))
    for i in range(4):
        put(6 + i, (g_rotor[i] - rotor[i] * along) * part["rnorm"])
    rot, inv, finv, u, v = part["rot"], part["inv"], part["finv"], part["u"], part["v"]
    g_u = focal_length * g_mx - finv * sum(g_screen[0][c] * rot[2][c] for c in range(3))
    g_v = focal_length * g_my - finv * sum(g_screen[1][c] * rot[2][c] for c in range(3))
    g_f = sum(g_screen[r][c] * screen[r][c] for r in range(2) for c in range(3))
    g_in = [g_u * inv, g_v * inv, -(g_f + g_u * u + g_v * v) * inv]
    for axis in range(3):
        put(
            axis,
            g_off[axis] + rot[0][axis] * g_in[0] + rot[1][axis] * g_in[1] + rot[2][axis] * g_in[2],
        )


def split(value):
    high = value.astype(BF16)
    return high, (value - high.astype(F32)).astype(BF16)


def matmul(a, b, dims=((1,), (0,))):
    return lax.dot_general(a, b, (dims, ((), ())), preferred_element_type=F32)


def spread_features(parts, scratch, count):
    tiles = sum(part.shape[1] for part in parts) // LANES
    at = 0
    for part in parts:
        for first in range(0, part.shape[1], LANES):
            for row in range(0, count, 8):
                rows = min(8, count - row)
                scratch[pl.ds(row * tiles + at, rows, stride=tiles), :] = part[
                    row : row + rows, first : first + LANES
                ]
            at += 1
    return tiles


def pack_kernel(shards, where, *refs):
    sources, (info, params, shard_of, local_of, goal, place_s, sems) = refs[:4], refs[4:]
    group = where[0]
    loads = [
        pltpu.make_async_copy(source, held, sems.at[k])
        for k, (source, held) in enumerate(zip(sources, (shard_of, local_of, goal, params)))
    ]
    for load in loads:
        load.start()
    for load in loads[:3]:
        load.wait()
    width = info.shape[1]
    tile_count, listed = local_of.shape
    rows_each = (info.shape[0] - 4) // tile_count
    columns = rows_each * width
    chunk = columns // shards
    info[0:3, :] = goal[...]
    for t in range(tile_count):
        place = (shard_of[t] ^ group) * chunk + (local_of[t : t + 1, :] - group * chunk)
        info[3:4, t * listed : (t + 1) * listed] = place.astype(F32)
        row_i = lax.broadcasted_iota(jnp.int32, (LANES, LANES), 0)
        col_i = lax.broadcasted_iota(jnp.int32, (LANES, LANES), 1)
        for first in range(0, listed, LANES):
            spread = jnp.broadcast_to(place[:, first : first + LANES].astype(F32), (LANES, LANES))
            place_s[first : first + LANES, :] = jnp.broadcast_to(
                jnp.sum(jnp.where(row_i == col_i, spread, 0.0), axis=1, keepdims=True), (LANES, LANES)
            )
        lane_of = lax.broadcasted_iota(jnp.int32, (8, LANES), 1).astype(F32)
        row_of = lax.broadcasted_iota(jnp.int32, (8, LANES), 0).astype(F32)
        for s in range(columns // LANES):
            best = jnp.full((8, LANES), -1.0, F32)
            column = lane_of + float(s * LANES)
            for first in range(0, listed, 8):
                best = jnp.where(
                    place_s[first : first + 8, :] == column, row_of + float(first), best
                )
            best = jnp.max(best, axis=0, keepdims=True)
            row, at = 4 + t * rows_each + s * LANES // width, s * LANES % width
            info[row : row + 1, at : at + LANES] = best
    loads[3].wait()


def pack(group, params, target, hit_shard, hit_local, shards):
    columns = params.shape[1]
    tile_count, listed = hit_local.shape
    width = target.shape[1]
    rows = 4 + tile_count * (columns // width)
    args = (hit_shard.reshape(tile_count, 1, listed), hit_local, target, params)
    return call(
        functools.partial(pack_kernel, shards),
        "pack",
        (jax.ShapeDtypeStruct((rows, width), F32), jax.ShapeDtypeStruct(params.shape, F32)),
        [smem()] + [pl.BlockSpec(memory_space=pltpu.HBM)] * 4,
        [
            pltpu.VMEM((tile_count, 1, listed), jnp.int32),
            pltpu.VMEM((tile_count, listed), jnp.int32),
            pltpu.VMEM(target.shape, F32),
            pltpu.VMEM((listed, LANES), F32),
            pltpu.SemaphoreType.DMA((4,)),
        ],
        (group.reshape(1),) + tuple(pltpu.with_memory_space_constraint(a, pltpu.HBM) for a in args),
        (vmem(), any_space()),
    )


def sent_rows(views):
    return (11 + 3 * views + 7) // 8 * 8


def cut_kernel(pieces, where, cams, params, *refs):
    parts, (feats, rows) = refs[:pieces], refs[pieces:]
    views = cams.shape[0]
    count = sent_rows(views)
    slabs = spread_features([params], feats, params.shape[0])

    def feat(f):
        return feats[f * slabs : (f + 1) * slabs, :]

    values = [feat(f) for f in range(11)]
    for v in range(views):
        values += shade(feat, [cams[v, i] for i in range(12)])
    values += [jnp.zeros((slabs, LANES), F32)] * (count - len(values))
    for f, value in enumerate(values):
        rows[pl.ds(f, slabs, stride=count), :] = value
    each = slabs // pieces
    for d in range(pieces):
        for h in range(each):
            first = (((where[0] ^ d) % pieces) * each + h) * count
            parts[d][:, h * LANES : (h + 1) * LANES] = rows[
                pl.ds(pl.multiple_of(first, 8), count), :
            ]


def cut(group, cameras, params, pieces):
    features, columns = params.shape
    slabs = columns // LANES
    count = sent_rows(cameras.shape[0])
    return list(
        call(
            functools.partial(cut_kernel, pieces),
            "cut",
            (jax.ShapeDtypeStruct((count, columns // pieces), F32),) * pieces,
            [smem()] * 2 + [vmem()],
            [
                pltpu.VMEM(((features + 8) * slabs, LANES), F32),
                pltpu.VMEM((count * (slabs + 1), LANES), F32),
            ],
            (group.reshape(1), cameras, params),
        )
    )


def lane_gather(source, lane):
    return jnp.take_along_axis(source, lane, axis=1, mode="promise_in_bounds")


def pixel_basis(pixels):
    pixel = lax.broadcasted_iota(jnp.int32, (8, pixels), 1)
    row = lax.broadcasted_iota(jnp.int32, (8, pixels), 0)
    middle = 0.5 * TILE_SIDE - 0.5
    u = (pixel % TILE_SIDE).astype(F32) - middle
    v = (pixel // TILE_SIDE).astype(F32) - middle
    value = jnp.where(row == 0, 1.0, 0.0)
    for at, term in ((1, u), (2, v), (3, u * u), (4, u * v), (5, v * v)):
        value = jnp.where(row == at, term, value)
    return value


def composite(tiles, first_group, me, rows, info_s, rendered, work):
    alpha_s, weight_s, pull_s, push_s, weight_2, entry_s, coef_s, colour_s, sums_s, index_s, acc_s, ninth_s = work
    groups = info_s.shape[0]
    listed = acc_s.shape[0] * LANES
    tile_count = info_s.shape[2] // listed
    pixels = info_s.shape[2] // tile_count
    parts = pixels // LANES
    halves = listed // LANES
    tiles_here = groups * tile_count
    spans = tiles_here * parts
    slabs = rows.shape[0] // ROWS - 1
    side = TILE_SIDE
    first_col, first_row = tiles

    def of_span(span):
        return pl.ds(span, listed, stride=LIST_STEP)

    def of_place(place):
        return pl.ds(place * LIST_STEP, spans)

    basis = pixel_basis(pixels)
    basis_3 = jnp.concatenate([basis, basis, basis], axis=0).astype(BF16)
    row_of = lax.broadcasted_iota(jnp.int32, (8, listed), 0)

    entries = []
    for n in range(tiles_here):
        g, t = n // tile_count, n % tile_count
        found = []
        for h in range(halves):
            first = t * listed + h * LANES
            at = info_s[g, 3:4, first : first + LANES].astype(jnp.int32)
            index_s[n * halves + h : n * halves + h + 1, :] = at
            at = jnp.broadcast_to(at, (8, LANES))
            lane, slab = at & (LANES - 1), at >> 7
            value = lane_gather(rows[0:8, :], lane)
            for s in range(1, slabs):
                value = jnp.where(
                    slab == s, lane_gather(rows[s * ROWS : s * ROWS + 8, :], lane), value
                )
            found.append(value)
        entries.append(jnp.concatenate(found, axis=1))
        for h in range(halves):
            entry_s[h, 8 * n : 8 * n + 8, :] = found[h]
    at = index_s[...]
    lane, slab = at & (LANES - 1), at >> 7
    ninth = lane_gather(rows[8:16, :], lane)
    for s in range(1, slabs):
        ninth = jnp.where(
            slab == s, lane_gather(rows[s * ROWS + 8 : s * ROWS + 16, :], lane), ninth
        )

    def of_lists(ref, f):
        at = pl.ds(f, tiles_here, stride=8)
        return jnp.concatenate([ref[h, at, :] for h in range(halves)], axis=1)

    tile_of = lax.broadcasted_iota(jnp.int32, (tiles_here, listed), 0)
    slot = (me ^ (first_group + tile_of // tile_count)) * tile_count + tile_of % tile_count
    mean_u = of_lists(entry_s, 2) - (((first_col + slot % 4) * side).astype(F32) + 0.5 * side)
    mean_v = of_lists(entry_s, 3) - (((first_row + slot // 4) * side).astype(F32) + 0.5 * side)
    quad_a = -0.5 * of_lists(entry_s, 4)
    quad_b = -of_lists(entry_s, 5)
    quad_c = -0.5 * of_lists(entry_s, 6)
    slope_u = 2.0 * quad_a * mean_u + quad_b * mean_v
    slope_v = 2.0 * quad_c * mean_v + quad_b * mean_u
    level = 0.5 * (slope_u * mean_u + slope_v * mean_v) + of_lists(entry_s, 7)
    for f, value in enumerate((level, -slope_u, -slope_v, quad_a, quad_b, quad_c)):
        for n in range(tiles_here):
            coef_s[f : f + 1, n * listed : (n + 1) * listed] = value[n : n + 1]
    coef_s[6:8, :] = jnp.zeros((2, tiles_here * listed), F32)
    coef = coef_s[...]
    terms = []
    for _ in range(3):
        terms.append(coef.astype(BF16).astype(F32))
        coef = coef - terms[-1]
    down = ((0,), (0,))
    power = matmul(jnp.concatenate(terms, axis=0).astype(BF16), basis_3, down)
    for n in range(tiles_here):
        for part in range(parts):
            alpha_s[of_span(n * parts + part), :] = jnp.exp(
                power[n * listed : (n + 1) * listed, part * LANES : (part + 1) * LANES]
            )
    colour_s[...] = jnp.zeros(colour_s.shape, F32)
    hues = []
    for n in range(tiles_here):
        last = jnp.concatenate([ninth[n * halves + h : n * halves + h + 1] for h in range(halves)], axis=1)
        colours = jnp.where(row_of < 2, entries[n], jnp.where(row_of == 2, last, 0.0))
        high = colours.astype(BF16).astype(F32)
        low = colours - high
        here = slice(n * listed, (n + 1) * listed)
        for at, value in ((0, high), (8, low), (16, high)):
            colour_s[24 * n + at : 24 * n + at + 8, here] = value
        hues.append(jnp.concatenate([high, low], axis=0).astype(BF16))

    unroll, quad = 32, 4
    steps = listed // unroll

    def forward(step, passed):
        for j in range(0, unroll, quad):
            at = [of_place(step * unroll + j + i) for i in range(quad)]
            alpha = [alpha_s[at[i], :] for i in range(quad)]
            keep = [1.0 - alpha[i] for i in range(quad)]
            two = keep[0] * keep[1]
            three = two * keep[2]
            weight_s[at[0], :] = alpha[0] * passed
            weight_s[at[1], :] = (alpha[1] * keep[0]) * passed
            weight_s[at[2], :] = (alpha[2] * two) * passed
            weight_s[at[3], :] = (alpha[3] * three) * passed
            passed = passed * (two * (keep[2] * keep[3]))
        return passed

    nought = jnp.zeros((spans, LANES), F32)
    lax.fori_loop(0, steps, forward, nought + 1.0)

    errors = []
    for n in range(tiles_here):
        g, t = n // tile_count, n % tile_count
        for part in range(parts):
            at = slice((n * parts + part) * LANES, (n * parts + part + 1) * LANES)
            weight_2[:listed, at], weight_2[listed:, at] = split(
                weight_s[of_span(n * parts + part), :]
            )
        at = slice(n * pixels, (n + 1) * pixels)
        image = matmul(hues[n], weight_2[:listed, at])
        image = image[0:8] + image[8:16] + matmul(hues[n], weight_2[listed:, at])[0:8]
        here = slice(t * pixels, (t + 1) * pixels)
        if rendered is not None and g == 0:
            rendered[:, here] = image[0:3]
        error = image - info_s[g, 0:8, here]
        high = error.astype(BF16).astype(F32)
        low = error - high
        errors += [high, high, low]

        hue = jnp.concatenate([high, low], axis=0).astype(BF16)
        across = ((1,), (1,))
        grads = matmul(hue, weight_2[:listed, at], across) + matmul(hue, weight_2[listed:, at], across)
        grads = grads[0:8] + grads[8:16]
        for h in range(halves):
            acc_s[h, 8 * n : 8 * n + 8, :] = grads[:, h * LANES : (h + 1) * LANES]
            row = n * halves + h
            ninth_s[row : row + 1, :] = grads[2:3, h * LANES : (h + 1) * LANES]
    pull = matmul(colour_s[...].astype(BF16), jnp.concatenate(errors, axis=0).astype(BF16), down)
    for n in range(tiles_here):
        for part in range(parts):
            pull_s[of_span(n * parts + part), :] = pull[
                n * listed : (n + 1) * listed, part * LANES : (part + 1) * LANES
            ]

    def backward(back, behind):
        for j in range(0, unroll, quad):
            at = [of_place(listed - 1 - (back * unroll + j + i)) for i in range(quad)]
            alpha = [alpha_s[at[i], :] for i in range(quad)]
            pull = [pull_s[at[i], :] for i in range(quad)]
            keep = [1.0 - alpha[i] for i in range(quad)]
            own = alpha[0] * pull[0]
            seen, through = behind, keep[0]
            for i in range(quad):
                push_s[at[i], :] = weight_s[at[i], :] * (pull[i] - seen)
                if i > 0:
                    own = own * keep[i] + alpha[i] * pull[i]
                    through = through * keep[i]
                seen = behind * through + own
            behind = seen
        return behind

    lax.fori_loop(0, steps, backward, nought)

    basis = basis.astype(BF16)
    for n in range(tiles_here):
        high, low = split(
            jnp.concatenate([push_s[of_span(n * parts + part), :] for part in range(parts)], axis=1)
        )
        moments = matmul(basis, high, across) + matmul(basis, low, across)
        for h in range(halves):
            sums_s[h, 8 * n : 8 * n + 8, :] = moments[:, h * LANES : (h + 1) * LANES]
    m_00, m_10, m_01, m_20, m_11, m_02 = [
        of_lists(sums_s, m) for m in range(6)
    ]
    n_10 = m_10 - mean_u * m_00
    n_01 = m_01 - mean_v * m_00
    for f, value in (
        (2, -(2.0 * quad_a * n_10 + quad_b * n_01)),
        (3, -(2.0 * quad_c * n_01 + quad_b * n_10)),
        (4, -0.5 * (m_20 - mean_u * (m_10 + n_10))),
        (5, -(m_11 - mean_u * m_01 - mean_v * n_10)),
        (6, -0.5 * (m_02 - mean_v * (m_01 + n_01))),
        (7, m_00),
    ):
        for h in range(halves):
            acc_s[h, pl.ds(f, tiles_here, stride=8), :] = value[:, h * LANES : (h + 1) * LANES]


def pool_sum(slab, info_s, acc_s, ninth_s):
    groups, _, width = info_s.shape
    listed = acc_s.shape[0] * LANES
    tile_count = width // listed
    halves = listed // LANES
    rows_each = (info_s.shape[1] - 4) // tile_count
    row_of = lax.broadcasted_iota(jnp.int32, (8, LANES), 0)

    totals, every = [], None
    for g in range(groups):
        total = jnp.zeros((8, LANES), F32)
        for t in range(tile_count):
            row, first = 4 + t * rows_each + slab * LANES // width, slab * LANES % width
            at = info_s[g, row : row + 1, first : first + LANES].astype(jnp.int32)
            at = jnp.broadcast_to(at, (8, LANES))
            n = g * tile_count + t
            every = at if every is None else jnp.where(row_of >= n * halves, at, every)
            lane, half = at & (LANES - 1), at >> 7
            for h in range(halves):
                here = lane_gather(acc_s[h, 8 * n : 8 * n + 8, :], lane)
                total = total + jnp.where(half == h, here, 0.0)
        totals.append(total)
    here = lane_gather(ninth_s[...], every & (LANES - 1))
    ninth = jnp.where(every >> 7 == row_of % halves, here, 0.0)
    return totals[0] + totals[1], jnp.sum(ninth, axis=0, keepdims=True)


def block_start(tile_id):
    within = tile_id % (TILES_X * TILES_Y)
    return (within % TILES_X) // 4 * 4, (within // TILES_X) // 2 * 2


def near_kernel(pieces, tile_ids, cams, where, own, other, *refs):
    parts = refs[:pieces]
    rendered, rows, partial, feats, info_s, *work = refs[pieces:]
    view = tile_ids[0] // (TILES_X * TILES_Y)
    cam = [cams[view, i] for i in range(12)]
    slabs = spread_features(parts, feats, parts[0].shape[0])
    projected = project_rows(lambda f: feats[f * slabs : (f + 1) * slabs, :], cam)
    colours = []
    for k in range(3):
        first = pl.multiple_of((11 + 3 * view + k) * slabs, slabs)
        colours.append(feats[pl.ds(first, slabs), :])
    for f, value in enumerate(colours[:2] + projected + [colours[2]] * 8):
        rows[pl.ds(f, slabs, stride=ROWS), :] = value
    info_s[0] = own[...]
    info_s[1] = other[...]
    composite(block_start(tile_ids[0]), 0, where[0], rows, info_s, rendered, work)
    for s in range(slabs):
        at = slice(s * LANES, (s + 1) * LANES)
        partial[0:8, at], partial[8:9, at] = pool_sum(s, info_s, *work[-2:])


def far_kernel(blocks, tile_ids, where, rows, partial, infos, *refs):
    *packets, info_s = refs[: len(refs) - 12]
    work = refs[len(refs) - 12 :]
    half = infos.shape[0] // 2
    info_s[0] = infos[:half, :]
    info_s[1] = infos[half:, :]
    composite(block_start(tile_ids[0]), 2, where[0], rows, info_s, None, work)
    share = (tile_ids[0] // (TILES_X * TILES_Y)).astype(F32)
    row_of = lax.broadcasted_iota(jnp.int32, (8, LANES), 0)
    lane_of = lax.broadcasted_iota(jnp.int32, (8, LANES), 1)
    chunk = packets[0].shape[1]
    for s in range(rows.shape[0] // ROWS - 1):
        total, ninth = pool_sum(s, info_s, *work[-2:])
        total = total + partial[0:8, s * LANES : (s + 1) * LANES]
        ninth = ninth + partial[8:9, s * LANES : (s + 1) * LANES]
        if blocks == 1:
            mine = share
        else:
            column = s * LANES + lane_of
            mine = jnp.where(column % where[2] // (where[2] // blocks) == where[1], share, 0.0)
        at = slice(s * LANES % chunk, s * LANES % chunk + LANES)
        packets[s * LANES // chunk][0:8, at] = total
        packets[s * LANES // chunk][8:16, at] = jnp.where(
            row_of == 0, jnp.broadcast_to(ninth, (8, LANES)), mine
        )


def join_kernel(first, second, out):
    half = first.shape[0]
    out[:half, :] = first[...]
    out[half:, :] = second[...]


def update_kernel(pieces, follows, where, cams, params, adam_m, adam_v, *refs):
    packets, refs = refs[:pieces], refs[pieces + 3 * follows :]
    sinks, (feats, rows, grads, made, sems) = refs[:3], refs[3:]
    features = params.shape[0]
    chunk = packets[0].shape[1]
    width = pieces * chunk
    slabs = width // LANES
    start = (where[0] ^ where[1]) // pieces * pieces * chunk
    for d in range(pieces):
        for h in range(chunk // LANES):
            slab = (where[0] ^ where[1] ^ d) % pieces * (chunk // LANES) + h
            rows[pl.ds(slab, ROWS, stride=slabs), :] = packets[d][:, h * LANES : (h + 1) * LANES]
    pulled = [rows[f * slabs : (f + 1) * slabs, :] for f in range(10)]
    view = pulled[9]
    cam = []
    for i in range(12):
        value = jnp.full((slabs, LANES), cams[0, i], F32)
        for v in range(1, cams.shape[0]):
            value = jnp.where(view == float(v), cams[v, i], value)
        cam.append(value)

    def put(f, value):
        grads[f * slabs : (f + 1) * slabs, :] = value

    def column(s):
        return pl.ds(pl.multiple_of(start + s * LANES, LANES), LANES)

    for s in range(slabs):
        for row in range(0, features, 8):
            count = min(8, features - row)
            feats[pl.ds(row * slabs + s, count, stride=slabs), :] = params[
                row : row + count, column(s)
            ]
    project_pull(
        lambda f: feats[f * slabs : (f + 1) * slabs, :], cam, pulled[2:8] + pulled[:2] + pulled[8:9], put
    )
    rate = learn_rate / (1.0 - beta_one**adam_steps)
    unbias = 1.0 / (1.0 - beta_two**adam_steps)
    stores = []
    order = list(range(16, features, 8)) + [0, 8]
    for row in order:
        count = min(8, features - row)
        span = slice(row, row + count)
        for s in range(slabs):
            here = (span, slice(s * LANES, (s + 1) * LANES))
            grad = grads[pl.ds(row * slabs + s, count, stride=slabs), :]
            moment = beta_one * adam_m[span, column(s)] + (1.0 - beta_one) * grad
            second = beta_two * adam_v[span, column(s)] + (1.0 - beta_two) * grad * grad
            made.at[1][here] = moment
            made.at[2][here] = second
            made.at[0][here] = params[span, column(s)] - rate * moment / (
                jnp.sqrt(second * unbias) + adam_eps
            )
        if row % 16 == 8 or row + count == features:
            first = row // 16 * 16
            span = pl.ds(first, row + count - first)
            columns = pl.ds(pl.multiple_of(start, LANES), width)
            for k in range(3):
                store = pltpu.make_async_copy(
                    made.at[k, span], sinks[k].at[span, columns], sems.at[k, first // 16]
                )
                store.start()
                stores.append(store)
    for store in stores:
        store.wait()


def vmem():
    return pl.BlockSpec(memory_space=pltpu.VMEM)


def smem():
    return pl.BlockSpec(memory_space=pltpu.SMEM)


def any_space():
    return pl.BlockSpec(memory_space=pl.ANY)


def call(kernel, name, out_shape, in_specs, scratch, args, out_specs=None, grant=32):
    return pl.pallas_call(
        kernel,
        out_shape=out_shape,
        in_specs=in_specs,
        out_specs=out_specs or tuple(vmem() for _ in out_shape),
        scratch_shapes=scratch,
        compiler_params=pltpu.CompilerParams(vmem_limit_bytes=grant * 1024 * 1024),
        name=name,
    )(*args)


def work_shapes(tile_count, pixels, listed):
    tiles = 2 * tile_count
    spans = tiles * pixels // LANES
    assert spans < LIST_STEP and tiles * listed // LANES == 8 and tiles == 4
    return [pltpu.VMEM(((listed + 1) * LIST_STEP, LANES), F32)] * 4 + [
        pltpu.VMEM((2 * listed, spans * LANES), BF16),
        pltpu.VMEM((listed // LANES, 8 * tiles + 8, LANES), F32),
        pltpu.VMEM((8, tiles * listed), F32),
        pltpu.VMEM((24 * tiles, tiles * listed), F32),
        pltpu.VMEM((listed // LANES, 8 * tiles + 8, LANES), F32),
        pltpu.VMEM((8, LANES), jnp.int32),
        pltpu.VMEM((listed // LANES, 8 * tiles + 8, LANES), F32),
        pltpu.VMEM((8, LANES), F32),
    ]


def near(tile_ids, cameras, where, own, other, parts, tile_count):
    width = sum(part.shape[1] for part in parts)
    features = parts[0].shape[0]
    slabs = width // LANES
    pixels = listed = own.shape[1] // tile_count
    return call(
        functools.partial(near_kernel, len(parts)),
        "near",
        (
            jax.ShapeDtypeStruct((3, own.shape[1]), F32),
            jax.ShapeDtypeStruct((ROWS * (slabs + 1), LANES), F32),
            jax.ShapeDtypeStruct((ROWS, width), F32),
        ),
        [smem()] * 3 + [vmem()] * (2 + len(parts)),
        [pltpu.VMEM(((features + 8) * slabs, LANES), F32), pltpu.VMEM((2,) + own.shape, F32)]
        + work_shapes(tile_count, pixels, listed),
        (tile_ids, cameras, where, own, other, *parts),
    )


def far(tile_ids, where, rows, partial, infos, pieces, tile_count, blocks):
    width = partial.shape[1]
    pixels = listed = infos.shape[1] // tile_count
    info = (infos.shape[0] // 2, infos.shape[1])
    return call(
        functools.partial(far_kernel, blocks),
        "far",
        (jax.ShapeDtypeStruct((ROWS, width // pieces), F32),) * pieces,
        [smem()] * 2 + [vmem()] * 3,
        [pltpu.VMEM((2,) + info, F32)] + work_shapes(tile_count, pixels, listed),
        (tile_ids, where, rows, partial, infos),
    )


def join(first, second):
    shape = (2 * first.shape[0], first.shape[1])
    return call(
        join_kernel, "join", (jax.ShapeDtypeStruct(shape, F32),), [vmem()] * 2, [], (first, second)
    )[0]


def update(own, first, cameras, params, adam_m, adam_v, packets, before):
    features = params.shape[0]
    width = sum(packet.shape[1] for packet in packets)
    slabs = width // LANES
    shape = jax.ShapeDtypeStruct(params.shape, F32)
    at = 5 + len(packets)
    return pl.pallas_call(
        functools.partial(update_kernel, len(packets), len(before) > 0),
        out_shape=(shape, shape, shape),
        in_specs=[smem()] * 2
        + [vmem()] * (3 + len(packets))
        + [any_space()] * len(before),
        out_specs=(any_space(),) * 3,
        scratch_shapes=[
            pltpu.VMEM(((features + 8) * slabs, LANES), F32),
            pltpu.VMEM(((ROWS + 1) * slabs, LANES), F32),
            pltpu.VMEM(((features + 8) * slabs, LANES), F32),
            pltpu.VMEM((3, features, width), F32),
            pltpu.SemaphoreType.DMA((3, (features + 15) // 16)),
        ],
        input_output_aliases={at + k: k for k in range(len(before))},
        compiler_params=pltpu.CompilerParams(vmem_limit_bytes=32 * 1024 * 1024),
        name="update",
    )(
        jnp.stack([own, jnp.int32(first)]).astype(jnp.int32),
        cameras, params, adam_m, adam_v, *packets, *before,
    )


def swap(value, axis, d):
    if d == 0:
        return value
    return lax.ppermute(value, axis, [(k, k ^ d) for k in range(lax.axis_size(axis))])


def local(params, adam_m, adam_v, cameras, target, tile_ids, hit_shard, hit_local):
    width = params.shape[1]
    tile_count, listed = hit_local.shape
    shards = lax.axis_size("gs")
    along = lax.axis_size("tile")
    chunk = width // shards
    group = lax.axis_index("gs")
    seat = lax.axis_index("tile")
    aligned = chunk % LANES == 0
    team = BLOCK_TILES // tile_count
    assert team == 4
    blocks = along // team

    info, params = pack(group, params, target, hit_shard, hit_local, shards)
    parts = cut(group, cameras, params, shards if aligned else 1)
    if not aligned:
        parts = [
            lax.dynamic_slice_in_dim(parts[0], (group ^ d) * chunk, chunk, axis=1)
            for d in range(shards)
        ]
    parts = [swap(parts[d], "gs", d) for d in range(shards)]
    beside = swap(info, "tile", 1)
    beyond = swap(join(info, beside), "tile", 2)
    if not aligned:
        parts = [jnp.concatenate(parts, axis=1)]
    where = jnp.stack([seat % team, seat // team, jnp.int32(chunk)]).astype(jnp.int32)
    rendered, rows, partial = near(tile_ids, cameras, where, info, beside, parts, tile_count)
    packets = far(tile_ids, where, rows, partial, beyond, len(parts), tile_count, blocks)
    if not aligned:
        packets = [packets[0][:, d * chunk : (d + 1) * chunk] for d in range(shards)]
    packets = [swap(packets[d], "gs", d) for d in range(shards)]
    if blocks > 1:
        packets = [block_sum(packet, along, team) for packet in packets]
    if aligned:
        own = group
    else:
        packets = [jnp.stack(packets)[jnp.arange(shards) ^ group].transpose(1, 0, 2).reshape(ROWS, -1)]
        own = jnp.int32(0)
    made = ()
    count = max(1, len(packets) // 2)
    for first in range(0, len(packets), count):
        made = update(
            own, first, cameras, params, adam_m, adam_v, packets[first : first + count], made
        )
    new_params, new_m, new_v = made
    return (rendered, new_params, new_m, new_v)


def block_sum(packet, along, team):
    step = team
    while step < along:
        packet = packet + swap(packet, "tile", step)
        step *= 2
    return packet


def solution(mesh):
    return jax.shard_map(
        local,
        mesh=mesh,
        in_specs=(
            P(None, ("groups", "gs")),
            P(None, ("groups", "gs")),
            P(None, ("groups", "gs")),
            P("groups", None),
            P(None, ("groups", "gs", "tile")),
            P(("groups", "gs", "tile")),
            P(("groups", "gs", "tile"), None, None),
            P(("groups", "gs", "tile"), None),
        ),
        out_specs=(
            P(None, ("groups", "gs", "tile")),
            P(None, ("groups", "gs")),
            P(None, ("groups", "gs")),
            P(None, ("groups", "gs")),
        ),
        check_vma=False,
    )
```

```python
import functools

import jax
import jax.numpy as jnp
from jax import lax
from jax.experimental import pallas as pl
from jax.experimental.pallas import tpu as pltpu
from jax.sharding import PartitionSpec as P

TILES_X = 120
TILES_Y = 68
TILE_SIDE = 16
BLOCK_TILES = 8
LANES = 128
ROWS = 16
LIST_STEP = 9
F32 = jnp.float32
BF16 = jnp.bfloat16

focal_length = 1000.0
center_x = 960.0
center_y = 540.0
dilation = 0.3
beta_one = 0.9
beta_two = 0.999
learn_rate = 0.01
adam_eps = 1e-08
adam_steps = 100.0
sh_const = (
    0.28209479177387814,
    0.4886025119029199,
    1.0925484305920792,
    0.31539156525252005,
    0.5462742152960396,
    0.5900435899266435,
    2.890611442640554,
    0.4570457994644658,
    0.3731763325901154,
    1.445305721320277,
)


def sh_basis(x, y, z):
    s = sh_const
    xx, yy, zz = x * x, y * y, z * z
    return [
        None,
        -s[1] * y,
        s[1] * z,
        -s[1] * x,
        s[2] * (x * y),
        -s[2] * (y * z),
        s[3] * (2.0 * zz - xx - yy),
        -s[2] * (x * z),
        s[4] * (xx - yy),
        -s[5] * y * (3.0 * xx - yy),
        s[6] * (x * y) * z,
        -s[7] * y * (4.0 * zz - xx - yy),
        s[8] * z * (2.0 * zz - 3.0 * xx - 3.0 * yy),
        -s[7] * x * (4.0 * zz - xx - yy),
        s[9] * z * (xx - yy),
        -s[5] * x * (xx - 3.0 * yy),
    ]


def sh_pull(h, x, y, z):
    s = sh_const
    xx, yy, zz = x * x, y * y, z * z
    xy, xz, yz = x * y, x * z, y * z
    diff = xx - yy
    ring = 4.0 * zz - xx - yy
    g_x = (
        -s[1] * h[3]
        + s[2] * (h[4] * y - h[7] * z)
        - (2.0 * s[3]) * h[6] * x
        + (2.0 * s[4]) * h[8] * x
        - (6.0 * s[5]) * h[9] * xy
        + s[6] * h[10] * yz
        + (2.0 * s[7]) * h[11] * xy
        - (6.0 * s[8]) * h[12] * xz
        - s[7] * h[13] * (ring - 2.0 * xx)
        + (2.0 * s[9]) * h[14] * xz
        - (3.0 * s[5]) * h[15] * diff
    )
    g_y = (
        -s[1] * h[1]
        + s[2] * (h[4] * x - h[5] * z)
        - (2.0 * s[3]) * h[6] * y
        - (2.0 * s[4]) * h[8] * y
        - (3.0 * s[5]) * h[9] * diff
        + s[6] * h[10] * xz
        - s[7] * h[11] * (ring - 2.0 * yy)
        - (6.0 * s[8]) * h[12] * yz
        + (2.0 * s[7]) * h[13] * xy
        - (2.0 * s[9]) * h[14] * yz
        + (6.0 * s[5]) * h[15] * xy
    )
    g_z = (
        s[1] * h[2]
        - s[2] * (h[5] * y + h[7] * x)
        + (4.0 * s[3]) * h[6] * z
        + s[6] * h[10] * xy
        - (8.0 * s[7]) * (h[11] * yz + h[13] * xz)
        + s[8] * h[12] * (6.0 * zz - 3.0 * xx - 3.0 * yy)
        + s[9] * h[14] * diff
    )
    return g_x, g_y, g_z


def project_parts(feat, cam):
    rot = [[cam[3 * r + c] for c in range(3)] for r in range(3)]
    off = [feat(a) - cam[9 + a] for a in range(3)]
    in_cam = [rot[r][0] * off[0] + rot[r][1] * off[1] + rot[r][2] * off[2] for r in range(3)]
    inv = 1.0 / in_cam[2]
    u = in_cam[0] * inv
    v = in_cam[1] * inv
    finv = focal_length * inv
    scale = [jnp.exp(2.0 * feat(3 + a)) for a in range(3)]
    quat = [feat(6 + a) for a in range(4)]
    rnorm = lax.rsqrt(quat[0] * quat[0] + quat[1] * quat[1] + quat[2] * quat[2] + quat[3] * quat[3])
    w, x, y, z = [q * rnorm for q in quat]
    turn = [
        [1.0 - 2.0 * (y * y + z * z), 2.0 * (x * y - w * z), 2.0 * (x * z + w * y)],
        [2.0 * (x * y + w * z), 1.0 - 2.0 * (x * x + z * z), 2.0 * (y * z - w * x)],
        [2.0 * (x * z - w * y), 2.0 * (y * z + w * x), 1.0 - 2.0 * (x * x + y * y)],
    ]
    screen = [
        [finv * (rot[0][c] - u * rot[2][c]) for c in range(3)],
        [finv * (rot[1][c] - v * rot[2][c]) for c in range(3)],
    ]
    axes = [
        [sum(screen[r][c] * turn[c][k] for c in range(3)) for k in range(3)] for r in range(2)
    ]
    wide = [[axes[r][k] * scale[k] for k in range(3)] for r in range(2)]
    cov_xx = sum(wide[0][k] * axes[0][k] for k in range(3)) + dilation
    cov_xy = sum(wide[0][k] * axes[1][k] for k in range(3))
    cov_yy = sum(wide[1][k] * axes[1][k] for k in range(3)) + dilation
    rdet = 1.0 / (cov_xx * cov_yy - cov_xy * cov_xy)
    conic = (cov_yy * rdet, -cov_xy * rdet, cov_xx * rdet)
    rlen = lax.rsqrt(off[0] * off[0] + off[1] * off[1] + off[2] * off[2])
    way = [off[a] * rlen for a in range(3)]
    return dict(
        rot=rot, inv=inv, u=u, v=v, finv=finv, scale=scale, rnorm=rnorm, rotor=(w, x, y, z), turn=turn,
        screen=screen, axes=axes, wide=wide, conic=conic, rlen=rlen, way=way,
    )


def shade(feat, cam):
    off = [feat(a) - cam[9 + a] for a in range(3)]
    rlen = lax.rsqrt(off[0] * off[0] + off[1] * off[1] + off[2] * off[2])
    basis = sh_basis(*[off[a] * rlen for a in range(3)])
    colours = []
    for k in range(3):
        total = 0.5 + sh_const[0] * feat(11 + 16 * k)
        for b in range(1, 16):
            total = total + feat(11 + 16 * k + b) * basis[b]
        colours.append(total)
    return colours


def project_rows(feat, cam):
    part = project_parts(feat, cam)
    mean_x = focal_length * part["u"] + center_x
    mean_y = focal_length * part["v"] + center_y
    logit = feat(10)
    log_opacity = jnp.minimum(logit, 0.0) - jnp.log(1.0 + jnp.exp(-jnp.abs(logit)))
    return [mean_x, mean_y, *part["conic"], log_opacity]


def flatten(part, basis):
    values = [value for row in part["rot"] for value in row]
    values += [part[key] for key in ("inv", "u", "v", "finv", "rnorm", "rlen")]
    values += list(part["rotor"]) + list(part["conic"]) + list(part["way"])
    for key in ("turn", "screen", "axes", "wide"):
        values += [value for row in part[key] for value in row]
    return values + basis[1:]


def unflatten(values):
    values = iter(values)

    def take(count):
        return [next(values) for _ in range(count)]

    def table(count):
        return [take(3) for _ in range(count)]

    part = dict(rot=table(3))
    for key in ("inv", "u", "v", "finv", "rnorm", "rlen"):
        part[key] = next(values)
    part["rotor"], part["conic"], part["way"] = take(4), take(3), take(3)
    for key, count in (("turn", 3), ("screen", 2), ("axes", 2), ("wide", 2)):
        part[key] = table(count)
    return part, [None] + take(15)


READY = 9 + 6 + 4 + 3 + 3 + 9 + 6 + 6 + 6 + 15


def project_pull(feat, part, basis, grads, put):
    g_mx, g_my, g_a, g_b, g_c, g_o = grads[:6]
    g_col = grads[6:9]
    way, rlen = part["way"], part["rlen"]
    pulled = [None]
    for k in range(3):
        put(11 + 16 * k, sh_const[0] * g_col[k])
    for b in range(1, 16):
        total = 0.0
        for k in range(3):
            put(11 + 16 * k + b, g_col[k] * basis[b])
            total = total + g_col[k] * feat(11 + 16 * k + b)
        pulled.append(total)
    g_way = sh_pull(pulled, *way)
    along = way[0] * g_way[0] + way[1] * g_way[1] + way[2] * g_way[2]
    g_off = [(g_way[a] - way[a] * along) * rlen for a in range(3)]
    put(10, g_o / (1.0 + jnp.exp(feat(10))))
    a, b, c = part["conic"]
    g_xx = -(a * a * g_a + a * b * g_b + b * b * g_c)
    g_xy = -(2.0 * a * b * g_a + (a * c + b * b) * g_b + 2.0 * b * c * g_c)
    g_yy = -(b * b * g_a + b * c * g_b + c * c * g_c)
    axes, wide, turn, screen = part["axes"], part["wide"], part["turn"], part["screen"]
    for k in range(3):
        g_scale = (
            g_xx * axes[0][k] * wide[0][k]
            + g_xy * axes[0][k] * wide[1][k]
            + g_yy * axes[1][k] * wide[1][k]
        )
        put(3 + k, 2.0 * g_scale)
    g_axes = [
        [2.0 * g_xx * wide[0][k] + g_xy * wide[1][k] for k in range(3)],
        [2.0 * g_yy * wide[1][k] + g_xy * wide[0][k] for k in range(3)],
    ]
    g_screen = [
        [sum(g_axes[r][k] * turn[c][k] for k in range(3)) for c in range(3)] for r in range(2)
    ]
    gm = [
        [g_axes[0][k] * screen[0][c] + g_axes[1][k] * screen[1][c] for k in range(3)]
        for c in range(3)
    ]
    w, x, y, z = part["rotor"]
    up_xy, up_xz, up_yz = gm[0][1] + gm[1][0], gm[0][2] + gm[2][0], gm[1][2] + gm[2][1]
    un_xy, un_xz, un_yz = gm[1][0] - gm[0][1], gm[0][2] - gm[2][0], gm[2][1] - gm[1][2]
    g_rotor = [
        2.0 * (z * un_xy + y * un_xz + x * un_yz),
        2.0 * (y * up_xy + z * up_xz + w * un_yz - 2.0 * x * (gm[1][1] + gm[2][2])),
        2.0 * (x * up_xy + z * up_yz + w * un_xz - 2.0 * y * (gm[0][0] + gm[2][2])),
        2.0 * (x * up_xz + y * up_yz + w * un_xy - 2.0 * z * (gm[0][0] + gm[1][1])),
    ]
    rotor = (w, x, y, z)
    along = sum(rotor[i] * g_rotor[i] for i in range(4))
    for i in range(4):
        put(6 + i, (g_rotor[i] - rotor[i] * along) * part["rnorm"])
    rot, inv, finv, u, v = part["rot"], part["inv"], part["finv"], part["u"], part["v"]
    g_u = focal_length * g_mx - finv * sum(g_screen[0][c] * rot[2][c] for c in range(3))
    g_v = focal_length * g_my - finv * sum(g_screen[1][c] * rot[2][c] for c in range(3))
    g_f = sum(g_screen[r][c] * screen[r][c] for r in range(2) for c in range(3))
    g_in = [g_u * inv, g_v * inv, -(g_f + g_u * u + g_v * v) * inv]
    for axis in range(3):
        put(
            axis,
            g_off[axis] + rot[0][axis] * g_in[0] + rot[1][axis] * g_in[1] + rot[2][axis] * g_in[2],
        )


def split(value):
    high = value.astype(BF16)
    return high, (value - high.astype(F32)).astype(BF16)


def matmul(a, b, dims=((1,), (0,))):
    return lax.dot_general(a, b, (dims, ((), ())), preferred_element_type=F32)


def spread_features(parts, scratch, count):
    tiles = sum(part.shape[1] for part in parts) // LANES
    at = 0
    for part in parts:
        for first in range(0, part.shape[1], LANES):
            for row in range(0, count, 8):
                rows = min(8, count - row)
                scratch[pl.ds(row * tiles + at, rows, stride=tiles), :] = part[
                    row : row + rows, first : first + LANES
                ]
            at += 1
    return tiles


def pack_kernel(shards, where, *refs):
    sources, (info, params, shard_of, local_of, goal, place_s, sems) = refs[:4], refs[4:]
    group = where[0]
    loads = [
        pltpu.make_async_copy(source, held, sems.at[k])
        for k, (source, held) in enumerate(zip(sources, (shard_of, local_of, goal, params)))
    ]
    for load in loads:
        load.start()
    for load in loads[:3]:
        load.wait()
    width = info.shape[1]
    tile_count, listed = local_of.shape
    rows_each = (info.shape[0] - 4) // tile_count
    columns = rows_each * width
    chunk = columns // shards
    info[0:3, :] = goal[...]
    for t in range(tile_count):
        place = (shard_of[t] ^ group) * chunk + (local_of[t : t + 1, :] - group * chunk)
        info[3:4, t * listed : (t + 1) * listed] = place.astype(F32)
        row_i = lax.broadcasted_iota(jnp.int32, (LANES, LANES), 0)
        col_i = lax.broadcasted_iota(jnp.int32, (LANES, LANES), 1)
        for first in range(0, listed, LANES):
            spread = jnp.broadcast_to(place[:, first : first + LANES].astype(F32), (LANES, LANES))
            place_s[first : first + LANES, :] = jnp.broadcast_to(
                jnp.sum(jnp.where(row_i == col_i, spread, 0.0), axis=1, keepdims=True), (LANES, LANES)
            )
        lane_of = lax.broadcasted_iota(jnp.int32, (8, LANES), 1).astype(F32)
        row_of = lax.broadcasted_iota(jnp.int32, (8, LANES), 0).astype(F32)
        for s in range(columns // LANES):
            best = jnp.full((8, LANES), -1.0, F32)
            column = lane_of + float(s * LANES)
            for first in range(0, listed, 8):
                best = jnp.where(
                    place_s[first : first + 8, :] == column, row_of + float(first), best
                )
            best = jnp.max(best, axis=0, keepdims=True)
            row, at = 4 + t * rows_each + s * LANES // width, s * LANES % width
            info[row : row + 1, at : at + LANES] = best
    loads[3].wait()


def pack(group, params, target, hit_shard, hit_local, shards):
    columns = params.shape[1]
    tile_count, listed = hit_local.shape
    width = target.shape[1]
    rows = 4 + tile_count * (columns // width)
    args = (hit_shard.reshape(tile_count, 1, listed), hit_local, target, params)
    return call(
        functools.partial(pack_kernel, shards),
        "pack",
        (jax.ShapeDtypeStruct((rows, width), F32), jax.ShapeDtypeStruct(params.shape, F32)),
        [smem()] + [pl.BlockSpec(memory_space=pltpu.HBM)] * 4,
        [
            pltpu.VMEM((tile_count, 1, listed), jnp.int32),
            pltpu.VMEM((tile_count, listed), jnp.int32),
            pltpu.VMEM(target.shape, F32),
            pltpu.VMEM((listed, LANES), F32),
            pltpu.SemaphoreType.DMA((4,)),
        ],
        (group.reshape(1),) + tuple(pltpu.with_memory_space_constraint(a, pltpu.HBM) for a in args),
        (vmem(), any_space()),
    )


def sent_rows(views):
    return (12 + 3 * views + 7) // 8 * 8


def cut_kernel(pieces, where, tile_ids, cams, params, *refs):
    parts, (feats, rows) = refs[:pieces], refs[pieces:]
    views = cams.shape[0]
    count = sent_rows(views)
    slabs = spread_features([params], feats, params.shape[0])

    def feat(f):
        return feats[f * slabs : (f + 1) * slabs, :]

    values = [feat(f) for f in range(11)]
    for v in range(views):
        values += shade(feat, [cams[v, i] for i in range(12)])
    values += [jnp.zeros((slabs, LANES), F32)] * (count - 1 - len(values))
    values.append(jnp.full((slabs, LANES), (tile_ids[0] // (TILES_X * TILES_Y)).astype(F32), F32))
    for f, value in enumerate(values):
        rows[pl.ds(f, slabs, stride=count), :] = value
    each = slabs // pieces
    for d in range(pieces):
        for h in range(each):
            first = (((where[0] ^ d) % pieces) * each + h) * count
            parts[d][:, h * LANES : (h + 1) * LANES] = rows[
                pl.ds(pl.multiple_of(first, 8), count), :
            ]


def cut(group, tile_ids, cameras, params, pieces):
    features, columns = params.shape
    slabs = columns // LANES
    count = sent_rows(cameras.shape[0])
    return list(
        call(
            functools.partial(cut_kernel, pieces),
            "cut",
            (jax.ShapeDtypeStruct((count, columns // pieces), F32),) * pieces,
            [smem()] * 3 + [vmem()],
            [
                pltpu.VMEM(((features + 8) * slabs, LANES), F32),
                pltpu.VMEM((count * (slabs + 1), LANES), F32),
            ],
            (group.reshape(1), tile_ids, cameras, params),
        )
    )


def lane_gather(source, lane):
    return jnp.take_along_axis(source, lane, axis=1, mode="promise_in_bounds")


def pixel_basis(pixels):
    pixel = lax.broadcasted_iota(jnp.int32, (8, pixels), 1)
    row = lax.broadcasted_iota(jnp.int32, (8, pixels), 0)
    middle = 0.5 * TILE_SIDE - 0.5
    u = (pixel % TILE_SIDE).astype(F32) - middle
    v = (pixel // TILE_SIDE).astype(F32) - middle
    value = jnp.where(row == 0, 1.0, 0.0)
    for at, term in ((1, u), (2, v), (3, u * u), (4, u * v), (5, v * v)):
        value = jnp.where(row == at, term, value)
    return value


def composite(tiles, first_group, me, rows, info_s, rendered, work):
    alpha_s, weight_s, pull_s, push_s, weight_2, entry_s, coef_s, colour_s, sums_s, index_s, acc_s, ninth_s = work
    groups = info_s.shape[0]
    listed = acc_s.shape[0] * LANES
    tile_count = info_s.shape[2] // listed
    pixels = info_s.shape[2] // tile_count
    parts = pixels // LANES
    halves = listed // LANES
    tiles_here = groups * tile_count
    spans = tiles_here * parts
    slabs = rows.shape[0] // ROWS - 1
    side = TILE_SIDE
    first_col, first_row = tiles

    def of_span(span):
        return pl.ds(span, listed, stride=LIST_STEP)

    def of_place(place):
        return pl.ds(place * LIST_STEP, spans)

    basis = pixel_basis(pixels)
    basis_3 = jnp.concatenate([basis, basis, basis], axis=0).astype(BF16)
    row_of = lax.broadcasted_iota(jnp.int32, (8, listed), 0)

    entries = []
    for n in range(tiles_here):
        g, t = n // tile_count, n % tile_count
        found = []
        for h in range(halves):
            first = t * listed + h * LANES
            at = info_s[g, 3:4, first : first + LANES].astype(jnp.int32)
            index_s[n * halves + h : n * halves + h + 1, :] = at
            at = jnp.broadcast_to(at, (8, LANES))
            lane, slab = at & (LANES - 1), at >> 7
            value = lane_gather(rows[0:8, :], lane)
            for s in range(1, slabs):
                value = jnp.where(
                    slab == s, lane_gather(rows[s * ROWS : s * ROWS + 8, :], lane), value
                )
            found.append(value)
        entries.append(jnp.concatenate(found, axis=1))
        for h in range(halves):
            entry_s[h, 8 * n : 8 * n + 8, :] = found[h]
    at = index_s[...]
    lane, slab = at & (LANES - 1), at >> 7
    ninth = lane_gather(rows[8:16, :], lane)
    for s in range(1, slabs):
        ninth = jnp.where(
            slab == s, lane_gather(rows[s * ROWS + 8 : s * ROWS + 16, :], lane), ninth
        )

    def of_lists(ref, f):
        at = pl.ds(f, tiles_here, stride=8)
        return jnp.concatenate([ref[h, at, :] for h in range(halves)], axis=1)

    tile_of = lax.broadcasted_iota(jnp.int32, (tiles_here, listed), 0)
    slot = (me ^ (first_group + tile_of // tile_count)) * tile_count + tile_of % tile_count
    mean_u = of_lists(entry_s, 2) - (((first_col + slot % 4) * side).astype(F32) + 0.5 * side)
    mean_v = of_lists(entry_s, 3) - (((first_row + slot // 4) * side).astype(F32) + 0.5 * side)
    quad_a = -0.5 * of_lists(entry_s, 4)
    quad_b = -of_lists(entry_s, 5)
    quad_c = -0.5 * of_lists(entry_s, 6)
    slope_u = 2.0 * quad_a * mean_u + quad_b * mean_v
    slope_v = 2.0 * quad_c * mean_v + quad_b * mean_u
    level = 0.5 * (slope_u * mean_u + slope_v * mean_v) + of_lists(entry_s, 7)
    for f, value in enumerate((level, -slope_u, -slope_v, quad_a, quad_b, quad_c)):
        for n in range(tiles_here):
            coef_s[f : f + 1, n * listed : (n + 1) * listed] = value[n : n + 1]
    coef_s[6:8, :] = jnp.zeros((2, tiles_here * listed), F32)
    coef = coef_s[...]
    terms = []
    for _ in range(3):
        terms.append(coef.astype(BF16).astype(F32))
        coef = coef - terms[-1]
    down = ((0,), (0,))
    power = matmul(jnp.concatenate(terms, axis=0).astype(BF16), basis_3, down)
    for n in range(tiles_here):
        for part in range(parts):
            alpha_s[of_span(n * parts + part), :] = jnp.exp(
                power[n * listed : (n + 1) * listed, part * LANES : (part + 1) * LANES]
            )
    colour_s[...] = jnp.zeros(colour_s.shape, F32)
    hues = []
    for n in range(tiles_here):
        last = jnp.concatenate([ninth[n * halves + h : n * halves + h + 1] for h in range(halves)], axis=1)
        colours = jnp.where(row_of < 2, entries[n], jnp.where(row_of == 2, last, 0.0))
        high = colours.astype(BF16).astype(F32)
        low = colours - high
        here = slice(n * listed, (n + 1) * listed)
        for at, value in ((0, high), (8, low), (16, high)):
            colour_s[24 * n + at : 24 * n + at + 8, here] = value
        hues.append(jnp.concatenate([high, low], axis=0).astype(BF16))

    unroll, quad = 32, 4
    steps = listed // unroll

    def forward(step, passed):
        for j in range(0, unroll, quad):
            at = [of_place(step * unroll + j + i) for i in range(quad)]
            alpha = [alpha_s[at[i], :] for i in range(quad)]
            keep = [1.0 - alpha[i] for i in range(quad)]
            two = keep[0] * keep[1]
            three = two * keep[2]
            weight_s[at[0], :] = alpha[0] * passed
            weight_s[at[1], :] = (alpha[1] * keep[0]) * passed
            weight_s[at[2], :] = (alpha[2] * two) * passed
            weight_s[at[3], :] = (alpha[3] * three) * passed
            passed = passed * (two * (keep[2] * keep[3]))
        return passed

    nought = jnp.zeros((spans, LANES), F32)
    lax.fori_loop(0, steps, forward, nought + 1.0)

    errors = []
    for n in range(tiles_here):
        g, t = n // tile_count, n % tile_count
        for part in range(parts):
            at = slice((n * parts + part) * LANES, (n * parts + part + 1) * LANES)
            weight_2[:listed, at], weight_2[listed:, at] = split(
                weight_s[of_span(n * parts + part), :]
            )
        at = slice(n * pixels, (n + 1) * pixels)
        image = matmul(hues[n], weight_2[:listed, at])
        image = image[0:8] + image[8:16] + matmul(hues[n], weight_2[listed:, at])[0:8]
        here = slice(t * pixels, (t + 1) * pixels)
        if rendered is not None and g == 0:
            rendered[:, here] = image[0:3]
        error = image - info_s[g, 0:8, here]
        high = error.astype(BF16).astype(F32)
        low = error - high
        errors += [high, high, low]

        hue = jnp.concatenate([high, low], axis=0).astype(BF16)
        across = ((1,), (1,))
        grads = matmul(hue, weight_2[:listed, at], across) + matmul(hue, weight_2[listed:, at], across)
        grads = grads[0:8] + grads[8:16]
        for h in range(halves):
            acc_s[h, 8 * n : 8 * n + 8, :] = grads[:, h * LANES : (h + 1) * LANES]
            row = n * halves + h
            ninth_s[row : row + 1, :] = grads[2:3, h * LANES : (h + 1) * LANES]
    pull = matmul(colour_s[...].astype(BF16), jnp.concatenate(errors, axis=0).astype(BF16), down)
    for n in range(tiles_here):
        for part in range(parts):
            pull_s[of_span(n * parts + part), :] = pull[
                n * listed : (n + 1) * listed, part * LANES : (part + 1) * LANES
            ]

    def backward(back, behind):
        for j in range(0, unroll, quad):
            at = [of_place(listed - 1 - (back * unroll + j + i)) for i in range(quad)]
            alpha = [alpha_s[at[i], :] for i in range(quad)]
            pull = [pull_s[at[i], :] for i in range(quad)]
            keep = [1.0 - alpha[i] for i in range(quad)]
            own = alpha[0] * pull[0]
            seen, through = behind, keep[0]
            for i in range(quad):
                push_s[at[i], :] = weight_s[at[i], :] * (pull[i] - seen)
                if i > 0:
                    own = own * keep[i] + alpha[i] * pull[i]
                    through = through * keep[i]
                seen = behind * through + own
            behind = seen
        return behind

    lax.fori_loop(0, steps, backward, nought)

    basis = basis.astype(BF16)
    for n in range(tiles_here):
        high, low = split(
            jnp.concatenate([push_s[of_span(n * parts + part), :] for part in range(parts)], axis=1)
        )
        moments = matmul(basis, high, across) + matmul(basis, low, across)
        for h in range(halves):
            sums_s[h, 8 * n : 8 * n + 8, :] = moments[:, h * LANES : (h + 1) * LANES]
    m_00, m_10, m_01, m_20, m_11, m_02 = [
        of_lists(sums_s, m) for m in range(6)
    ]
    n_10 = m_10 - mean_u * m_00
    n_01 = m_01 - mean_v * m_00
    for f, value in (
        (2, -(2.0 * quad_a * n_10 + quad_b * n_01)),
        (3, -(2.0 * quad_c * n_01 + quad_b * n_10)),
        (4, -0.5 * (m_20 - mean_u * (m_10 + n_10))),
        (5, -(m_11 - mean_u * m_01 - mean_v * n_10)),
        (6, -0.5 * (m_02 - mean_v * (m_01 + n_01))),
        (7, m_00),
    ):
        for h in range(halves):
            acc_s[h, pl.ds(f, tiles_here, stride=8), :] = value[:, h * LANES : (h + 1) * LANES]


def pool_sum(slab, info_s, acc_s, ninth_s):
    groups, _, width = info_s.shape
    listed = acc_s.shape[0] * LANES
    tile_count = width // listed
    halves = listed // LANES
    rows_each = (info_s.shape[1] - 4) // tile_count
    row_of = lax.broadcasted_iota(jnp.int32, (8, LANES), 0)

    totals, every = [], None
    for g in range(groups):
        total = jnp.zeros((8, LANES), F32)
        for t in range(tile_count):
            row, first = 4 + t * rows_each + slab * LANES // width, slab * LANES % width
            at = info_s[g, row : row + 1, first : first + LANES].astype(jnp.int32)
            at = jnp.broadcast_to(at, (8, LANES))
            n = g * tile_count + t
            every = at if every is None else jnp.where(row_of >= n * halves, at, every)
            lane, half = at & (LANES - 1), at >> 7
            for h in range(halves):
                here = lane_gather(acc_s[h, 8 * n : 8 * n + 8, :], lane)
                total = total + jnp.where(half == h, here, 0.0)
        totals.append(total)
    here = lane_gather(ninth_s[...], every & (LANES - 1))
    ninth = jnp.where(every >> 7 == row_of % halves, here, 0.0)
    return totals[0] + totals[1], jnp.sum(ninth, axis=0, keepdims=True)


def block_start(tile_id):
    within = tile_id % (TILES_X * TILES_Y)
    return (within % TILES_X) // 4 * 4, (within // TILES_X) // 2 * 2


def near_kernel(pieces, tile_ids, cams, where, own, other, *refs):
    parts = refs[:pieces]
    rendered, rows, partial, feats, info_s, *work = refs[pieces:]
    view = tile_ids[0] // (TILES_X * TILES_Y)
    cam = [cams[view, i] for i in range(12)]
    slabs = spread_features(parts, feats, parts[0].shape[0])
    projected = project_rows(lambda f: feats[f * slabs : (f + 1) * slabs, :], cam)
    colours = []
    for k in range(3):
        first = pl.multiple_of((11 + 3 * view + k) * slabs, slabs)
        colours.append(feats[pl.ds(first, slabs), :])
    for f, value in enumerate(colours[:2] + projected + [colours[2]] * 8):
        rows[pl.ds(f, slabs, stride=ROWS), :] = value
    info_s[0] = own[...]
    info_s[1] = other[...]
    composite(block_start(tile_ids[0]), 0, where[0], rows, info_s, rendered, work)
    for s in range(slabs):
        at = slice(s * LANES, (s + 1) * LANES)
        partial[0:8, at], partial[8:9, at] = pool_sum(s, info_s, *work[-2:])


def far_kernel(blocks, tile_ids, where, rows, partial, infos, *refs):
    *packets, info_s = refs[: len(refs) - 12]
    work = refs[len(refs) - 12 :]
    half = infos.shape[0] // 2
    info_s[0] = infos[:half, :]
    info_s[1] = infos[half:, :]
    composite(block_start(tile_ids[0]), 2, where[0], rows, info_s, None, work)
    share = (tile_ids[0] // (TILES_X * TILES_Y)).astype(F32)
    row_of = lax.broadcasted_iota(jnp.int32, (8, LANES), 0)
    lane_of = lax.broadcasted_iota(jnp.int32, (8, LANES), 1)
    chunk = packets[0].shape[1]
    for s in range(rows.shape[0] // ROWS - 1):
        total, ninth = pool_sum(s, info_s, *work[-2:])
        total = total + partial[0:8, s * LANES : (s + 1) * LANES]
        ninth = ninth + partial[8:9, s * LANES : (s + 1) * LANES]
        if blocks == 1:
            mine = share
        else:
            column = s * LANES + lane_of
            mine = jnp.where(column % where[2] // (where[2] // blocks) == where[1], share, 0.0)
        at = slice(s * LANES % chunk, s * LANES % chunk + LANES)
        packets[s * LANES // chunk][0:8, at] = total
        packets[s * LANES // chunk][8:16, at] = jnp.where(
            row_of == 0, jnp.broadcast_to(ninth, (8, LANES)), mine
        )


def join_kernel(first, second, out):
    half = first.shape[0]
    out[:half, :] = first[...]
    out[half:, :] = second[...]


def update_kernel(pieces, follows, prepares, ready, where, cams, params, adam_m, adam_v, *refs):
    packets, refs = refs[:pieces], refs[pieces:]
    senders, refs = refs[: pieces * prepares], refs[pieces * prepares :]
    made_ready, refs = refs[: 2 * ready], refs[2 * ready + 3 * follows :]
    sinks, refs = refs[:3], refs[3:]
    next_ready, (feats, rows, grads, made, sems) = refs[: 2 * prepares], refs[2 * prepares :]
    features = params.shape[0]
    chunk = packets[0].shape[1]
    width = pieces * chunk
    slabs = width // LANES
    place = where[0] ^ where[1]
    start = place // pieces * pieces * chunk
    for d in range(pieces):
        for h in range(chunk // LANES):
            slab = (place ^ d) % pieces * (chunk // LANES) + h
            rows[pl.ds(slab, ROWS, stride=slabs), :] = packets[d][:, h * LANES : (h + 1) * LANES]
    pulled = [rows[f * slabs : (f + 1) * slabs, :] for f in range(10)]

    def put(f, value):
        grads[f * slabs : (f + 1) * slabs, :] = value

    def column(s):
        return pl.ds(pl.multiple_of(start + s * LANES, LANES), LANES)

    def forward(first, held, view):
        for s in range(slabs):
            at = pl.ds(pl.multiple_of(first + s * LANES, LANES), LANES)
            for row in range(0, features, 8):
                count = min(8, features - row)
                held[pl.ds(row * slabs + s, count, stride=slabs), :] = params[row : row + count, at]
        cam = []
        for i in range(12):
            value = jnp.full((slabs, LANES), cams[0, i], F32)
            for v in range(1, cams.shape[0]):
                value = jnp.where(view == float(v), cams[v, i], value)
            cam.append(value)
        part = project_parts(lambda f: held[f * slabs : (f + 1) * slabs, :], cam)
        return part, sh_basis(*part["way"])

    if ready:
        feats, saved = made_ready
        part, basis = unflatten([saved[8 * i : 8 * i + slabs, :] for i in range(READY)])
    else:
        part, basis = forward(start, feats, pulled[9])
    project_pull(
        lambda f: feats[f * slabs : (f + 1) * slabs, :],
        part, basis, pulled[2:8] + pulled[:2] + pulled[8:9], put,
    )
    rate = learn_rate / (1.0 - beta_one**adam_steps)
    unbias = 1.0 / (1.0 - beta_two**adam_steps)
    stores = []
    order = list(range(16, features, 8)) + [0, 8]
    for row in order:
        count = min(8, features - row)
        span = slice(row, row + count)
        for s in range(slabs):
            here = (span, slice(s * LANES, (s + 1) * LANES))
            grad = grads[pl.ds(row * slabs + s, count, stride=slabs), :]
            moment = beta_one * adam_m[span, column(s)] + (1.0 - beta_one) * grad
            second = beta_two * adam_v[span, column(s)] + (1.0 - beta_two) * grad * grad
            made.at[1][here] = moment
            made.at[2][here] = second
            made.at[0][here] = params[span, column(s)] - rate * moment / (
                jnp.sqrt(second * unbias) + adam_eps
            )
        if row % 16 == 8 or row + count == features:
            first = row // 16 * 16
            span = pl.ds(first, row + count - first)
            columns = pl.ds(pl.multiple_of(start, LANES), width)
            for k in range(3):
                store = pltpu.make_async_copy(
                    made.at[k, span], sinks[k].at[span, columns], sems.at[k, first // 16]
                )
                store.start()
                stores.append(store)
    if prepares:
        held, saved = next_ready
        place = place ^ pieces
        for d in range(pieces):
            for h in range(chunk // LANES):
                slab = (place ^ d) % pieces * (chunk // LANES) + h
                last = senders[d].shape[0] - 1
                rows[pl.ds(slab, 1), :] = senders[d][last : last + 1, h * LANES : (h + 1) * LANES]
        part, basis = forward(place // pieces * pieces * chunk, held, rows[:slabs, :])
        for i, value in enumerate(flatten(part, basis)):
            saved[8 * i : 8 * i + slabs, :] = value
    for store in stores:
        store.wait()


def vmem():
    return pl.BlockSpec(memory_space=pltpu.VMEM)


def smem():
    return pl.BlockSpec(memory_space=pltpu.SMEM)


def any_space():
    return pl.BlockSpec(memory_space=pl.ANY)


def call(kernel, name, out_shape, in_specs, scratch, args, out_specs=None, grant=32):
    return pl.pallas_call(
        kernel,
        out_shape=out_shape,
        in_specs=in_specs,
        out_specs=out_specs or tuple(vmem() for _ in out_shape),
        scratch_shapes=scratch,
        compiler_params=pltpu.CompilerParams(vmem_limit_bytes=grant * 1024 * 1024),
        name=name,
    )(*args)


def work_shapes(tile_count, pixels, listed):
    tiles = 2 * tile_count
    spans = tiles * pixels // LANES
    assert spans < LIST_STEP and tiles * listed // LANES == 8 and tiles == 4
    return [pltpu.VMEM(((listed + 1) * LIST_STEP, LANES), F32)] * 4 + [
        pltpu.VMEM((2 * listed, spans * LANES), BF16),
        pltpu.VMEM((listed // LANES, 8 * tiles + 8, LANES), F32),
        pltpu.VMEM((8, tiles * listed), F32),
        pltpu.VMEM((24 * tiles, tiles * listed), F32),
        pltpu.VMEM((listed // LANES, 8 * tiles + 8, LANES), F32),
        pltpu.VMEM((8, LANES), jnp.int32),
        pltpu.VMEM((listed // LANES, 8 * tiles + 8, LANES), F32),
        pltpu.VMEM((8, LANES), F32),
    ]


def near(tile_ids, cameras, where, own, other, parts, tile_count):
    width = sum(part.shape[1] for part in parts)
    features = parts[0].shape[0]
    slabs = width // LANES
    pixels = listed = own.shape[1] // tile_count
    return call(
        functools.partial(near_kernel, len(parts)),
        "near",
        (
            jax.ShapeDtypeStruct((3, own.shape[1]), F32),
            jax.ShapeDtypeStruct((ROWS * (slabs + 1), LANES), F32),
            jax.ShapeDtypeStruct((ROWS, width), F32),
        ),
        [smem()] * 3 + [vmem()] * (2 + len(parts)),
        [pltpu.VMEM(((features + 8) * slabs, LANES), F32), pltpu.VMEM((2,) + own.shape, F32)]
        + work_shapes(tile_count, pixels, listed),
        (tile_ids, cameras, where, own, other, *parts),
    )


def far(tile_ids, where, rows, partial, infos, pieces, tile_count, blocks):
    width = partial.shape[1]
    pixels = listed = infos.shape[1] // tile_count
    info = (infos.shape[0] // 2, infos.shape[1])
    return call(
        functools.partial(far_kernel, blocks),
        "far",
        (jax.ShapeDtypeStruct((ROWS, width // pieces), F32),) * pieces,
        [smem()] * 2 + [vmem()] * 3,
        [pltpu.VMEM((2,) + info, F32)] + work_shapes(tile_count, pixels, listed),
        (tile_ids, where, rows, partial, infos),
    )


def join(first, second):
    shape = (2 * first.shape[0], first.shape[1])
    return call(
        join_kernel, "join", (jax.ShapeDtypeStruct(shape, F32),), [vmem()] * 2, [], (first, second)
    )[0]


def update(own, first, cameras, params, adam_m, adam_v, packets, before, senders, ready):
    features = params.shape[0]
    width = sum(packet.shape[1] for packet in packets)
    slabs = width // LANES
    shape = jax.ShapeDtypeStruct(params.shape, F32)
    by_feature = ((features + 8) * slabs, LANES)
    prepares = len(senders) > 0
    at = 5 + len(packets) + len(senders) + len(ready)
    out = pl.pallas_call(
        functools.partial(update_kernel, len(packets), len(before) > 0, prepares, len(ready) > 0),
        out_shape=(shape, shape, shape)
        + (jax.ShapeDtypeStruct(by_feature, F32), jax.ShapeDtypeStruct((8 * READY, LANES), F32))
        * prepares,
        in_specs=[smem()] * 2
        + [vmem()] * (3 + len(packets) + len(senders) + len(ready))
        + [any_space()] * len(before),
        out_specs=(any_space(),) * 3 + (vmem(),) * (2 * prepares),
        scratch_shapes=[
            pltpu.VMEM(by_feature, F32),
            pltpu.VMEM(((ROWS + 1) * slabs, LANES), F32),
            pltpu.VMEM(by_feature, F32),
            pltpu.VMEM((3, features, width), F32),
            pltpu.SemaphoreType.DMA((3, (features + 15) // 16)),
        ],
        input_output_aliases={at + k: k for k in range(len(before))},
        compiler_params=pltpu.CompilerParams(vmem_limit_bytes=32 * 1024 * 1024),
        name="update",
    )(
        jnp.stack([own, jnp.int32(first)]).astype(jnp.int32),
        cameras, params, adam_m, adam_v, *packets, *senders, *ready, *before,
    )
    return out[:3], out[3:]


def swap(value, axis, d):
    if d == 0:
        return value
    return lax.ppermute(value, axis, [(k, k ^ d) for k in range(lax.axis_size(axis))])


def local(params, adam_m, adam_v, cameras, target, tile_ids, hit_shard, hit_local):
    width = params.shape[1]
    tile_count, listed = hit_local.shape
    shards = lax.axis_size("gs")
    along = lax.axis_size("tile")
    chunk = width // shards
    group = lax.axis_index("gs")
    seat = lax.axis_index("tile")
    aligned = chunk % LANES == 0
    team = BLOCK_TILES // tile_count
    assert team == 4
    blocks = along // team

    info, params = pack(group, params, target, hit_shard, hit_local, shards)
    parts = cut(group, tile_ids, cameras, params, shards if aligned else 1)
    if not aligned:
        parts = [
            lax.dynamic_slice_in_dim(parts[0], (group ^ d) * chunk, chunk, axis=1)
            for d in range(shards)
        ]
    parts = [swap(parts[d], "gs", d) for d in range(shards)]
    beside = swap(info, "tile", 1)
    beyond = swap(join(info, beside), "tile", 2)
    if not aligned:
        parts = [jnp.concatenate(parts, axis=1)]
    where = jnp.stack([seat % team, seat // team, jnp.int32(chunk)]).astype(jnp.int32)
    rendered, rows, partial = near(tile_ids, cameras, where, info, beside, parts, tile_count)
    packets = far(tile_ids, where, rows, partial, beyond, len(parts), tile_count, blocks)
    if not aligned:
        packets = [packets[0][:, d * chunk : (d + 1) * chunk] for d in range(shards)]
    packets = [swap(packets[d], "gs", d) for d in range(shards)]
    if blocks > 1:
        packets = [block_sum(packet, along, team) for packet in packets]
    if aligned:
        own = group
    else:
        packets = [jnp.stack(packets)[jnp.arange(shards) ^ group].transpose(1, 0, 2).reshape(ROWS, -1)]
        own = jnp.int32(0)
    made = ready = ()
    count = max(1, len(packets) // 2)
    for first in range(0, len(packets), count):
        known = first == 0 and len(packets) == 2 * count and blocks == 1
        made, ready = update(
            own, first, cameras, params, adam_m, adam_v, packets[first : first + count], made,
            parts[count:] if known else [], ready,
        )
    new_params, new_m, new_v = made
    return (rendered, new_params, new_m, new_v)


def block_sum(packet, along, team):
    step = team
    while step < along:
        packet = packet + swap(packet, "tile", step)
        step *= 2
    return packet


def solution(mesh):
    return jax.shard_map(
        local,
        mesh=mesh,
        in_specs=(
            P(None, ("groups", "gs")),
            P(None, ("groups", "gs")),
            P(None, ("groups", "gs")),
            P("groups", None),
            P(None, ("groups", "gs", "tile")),
            P(("groups", "gs", "tile")),
            P(("groups", "gs", "tile"), None, None),
            P(("groups", "gs", "tile"), None),
        ),
        out_specs=(
            P(None, ("groups", "gs", "tile")),
            P(None, ("groups", "gs")),
            P(None, ("groups", "gs")),
            P(None, ("groups", "gs")),
        ),
        check_vma=False,
    )
```

```python
import functools

import jax
import jax.numpy as jnp
from jax import lax
from jax.experimental import pallas as pl
from jax.experimental.pallas import tpu as pltpu
from jax.sharding import PartitionSpec as P

TILES_X = 120
TILES_Y = 68
TILE_SIDE = 16
BLOCK_TILES = 8
LANES = 128
ROWS = 16
LIST_STEP = 9
F32 = jnp.float32
BF16 = jnp.bfloat16

focal_length = 1000.0
center_x = 960.0
center_y = 540.0
dilation = 0.3
beta_one = 0.9
beta_two = 0.999
learn_rate = 0.01
adam_eps = 1e-08
adam_steps = 100.0
sh_const = (
    0.28209479177387814,
    0.4886025119029199,
    1.0925484305920792,
    0.31539156525252005,
    0.5462742152960396,
    0.5900435899266435,
    2.890611442640554,
    0.4570457994644658,
    0.3731763325901154,
    1.445305721320277,
)


def sh_basis(x, y, z):
    s = sh_const
    xx, yy, zz = x * x, y * y, z * z
    return [
        None,
        -s[1] * y,
        s[1] * z,
        -s[1] * x,
        s[2] * (x * y),
        -s[2] * (y * z),
        s[3] * (2.0 * zz - xx - yy),
        -s[2] * (x * z),
        s[4] * (xx - yy),
        -s[5] * y * (3.0 * xx - yy),
        s[6] * (x * y) * z,
        -s[7] * y * (4.0 * zz - xx - yy),
        s[8] * z * (2.0 * zz - 3.0 * xx - 3.0 * yy),
        -s[7] * x * (4.0 * zz - xx - yy),
        s[9] * z * (xx - yy),
        -s[5] * x * (xx - 3.0 * yy),
    ]


def sh_pull(h, x, y, z):
    s = sh_const
    xx, yy, zz = x * x, y * y, z * z
    xy, xz, yz = x * y, x * z, y * z
    diff = xx - yy
    ring = 4.0 * zz - xx - yy
    g_x = (
        -s[1] * h[3]
        + s[2] * (h[4] * y - h[7] * z)
        - (2.0 * s[3]) * h[6] * x
        + (2.0 * s[4]) * h[8] * x
        - (6.0 * s[5]) * h[9] * xy
        + s[6] * h[10] * yz
        + (2.0 * s[7]) * h[11] * xy
        - (6.0 * s[8]) * h[12] * xz
        - s[7] * h[13] * (ring - 2.0 * xx)
        + (2.0 * s[9]) * h[14] * xz
        - (3.0 * s[5]) * h[15] * diff
    )
    g_y = (
        -s[1] * h[1]
        + s[2] * (h[4] * x - h[5] * z)
        - (2.0 * s[3]) * h[6] * y
        - (2.0 * s[4]) * h[8] * y
        - (3.0 * s[5]) * h[9] * diff
        + s[6] * h[10] * xz
        - s[7] * h[11] * (ring - 2.0 * yy)
        - (6.0 * s[8]) * h[12] * yz
        + (2.0 * s[7]) * h[13] * xy
        - (2.0 * s[9]) * h[14] * yz
        + (6.0 * s[5]) * h[15] * xy
    )
    g_z = (
        s[1] * h[2]
        - s[2] * (h[5] * y + h[7] * x)
        + (4.0 * s[3]) * h[6] * z
        + s[6] * h[10] * xy
        - (8.0 * s[7]) * (h[11] * yz + h[13] * xz)
        + s[8] * h[12] * (6.0 * zz - 3.0 * xx - 3.0 * yy)
        + s[9] * h[14] * diff
    )
    return g_x, g_y, g_z


def project_parts(feat, cam):
    rot = [[cam[3 * r + c] for c in range(3)] for r in range(3)]
    off = [feat(a) - cam[9 + a] for a in range(3)]
    in_cam = [rot[r][0] * off[0] + rot[r][1] * off[1] + rot[r][2] * off[2] for r in range(3)]
    inv = 1.0 / in_cam[2]
    u = in_cam[0] * inv
    v = in_cam[1] * inv
    finv = focal_length * inv
    scale = [jnp.exp(2.0 * feat(3 + a)) for a in range(3)]
    quat = [feat(6 + a) for a in range(4)]
    rnorm = lax.rsqrt(quat[0] * quat[0] + quat[1] * quat[1] + quat[2] * quat[2] + quat[3] * quat[3])
    w, x, y, z = [q * rnorm for q in quat]
    turn = [
        [1.0 - 2.0 * (y * y + z * z), 2.0 * (x * y - w * z), 2.0 * (x * z + w * y)],
        [2.0 * (x * y + w * z), 1.0 - 2.0 * (x * x + z * z), 2.0 * (y * z - w * x)],
        [2.0 * (x * z - w * y), 2.0 * (y * z + w * x), 1.0 - 2.0 * (x * x + y * y)],
    ]
    screen = [
        [finv * (rot[0][c] - u * rot[2][c]) for c in range(3)],
        [finv * (rot[1][c] - v * rot[2][c]) for c in range(3)],
    ]
    axes = [
        [sum(screen[r][c] * turn[c][k] for c in range(3)) for k in range(3)] for r in range(2)
    ]
    wide = [[axes[r][k] * scale[k] for k in range(3)] for r in range(2)]
    cov_xx = sum(wide[0][k] * axes[0][k] for k in range(3)) + dilation
    cov_xy = sum(wide[0][k] * axes[1][k] for k in range(3))
    cov_yy = sum(wide[1][k] * axes[1][k] for k in range(3)) + dilation
    rdet = 1.0 / (cov_xx * cov_yy - cov_xy * cov_xy)
    conic = (cov_yy * rdet, -cov_xy * rdet, cov_xx * rdet)
    rlen = lax.rsqrt(off[0] * off[0] + off[1] * off[1] + off[2] * off[2])
    way = [off[a] * rlen for a in range(3)]
    return dict(
        rot=rot, inv=inv, u=u, v=v, finv=finv, scale=scale, rnorm=rnorm, rotor=(w, x, y, z), turn=turn,
        screen=screen, axes=axes, wide=wide, conic=conic, rlen=rlen, way=way,
    )


def shade(feat, cam):
    off = [feat(a) - cam[9 + a] for a in range(3)]
    rlen = lax.rsqrt(off[0] * off[0] + off[1] * off[1] + off[2] * off[2])
    basis = sh_basis(*[off[a] * rlen for a in range(3)])
    colours = []
    for k in range(3):
        total = 0.5 + sh_const[0] * feat(11 + 16 * k)
        for b in range(1, 16):
            total = total + feat(11 + 16 * k + b) * basis[b]
        colours.append(total)
    return colours


def project_rows(feat, cam):
    part = project_parts(feat, cam)
    mean_x = focal_length * part["u"] + center_x
    mean_y = focal_length * part["v"] + center_y
    logit = feat(10)
    log_opacity = jnp.minimum(logit, 0.0) - jnp.log(1.0 + jnp.exp(-jnp.abs(logit)))
    return [mean_x, mean_y, *part["conic"], log_opacity]


def flatten(part, basis):
    values = [value for row in part["rot"] for value in row]
    values += [part[key] for key in ("inv", "u", "v", "finv", "rnorm", "rlen")]
    values += list(part["rotor"]) + list(part["conic"]) + list(part["way"])
    for key in ("turn", "screen", "axes", "wide"):
        values += [value for row in part[key] for value in row]
    return values + basis[1:]


def unflatten(values):
    values = iter(values)

    def take(count):
        return [next(values) for _ in range(count)]

    def table(count):
        return [take(3) for _ in range(count)]

    part = dict(rot=table(3))
    for key in ("inv", "u", "v", "finv", "rnorm", "rlen"):
        part[key] = next(values)
    part["rotor"], part["conic"], part["way"] = take(4), take(3), take(3)
    for key, count in (("turn", 3), ("screen", 2), ("axes", 2), ("wide", 2)):
        part[key] = table(count)
    return part, [None] + take(15)


READY = 9 + 6 + 4 + 3 + 3 + 9 + 6 + 6 + 6 + 15


def project_pull(feat, part, basis, grads, put):
    g_mx, g_my, g_a, g_b, g_c, g_o = grads[:6]
    g_col = grads[6:9]
    way, rlen = part["way"], part["rlen"]
    pulled = [None]
    for k in range(3):
        put(11 + 16 * k, sh_const[0] * g_col[k])
    for b in range(1, 16):
        total = 0.0
        for k in range(3):
            put(11 + 16 * k + b, g_col[k] * basis[b])
            total = total + g_col[k] * feat(11 + 16 * k + b)
        pulled.append(total)
    g_way = sh_pull(pulled, *way)
    along = way[0] * g_way[0] + way[1] * g_way[1] + way[2] * g_way[2]
    g_off = [(g_way[a] - way[a] * along) * rlen for a in range(3)]
    put(10, g_o / (1.0 + jnp.exp(feat(10))))
    a, b, c = part["conic"]
    g_xx = -(a * a * g_a + a * b * g_b + b * b * g_c)
    g_xy = -(2.0 * a * b * g_a + (a * c + b * b) * g_b + 2.0 * b * c * g_c)
    g_yy = -(b * b * g_a + b * c * g_b + c * c * g_c)
    axes, wide, turn, screen = part["axes"], part["wide"], part["turn"], part["screen"]
    for k in range(3):
        g_scale = (
            g_xx * axes[0][k] * wide[0][k]
            + g_xy * axes[0][k] * wide[1][k]
            + g_yy * axes[1][k] * wide[1][k]
        )
        put(3 + k, 2.0 * g_scale)
    g_axes = [
        [2.0 * g_xx * wide[0][k] + g_xy * wide[1][k] for k in range(3)],
        [2.0 * g_yy * wide[1][k] + g_xy * wide[0][k] for k in range(3)],
    ]
    g_screen = [
        [sum(g_axes[r][k] * turn[c][k] for k in range(3)) for c in range(3)] for r in range(2)
    ]
    gm = [
        [g_axes[0][k] * screen[0][c] + g_axes[1][k] * screen[1][c] for k in range(3)]
        for c in range(3)
    ]
    w, x, y, z = part["rotor"]
    up_xy, up_xz, up_yz = gm[0][1] + gm[1][0], gm[0][2] + gm[2][0], gm[1][2] + gm[2][1]
    un_xy, un_xz, un_yz = gm[1][0] - gm[0][1], gm[0][2] - gm[2][0], gm[2][1] - gm[1][2]
    g_rotor = [
        2.0 * (z * un_xy + y * un_xz + x * un_yz),
        2.0 * (y * up_xy + z * up_xz + w * un_yz - 2.0 * x * (gm[1][1] + gm[2][2])),
        2.0 * (x * up_xy + z * up_yz + w * un_xz - 2.0 * y * (gm[0][0] + gm[2][2])),
        2.0 * (x * up_xz + y * up_yz + w * un_xy - 2.0 * z * (gm[0][0] + gm[1][1])),
    ]
    rotor = (w, x, y, z)
    along = sum(rotor[i] * g_rotor[i] for i in range(4))
    for i in range(4):
        put(6 + i, (g_rotor[i] - rotor[i] * along) * part["rnorm"])
    rot, inv, finv, u, v = part["rot"], part["inv"], part["finv"], part["u"], part["v"]
    g_u = focal_length * g_mx - finv * sum(g_screen[0][c] * rot[2][c] for c in range(3))
    g_v = focal_length * g_my - finv * sum(g_screen[1][c] * rot[2][c] for c in range(3))
    g_f = sum(g_screen[r][c] * screen[r][c] for r in range(2) for c in range(3))
    g_in = [g_u * inv, g_v * inv, -(g_f + g_u * u + g_v * v) * inv]
    for axis in range(3):
        put(
            axis,
            g_off[axis] + rot[0][axis] * g_in[0] + rot[1][axis] * g_in[1] + rot[2][axis] * g_in[2],
        )


def split(value):
    high = value.astype(BF16)
    return high, (value - high.astype(F32)).astype(BF16)


def matmul(a, b, dims=((1,), (0,))):
    return lax.dot_general(a, b, (dims, ((), ())), preferred_element_type=F32)


def spread_features(parts, scratch, count):
    tiles = sum(part.shape[1] for part in parts) // LANES
    at = 0
    for part in parts:
        for first in range(0, part.shape[1], LANES):
            for row in range(0, count, 8):
                rows = min(8, count - row)
                scratch[pl.ds(row * tiles + at, rows, stride=tiles), :] = part[
                    row : row + rows, first : first + LANES
                ]
            at += 1
    return tiles


def pack_kernel(shards, where, *refs):
    sources, (info, params, shard_of, local_of, goal, place_s, sems) = refs[:4], refs[4:]
    group = where[0]
    loads = [
        pltpu.make_async_copy(source, held, sems.at[k])
        for k, (source, held) in enumerate(zip(sources, (shard_of, local_of, goal, params)))
    ]
    for load in loads:
        load.start()
    for load in loads[:3]:
        load.wait()
    width = info.shape[1]
    tile_count, listed = local_of.shape
    rows_each = (info.shape[0] - 4) // tile_count
    columns = rows_each * width
    chunk = columns // shards
    info[0:3, :] = goal[...]
    for t in range(tile_count):
        place = (shard_of[t] ^ group) * chunk + (local_of[t : t + 1, :] - group * chunk)
        info[3:4, t * listed : (t + 1) * listed] = place.astype(F32)
        row_i = lax.broadcasted_iota(jnp.int32, (LANES, LANES), 0)
        col_i = lax.broadcasted_iota(jnp.int32, (LANES, LANES), 1)
        for first in range(0, listed, LANES):
            spread = jnp.broadcast_to(place[:, first : first + LANES].astype(F32), (LANES, LANES))
            place_s[first : first + LANES, :] = jnp.broadcast_to(
                jnp.sum(jnp.where(row_i == col_i, spread, 0.0), axis=1, keepdims=True), (LANES, LANES)
            )
        lane_of = lax.broadcasted_iota(jnp.int32, (8, LANES), 1).astype(F32)
        row_of = lax.broadcasted_iota(jnp.int32, (8, LANES), 0).astype(F32)
        for s in range(columns // LANES):
            best = jnp.full((8, LANES), -1.0, F32)
            column = lane_of + float(s * LANES)
            for first in range(0, listed, 8):
                best = jnp.where(
                    place_s[first : first + 8, :] == column, row_of + float(first), best
                )
            best = jnp.max(best, axis=0, keepdims=True)
            row, at = 4 + t * rows_each + s * LANES // width, s * LANES % width
            info[row : row + 1, at : at + LANES] = best
    loads[3].wait()


def pack(group, params, target, hit_shard, hit_local, shards):
    columns = params.shape[1]
    tile_count, listed = hit_local.shape
    width = target.shape[1]
    rows = 4 + tile_count * (columns // width)
    args = (hit_shard.reshape(tile_count, 1, listed), hit_local, target, params)
    return call(
        functools.partial(pack_kernel, shards),
        "pack",
        (jax.ShapeDtypeStruct((rows, width), F32), jax.ShapeDtypeStruct(params.shape, F32)),
        [smem()] + [pl.BlockSpec(memory_space=pltpu.HBM)] * 4,
        [
            pltpu.VMEM((tile_count, 1, listed), jnp.int32),
            pltpu.VMEM((tile_count, listed), jnp.int32),
            pltpu.VMEM(target.shape, F32),
            pltpu.VMEM((listed, LANES), F32),
            pltpu.SemaphoreType.DMA((4,)),
        ],
        (group.reshape(1),) + tuple(pltpu.with_memory_space_constraint(a, pltpu.HBM) for a in args),
        (vmem(), any_space()),
    )


def sent_rows(views):
    return (12 + 3 * views + 7) // 8 * 8


def cut_kernel(pieces, where, tile_ids, cams, params, *refs):
    parts, (feats, rows) = refs[:pieces], refs[pieces:]
    views = cams.shape[0]
    count = sent_rows(views)
    slabs = spread_features([params], feats, params.shape[0])

    def feat(f):
        return feats[f * slabs : (f + 1) * slabs, :]

    values = [feat(f) for f in range(11)]
    for v in range(views):
        values += shade(feat, [cams[v, i] for i in range(12)])
    values += [jnp.zeros((slabs, LANES), F32)] * (count - 1 - len(values))
    values.append(jnp.full((slabs, LANES), (tile_ids[0] // (TILES_X * TILES_Y)).astype(F32), F32))
    for f, value in enumerate(values):
        rows[pl.ds(f, slabs, stride=count), :] = value
    each = slabs // pieces
    for d in range(pieces):
        for h in range(each):
            first = (((where[0] ^ d) % pieces) * each + h) * count
            parts[d][:, h * LANES : (h + 1) * LANES] = rows[
                pl.ds(pl.multiple_of(first, 8), count), :
            ]


def cut(group, tile_ids, cameras, params, pieces):
    features, columns = params.shape
    slabs = columns // LANES
    count = sent_rows(cameras.shape[0])
    return list(
        call(
            functools.partial(cut_kernel, pieces),
            "cut",
            (jax.ShapeDtypeStruct((count, columns // pieces), F32),) * pieces,
            [smem()] * 3 + [vmem()],
            [
                pltpu.VMEM(((features + 8) * slabs, LANES), F32),
                pltpu.VMEM((count * (slabs + 1), LANES), F32),
            ],
            (group.reshape(1), tile_ids, cameras, params),
        )
    )


def lane_gather(source, lane):
    return jnp.take_along_axis(source, lane, axis=1, mode="promise_in_bounds")


def pixel_basis(pixels):
    pixel = lax.broadcasted_iota(jnp.int32, (8, pixels), 1)
    row = lax.broadcasted_iota(jnp.int32, (8, pixels), 0)
    middle = 0.5 * TILE_SIDE - 0.5
    u = (pixel % TILE_SIDE).astype(F32) - middle
    v = (pixel // TILE_SIDE).astype(F32) - middle
    value = jnp.where(row == 0, 1.0, 0.0)
    for at, term in ((1, u), (2, v), (3, u * u), (4, u * v), (5, v * v)):
        value = jnp.where(row == at, term, value)
    return value


def composite(tiles, first_group, me, rows, info_s, rendered, work):
    alpha_s, weight_s, pull_s, push_s, weight_2, entry_s, coef_s, colour_s, sums_s, index_s, acc_s, ninth_s = work
    groups = info_s.shape[0]
    listed = acc_s.shape[0] * LANES
    tile_count = info_s.shape[2] // listed
    pixels = info_s.shape[2] // tile_count
    parts = pixels // LANES
    halves = listed // LANES
    tiles_here = groups * tile_count
    spans = tiles_here * parts
    slabs = rows.shape[0] // ROWS - 1
    side = TILE_SIDE
    first_col, first_row = tiles

    def of_span(span):
        return pl.ds(span, listed, stride=LIST_STEP)

    def of_place(place):
        return pl.ds(place * LIST_STEP, spans)

    basis = pixel_basis(pixels)
    basis_3 = jnp.concatenate([basis, basis, basis], axis=0).astype(BF16)
    row_of = lax.broadcasted_iota(jnp.int32, (8, listed), 0)

    entries = []
    for n in range(tiles_here):
        g, t = n // tile_count, n % tile_count
        found = []
        for h in range(halves):
            first = t * listed + h * LANES
            at = info_s[g, 3:4, first : first + LANES].astype(jnp.int32)
            index_s[n * halves + h : n * halves + h + 1, :] = at
            at = jnp.broadcast_to(at, (8, LANES))
            lane, slab = at & (LANES - 1), at >> 7
            value = lane_gather(rows[0:8, :], lane)
            for s in range(1, slabs):
                value = jnp.where(
                    slab == s, lane_gather(rows[s * ROWS : s * ROWS + 8, :], lane), value
                )
            found.append(value)
        entries.append(jnp.concatenate(found, axis=1))
        for h in range(halves):
            entry_s[h, 8 * n : 8 * n + 8, :] = found[h]
    at = index_s[...]
    lane, slab = at & (LANES - 1), at >> 7
    ninth = lane_gather(rows[8:16, :], lane)
    for s in range(1, slabs):
        ninth = jnp.where(
            slab == s, lane_gather(rows[s * ROWS + 8 : s * ROWS + 16, :], lane), ninth
        )

    def of_lists(ref, f):
        at = pl.ds(f, tiles_here, stride=8)
        return jnp.concatenate([ref[h, at, :] for h in range(halves)], axis=1)

    tile_of = lax.broadcasted_iota(jnp.int32, (tiles_here, listed), 0)
    slot = (me ^ (first_group + tile_of // tile_count)) * tile_count + tile_of % tile_count
    mean_u = of_lists(entry_s, 2) - (((first_col + slot % 4) * side).astype(F32) + 0.5 * side)
    mean_v = of_lists(entry_s, 3) - (((first_row + slot // 4) * side).astype(F32) + 0.5 * side)
    quad_a = -0.5 * of_lists(entry_s, 4)
    quad_b = -of_lists(entry_s, 5)
    quad_c = -0.5 * of_lists(entry_s, 6)
    slope_u = 2.0 * quad_a * mean_u + quad_b * mean_v
    slope_v = 2.0 * quad_c * mean_v + quad_b * mean_u
    level = 0.5 * (slope_u * mean_u + slope_v * mean_v) + of_lists(entry_s, 7)
    for f, value in enumerate((level, -slope_u, -slope_v, quad_a, quad_b, quad_c)):
        for n in range(tiles_here):
            coef_s[f : f + 1, n * listed : (n + 1) * listed] = value[n : n + 1]
    coef_s[6:8, :] = jnp.zeros((2, tiles_here * listed), F32)
    coef = coef_s[...]
    terms = []
    for _ in range(3):
        terms.append(coef.astype(BF16).astype(F32))
        coef = coef - terms[-1]
    down = ((0,), (0,))
    power = matmul(jnp.concatenate(terms, axis=0).astype(BF16), basis_3, down)
    for n in range(tiles_here):
        for part in range(parts):
            alpha_s[of_span(n * parts + part), :] = jnp.exp(
                power[n * listed : (n + 1) * listed, part * LANES : (part + 1) * LANES]
            )
    colour_s[...] = jnp.zeros(colour_s.shape, F32)
    hues = []
    for n in range(tiles_here):
        last = jnp.concatenate([ninth[n * halves + h : n * halves + h + 1] for h in range(halves)], axis=1)
        colours = jnp.where(row_of < 2, entries[n], jnp.where(row_of == 2, last, 0.0))
        high = colours.astype(BF16).astype(F32)
        low = colours - high
        here = slice(n * listed, (n + 1) * listed)
        for at, value in ((0, high), (8, low), (16, high)):
            colour_s[24 * n + at : 24 * n + at + 8, here] = value
        hues.append(jnp.concatenate([high, low], axis=0).astype(BF16))

    unroll, quad = 32, 4
    steps = listed // unroll

    def forward(step, passed):
        for j in range(0, unroll, quad):
            at = [of_place(step * unroll + j + i) for i in range(quad)]
            alpha = [alpha_s[at[i], :] for i in range(quad)]
            keep = [1.0 - alpha[i] for i in range(quad)]
            two = keep[0] * keep[1]
            three = two * keep[2]
            weight_s[at[0], :] = alpha[0] * passed
            weight_s[at[1], :] = (alpha[1] * keep[0]) * passed
            weight_s[at[2], :] = (alpha[2] * two) * passed
            weight_s[at[3], :] = (alpha[3] * three) * passed
            passed = passed * (two * (keep[2] * keep[3]))
        return passed

    nought = jnp.zeros((spans, LANES), F32)
    lax.fori_loop(0, steps, forward, nought + 1.0)

    errors = []
    for n in range(tiles_here):
        g, t = n // tile_count, n % tile_count
        for part in range(parts):
            at = slice((n * parts + part) * LANES, (n * parts + part + 1) * LANES)
            weight_2[:listed, at], weight_2[listed:, at] = split(
                weight_s[of_span(n * parts + part), :]
            )
        at = slice(n * pixels, (n + 1) * pixels)
        image = matmul(hues[n], weight_2[:listed, at])
        image = image[0:8] + image[8:16] + matmul(hues[n], weight_2[listed:, at])[0:8]
        here = slice(t * pixels, (t + 1) * pixels)
        if rendered is not None and g == 0:
            rendered[:, here] = image[0:3]
        error = image - info_s[g, 0:8, here]
        high = error.astype(BF16).astype(F32)
        low = error - high
        errors += [high, high, low]

        hue = jnp.concatenate([high, low], axis=0).astype(BF16)
        across = ((1,), (1,))
        grads = matmul(hue, weight_2[:listed, at], across) + matmul(hue, weight_2[listed:, at], across)
        grads = grads[0:8] + grads[8:16]
        for h in range(halves):
            acc_s[h, 8 * n : 8 * n + 8, :] = grads[:, h * LANES : (h + 1) * LANES]
            row = n * halves + h
            ninth_s[row : row + 1, :] = grads[2:3, h * LANES : (h + 1) * LANES]
    pull = matmul(colour_s[...].astype(BF16), jnp.concatenate(errors, axis=0).astype(BF16), down)
    for n in range(tiles_here):
        for part in range(parts):
            pull_s[of_span(n * parts + part), :] = pull[
                n * listed : (n + 1) * listed, part * LANES : (part + 1) * LANES
            ]

    def backward(back, behind):
        for j in range(0, unroll, quad):
            at = [of_place(listed - 1 - (back * unroll + j + i)) for i in range(quad)]
            alpha = [alpha_s[at[i], :] for i in range(quad)]
            pull = [pull_s[at[i], :] for i in range(quad)]
            keep = [1.0 - alpha[i] for i in range(quad)]
            own = alpha[0] * pull[0]
            seen, through = behind, keep[0]
            for i in range(quad):
                push_s[at[i], :] = weight_s[at[i], :] * (pull[i] - seen)
                if i > 0:
                    own = own * keep[i] + alpha[i] * pull[i]
                    through = through * keep[i]
                seen = behind * through + own
            behind = seen
        return behind

    lax.fori_loop(0, steps, backward, nought)

    basis = basis.astype(BF16)
    for n in range(tiles_here):
        high, low = split(
            jnp.concatenate([push_s[of_span(n * parts + part), :] for part in range(parts)], axis=1)
        )
        moments = matmul(basis, high, across) + matmul(basis, low, across)
        for h in range(halves):
            sums_s[h, 8 * n : 8 * n + 8, :] = moments[:, h * LANES : (h + 1) * LANES]
    m_00, m_10, m_01, m_20, m_11, m_02 = [
        of_lists(sums_s, m) for m in range(6)
    ]
    n_10 = m_10 - mean_u * m_00
    n_01 = m_01 - mean_v * m_00
    for f, value in (
        (2, -(2.0 * quad_a * n_10 + quad_b * n_01)),
        (3, -(2.0 * quad_c * n_01 + quad_b * n_10)),
        (4, -0.5 * (m_20 - mean_u * (m_10 + n_10))),
        (5, -(m_11 - mean_u * m_01 - mean_v * n_10)),
        (6, -0.5 * (m_02 - mean_v * (m_01 + n_01))),
        (7, m_00),
    ):
        for h in range(halves):
            acc_s[h, pl.ds(f, tiles_here, stride=8), :] = value[:, h * LANES : (h + 1) * LANES]


def pool_sum(slab, info_s, acc_s, ninth_s):
    groups, _, width = info_s.shape
    listed = acc_s.shape[0] * LANES
    tile_count = width // listed
    halves = listed // LANES
    rows_each = (info_s.shape[1] - 4) // tile_count
    row_of = lax.broadcasted_iota(jnp.int32, (8, LANES), 0)

    totals, every = [], None
    for g in range(groups):
        total = jnp.zeros((8, LANES), F32)
        for t in range(tile_count):
            row, first = 4 + t * rows_each + slab * LANES // width, slab * LANES % width
            at = info_s[g, row : row + 1, first : first + LANES].astype(jnp.int32)
            at = jnp.broadcast_to(at, (8, LANES))
            n = g * tile_count + t
            every = at if every is None else jnp.where(row_of >= n * halves, at, every)
            lane, half = at & (LANES - 1), at >> 7
            for h in range(halves):
                here = lane_gather(acc_s[h, 8 * n : 8 * n + 8, :], lane)
                total = total + jnp.where(half == h, here, 0.0)
        totals.append(total)
    here = lane_gather(ninth_s[...], every & (LANES - 1))
    ninth = jnp.where(every >> 7 == row_of % halves, here, 0.0)
    return totals[0] + totals[1], jnp.sum(ninth, axis=0, keepdims=True)


def block_start(tile_id):
    within = tile_id % (TILES_X * TILES_Y)
    return (within % TILES_X) // 4 * 4, (within // TILES_X) // 2 * 2


def near_kernel(pieces, tile_ids, cams, where, own, other, *refs):
    parts = refs[:pieces]
    rendered, rows, partial, feats, info_s, *work = refs[pieces:]
    view = tile_ids[0] // (TILES_X * TILES_Y)
    cam = [cams[view, i] for i in range(12)]
    slabs = spread_features(parts, feats, parts[0].shape[0])
    projected = project_rows(lambda f: feats[f * slabs : (f + 1) * slabs, :], cam)
    colours = []
    for k in range(3):
        first = pl.multiple_of((11 + 3 * view + k) * slabs, slabs)
        colours.append(feats[pl.ds(first, slabs), :])
    for f, value in enumerate(colours[:2] + projected + [colours[2]] * 8):
        rows[pl.ds(f, slabs, stride=ROWS), :] = value
    info_s[0] = own[...]
    info_s[1] = other[...]
    composite(block_start(tile_ids[0]), 0, where[0], rows, info_s, rendered, work)
    for s in range(slabs):
        at = slice(s * LANES, (s + 1) * LANES)
        partial[0:8, at], partial[8:9, at] = pool_sum(s, info_s, *work[-2:])


def far_kernel(blocks, tile_ids, where, rows, partial, infos, *refs):
    *packets, info_s = refs[: len(refs) - 12]
    work = refs[len(refs) - 12 :]
    half = infos.shape[0] // 2
    info_s[0] = infos[:half, :]
    info_s[1] = infos[half:, :]
    composite(block_start(tile_ids[0]), 2, where[0], rows, info_s, None, work)
    share = (tile_ids[0] // (TILES_X * TILES_Y)).astype(F32)
    row_of = lax.broadcasted_iota(jnp.int32, (8, LANES), 0)
    lane_of = lax.broadcasted_iota(jnp.int32, (8, LANES), 1)
    chunk = packets[0].shape[1]
    for s in range(rows.shape[0] // ROWS - 1):
        total, ninth = pool_sum(s, info_s, *work[-2:])
        total = total + partial[0:8, s * LANES : (s + 1) * LANES]
        ninth = ninth + partial[8:9, s * LANES : (s + 1) * LANES]
        if blocks == 1:
            mine = share
        else:
            column = s * LANES + lane_of
            mine = jnp.where(column % where[2] // (where[2] // blocks) == where[1], share, 0.0)
        at = slice(s * LANES % chunk, s * LANES % chunk + LANES)
        packets[s * LANES // chunk][0:8, at] = total
        packets[s * LANES // chunk][8:16, at] = jnp.where(
            row_of == 0, jnp.broadcast_to(ninth, (8, LANES)), mine
        )


def join_kernel(first, second, out):
    half = first.shape[0]
    out[:half, :] = first[...]
    out[half:, :] = second[...]


def update_kernel(pieces, final, follows, prepares, ready, where, cams, params, adam_m, adam_v, *refs):
    packets, refs = refs[:pieces], refs[pieces:]
    senders, refs = refs[: pieces * prepares], refs[pieces * prepares :]
    made_ready, refs = refs[: 2 * ready], refs[2 * ready :]
    earlier, refs = refs[:follows], refs[follows:]
    if final:
        sinks, (feats, rows, grads, made, sems) = refs[:3], refs[3:]
    else:
        made, refs = refs[0], refs[1:]
        next_ready, (feats, rows, grads) = refs[: 2 * prepares], refs[2 * prepares :]
    features = params.shape[0]
    chunk = packets[0].shape[1]
    width = pieces * chunk
    slabs = width // LANES
    place = where[0] ^ where[1]
    start = place // pieces * pieces * chunk
    stores = []
    if follows:
        other = pl.ds(pl.multiple_of((place ^ pieces) // pieces * pieces * chunk, LANES), width)
        for k in range(3):
            store = pltpu.make_async_copy(
                earlier[0].at[k], sinks[k].at[:, other], sems.at[k, (features + 15) // 16]
            )
            store.start()
            stores.append(store)
    for d in range(pieces):
        for h in range(chunk // LANES):
            slab = (place ^ d) % pieces * (chunk // LANES) + h
            rows[pl.ds(slab, ROWS, stride=slabs), :] = packets[d][:, h * LANES : (h + 1) * LANES]
    pulled = [rows[f * slabs : (f + 1) * slabs, :] for f in range(10)]

    def put(f, value):
        grads[f * slabs : (f + 1) * slabs, :] = value

    def column(s):
        return pl.ds(pl.multiple_of(start + s * LANES, LANES), LANES)

    def forward(first, held, view):
        for s in range(slabs):
            at = pl.ds(pl.multiple_of(first + s * LANES, LANES), LANES)
            for row in range(0, features, 8):
                count = min(8, features - row)
                held[pl.ds(row * slabs + s, count, stride=slabs), :] = params[row : row + count, at]
        cam = []
        for i in range(12):
            value = jnp.full((slabs, LANES), cams[0, i], F32)
            for v in range(1, cams.shape[0]):
                value = jnp.where(view == float(v), cams[v, i], value)
            cam.append(value)
        part = project_parts(lambda f: held[f * slabs : (f + 1) * slabs, :], cam)
        return part, sh_basis(*part["way"])

    if ready:
        feats, saved = made_ready
        part, basis = unflatten([saved[8 * i : 8 * i + slabs, :] for i in range(READY)])
    else:
        part, basis = forward(start, feats, pulled[9])
    project_pull(
        lambda f: feats[f * slabs : (f + 1) * slabs, :],
        part, basis, pulled[2:8] + pulled[:2] + pulled[8:9], put,
    )
    rate = learn_rate / (1.0 - beta_one**adam_steps)
    unbias = 1.0 / (1.0 - beta_two**adam_steps)
    order = list(range(16, features, 8)) + [0, 8]
    for row in order:
        count = min(8, features - row)
        span = slice(row, row + count)
        for s in range(slabs):
            here = (span, slice(s * LANES, (s + 1) * LANES))
            grad = grads[pl.ds(row * slabs + s, count, stride=slabs), :]
            moment = beta_one * adam_m[span, column(s)] + (1.0 - beta_one) * grad
            second = beta_two * adam_v[span, column(s)] + (1.0 - beta_two) * grad * grad
            made.at[1][here] = moment
            made.at[2][here] = second
            made.at[0][here] = params[span, column(s)] - rate * moment / (
                jnp.sqrt(second * unbias) + adam_eps
            )
        if final and (row % 16 == 8 or row + count == features):
            first = row // 16 * 16
            span = pl.ds(first, row + count - first)
            columns = pl.ds(pl.multiple_of(start, LANES), width)
            for k in range(3):
                store = pltpu.make_async_copy(
                    made.at[k, span], sinks[k].at[span, columns], sems.at[k, first // 16]
                )
                store.start()
                stores.append(store)
    if prepares:
        held, saved = next_ready
        place = place ^ pieces
        for d in range(pieces):
            for h in range(chunk // LANES):
                slab = (place ^ d) % pieces * (chunk // LANES) + h
                last = senders[d].shape[0] - 1
                rows[pl.ds(slab, 1), :] = senders[d][last : last + 1, h * LANES : (h + 1) * LANES]
        part, basis = forward(place // pieces * pieces * chunk, held, rows[:slabs, :])
        for i, value in enumerate(flatten(part, basis)):
            saved[8 * i : 8 * i + slabs, :] = value
    for store in stores:
        store.wait()


def vmem():
    return pl.BlockSpec(memory_space=pltpu.VMEM)


def smem():
    return pl.BlockSpec(memory_space=pltpu.SMEM)


def any_space():
    return pl.BlockSpec(memory_space=pl.ANY)


def call(kernel, name, out_shape, in_specs, scratch, args, out_specs=None, grant=32):
    return pl.pallas_call(
        kernel,
        out_shape=out_shape,
        in_specs=in_specs,
        out_specs=out_specs or tuple(vmem() for _ in out_shape),
        scratch_shapes=scratch,
        compiler_params=pltpu.CompilerParams(vmem_limit_bytes=grant * 1024 * 1024),
        name=name,
    )(*args)


def work_shapes(tile_count, pixels, listed):
    tiles = 2 * tile_count
    spans = tiles * pixels // LANES
    assert spans < LIST_STEP and tiles * listed // LANES == 8 and tiles == 4
    return [pltpu.VMEM(((listed + 1) * LIST_STEP, LANES), F32)] * 4 + [
        pltpu.VMEM((2 * listed, spans * LANES), BF16),
        pltpu.VMEM((listed // LANES, 8 * tiles + 8, LANES), F32),
        pltpu.VMEM((8, tiles * listed), F32),
        pltpu.VMEM((24 * tiles, tiles * listed), F32),
        pltpu.VMEM((listed // LANES, 8 * tiles + 8, LANES), F32),
        pltpu.VMEM((8, LANES), jnp.int32),
        pltpu.VMEM((listed // LANES, 8 * tiles + 8, LANES), F32),
        pltpu.VMEM((8, LANES), F32),
    ]


def near(tile_ids, cameras, where, own, other, parts, tile_count):
    width = sum(part.shape[1] for part in parts)
    features = parts[0].shape[0]
    slabs = width // LANES
    pixels = listed = own.shape[1] // tile_count
    return call(
        functools.partial(near_kernel, len(parts)),
        "near",
        (
            jax.ShapeDtypeStruct((3, own.shape[1]), F32),
            jax.ShapeDtypeStruct((ROWS * (slabs + 1), LANES), F32),
            jax.ShapeDtypeStruct((ROWS, width), F32),
        ),
        [smem()] * 3 + [vmem()] * (2 + len(parts)),
        [pltpu.VMEM(((features + 8) * slabs, LANES), F32), pltpu.VMEM((2,) + own.shape, F32)]
        + work_shapes(tile_count, pixels, listed),
        (tile_ids, cameras, where, own, other, *parts),
    )


def far(tile_ids, where, rows, partial, infos, pieces, tile_count, blocks):
    width = partial.shape[1]
    pixels = listed = infos.shape[1] // tile_count
    info = (infos.shape[0] // 2, infos.shape[1])
    return call(
        functools.partial(far_kernel, blocks),
        "far",
        (jax.ShapeDtypeStruct((ROWS, width // pieces), F32),) * pieces,
        [smem()] * 2 + [vmem()] * 3,
        [pltpu.VMEM((2,) + info, F32)] + work_shapes(tile_count, pixels, listed),
        (tile_ids, where, rows, partial, infos),
    )


def join(first, second):
    shape = (2 * first.shape[0], first.shape[1])
    return call(
        join_kernel, "join", (jax.ShapeDtypeStruct(shape, F32),), [vmem()] * 2, [], (first, second)
    )[0]


def update(own, first, cameras, params, adam_m, adam_v, packets, earlier, senders, ready, final):
    features = params.shape[0]
    width = sum(packet.shape[1] for packet in packets)
    slabs = width // LANES
    shape = jax.ShapeDtypeStruct(params.shape, F32)
    by_feature = ((features + 8) * slabs, LANES)
    prepares = len(senders) > 0
    scratch = [
        pltpu.VMEM(by_feature, F32),
        pltpu.VMEM(((ROWS + 1) * slabs, LANES), F32),
        pltpu.VMEM(by_feature, F32),
    ]
    results = (3, features, width)
    if final:
        out_shape, out_specs = (shape, shape, shape), (any_space(),) * 3
        scratch += [
            pltpu.VMEM(results, F32),
            pltpu.SemaphoreType.DMA((3, (features + 15) // 16 + 1)),
        ]
    else:
        out_shape = (jax.ShapeDtypeStruct(results, F32),)
        if prepares:
            out_shape += (
                jax.ShapeDtypeStruct(by_feature, F32),
                jax.ShapeDtypeStruct((8 * READY, LANES), F32),
            )
        out_specs = (vmem(),) * len(out_shape)
    return call(
        functools.partial(
            update_kernel, len(packets), final, len(earlier), prepares, len(ready) > 0
        ),
        "update",
        out_shape,
        [smem()] * 2
        + [vmem()] * (3 + len(packets) + len(senders) + len(ready) + len(earlier)),
        scratch,
        (
            jnp.stack([own, jnp.int32(first)]).astype(jnp.int32),
            cameras, params, adam_m, adam_v, *packets, *senders, *ready, *earlier,
        ),
        out_specs,
    )


def swap(value, axis, d):
    if d == 0:
        return value
    return lax.ppermute(value, axis, [(k, k ^ d) for k in range(lax.axis_size(axis))])


def local(params, adam_m, adam_v, cameras, target, tile_ids, hit_shard, hit_local):
    width = params.shape[1]
    tile_count, listed = hit_local.shape
    shards = lax.axis_size("gs")
    along = lax.axis_size("tile")
    chunk = width // shards
    group = lax.axis_index("gs")
    seat = lax.axis_index("tile")
    aligned = chunk % LANES == 0
    team = BLOCK_TILES // tile_count
    assert team == 4
    blocks = along // team

    info, params = pack(group, params, target, hit_shard, hit_local, shards)
    parts = cut(group, tile_ids, cameras, params, shards if aligned else 1)
    if not aligned:
        parts = [
            lax.dynamic_slice_in_dim(parts[0], (group ^ d) * chunk, chunk, axis=1)
            for d in range(shards)
        ]
    parts = [swap(parts[d], "gs", d) for d in range(shards)]
    beside = swap(info, "tile", 1)
    beyond = swap(join(info, beside), "tile", 2)
    if not aligned:
        parts = [jnp.concatenate(parts, axis=1)]
    where = jnp.stack([seat % team, seat // team, jnp.int32(chunk)]).astype(jnp.int32)
    rendered, rows, partial = near(tile_ids, cameras, where, info, beside, parts, tile_count)
    packets = far(tile_ids, where, rows, partial, beyond, len(parts), tile_count, blocks)
    if not aligned:
        packets = [packets[0][:, d * chunk : (d + 1) * chunk] for d in range(shards)]
    packets = [swap(packets[d], "gs", d) for d in range(shards)]
    if blocks > 1:
        packets = [block_sum(packet, along, team) for packet in packets]
    if aligned:
        own = group
    else:
        packets = [jnp.stack(packets)[jnp.arange(shards) ^ group].transpose(1, 0, 2).reshape(ROWS, -1)]
        own = jnp.int32(0)
    earlier, ready = [], []
    half = len(packets) // 2
    if half > 0:
        out = update(
            own, 0, cameras, params, adam_m, adam_v, packets[:half], [],
            parts[half:] if blocks == 1 else [], [], False,
        )
        earlier, ready = list(out[:1]), list(out[1:])
    new_params, new_m, new_v = update(
        own, half, cameras, params, adam_m, adam_v, packets[half:], earlier, [], ready, True
    )
    return (rendered, new_params, new_m, new_v)


def block_sum(packet, along, team):
    step = team
    while step < along:
        packet = packet + swap(packet, "tile", step)
        step *= 2
    return packet


def solution(mesh):
    return jax.shard_map(
        local,
        mesh=mesh,
        in_specs=(
            P(None, ("groups", "gs")),
            P(None, ("groups", "gs")),
            P(None, ("groups", "gs")),
            P("groups", None),
            P(None, ("groups", "gs", "tile")),
            P(("groups", "gs", "tile")),
            P(("groups", "gs", "tile"), None, None),
            P(("groups", "gs", "tile"), None),
        ),
        out_specs=(
            P(None, ("groups", "gs", "tile")),
            P(None, ("groups", "gs")),
            P(None, ("groups", "gs")),
            P(None, ("groups", "gs")),
        ),
        check_vma=False,
    )
```

```python
import functools

import jax
import jax.numpy as jnp
from jax import lax
from jax.experimental import pallas as pl
from jax.experimental.pallas import tpu as pltpu
from jax.sharding import PartitionSpec as P

TILES_X = 120
TILES_Y = 68
TILE_SIDE = 16
BLOCK_TILES = 8
LANES = 128
ROWS = 16
LIST_STEP = 9
F32 = jnp.float32
BF16 = jnp.bfloat16

focal_length = 1000.0
center_x = 960.0
center_y = 540.0
dilation = 0.3
beta_one = 0.9
beta_two = 0.999
learn_rate = 0.01
adam_eps = 1e-08
adam_steps = 100.0
sh_const = (
    0.28209479177387814,
    0.4886025119029199,
    1.0925484305920792,
    0.31539156525252005,
    0.5462742152960396,
    0.5900435899266435,
    2.890611442640554,
    0.4570457994644658,
    0.3731763325901154,
    1.445305721320277,
)


def sh_basis(x, y, z):
    s = sh_const
    xx, yy, zz = x * x, y * y, z * z
    return [
        None,
        -s[1] * y,
        s[1] * z,
        -s[1] * x,
        s[2] * (x * y),
        -s[2] * (y * z),
        s[3] * (2.0 * zz - xx - yy),
        -s[2] * (x * z),
        s[4] * (xx - yy),
        -s[5] * y * (3.0 * xx - yy),
        s[6] * (x * y) * z,
        -s[7] * y * (4.0 * zz - xx - yy),
        s[8] * z * (2.0 * zz - 3.0 * xx - 3.0 * yy),
        -s[7] * x * (4.0 * zz - xx - yy),
        s[9] * z * (xx - yy),
        -s[5] * x * (xx - 3.0 * yy),
    ]


def sh_pull(h, x, y, z):
    s = sh_const
    xx, yy, zz = x * x, y * y, z * z
    xy, xz, yz = x * y, x * z, y * z
    diff = xx - yy
    ring = 4.0 * zz - xx - yy
    g_x = (
        -s[1] * h[3]
        + s[2] * (h[4] * y - h[7] * z)
        - (2.0 * s[3]) * h[6] * x
        + (2.0 * s[4]) * h[8] * x
        - (6.0 * s[5]) * h[9] * xy
        + s[6] * h[10] * yz
        + (2.0 * s[7]) * h[11] * xy
        - (6.0 * s[8]) * h[12] * xz
        - s[7] * h[13] * (ring - 2.0 * xx)
        + (2.0 * s[9]) * h[14] * xz
        - (3.0 * s[5]) * h[15] * diff
    )
    g_y = (
        -s[1] * h[1]
        + s[2] * (h[4] * x - h[5] * z)
        - (2.0 * s[3]) * h[6] * y
        - (2.0 * s[4]) * h[8] * y
        - (3.0 * s[5]) * h[9] * diff
        + s[6] * h[10] * xz
        - s[7] * h[11] * (ring - 2.0 * yy)
        - (6.0 * s[8]) * h[12] * yz
        + (2.0 * s[7]) * h[13] * xy
        - (2.0 * s[9]) * h[14] * yz
        + (6.0 * s[5]) * h[15] * xy
    )
    g_z = (
        s[1] * h[2]
        - s[2] * (h[5] * y + h[7] * x)
        + (4.0 * s[3]) * h[6] * z
        + s[6] * h[10] * xy
        - (8.0 * s[7]) * (h[11] * yz + h[13] * xz)
        + s[8] * h[12] * (6.0 * zz - 3.0 * xx - 3.0 * yy)
        + s[9] * h[14] * diff
    )
    return g_x, g_y, g_z


def project_parts(feat, cam):
    rot = [[cam[3 * r + c] for c in range(3)] for r in range(3)]
    off = [feat(a) - cam[9 + a] for a in range(3)]
    in_cam = [rot[r][0] * off[0] + rot[r][1] * off[1] + rot[r][2] * off[2] for r in range(3)]
    inv = 1.0 / in_cam[2]
    u = in_cam[0] * inv
    v = in_cam[1] * inv
    finv = focal_length * inv
    scale = [jnp.exp(2.0 * feat(3 + a)) for a in range(3)]
    quat = [feat(6 + a) for a in range(4)]
    rnorm = lax.rsqrt(quat[0] * quat[0] + quat[1] * quat[1] + quat[2] * quat[2] + quat[3] * quat[3])
    w, x, y, z = [q * rnorm for q in quat]
    turn = [
        [1.0 - 2.0 * (y * y + z * z), 2.0 * (x * y - w * z), 2.0 * (x * z + w * y)],
        [2.0 * (x * y + w * z), 1.0 - 2.0 * (x * x + z * z), 2.0 * (y * z - w * x)],
        [2.0 * (x * z - w * y), 2.0 * (y * z + w * x), 1.0 - 2.0 * (x * x + y * y)],
    ]
    screen = [
        [finv * (rot[0][c] - u * rot[2][c]) for c in range(3)],
        [finv * (rot[1][c] - v * rot[2][c]) for c in range(3)],
    ]
    axes = [
        [sum(screen[r][c] * turn[c][k] for c in range(3)) for k in range(3)] for r in range(2)
    ]
    wide = [[axes[r][k] * scale[k] for k in range(3)] for r in range(2)]
    cov_xx = sum(wide[0][k] * axes[0][k] for k in range(3)) + dilation
    cov_xy = sum(wide[0][k] * axes[1][k] for k in range(3))
    cov_yy = sum(wide[1][k] * axes[1][k] for k in range(3)) + dilation
    rdet = 1.0 / (cov_xx * cov_yy - cov_xy * cov_xy)
    conic = (cov_yy * rdet, -cov_xy * rdet, cov_xx * rdet)
    rlen = lax.rsqrt(off[0] * off[0] + off[1] * off[1] + off[2] * off[2])
    way = [off[a] * rlen for a in range(3)]
    return dict(
        rot=rot, inv=inv, u=u, v=v, finv=finv, scale=scale, rnorm=rnorm, rotor=(w, x, y, z), turn=turn,
        screen=screen, axes=axes, wide=wide, conic=conic, rlen=rlen, way=way,
    )


def shade(feat, cam):
    off = [feat(a) - cam[9 + a] for a in range(3)]
    rlen = lax.rsqrt(off[0] * off[0] + off[1] * off[1] + off[2] * off[2])
    basis = sh_basis(*[off[a] * rlen for a in range(3)])
    colours = []
    for k in range(3):
        total = 0.5 + sh_const[0] * feat(11 + 16 * k)
        for b in range(1, 16):
            total = total + feat(11 + 16 * k + b) * basis[b]
        colours.append(total)
    return colours


def project_rows(feat, cam):
    part = project_parts(feat, cam)
    mean_x = focal_length * part["u"] + center_x
    mean_y = focal_length * part["v"] + center_y
    logit = feat(10)
    log_opacity = jnp.minimum(logit, 0.0) - jnp.log(1.0 + jnp.exp(-jnp.abs(logit)))
    return [mean_x, mean_y, *part["conic"], log_opacity]


def flatten(part, basis):
    values = [value for row in part["rot"] for value in row]
    values += [part[key] for key in ("inv", "u", "v", "finv", "rnorm", "rlen")]
    values += list(part["rotor"]) + list(part["conic"]) + list(part["way"])
    for key in ("turn", "screen", "axes", "wide"):
        values += [value for row in part[key] for value in row]
    return values + basis[1:]


def unflatten(values):
    values = iter(values)

    def take(count):
        return [next(values) for _ in range(count)]

    def table(count):
        return [take(3) for _ in range(count)]

    part = dict(rot=table(3))
    for key in ("inv", "u", "v", "finv", "rnorm", "rlen"):
        part[key] = next(values)
    part["rotor"], part["conic"], part["way"] = take(4), take(3), take(3)
    for key, count in (("turn", 3), ("screen", 2), ("axes", 2), ("wide", 2)):
        part[key] = table(count)
    return part, [None] + take(15)


READY = 9 + 6 + 4 + 3 + 3 + 9 + 6 + 6 + 6 + 15


def project_pull(feat, part, basis, grads, put):
    g_mx, g_my, g_a, g_b, g_c, g_o = grads[:6]
    g_col = grads[6:9]
    way, rlen = part["way"], part["rlen"]
    pulled = [None]
    for k in range(3):
        put(11 + 16 * k, sh_const[0] * g_col[k])
    for b in range(1, 16):
        total = 0.0
        for k in range(3):
            put(11 + 16 * k + b, g_col[k] * basis[b])
            total = total + g_col[k] * feat(11 + 16 * k + b)
        pulled.append(total)
    g_way = sh_pull(pulled, *way)
    along = way[0] * g_way[0] + way[1] * g_way[1] + way[2] * g_way[2]
    g_off = [(g_way[a] - way[a] * along) * rlen for a in range(3)]
    put(10, g_o / (1.0 + jnp.exp(feat(10))))
    a, b, c = part["conic"]
    g_xx = -(a * a * g_a + a * b * g_b + b * b * g_c)
    g_xy = -(2.0 * a * b * g_a + (a * c + b * b) * g_b + 2.0 * b * c * g_c)
    g_yy = -(b * b * g_a + b * c * g_b + c * c * g_c)
    axes, wide, turn, screen = part["axes"], part["wide"], part["turn"], part["screen"]
    for k in range(3):
        g_scale = (
            g_xx * axes[0][k] * wide[0][k]
            + g_xy * axes[0][k] * wide[1][k]
            + g_yy * axes[1][k] * wide[1][k]
        )
        put(3 + k, 2.0 * g_scale)
    g_axes = [
        [2.0 * g_xx * wide[0][k] + g_xy * wide[1][k] for k in range(3)],
        [2.0 * g_yy * wide[1][k] + g_xy * wide[0][k] for k in range(3)],
    ]
    g_screen = [
        [sum(g_axes[r][k] * turn[c][k] for k in range(3)) for c in range(3)] for r in range(2)
    ]
    gm = [
        [g_axes[0][k] * screen[0][c] + g_axes[1][k] * screen[1][c] for k in range(3)]
        for c in range(3)
    ]
    w, x, y, z = part["rotor"]
    up_xy, up_xz, up_yz = gm[0][1] + gm[1][0], gm[0][2] + gm[2][0], gm[1][2] + gm[2][1]
    un_xy, un_xz, un_yz = gm[1][0] - gm[0][1], gm[0][2] - gm[2][0], gm[2][1] - gm[1][2]
    g_rotor = [
        2.0 * (z * un_xy + y * un_xz + x * un_yz),
        2.0 * (y * up_xy + z * up_xz + w * un_yz - 2.0 * x * (gm[1][1] + gm[2][2])),
        2.0 * (x * up_xy + z * up_yz + w * un_xz - 2.0 * y * (gm[0][0] + gm[2][2])),
        2.0 * (x * up_xz + y * up_yz + w * un_xy - 2.0 * z * (gm[0][0] + gm[1][1])),
    ]
    rotor = (w, x, y, z)
    along = sum(rotor[i] * g_rotor[i] for i in range(4))
    for i in range(4):
        put(6 + i, (g_rotor[i] - rotor[i] * along) * part["rnorm"])
    rot, inv, finv, u, v = part["rot"], part["inv"], part["finv"], part["u"], part["v"]
    g_u = focal_length * g_mx - finv * sum(g_screen[0][c] * rot[2][c] for c in range(3))
    g_v = focal_length * g_my - finv * sum(g_screen[1][c] * rot[2][c] for c in range(3))
    g_f = sum(g_screen[r][c] * screen[r][c] for r in range(2) for c in range(3))
    g_in = [g_u * inv, g_v * inv, -(g_f + g_u * u + g_v * v) * inv]
    for axis in range(3):
        put(
            axis,
            g_off[axis] + rot[0][axis] * g_in[0] + rot[1][axis] * g_in[1] + rot[2][axis] * g_in[2],
        )


def split(value):
    high = value.astype(BF16)
    return high, (value - high.astype(F32)).astype(BF16)


def matmul(a, b, dims=((1,), (0,))):
    return lax.dot_general(a, b, (dims, ((), ())), preferred_element_type=F32)


def spread_features(parts, scratch, count):
    tiles = sum(part.shape[1] for part in parts) // LANES
    at = 0
    for part in parts:
        for first in range(0, part.shape[1], LANES):
            for row in range(0, count, 8):
                rows = min(8, count - row)
                scratch[pl.ds(row * tiles + at, rows, stride=tiles), :] = part[
                    row : row + rows, first : first + LANES
                ]
            at += 1
    return tiles


def pack_kernel(shards, where, *refs):
    sources, (info, params, shard_of, local_of, goal, place_s, sems) = refs[:4], refs[4:]
    group = where[0]
    loads = [
        pltpu.make_async_copy(source, held, sems.at[k])
        for k, (source, held) in enumerate(zip(sources, (shard_of, local_of, goal, params)))
    ]
    for load in loads:
        load.start()
    for load in loads[:3]:
        load.wait()
    width = info.shape[1]
    tile_count, listed = local_of.shape
    rows_each = (info.shape[0] - 4) // tile_count
    columns = rows_each * width
    chunk = columns // shards
    info[0:3, :] = goal[...]
    for t in range(tile_count):
        place = (shard_of[t] ^ group) * chunk + (local_of[t : t + 1, :] - group * chunk)
        info[3:4, t * listed : (t + 1) * listed] = place.astype(F32)
        row_i = lax.broadcasted_iota(jnp.int32, (LANES, LANES), 0)
        col_i = lax.broadcasted_iota(jnp.int32, (LANES, LANES), 1)
        for first in range(0, listed, LANES):
            spread = jnp.broadcast_to(place[:, first : first + LANES].astype(F32), (LANES, LANES))
            place_s[first : first + LANES, :] = jnp.broadcast_to(
                jnp.sum(jnp.where(row_i == col_i, spread, 0.0), axis=1, keepdims=True), (LANES, LANES)
            )
        lane_of = lax.broadcasted_iota(jnp.int32, (8, LANES), 1).astype(F32)
        row_of = lax.broadcasted_iota(jnp.int32, (8, LANES), 0).astype(F32)
        for s in range(columns // LANES):
            best = jnp.full((8, LANES), -1.0, F32)
            column = lane_of + float(s * LANES)
            for first in range(0, listed, 8):
                best = jnp.where(
                    place_s[first : first + 8, :] == column, row_of + float(first), best
                )
            best = jnp.max(best, axis=0, keepdims=True)
            row, at = 4 + t * rows_each + s * LANES // width, s * LANES % width
            info[row : row + 1, at : at + LANES] = best
    loads[3].wait()


def pack(group, params, target, hit_shard, hit_local, shards):
    columns = params.shape[1]
    tile_count, listed = hit_local.shape
    width = target.shape[1]
    rows = 4 + tile_count * (columns // width)
    args = (hit_shard.reshape(tile_count, 1, listed), hit_local, target, params)
    return call(
        functools.partial(pack_kernel, shards),
        "pack",
        (jax.ShapeDtypeStruct((rows, width), F32), jax.ShapeDtypeStruct(params.shape, F32)),
        [smem()] + [pl.BlockSpec(memory_space=pltpu.HBM)] * 4,
        [
            pltpu.VMEM((tile_count, 1, listed), jnp.int32),
            pltpu.VMEM((tile_count, listed), jnp.int32),
            pltpu.VMEM(target.shape, F32),
            pltpu.VMEM((listed, LANES), F32),
            pltpu.SemaphoreType.DMA((4,)),
        ],
        (group.reshape(1),) + tuple(pltpu.with_memory_space_constraint(a, pltpu.HBM) for a in args),
        (vmem(), any_space()),
    )


def sent_rows(views):
    return (12 + 3 * views + 7) // 8 * 8


def cut_kernel(pieces, where, tile_ids, cams, params, *refs):
    parts, (feats, rows) = refs[:pieces], refs[pieces:]
    views = cams.shape[0]
    count = sent_rows(views)
    slabs = spread_features([params], feats, params.shape[0])

    def feat(f):
        return feats[f * slabs : (f + 1) * slabs, :]

    values = [feat(f) for f in range(11)]
    for v in range(views):
        values += shade(feat, [cams[v, i] for i in range(12)])
    values += [jnp.zeros((slabs, LANES), F32)] * (count - 1 - len(values))
    values.append(jnp.full((slabs, LANES), (tile_ids[0] // (TILES_X * TILES_Y)).astype(F32), F32))
    for f, value in enumerate(values):
        rows[pl.ds(f, slabs, stride=count), :] = value
    each = slabs // pieces
    for d in range(pieces):
        for h in range(each):
            first = (((where[0] ^ d) % pieces) * each + h) * count
            parts[d][:, h * LANES : (h + 1) * LANES] = rows[
                pl.ds(pl.multiple_of(first, 8), count), :
            ]


def cut(group, tile_ids, cameras, params, pieces):
    features, columns = params.shape
    slabs = columns // LANES
    count = sent_rows(cameras.shape[0])
    return list(
        call(
            functools.partial(cut_kernel, pieces),
            "cut",
            (jax.ShapeDtypeStruct((count, columns // pieces), F32),) * pieces,
            [smem()] * 3 + [vmem()],
            [
                pltpu.VMEM(((features + 8) * slabs, LANES), F32),
                pltpu.VMEM((count * (slabs + 1), LANES), F32),
            ],
            (group.reshape(1), tile_ids, cameras, params),
        )
    )


def lane_gather(source, lane):
    return jnp.take_along_axis(source, lane, axis=1, mode="promise_in_bounds")


def pixel_basis(pixels):
    pixel = lax.broadcasted_iota(jnp.int32, (8, pixels), 1)
    row = lax.broadcasted_iota(jnp.int32, (8, pixels), 0)
    middle = 0.5 * TILE_SIDE - 0.5
    u = (pixel % TILE_SIDE).astype(F32) - middle
    v = (pixel // TILE_SIDE).astype(F32) - middle
    value = jnp.where(row == 0, 1.0, 0.0)
    for at, term in ((1, u), (2, v), (3, u * u), (4, u * v), (5, v * v)):
        value = jnp.where(row == at, term, value)
    return value


def composite(tiles, first_group, me, rows, info_s, rendered, work):
    alpha_s, weight_s, pull_s, push_s, weight_2, entry_s, coef_s, colour_s, sums_s, index_s, acc_s, ninth_s = work
    groups = info_s.shape[0]
    listed = acc_s.shape[0] * LANES
    tile_count = info_s.shape[2] // listed
    pixels = info_s.shape[2] // tile_count
    parts = pixels // LANES
    halves = listed // LANES
    tiles_here = groups * tile_count
    spans = tiles_here * parts
    slabs = rows.shape[0] // ROWS - 1
    side = TILE_SIDE
    first_col, first_row = tiles

    def of_span(span):
        return pl.ds(span, listed, stride=LIST_STEP)

    def of_place(place):
        return pl.ds(place * LIST_STEP, spans)

    basis = pixel_basis(pixels)
    basis_3 = jnp.concatenate([basis, basis, basis], axis=0).astype(BF16)
    row_of = lax.broadcasted_iota(jnp.int32, (8, listed), 0)

    entries = []
    for n in range(tiles_here):
        g, t = n // tile_count, n % tile_count
        found = []
        for h in range(halves):
            first = t * listed + h * LANES
            at = info_s[g, 3:4, first : first + LANES].astype(jnp.int32)
            index_s[n * halves + h : n * halves + h + 1, :] = at
            at = jnp.broadcast_to(at, (8, LANES))
            lane, slab = at & (LANES - 1), at >> 7
            value = lane_gather(rows[0:8, :], lane)
            for s in range(1, slabs):
                value = jnp.where(
                    slab == s, lane_gather(rows[s * ROWS : s * ROWS + 8, :], lane), value
                )
            found.append(value)
        entries.append(jnp.concatenate(found, axis=1))
        for h in range(halves):
            entry_s[h, 8 * n : 8 * n + 8, :] = found[h]
    at = index_s[...]
    lane, slab = at & (LANES - 1), at >> 7
    ninth = lane_gather(rows[8:16, :], lane)
    for s in range(1, slabs):
        ninth = jnp.where(
            slab == s, lane_gather(rows[s * ROWS + 8 : s * ROWS + 16, :], lane), ninth
        )

    def of_lists(ref, f):
        at = pl.ds(f, tiles_here, stride=8)
        return jnp.concatenate([ref[h, at, :] for h in range(halves)], axis=1)

    tile_of = lax.broadcasted_iota(jnp.int32, (tiles_here, listed), 0)
    slot = (me ^ (first_group + tile_of // tile_count)) * tile_count + tile_of % tile_count
    mean_u = of_lists(entry_s, 2) - (((first_col + slot % 4) * side).astype(F32) + 0.5 * side)
    mean_v = of_lists(entry_s, 3) - (((first_row + slot // 4) * side).astype(F32) + 0.5 * side)
    quad_a = -0.5 * of_lists(entry_s, 4)
    quad_b = -of_lists(entry_s, 5)
    quad_c = -0.5 * of_lists(entry_s, 6)
    slope_u = 2.0 * quad_a * mean_u + quad_b * mean_v
    slope_v = 2.0 * quad_c * mean_v + quad_b * mean_u
    level = 0.5 * (slope_u * mean_u + slope_v * mean_v) + of_lists(entry_s, 7)
    for f, value in enumerate((level, -slope_u, -slope_v, quad_a, quad_b, quad_c)):
        for n in range(tiles_here):
            coef_s[f : f + 1, n * listed : (n + 1) * listed] = value[n : n + 1]
    coef_s[6:8, :] = jnp.zeros((2, tiles_here * listed), F32)
    coef = coef_s[...]
    terms = []
    for _ in range(3):
        terms.append(coef.astype(BF16).astype(F32))
        coef = coef - terms[-1]
    down = ((0,), (0,))
    power = matmul(jnp.concatenate(terms, axis=0).astype(BF16), basis_3, down)
    for n in range(tiles_here):
        for part in range(parts):
            alpha_s[of_span(n * parts + part), :] = jnp.exp(
                power[n * listed : (n + 1) * listed, part * LANES : (part + 1) * LANES]
            )
    colour_s[...] = jnp.zeros(colour_s.shape, F32)
    hues = []
    for n in range(tiles_here):
        last = jnp.concatenate([ninth[n * halves + h : n * halves + h + 1] for h in range(halves)], axis=1)
        colours = jnp.where(row_of < 2, entries[n], jnp.where(row_of == 2, last, 0.0))
        high = colours.astype(BF16).astype(F32)
        low = colours - high
        here = slice(n * listed, (n + 1) * listed)
        for at, value in ((0, high), (8, low), (16, high)):
            colour_s[24 * n + at : 24 * n + at + 8, here] = value
        hues.append(jnp.concatenate([high, low], axis=0).astype(BF16))

    unroll, quad = 32, 4
    steps = listed // unroll

    def forward(step, passed):
        for j in range(0, unroll, quad):
            at = [of_place(step * unroll + j + i) for i in range(quad)]
            alpha = [alpha_s[at[i], :] for i in range(quad)]
            keep = [1.0 - alpha[i] for i in range(quad)]
            two = keep[0] * keep[1]
            three = two * keep[2]
            weight_s[at[0], :] = alpha[0] * passed
            weight_s[at[1], :] = (alpha[1] * keep[0]) * passed
            weight_s[at[2], :] = (alpha[2] * two) * passed
            weight_s[at[3], :] = (alpha[3] * three) * passed
            passed = passed * (two * (keep[2] * keep[3]))
        return passed

    nought = jnp.zeros((spans, LANES), F32)
    lax.fori_loop(0, steps, forward, nought + 1.0)

    errors = []
    for n in range(tiles_here):
        g, t = n // tile_count, n % tile_count
        for part in range(parts):
            at = slice((n * parts + part) * LANES, (n * parts + part + 1) * LANES)
            weight_2[:listed, at], weight_2[listed:, at] = split(
                weight_s[of_span(n * parts + part), :]
            )
        at = slice(n * pixels, (n + 1) * pixels)
        image = matmul(hues[n], weight_2[:listed, at])
        image = image[0:8] + image[8:16] + matmul(hues[n], weight_2[listed:, at])[0:8]
        here = slice(t * pixels, (t + 1) * pixels)
        if rendered is not None and g == 0:
            rendered[:, here] = image[0:3]
        error = image - info_s[g, 0:8, here]
        high = error.astype(BF16).astype(F32)
        low = error - high
        errors += [high, high, low]

        hue = jnp.concatenate([high, low], axis=0).astype(BF16)
        across = ((1,), (1,))
        grads = matmul(hue, weight_2[:listed, at], across) + matmul(hue, weight_2[listed:, at], across)
        grads = grads[0:8] + grads[8:16]
        for h in range(halves):
            acc_s[h, 8 * n : 8 * n + 8, :] = grads[:, h * LANES : (h + 1) * LANES]
            row = n * halves + h
            ninth_s[row : row + 1, :] = grads[2:3, h * LANES : (h + 1) * LANES]
    pull = matmul(colour_s[...].astype(BF16), jnp.concatenate(errors, axis=0).astype(BF16), down)
    for n in range(tiles_here):
        for part in range(parts):
            pull_s[of_span(n * parts + part), :] = pull[
                n * listed : (n + 1) * listed, part * LANES : (part + 1) * LANES
            ]

    def backward(back, behind):
        for j in range(0, unroll, quad):
            at = [of_place(listed - 1 - (back * unroll + j + i)) for i in range(quad)]
            alpha = [alpha_s[at[i], :] for i in range(quad)]
            pull = [pull_s[at[i], :] for i in range(quad)]
            keep = [1.0 - alpha[i] for i in range(quad)]
            own = alpha[0] * pull[0]
            seen, through = behind, keep[0]
            for i in range(quad):
                push_s[at[i], :] = weight_s[at[i], :] * (pull[i] - seen)
                if i > 0:
                    own = own * keep[i] + alpha[i] * pull[i]
                    through = through * keep[i]
                seen = behind * through + own
            behind = seen
        return behind

    lax.fori_loop(0, steps, backward, nought)

    basis = basis.astype(BF16)
    for n in range(tiles_here):
        high, low = split(
            jnp.concatenate([push_s[of_span(n * parts + part), :] for part in range(parts)], axis=1)
        )
        moments = matmul(basis, high, across) + matmul(basis, low, across)
        for h in range(halves):
            sums_s[h, 8 * n : 8 * n + 8, :] = moments[:, h * LANES : (h + 1) * LANES]
    m_00, m_10, m_01, m_20, m_11, m_02 = [
        of_lists(sums_s, m) for m in range(6)
    ]
    n_10 = m_10 - mean_u * m_00
    n_01 = m_01 - mean_v * m_00
    for f, value in (
        (2, -(2.0 * quad_a * n_10 + quad_b * n_01)),
        (3, -(2.0 * quad_c * n_01 + quad_b * n_10)),
        (4, -0.5 * (m_20 - mean_u * (m_10 + n_10))),
        (5, -(m_11 - mean_u * m_01 - mean_v * n_10)),
        (6, -0.5 * (m_02 - mean_v * (m_01 + n_01))),
        (7, m_00),
    ):
        for h in range(halves):
            acc_s[h, pl.ds(f, tiles_here, stride=8), :] = value[:, h * LANES : (h + 1) * LANES]


def pool_sum(slab, info_s, acc_s, ninth_s):
    groups, _, width = info_s.shape
    listed = acc_s.shape[0] * LANES
    tile_count = width // listed
    halves = listed // LANES
    rows_each = (info_s.shape[1] - 4) // tile_count
    row_of = lax.broadcasted_iota(jnp.int32, (8, LANES), 0)

    totals, every = [], None
    for g in range(groups):
        total = jnp.zeros((8, LANES), F32)
        for t in range(tile_count):
            row, first = 4 + t * rows_each + slab * LANES // width, slab * LANES % width
            at = info_s[g, row : row + 1, first : first + LANES].astype(jnp.int32)
            at = jnp.broadcast_to(at, (8, LANES))
            n = g * tile_count + t
            every = at if every is None else jnp.where(row_of >= n * halves, at, every)
            lane, half = at & (LANES - 1), at >> 7
            for h in range(halves):
                here = lane_gather(acc_s[h, 8 * n : 8 * n + 8, :], lane)
                total = total + jnp.where(half == h, here, 0.0)
        totals.append(total)
    here = lane_gather(ninth_s[...], every & (LANES - 1))
    ninth = jnp.where(every >> 7 == row_of % halves, here, 0.0)
    return totals[0] + totals[1], jnp.sum(ninth, axis=0, keepdims=True)


def block_start(tile_id):
    within = tile_id % (TILES_X * TILES_Y)
    return (within % TILES_X) // 4 * 4, (within // TILES_X) // 2 * 2


def near_kernel(pieces, tile_ids, cams, where, own, other, *refs):
    parts = refs[:pieces]
    rendered, rows, partial, feats, info_s, *work = refs[pieces:]
    view = tile_ids[0] // (TILES_X * TILES_Y)
    cam = [cams[view, i] for i in range(12)]
    slabs = spread_features(parts, feats, parts[0].shape[0])
    projected = project_rows(lambda f: feats[f * slabs : (f + 1) * slabs, :], cam)
    colours = []
    for k in range(3):
        first = pl.multiple_of((11 + 3 * view + k) * slabs, slabs)
        colours.append(feats[pl.ds(first, slabs), :])
    for f, value in enumerate(colours[:2] + projected + [colours[2]] * 8):
        rows[pl.ds(f, slabs, stride=ROWS), :] = value
    info_s[0] = own[...]
    info_s[1] = other[...]
    composite(block_start(tile_ids[0]), 0, where[0], rows, info_s, rendered, work)
    for s in range(slabs):
        at = slice(s * LANES, (s + 1) * LANES)
        partial[0:8, at], partial[8:9, at] = pool_sum(s, info_s, *work[-2:])


def packet_width(packet):
    return packet.shape[1] - (LANES if packet.shape[0] == 8 else 0)


def far_kernel(blocks, tile_ids, where, rows, partial, infos, *refs):
    *packets, info_s = refs[: len(refs) - 12]
    work = refs[len(refs) - 12 :]
    half = infos.shape[0] // 2
    info_s[0] = infos[:half, :]
    info_s[1] = infos[half:, :]
    composite(block_start(tile_ids[0]), 2, where[0], rows, info_s, None, work)
    share = (tile_ids[0] // (TILES_X * TILES_Y)).astype(F32)
    row_of = lax.broadcasted_iota(jnp.int32, (8, LANES), 0)
    lane_of = lax.broadcasted_iota(jnp.int32, (8, LANES), 1)
    chunk = packet_width(packets[0])
    compact = packets[0].shape[0] == 8
    if compact:
        for packet in packets:
            packet[:, chunk:] = jnp.zeros((8, LANES), F32)
    for s in range(rows.shape[0] // ROWS - 1):
        total, ninth = pool_sum(s, info_s, *work[-2:])
        total = total + partial[0:8, s * LANES : (s + 1) * LANES]
        ninth = ninth + partial[8:9, s * LANES : (s + 1) * LANES]
        if blocks == 1:
            mine = share
        else:
            column = s * LANES + lane_of
            mine = jnp.where(column % where[2] // (where[2] // blocks) == where[1], share, 0.0)
        at = slice(s * LANES % chunk, s * LANES % chunk + LANES)
        packets[s * LANES // chunk][0:8, at] = total
        if compact:
            each, h = chunk // LANES, s % (chunk // LANES)
            mine = jnp.broadcast_to(mine, (8, LANES))[0:1]
            packets[s * LANES // chunk][h : h + 1, chunk:] = ninth
            packets[s * LANES // chunk][each + h : each + h + 1, chunk:] = mine
        else:
            packets[s * LANES // chunk][8:16, at] = jnp.where(
                row_of == 0, jnp.broadcast_to(ninth, (8, LANES)), mine
            )


def join_kernel(first, second, out):
    half = first.shape[0]
    out[:half, :] = first[...]
    out[half:, :] = second[...]


def update_kernel(pieces, final, follows, prepares, ready, where, cams, params, adam_m, adam_v, *refs):
    packets, refs = refs[:pieces], refs[pieces:]
    senders, refs = refs[: pieces * prepares], refs[pieces * prepares :]
    made_ready, refs = refs[: 2 * ready], refs[2 * ready :]
    earlier, refs = refs[:follows], refs[follows:]
    if final:
        sinks, (feats, rows, grads, made, sems) = refs[:3], refs[3:]
    else:
        made, refs = refs[0], refs[1:]
        next_ready, (feats, rows, grads) = refs[: 2 * prepares], refs[2 * prepares :]
    features = params.shape[0]
    chunk = packet_width(packets[0])
    width = pieces * chunk
    slabs = width // LANES
    place = where[0] ^ where[1]
    start = place // pieces * pieces * chunk
    stores = []
    if follows:
        other = pl.ds(pl.multiple_of((place ^ pieces) // pieces * pieces * chunk, LANES), width)
        for k in range(3):
            store = pltpu.make_async_copy(
                earlier[0].at[k], sinks[k].at[:, other], sems.at[k, (features + 15) // 16]
            )
            store.start()
            stores.append(store)
    for d in range(pieces):
        for h in range(chunk // LANES):
            slab = (place ^ d) % pieces * (chunk // LANES) + h
            packet, each = packets[d], chunk // LANES
            count = packet.shape[0]
            rows[pl.ds(slab, count, stride=slabs), :] = packet[:, h * LANES : (h + 1) * LANES]
            if count == 8:
                rows[pl.ds(8 * slabs + slab, 1), :] = packet[h : h + 1, chunk:]
                rows[pl.ds(9 * slabs + slab, 1), :] = packet[each + h : each + h + 1, chunk:]
    pulled = [rows[f * slabs : (f + 1) * slabs, :] for f in range(10)]

    def put(f, value):
        grads[f * slabs : (f + 1) * slabs, :] = value

    def column(s):
        return pl.ds(pl.multiple_of(start + s * LANES, LANES), LANES)

    def forward(first, held, view):
        for s in range(slabs):
            at = pl.ds(pl.multiple_of(first + s * LANES, LANES), LANES)
            for row in range(0, features, 8):
                count = min(8, features - row)
                held[pl.ds(row * slabs + s, count, stride=slabs), :] = params[row : row + count, at]
        cam = []
        for i in range(12):
            value = jnp.full((slabs, LANES), cams[0, i], F32)
            for v in range(1, cams.shape[0]):
                value = jnp.where(view == float(v), cams[v, i], value)
            cam.append(value)
        part = project_parts(lambda f: held[f * slabs : (f + 1) * slabs, :], cam)
        return part, sh_basis(*part["way"])

    if ready:
        feats, saved = made_ready
        part, basis = unflatten([saved[8 * i : 8 * i + slabs, :] for i in range(READY)])
    else:
        part, basis = forward(start, feats, pulled[9])
    project_pull(
        lambda f: feats[f * slabs : (f + 1) * slabs, :],
        part, basis, pulled[2:8] + pulled[:2] + pulled[8:9], put,
    )
    rate = learn_rate / (1.0 - beta_one**adam_steps)
    unbias = 1.0 / (1.0 - beta_two**adam_steps)
    order = list(range(16, features, 8)) + [0, 8]
    for row in order:
        count = min(8, features - row)
        span = slice(row, row + count)
        for s in range(slabs):
            here = (span, slice(s * LANES, (s + 1) * LANES))
            grad = grads[pl.ds(row * slabs + s, count, stride=slabs), :]
            moment = beta_one * adam_m[span, column(s)] + (1.0 - beta_one) * grad
            second = beta_two * adam_v[span, column(s)] + (1.0 - beta_two) * grad * grad
            made.at[1][here] = moment
            made.at[2][here] = second
            made.at[0][here] = params[span, column(s)] - rate * moment / (
                jnp.sqrt(second * unbias) + adam_eps
            )
        if final and (row % 16 == 8 or row + count == features):
            first = row // 16 * 16
            span = pl.ds(first, row + count - first)
            columns = pl.ds(pl.multiple_of(start, LANES), width)
            for k in range(3):
                store = pltpu.make_async_copy(
                    made.at[k, span], sinks[k].at[span, columns], sems.at[k, first // 16]
                )
                store.start()
                stores.append(store)
    if prepares:
        held, saved = next_ready
        place = place ^ pieces
        for d in range(pieces):
            for h in range(chunk // LANES):
                slab = (place ^ d) % pieces * (chunk // LANES) + h
                last = senders[d].shape[0] - 1
                rows[pl.ds(slab, 1), :] = senders[d][last : last + 1, h * LANES : (h + 1) * LANES]
        part, basis = forward(place // pieces * pieces * chunk, held, rows[:slabs, :])
        for i, value in enumerate(flatten(part, basis)):
            saved[8 * i : 8 * i + slabs, :] = value
    for store in stores:
        store.wait()


def vmem():
    return pl.BlockSpec(memory_space=pltpu.VMEM)


def smem():
    return pl.BlockSpec(memory_space=pltpu.SMEM)


def any_space():
    return pl.BlockSpec(memory_space=pl.ANY)


def call(kernel, name, out_shape, in_specs, scratch, args, out_specs=None, grant=32):
    return pl.pallas_call(
        kernel,
        out_shape=out_shape,
        in_specs=in_specs,
        out_specs=out_specs or tuple(vmem() for _ in out_shape),
        scratch_shapes=scratch,
        compiler_params=pltpu.CompilerParams(vmem_limit_bytes=grant * 1024 * 1024),
        name=name,
    )(*args)


def work_shapes(tile_count, pixels, listed):
    tiles = 2 * tile_count
    spans = tiles * pixels // LANES
    assert spans < LIST_STEP and tiles * listed // LANES == 8 and tiles == 4
    return [pltpu.VMEM(((listed + 1) * LIST_STEP, LANES), F32)] * 4 + [
        pltpu.VMEM((2 * listed, spans * LANES), BF16),
        pltpu.VMEM((listed // LANES, 8 * tiles + 8, LANES), F32),
        pltpu.VMEM((8, tiles * listed), F32),
        pltpu.VMEM((24 * tiles, tiles * listed), F32),
        pltpu.VMEM((listed // LANES, 8 * tiles + 8, LANES), F32),
        pltpu.VMEM((8, LANES), jnp.int32),
        pltpu.VMEM((listed // LANES, 8 * tiles + 8, LANES), F32),
        pltpu.VMEM((8, LANES), F32),
    ]


def near(tile_ids, cameras, where, own, other, parts, tile_count):
    width = sum(part.shape[1] for part in parts)
    features = parts[0].shape[0]
    slabs = width // LANES
    pixels = listed = own.shape[1] // tile_count
    return call(
        functools.partial(near_kernel, len(parts)),
        "near",
        (
            jax.ShapeDtypeStruct((3, own.shape[1]), F32),
            jax.ShapeDtypeStruct((ROWS * (slabs + 1), LANES), F32),
            jax.ShapeDtypeStruct((ROWS, width), F32),
        ),
        [smem()] * 3 + [vmem()] * (2 + len(parts)),
        [pltpu.VMEM(((features + 8) * slabs, LANES), F32), pltpu.VMEM((2,) + own.shape, F32)]
        + work_shapes(tile_count, pixels, listed),
        (tile_ids, cameras, where, own, other, *parts),
    )


def far(tile_ids, where, rows, partial, infos, pieces, tile_count, blocks):
    width = partial.shape[1]
    pixels = listed = infos.shape[1] // tile_count
    info = (infos.shape[0] // 2, infos.shape[1])
    shape = (ROWS, width)
    if pieces > 1:
        assert width // pieces // LANES <= 4
        shape = (8, width // pieces + LANES)
    return call(
        functools.partial(far_kernel, blocks),
        "far",
        (jax.ShapeDtypeStruct(shape, F32),) * pieces,
        [smem()] * 2 + [vmem()] * 3,
        [pltpu.VMEM((2,) + info, F32)] + work_shapes(tile_count, pixels, listed),
        (tile_ids, where, rows, partial, infos),
    )


def join(first, second):
    shape = (2 * first.shape[0], first.shape[1])
    return call(
        join_kernel, "join", (jax.ShapeDtypeStruct(shape, F32),), [vmem()] * 2, [], (first, second)
    )[0]


def update(own, first, cameras, params, adam_m, adam_v, packets, earlier, senders, ready, final):
    features = params.shape[0]
    width = sum(packet_width(packet) for packet in packets)
    slabs = width // LANES
    shape = jax.ShapeDtypeStruct(params.shape, F32)
    by_feature = ((features + 8) * slabs, LANES)
    prepares = len(senders) > 0
    scratch = [
        pltpu.VMEM(by_feature, F32),
        pltpu.VMEM(((ROWS + 1) * slabs, LANES), F32),
        pltpu.VMEM(by_feature, F32),
    ]
    results = (3, features, width)
    if final:
        out_shape, out_specs = (shape, shape, shape), (any_space(),) * 3
        scratch += [
            pltpu.VMEM(results, F32),
            pltpu.SemaphoreType.DMA((3, (features + 15) // 16 + 1)),
        ]
    else:
        out_shape = (jax.ShapeDtypeStruct(results, F32),)
        if prepares:
            out_shape += (
                jax.ShapeDtypeStruct(by_feature, F32),
                jax.ShapeDtypeStruct((8 * READY, LANES), F32),
            )
        out_specs = (vmem(),) * len(out_shape)
    return call(
        functools.partial(
            update_kernel, len(packets), final, len(earlier), prepares, len(ready) > 0
        ),
        "update",
        out_shape,
        [smem()] * 2
        + [vmem()] * (3 + len(packets) + len(senders) + len(ready) + len(earlier)),
        scratch,
        (
            jnp.stack([own, jnp.int32(first)]).astype(jnp.int32),
            cameras, params, adam_m, adam_v, *packets, *senders, *ready, *earlier,
        ),
        out_specs,
    )


def swap(value, axis, d):
    if d == 0:
        return value
    return lax.ppermute(value, axis, [(k, k ^ d) for k in range(lax.axis_size(axis))])


def local(params, adam_m, adam_v, cameras, target, tile_ids, hit_shard, hit_local):
    width = params.shape[1]
    tile_count, listed = hit_local.shape
    shards = lax.axis_size("gs")
    along = lax.axis_size("tile")
    chunk = width // shards
    group = lax.axis_index("gs")
    seat = lax.axis_index("tile")
    aligned = chunk % LANES == 0
    team = BLOCK_TILES // tile_count
    assert team == 4
    blocks = along // team

    info, params = pack(group, params, target, hit_shard, hit_local, shards)
    parts = cut(group, tile_ids, cameras, params, shards if aligned else 1)
    if not aligned:
        parts = [
            lax.dynamic_slice_in_dim(parts[0], (group ^ d) * chunk, chunk, axis=1)
            for d in range(shards)
        ]
    parts = [swap(parts[d], "gs", d) for d in range(shards)]
    beside = swap(info, "tile", 1)
    beyond = swap(join(info, beside), "tile", 2)
    if not aligned:
        parts = [jnp.concatenate(parts, axis=1)]
    where = jnp.stack([seat % team, seat // team, jnp.int32(chunk)]).astype(jnp.int32)
    rendered, rows, partial = near(tile_ids, cameras, where, info, beside, parts, tile_count)
    packets = far(tile_ids, where, rows, partial, beyond, len(parts), tile_count, blocks)
    if not aligned:
        packets = [packets[0][:, d * chunk : (d + 1) * chunk] for d in range(shards)]
    packets = [swap(packets[d], "gs", d) for d in range(shards)]
    if blocks > 1:
        packets = [block_sum(packet, along, team) for packet in packets]
    if aligned:
        own = group
    else:
        packets = [jnp.stack(packets)[jnp.arange(shards) ^ group].transpose(1, 0, 2).reshape(ROWS, -1)]
        own = jnp.int32(0)
    earlier, ready = [], []
    half = len(packets) // 2
    if half > 0:
        out = update(
            own, 0, cameras, params, adam_m, adam_v, packets[:half], [],
            parts[half:] if blocks == 1 else [], [], False,
        )
        earlier, ready = list(out[:1]), list(out[1:])
    new_params, new_m, new_v = update(
        own, half, cameras, params, adam_m, adam_v, packets[half:], earlier, [], ready, True
    )
    return (rendered, new_params, new_m, new_v)


def block_sum(packet, along, team):
    step = team
    while step < along:
        packet = packet + swap(packet, "tile", step)
        step *= 2
    return packet


def solution(mesh):
    return jax.shard_map(
        local,
        mesh=mesh,
        in_specs=(
            P(None, ("groups", "gs")),
            P(None, ("groups", "gs")),
            P(None, ("groups", "gs")),
            P("groups", None),
            P(None, ("groups", "gs", "tile")),
            P(("groups", "gs", "tile")),
            P(("groups", "gs", "tile"), None, None),
            P(("groups", "gs", "tile"), None),
        ),
        out_specs=(
            P(None, ("groups", "gs", "tile")),
            P(None, ("groups", "gs")),
            P(None, ("groups", "gs")),
            P(None, ("groups", "gs")),
        ),
        check_vma=False,
    )
```

```python
import functools

import jax
import jax.numpy as jnp
from jax import lax
from jax.experimental import pallas as pl
from jax.experimental.pallas import tpu as pltpu
from jax.sharding import PartitionSpec as P

TILES_X = 120
TILES_Y = 68
TILE_SIDE = 16
BLOCK_TILES = 8
LANES = 128
ROWS = 16
LIST_STEP = 9
F32 = jnp.float32
BF16 = jnp.bfloat16

focal_length = 1000.0
center_x = 960.0
center_y = 540.0
dilation = 0.3
beta_one = 0.9
beta_two = 0.999
learn_rate = 0.01
adam_eps = 1e-08
adam_steps = 100.0
sh_const = (
    0.28209479177387814,
    0.4886025119029199,
    1.0925484305920792,
    0.31539156525252005,
    0.5462742152960396,
    0.5900435899266435,
    2.890611442640554,
    0.4570457994644658,
    0.3731763325901154,
    1.445305721320277,
)


def sh_basis(x, y, z):
    s = sh_const
    xx, yy, zz = x * x, y * y, z * z
    return [
        None,
        -s[1] * y,
        s[1] * z,
        -s[1] * x,
        s[2] * (x * y),
        -s[2] * (y * z),
        s[3] * (2.0 * zz - xx - yy),
        -s[2] * (x * z),
        s[4] * (xx - yy),
        -s[5] * y * (3.0 * xx - yy),
        s[6] * (x * y) * z,
        -s[7] * y * (4.0 * zz - xx - yy),
        s[8] * z * (2.0 * zz - 3.0 * xx - 3.0 * yy),
        -s[7] * x * (4.0 * zz - xx - yy),
        s[9] * z * (xx - yy),
        -s[5] * x * (xx - 3.0 * yy),
    ]


def sh_pull(h, x, y, z):
    s = sh_const
    xx, yy, zz = x * x, y * y, z * z
    xy, xz, yz = x * y, x * z, y * z
    diff = xx - yy
    ring = 4.0 * zz - xx - yy
    g_x = (
        -s[1] * h[3]
        + s[2] * (h[4] * y - h[7] * z)
        - (2.0 * s[3]) * h[6] * x
        + (2.0 * s[4]) * h[8] * x
        - (6.0 * s[5]) * h[9] * xy
        + s[6] * h[10] * yz
        + (2.0 * s[7]) * h[11] * xy
        - (6.0 * s[8]) * h[12] * xz
        - s[7] * h[13] * (ring - 2.0 * xx)
        + (2.0 * s[9]) * h[14] * xz
        - (3.0 * s[5]) * h[15] * diff
    )
    g_y = (
        -s[1] * h[1]
        + s[2] * (h[4] * x - h[5] * z)
        - (2.0 * s[3]) * h[6] * y
        - (2.0 * s[4]) * h[8] * y
        - (3.0 * s[5]) * h[9] * diff
        + s[6] * h[10] * xz
        - s[7] * h[11] * (ring - 2.0 * yy)
        - (6.0 * s[8]) * h[12] * yz
        + (2.0 * s[7]) * h[13] * xy
        - (2.0 * s[9]) * h[14] * yz
        + (6.0 * s[5]) * h[15] * xy
    )
    g_z = (
        s[1] * h[2]
        - s[2] * (h[5] * y + h[7] * x)
        + (4.0 * s[3]) * h[6] * z
        + s[6] * h[10] * xy
        - (8.0 * s[7]) * (h[11] * yz + h[13] * xz)
        + s[8] * h[12] * (6.0 * zz - 3.0 * xx - 3.0 * yy)
        + s[9] * h[14] * diff
    )
    return g_x, g_y, g_z


def project_parts(feat, cam):
    rot = [[cam[3 * r + c] for c in range(3)] for r in range(3)]
    off = [feat(a) - cam[9 + a] for a in range(3)]
    in_cam = [rot[r][0] * off[0] + rot[r][1] * off[1] + rot[r][2] * off[2] for r in range(3)]
    inv = 1.0 / in_cam[2]
    u = in_cam[0] * inv
    v = in_cam[1] * inv
    finv = focal_length * inv
    scale = [jnp.exp(2.0 * feat(3 + a)) for a in range(3)]
    quat = [feat(6 + a) for a in range(4)]
    rnorm = lax.rsqrt(quat[0] * quat[0] + quat[1] * quat[1] + quat[2] * quat[2] + quat[3] * quat[3])
    w, x, y, z = [q * rnorm for q in quat]
    turn = [
        [1.0 - 2.0 * (y * y + z * z), 2.0 * (x * y - w * z), 2.0 * (x * z + w * y)],
        [2.0 * (x * y + w * z), 1.0 - 2.0 * (x * x + z * z), 2.0 * (y * z - w * x)],
        [2.0 * (x * z - w * y), 2.0 * (y * z + w * x), 1.0 - 2.0 * (x * x + y * y)],
    ]
    screen = [
        [finv * (rot[0][c] - u * rot[2][c]) for c in range(3)],
        [finv * (rot[1][c] - v * rot[2][c]) for c in range(3)],
    ]
    axes = [
        [sum(screen[r][c] * turn[c][k] for c in range(3)) for k in range(3)] for r in range(2)
    ]
    wide = [[axes[r][k] * scale[k] for k in range(3)] for r in range(2)]
    cov_xx = sum(wide[0][k] * axes[0][k] for k in range(3)) + dilation
    cov_xy = sum(wide[0][k] * axes[1][k] for k in range(3))
    cov_yy = sum(wide[1][k] * axes[1][k] for k in range(3)) + dilation
    rdet = 1.0 / (cov_xx * cov_yy - cov_xy * cov_xy)
    conic = (cov_yy * rdet, -cov_xy * rdet, cov_xx * rdet)
    rlen = lax.rsqrt(off[0] * off[0] + off[1] * off[1] + off[2] * off[2])
    way = [off[a] * rlen for a in range(3)]
    return dict(
        rot=rot, inv=inv, u=u, v=v, finv=finv, scale=scale, rnorm=rnorm, rotor=(w, x, y, z), turn=turn,
        screen=screen, axes=axes, wide=wide, conic=conic, rlen=rlen, way=way,
    )


def shade(feat, cam):
    off = [feat(a) - cam[9 + a] for a in range(3)]
    rlen = lax.rsqrt(off[0] * off[0] + off[1] * off[1] + off[2] * off[2])
    basis = sh_basis(*[off[a] * rlen for a in range(3)])
    colours = []
    for k in range(3):
        total = 0.5 + sh_const[0] * feat(11 + 16 * k)
        for b in range(1, 16):
            total = total + feat(11 + 16 * k + b) * basis[b]
        colours.append(total)
    return colours


def project_rows(feat, cam):
    part = project_parts(feat, cam)
    mean_x = focal_length * part["u"] + center_x
    mean_y = focal_length * part["v"] + center_y
    logit = feat(10)
    log_opacity = jnp.minimum(logit, 0.0) - jnp.log(1.0 + jnp.exp(-jnp.abs(logit)))
    return [mean_x, mean_y, *part["conic"], log_opacity]


def flatten(part, basis):
    values = [value for row in part["rot"] for value in row]
    values += [part[key] for key in ("inv", "u", "v", "finv", "rnorm", "rlen")]
    values += list(part["rotor"]) + list(part["conic"]) + list(part["way"])
    for key in ("turn", "screen", "axes", "wide"):
        values += [value for row in part[key] for value in row]
    return values + basis[1:]


def unflatten(values):
    values = iter(values)

    def take(count):
        return [next(values) for _ in range(count)]

    def table(count):
        return [take(3) for _ in range(count)]

    part = dict(rot=table(3))
    for key in ("inv", "u", "v", "finv", "rnorm", "rlen"):
        part[key] = next(values)
    part["rotor"], part["conic"], part["way"] = take(4), take(3), take(3)
    for key, count in (("turn", 3), ("screen", 2), ("axes", 2), ("wide", 2)):
        part[key] = table(count)
    return part, [None] + take(15)


READY = 9 + 6 + 4 + 3 + 3 + 9 + 6 + 6 + 6 + 15


def project_pull(feat, part, basis, grads, put):
    g_mx, g_my, g_a, g_b, g_c, g_o = grads[:6]
    g_col = grads[6:9]
    way, rlen = part["way"], part["rlen"]
    pulled = [None]
    for k in range(3):
        put(11 + 16 * k, sh_const[0] * g_col[k])
    for b in range(1, 16):
        total = 0.0
        for k in range(3):
            put(11 + 16 * k + b, g_col[k] * basis[b])
            total = total + g_col[k] * feat(11 + 16 * k + b)
        pulled.append(total)
    g_way = sh_pull(pulled, *way)
    along = way[0] * g_way[0] + way[1] * g_way[1] + way[2] * g_way[2]
    g_off = [(g_way[a] - way[a] * along) * rlen for a in range(3)]
    put(10, g_o / (1.0 + jnp.exp(feat(10))))
    a, b, c = part["conic"]
    g_xx = -(a * a * g_a + a * b * g_b + b * b * g_c)
    g_xy = -(2.0 * a * b * g_a + (a * c + b * b) * g_b + 2.0 * b * c * g_c)
    g_yy = -(b * b * g_a + b * c * g_b + c * c * g_c)
    axes, wide, turn, screen = part["axes"], part["wide"], part["turn"], part["screen"]
    for k in range(3):
        g_scale = (
            g_xx * axes[0][k] * wide[0][k]
            + g_xy * axes[0][k] * wide[1][k]
            + g_yy * axes[1][k] * wide[1][k]
        )
        put(3 + k, 2.0 * g_scale)
    g_axes = [
        [2.0 * g_xx * wide[0][k] + g_xy * wide[1][k] for k in range(3)],
        [2.0 * g_yy * wide[1][k] + g_xy * wide[0][k] for k in range(3)],
    ]
    g_screen = [
        [sum(g_axes[r][k] * turn[c][k] for k in range(3)) for c in range(3)] for r in range(2)
    ]
    gm = [
        [g_axes[0][k] * screen[0][c] + g_axes[1][k] * screen[1][c] for k in range(3)]
        for c in range(3)
    ]
    w, x, y, z = part["rotor"]
    up_xy, up_xz, up_yz = gm[0][1] + gm[1][0], gm[0][2] + gm[2][0], gm[1][2] + gm[2][1]
    un_xy, un_xz, un_yz = gm[1][0] - gm[0][1], gm[0][2] - gm[2][0], gm[2][1] - gm[1][2]
    g_rotor = [
        2.0 * (z * un_xy + y * un_xz + x * un_yz),
        2.0 * (y * up_xy + z * up_xz + w * un_yz - 2.0 * x * (gm[1][1] + gm[2][2])),
        2.0 * (x * up_xy + z * up_yz + w * un_xz - 2.0 * y * (gm[0][0] + gm[2][2])),
        2.0 * (x * up_xz + y * up_yz + w * un_xy - 2.0 * z * (gm[0][0] + gm[1][1])),
    ]
    rotor = (w, x, y, z)
    along = sum(rotor[i] * g_rotor[i] for i in range(4))
    for i in range(4):
        put(6 + i, (g_rotor[i] - rotor[i] * along) * part["rnorm"])
    rot, inv, finv, u, v = part["rot"], part["inv"], part["finv"], part["u"], part["v"]
    g_u = focal_length * g_mx - finv * sum(g_screen[0][c] * rot[2][c] for c in range(3))
    g_v = focal_length * g_my - finv * sum(g_screen[1][c] * rot[2][c] for c in range(3))
    g_f = sum(g_screen[r][c] * screen[r][c] for r in range(2) for c in range(3))
    g_in = [g_u * inv, g_v * inv, -(g_f + g_u * u + g_v * v) * inv]
    for axis in range(3):
        put(
            axis,
            g_off[axis] + rot[0][axis] * g_in[0] + rot[1][axis] * g_in[1] + rot[2][axis] * g_in[2],
        )


def split(value):
    high = value.astype(BF16)
    return high, (value - high.astype(F32)).astype(BF16)


def matmul(a, b, dims=((1,), (0,))):
    return lax.dot_general(a, b, (dims, ((), ())), preferred_element_type=F32)


def spread_features(parts, scratch, count):
    tiles = sum(part.shape[1] for part in parts) // LANES
    at = 0
    for part in parts:
        for first in range(0, part.shape[1], LANES):
            for row in range(0, count, 8):
                rows = min(8, count - row)
                scratch[pl.ds(row * tiles + at, rows, stride=tiles), :] = part[
                    row : row + rows, first : first + LANES
                ]
            at += 1
    return tiles


def pack_kernel(shards, where, *refs):
    sources, (info, params, shard_of, local_of, goal, place_s, sems) = refs[:4], refs[4:]
    group = where[0]
    loads = [
        pltpu.make_async_copy(source, held, sems.at[k])
        for k, (source, held) in enumerate(zip(sources, (shard_of, local_of, goal, params)))
    ]
    for load in loads:
        load.start()
    for load in loads[:3]:
        load.wait()
    width = info.shape[1]
    tile_count, listed = local_of.shape
    rows_each = (info.shape[0] - 4) // tile_count
    columns = rows_each * width
    chunk = columns // shards
    info[0:3, :] = goal[...]
    for t in range(tile_count):
        place = (shard_of[t] ^ group) * chunk + (local_of[t : t + 1, :] - group * chunk)
        info[3:4, t * listed : (t + 1) * listed] = place.astype(F32)
        row_i = lax.broadcasted_iota(jnp.int32, (LANES, LANES), 0)
        col_i = lax.broadcasted_iota(jnp.int32, (LANES, LANES), 1)
        for first in range(0, listed, LANES):
            spread = jnp.broadcast_to(place[:, first : first + LANES].astype(F32), (LANES, LANES))
            place_s[first : first + LANES, :] = jnp.broadcast_to(
                jnp.sum(jnp.where(row_i == col_i, spread, 0.0), axis=1, keepdims=True), (LANES, LANES)
            )
        lane_of = lax.broadcasted_iota(jnp.int32, (8, LANES), 1).astype(F32)
        row_of = lax.broadcasted_iota(jnp.int32, (8, LANES), 0).astype(F32)
        for s in range(columns // LANES):
            best = jnp.full((8, LANES), -1.0, F32)
            column = lane_of + float(s * LANES)
            for first in range(0, listed, 8):
                best = jnp.where(
                    place_s[first : first + 8, :] == column, row_of + float(first), best
                )
            best = jnp.max(best, axis=0, keepdims=True)
            row, at = 4 + t * rows_each + s * LANES // width, s * LANES % width
            info[row : row + 1, at : at + LANES] = best
    loads[3].wait()


def pack(group, params, target, hit_shard, hit_local, shards):
    columns = params.shape[1]
    tile_count, listed = hit_local.shape
    width = target.shape[1]
    rows = 4 + tile_count * (columns // width)
    args = (hit_shard.reshape(tile_count, 1, listed), hit_local, target, params)
    return call(
        functools.partial(pack_kernel, shards),
        "pack",
        (jax.ShapeDtypeStruct((rows, width), F32), jax.ShapeDtypeStruct(params.shape, F32)),
        [smem()] + [pl.BlockSpec(memory_space=pltpu.HBM)] * 4,
        [
            pltpu.VMEM((tile_count, 1, listed), jnp.int32),
            pltpu.VMEM((tile_count, listed), jnp.int32),
            pltpu.VMEM(target.shape, F32),
            pltpu.VMEM((listed, LANES), F32),
            pltpu.SemaphoreType.DMA((4,)),
        ],
        (group.reshape(1),) + tuple(pltpu.with_memory_space_constraint(a, pltpu.HBM) for a in args),
        (vmem(), any_space()),
    )


def sent_rows(views):
    return (12 + 3 * views + 7) // 8 * 8


def cut_kernel(pieces, where, tile_ids, cams, params, *refs):
    parts, (feats, rows) = refs[:pieces], refs[pieces:]
    views = cams.shape[0]
    count = sent_rows(views)
    slabs = spread_features([params], feats, params.shape[0])

    def feat(f):
        return feats[f * slabs : (f + 1) * slabs, :]

    values = [feat(f) for f in range(11)]
    for v in range(views):
        values += shade(feat, [cams[v, i] for i in range(12)])
    values += [jnp.zeros((slabs, LANES), F32)] * (count - 1 - len(values))
    values.append(jnp.full((slabs, LANES), (tile_ids[0] // (TILES_X * TILES_Y)).astype(F32), F32))
    for f, value in enumerate(values):
        rows[pl.ds(f, slabs, stride=count), :] = value
    each = slabs // pieces
    for d in range(pieces):
        for h in range(each):
            first = (((where[0] ^ d) % pieces) * each + h) * count
            parts[d][:, h * LANES : (h + 1) * LANES] = rows[
                pl.ds(pl.multiple_of(first, 8), count), :
            ]


def cut(group, tile_ids, cameras, params, pieces):
    features, columns = params.shape
    slabs = columns // LANES
    count = sent_rows(cameras.shape[0])
    return list(
        call(
            functools.partial(cut_kernel, pieces),
            "cut",
            (jax.ShapeDtypeStruct((count, columns // pieces), F32),) * pieces,
            [smem()] * 3 + [vmem()],
            [
                pltpu.VMEM(((features + 8) * slabs, LANES), F32),
                pltpu.VMEM((count * (slabs + 1), LANES), F32),
            ],
            (group.reshape(1), tile_ids, cameras, params),
        )
    )


def lane_gather(source, lane):
    return jnp.take_along_axis(source, lane, axis=1, mode="promise_in_bounds")


def pixel_basis(pixels):
    pixel = lax.broadcasted_iota(jnp.int32, (8, pixels), 1)
    row = lax.broadcasted_iota(jnp.int32, (8, pixels), 0)
    middle = 0.5 * TILE_SIDE - 0.5
    u = (pixel % TILE_SIDE).astype(F32) - middle
    v = (pixel // TILE_SIDE).astype(F32) - middle
    value = jnp.where(row == 0, 1.0, 0.0)
    for at, term in ((1, u), (2, v), (3, u * u), (4, u * v), (5, v * v)):
        value = jnp.where(row == at, term, value)
    return value


def composite(tiles, first_group, me, rows, info_s, rendered, work):
    alpha_s, weight_s, pull_s, push_s, weight_2, entry_s, coef_s, colour_s, sums_s, index_s, acc_s, ninth_s = work
    groups = info_s.shape[0]
    listed = acc_s.shape[0] * LANES
    tile_count = info_s.shape[2] // listed
    pixels = info_s.shape[2] // tile_count
    parts = pixels // LANES
    halves = listed // LANES
    tiles_here = groups * tile_count
    spans = tiles_here * parts
    slabs = rows.shape[0] // ROWS - 1
    side = TILE_SIDE
    first_col, first_row = tiles

    def of_span(span):
        return pl.ds(span, listed, stride=LIST_STEP)

    def of_place(place):
        return pl.ds(place * LIST_STEP, spans)

    basis = pixel_basis(pixels)
    basis_3 = jnp.concatenate([basis, basis, basis], axis=0).astype(BF16)
    row_of = lax.broadcasted_iota(jnp.int32, (8, listed), 0)

    entries = []
    for n in range(tiles_here):
        g, t = n // tile_count, n % tile_count
        found = []
        for h in range(halves):
            first = t * listed + h * LANES
            at = info_s[g, 3:4, first : first + LANES].astype(jnp.int32)
            index_s[n * halves + h : n * halves + h + 1, :] = at
            at = jnp.broadcast_to(at, (8, LANES))
            lane, slab = at & (LANES - 1), at >> 7
            value = lane_gather(rows[0:8, :], lane)
            for s in range(1, slabs):
                value = jnp.where(
                    slab == s, lane_gather(rows[s * ROWS : s * ROWS + 8, :], lane), value
                )
            found.append(value)
        entries.append(jnp.concatenate(found, axis=1))
        for h in range(halves):
            entry_s[h, 8 * n : 8 * n + 8, :] = found[h]
    at = index_s[...]
    lane, slab = at & (LANES - 1), at >> 7
    ninth = lane_gather(rows[8:16, :], lane)
    for s in range(1, slabs):
        ninth = jnp.where(
            slab == s, lane_gather(rows[s * ROWS + 8 : s * ROWS + 16, :], lane), ninth
        )

    def of_lists(ref, f):
        at = pl.ds(f, tiles_here, stride=8)
        return jnp.concatenate([ref[h, at, :] for h in range(halves)], axis=1)

    tile_of = lax.broadcasted_iota(jnp.int32, (tiles_here, listed), 0)
    slot = (me ^ (first_group + tile_of // tile_count)) * tile_count + tile_of % tile_count
    mean_u = of_lists(entry_s, 2) - (((first_col + slot % 4) * side).astype(F32) + 0.5 * side)
    mean_v = of_lists(entry_s, 3) - (((first_row + slot // 4) * side).astype(F32) + 0.5 * side)
    quad_a = -0.5 * of_lists(entry_s, 4)
    quad_b = -of_lists(entry_s, 5)
    quad_c = -0.5 * of_lists(entry_s, 6)
    slope_u = 2.0 * quad_a * mean_u + quad_b * mean_v
    slope_v = 2.0 * quad_c * mean_v + quad_b * mean_u
    level = 0.5 * (slope_u * mean_u + slope_v * mean_v) + of_lists(entry_s, 7)
    for f, value in enumerate((level, -slope_u, -slope_v, quad_a, quad_b, quad_c)):
        for n in range(tiles_here):
            coef_s[f : f + 1, n * listed : (n + 1) * listed] = value[n : n + 1]
    coef_s[6:8, :] = jnp.zeros((2, tiles_here * listed), F32)
    coef = coef_s[...]
    terms = []
    for _ in range(3):
        terms.append(coef.astype(BF16).astype(F32))
        coef = coef - terms[-1]
    down = ((0,), (0,))
    power = matmul(jnp.concatenate(terms, axis=0).astype(BF16), basis_3, down)
    for n in range(tiles_here):
        for part in range(parts):
            alpha_s[of_span(n * parts + part), :] = jnp.exp(
                power[n * listed : (n + 1) * listed, part * LANES : (part + 1) * LANES]
            )
    colour_s[...] = jnp.zeros(colour_s.shape, F32)
    hues = []
    for n in range(tiles_here):
        last = jnp.concatenate([ninth[n * halves + h : n * halves + h + 1] for h in range(halves)], axis=1)
        colours = jnp.where(row_of < 2, entries[n], jnp.where(row_of == 2, last, 0.0))
        high = colours.astype(BF16).astype(F32)
        low = colours - high
        here = slice(n * listed, (n + 1) * listed)
        for at, value in ((0, high), (8, low), (16, high)):
            colour_s[24 * n + at : 24 * n + at + 8, here] = value
        hues.append(jnp.concatenate([high, low], axis=0).astype(BF16))

    unroll, quad = 32, 4
    steps = listed // unroll

    def forward(step, passed):
        for j in range(0, unroll, quad):
            at = [of_place(step * unroll + j + i) for i in range(quad)]
            alpha = [alpha_s[at[i], :] for i in range(quad)]
            keep = [1.0 - alpha[i] for i in range(quad)]
            two = keep[0] * keep[1]
            three = two * keep[2]
            weight_s[at[0], :] = alpha[0] * passed
            weight_s[at[1], :] = (alpha[1] * keep[0]) * passed
            weight_s[at[2], :] = (alpha[2] * two) * passed
            weight_s[at[3], :] = (alpha[3] * three) * passed
            passed = passed * (two * (keep[2] * keep[3]))
        return passed

    nought = jnp.zeros((spans, LANES), F32)
    lax.fori_loop(0, steps, forward, nought + 1.0)

    errors = []
    for n in range(tiles_here):
        g, t = n // tile_count, n % tile_count
        for part in range(parts):
            at = slice((n * parts + part) * LANES, (n * parts + part + 1) * LANES)
            weight_2[:listed, at], weight_2[listed:, at] = split(
                weight_s[of_span(n * parts + part), :]
            )
        at = slice(n * pixels, (n + 1) * pixels)
        image = matmul(hues[n], weight_2[:listed, at])
        image = image[0:8] + image[8:16] + matmul(hues[n], weight_2[listed:, at])[0:8]
        here = slice(t * pixels, (t + 1) * pixels)
        if rendered is not None and g == 0:
            rendered[:, here] = image[0:3]
        error = image - info_s[g, 0:8, here]
        high = error.astype(BF16).astype(F32)
        low = error - high
        errors += [high, high, low]

        hue = jnp.concatenate([high, low], axis=0).astype(BF16)
        across = ((1,), (1,))
        grads = matmul(hue, weight_2[:listed, at], across) + matmul(hue, weight_2[listed:, at], across)
        grads = grads[0:8] + grads[8:16]
        for h in range(halves):
            acc_s[h, 8 * n : 8 * n + 8, :] = grads[:, h * LANES : (h + 1) * LANES]
            row = n * halves + h
            ninth_s[row : row + 1, :] = grads[2:3, h * LANES : (h + 1) * LANES]
    pull = matmul(colour_s[...].astype(BF16), jnp.concatenate(errors, axis=0).astype(BF16), down)
    for n in range(tiles_here):
        for part in range(parts):
            pull_s[of_span(n * parts + part), :] = pull[
                n * listed : (n + 1) * listed, part * LANES : (part + 1) * LANES
            ]

    def backward(back, behind):
        for j in range(0, unroll, quad):
            at = [of_place(listed - 1 - (back * unroll + j + i)) for i in range(quad)]
            alpha = [alpha_s[at[i], :] for i in range(quad)]
            pull = [pull_s[at[i], :] for i in range(quad)]
            keep = [1.0 - alpha[i] for i in range(quad)]
            own = alpha[0] * pull[0]
            seen, through = behind, keep[0]
            for i in range(quad):
                push_s[at[i], :] = weight_s[at[i], :] * (pull[i] - seen)
                if i > 0:
                    own = own * keep[i] + alpha[i] * pull[i]
                    through = through * keep[i]
                seen = behind * through + own
            behind = seen
        return behind

    lax.fori_loop(0, steps, backward, nought)

    basis = basis.astype(BF16)
    for n in range(tiles_here):
        high, low = split(
            jnp.concatenate([push_s[of_span(n * parts + part), :] for part in range(parts)], axis=1)
        )
        moments = matmul(basis, high, across) + matmul(basis, low, across)
        for h in range(halves):
            sums_s[h, 8 * n : 8 * n + 8, :] = moments[:, h * LANES : (h + 1) * LANES]
    m_00, m_10, m_01, m_20, m_11, m_02 = [
        of_lists(sums_s, m) for m in range(6)
    ]
    n_10 = m_10 - mean_u * m_00
    n_01 = m_01 - mean_v * m_00
    for f, value in (
        (2, -(2.0 * quad_a * n_10 + quad_b * n_01)),
        (3, -(2.0 * quad_c * n_01 + quad_b * n_10)),
        (4, -0.5 * (m_20 - mean_u * (m_10 + n_10))),
        (5, -(m_11 - mean_u * m_01 - mean_v * n_10)),
        (6, -0.5 * (m_02 - mean_v * (m_01 + n_01))),
        (7, m_00),
    ):
        for h in range(halves):
            acc_s[h, pl.ds(f, tiles_here, stride=8), :] = value[:, h * LANES : (h + 1) * LANES]


def pool_sum(slab, info_s, acc_s, ninth_s):
    groups, _, width = info_s.shape
    listed = acc_s.shape[0] * LANES
    tile_count = width // listed
    halves = listed // LANES
    rows_each = (info_s.shape[1] - 4) // tile_count
    row_of = lax.broadcasted_iota(jnp.int32, (8, LANES), 0)

    totals, every = [], None
    for g in range(groups):
        total = jnp.zeros((8, LANES), F32)
        for t in range(tile_count):
            row, first = 4 + t * rows_each + slab * LANES // width, slab * LANES % width
            at = info_s[g, row : row + 1, first : first + LANES].astype(jnp.int32)
            at = jnp.broadcast_to(at, (8, LANES))
            n = g * tile_count + t
            every = at if every is None else jnp.where(row_of >= n * halves, at, every)
            lane, half = at & (LANES - 1), at >> 7
            for h in range(halves):
                here = lane_gather(acc_s[h, 8 * n : 8 * n + 8, :], lane)
                total = total + jnp.where(half == h, here, 0.0)
        totals.append(total)
    here = lane_gather(ninth_s[...], every & (LANES - 1))
    ninth = jnp.where(every >> 7 == row_of % halves, here, 0.0)
    return totals[0] + totals[1], jnp.sum(ninth, axis=0, keepdims=True)


def block_start(tile_id):
    within = tile_id % (TILES_X * TILES_Y)
    return (within % TILES_X) // 4 * 4, (within // TILES_X) // 2 * 2


def near_kernel(pieces, tile_ids, cams, where, own, other, *refs):
    parts = refs[:pieces]
    rendered, rows, partial, feats, info_s, *work = refs[pieces:]
    view = tile_ids[0] // (TILES_X * TILES_Y)
    cam = [cams[view, i] for i in range(12)]
    slabs = spread_features(parts, feats, parts[0].shape[0])
    projected = project_rows(lambda f: feats[f * slabs : (f + 1) * slabs, :], cam)
    colours = []
    for k in range(3):
        first = pl.multiple_of((11 + 3 * view + k) * slabs, slabs)
        colours.append(feats[pl.ds(first, slabs), :])
    for f, value in enumerate(colours[:2] + projected + [colours[2]] * 8):
        rows[pl.ds(f, slabs, stride=ROWS), :] = value
    info_s[0] = own[...]
    info_s[1] = other[...]
    composite(block_start(tile_ids[0]), 0, where[0], rows, info_s, rendered, work)
    for s in range(slabs):
        at = slice(s * LANES, (s + 1) * LANES)
        partial[0:8, at], partial[8:9, at] = pool_sum(s, info_s, *work[-2:])


def packet_width(packet):
    return packet.shape[1] - (LANES if packet.shape[0] == 8 else 0)


def far_kernel(blocks, tile_ids, where, rows, partial, infos, *refs):
    *packets, info_s = refs[: len(refs) - 12]
    work = refs[len(refs) - 12 :]
    half = infos.shape[0] // 2
    info_s[0] = infos[:half, :]
    info_s[1] = infos[half:, :]
    composite(block_start(tile_ids[0]), 2, where[0], rows, info_s, None, work)
    share = (tile_ids[0] // (TILES_X * TILES_Y)).astype(F32)
    row_of = lax.broadcasted_iota(jnp.int32, (8, LANES), 0)
    lane_of = lax.broadcasted_iota(jnp.int32, (8, LANES), 1)
    chunk = packet_width(packets[0])
    compact = packets[0].shape[0] == 8
    if compact:
        for packet in packets:
            packet[:, chunk:] = jnp.zeros((8, LANES), F32)
    for s in range(rows.shape[0] // ROWS - 1):
        total, ninth = pool_sum(s, info_s, *work[-2:])
        total = total + partial[0:8, s * LANES : (s + 1) * LANES]
        ninth = ninth + partial[8:9, s * LANES : (s + 1) * LANES]
        if blocks == 1:
            mine = share
        else:
            column = s * LANES + lane_of
            mine = jnp.where(column % where[2] // (where[2] // blocks) == where[1], share, 0.0)
        at = slice(s * LANES % chunk, s * LANES % chunk + LANES)
        packets[s * LANES // chunk][0:8, at] = total
        if compact:
            each, h = chunk // LANES, s % (chunk // LANES)
            mine = jnp.broadcast_to(mine, (8, LANES))[0:1]
            packets[s * LANES // chunk][h : h + 1, chunk:] = ninth
            packets[s * LANES // chunk][each + h : each + h + 1, chunk:] = mine
        else:
            packets[s * LANES // chunk][8:16, at] = jnp.where(
                row_of == 0, jnp.broadcast_to(ninth, (8, LANES)), mine
            )


def join_kernel(first, second, out):
    half = first.shape[0]
    out[:half, :] = first[...]
    out[half:, :] = second[...]


def update_kernel(pieces, first_piece, final, follows, prepares, ready, where, cams, params, adam_m, adam_v, *refs):
    packets, refs = refs[:pieces], refs[pieces:]
    senders, refs = refs[: pieces * prepares], refs[pieces * prepares :]
    made_ready, refs = refs[: 2 * ready], refs[2 * ready :]
    earlier, refs = refs[:follows], refs[follows:]
    if final:
        sinks, (feats, rows, grads, made, sems) = refs[:3], refs[3:]
    else:
        made, refs = refs[0], refs[1:]
        next_ready, (feats, rows, grads) = refs[: 2 * prepares], refs[2 * prepares :]
    features = params.shape[0]
    chunk = packet_width(packets[0])
    width = pieces * chunk
    slabs = width // LANES
    place = where[3] ^ first_piece
    start = place // pieces * pieces * chunk
    stores = []
    if follows:
        other = pl.ds(pl.multiple_of((place ^ pieces) // pieces * pieces * chunk, LANES), width)
        for k in range(3):
            store = pltpu.make_async_copy(
                earlier[0].at[k], sinks[k].at[:, other], sems.at[k, (features + 15) // 16]
            )
            store.start()
            stores.append(store)
    for d in range(pieces):
        for h in range(chunk // LANES):
            slab = (place ^ d) % pieces * (chunk // LANES) + h
            packet, each = packets[d], chunk // LANES
            count = packet.shape[0]
            rows[pl.ds(slab, count, stride=slabs), :] = packet[:, h * LANES : (h + 1) * LANES]
            if count == 8:
                rows[pl.ds(8 * slabs + slab, 1), :] = packet[h : h + 1, chunk:]
                rows[pl.ds(9 * slabs + slab, 1), :] = packet[each + h : each + h + 1, chunk:]
    pulled = [rows[f * slabs : (f + 1) * slabs, :] for f in range(10)]

    def put(f, value):
        grads[f * slabs : (f + 1) * slabs, :] = value

    def column(s):
        return pl.ds(pl.multiple_of(start + s * LANES, LANES), LANES)

    def forward(first, held, view):
        for s in range(slabs):
            at = pl.ds(pl.multiple_of(first + s * LANES, LANES), LANES)
            for row in range(0, features, 8):
                count = min(8, features - row)
                held[pl.ds(row * slabs + s, count, stride=slabs), :] = params[row : row + count, at]
        cam = []
        for i in range(12):
            value = jnp.full((slabs, LANES), cams[0, i], F32)
            for v in range(1, cams.shape[0]):
                value = jnp.where(view == float(v), cams[v, i], value)
            cam.append(value)
        part = project_parts(lambda f: held[f * slabs : (f + 1) * slabs, :], cam)
        return part, sh_basis(*part["way"])

    if ready:
        feats, saved = made_ready
        part, basis = unflatten([saved[8 * i : 8 * i + slabs, :] for i in range(READY)])
    else:
        part, basis = forward(start, feats, pulled[9])
    project_pull(
        lambda f: feats[f * slabs : (f + 1) * slabs, :],
        part, basis, pulled[2:8] + pulled[:2] + pulled[8:9], put,
    )
    rate = learn_rate / (1.0 - beta_one**adam_steps)
    unbias = 1.0 / (1.0 - beta_two**adam_steps)
    order = list(range(16, features, 8)) + [0, 8]
    for row in order:
        count = min(8, features - row)
        span = slice(row, row + count)
        for s in range(slabs):
            here = (span, slice(s * LANES, (s + 1) * LANES))
            grad = grads[pl.ds(row * slabs + s, count, stride=slabs), :]
            moment = beta_one * adam_m[span, column(s)] + (1.0 - beta_one) * grad
            second = beta_two * adam_v[span, column(s)] + (1.0 - beta_two) * grad * grad
            made.at[1][here] = moment
            made.at[2][here] = second
            made.at[0][here] = params[span, column(s)] - rate * moment / (
                jnp.sqrt(second * unbias) + adam_eps
            )
        if final and (row % 16 == 8 or row + count == features):
            first = row // 16 * 16
            span = pl.ds(first, row + count - first)
            columns = pl.ds(pl.multiple_of(start, LANES), width)
            for k in range(3):
                store = pltpu.make_async_copy(
                    made.at[k, span], sinks[k].at[span, columns], sems.at[k, first // 16]
                )
                store.start()
                stores.append(store)
    if prepares:
        held, saved = next_ready
        place = place ^ pieces
        for d in range(pieces):
            for h in range(chunk // LANES):
                slab = (place ^ d) % pieces * (chunk // LANES) + h
                last = senders[d].shape[0] - 1
                rows[pl.ds(slab, 1), :] = senders[d][last : last + 1, h * LANES : (h + 1) * LANES]
        part, basis = forward(place // pieces * pieces * chunk, held, rows[:slabs, :])
        for i, value in enumerate(flatten(part, basis)):
            saved[8 * i : 8 * i + slabs, :] = value
    for store in stores:
        store.wait()


def vmem():
    return pl.BlockSpec(memory_space=pltpu.VMEM)


def smem():
    return pl.BlockSpec(memory_space=pltpu.SMEM)


def any_space():
    return pl.BlockSpec(memory_space=pl.ANY)


def call(kernel, name, out_shape, in_specs, scratch, args, out_specs=None, grant=32):
    return pl.pallas_call(
        kernel,
        out_shape=out_shape,
        in_specs=in_specs,
        out_specs=out_specs or tuple(vmem() for _ in out_shape),
        scratch_shapes=scratch,
        compiler_params=pltpu.CompilerParams(vmem_limit_bytes=grant * 1024 * 1024),
        name=name,
    )(*args)


def work_shapes(tile_count, pixels, listed):
    tiles = 2 * tile_count
    spans = tiles * pixels // LANES
    assert spans < LIST_STEP and tiles * listed // LANES == 8 and tiles == 4
    return [pltpu.VMEM(((listed + 1) * LIST_STEP, LANES), F32)] * 4 + [
        pltpu.VMEM((2 * listed, spans * LANES), BF16),
        pltpu.VMEM((listed // LANES, 8 * tiles + 8, LANES), F32),
        pltpu.VMEM((8, tiles * listed), F32),
        pltpu.VMEM((24 * tiles, tiles * listed), F32),
        pltpu.VMEM((listed // LANES, 8 * tiles + 8, LANES), F32),
        pltpu.VMEM((8, LANES), jnp.int32),
        pltpu.VMEM((listed // LANES, 8 * tiles + 8, LANES), F32),
        pltpu.VMEM((8, LANES), F32),
    ]


def near(tile_ids, cameras, where, own, other, parts, tile_count):
    width = sum(part.shape[1] for part in parts)
    features = parts[0].shape[0]
    slabs = width // LANES
    pixels = listed = own.shape[1] // tile_count
    return call(
        functools.partial(near_kernel, len(parts)),
        "near",
        (
            jax.ShapeDtypeStruct((3, own.shape[1]), F32),
            jax.ShapeDtypeStruct((ROWS * (slabs + 1), LANES), F32),
            jax.ShapeDtypeStruct((ROWS, width), F32),
        ),
        [smem()] * 3 + [vmem()] * (2 + len(parts)),
        [pltpu.VMEM(((features + 8) * slabs, LANES), F32), pltpu.VMEM((2,) + own.shape, F32)]
        + work_shapes(tile_count, pixels, listed),
        (tile_ids, cameras, where, own, other, *parts),
    )


def far(tile_ids, where, rows, partial, infos, pieces, tile_count, blocks):
    width = partial.shape[1]
    pixels = listed = infos.shape[1] // tile_count
    info = (infos.shape[0] // 2, infos.shape[1])
    shape = (ROWS, width)
    if pieces > 1:
        assert width // pieces // LANES <= 4
        shape = (8, width // pieces + LANES)
    return call(
        functools.partial(far_kernel, blocks),
        "far",
        (jax.ShapeDtypeStruct(shape, F32),) * pieces,
        [smem()] * 2 + [vmem()] * 3,
        [pltpu.VMEM((2,) + info, F32)] + work_shapes(tile_count, pixels, listed),
        (tile_ids, where, rows, partial, infos),
    )


def join(first, second):
    shape = (2 * first.shape[0], first.shape[1])
    return call(
        join_kernel, "join", (jax.ShapeDtypeStruct(shape, F32),), [vmem()] * 2, [], (first, second)
    )[0]


def update(where, first, cameras, params, adam_m, adam_v, packets, earlier, senders, ready, final):
    features = params.shape[0]
    width = sum(packet_width(packet) for packet in packets)
    slabs = width // LANES
    shape = jax.ShapeDtypeStruct(params.shape, F32)
    by_feature = ((features + 8) * slabs, LANES)
    prepares = len(senders) > 0
    scratch = [
        pltpu.VMEM(by_feature, F32),
        pltpu.VMEM(((ROWS + 1) * slabs, LANES), F32),
        pltpu.VMEM(by_feature, F32),
    ]
    results = (3, features, width)
    if final:
        out_shape, out_specs = (shape, shape, shape), (any_space(),) * 3
        scratch += [
            pltpu.VMEM(results, F32),
            pltpu.SemaphoreType.DMA((3, (features + 15) // 16 + 1)),
        ]
    else:
        out_shape = (jax.ShapeDtypeStruct(results, F32),)
        if prepares:
            out_shape += (
                jax.ShapeDtypeStruct(by_feature, F32),
                jax.ShapeDtypeStruct((8 * READY, LANES), F32),
            )
        out_specs = (vmem(),) * len(out_shape)
    return call(
        functools.partial(
            update_kernel, len(packets), first, final, len(earlier), prepares, len(ready) > 0
        ),
        "update",
        out_shape,
        [smem()] * 2
        + [vmem()] * (3 + len(packets) + len(senders) + len(ready) + len(earlier)),
        scratch,
        (
            where, cameras, params, adam_m, adam_v, *packets, *senders, *ready, *earlier,
        ),
        out_specs,
    )


def swap(value, axis, d):
    if d == 0:
        return value
    return lax.ppermute(value, axis, [(k, k ^ d) for k in range(lax.axis_size(axis))])


def local(params, adam_m, adam_v, cameras, target, tile_ids, hit_shard, hit_local):
    width = params.shape[1]
    tile_count, listed = hit_local.shape
    shards = lax.axis_size("gs")
    along = lax.axis_size("tile")
    chunk = width // shards
    group = lax.axis_index("gs")
    seat = lax.axis_index("tile")
    aligned = chunk % LANES == 0
    team = BLOCK_TILES // tile_count
    assert team == 4
    blocks = along // team

    info, params = pack(group, params, target, hit_shard, hit_local, shards)
    parts = cut(group, tile_ids, cameras, params, shards if aligned else 1)
    if not aligned:
        parts = [
            lax.dynamic_slice_in_dim(parts[0], (group ^ d) * chunk, chunk, axis=1)
            for d in range(shards)
        ]
    parts = [swap(parts[d], "gs", d) for d in range(shards)]
    beside = swap(info, "tile", 1)
    beyond = swap(join(info, beside), "tile", 2)
    if not aligned:
        parts = [jnp.concatenate(parts, axis=1)]
    own = group if aligned else jnp.int32(0)
    where = jnp.stack([seat % team, seat // team, jnp.int32(chunk), own]).astype(jnp.int32)
    rendered, rows, partial = near(tile_ids, cameras, where, info, beside, parts, tile_count)
    packets = far(tile_ids, where, rows, partial, beyond, len(parts), tile_count, blocks)
    if not aligned:
        packets = [packets[0][:, d * chunk : (d + 1) * chunk] for d in range(shards)]
    packets = [swap(packets[d], "gs", d) for d in range(shards)]
    if blocks > 1:
        packets = [block_sum(packet, along, team) for packet in packets]
    if not aligned:
        packets = [jnp.stack(packets)[jnp.arange(shards) ^ group].transpose(1, 0, 2).reshape(ROWS, -1)]
    earlier, ready = [], []
    half = len(packets) // 2
    if half > 0:
        out = update(
            where, 0, cameras, params, adam_m, adam_v, packets[:half], [],
            parts[half:] if blocks == 1 else [], [], False,
        )
        earlier, ready = list(out[:1]), list(out[1:])
    new_params, new_m, new_v = update(
        where, half, cameras, params, adam_m, adam_v, packets[half:], earlier, [], ready, True
    )
    return (rendered, new_params, new_m, new_v)


def block_sum(packet, along, team):
    step = team
    while step < along:
        packet = packet + swap(packet, "tile", step)
        step *= 2
    return packet


def solution(mesh):
    return jax.shard_map(
        local,
        mesh=mesh,
        in_specs=(
            P(None, ("groups", "gs")),
            P(None, ("groups", "gs")),
            P(None, ("groups", "gs")),
            P("groups", None),
            P(None, ("groups", "gs", "tile")),
            P(("groups", "gs", "tile")),
            P(("groups", "gs", "tile"), None, None),
            P(("groups", "gs", "tile"), None),
        ),
        out_specs=(
            P(None, ("groups", "gs", "tile")),
            P(None, ("groups", "gs")),
            P(None, ("groups", "gs")),
            P(None, ("groups", "gs")),
        ),
        check_vma=False,
    )
```
